32 devices in a mesh: seq: 8 (over z, y), rows: 4 (over x, core).
Axes of the slice: x: 2, y: 2, z: 4, core: 2. Of those that a mesh axis runs over, the one named last changes fastest.
Arguments:
- inputs: bfloat16 [8, 1024, 2048], P('rows', 'seq'), may hold values from -6 to 6
- segment_ids: int32 [8, 1024], P('rows', 'seq'), may hold values from 0 to 1, as said below
- mix_gain: float32 [2048], replicated, may hold values from 0.25 to 1.75
- in_weight: bfloat16 [2048, 2, 2560], P(None, None, 'seq'), may hold values from -0.125 to 0.125
- conv_weight: float32 [4, 2560], replicated, may hold values from -3 to 3
- conv_bias: float32 [2560], replicated, may hold values from -3 to 3
- gate_weight: bfloat16 [160, 2, 2560], replicated, may hold values from -0.5 to 0.5
- gate_bias: float32 [2, 2560], replicated, may hold values from -3 to 3
- decay_param: float32 [2560], replicated, may hold values from 2 to 9
- out_weight: bfloat16 [2048, 2560], P(None, 'seq'), may hold values from -0.3125 to 0.3125
- mlp_gain: float32 [2048], replicated, may hold values from 0.25 to 1.75
- mlp_in: bfloat16 [2048, 2, 6144], P(None, None, 'seq'), may hold values from -0.125 to 0.125
- down_weight: bfloat16 [2048, 6144], P(None, 'seq'), may hold values from -0.109375 to 0.109375
- cotangent: bfloat16 [8, 1024, 2048], P('rows', 'seq'), may hold values from -6 to 6
Outputs:
- outputs: bfloat16 [8, 1024, 2048], P('rows', 'seq')
- grad_inputs: float32 [8, 1024, 2048], P('rows', 'seq')
- grad_mix_gain: float32 [2048], P(('seq', 'rows'))
- grad_in_weight: float32 [2048, 2, 2560], P(('seq', 'rows'))
- grad_conv_weight: float32 [4, 2560], P(None, ('seq', 'rows'))
- grad_conv_bias: float32 [2560], P(('seq', 'rows'))
- grad_gate_weight: float32 [160, 2, 2560], P(None, None, ('seq', 'rows'))
- grad_gate_bias: float32 [2, 2560], P(None, ('seq', 'rows'))
- grad_decay_param: float32 [2560], P(('seq', 'rows'))
- grad_out_weight: float32 [2048, 2560], P(('seq', 'rows'))
- grad_mlp_gain: float32 [2048], P(('seq', 'rows'))
- grad_mlp_in: float32 [2048, 2, 6144], P(('seq', 'rows'))
- grad_down_weight: float32 [2048, 6144], P(('seq', 'rows'))
The draws below stay inside these ranges and needn't reach their ends.
Inputs may be any that keep to these rules, and one draw needn't show every extreme that they name: `segment_ids`: in each row the ids start at 0 and rise by 0 or 1 from one position to the next; in each aligned group of 2 rows one row holds a single document and another reaches the largest id.
All inputs are finite; a program needn't handle non-finite values.
Results may differ from the reference program's by a relative error of at most 0.011.
Values may be sent and summed in bfloat16 or wider, within the bound.
A program may use at most 896 MiB of HBM per device.

```python
import jax
import jax.numpy as jnp
from jax import lax

D = 2048
R = 2560
F = 6144
CONV = 4
MICRO = 2
DOC_LEN = 512
BW = 160
LEN = 1024
BATCH = 8


def draw_segment_ids(key, part):
    key = jax.random.fold_in(key, 11)
    first_key, second_key = jax.random.split(key)
    starts = (jax.random.randint(first_key, (BATCH, LEN), 0, DOC_LEN) == 0).astype(jnp.int32)
    position = jnp.arange(LEN)[None, :]
    starts = jnp.where(position > 0, starts, 0)
    groups = BATCH // MICRO
    doc_most = LEN // DOC_LEN
    spacing = LEN // doc_most
    chosen = jax.random.randint(second_key, (groups, 1), 0, MICRO)
    member = jnp.arange(MICRO)[None, :]
    row_pick = (member == chosen).reshape(BATCH, 1)
    full_pick = (member == (chosen + 1) % MICRO).reshape(BATCH, 1)
    regular = (position % spacing == 0) & (position > 0)
    starts = jnp.where(full_pick & regular, 1, starts)
    starts = jnp.where(row_pick, 0, starts)
    return jnp.minimum(jnp.cumsum(starts, axis=1), doc_most - 1).astype(jnp.int32)


def draw_decay_param(key, part):
    key = jax.random.fold_in(key, 5)
    spread = jax.random.uniform(key, (R,), jnp.float32)
    return 2.0 + 7.0 * spread


def block_levels(own_key, dims, cuts, smallest, top_value):
    loudness, own = 1.0, jax.random.fold_in(own_key, 6)
    for dim, shards_of in cuts:
        heights = jnp.exp(jax.random.uniform(jax.random.fold_in(own, dim), (shards_of,), jnp.float32, smallest / len(cuts), top_value / len(cuts)))
        loudness = loudness * jnp.repeat(heights, dims[dim] // shards_of).reshape([-1 if axis == dim else 1 for axis in range(len(dims))])
    return loudness


def normal_values(stream_key, dims, width, limit, cuts=(), held_as=jnp.bfloat16):
    level = block_levels(stream_key, dims, cuts, -0.22, 0.18) if cuts else 1.0
    values = jax.random.normal(stream_key, dims, jnp.float32) * width * level
    return jnp.minimum(jnp.maximum(values, -limit), limit).astype(held_as)


def setup_inputs(seed: int = 0) -> dict:
    key_list = jax.random.split(jax.random.key(seed), 15)
    return {
        "inputs": normal_values(key_list[0], (BATCH, LEN, D), 1.0, 6.0, ((0, 4), (1, 8))),
        "segment_ids": draw_segment_ids(jax.random.fold_in(key_list[14], 71), 0),
        "mix_gain": jnp.clip(1.0 + 0.15 * jax.random.normal(key_list[2], (D,), jnp.float32), 0.25, 1.75),
        "in_weight": normal_values(key_list[3], (D, 2, R), D ** -0.5, 0.125, ((2, 8),)),
        "conv_weight": normal_values(key_list[4], (CONV, R), CONV ** -0.5, 3.0, (), jnp.float32),
        "conv_bias": normal_values(key_list[5], (R,), 0.5, 3.0, (), jnp.float32),
        "gate_weight": normal_values(key_list[6], (BW, 2, R), BW ** -0.5, 0.5),
        "gate_bias": normal_values(key_list[7], (2, R), 0.5, 3.0, (), jnp.float32),
        "decay_param": draw_decay_param(jax.random.fold_in(key_list[14], 71), 0),
        "out_weight": normal_values(key_list[9], (D, R), (R // 8) ** -0.5, 0.3125, ((1, 8),)),
        "mlp_gain": jnp.clip(1.0 + 0.15 * jax.random.normal(key_list[10], (D,), jnp.float32), 0.25, 1.75),
        "mlp_in": normal_values(key_list[11], (D, 2, F), D ** -0.5, 0.125, ((2, 8),)),
        "down_weight": normal_values(key_list[12], (D, F), (F // 2) ** -0.5, 0.109375, ((1, 8),)),
        "cotangent": normal_values(key_list[13], (BATCH, LEN, D), 1.0, 6.0, ((0, 4), (1, 8))),
    }


EPS = 1e-06
HIGH = lax.Precision.HIGHEST

@jax.custom_vjp
def low(v):
    return lax.optimization_barrier(v.astype(jnp.bfloat16)).astype(jnp.float32)

@jax.custom_vjp
def low_back(v):
    return v

def low_keep(v):
    return (low(v), None)

def low_pass(kept, grad):
    return (grad,)

def back_keep(v):
    return (v, None)

def back_low(kept, grad):
    return (low(grad),)
low.defvjp(low_keep, low_pass)
low_back.defvjp(back_keep, back_low)

def rms_norm(values, scale_vec):
    return values * lax.rsqrt(lax.optimization_barrier(jnp.mean(values * values, axis=-1, keepdims=True)) + EPS) * scale_vec

def gelu(values):
    return jax.nn.gelu(values, approximate=True)

def pair_combine(earlier, later_pair):
    return (earlier[0] * later_pair[0], later_pair[0] * earlier[1] + later_pair[1])

def recurrence_inputs(conv_vals, gate_logits, decay_param, reset_flags):
    recur_gate = jax.nn.sigmoid(gate_logits[..., 0, :])
    input_gate = jax.nn.sigmoid(gate_logits[..., 1, :])
    log_decay = -8.0 * jax.nn.softplus(-decay_param) * recur_gate
    carry_mask = 1.0 - reset_flags
    decays = jnp.exp(log_decay) * carry_mask
    normalizer = reset_flags + carry_mask * jnp.sqrt(-jnp.expm1(2.0 * log_decay))
    return (decays, normalizer * input_gate * conv_vals)

def block_forward(params, row_in, row_segs):
    mix_gain, in_weight, conv_weight, conv_bias, gate_weight, gate_bias, decay_param, out_weight, mlp_gain, mlp_in, down_weight = params
    length = row_in.shape[0]
    conv_taps = conv_weight.shape[0]
    recur_width = conv_weight.shape[1]
    block_width = gate_weight.shape[0]
    block_count = recur_width // block_width
    normed = low(rms_norm(row_in, mix_gain))
    branches = low_back(jnp.einsum('td,dkr->tkr', normed, in_weight, precision=HIGH))
    gate_branch = branches[:, 0]
    recur_in = low(branches[:, 1])
    shifted_segs = jnp.concatenate([jnp.full((conv_taps - 1,), -1, jnp.int32), row_segs.astype(jnp.int32)])
    padded = jnp.concatenate([jnp.zeros((conv_taps - 1, recur_width), jnp.float32), recur_in], axis=0)
    conv_out = conv_bias
    for k in range(conv_taps):
        same_mask = (shifted_segs[conv_taps - 1 - k:conv_taps - 1 - k + length] == row_segs).astype(jnp.float32)
        conv_out = conv_out + conv_weight[k] * padded[conv_taps - 1 - k:conv_taps - 1 - k + length] * same_mask[:, None]
    reset_flags = (shifted_segs[conv_taps - 2:conv_taps - 2 + length] != row_segs).astype(jnp.float32)
    conv_low = low(conv_out)
    conv_blocks = conv_low.reshape(length, block_count, block_width)
    gate_blocks = gate_weight.reshape(block_width, 2, block_count, block_width)
    gate_prod = jnp.einsum('tnj,jknc->tknc', conv_blocks, gate_blocks, precision=HIGH)
    gate_logits = low_back(gate_prod).reshape(length, 2, recur_width) + gate_bias
    decays, driven = recurrence_inputs(conv_low, gate_logits, decay_param, reset_flags[:, None])
    states = lax.associative_scan(pair_combine, (decays, driven), axis=0)[1]
    states_low = low_back(low(states))
    mixed = low(gelu(gate_branch) * states_low)
    mix_out = low_back(jnp.einsum('tr,dr->td', mixed, out_weight, precision=HIGH))
    middle = row_in + mix_out
    normed_two = low(rms_norm(middle, mlp_gain))
    gate_up = low_back(jnp.einsum('td,dkf->tkf', normed_two, mlp_in, precision=HIGH))
    hidden = low(gelu(gate_up[:, 0]) * gate_up[:, 1])
    return middle + jnp.einsum('tf,df->td', hidden, down_weight, precision=HIGH)

def reference(inputs, segment_ids, mix_gain, in_weight, conv_weight, conv_bias, gate_weight, gate_bias, decay_param, out_weight, mlp_gain, mlp_in, down_weight, cotangent):
    params = tuple((p.astype(jnp.float32) for p in (mix_gain, in_weight, conv_weight, conv_bias, gate_weight, gate_bias, decay_param, out_weight, mlp_gain, mlp_in, down_weight)))

    def one_row(totals, row_data):
        row_in, row_segs, row_cot = row_data

        def forward(weights, values):
            return block_forward(weights, values, row_segs)
        result, pullback = jax.vjp(forward, params, row_in.astype(jnp.float32))
        grad_terms, grad_row = pullback(row_cot.astype(jnp.float32))
        totals = jax.tree.map(jnp.add, totals, grad_terms)
        return (totals, (result.astype(jnp.bfloat16), grad_row))
    zero_grads = jax.tree.map(jnp.zeros_like, params)
    totals, (outputs, grad_inputs) = lax.scan(one_row, zero_grads, (inputs, segment_ids, cotangent))
    return (outputs, grad_inputs, totals[0], totals[1], totals[2], totals[3], totals[4], totals[5], totals[6], totals[7], totals[8], totals[9], totals[10])
```

```python
import functools

import jax
import jax.numpy as jnp
from jax import lax
from jax.experimental import pallas as pl
from jax.experimental.pallas import tpu as pltpu
from jax.sharding import Mesh
from jax.sharding import PartitionSpec as P

EPS = 1e-06
MESH = pl.DeviceIdType.MESH
PLANE = ("i", "g", "c")
EVERY = ("t", "i", "g", "c")
F32 = jnp.float32
BF16 = jnp.bfloat16
GELU_A = 0.7978845608028654
GELU_B = 0.044715
HALO = 8
LANES = 128


def gelu_parts(x):
    square = x * x
    th = jnp.tanh(GELU_A * x * (1.0 + GELU_B * square))
    half = 0.5 * (1.0 + th)
    slope = half + 0.5 * x * (1.0 - th * th) * (GELU_A * (1.0 + 3.0 * GELU_B * square))
    return x * half, slope


def one_minus_exp(y):
    series = 1.0 + y * (-1.0 / 2 + y * (1.0 / 6 + y * (-1.0 / 24 + y * (1.0 / 120 + y * (-1.0 / 720 + y * (1.0 / 5040))))))
    return jnp.where(y < 0.35, y * series, 1.0 - jnp.exp(-y))


def sigmoid(x):
    return 1.0 / (1.0 + jnp.exp(-x))


def gate_values(conv_low, wg0, wg1, vec):
    logits0 = jnp.dot(conv_low, wg0, preferred_element_type=F32) + vec[5:6]
    logits1 = jnp.dot(conv_low, wg1, preferred_element_type=F32) + vec[6:7]
    recur_gate = sigmoid(logits0)
    input_gate = sigmoid(logits1)
    log_decay = -vec[7:8] * recur_gate
    return recur_gate, input_gate, log_decay


def greet(count):
    me = lax.axis_index("t")
    barrier = pltpu.get_barrier_semaphore()
    for step in range(1, count):
        pl.semaphore_signal(barrier, inc=1, device_id={"t": lax.rem(me + step, count)}, device_id_type=MESH)
    pl.semaphore_wait(barrier, count - 1)
    return me


def put_tiles(ref, at, values):
    tiles, lanes = ref.shape[0], ref.shape[2]
    short = tiles * lanes - values.shape[1]
    if short:
        values = jnp.concatenate([values, jnp.zeros((values.shape[0], short), values.dtype)], axis=1)
    for j in range(tiles):
        ref[j, at, :] = values[:, j * lanes : (j + 1) * lanes]


def get_tiles(ref, at, width):
    joined = jnp.concatenate([ref[j, at, :] for j in range(ref.shape[0])], axis=1)
    return joined[:, :width]


def join_tiles(parts, width):
    return jnp.concatenate(parts, axis=1)[:, :width]


def exchange(count, me, send, slots, send_sem, recv_sem):
    for step in range(1, count):
        pltpu.make_async_remote_copy(
            src_ref=send,
            dst_ref=slots.at[me],
            send_sem=send_sem.at[step],
            recv_sem=recv_sem.at[step],
            device_id={"t": lax.rem(me + step, count)},
            device_id_type=MESH,
        ).start()
    for step in range(1, count):
        other = lax.rem(me + count - step, count)
        pltpu.make_async_remote_copy(
            src_ref=send,
            dst_ref=slots.at[other],
            send_sem=send_sem.at[step],
            recv_sem=recv_sem.at[step],
            device_id={"t": other},
            device_id_type=MESH,
        ).wait()


def mixer_forward_kernel(
    count, seg, recur, gate, mask, wg0, wg1, vec_ref, conv_out, decay_out, states_out, mixed_out, halo_out, cin_out,
    drive, h_ref, a_ref, ext, halo_send, halo_recv, summary, slots, send_sem, recv_sem, halo_sems,
):
    me = greet(count)
    rows = 8
    for r in range(rows):
        halo_send[r * HALO : (r + 1) * HALO, :] = recur[
            (rows + r) * seg + seg - 16 : (rows + r) * seg + seg, :
        ].astype(F32)[16 - HALO :]
    halo_copy = pltpu.make_async_remote_copy(
        src_ref=halo_send,
        dst_ref=halo_recv,
        send_sem=halo_sems.at[0],
        recv_sem=halo_sems.at[1],
        device_id={"t": lax.rem(me + 1, count)},
        device_id_type=MESH,
    )
    halo_copy.start()
    halo_copy.wait()
    for r in range(rows):
        halo_out[r * HALO : (r + 1) * HALO, :] = halo_recv[r * HALO : (r + 1) * HALO, :]
        halo_out[(rows + r) * HALO : (rows + r + 1) * HALO, :] = recur[r * seg + seg - 16 : r * seg + seg, :].astype(F32)[
            16 - HALO :
        ]
    vec = vec_ref[...]

    def local(s, none):
        at = pl.ds(pl.multiple_of(s * seg, seg), seg)
        x = recur[at, :].astype(F32)
        ext[0:HALO, :] = halo_out[pl.ds(pl.multiple_of(s * HALO, HALO), HALO), :]
        ext[HALO : HALO + seg, :] = x
        m = mask[at, :]
        conv = vec[4:5] + vec[0:1] * x
        for k in range(1, 4):
            conv = conv + vec[k : k + 1] * ext[HALO - k : HALO - k + seg, :] * m[:, k - 1 : k]
        conv_low = conv.astype(BF16)
        conv_out[at, :] = conv_low
        recur_gate, input_gate, log_decay = gate_values(conv_low, wg0[...], wg1[...], vec)
        keep = m[:, 0:1]
        put_tiles(decay_out, at, jnp.exp(log_decay) * keep)
        scale = (1.0 - keep) + keep * jnp.sqrt(one_minus_exp(-2.0 * log_decay))
        put_tiles(drive, at, scale * input_gate * conv_low.astype(F32))
        return none

    lax.fori_loop(0, 2 * rows, local, 0)

    tiles, lanes = drive.shape[0], drive.shape[2]

    def scan(k, carried):
        at = pl.ds(k, 2 * rows, stride=seg)
        after = []
        for j in range(tiles):
            h, a = carried[j]
            d = decay_out[j, at, :]
            h = d * h + drive[j, at, :]
            a = a * d
            h_ref[j, at, :] = h
            a_ref[j, at, :] = a
            after.append((h, a))
        return tuple(after)

    width = recur.shape[1]
    start = (jnp.zeros((2 * rows, lanes), F32), jnp.ones((2 * rows, lanes), F32))
    last = lax.fori_loop(0, seg, scan, (start,) * tiles, unroll=4)
    last_h = join_tiles([part[0] for part in last], width)
    last_a = join_tiles([part[1] for part in last], width)
    summary[0:rows, :] = last_a[rows:] * last_a[:rows]
    summary[rows : 2 * rows, :] = last_a[rows:] * last_h[:rows] + last_h[rows:]
    exchange(count, me, summary, slots, send_sem, recv_sem)
    carry = jnp.zeros((rows, width), F32)
    for z in range(count - 1):
        carry = jnp.where(z < me, slots[z, 0:rows, :] * carry + slots[z, rows : 2 * rows, :], carry)
    cin_out[0:rows, :] = carry
    cin_out[rows : 2 * rows, :] = last_a[:rows] * carry + last_h[:rows]

    def finish(s, none):
        at = pl.ds(pl.multiple_of(s * seg, seg), seg)
        states = get_tiles(h_ref, at, width) + get_tiles(a_ref, at, width) * cin_out[pl.ds(s, 1), :]
        states_out[at, :] = states
        act, _ = gelu_parts(gate[at, :])
        mixed_out[at, :] = (act * states.astype(BF16).astype(F32)).astype(BF16)
        return none

    lax.fori_loop(0, 2 * rows, finish, 0)


def mixer_backward_kernel(
    count, seg, grad_mixed, gate, states, decay, conv_low_ref, recur, halo, cin, mask, wg0, wg1, wg0t, wg1t, vec_ref,
    grad_gate_out, grad_recur_out, gw0_out, gw1_out, small_out,
    tot, prod, gc, ext, halo_send, halo_recv, summary, slots, uin, send_sem, recv_sem, halo_sems,
):
    me = greet(count)
    rows = 8
    width = recur.shape[1]
    vec = vec_ref[...]

    def local(s, none):
        at = pl.ds(pl.multiple_of(s * seg, seg), seg)
        act, slope = gelu_parts(gate[at, :])
        gm = grad_mixed[at, :].astype(F32)
        grad_gate_out[at, :] = (gm * states[at, :].astype(BF16).astype(F32) * slope).astype(BF16)
        put_tiles(tot, at, (gm * act).astype(BF16).astype(F32))
        return none

    lax.fori_loop(0, 2 * rows, local, 0)

    tiles, lanes = tot.shape[0], tot.shape[2]

    def scan(k, carried):
        at = pl.ds(seg - 1 - k, 2 * rows, stride=seg)
        after = []
        for j in range(tiles):
            u, p = carried[j]
            d = decay[j, at, :]
            total = tot[j, at, :] + u
            tot[j, at, :] = total
            prod[j, at, :] = p
            after.append((d * total, d * p))
        return tuple(after)

    start = (jnp.zeros((2 * rows, lanes), F32), jnp.ones((2 * rows, lanes), F32))
    last = lax.fori_loop(0, seg, scan, (start,) * tiles, unroll=4)
    u = join_tiles([part[0] for part in last], width)
    p = join_tiles([part[1] for part in last], width)
    summary[0:rows, :] = p[:rows] * p[rows:]
    summary[rows : 2 * rows, :] = p[:rows] * u[rows:] + u[:rows]
    exchange(count, me, summary, slots, send_sem, recv_sem)
    carry = jnp.zeros((rows, width), F32)
    for z in range(count - 1, 0, -1):
        carry = jnp.where(z > me, slots[z, 0:rows, :] * carry + slots[z, rows : 2 * rows, :], carry)
    uin[rows : 2 * rows, :] = carry
    uin[0:rows, :] = p[rows:] * carry + u[rows:]
    gw0_out[...] = jnp.zeros_like(gw0_out)
    gw1_out[...] = jnp.zeros_like(gw1_out)
    small_out[...] = jnp.zeros_like(small_out)

    def gates(s, none):
        at = pl.ds(pl.multiple_of(s * seg, seg), seg)
        total = get_tiles(tot, at, width) + get_tiles(prod, at, width) * uin[pl.ds(s, 1), :]
        ext[HALO - 1 : HALO, :] = cin[pl.ds(s, 1), :]
        ext[HALO : HALO + seg, :] = states[at, :]
        before = ext[HALO - 1 : HALO - 1 + seg, :]
        conv_low = conv_low_ref[at, :]
        conv_vals = conv_low.astype(F32)
        m = mask[at, :]
        keep = m[:, 0:1]
        recur_gate, input_gate, log_decay = gate_values(conv_low, wg0[...], wg1[...], vec)
        root = jnp.sqrt(one_minus_exp(-2.0 * log_decay))
        scale = (1.0 - keep) + keep * root
        driven_in = total * conv_vals
        grad_log = total * before * get_tiles(decay, at, width) - driven_in * input_gate * keep * (jnp.exp(2.0 * log_decay) / root)
        grad0 = grad_log * log_decay * (1.0 - recur_gate)
        grad1 = driven_in * scale * input_gate * (1.0 - input_gate)
        low0 = grad0.astype(BF16)
        low1 = grad1.astype(BF16)
        grad_conv = (
            total * scale * input_gate
            + jnp.dot(low0, wg0t[...], preferred_element_type=F32)
            + jnp.dot(low1, wg1t[...], preferred_element_type=F32)
        )
        gc[at, :] = grad_conv
        turned = (((0,), (0,)), ((), ()))
        gw0_out[...] += lax.dot_general(conv_low, low0, turned, preferred_element_type=F32)
        gw1_out[...] += lax.dot_general(conv_low, low1, turned, preferred_element_type=F32)
        x = recur[at, :].astype(F32)
        ext[0:HALO, :] = halo[pl.ds(pl.multiple_of(s * HALO, HALO), HALO), :]
        ext[HALO : HALO + seg, :] = x

        def add(row, values):
            small_out[row : row + 1, :] += jnp.sum(values, axis=0, keepdims=True)

        add(0, grad_conv * x)
        for k in range(1, 4):
            add(k, grad_conv * ext[HALO - k : HALO - k + seg, :] * m[:, k - 1 : k])
        add(4, grad_conv)
        add(5, grad0)
        add(6, grad1)
        add(7, grad_log * recur_gate)
        return none

    lax.fori_loop(0, 2 * rows, gates, 0)
    small_out[7:8, :] = small_out[7:8, :] * vec[8:9]
    for r in range(rows):
        halo_send[r * HALO : (r + 1) * HALO, :] = gc[r * seg : r * seg + HALO, :]
    halo_copy = pltpu.make_async_remote_copy(
        src_ref=halo_send,
        dst_ref=halo_recv,
        send_sem=halo_sems.at[0],
        recv_sem=halo_sems.at[1],
        device_id={"t": lax.rem(me + count - 1, count)},
        device_id_type=MESH,
    )
    halo_copy.start()
    halo_copy.wait()

    def back(s, none):
        at = pl.ds(pl.multiple_of(s * seg, seg), seg)
        m = mask[at, :]
        ext[0:seg, :] = gc[at, :]
        result = vec[0:1] * gc[at, :]

        @pl.when(s < rows)
        def _():
            ext[seg : seg + HALO, :] = gc[pl.ds(pl.multiple_of((s + rows) * seg, seg), HALO), :]

        @pl.when(s >= rows)
        def _():
            ext[seg : seg + HALO, :] = halo_recv[pl.ds(pl.multiple_of((s - rows) * HALO, HALO), HALO), :]

        for k in range(1, 4):
            result = result + vec[k : k + 1] * ext[k : k + seg, :] * m[:, 2 + k : 3 + k]
        grad_recur_out[at, :] = result.astype(BF16)
        return none

    lax.fori_loop(0, 2 * rows, back, 0)


def whole(count):
    return [pl.BlockSpec(memory_space=pltpu.VMEM)] * count


def mixer_params(number):
    return pltpu.CompilerParams(collective_id=number, has_side_effects=True, vmem_limit_bytes=60 * 1024 * 1024)


def mixer_forward(count, seg, recur, gate, mask, wg0, wg1, vec):
    n, width = recur.shape
    full = functools.partial(jax.ShapeDtypeStruct, (n, width))
    tiles = -(-width // LANES)
    tiled = jax.ShapeDtypeStruct((tiles, n, LANES), F32)
    return pl.pallas_call(
        functools.partial(mixer_forward_kernel, count, seg),
        name="mixer_forward",
        out_shape=(
            full(BF16), tiled, full(F32), full(BF16),
            jax.ShapeDtypeStruct((16 * HALO, width), F32), jax.ShapeDtypeStruct((16, width), F32),
        ),
        in_specs=whole(6),
        out_specs=tuple(whole(6)),
        scratch_shapes=[
            pltpu.VMEM((tiles, n, LANES), F32),
            pltpu.VMEM((tiles, n, LANES), F32),
            pltpu.VMEM((tiles, n, LANES), F32),
            pltpu.VMEM((seg + HALO, width), F32),
            pltpu.VMEM((8 * HALO, width), F32),
            pltpu.VMEM((8 * HALO, width), F32),
            pltpu.VMEM((16, width), F32),
            pltpu.VMEM((count, 16, width), F32),
            pltpu.SemaphoreType.DMA((count,)),
            pltpu.SemaphoreType.DMA((count,)),
            pltpu.SemaphoreType.DMA((2,)),
        ],
        compiler_params=mixer_params(1),
    )(recur, gate, mask, wg0, wg1, vec)


def mixer_backward(count, seg, grad_mixed, gate, states, decay, conv_low, recur, halo, cin, mask, wg0, wg1, wg0t, wg1t, vec):
    n, width = recur.shape
    full = functools.partial(jax.ShapeDtypeStruct, (n, width))
    tiles = -(-width // LANES)
    tiled = jax.ShapeDtypeStruct((tiles, n, LANES), F32)
    return pl.pallas_call(
        functools.partial(mixer_backward_kernel, count, seg),
        name="mixer_backward",
        out_shape=(
            full(BF16), full(BF16),
            jax.ShapeDtypeStruct((width, width), F32), jax.ShapeDtypeStruct((width, width), F32),
            jax.ShapeDtypeStruct((8, width), F32),
        ),
        in_specs=whole(14),
        out_specs=tuple(whole(5)),
        scratch_shapes=[
            pltpu.VMEM((tiles, n, LANES), F32),
            pltpu.VMEM((tiles, n, LANES), F32),
            pltpu.VMEM((n, width), F32),
            pltpu.VMEM((seg + HALO, width), F32),
            pltpu.VMEM((8 * HALO, width), F32),
            pltpu.VMEM((8 * HALO, width), F32),
            pltpu.VMEM((16, width), F32),
            pltpu.VMEM((count, 16, width), F32),
            pltpu.VMEM((16, width), F32),
            pltpu.SemaphoreType.DMA((count,)),
            pltpu.SemaphoreType.DMA((count,)),
            pltpu.SemaphoreType.DMA((2,)),
        ],
        compiler_params=mixer_params(2),
    )(grad_mixed, gate, states, decay, conv_low, recur, halo, cin, mask, wg0, wg1, wg0t, wg1t, vec)


def gather_tokens(block):
    return lax.all_gather(block, PLANE, axis=0, tiled=True)


def scatter_tokens(partial):
    return lax.psum_scatter(partial, PLANE, scatter_dimension=0, tiled=True)


def rms(values):
    return lax.rsqrt(jnp.mean(values * values, axis=-1, keepdims=True) + EPS)


def rms_back(values, scale, gain, grad):
    weighted = grad * gain
    inner = jnp.mean(values * weighted, axis=-1, keepdims=True)
    return scale * weighted - values * (scale * scale * scale * inner), jnp.sum(grad * values * scale, axis=0)


def nt(left, right, out):
    return lax.dot_general(left, right, (((1,), (1,)), ((), ())), preferred_element_type=F32).astype(out)


def tn(left, right, out):
    return lax.dot_general(left, right, (((0,), (0,)), ((), ())), preferred_element_type=F32).astype(out)


def nn(left, right, out):
    return jnp.dot(left, right, preferred_element_type=F32).astype(out)


def per_device(
    inputs, segment_ids, mix_gain, in_weight, conv_weight, conv_bias, gate_weight, gate_bias, decay_param, out_weight,
    mlp_gain, mlp_in, down_weight, cotangent,
):
    planes = lax.axis_size("t")
    rows_here, seg, width = inputs.shape
    row_groups = lax.axis_size("g") * lax.axis_size("c")
    own_tokens = rows_here * seg
    recur_width = conv_weight.shape[1]
    block_width = gate_weight.shape[0]
    members = 2 * row_groups
    channels = recur_width // members
    t, i = lax.axis_index("t"), lax.axis_index("i")
    r = lax.axis_index("g") * lax.axis_size("c") + lax.axis_index("c")
    member = 2 * r + i
    first = member * channels

    def member_columns(weight):
        if planes == row_groups:
            part = weight.shape[0] // row_groups
            quarter = lax.dynamic_slice_in_dim(weight, r * part, part, 0)
            quarters = lax.all_gather(quarter, "t", axis=0, tiled=False)
            return lax.all_to_all(quarters, ("g", "c"), 0, 0, tiled=True).reshape(weight.shape)
        every = lax.all_gather(weight, ("t", "i"), axis=1, tiled=True)
        return lax.dynamic_slice_in_dim(every, first, channels, 1)

    in_gate = in_weight[:, 0]
    in_recur = in_weight[:, 1]
    mixer_w = member_columns(jnp.concatenate([in_gate, in_recur, out_weight], axis=0))
    w_gate, w_recur, w_out = mixer_w[:width], mixer_w[width : 2 * width], mixer_w[2 * width :]
    hidden_part = mlp_in.shape[2] // row_groups

    def own_part(weight):
        return lax.dynamic_slice_in_dim(weight.T, r * hidden_part, hidden_part, 0)

    mlp_w = jnp.concatenate([own_part(mlp_in[:, 0]), own_part(mlp_in[:, 1]), own_part(down_weight)], axis=0)
    mlp_w = lax.all_gather(mlp_w, "t", axis=0, tiled=False)
    mlp_w = mlp_w.reshape(planes, 3, hidden_part, width)
    w_left = mlp_w[:, 0].reshape(-1, width)
    w_right = mlp_w[:, 1].reshape(-1, width)
    w_down = mlp_w[:, 2].reshape(-1, width)

    ids = lax.all_gather((segment_ids + 1).astype(F32), ("g", "c"), axis=0, tiled=True)
    ids = lax.all_gather(ids, ("t", "i"), axis=1, tiled=True)
    span = 2 * seg
    ids = jnp.pad(ids, ((0, 0), (HALO, HALO)))
    ids = lax.dynamic_slice_in_dim(ids, t * span, span + 2 * HALO, 1)
    here = ids[:, HALO : HALO + span]
    columns = [(ids[:, HALO - k : HALO - k + span] == here) for k in (1, 2, 3)]
    columns += [(ids[:, HALO + k : HALO + k + span] == here) for k in (1, 2, 3)]
    columns += [jnp.zeros_like(columns[0])] * 2
    mask = jnp.stack(columns, axis=-1).astype(F32)
    mask = mask.reshape(mask.shape[0], 2, seg, 8).transpose(1, 0, 2, 3).reshape(-1, 8)

    def own(values):
        return lax.dynamic_slice_in_dim(values, first, channels, values.ndim - 1)

    decay_own = own(decay_param)
    vec = jnp.concatenate(
        [
            own(conv_weight),
            own(conv_bias)[None],
            own(gate_bias),
            8.0 * jax.nn.softplus(-decay_own)[None],
            8.0 * jax.nn.sigmoid(-decay_own)[None],
            jnp.zeros((7, channels), F32),
        ]
    )
    blocks = channels // block_width
    gate_own = own(gate_weight).reshape(block_width, 2, blocks, block_width)
    spread = jnp.zeros((2, blocks, block_width, blocks, block_width), BF16)
    for n in range(blocks):
        spread = spread.at[:, n, :, n, :].set(gate_own[:, :, n, :].transpose(1, 0, 2))
    spread = spread.reshape(2, channels, channels)
    wg0, wg1 = spread[0], spread[1]

    flat_in = inputs.reshape(own_tokens, width).astype(F32)
    scale_in = rms(flat_in)
    normed = gather_tokens((flat_in * scale_in * mix_gain).astype(BF16))
    cot_own = cotangent.reshape(own_tokens, width)
    cot = gather_tokens(cot_own)
    gate_branch = nn(normed, w_gate, F32)
    recur = nn(normed, w_recur, BF16)
    conv_low, decay, states, mixed, halo, cin = mixer_forward(planes, seg, recur, gate_branch, mask, wg0, wg1, vec)
    middle = flat_in + scatter_tokens(nt(mixed, w_out, BF16)).astype(F32)
    scale_mid = rms(middle)
    normed_two = gather_tokens((middle * scale_mid * mlp_gain).astype(BF16))
    left = nt(normed_two, w_left, F32)
    right = nt(normed_two, w_right, F32)
    act, slope = gelu_parts(left)
    hidden = (act * right).astype(BF16)
    down = scatter_tokens(nn(hidden, w_down, BF16))
    outputs = (middle + down.astype(F32)).astype(BF16).reshape(inputs.shape)

    grad_hidden = nt(cot, w_down, F32)
    grad_left = (grad_hidden * right * slope).astype(BF16)
    grad_right = (grad_hidden * act).astype(BF16)
    partial = lax.dot(grad_left, w_left, preferred_element_type=F32) + lax.dot(
        grad_right, w_right, preferred_element_type=F32
    )
    grad_normed_two = scatter_tokens(partial.astype(BF16)).astype(F32)
    grad_mid_norm, grad_mlp_gain = rms_back(middle, scale_mid, mlp_gain, grad_normed_two)
    grad_middle = cot_own.astype(F32) + grad_mid_norm
    grad_mid = gather_tokens(grad_middle.astype(BF16))
    grad_mixed = nn(grad_mid, w_out, F32)
    grad_gate, grad_recur, gw0, gw1, small = mixer_backward(
        planes, seg, grad_mixed, gate_branch, states, decay, conv_low, recur, halo, cin, mask, wg0, wg1, wg0.T, wg1.T, vec
    )
    partial = lax.dot_general(grad_gate, w_gate, (((1,), (1,)), ((), ())), preferred_element_type=F32) + lax.dot_general(
        grad_recur, w_recur, (((1,), (1,)), ((), ())), preferred_element_type=F32
    )
    grad_normed = scatter_tokens(partial.astype(BF16)).astype(F32)
    grad_in_norm, grad_mix_gain = rms_back(flat_in, scale_in, mix_gain, grad_normed)
    grad_inputs = (grad_middle + grad_in_norm).reshape(inputs.shape)

    def to_owners(grad):
        reduced = lax.psum_scatter(grad, "t", scatter_dimension=0, tiled=True)
        return lax.all_to_all(reduced.reshape(members, -1, grad.shape[1]), PLANE, 0, 0, tiled=True)

    own_rows = width // (planes * members)
    mlp_grads = to_owners(
        jnp.concatenate([tn(normed_two, grad_left, BF16), tn(normed_two, grad_right, BF16), tn(cot, hidden, BF16)], axis=1)
    )
    mixer_grads = to_owners(
        jnp.concatenate([tn(normed, grad_gate, BF16), tn(normed, grad_recur, BF16), tn(grad_mid, mixed, BF16)], axis=1)
    )
    mlp_grads = mlp_grads.reshape(2, row_groups, own_rows, 3, planes, hidden_part).astype(F32)
    mlp_grads = mlp_grads.transpose(2, 3, 4, 0, 1, 5).reshape(own_rows, 3, -1)
    mixer_grads = mixer_grads.reshape(2, row_groups, own_rows, 3, channels).astype(F32)
    mixer_grads = mixer_grads.transpose(2, 3, 1, 0, 4).reshape(own_rows, 3, -1)

    column_block = lax.broadcasted_iota(jnp.int32, (block_width, channels), 1) // block_width

    def diagonal(gw):
        return sum(
            jnp.where(column_block == n, gw[n * block_width : (n + 1) * block_width], 0.0) for n in range(blocks)
        )

    gate_grads = jnp.concatenate([diagonal(gw0), diagonal(gw1), small], axis=0)
    if planes == row_groups:
        pieces = gate_grads.reshape(gate_grads.shape[0], row_groups, -1).transpose(1, 0, 2)
        pieces = lax.all_to_all(pieces, ("g", "c"), 0, 0, tiled=True)
        gate_grads = lax.psum_scatter(pieces, "t", scatter_dimension=0, tiled=False)
    else:
        placed = jnp.zeros((gate_grads.shape[0], recur_width), F32)
        placed = lax.dynamic_update_slice_in_dim(placed, gate_grads, first, 1)
        gate_grads = lax.psum_scatter(placed, EVERY, scatter_dimension=1, tiled=True)
    grad_gate_weight = jnp.stack([gate_grads[:block_width], gate_grads[block_width : 2 * block_width]], axis=1)
    small = gate_grads[2 * block_width :]
    return (
        outputs,
        grad_inputs,
        lax.psum_scatter(grad_mix_gain, EVERY, scatter_dimension=0, tiled=True),
        mixer_grads[:, :2],
        small[0:4],
        small[4],
        grad_gate_weight,
        small[5:7],
        small[7],
        mixer_grads[:, 2],
        lax.psum_scatter(grad_mlp_gain, EVERY, scatter_dimension=0, tiled=True),
        mlp_grads[:, :2],
        mlp_grads[:, 2],
    )


def solution(mesh):
    seq, rows = mesh.shape["seq"], mesh.shape["rows"]
    grid = Mesh(mesh.devices.reshape(seq // 2, 2, rows // 2, 2), EVERY)
    row_axes, seq_axes = ("g", "c"), ("t", "i")
    tokens = P(row_axes, seq_axes, None)
    return jax.shard_map(
        per_device,
        mesh=grid,
        in_specs=(
            tokens,
            P(row_axes, seq_axes),
            P(),
            P(None, None, seq_axes),
            P(),
            P(),
            P(),
            P(),
            P(),
            P(None, seq_axes),
            P(),
            P(None, None, seq_axes),
            P(None, seq_axes),
            tokens,
        ),
        out_specs=(
            tokens,
            tokens,
            P(EVERY),
            P(EVERY, None, None),
            P(None, EVERY),
            P(EVERY),
            P(None, None, EVERY),
            P(None, EVERY),
            P(EVERY),
            P(EVERY, None),
            P(EVERY),
            P(EVERY, None, None),
            P(EVERY, None),
        ),
        check_vma=False,
    )
```

```python
import functools

import jax
import jax.numpy as jnp
from jax import lax
from jax.experimental import pallas as pl
from jax.experimental.pallas import tpu as pltpu
from jax.sharding import Mesh
from jax.sharding import PartitionSpec as P

EPS = 1e-06
MESH = pl.DeviceIdType.MESH
PLANE = ("i", "g", "c")
EVERY = ("t", "i", "g", "c")
F32 = jnp.float32
BF16 = jnp.bfloat16
GELU_A = 0.7978845608028654
GELU_B = 0.044715
HALO = 8
LANES = 128


def gelu_parts(x):
    square = x * x
    th = jnp.tanh(GELU_A * x * (1.0 + GELU_B * square))
    half = 0.5 * (1.0 + th)
    slope = half + 0.5 * x * (1.0 - th * th) * (GELU_A * (1.0 + 3.0 * GELU_B * square))
    return x * half, slope


def one_minus_exp(y):
    series = 1.0 + y * (-1.0 / 2 + y * (1.0 / 6 + y * (-1.0 / 24 + y * (1.0 / 120 + y * (-1.0 / 720 + y * (1.0 / 5040))))))
    return jnp.where(y < 0.35, y * series, 1.0 - jnp.exp(-y))


def sigmoid(x):
    return 1.0 / (1.0 + jnp.exp(-x))


def gate_values(conv_low, wg0, wg1, vec):
    logits0 = jnp.dot(conv_low, wg0, preferred_element_type=F32) + vec[5:6]
    logits1 = jnp.dot(conv_low, wg1, preferred_element_type=F32) + vec[6:7]
    recur_gate = sigmoid(logits0)
    input_gate = sigmoid(logits1)
    log_decay = -vec[7:8] * recur_gate
    return recur_gate, input_gate, log_decay


def greet(count):
    me = lax.axis_index("t")
    barrier = pltpu.get_barrier_semaphore()
    for step in range(1, count):
        pl.semaphore_signal(barrier, inc=1, device_id={"t": lax.rem(me + step, count)}, device_id_type=MESH)
    pl.semaphore_wait(barrier, count - 1)
    return me


def put_tiles(ref, at, values):
    tiles, lanes = ref.shape[0], ref.shape[2]
    short = tiles * lanes - values.shape[1]
    if short:
        values = jnp.concatenate([values, jnp.zeros((values.shape[0], short), values.dtype)], axis=1)
    for j in range(tiles):
        ref[j, at, :] = values[:, j * lanes : (j + 1) * lanes]


def get_tiles(ref, at, width):
    joined = jnp.concatenate([ref[j, at, :] for j in range(ref.shape[0])], axis=1)
    return joined[:, :width]


def join_tiles(parts, width):
    return jnp.concatenate(parts, axis=1)[:, :width]


def exchange(count, me, send, slots, send_sem, recv_sem):
    for step in range(1, count):
        pltpu.make_async_remote_copy(
            src_ref=send,
            dst_ref=slots.at[me],
            send_sem=send_sem.at[step],
            recv_sem=recv_sem.at[step],
            device_id={"t": lax.rem(me + step, count)},
            device_id_type=MESH,
        ).start()
    for step in range(1, count):
        other = lax.rem(me + count - step, count)
        pltpu.make_async_remote_copy(
            src_ref=send,
            dst_ref=slots.at[other],
            send_sem=send_sem.at[step],
            recv_sem=recv_sem.at[step],
            device_id={"t": other},
            device_id_type=MESH,
        ).wait()


def mixer_forward_kernel(
    count, seg, recur, gate, mask, wg0, wg1, vec_ref, conv_out, decay_out, states_out, mixed_out, halo_out, cin_out,
    drive, h_ref, a_ref, ext, halo_send, halo_recv, summary, slots, send_sem, recv_sem, halo_sems,
):
    me = greet(count)
    rows = 8
    for r in range(rows):
        halo_send[r * HALO : (r + 1) * HALO, :] = recur[
            (rows + r) * seg + seg - 16 : (rows + r) * seg + seg, :
        ].astype(F32)[16 - HALO :]
    halo_copy = pltpu.make_async_remote_copy(
        src_ref=halo_send,
        dst_ref=halo_recv,
        send_sem=halo_sems.at[0],
        recv_sem=halo_sems.at[1],
        device_id={"t": lax.rem(me + 1, count)},
        device_id_type=MESH,
    )
    halo_copy.start()
    halo_copy.wait()
    for r in range(rows):
        halo_out[r * HALO : (r + 1) * HALO, :] = halo_recv[r * HALO : (r + 1) * HALO, :]
        halo_out[(rows + r) * HALO : (rows + r + 1) * HALO, :] = recur[r * seg + seg - 16 : r * seg + seg, :].astype(F32)[
            16 - HALO :
        ]
    vec = vec_ref[...]

    def local(s, none):
        at = pl.ds(pl.multiple_of(s * seg, seg), seg)
        x = recur[at, :].astype(F32)
        ext[0:HALO, :] = halo_out[pl.ds(pl.multiple_of(s * HALO, HALO), HALO), :]
        ext[HALO : HALO + seg, :] = x
        m = mask[at, :]
        conv = vec[4:5] + vec[0:1] * x
        for k in range(1, 4):
            conv = conv + vec[k : k + 1] * ext[HALO - k : HALO - k + seg, :] * m[:, k - 1 : k]
        conv_low = conv.astype(BF16)
        conv_out[at, :] = conv_low
        recur_gate, input_gate, log_decay = gate_values(conv_low, wg0[...], wg1[...], vec)
        keep = m[:, 0:1]
        put_tiles(decay_out, at, jnp.exp(log_decay) * keep)
        scale = (1.0 - keep) + keep * jnp.sqrt(one_minus_exp(-2.0 * log_decay))
        put_tiles(drive, at, scale * input_gate * conv_low.astype(F32))
        return none

    lax.fori_loop(0, 2 * rows, local, 0)

    tiles, lanes = drive.shape[0], drive.shape[2]

    def scan(k, carried):
        at = pl.ds(k, 2 * rows, stride=seg)
        after = []
        for j in range(tiles):
            h, a = carried[j]
            d = decay_out[j, at, :]
            h = d * h + drive[j, at, :]
            a = a * d
            h_ref[j, at, :] = h
            a_ref[j, at, :] = a
            after.append((h, a))
        return tuple(after)

    width = recur.shape[1]
    start = (jnp.zeros((2 * rows, lanes), F32), jnp.ones((2 * rows, lanes), F32))
    last = lax.fori_loop(0, seg, scan, (start,) * tiles, unroll=4)
    last_h = join_tiles([part[0] for part in last], width)
    last_a = join_tiles([part[1] for part in last], width)
    summary[0:rows, :] = last_a[rows:] * last_a[:rows]
    summary[rows : 2 * rows, :] = last_a[rows:] * last_h[:rows] + last_h[rows:]
    exchange(count, me, summary, slots, send_sem, recv_sem)
    carry = jnp.zeros((rows, width), F32)
    for z in range(count - 1):
        carry = jnp.where(z < me, slots[z, 0:rows, :] * carry + slots[z, rows : 2 * rows, :], carry)
    cin_out[0:rows, :] = carry
    cin_out[rows : 2 * rows, :] = last_a[:rows] * carry + last_h[:rows]

    def finish(s, none):
        at = pl.ds(pl.multiple_of(s * seg, seg), seg)
        states = get_tiles(h_ref, at, width) + get_tiles(a_ref, at, width) * cin_out[pl.ds(s, 1), :]
        states_out[at, :] = states
        act, _ = gelu_parts(gate[at, :])
        mixed_out[at, :] = (act * states.astype(BF16).astype(F32)).astype(BF16)
        return none

    lax.fori_loop(0, 2 * rows, finish, 0)


def mixer_backward_kernel(
    count, seg, grad_mixed, gate, states, decay, conv_low_ref, recur, halo, cin, mask, wg0, wg1, wg0t, wg1t, vec_ref,
    grad_gate_out, grad_recur_out, gw0_out, gw1_out, small_out,
    tot, prod, gc, ext, halo_send, halo_recv, summary, slots, uin, send_sem, recv_sem, halo_sems,
):
    me = greet(count)
    rows = 8
    width = recur.shape[1]
    vec = vec_ref[...]

    def local(s, none):
        at = pl.ds(pl.multiple_of(s * seg, seg), seg)
        act, slope = gelu_parts(gate[at, :])
        gm = grad_mixed[at, :].astype(F32)
        grad_gate_out[at, :] = (gm * states[at, :].astype(BF16).astype(F32) * slope).astype(BF16)
        put_tiles(tot, at, (gm * act).astype(BF16).astype(F32))
        return none

    lax.fori_loop(0, 2 * rows, local, 0)

    tiles, lanes = tot.shape[0], tot.shape[2]

    def scan(k, carried):
        at = pl.ds(seg - 1 - k, 2 * rows, stride=seg)
        after = []
        for j in range(tiles):
            u, p = carried[j]
            d = decay[j, at, :]
            total = tot[j, at, :] + u
            tot[j, at, :] = total
            prod[j, at, :] = p
            after.append((d * total, d * p))
        return tuple(after)

    start = (jnp.zeros((2 * rows, lanes), F32), jnp.ones((2 * rows, lanes), F32))
    last = lax.fori_loop(0, seg, scan, (start,) * tiles, unroll=4)
    u = join_tiles([part[0] for part in last], width)
    p = join_tiles([part[1] for part in last], width)
    summary[0:rows, :] = p[:rows] * p[rows:]
    summary[rows : 2 * rows, :] = p[:rows] * u[rows:] + u[:rows]
    exchange(count, me, summary, slots, send_sem, recv_sem)
    carry = jnp.zeros((rows, width), F32)
    for z in range(count - 1, 0, -1):
        carry = jnp.where(z > me, slots[z, 0:rows, :] * carry + slots[z, rows : 2 * rows, :], carry)
    uin[rows : 2 * rows, :] = carry
    uin[0:rows, :] = p[rows:] * carry + u[rows:]
    gw0_out[...] = jnp.zeros_like(gw0_out)
    gw1_out[...] = jnp.zeros_like(gw1_out)
    small_out[...] = jnp.zeros_like(small_out)

    def gates(s, none):
        at = pl.ds(pl.multiple_of(s * seg, seg), seg)
        total = get_tiles(tot, at, width) + get_tiles(prod, at, width) * uin[pl.ds(s, 1), :]
        ext[HALO - 1 : HALO, :] = cin[pl.ds(s, 1), :]
        ext[HALO : HALO + seg, :] = states[at, :]
        before = ext[HALO - 1 : HALO - 1 + seg, :]
        conv_low = conv_low_ref[at, :]
        conv_vals = conv_low.astype(F32)
        m = mask[at, :]
        keep = m[:, 0:1]
        recur_gate, input_gate, log_decay = gate_values(conv_low, wg0[...], wg1[...], vec)
        root = jnp.sqrt(one_minus_exp(-2.0 * log_decay))
        scale = (1.0 - keep) + keep * root
        driven_in = total * conv_vals
        grad_log = total * before * get_tiles(decay, at, width) - driven_in * input_gate * keep * (jnp.exp(2.0 * log_decay) / root)
        grad0 = grad_log * log_decay * (1.0 - recur_gate)
        grad1 = driven_in * scale * input_gate * (1.0 - input_gate)
        low0 = grad0.astype(BF16)
        low1 = grad1.astype(BF16)
        grad_conv = (
            total * scale * input_gate
            + jnp.dot(low0, wg0t[...], preferred_element_type=F32)
            + jnp.dot(low1, wg1t[...], preferred_element_type=F32)
        )
        gc[at, :] = grad_conv
        turned = (((0,), (0,)), ((), ()))
        gw0_out[...] += lax.dot_general(conv_low, low0, turned, preferred_element_type=F32)
        gw1_out[...] += lax.dot_general(conv_low, low1, turned, preferred_element_type=F32)
        x = recur[at, :].astype(F32)
        ext[0:HALO, :] = halo[pl.ds(pl.multiple_of(s * HALO, HALO), HALO), :]
        ext[HALO : HALO + seg, :] = x

        def add(row, values):
            small_out[row : row + 1, :] += jnp.sum(values, axis=0, keepdims=True)

        add(0, grad_conv * x)
        for k in range(1, 4):
            add(k, grad_conv * ext[HALO - k : HALO - k + seg, :] * m[:, k - 1 : k])
        add(4, grad_conv)
        add(5, grad0)
        add(6, grad1)
        add(7, grad_log * recur_gate)
        return none

    lax.fori_loop(0, 2 * rows, gates, 0)
    small_out[7:8, :] = small_out[7:8, :] * vec[8:9]
    for r in range(rows):
        halo_send[r * HALO : (r + 1) * HALO, :] = gc[r * seg : r * seg + HALO, :]
    halo_copy = pltpu.make_async_remote_copy(
        src_ref=halo_send,
        dst_ref=halo_recv,
        send_sem=halo_sems.at[0],
        recv_sem=halo_sems.at[1],
        device_id={"t": lax.rem(me + count - 1, count)},
        device_id_type=MESH,
    )
    halo_copy.start()
    halo_copy.wait()

    def back(s, none):
        at = pl.ds(pl.multiple_of(s * seg, seg), seg)
        m = mask[at, :]
        ext[0:seg, :] = gc[at, :]
        result = vec[0:1] * gc[at, :]

        @pl.when(s < rows)
        def _():
            ext[seg : seg + HALO, :] = gc[pl.ds(pl.multiple_of((s + rows) * seg, seg), HALO), :]

        @pl.when(s >= rows)
        def _():
            ext[seg : seg + HALO, :] = halo_recv[pl.ds(pl.multiple_of((s - rows) * HALO, HALO), HALO), :]

        for k in range(1, 4):
            result = result + vec[k : k + 1] * ext[k : k + seg, :] * m[:, 2 + k : 3 + k]
        grad_recur_out[at, :] = result.astype(BF16)
        return none

    lax.fori_loop(0, 2 * rows, back, 0)


def whole(count):
    return [pl.BlockSpec(memory_space=pltpu.VMEM)] * count


def mixer_params(number):
    return pltpu.CompilerParams(collective_id=number, has_side_effects=True, vmem_limit_bytes=60 * 1024 * 1024)


def mixer_forward(count, seg, recur, gate, mask, wg0, wg1, vec):
    n, width = recur.shape
    full = functools.partial(jax.ShapeDtypeStruct, (n, width))
    tiles = -(-width // LANES)
    tiled = jax.ShapeDtypeStruct((tiles, n, LANES), F32)
    return pl.pallas_call(
        functools.partial(mixer_forward_kernel, count, seg),
        name="mixer_forward",
        out_shape=(
            full(BF16), tiled, full(F32), full(BF16),
            jax.ShapeDtypeStruct((16 * HALO, width), F32), jax.ShapeDtypeStruct((16, width), F32),
        ),
        in_specs=whole(6),
        out_specs=tuple(whole(6)),
        scratch_shapes=[
            pltpu.VMEM((tiles, n, LANES), F32),
            pltpu.VMEM((tiles, n, LANES), F32),
            pltpu.VMEM((tiles, n, LANES), F32),
            pltpu.VMEM((seg + HALO, width), F32),
            pltpu.VMEM((8 * HALO, width), F32),
            pltpu.VMEM((8 * HALO, width), F32),
            pltpu.VMEM((16, width), F32),
            pltpu.VMEM((count, 16, width), F32),
            pltpu.SemaphoreType.DMA((count,)),
            pltpu.SemaphoreType.DMA((count,)),
            pltpu.SemaphoreType.DMA((2,)),
        ],
        compiler_params=mixer_params(1),
    )(recur, gate, mask, wg0, wg1, vec)


def mixer_backward(count, seg, grad_mixed, gate, states, decay, conv_low, recur, halo, cin, mask, wg0, wg1, wg0t, wg1t, vec):
    n, width = recur.shape
    full = functools.partial(jax.ShapeDtypeStruct, (n, width))
    tiles = -(-width // LANES)
    tiled = jax.ShapeDtypeStruct((tiles, n, LANES), F32)
    return pl.pallas_call(
        functools.partial(mixer_backward_kernel, count, seg),
        name="mixer_backward",
        out_shape=(
            full(BF16), full(BF16),
            jax.ShapeDtypeStruct((width, width), F32), jax.ShapeDtypeStruct((width, width), F32),
            jax.ShapeDtypeStruct((8, width), F32),
        ),
        in_specs=whole(14),
        out_specs=tuple(whole(5)),
        scratch_shapes=[
            pltpu.VMEM((tiles, n, LANES), F32),
            pltpu.VMEM((tiles, n, LANES), F32),
            pltpu.VMEM((n, width), F32),
            pltpu.VMEM((seg + HALO, width), F32),
            pltpu.VMEM((8 * HALO, width), F32),
            pltpu.VMEM((8 * HALO, width), F32),
            pltpu.VMEM((16, width), F32),
            pltpu.VMEM((count, 16, width), F32),
            pltpu.VMEM((16, width), F32),
            pltpu.SemaphoreType.DMA((count,)),
            pltpu.SemaphoreType.DMA((count,)),
            pltpu.SemaphoreType.DMA((2,)),
        ],
        compiler_params=mixer_params(2),
    )(grad_mixed, gate, states, decay, conv_low, recur, halo, cin, mask, wg0, wg1, wg0t, wg1t, vec)


class Place:
    def __init__(self):
        self.i, self.g, self.c = lax.axis_index("i"), lax.axis_index("g"), lax.axis_index("c")
        self.core, self.across, self.along = {"c": 1 - self.c}, {"g": 1 - self.g}, {"i": 1 - self.i}

    def chunk(self, di, dg, dc):
        i = 1 - self.i if di else self.i
        g = 1 - self.g if dg else self.g
        c = 1 - self.c if dc else self.c
        return (i * 2 + g) * 2 + c

    def greet(self):
        barrier = pltpu.get_barrier_semaphore()
        for peer in (self.core, self.across, self.along):
            pl.semaphore_signal(barrier, inc=1, device_id=peer, device_id_type=MESH)
        pl.semaphore_wait(barrier, 3)


class Gather:
    COPIES = 11

    def __init__(self, place, block, out, send, recv):
        self.place, self.block, self.out, self.send, self.recv = place, block, out, send, recv
        self.tokens = block.shape[0]
        self.half = self.tokens // 2

    def rows(self, chunk, part):
        start = chunk * self.tokens + (self.half if part == 1 else 0)
        return self.out.at[pl.ds(pl.multiple_of(start, self.half), self.tokens if part == 2 else self.half)]

    def mine(self, part):
        if part == 2:
            return self.block
        return self.block.at[pl.ds(part * self.half, self.half)]

    def copy(self, number, source, chunk, part, peer):
        return pltpu.make_async_remote_copy(
            src_ref=source,
            dst_ref=self.rows(chunk, part),
            send_sem=self.send.at[number],
            recv_sem=self.recv.at[number],
            device_id=peer,
            device_id_type=MESH,
        )

    def begin(self, part):
        place = self.place
        own = place.chunk(0, 0, 0)
        self.kept = getattr(self, "kept", [])
        mine = self.mine(part)
        order = ((0 + part, place.across), (2 + part, place.along))
        for number, peer in order:
            self.kept.append((self.copy(number, mine, own, part, peer), None))
            self.kept[-1][0].start()
        self.kept.append((self.copy(4 + part, mine, own, part, place.core), None))
        self.kept[-1][0].start()
        keep = pltpu.make_async_copy(mine, self.rows(own, part), self.send.at[self.COPIES + part])
        keep.start()
        self.local = getattr(self, "local", []) + [keep]

    def arrived(self, number, chunk, part):
        self.copy(number, self.rows(chunk, part), chunk, part, self.place.core).wait_recv()

    def forward(self, number, chunk, part, peer):
        moved = self.copy(number, self.rows(chunk, part), chunk, part, peer)
        moved.start()
        self.kept.append((moved, None))

    def pass_on(self):
        place = self.place
        ax, al, dia = place.chunk(0, 1, 0), place.chunk(1, 0, 0), place.chunk(1, 1, 0)
        self.arrived(0, ax, 0)
        self.forward(6, ax, 0, place.along)
        self.arrived(3, al, 1)
        self.forward(7, al, 1, place.across)
        self.arrived(1, ax, 1)
        self.forward(8, ax, 2, place.core)
        self.arrived(2, al, 0)
        self.forward(9, al, 2, place.core)
        self.arrived(6, dia, 0)
        self.arrived(7, dia, 1)
        self.forward(10, dia, 2, place.core)

    def finish(self):
        place = self.place
        self.arrived(4, place.chunk(0, 0, 1), 0)
        self.arrived(5, place.chunk(0, 0, 1), 1)
        self.arrived(8, place.chunk(0, 1, 1), 2)
        self.arrived(9, place.chunk(1, 0, 1), 2)
        self.arrived(10, place.chunk(1, 1, 1), 2)
        for moved, _ in self.kept:
            moved.wait_send()
        for keep in self.local:
            keep.wait()


GATHER_SEMS = Gather.COPIES + 2
SLICE = 16


def first_gather_kernel(planes, normed, cot, ids, normed_out, cot_out, ids_out, before_out, after_out, *sems):
    place = Place()
    place.greet()
    me = lax.axis_index("t")
    gathers = []
    for number, (block, out) in enumerate(((normed, normed_out), (cot, cot_out))):
        gather = Gather(place, block, out, sems[2 * number], sems[2 * number + 1])
        gather.begin(0)
        gather.begin(1)
        gathers.append(gather)
    for gather in gathers:
        gather.pass_on()
    for gather in gathers:
        gather.finish()


class Scatter:
    def __init__(self, place, product, core_send, core_recv, held, acc, across_recv, along_recv, second, second_recv, send, recv):
        self.place, self.product = place, product
        self.core_send, self.core_recv, self.held, self.acc = core_send, core_recv, held, acc
        self.across_recv, self.along_recv, self.second, self.second_recv = across_recv, along_recv, second, second_recv
        self.send, self.recv = send, recv
        self.kept = []

    def copy(self, number, source, target, peer):
        return pltpu.make_async_remote_copy(
            src_ref=source,
            dst_ref=target,
            send_sem=self.send.at[number],
            recv_sem=self.recv.at[number],
            device_id=peer,
            device_id_type=MESH,
        )

    def start(self, *parts):
        moved = self.copy(*parts)
        moved.start()
        self.kept.append(moved)

    def run(self):
        place = self.place
        order = ((1, 1), (0, 1), (1, 0), (0, 0))
        tile = 256
        per_half = self.held.shape[3] // tile
        for di, dg in order:
            q = 2 * di + dg
            chunk = place.chunk(di, dg, 1)

            def send_tile(n, none):
                at = pl.ds(pl.multiple_of(n % per_half * tile, tile), tile)
                self.core_send[q, n // per_half, :, at] = self.product(chunk, n).astype(BF16)
                return none

            lax.fori_loop(0, 2 * per_half, send_tile, 0)
            self.start(q, self.core_send.at[q], self.core_recv.at[q], place.core)
        for di, dg in order:
            q = 2 * di + dg
            chunk = place.chunk(di, dg, 0)
            self.copy(q, self.core_send.at[q], self.core_recv.at[q], place.core).wait_recv()

            def sum_tile(n, none):
                at = pl.ds(pl.multiple_of(n % per_half * tile, tile), tile)
                value = self.product(chunk, n) + self.core_recv[q, n // per_half, :, at].astype(F32)
                if q:
                    self.held[q - 1, n // per_half, :, at] = value.astype(BF16)
                else:
                    self.acc[n // per_half, :, at] = value
                return none

            lax.fori_loop(0, 2 * per_half, sum_tile, 0)
            if dg:
                self.start(4 + di, self.held.at[q - 1, 0], self.across_recv.at[di], place.across)
            if di:
                self.start(6 + dg, self.held.at[q - 1, 1], self.along_recv.at[dg], place.along)
        for half, number, buffer, mine, peer, out in (
            (0, 5, self.across_recv, 2, place.along, 8),
            (1, 7, self.along_recv, 1, place.across, 9),
        ):
            self.copy(number, buffer.at[1], buffer.at[1], place.core).wait_recv()

            def add_rows(n, none):
                at = pl.ds(pl.multiple_of(n * SLICE, SLICE), SLICE)
                total = self.held[mine - 1, half, at, :].astype(F32) + buffer[1, at, :].astype(F32)
                self.second[half, at, :] = total.astype(BF16)
                return none

            lax.fori_loop(0, self.held.shape[2] // SLICE, add_rows, 0)
            self.start(out, self.second.at[half], self.second_recv.at[half], peer)
        for number, buffer in ((4, self.across_recv), (6, self.along_recv)):
            self.copy(number, buffer.at[0], buffer.at[0], place.core).wait_recv()
        for number, half in ((8, 0), (9, 1)):
            self.copy(number, self.second.at[half], self.second_recv.at[half], place.core).wait_recv()

    def rows(self, at):
        first = self.acc[0, at, :] + self.across_recv[0, at, :].astype(F32) + self.second_recv[0, at, :].astype(F32)
        last = self.acc[1, at, :] + self.along_recv[0, at, :].astype(F32) + self.second_recv[1, at, :].astype(F32)
        return jnp.concatenate([first, last], axis=1)

    def finish(self):
        for moved in self.kept:
            moved.wait_send()

    @staticmethod
    def scratch(tokens, width):
        half = width // 2
        return [
            pltpu.VMEM((4, 2, tokens, half), BF16),
            pltpu.VMEM((4, 2, tokens, half), BF16),
            pltpu.VMEM((3, 2, tokens, half), BF16),
            pltpu.VMEM((2, tokens, half), F32),
            pltpu.VMEM((2, tokens, half), BF16),
            pltpu.VMEM((2, tokens, half), BF16),
            pltpu.VMEM((2, tokens, half), BF16),
            pltpu.VMEM((2, tokens, half), BF16),
            pltpu.SemaphoreType.DMA((10,)),
            pltpu.SemaphoreType.DMA((10,)),
        ]


SCATTER_BUFFERS = 10


def pair_product(lefts, rights, tokens):
    def product(chunk, n):
        at = pl.ds(pl.multiple_of(chunk * tokens, tokens), tokens)
        cols = pl.ds(pl.multiple_of(n * 256, 256), 256)
        total = None
        for left, right in zip(lefts, rights):
            term = jnp.dot(left[at, :], right[:, cols], preferred_element_type=F32)
            total = term if total is None else total + term
        return total

    return product


def for_slices(start, stop, body):
    def step(n, none):
        body(pl.ds(pl.multiple_of(n * SLICE, SLICE), SLICE))
        return none

    lax.fori_loop(start // SLICE, stop // SLICE, step, 0)


def middle_kernel(left, right, own_in, gain, middle_out, gathered, *scratch):
    buffers, (block, send, recv) = scratch[:SCATTER_BUFFERS], scratch[SCATTER_BUFFERS:]
    tokens = own_in.shape[0]
    place = Place()
    place.greet()
    scatter = Scatter(place, pair_product([left], [right], tokens), *buffers)
    scatter.run()

    def body(at):
        middle = own_in[at, :].astype(F32) + scatter.rows(at)
        middle_out[at, :] = middle
        block[at, :] = (middle * rms(middle) * gain[...]).astype(BF16)

    gather = Gather(place, block, gathered, send, recv)
    for part in (0, 1):
        for_slices(part * tokens // 2, (part + 1) * tokens // 2, body)
        gather.begin(part)
    gather.pass_on()
    scatter.finish()
    gather.finish()


def turn_kernel(left0, left1, right0, right1, middle, gain, cot, grad_middle_out, gain_out, gathered, *scratch):
    buffers, (block, send, recv) = scratch[:SCATTER_BUFFERS], scratch[SCATTER_BUFFERS:]
    tokens = cot.shape[0]
    place = Place()
    place.greet()
    scatter = Scatter(place, pair_product([left0, left1], [right0, right1], tokens), *buffers)
    scatter.run()
    gain_out[...] = jnp.zeros_like(gain_out)

    def body(at):
        values = middle[at, :]
        grad = scatter.rows(at)
        scale = rms(values)
        weighted = grad * gain[...]
        inner = jnp.mean(values * weighted, axis=-1, keepdims=True)
        total = cot[at, :].astype(F32) + scale * weighted - values * (scale * scale * scale * inner)
        grad_middle_out[at, :] = total
        block[at, :] = total.astype(BF16)
        term = grad * values * scale
        gain_out[...] += term[0:8] + term[8:16]

    gather = Gather(place, block, gathered, send, recv)
    for part in (0, 1):
        for_slices(part * tokens // 2, (part + 1) * tokens // 2, body)
        gather.begin(part)
    gather.pass_on()
    scatter.finish()
    gather.finish()


def scatter_kernel(count, *refs):
    lefts, rights, out, buffers = refs[:count], refs[count : 2 * count], refs[2 * count], refs[2 * count + 1 :]
    tokens = out.shape[0]
    place = Place()
    place.greet()
    scatter = Scatter(place, pair_product(lefts, rights, tokens), *buffers)
    scatter.run()

    def body(at):
        out[at, :] = scatter.rows(at).astype(out.dtype)

    for_slices(0, tokens, body)
    scatter.finish()


ANYWHERE = pl.BlockSpec(memory_space=pl.ANY)
GATHER_SCRATCH = [pltpu.SemaphoreType.DMA((GATHER_SEMS,))] * 2


def first_gather(planes, normed, cot):
    tokens, width = normed.shape
    full = jax.ShapeDtypeStruct((8 * tokens, width), BF16)

    def kernel(normed_ref, cot_ref, normed_out, cot_out, *sems):
        first_gather_kernel(planes, normed_ref, cot_ref, None, normed_out, cot_out, None, None, None, *sems)

    return pl.pallas_call(
        kernel,
        name="first_gather",
        out_shape=(full, full),
        in_specs=[ANYWHERE] * 2,
        out_specs=(ANYWHERE,) * 2,
        scratch_shapes=GATHER_SCRATCH * 2,
        compiler_params=mixer_params(3),
    )(normed, cot)


def middle_step(mixed, w_out, own_in, gain):
    tokens, width = own_in.shape
    return pl.pallas_call(
        middle_kernel,
        name="middle_step",
        out_shape=(jax.ShapeDtypeStruct((tokens, width), F32), jax.ShapeDtypeStruct((8 * tokens, width), BF16)),
        in_specs=whole(4),
        out_specs=(pl.BlockSpec(memory_space=pltpu.VMEM), ANYWHERE),
        scratch_shapes=Scatter.scratch(tokens, width) + [pltpu.VMEM((tokens, width), BF16)] + GATHER_SCRATCH,
        compiler_params=mixer_params(4),
    )(mixed, w_out, own_in, gain[None])


def turn_step(left0, left1, right0, right1, middle, gain, cot):
    tokens, width = cot.shape
    return pl.pallas_call(
        turn_kernel,
        name="turn_step",
        out_shape=(
            jax.ShapeDtypeStruct((tokens, width), F32),
            jax.ShapeDtypeStruct((8, width), F32),
            jax.ShapeDtypeStruct((8 * tokens, width), BF16),
        ),
        in_specs=whole(7),
        out_specs=(*whole(2), ANYWHERE),
        scratch_shapes=Scatter.scratch(tokens, width) + [pltpu.VMEM((tokens, width), BF16)] + GATHER_SCRATCH,
        compiler_params=mixer_params(5),
    )(left0, left1, right0, right1, middle, gain[None], cot)


def scatter_step(number, lefts, rights):
    tokens, width = lefts[0].shape[0] // 8, rights[0].shape[1]
    return pl.pallas_call(
        functools.partial(scatter_kernel, len(lefts)),
        name="scatter_step",
        out_shape=jax.ShapeDtypeStruct((tokens, width), F32),
        in_specs=whole(2 * len(lefts)),
        out_specs=pl.BlockSpec(memory_space=pltpu.VMEM),
        scratch_shapes=Scatter.scratch(tokens, width),
        compiler_params=mixer_params(number),
    )(*lefts, *rights)


def swap_kernel(groups, quarters, out, send, recv):
    g, c = lax.axis_index("g"), lax.axis_index("c")
    me = g * 2 + c
    barrier = pltpu.get_barrier_semaphore()
    for step in range(1, groups):
        other = lax.rem(me + step, groups)
        pl.semaphore_signal(barrier, inc=1, device_id={"g": other // 2, "c": other % 2}, device_id_type=MESH)
    pl.semaphore_wait(barrier, groups - 1)
    keep = pltpu.make_async_copy(quarters.at[me], out.at[:, me], send.at[0])
    keep.start()
    moved = []
    for step in range(1, groups):
        other = lax.rem(me + step, groups)
        copy = pltpu.make_async_remote_copy(
            src_ref=quarters.at[other],
            dst_ref=out.at[:, me],
            send_sem=send.at[step],
            recv_sem=recv.at[step],
            device_id={"g": other // 2, "c": other % 2},
            device_id_type=MESH,
        )
        copy.start()
        moved.append(copy)
    for step in range(1, groups):
        other = lax.rem(me + groups - step, groups)
        pltpu.make_async_remote_copy(
            src_ref=quarters.at[other],
            dst_ref=out.at[:, other],
            send_sem=send.at[step],
            recv_sem=recv.at[step],
            device_id={"g": other // 2, "c": other % 2},
            device_id_type=MESH,
        ).wait_recv()
    for copy in moved:
        copy.wait_send()
    keep.wait()


def swap(quarters):
    groups, kinds, part, width = quarters.shape
    return pl.pallas_call(
        functools.partial(swap_kernel, groups),
        name="swap",
        out_shape=jax.ShapeDtypeStruct((kinds, groups, part, width), quarters.dtype),
        in_specs=[ANYWHERE],
        out_specs=ANYWHERE,
        scratch_shapes=[pltpu.SemaphoreType.DMA((groups,)), pltpu.SemaphoreType.DMA((groups,))],
        compiler_params=mixer_params(6),
    )(quarters)


def rms(values):
    return lax.rsqrt(jnp.mean(values * values, axis=-1, keepdims=True) + EPS)


def rms_back(values, scale, gain, grad):
    weighted = grad * gain
    inner = jnp.mean(values * weighted, axis=-1, keepdims=True)
    return scale * weighted - values * (scale * scale * scale * inner), jnp.sum(grad * values * scale, axis=0)


def nt(left, right, out):
    return lax.dot_general(left, right, (((1,), (1,)), ((), ())), preferred_element_type=F32).astype(out)


def tn(left, right, out):
    return lax.dot_general(left, right, (((0,), (0,)), ((), ())), preferred_element_type=F32).astype(out)


def nn(left, right, out):
    return jnp.dot(left, right, preferred_element_type=F32).astype(out)


def per_device(
    inputs, segment_ids, mix_gain, in_weight, conv_weight, conv_bias, gate_weight, gate_bias, decay_param, out_weight,
    mlp_gain, mlp_in, down_weight, cotangent,
):
    planes = lax.axis_size("t")
    rows_here, seg, width = inputs.shape
    row_groups = lax.axis_size("g") * lax.axis_size("c")
    own_tokens = rows_here * seg
    recur_width = conv_weight.shape[1]
    block_width = gate_weight.shape[0]
    members = 2 * row_groups
    channels = recur_width // members
    t, i = lax.axis_index("t"), lax.axis_index("i")
    r = lax.axis_index("g") * lax.axis_size("c") + lax.axis_index("c")
    member = 2 * r + i
    first = member * channels

    mixer_own = jnp.stack([in_weight[:, 0].T, in_weight[:, 1].T, out_weight.T])
    if planes == row_groups:
        part = channels // row_groups
        quarter = lax.dynamic_slice_in_dim(mixer_own, r * part, part, 1)
        mixer_w = swap(lax.all_gather(quarter, "t", axis=0, tiled=False))
    else:
        every = lax.all_gather(mixer_own, ("t", "i"), axis=1, tiled=True)
        mixer_w = lax.dynamic_slice_in_dim(every, first, channels, 1)
    mixer_w = mixer_w.reshape(3, channels, width)
    w_gate, w_recur, w_out = mixer_w[0], mixer_w[1], mixer_w[2]
    hidden_part = mlp_in.shape[2] // row_groups

    def own_part(weight):
        return lax.dynamic_slice_in_dim(weight.T, r * hidden_part, hidden_part, 0)

    mlp_w = jnp.concatenate([own_part(mlp_in[:, 0]), own_part(mlp_in[:, 1]), own_part(down_weight)], axis=0)
    mlp_w = lax.all_gather(mlp_w, "t", axis=0, tiled=False)
    mlp_w = mlp_w.reshape(planes, 3, hidden_part, width)
    w_left = mlp_w[:, 0].reshape(-1, width)
    w_right = mlp_w[:, 1].reshape(-1, width)
    w_down = mlp_w[:, 2].reshape(-1, width)

    ids = lax.all_gather((segment_ids + 1).astype(F32), ("g", "c"), axis=0, tiled=True)
    ids = lax.all_gather(ids, ("t", "i"), axis=1, tiled=True)
    span = 2 * seg
    ids = jnp.pad(ids, ((0, 0), (HALO, HALO)))
    ids = lax.dynamic_slice_in_dim(ids, t * span, span + 2 * HALO, 1)
    here = ids[:, HALO : HALO + span]
    columns = [(ids[:, HALO - k : HALO - k + span] == here) for k in (1, 2, 3)]
    columns += [(ids[:, HALO + k : HALO + k + span] == here) for k in (1, 2, 3)]
    columns += [jnp.zeros_like(columns[0])] * 2
    mask = jnp.stack(columns, axis=-1).astype(F32)
    mask = mask.reshape(mask.shape[0], 2, seg, 8).transpose(1, 0, 2, 3).reshape(-1, 8)

    def own(values):
        return lax.dynamic_slice_in_dim(values, first, channels, values.ndim - 1)

    decay_own = own(decay_param)
    vec = jnp.concatenate(
        [
            own(conv_weight),
            own(conv_bias)[None],
            own(gate_bias),
            8.0 * jax.nn.softplus(-decay_own)[None],
            8.0 * jax.nn.sigmoid(-decay_own)[None],
            jnp.zeros((7, channels), F32),
        ]
    )
    blocks = channels // block_width
    gate_own = own(gate_weight).reshape(block_width, 2, blocks, block_width)
    spread = jnp.zeros((2, blocks, block_width, blocks, block_width), BF16)
    for n in range(blocks):
        spread = spread.at[:, n, :, n, :].set(gate_own[:, :, n, :].transpose(1, 0, 2))
    spread = spread.reshape(2, channels, channels)
    wg0, wg1 = spread[0], spread[1]

    own_in = inputs.reshape(own_tokens, width)
    flat_in = own_in.astype(F32)
    scale_in = rms(flat_in)
    cot_own = cotangent.reshape(own_tokens, width)
    normed, cot = first_gather(planes, (flat_in * scale_in * mix_gain).astype(BF16), cot_own)
    gate_branch = nt(normed, w_gate, F32)
    recur = nt(normed, w_recur, BF16)
    conv_low, decay, states, mixed, halo, cin = mixer_forward(planes, seg, recur, gate_branch, mask, wg0, wg1, vec)
    middle, normed_two = middle_step(mixed, w_out, own_in, mlp_gain)
    left = nt(normed_two, w_left, F32)
    right = nt(normed_two, w_right, F32)
    act, slope = gelu_parts(left)
    hidden = (act * right).astype(BF16)

    grad_hidden = nt(cot, w_down, F32)
    grad_left = (grad_hidden * right * slope).astype(BF16)
    grad_right = (grad_hidden * act).astype(BF16)
    grad_middle, grad_mlp_gain, grad_mid = turn_step(grad_left, grad_right, w_left, w_right, middle, mlp_gain, cot_own)
    grad_mlp_gain = jnp.sum(grad_mlp_gain, axis=0)
    grad_mixed = nt(grad_mid, w_out, F32)
    grad_gate, grad_recur, gw0, gw1, small = mixer_backward(
        planes, seg, grad_mixed, gate_branch, states, decay, conv_low, recur, halo, cin, mask, wg0, wg1, wg0.T, wg1.T, vec
    )
    grad_normed = scatter_step(7, [grad_gate, grad_recur], [w_gate, w_recur])
    grad_in_norm, grad_mix_gain = rms_back(flat_in, scale_in, mix_gain, grad_normed)
    grad_inputs = (grad_middle + grad_in_norm).reshape(inputs.shape)
    down = scatter_step(8, [hidden], [w_down])
    outputs = (middle + down).astype(BF16).reshape(inputs.shape)

    def to_owners(grad):
        reduced = lax.psum_scatter(grad, "t", scatter_dimension=0, tiled=True)
        return lax.all_to_all(reduced.reshape(members, -1, grad.shape[1]), PLANE, 0, 0, tiled=True)

    own_rows = width // (planes * members)
    mlp_grads = to_owners(
        jnp.concatenate([tn(normed_two, grad_left, BF16), tn(normed_two, grad_right, BF16), tn(cot, hidden, BF16)], axis=1)
    )
    mixer_grads = to_owners(
        jnp.concatenate([tn(normed, grad_gate, BF16), tn(normed, grad_recur, BF16), tn(grad_mid, mixed, BF16)], axis=1)
    )
    mlp_grads = mlp_grads.reshape(2, row_groups, own_rows, 3, planes, hidden_part).astype(F32)
    mlp_grads = mlp_grads.transpose(2, 3, 4, 0, 1, 5).reshape(own_rows, 3, -1)
    mixer_grads = mixer_grads.reshape(2, row_groups, own_rows, 3, channels).astype(F32)
    mixer_grads = mixer_grads.transpose(2, 3, 1, 0, 4).reshape(own_rows, 3, -1)

    column_block = lax.broadcasted_iota(jnp.int32, (block_width, channels), 1) // block_width

    def diagonal(gw):
        return sum(
            jnp.where(column_block == n, gw[n * block_width : (n + 1) * block_width], 0.0) for n in range(blocks)
        )

    gate_grads = jnp.concatenate([diagonal(gw0), diagonal(gw1), small], axis=0)
    if planes == row_groups:
        pieces = gate_grads.reshape(gate_grads.shape[0], row_groups, -1).transpose(1, 0, 2)
        pieces = lax.all_to_all(pieces, ("g", "c"), 0, 0, tiled=True)
        gate_grads = lax.psum_scatter(pieces, "t", scatter_dimension=0, tiled=False)
    else:
        placed = jnp.zeros((gate_grads.shape[0], recur_width), F32)
        placed = lax.dynamic_update_slice_in_dim(placed, gate_grads, first, 1)
        gate_grads = lax.psum_scatter(placed, EVERY, scatter_dimension=1, tiled=True)
    grad_gate_weight = jnp.stack([gate_grads[:block_width], gate_grads[block_width : 2 * block_width]], axis=1)
    small = gate_grads[2 * block_width :]
    return (
        outputs,
        grad_inputs,
        lax.psum_scatter(grad_mix_gain, EVERY, scatter_dimension=0, tiled=True),
        mixer_grads[:, :2],
        small[0:4],
        small[4],
        grad_gate_weight,
        small[5:7],
        small[7],
        mixer_grads[:, 2],
        lax.psum_scatter(grad_mlp_gain, EVERY, scatter_dimension=0, tiled=True),
        mlp_grads[:, :2],
        mlp_grads[:, 2],
    )


def solution(mesh):
    seq, rows = mesh.shape["seq"], mesh.shape["rows"]
    grid = Mesh(mesh.devices.reshape(seq // 2, 2, rows // 2, 2), EVERY)
    row_axes, seq_axes = ("g", "c"), ("t", "i")
    tokens = P(row_axes, seq_axes, None)
    return jax.shard_map(
        per_device,
        mesh=grid,
        in_specs=(
            tokens,
            P(row_axes, seq_axes),
            P(),
            P(None, None, seq_axes),
            P(),
            P(),
            P(),
            P(),
            P(),
            P(None, seq_axes),
            P(),
            P(None, None, seq_axes),
            P(None, seq_axes),
            tokens,
        ),
        out_specs=(
            tokens,
            tokens,
            P(EVERY),
            P(EVERY, None, None),
            P(None, EVERY),
            P(EVERY),
            P(None, None, EVERY),
            P(None, EVERY),
            P(EVERY),
            P(EVERY, None),
            P(EVERY),
            P(EVERY, None, None),
            P(EVERY, None),
        ),
        check_vma=False,
    )
```

```python
import functools

import jax
import jax.numpy as jnp
from jax import lax
from jax.experimental import pallas as pl
from jax.experimental.pallas import tpu as pltpu
from jax.sharding import Mesh
from jax.sharding import PartitionSpec as P

EPS = 1e-06
MESH = pl.DeviceIdType.MESH
PLANE = ("i", "g", "c")
EVERY = ("t", "i", "g", "c")
F32 = jnp.float32
BF16 = jnp.bfloat16
GELU_A = 0.7978845608028654
GELU_B = 0.044715
HALO = 8
LANES = 128
SLICE = 16
ANYWHERE = pl.BlockSpec(memory_space=pl.ANY)
GATHER_SCRATCH = [pltpu.SemaphoreType.DMA((13,))] * 2


def gelu_parts(x):
    square = x * x
    th = jnp.tanh(GELU_A * x * (1.0 + GELU_B * square))
    half = 0.5 * (1.0 + th)
    slope = half + 0.5 * x * (1.0 - th * th) * (GELU_A * (1.0 + 3.0 * GELU_B * square))
    return x * half, slope


def one_minus_exp(y):
    series = 1.0 + y * (-1.0 / 2 + y * (1.0 / 6 + y * (-1.0 / 24 + y * (1.0 / 120 + y * (-1.0 / 720 + y * (1.0 / 5040))))))
    return jnp.where(y < 0.35, y * series, 1.0 - jnp.exp(-y))


def sigmoid(x):
    return 1.0 / (1.0 + jnp.exp(-x))


def gate_values(conv_low, wg0, wg1, vec):
    logits0 = jnp.dot(conv_low, wg0, preferred_element_type=F32) + vec[5:6]
    logits1 = jnp.dot(conv_low, wg1, preferred_element_type=F32) + vec[6:7]
    recur_gate = sigmoid(logits0)
    input_gate = sigmoid(logits1)
    log_decay = -vec[7:8] * recur_gate
    return recur_gate, input_gate, log_decay


def greet(count):
    me = lax.axis_index("t")
    barrier = pltpu.get_barrier_semaphore()
    for step in range(1, count):
        pl.semaphore_signal(barrier, inc=1, device_id={"t": lax.rem(me + step, count)}, device_id_type=MESH)
    pl.semaphore_wait(barrier, count - 1)
    return me


def put_tiles(ref, at, values):
    tiles, lanes = ref.shape[0], ref.shape[2]
    short = tiles * lanes - values.shape[1]
    if short:
        values = jnp.concatenate([values, jnp.zeros((values.shape[0], short), values.dtype)], axis=1)
    for j in range(tiles):
        ref[j, at, :] = values[:, j * lanes : (j + 1) * lanes]


def get_tiles(ref, at, width):
    joined = jnp.concatenate([ref[j, at, :] for j in range(ref.shape[0])], axis=1)
    return joined[:, :width]


def join_tiles(parts, width):
    return jnp.concatenate(parts, axis=1)[:, :width]


def exchange(count, me, send, slots, send_sem, recv_sem):
    for step in range(1, count):
        pltpu.make_async_remote_copy(
            src_ref=send,
            dst_ref=slots.at[me],
            send_sem=send_sem.at[step],
            recv_sem=recv_sem.at[step],
            device_id={"t": lax.rem(me + step, count)},
            device_id_type=MESH,
        ).start()
    for step in range(1, count):
        other = lax.rem(me + count - step, count)
        pltpu.make_async_remote_copy(
            src_ref=send,
            dst_ref=slots.at[other],
            send_sem=send_sem.at[step],
            recv_sem=recv_sem.at[step],
            device_id={"t": other},
            device_id_type=MESH,
        ).wait()


def mixer_forward_kernel(
    count, seg, rows_here, recur, gate, ids, ids_before, ids_after, wg0, wg1, vec_ref, cot, quarters,
    conv_out, decay_out, states_out, mixed_out, halo_out, cin_out, mask, cot_out, swapped,
    drive, h_ref, a_ref, ext, halo_send, halo_recv, summary, slots, send_sem, recv_sem, halo_sems,
    gather_send, gather_recv, swap_send, swap_recv,
):
    place = Place()
    me = lax.axis_index("t")
    place.greet([place.peer(0, 1, 1)] + [{"t": lax.rem(me + step, count)} for step in range(1, count)])
    gather = Gather(place, cot, cot_out, gather_send, gather_recv)
    move = Swap(quarters, swapped, swap_send, swap_recv)
    rows = 8
    for r in range(rows):
        halo_send[r * HALO : (r + 1) * HALO, :] = recur[
            (rows + r) * seg + seg - 16 : (rows + r) * seg + seg, :
        ].astype(F32)[16 - HALO :]
    halo_copy = pltpu.make_async_remote_copy(
        src_ref=halo_send,
        dst_ref=halo_recv,
        send_sem=halo_sems.at[0],
        recv_sem=halo_sems.at[1],
        device_id={"t": lax.rem(me + 1, count)},
        device_id_type=MESH,
    )
    halo_copy.start()
    gather.begin(0)
    gather.begin(1)
    move.begin()
    halo_copy.wait()
    for r in range(rows):
        halo_out[r * HALO : (r + 1) * HALO, :] = halo_recv[r * HALO : (r + 1) * HALO, :]
        halo_out[(rows + r) * HALO : (rows + r + 1) * HALO, :] = recur[r * seg + seg - 16 : r * seg + seg, :].astype(F32)[
            16 - HALO :
        ]
    vec = vec_ref[...]

    def ids_of(ref, s):
        chunk = s // rows_here
        return ref[chunk, s % rows_here : s % rows_here + 1, :]

    nothing = jnp.zeros((1, LANES), F32)
    for s in range(2 * rows):
        here = ids_of(ids, s)
        back = ids_of(ids, s - rows) if s >= rows else jnp.where(me > 0, ids_of(ids_before, s + rows), nothing)
        ahead = ids_of(ids, s + rows) if s < rows else jnp.where(me < count - 1, ids_of(ids_after, s - rows), nothing)
        lines = [jnp.concatenate([back[:, seg - k :], here[:, : seg - k]], axis=1) for k in (1, 2, 3)]
        lines += [jnp.concatenate([here[:, k:], ahead[:, :k]], axis=1) for k in (1, 2, 3)]
        lines = [jnp.where(line == here, 1.0, 0.0) for line in lines] + [nothing] * 2
        mask[s * seg : (s + 1) * seg, :] = jnp.concatenate(lines, axis=0).T

    def local(s, none):
        at = pl.ds(pl.multiple_of(s * seg, seg), seg)
        x = recur[at, :].astype(F32)
        ext[0:HALO, :] = halo_out[pl.ds(pl.multiple_of(s * HALO, HALO), HALO), :]
        ext[HALO : HALO + seg, :] = x
        m = mask[at, :]
        conv = vec[4:5] + vec[0:1] * x
        for k in range(1, 4):
            conv = conv + vec[k : k + 1] * ext[HALO - k : HALO - k + seg, :] * m[:, k - 1 : k]
        conv_low = conv.astype(BF16)
        conv_out[at, :] = conv_low
        recur_gate, input_gate, log_decay = gate_values(conv_low, wg0[...], wg1[...], vec)
        keep = m[:, 0:1]
        put_tiles(decay_out, at, jnp.exp(log_decay) * keep)
        scale = (1.0 - keep) + keep * jnp.sqrt(one_minus_exp(-2.0 * log_decay))
        put_tiles(drive, at, scale * input_gate * conv_low.astype(F32))
        return none

    lax.fori_loop(0, 2 * rows, local, 0)
    gather.pass_first()
    tiles, lanes = drive.shape[0], drive.shape[2]

    def scan(k, carried):
        at = pl.ds(k, 2 * rows, stride=seg)
        after = []
        for j in range(tiles):
            h, a = carried[j]
            d = decay_out[j, at, :]
            h = d * h + drive[j, at, :]
            a = a * d
            h_ref[j, at, :] = h
            a_ref[j, at, :] = a
            after.append((h, a))
        return tuple(after)

    width = recur.shape[1]
    start = (jnp.zeros((2 * rows, lanes), F32), jnp.ones((2 * rows, lanes), F32))
    last = lax.fori_loop(0, seg, scan, (start,) * tiles, unroll=4)
    last_h = join_tiles([part[0] for part in last], width)
    last_a = join_tiles([part[1] for part in last], width)
    summary[0:rows, :] = last_a[rows:] * last_a[:rows]
    summary[rows : 2 * rows, :] = last_a[rows:] * last_h[:rows] + last_h[rows:]
    gather.pass_second()
    exchange(count, me, summary, slots, send_sem, recv_sem)
    carry = jnp.zeros((rows, width), F32)
    for z in range(count - 1):
        carry = jnp.where(z < me, slots[z, 0:rows, :] * carry + slots[z, rows : 2 * rows, :], carry)
    cin_out[0:rows, :] = carry
    cin_out[rows : 2 * rows, :] = last_a[:rows] * carry + last_h[:rows]

    def finish(s, none):
        at = pl.ds(pl.multiple_of(s * seg, seg), seg)
        states = get_tiles(h_ref, at, width) + get_tiles(a_ref, at, width) * cin_out[pl.ds(s, 1), :]
        states_out[at, :] = states
        act, _ = gelu_parts(gate[at, :])
        mixed_out[at, :] = (act * states.astype(BF16).astype(F32)).astype(BF16)
        return none

    lax.fori_loop(0, 2 * rows, finish, 0)
    gather.pass_third()
    gather.finish()
    move.finish()


def mixer_backward_kernel(
    count, seg, grad_mixed, gate, states, decay, conv_low_ref, recur, halo, cin, mask, wg0, wg1, wg0t, wg1t, vec_ref,
    grad_gate_out, grad_recur_out, gw0_out, gw1_out, small_out,
    tot, prod, gc, ext, halo_send, halo_recv, summary, slots, uin, send_sem, recv_sem, halo_sems,
):
    me = greet(count)
    rows = 8
    width = recur.shape[1]
    vec = vec_ref[...]

    def local(s, none):
        at = pl.ds(pl.multiple_of(s * seg, seg), seg)
        act, slope = gelu_parts(gate[at, :])
        gm = grad_mixed[at, :].astype(F32)
        grad_gate_out[at, :] = (gm * states[at, :].astype(BF16).astype(F32) * slope).astype(BF16)
        put_tiles(tot, at, (gm * act).astype(BF16).astype(F32))
        return none

    lax.fori_loop(0, 2 * rows, local, 0)

    tiles, lanes = tot.shape[0], tot.shape[2]

    def scan(k, carried):
        at = pl.ds(seg - 1 - k, 2 * rows, stride=seg)
        after = []
        for j in range(tiles):
            u, p = carried[j]
            d = decay[j, at, :]
            total = tot[j, at, :] + u
            tot[j, at, :] = total
            prod[j, at, :] = p
            after.append((d * total, d * p))
        return tuple(after)

    start = (jnp.zeros((2 * rows, lanes), F32), jnp.ones((2 * rows, lanes), F32))
    last = lax.fori_loop(0, seg, scan, (start,) * tiles, unroll=4)
    u = join_tiles([part[0] for part in last], width)
    p = join_tiles([part[1] for part in last], width)
    summary[0:rows, :] = p[:rows] * p[rows:]
    summary[rows : 2 * rows, :] = p[:rows] * u[rows:] + u[:rows]
    exchange(count, me, summary, slots, send_sem, recv_sem)
    carry = jnp.zeros((rows, width), F32)
    for z in range(count - 1, 0, -1):
        carry = jnp.where(z > me, slots[z, 0:rows, :] * carry + slots[z, rows : 2 * rows, :], carry)
    uin[rows : 2 * rows, :] = carry
    uin[0:rows, :] = p[rows:] * carry + u[rows:]
    gw0_out[...] = jnp.zeros_like(gw0_out)
    gw1_out[...] = jnp.zeros_like(gw1_out)
    small_out[...] = jnp.zeros_like(small_out)

    def gates(s, none):
        at = pl.ds(pl.multiple_of(s * seg, seg), seg)
        total = get_tiles(tot, at, width) + get_tiles(prod, at, width) * uin[pl.ds(s, 1), :]
        ext[HALO - 1 : HALO, :] = cin[pl.ds(s, 1), :]
        ext[HALO : HALO + seg, :] = states[at, :]
        before = ext[HALO - 1 : HALO - 1 + seg, :]
        conv_low = conv_low_ref[at, :]
        conv_vals = conv_low.astype(F32)
        m = mask[at, :]
        keep = m[:, 0:1]
        recur_gate, input_gate, log_decay = gate_values(conv_low, wg0[...], wg1[...], vec)
        root = jnp.sqrt(one_minus_exp(-2.0 * log_decay))
        scale = (1.0 - keep) + keep * root
        driven_in = total * conv_vals
        grad_log = total * before * get_tiles(decay, at, width) - driven_in * input_gate * keep * (jnp.exp(2.0 * log_decay) / root)
        grad0 = grad_log * log_decay * (1.0 - recur_gate)
        grad1 = driven_in * scale * input_gate * (1.0 - input_gate)
        low0 = grad0.astype(BF16)
        low1 = grad1.astype(BF16)
        grad_conv = (
            total * scale * input_gate
            + jnp.dot(low0, wg0t[...], preferred_element_type=F32)
            + jnp.dot(low1, wg1t[...], preferred_element_type=F32)
        )
        gc[at, :] = grad_conv
        turned = (((0,), (0,)), ((), ()))
        gw0_out[...] += lax.dot_general(conv_low, low0, turned, preferred_element_type=F32)
        gw1_out[...] += lax.dot_general(conv_low, low1, turned, preferred_element_type=F32)
        x = recur[at, :].astype(F32)
        ext[0:HALO, :] = halo[pl.ds(pl.multiple_of(s * HALO, HALO), HALO), :]
        ext[HALO : HALO + seg, :] = x

        def add(row, values):
            small_out[row : row + 1, :] += jnp.sum(values, axis=0, keepdims=True)

        add(0, grad_conv * x)
        for k in range(1, 4):
            add(k, grad_conv * ext[HALO - k : HALO - k + seg, :] * m[:, k - 1 : k])
        add(4, grad_conv)
        add(5, grad0)
        add(6, grad1)
        add(7, grad_log * recur_gate)
        return none

    lax.fori_loop(0, 2 * rows, gates, 0)
    small_out[7:8, :] = small_out[7:8, :] * vec[8:9]
    for r in range(rows):
        halo_send[r * HALO : (r + 1) * HALO, :] = gc[r * seg : r * seg + HALO, :]
    halo_copy = pltpu.make_async_remote_copy(
        src_ref=halo_send,
        dst_ref=halo_recv,
        send_sem=halo_sems.at[0],
        recv_sem=halo_sems.at[1],
        device_id={"t": lax.rem(me + count - 1, count)},
        device_id_type=MESH,
    )
    halo_copy.start()
    halo_copy.wait()

    def back(s, none):
        at = pl.ds(pl.multiple_of(s * seg, seg), seg)
        m = mask[at, :]
        ext[0:seg, :] = gc[at, :]
        result = vec[0:1] * gc[at, :]

        @pl.when(s < rows)
        def _():
            ext[seg : seg + HALO, :] = gc[pl.ds(pl.multiple_of((s + rows) * seg, seg), HALO), :]

        @pl.when(s >= rows)
        def _():
            ext[seg : seg + HALO, :] = halo_recv[pl.ds(pl.multiple_of((s - rows) * HALO, HALO), HALO), :]

        for k in range(1, 4):
            result = result + vec[k : k + 1] * ext[k : k + seg, :] * m[:, 2 + k : 3 + k]
        grad_recur_out[at, :] = result.astype(BF16)
        return none

    lax.fori_loop(0, 2 * rows, back, 0)


def whole(count):
    return [pl.BlockSpec(memory_space=pltpu.VMEM)] * count


def mixer_params(number):
    return pltpu.CompilerParams(collective_id=number, has_side_effects=True, vmem_limit_bytes=60 * 1024 * 1024)


def mixer_forward(count, seg, rows_here, recur, gate, ids, wg0, wg1, vec, cot, quarters):
    n, width = recur.shape
    full = functools.partial(jax.ShapeDtypeStruct, (n, width))
    tiles = -(-width // LANES)
    tiled = jax.ShapeDtypeStruct((tiles, n, LANES), F32)
    groups, kinds, part, depth = quarters.shape
    return pl.pallas_call(
        functools.partial(mixer_forward_kernel, count, seg, rows_here),
        name="mixer_forward",
        out_shape=(
            full(BF16), tiled, full(F32), full(BF16),
            jax.ShapeDtypeStruct((16 * HALO, width), F32), jax.ShapeDtypeStruct((16, width), F32),
            jax.ShapeDtypeStruct((n, 8), F32),
            jax.ShapeDtypeStruct((8 * cot.shape[0], cot.shape[1]), BF16),
            jax.ShapeDtypeStruct((kinds, groups, part, depth), BF16),
        ),
        in_specs=whole(8) + [ANYWHERE] * 2,
        out_specs=(*whole(7), ANYWHERE, ANYWHERE),
        scratch_shapes=[
            pltpu.VMEM((tiles, n, LANES), F32),
            pltpu.VMEM((tiles, n, LANES), F32),
            pltpu.VMEM((tiles, n, LANES), F32),
            pltpu.VMEM((seg + HALO, width), F32),
            pltpu.VMEM((8 * HALO, width), F32),
            pltpu.VMEM((8 * HALO, width), F32),
            pltpu.VMEM((16, width), F32),
            pltpu.VMEM((count, 16, width), F32),
            pltpu.SemaphoreType.DMA((count,)),
            pltpu.SemaphoreType.DMA((count,)),
            pltpu.SemaphoreType.DMA((2,)),
            *GATHER_SCRATCH,
            *swap_scratch(groups),
        ],
        compiler_params=mixer_params(1),
    )(recur, gate, *ids, wg0, wg1, vec, cot, quarters)


def mixer_backward(count, seg, grad_mixed, gate, states, decay, conv_low, recur, halo, cin, mask, wg0, wg1, wg0t, wg1t, vec):
    n, width = recur.shape
    full = functools.partial(jax.ShapeDtypeStruct, (n, width))
    tiles = -(-width // LANES)
    tiled = jax.ShapeDtypeStruct((tiles, n, LANES), F32)
    return pl.pallas_call(
        functools.partial(mixer_backward_kernel, count, seg),
        name="mixer_backward",
        out_shape=(
            full(BF16), full(BF16),
            jax.ShapeDtypeStruct((width, width), F32), jax.ShapeDtypeStruct((width, width), F32),
            jax.ShapeDtypeStruct((8, width), F32),
        ),
        in_specs=whole(14),
        out_specs=tuple(whole(5)),
        scratch_shapes=[
            pltpu.VMEM((tiles, n, LANES), F32),
            pltpu.VMEM((tiles, n, LANES), F32),
            pltpu.VMEM((n, width), F32),
            pltpu.VMEM((seg + HALO, width), F32),
            pltpu.VMEM((8 * HALO, width), F32),
            pltpu.VMEM((8 * HALO, width), F32),
            pltpu.VMEM((16, width), F32),
            pltpu.VMEM((count, 16, width), F32),
            pltpu.VMEM((16, width), F32),
            pltpu.SemaphoreType.DMA((count,)),
            pltpu.SemaphoreType.DMA((count,)),
            pltpu.SemaphoreType.DMA((2,)),
        ],
        compiler_params=mixer_params(2),
    )(grad_mixed, gate, states, decay, conv_low, recur, halo, cin, mask, wg0, wg1, wg0t, wg1t, vec)


class Place:
    def __init__(self):
        self.i, self.g, self.c = lax.axis_index("i"), lax.axis_index("g"), lax.axis_index("c")
        self.core, self.across, self.along = {"c": 1 - self.c}, {"g": 1 - self.g}, {"i": 1 - self.i}

    def chunk(self, di, dg, dc):
        i = 1 - self.i if di else self.i
        g = 1 - self.g if dg else self.g
        c = 1 - self.c if dc else self.c
        return (i * 2 + g) * 2 + c

    def peer(self, di, dg, dc):
        return {
            "i": 1 - self.i if di else self.i,
            "g": 1 - self.g if dg else self.g,
            "c": 1 - self.c if dc else self.c,
        }

    def greet(self, more=()):
        barrier = pltpu.get_barrier_semaphore()
        peers = [self.core, self.across, self.along, *more]
        for peer in peers:
            pl.semaphore_signal(barrier, inc=1, device_id=peer, device_id_type=MESH)
        pl.semaphore_wait(barrier, len(peers))


class Gather:
    COPIES = 11

    def __init__(self, place, block, out, send, recv):
        self.place, self.block, self.out, self.send, self.recv = place, block, out, send, recv
        self.tokens = block.shape[0]
        self.half = self.tokens // 2

    def rows(self, chunk, part):
        start = chunk * self.tokens + (self.half if part == 1 else 0)
        return self.out.at[pl.ds(pl.multiple_of(start, self.half), self.tokens if part == 2 else self.half)]

    def mine(self, part):
        if part == 2:
            return self.block
        return self.block.at[pl.ds(part * self.half, self.half)]

    def copy(self, number, source, chunk, part, peer):
        return pltpu.make_async_remote_copy(
            src_ref=source,
            dst_ref=self.rows(chunk, part),
            send_sem=self.send.at[number],
            recv_sem=self.recv.at[number],
            device_id=peer,
            device_id_type=MESH,
        )

    def begin(self, part):
        place = self.place
        own = place.chunk(0, 0, 0)
        self.kept = getattr(self, "kept", [])
        mine = self.mine(part)
        order = ((0 + part, place.across), (2 + part, place.along))
        for number, peer in order:
            self.kept.append((self.copy(number, mine, own, part, peer), None))
            self.kept[-1][0].start()
        self.kept.append((self.copy(4 + part, mine, own, part, place.core), None))
        self.kept[-1][0].start()
        keep = pltpu.make_async_copy(mine, self.rows(own, part), self.send.at[self.COPIES + part])
        keep.start()
        self.local = getattr(self, "local", []) + [keep]

    def arrived(self, number, chunk, part):
        self.copy(number, self.rows(chunk, part), chunk, part, self.place.core).wait_recv()

    def forward(self, number, chunk, part, peer):
        moved = self.copy(number, self.rows(chunk, part), chunk, part, peer)
        moved.start()
        self.kept.append((moved, None))

    def pass_first(self):
        place = self.place
        ax, al = place.chunk(0, 1, 0), place.chunk(1, 0, 0)
        self.arrived(0, ax, 0)
        self.forward(6, ax, 0, place.along)
        self.arrived(3, al, 1)
        self.forward(7, al, 1, place.across)

    def pass_second(self):
        place = self.place
        ax, al = place.chunk(0, 1, 0), place.chunk(1, 0, 0)
        self.arrived(1, ax, 1)
        self.forward(8, ax, 2, place.core)
        self.arrived(2, al, 0)
        self.forward(9, al, 2, place.core)

    def pass_third(self):
        dia = self.place.chunk(1, 1, 0)
        self.arrived(6, dia, 0)
        self.arrived(7, dia, 1)
        self.forward(10, dia, 2, self.place.core)

    def pass_on(self):
        self.pass_first()
        self.pass_second()
        self.pass_third()

    def finish(self):
        place = self.place
        self.arrived(4, place.chunk(0, 0, 1), 0)
        self.arrived(5, place.chunk(0, 0, 1), 1)
        self.arrived(8, place.chunk(0, 1, 1), 2)
        self.arrived(9, place.chunk(1, 0, 1), 2)
        self.arrived(10, place.chunk(1, 1, 1), 2)
        for moved, _ in self.kept:
            moved.wait_send()
        for keep in self.local:
            keep.wait()


OTHERS = [(di, dg, dc) for di in (0, 1) for dg in (0, 1) for dc in (0, 1) if di or dg or dc]


def first_gather_kernel(count, normed, ids, normed_out, ids_out, before_out, after_out, plane_ids, before, after, send, recv, ids_send, ids_recv):
    place = Place()
    me = lax.axis_index("t")
    up, down = {"t": lax.rem(me + 1, count)}, {"t": lax.rem(me + count - 1, count)}
    place.greet([place.peer(*offset) for offset in OTHERS if sum(offset) > 1] + [up, down])
    gather = Gather(place, normed, normed_out, send, recv)
    gather.begin(0)
    gather.begin(1)
    own = place.chunk(0, 0, 0)
    moved = []

    def move(number, source, target, peer):
        copy = pltpu.make_async_remote_copy(
            src_ref=source,
            dst_ref=target,
            send_sem=ids_send.at[number],
            recv_sem=ids_recv.at[number],
            device_id=peer,
            device_id_type=MESH,
        )
        copy.start()
        moved.append(copy)

    for number, offset in enumerate(OTHERS):
        move(number, ids, plane_ids.at[own], place.peer(*offset))
    plane_ids[own] = ids[...]
    for number, offset in enumerate(OTHERS):
        chunk = place.chunk(*offset)
        pltpu.make_async_remote_copy(
            src_ref=ids,
            dst_ref=plane_ids.at[chunk],
            send_sem=ids_send.at[number],
            recv_sem=ids_recv.at[number],
            device_id=place.peer(*offset),
            device_id_type=MESH,
        ).wait_recv()
    move(7, plane_ids, before, up)
    move(8, plane_ids, after, down)
    gather.pass_on()
    for copy in moved[7:]:
        copy.wait_recv()
    for copy in moved:
        copy.wait_send()
    ids_out[...] = plane_ids[...]
    before_out[...] = before[...]
    after_out[...] = after[...]
    gather.finish()


class Scatter:
    def __init__(self, place, product, core_send, core_recv, held, acc, across_recv, along_recv, second, second_recv, send, recv):
        self.place, self.product = place, product
        self.core_send, self.core_recv, self.held, self.acc = core_send, core_recv, held, acc
        self.across_recv, self.along_recv, self.second, self.second_recv = across_recv, along_recv, second, second_recv
        self.send, self.recv = send, recv
        self.kept = []

    def copy(self, number, source, target, peer):
        return pltpu.make_async_remote_copy(
            src_ref=source,
            dst_ref=target,
            send_sem=self.send.at[number],
            recv_sem=self.recv.at[number],
            device_id=peer,
            device_id_type=MESH,
        )

    def start(self, *parts):
        moved = self.copy(*parts)
        moved.start()
        self.kept.append(moved)

    def run(self):
        place = self.place
        order = ((1, 1), (0, 1), (1, 0), (0, 0))
        tile = 256
        per_half = self.held.shape[3] // tile
        def give(di, dg):
            q = 2 * di + dg
            chunk = place.chunk(di, dg, 1)

            def send_tile(n, none):
                at = pl.ds(pl.multiple_of(n % per_half * tile, tile), tile)
                self.core_send[q, n // per_half, :, at] = self.product(chunk, n).astype(BF16)
                return none

            lax.fori_loop(0, 2 * per_half, send_tile, 0)
            self.start(q, self.core_send.at[q], self.core_recv.at[q], place.core)

        def take(di, dg):
            q = 2 * di + dg
            chunk = place.chunk(di, dg, 0)
            self.copy(q, self.core_send.at[q], self.core_recv.at[q], place.core).wait_recv()

            def sum_tile(n, none):
                at = pl.ds(pl.multiple_of(n % per_half * tile, tile), tile)
                value = self.product(chunk, n) + self.core_recv[q, n // per_half, :, at].astype(F32)
                if q:
                    self.held[q - 1, n // per_half, :, at] = value.astype(BF16)
                else:
                    self.acc[n // per_half, :, at] = value
                return none

            lax.fori_loop(0, 2 * per_half, sum_tile, 0)
            if dg:
                self.start(4 + di, self.held.at[q - 1, 0], self.across_recv.at[di], place.across)
            if di:
                self.start(6 + dg, self.held.at[q - 1, 1], self.along_recv.at[dg], place.along)

        give(*order[0])
        give(*order[1])
        take(*order[0])
        give(*order[2])
        take(*order[1])
        give(*order[3])
        take(*order[2])
        take(*order[3])
        for half, number, buffer, mine, peer, out in (
            (0, 5, self.across_recv, 2, place.along, 8),
            (1, 7, self.along_recv, 1, place.across, 9),
        ):
            self.copy(number, buffer.at[1], buffer.at[1], place.core).wait_recv()

            def add_rows(n, none):
                at = pl.ds(pl.multiple_of(n * SLICE, SLICE), SLICE)
                total = self.held[mine - 1, half, at, :].astype(F32) + buffer[1, at, :].astype(F32)
                self.second[half, at, :] = total.astype(BF16)
                return none

            lax.fori_loop(0, self.held.shape[2] // SLICE, add_rows, 0)
            self.start(out, self.second.at[half], self.second_recv.at[half], peer)
        for number, buffer in ((4, self.across_recv), (6, self.along_recv)):
            self.copy(number, buffer.at[0], buffer.at[0], place.core).wait_recv()
        for number, half in ((8, 0), (9, 1)):
            self.copy(number, self.second.at[half], self.second_recv.at[half], place.core).wait_recv()

    def rows(self, at):
        first = self.acc[0, at, :] + self.across_recv[0, at, :].astype(F32) + self.second_recv[0, at, :].astype(F32)
        last = self.acc[1, at, :] + self.along_recv[0, at, :].astype(F32) + self.second_recv[1, at, :].astype(F32)
        return jnp.concatenate([first, last], axis=1)

    def finish(self):
        for moved in self.kept:
            moved.wait_send()

    @staticmethod
    def scratch(tokens, width):
        half = width // 2
        return [
            pltpu.VMEM((4, 2, tokens, half), BF16),
            pltpu.VMEM((4, 2, tokens, half), BF16),
            pltpu.VMEM((3, 2, tokens, half), BF16),
            pltpu.VMEM((2, tokens, half), F32),
            pltpu.VMEM((2, tokens, half), BF16),
            pltpu.VMEM((2, tokens, half), BF16),
            pltpu.VMEM((2, tokens, half), BF16),
            pltpu.VMEM((2, tokens, half), BF16),
            pltpu.SemaphoreType.DMA((10,)),
            pltpu.SemaphoreType.DMA((10,)),
        ]


SCATTER_BUFFERS = 10


def pair_product(lefts, rights, tokens):
    def product(chunk, n):
        at = pl.ds(pl.multiple_of(chunk * tokens, tokens), tokens)
        cols = pl.ds(pl.multiple_of(n * 256, 256), 256)
        total = None
        for left, right in zip(lefts, rights):
            term = jnp.dot(left[at, :], right[:, cols], preferred_element_type=F32)
            total = term if total is None else total + term
        return total

    return product


def for_slices(start, stop, body):
    def step(n, none):
        body(pl.ds(pl.multiple_of(n * SLICE, SLICE), SLICE))
        return none

    lax.fori_loop(start // SLICE, stop // SLICE, step, 0)


def middle_kernel(left, right, own_in, gain, middle_out, gathered, *scratch):
    buffers, (block, send, recv) = scratch[:SCATTER_BUFFERS], scratch[SCATTER_BUFFERS:]
    tokens = own_in.shape[0]
    place = Place()
    place.greet()
    scatter = Scatter(place, pair_product([left], [right], tokens), *buffers)
    scatter.run()

    def body(at):
        middle = own_in[at, :].astype(F32) + scatter.rows(at)
        middle_out[at, :] = middle
        block[at, :] = (middle * rms(middle) * gain[...]).astype(BF16)

    gather = Gather(place, block, gathered, send, recv)
    for part in (0, 1):
        for_slices(part * tokens // 2, (part + 1) * tokens // 2, body)
        gather.begin(part)
    gather.pass_on()
    scatter.finish()
    gather.finish()


def turn_kernel(left0, left1, right0, right1, middle, gain, cot, grad_middle_out, gain_out, gathered, *scratch):
    buffers, (block, send, recv) = scratch[:SCATTER_BUFFERS], scratch[SCATTER_BUFFERS:]
    tokens = cot.shape[0]
    place = Place()
    place.greet()
    scatter = Scatter(place, pair_product([left0, left1], [right0, right1], tokens), *buffers)
    scatter.run()
    gain_out[...] = jnp.zeros_like(gain_out)

    def body(at):
        values = middle[at, :]
        grad = scatter.rows(at)
        scale = rms(values)
        weighted = grad * gain[...]
        inner = jnp.mean(values * weighted, axis=-1, keepdims=True)
        total = cot[at, :].astype(F32) + scale * weighted - values * (scale * scale * scale * inner)
        grad_middle_out[at, :] = total
        block[at, :] = total.astype(BF16)
        term = grad * values * scale
        gain_out[...] += term[0:8] + term[8:16]

    gather = Gather(place, block, gathered, send, recv)
    for part in (0, 1):
        for_slices(part * tokens // 2, (part + 1) * tokens // 2, body)
        gather.begin(part)
    gather.pass_on()
    scatter.finish()
    gather.finish()


def scatter_kernel(count, *refs):
    lefts, rights, out, buffers = refs[:count], refs[count : 2 * count], refs[2 * count], refs[2 * count + 1 :]
    tokens = out.shape[0]
    place = Place()
    place.greet()
    scatter = Scatter(place, pair_product(lefts, rights, tokens), *buffers)
    scatter.run()

    def body(at):
        out[at, :] = scatter.rows(at).astype(out.dtype)

    for_slices(0, tokens, body)
    scatter.finish()


def first_gather(planes, normed, ids):
    tokens, width = normed.shape
    every = (8, *ids.shape)
    return pl.pallas_call(
        functools.partial(first_gather_kernel, planes),
        name="first_gather",
        out_shape=(jax.ShapeDtypeStruct((8 * tokens, width), BF16), *[jax.ShapeDtypeStruct(every, F32)] * 3),
        in_specs=[ANYWHERE, *whole(1)],
        out_specs=(ANYWHERE, *whole(3)),
        scratch_shapes=[pltpu.VMEM(every, F32)] * 3 + GATHER_SCRATCH + [pltpu.SemaphoreType.DMA((9,))] * 2,
        compiler_params=mixer_params(3),
    )(normed, ids)


def middle_step(mixed, w_out, own_in, gain):
    tokens, width = own_in.shape
    return pl.pallas_call(
        middle_kernel,
        name="middle_step",
        out_shape=(jax.ShapeDtypeStruct((tokens, width), F32), jax.ShapeDtypeStruct((8 * tokens, width), BF16)),
        in_specs=whole(4),
        out_specs=(pl.BlockSpec(memory_space=pltpu.VMEM), ANYWHERE),
        scratch_shapes=Scatter.scratch(tokens, width) + [pltpu.VMEM((tokens, width), BF16)] + GATHER_SCRATCH,
        compiler_params=mixer_params(4),
    )(mixed, w_out, own_in, gain[None])


def turn_step(left0, left1, right0, right1, middle, gain, cot):
    tokens, width = cot.shape
    return pl.pallas_call(
        turn_kernel,
        name="turn_step",
        out_shape=(
            jax.ShapeDtypeStruct((tokens, width), F32),
            jax.ShapeDtypeStruct((8, width), F32),
            jax.ShapeDtypeStruct((8 * tokens, width), BF16),
        ),
        in_specs=whole(7),
        out_specs=(*whole(2), ANYWHERE),
        scratch_shapes=Scatter.scratch(tokens, width) + [pltpu.VMEM((tokens, width), BF16)] + GATHER_SCRATCH,
        compiler_params=mixer_params(5),
    )(left0, left1, right0, right1, middle, gain[None], cot)


def scatter_step(number, lefts, rights):
    tokens, width = lefts[0].shape[0] // 8, rights[0].shape[1]
    return pl.pallas_call(
        functools.partial(scatter_kernel, len(lefts)),
        name="scatter_step",
        out_shape=jax.ShapeDtypeStruct((tokens, width), F32),
        in_specs=whole(2 * len(lefts)),
        out_specs=pl.BlockSpec(memory_space=pltpu.VMEM),
        scratch_shapes=Scatter.scratch(tokens, width),
        compiler_params=mixer_params(number),
    )(*lefts, *rights)


class Swap:
    def __init__(self, quarters, out, send, recv):
        self.quarters, self.out, self.send, self.recv = quarters, out, send, recv
        self.groups = quarters.shape[0]
        self.me = lax.axis_index("g") * 2 + lax.axis_index("c")

    def copy(self, step, other, slot):
        return pltpu.make_async_remote_copy(
            src_ref=self.quarters.at[other],
            dst_ref=self.out.at[:, slot],
            send_sem=self.send.at[step],
            recv_sem=self.recv.at[step],
            device_id={"g": other // 2, "c": other % 2},
            device_id_type=MESH,
        )

    def peers(self):
        others = [lax.rem(self.me + step, self.groups) for step in range(1, self.groups)]
        return [{"g": other // 2, "c": other % 2} for other in others]

    def begin(self):
        self.keep = pltpu.make_async_copy(self.quarters.at[self.me], self.out.at[:, self.me], self.send.at[0])
        self.keep.start()
        self.moved = []
        for step in range(1, self.groups):
            self.moved.append(self.copy(step, lax.rem(self.me + step, self.groups), self.me))
            self.moved[-1].start()

    def finish(self):
        for step in range(1, self.groups):
            other = lax.rem(self.me + self.groups - step, self.groups)
            self.copy(step, other, other).wait_recv()
        for copy in self.moved:
            copy.wait_send()
        self.keep.wait()


def swap_scratch(groups):
    return [pltpu.SemaphoreType.DMA((groups,)), pltpu.SemaphoreType.DMA((groups,))]


def swap_kernel(quarters, out, send, recv):
    move = Swap(quarters, out, send, recv)
    barrier = pltpu.get_barrier_semaphore()
    for peer in move.peers():
        pl.semaphore_signal(barrier, inc=1, device_id=peer, device_id_type=MESH)
    pl.semaphore_wait(barrier, move.groups - 1)
    move.begin()
    move.finish()


def swap(quarters):
    groups, kinds, part, width = quarters.shape
    return pl.pallas_call(
        swap_kernel,
        name="swap",
        out_shape=jax.ShapeDtypeStruct((kinds, groups, part, width), quarters.dtype),
        in_specs=[ANYWHERE],
        out_specs=ANYWHERE,
        scratch_shapes=swap_scratch(groups),
        compiler_params=mixer_params(6),
    )(quarters)


def small_kernel(count, with_gates, pieces, gains, gates_out, gains_out, rows_recv, gains_recv, gains_sum, gates_all, gains_all, send, recv):
    place = Place()
    me = lax.axis_index("t")
    place.greet(
        [place.peer(*offset) for offset in OTHERS if sum(offset) > 1]
        + [{"t": lax.rem(me + step, count)} for step in range(1, count)]
    )
    own = place.chunk(0, 0, 0)
    rank = place.g * 2 + place.c
    moved = []

    def move(number, source, target, peer):
        copy = pltpu.make_async_remote_copy(
            src_ref=source,
            dst_ref=target,
            send_sem=send.at[number],
            recv_sem=recv.at[number],
            device_id=peer,
            device_id_type=MESH,
        )
        return copy

    def start(*parts):
        copy = move(*parts)
        copy.start()
        moved.append(copy)

    for number, offset in enumerate(OTHERS):
        peer, chunk = place.peer(*offset), place.chunk(*offset)
        start(number, gains.at[chunk], gains_recv.at[own], peer)
        if with_gates and not offset[0]:
            start(7 + number, pieces.at[lax.rem(chunk, 4)], rows_recv.at[rank], peer)
    gains_recv[own] = gains[own]
    if with_gates:
        rows_recv[rank] = pieces[rank]
    for number, offset in enumerate(OTHERS):
        peer, chunk = place.peer(*offset), place.chunk(*offset)
        move(number, gains.at[chunk], gains_recv.at[chunk], peer).wait_recv()
        if with_gates and not offset[0]:
            other = lax.rem(chunk, 4)
            move(7 + number, pieces.at[other], rows_recv.at[other], peer).wait_recv()
    total = gains_recv[0]
    for n in range(1, 8):
        total = total + gains_recv[n]
    gains_sum[...] = total
    for step in range(1, count):
        to = lax.rem(me + step, count)
        start(10 + 2 * step, gains_sum, gains_all.at[me], {"t": to})
        if with_gates:
            start(11 + 2 * step, rows_recv.at[to], gates_all.at[me], {"t": to})
    gains_all[me] = total
    if with_gates:
        gates_all[me] = rows_recv[me]
    for step in range(1, count):
        other = lax.rem(me + count - step, count)
        move(10 + 2 * step, gains_sum, gains_all.at[other], {"t": other}).wait_recv()
        if with_gates:
            move(11 + 2 * step, rows_recv.at[other], gates_all.at[other], {"t": other}).wait_recv()
    row = gains_all[0, pl.ds(me, 1), :]
    for z in range(1, count):
        row = row + gains_all[z, pl.ds(me, 1), :]
    gains_out[...] = jnp.broadcast_to(row, gains_out.shape)
    if with_gates:
        gates = gates_all[0].astype(F32)
        for z in range(1, count):
            gates = gates + gates_all[z].astype(F32)
        gates_out[...] = gates
    else:
        gates_out[...] = jnp.zeros_like(gates_out)
    for copy in moved:
        copy.wait_send()


def small_step(planes, pieces, gains):
    with_gates = pieces.shape[0] == planes
    slots = max(planes, 4) if with_gates else 1
    block = pieces.shape[1:] if with_gates else (16, LANES)
    pieces = pieces if with_gates else jnp.zeros((1, *block), BF16)
    sems = 12 + 2 * planes
    return pl.pallas_call(
        functools.partial(small_kernel, planes, with_gates),
        name="small_step",
        out_shape=(jax.ShapeDtypeStruct(block, F32), jax.ShapeDtypeStruct((8, LANES), F32)),
        in_specs=whole(2),
        out_specs=tuple(whole(2)),
        scratch_shapes=[
            pltpu.VMEM((slots, *block), BF16),
            pltpu.VMEM(gains.shape, F32),
            pltpu.VMEM(gains.shape[1:], F32),
            pltpu.VMEM((slots, *block), BF16),
            pltpu.VMEM((planes, *gains.shape[1:]), F32),
            pltpu.SemaphoreType.DMA((sems,)),
            pltpu.SemaphoreType.DMA((sems,)),
        ],
        compiler_params=mixer_params(9),
    )(pieces, gains)


def rms(values):
    return lax.rsqrt(jnp.mean(values * values, axis=-1, keepdims=True) + EPS)


def rms_back(values, scale, gain, grad):
    weighted = grad * gain
    inner = jnp.mean(values * weighted, axis=-1, keepdims=True)
    return scale * weighted - values * (scale * scale * scale * inner), jnp.sum(grad * values * scale, axis=0)


def nt(left, right, out):
    return lax.dot_general(left, right, (((1,), (1,)), ((), ())), preferred_element_type=F32).astype(out)


def tn(left, right, out):
    return lax.dot_general(left, right, (((0,), (0,)), ((), ())), preferred_element_type=F32).astype(out)


def nn(left, right, out):
    return jnp.dot(left, right, preferred_element_type=F32).astype(out)


def per_device(
    inputs, segment_ids, mix_gain, in_weight, conv_weight, conv_bias, gate_weight, gate_bias, decay_param, out_weight,
    mlp_gain, mlp_in, down_weight, cotangent,
):
    planes = lax.axis_size("t")
    rows_here, seg, width = inputs.shape
    row_groups = lax.axis_size("g") * lax.axis_size("c")
    own_tokens = rows_here * seg
    recur_width = conv_weight.shape[1]
    block_width = gate_weight.shape[0]
    members = 2 * row_groups
    channels = recur_width // members
    t, i = lax.axis_index("t"), lax.axis_index("i")
    r = lax.axis_index("g") * lax.axis_size("c") + lax.axis_index("c")
    member = 2 * r + i
    first = member * channels

    own_in = inputs.reshape(own_tokens, width)
    flat_in = own_in.astype(F32)
    scale_in = rms(flat_in)
    cot_own = cotangent.reshape(own_tokens, width)
    own_ids = jnp.pad((segment_ids + 1).astype(F32), ((0, 8 - rows_here), (0, 0)))

    normed, *ids = first_gather(planes, (flat_in * scale_in * mix_gain).astype(BF16), own_ids)
    mlp_in, down_weight, normed = lax.optimization_barrier((mlp_in, down_weight, normed))

    direct = planes == row_groups
    in_own = in_weight.transpose(1, 2, 0)
    out_own = out_weight.T[None]
    part = channels // row_groups if direct else 0

    def quarter(weight, part):
        return lax.dynamic_slice_in_dim(weight, r * part, part, weight.ndim - 1)

    def spread_units(weight):
        return lax.all_gather(weight, "t", axis=0, tiled=False)

    def whole_units(weight):
        every = lax.all_gather(weight, ("t", "i"), axis=1, tiled=True)
        return lax.dynamic_slice_in_dim(every, first, channels, 1)

    if direct:
        in_w = swap(spread_units(quarter(in_weight, part).transpose(1, 2, 0)))
        out_quarters = spread_units(quarter(out_weight, part).T[None])
    else:
        in_w = whole_units(in_own)
        out_quarters = jnp.zeros((row_groups, 1, 16, width), BF16)
    w_gate, w_recur = in_w.reshape(2, channels, width)
    hidden_part = mlp_in.shape[2] // row_groups
    mlp_w = spread_units(quarter(mlp_in, hidden_part).transpose(1, 2, 0))
    w_left = mlp_w[:, 0].reshape(-1, width)
    w_right = mlp_w[:, 1].reshape(-1, width)
    w_down = spread_units(quarter(down_weight, hidden_part).T).reshape(-1, width)

    def own(values):
        return lax.dynamic_slice_in_dim(values, first, channels, values.ndim - 1)

    decay_own = own(decay_param)
    vec = jnp.concatenate(
        [
            own(conv_weight),
            own(conv_bias)[None],
            own(gate_bias),
            8.0 * jax.nn.softplus(-decay_own)[None],
            8.0 * jax.nn.sigmoid(-decay_own)[None],
            jnp.zeros((7, channels), F32),
        ]
    )
    blocks = channels // block_width
    gate_own = own(gate_weight).reshape(block_width, 2, blocks, block_width)
    spread = jnp.zeros((2, blocks, block_width, blocks, block_width), BF16)
    for n in range(blocks):
        spread = spread.at[:, n, :, n, :].set(gate_own[:, :, n, :].transpose(1, 0, 2))
    spread = spread.reshape(2, channels, channels)
    wg0, wg1 = spread[0], spread[1]

    gate_branch = nt(normed, w_gate, F32)
    recur = nt(normed, w_recur, BF16)
    conv_low, decay, states, mixed, halo, cin, mask, cot, w_out = mixer_forward(
        planes, seg, rows_here, recur, gate_branch, ids, wg0, wg1, vec, cot_own, out_quarters
    )
    w_out = (w_out if direct else whole_units(out_own)).reshape(channels, width)
    middle, normed_two = middle_step(mixed, w_out, own_in, mlp_gain)
    left = nt(normed_two, w_left, F32)
    right = nt(normed_two, w_right, F32)
    act, slope = gelu_parts(left)
    hidden = (act * right).astype(BF16)

    def over_planes(grad):
        return lax.psum_scatter(grad, "t", scatter_dimension=0, tiled=True)

    def to_owners(reduced):
        return lax.all_to_all(reduced.reshape(members, -1, reduced.shape[1]), PLANE, 0, 0, tiled=True)

    grad_down = tn(cot, hidden, BF16)
    grad_down, hidden, w_down = lax.optimization_barrier((grad_down, hidden, w_down))
    grad_down = over_planes(grad_down)
    grad_hidden = nt(cot, w_down, F32)
    grad_left = (grad_hidden * right * slope).astype(BF16)
    grad_right = (grad_hidden * act).astype(BF16)
    grad_mlp_in = jnp.concatenate([tn(normed_two, grad_left, BF16), tn(normed_two, grad_right, BF16)], axis=1)
    grad_mlp_in, grad_left, grad_right = lax.optimization_barrier((grad_mlp_in, grad_left, grad_right))
    grad_mlp_in = over_planes(grad_mlp_in)
    grad_middle, grad_mlp_gain, grad_mid = turn_step(grad_left, grad_right, w_left, w_right, middle, mlp_gain, cot_own)
    grad_down, grad_mid = lax.optimization_barrier((grad_down, grad_mid))
    grad_mlp_gain = jnp.sum(grad_mlp_gain, axis=0)
    grad_out = tn(grad_mid, mixed, BF16)
    grad_mixed = nt(grad_mid, w_out, F32)
    grad_out, grad_mixed = lax.optimization_barrier((grad_out, grad_mixed))
    grad_out = over_planes(grad_out)
    grad_gate, grad_recur, gw0, gw1, small = mixer_backward(
        planes, seg, grad_mixed, gate_branch, states, decay, conv_low, recur, halo, cin, mask, wg0, wg1, wg0.T, wg1.T, vec
    )
    grad_mlp_in, grad_gate, grad_recur = lax.optimization_barrier((grad_mlp_in, grad_gate, grad_recur))
    grad_in = jnp.concatenate([tn(normed, grad_gate, BF16), tn(normed, grad_recur, BF16)], axis=1)
    grad_in, grad_gate, grad_recur = lax.optimization_barrier((grad_in, grad_gate, grad_recur))
    grad_in = over_planes(grad_in)
    grad_normed = scatter_step(7, [grad_gate, grad_recur], [w_gate, w_recur])
    grad_in_norm, grad_mix_gain = rms_back(flat_in, scale_in, mix_gain, grad_normed)
    grad_inputs = (grad_middle + grad_in_norm).reshape(inputs.shape)
    grad_out, hidden, grad_normed = lax.optimization_barrier((grad_out, hidden, grad_normed))
    down = scatter_step(8, [hidden], [w_down])
    outputs = (middle + down).astype(BF16).reshape(inputs.shape)

    own_rows = width // (planes * members)

    def hidden_order(reduced, kinds):
        grad = to_owners(reduced).reshape(2, row_groups, own_rows, kinds, planes, hidden_part).astype(F32)
        return grad.transpose(2, 3, 4, 0, 1, 5).reshape(own_rows, kinds, -1)

    def channel_order(reduced, kinds):
        grad = to_owners(reduced).reshape(2, row_groups, own_rows, kinds, channels).astype(F32)
        return grad.transpose(2, 3, 1, 0, 4).reshape(own_rows, kinds, -1)

    column_block = lax.broadcasted_iota(jnp.int32, (block_width, channels), 1) // block_width

    def diagonal(gw):
        return sum(
            jnp.where(column_block == n, gw[n * block_width : (n + 1) * block_width], 0.0) for n in range(blocks)
        )

    gate_grads = jnp.concatenate([diagonal(gw0), diagonal(gw1), small], axis=0)
    pieces = jnp.zeros((0, 8, LANES), F32)
    if direct:
        pieces = gate_grads.reshape(gate_grads.shape[0], row_groups, -1).transpose(1, 0, 2)
        pieces = jnp.pad(pieces.astype(BF16), ((0, 0), (0, -pieces.shape[1] % 16), (0, LANES - part)))
    gains = jnp.stack([grad_mlp_gain, grad_mix_gain]).reshape(2, planes, members, own_rows)
    gains = gains.transpose(2, 1, 0, 3).reshape(members, planes, 2 * own_rows)
    short = LANES - 2 * own_rows
    gains = jnp.pad(gains, ((0, 0), (0, -planes % 8), (0, short)))
    gate_sums, gains = small_step(planes, pieces, gains)
    if direct:
        gate_grads = gate_sums[:, :part]
    else:
        placed = jnp.zeros((gate_grads.shape[0], recur_width), F32)
        placed = lax.dynamic_update_slice_in_dim(placed, gate_grads, first, 1)
        gate_grads = lax.psum_scatter(placed, EVERY, scatter_dimension=1, tiled=True)
    grad_gate_weight = jnp.stack([gate_grads[:block_width], gate_grads[block_width : 2 * block_width]], axis=1)
    small = gate_grads[2 * block_width : 2 * block_width + 8]
    mlp_in_grads = hidden_order(grad_mlp_in, 2)
    return (
        outputs,
        grad_inputs,
        gains[0, own_rows : 2 * own_rows],
        channel_order(grad_in, 2),
        small[0:4],
        small[4],
        grad_gate_weight,
        small[5:7],
        small[7],
        channel_order(grad_out, 1)[:, 0],
        gains[0, :own_rows],
        mlp_in_grads,
        hidden_order(grad_down, 1)[:, 0],
    )


def solution(mesh):
    seq, rows = mesh.shape["seq"], mesh.shape["rows"]
    grid = Mesh(mesh.devices.reshape(seq // 2, 2, rows // 2, 2), EVERY)
    row_axes, seq_axes = ("g", "c"), ("t", "i")
    tokens = P(row_axes, seq_axes, None)
    return jax.shard_map(
        per_device,
        mesh=grid,
        in_specs=(
            tokens,
            P(row_axes, seq_axes),
            P(),
            P(None, None, seq_axes),
            P(),
            P(),
            P(),
            P(),
            P(),
            P(None, seq_axes),
            P(),
            P(None, None, seq_axes),
            P(None, seq_axes),
            tokens,
        ),
        out_specs=(
            tokens,
            tokens,
            P(EVERY),
            P(EVERY, None, None),
            P(None, EVERY),
            P(EVERY),
            P(None, None, EVERY),
            P(None, EVERY),
            P(EVERY),
            P(EVERY, None),
            P(EVERY),
            P(EVERY, None, None),
            P(EVERY, None),
        ),
        check_vma=False,
    )
```

```python
import functools

import jax
import jax.numpy as jnp
from jax import lax
from jax.experimental import pallas as pl
from jax.experimental.pallas import tpu as pltpu
from jax.sharding import Mesh
from jax.sharding import PartitionSpec as P

EPS = 1e-06
MESH = pl.DeviceIdType.MESH
PLANE = ("i", "g", "c")
EVERY = ("t", "i", "g", "c")
F32 = jnp.float32
BF16 = jnp.bfloat16
GELU_A = 0.7978845608028654
GELU_B = 0.044715
HALO = 8
LANES = 128
SLICE = 16
ANYWHERE = pl.BlockSpec(memory_space=pl.ANY)
GATHER_SCRATCH = [pltpu.SemaphoreType.DMA((13,))] * 2


def gelu_parts(x):
    square = x * x
    th = jnp.tanh(GELU_A * x * (1.0 + GELU_B * square))
    half = 0.5 * (1.0 + th)
    slope = half + 0.5 * x * (1.0 - th * th) * (GELU_A * (1.0 + 3.0 * GELU_B * square))
    return x * half, slope


def one_minus_exp(y):
    series = 1.0 + y * (-1.0 / 2 + y * (1.0 / 6 + y * (-1.0 / 24 + y * (1.0 / 120 + y * (-1.0 / 720 + y * (1.0 / 5040))))))
    return jnp.where(y < 0.35, y * series, 1.0 - jnp.exp(-y))


def sigmoid(x):
    return 1.0 / (1.0 + jnp.exp(-x))


def gate_values(conv_low, wg0, wg1, vec):
    logits0 = jnp.dot(conv_low, wg0, preferred_element_type=F32) + vec[5:6]
    logits1 = jnp.dot(conv_low, wg1, preferred_element_type=F32) + vec[6:7]
    recur_gate = sigmoid(logits0)
    input_gate = sigmoid(logits1)
    log_decay = -vec[7:8] * recur_gate
    return recur_gate, input_gate, log_decay


def greet(count):
    me = lax.axis_index("t")
    barrier = pltpu.get_barrier_semaphore()
    for step in range(1, count):
        pl.semaphore_signal(barrier, inc=1, device_id={"t": lax.rem(me + step, count)}, device_id_type=MESH)
    pl.semaphore_wait(barrier, count - 1)
    return me


def put_tiles(ref, at, values):
    tiles, lanes = ref.shape[0], ref.shape[2]
    short = tiles * lanes - values.shape[1]
    if short:
        values = jnp.concatenate([values, jnp.zeros((values.shape[0], short), values.dtype)], axis=1)
    for j in range(tiles):
        ref[j, at, :] = values[:, j * lanes : (j + 1) * lanes]


def get_tiles(ref, at, width):
    joined = jnp.concatenate([ref[j, at, :] for j in range(ref.shape[0])], axis=1)
    return joined[:, :width]


def join_tiles(parts, width):
    return jnp.concatenate(parts, axis=1)[:, :width]


def exchange(count, me, send, slots, send_sem, recv_sem):
    for step in range(1, count):
        pltpu.make_async_remote_copy(
            src_ref=send,
            dst_ref=slots.at[me],
            send_sem=send_sem.at[step],
            recv_sem=recv_sem.at[step],
            device_id={"t": lax.rem(me + step, count)},
            device_id_type=MESH,
        ).start()
    for step in range(1, count):
        other = lax.rem(me + count - step, count)
        pltpu.make_async_remote_copy(
            src_ref=send,
            dst_ref=slots.at[other],
            send_sem=send_sem.at[step],
            recv_sem=recv_sem.at[step],
            device_id={"t": other},
            device_id_type=MESH,
        ).wait()


def mixer_forward_kernel(
    count, seg, rows_here, recur, gate, ids, ids_before, ids_after, wg0, wg1, vec_ref, cot, quarters,
    conv_out, decay_out, states_out, mixed_out, halo_out, cin_out, mask, cot_out, swapped,
    drive, h_ref, a_ref, ext, halo_send, halo_recv, summary, slots, send_sem, recv_sem, halo_sems,
    gather_send, gather_recv, swap_send, swap_recv,
):
    place = Place()
    me = lax.axis_index("t")
    place.greet([place.peer(0, 1, 1)] + [{"t": lax.rem(me + step, count)} for step in range(1, count)])
    gather = Gather(place, cot, cot_out, gather_send, gather_recv)
    move = Swap(quarters, swapped, swap_send, swap_recv)
    rows = 8
    for r in range(rows):
        halo_send[r * HALO : (r + 1) * HALO, :] = recur[
            (rows + r) * seg + seg - 16 : (rows + r) * seg + seg, :
        ].astype(F32)[16 - HALO :]
    halo_copy = pltpu.make_async_remote_copy(
        src_ref=halo_send,
        dst_ref=halo_recv,
        send_sem=halo_sems.at[0],
        recv_sem=halo_sems.at[1],
        device_id={"t": lax.rem(me + 1, count)},
        device_id_type=MESH,
    )
    halo_copy.start()
    gather.begin(0)
    gather.begin(1)
    move.begin()
    halo_copy.wait()
    for r in range(rows):
        halo_out[r * HALO : (r + 1) * HALO, :] = halo_recv[r * HALO : (r + 1) * HALO, :]
        halo_out[(rows + r) * HALO : (rows + r + 1) * HALO, :] = recur[r * seg + seg - 16 : r * seg + seg, :].astype(F32)[
            16 - HALO :
        ]
    vec = vec_ref[...]

    def ids_of(ref, s):
        chunk = s // rows_here
        return ref[chunk, s % rows_here : s % rows_here + 1, :]

    nothing = jnp.zeros((1, LANES), F32)
    for s in range(2 * rows):
        here = ids_of(ids, s)
        back = ids_of(ids, s - rows) if s >= rows else jnp.where(me > 0, ids_of(ids_before, s + rows), nothing)
        ahead = ids_of(ids, s + rows) if s < rows else jnp.where(me < count - 1, ids_of(ids_after, s - rows), nothing)
        lines = [jnp.concatenate([back[:, seg - k :], here[:, : seg - k]], axis=1) for k in (1, 2, 3)]
        lines += [jnp.concatenate([here[:, k:], ahead[:, :k]], axis=1) for k in (1, 2, 3)]
        lines = [jnp.where(line == here, 1.0, 0.0) for line in lines] + [nothing] * 2
        mask[s * seg : (s + 1) * seg, :] = jnp.concatenate(lines, axis=0).T

    def local(s, none):
        at = pl.ds(pl.multiple_of(s * seg, seg), seg)
        x = recur[at, :].astype(F32)
        ext[0:HALO, :] = halo_out[pl.ds(pl.multiple_of(s * HALO, HALO), HALO), :]
        ext[HALO : HALO + seg, :] = x
        m = mask[at, :]
        conv = vec[4:5] + vec[0:1] * x
        for k in range(1, 4):
            conv = conv + vec[k : k + 1] * ext[HALO - k : HALO - k + seg, :] * m[:, k - 1 : k]
        conv_low = conv.astype(BF16)
        conv_out[at, :] = conv_low
        recur_gate, input_gate, log_decay = gate_values(conv_low, wg0[...], wg1[...], vec)
        keep = m[:, 0:1]
        put_tiles(decay_out, at, jnp.exp(log_decay) * keep)
        scale = (1.0 - keep) + keep * jnp.sqrt(one_minus_exp(-2.0 * log_decay))
        put_tiles(drive, at, scale * input_gate * conv_low.astype(F32))
        return none

    lax.fori_loop(0, 2 * rows, local, 0)
    gather.pass_first()
    tiles, lanes = drive.shape[0], drive.shape[2]

    def scan(k, carried):
        at = pl.ds(k, 2 * rows, stride=seg)
        after = []
        for j in range(tiles):
            h, a = carried[j]
            d = decay_out[j, at, :]
            h = d * h + drive[j, at, :]
            a = a * d
            h_ref[j, at, :] = h
            a_ref[j, at, :] = a
            after.append((h, a))
        return tuple(after)

    width = recur.shape[1]
    start = (jnp.zeros((2 * rows, lanes), F32), jnp.ones((2 * rows, lanes), F32))
    last = lax.fori_loop(0, seg, scan, (start,) * tiles, unroll=4)
    last_h = join_tiles([part[0] for part in last], width)
    last_a = join_tiles([part[1] for part in last], width)
    summary[0:rows, :] = last_a[rows:] * last_a[:rows]
    summary[rows : 2 * rows, :] = last_a[rows:] * last_h[:rows] + last_h[rows:]
    gather.pass_second()
    exchange(count, me, summary, slots, send_sem, recv_sem)
    carry = jnp.zeros((rows, width), F32)
    for z in range(count - 1):
        carry = jnp.where(z < me, slots[z, 0:rows, :] * carry + slots[z, rows : 2 * rows, :], carry)
    cin_out[0:rows, :] = carry
    cin_out[rows : 2 * rows, :] = last_a[:rows] * carry + last_h[:rows]

    def finish(s, none):
        at = pl.ds(pl.multiple_of(s * seg, seg), seg)
        states = get_tiles(h_ref, at, width) + get_tiles(a_ref, at, width) * cin_out[pl.ds(s, 1), :]
        states_out[at, :] = states
        act, _ = gelu_parts(gate[at, :])
        mixed_out[at, :] = (act * states.astype(BF16).astype(F32)).astype(BF16)
        return none

    lax.fori_loop(0, 2 * rows, finish, 0)
    gather.pass_third()
    gather.finish()
    move.finish()


def mixer_backward_kernel(
    count, seg, grad_mixed, gate, states, decay, conv_low_ref, recur, halo, cin, mask, wg0, wg1, wg0t, wg1t, vec_ref,
    hidden, w_down, grad_gate_out, grad_recur_out, gw0_out, gw1_out, small_out, down_out,
    tot, prod, ext, halo_send, halo_recv, summary, slots, uin, send_sem, recv_sem, halo_sems, *buffers,
):
    place = Place()
    me = lax.axis_index("t")
    place.greet([{"t": lax.rem(me + step, count)} for step in range(1, count)])
    scatter = Scatter(place, pair_product([hidden], [w_down], down_out.shape[0]), *buffers)
    scatter.run_first()
    rows = 8
    width = recur.shape[1]
    vec = vec_ref[...]

    def local(s, none):
        at = pl.ds(pl.multiple_of(s * seg, seg), seg)
        act, slope = gelu_parts(gate[at, :])
        gm = grad_mixed[at, :].astype(F32)
        grad_gate_out[at, :] = (gm * states[at, :].astype(BF16).astype(F32) * slope).astype(BF16)
        put_tiles(tot, at, (gm * act).astype(BF16).astype(F32))
        return none

    lax.fori_loop(0, 2 * rows, local, 0)

    tiles, lanes = tot.shape[0], tot.shape[2]

    def scan(k, carried):
        at = pl.ds(seg - 1 - k, 2 * rows, stride=seg)
        after = []
        for j in range(tiles):
            u, p = carried[j]
            d = decay[j, at, :]
            total = tot[j, at, :] + u
            tot[j, at, :] = total
            prod[j, at, :] = p
            after.append((d * total, d * p))
        return tuple(after)

    start = (jnp.zeros((2 * rows, lanes), F32), jnp.ones((2 * rows, lanes), F32))
    last = lax.fori_loop(0, seg, scan, (start,) * tiles, unroll=4)
    u = join_tiles([part[0] for part in last], width)
    p = join_tiles([part[1] for part in last], width)
    scatter.run_second()
    summary[0:rows, :] = p[:rows] * p[rows:]
    summary[rows : 2 * rows, :] = p[:rows] * u[rows:] + u[:rows]
    exchange(count, me, summary, slots, send_sem, recv_sem)
    carry = jnp.zeros((rows, width), F32)
    for z in range(count - 1, 0, -1):
        carry = jnp.where(z > me, slots[z, 0:rows, :] * carry + slots[z, rows : 2 * rows, :], carry)
    uin[rows : 2 * rows, :] = carry
    uin[0:rows, :] = p[rows:] * carry + u[rows:]
    gw0_out[...] = jnp.zeros_like(gw0_out)
    gw1_out[...] = jnp.zeros_like(gw1_out)
    small_out[...] = jnp.zeros_like(small_out)

    def gates(s, none):
        at = pl.ds(pl.multiple_of(s * seg, seg), seg)
        total = get_tiles(tot, at, width) + get_tiles(prod, at, width) * uin[pl.ds(s, 1), :]
        ext[HALO - 1 : HALO, :] = cin[pl.ds(s, 1), :]
        ext[HALO : HALO + seg, :] = states[at, :]
        before = ext[HALO - 1 : HALO - 1 + seg, :]
        conv_low = conv_low_ref[at, :]
        conv_vals = conv_low.astype(F32)
        m = mask[at, :]
        keep = m[:, 0:1]
        recur_gate, input_gate, log_decay = gate_values(conv_low, wg0[...], wg1[...], vec)
        root = jnp.sqrt(one_minus_exp(-2.0 * log_decay))
        scale = (1.0 - keep) + keep * root
        driven_in = total * conv_vals
        grad_log = total * before * get_tiles(decay, at, width) - driven_in * input_gate * keep * (jnp.exp(2.0 * log_decay) / root)
        grad0 = grad_log * log_decay * (1.0 - recur_gate)
        grad1 = driven_in * scale * input_gate * (1.0 - input_gate)
        low0 = grad0.astype(BF16)
        low1 = grad1.astype(BF16)
        grad_conv = (
            total * scale * input_gate
            + jnp.dot(low0, wg0t[...], preferred_element_type=F32)
            + jnp.dot(low1, wg1t[...], preferred_element_type=F32)
        )
        put_tiles(tot, at, grad_conv)
        turned = (((0,), (0,)), ((), ()))
        gw0_out[...] += lax.dot_general(conv_low, low0, turned, preferred_element_type=F32)
        gw1_out[...] += lax.dot_general(conv_low, low1, turned, preferred_element_type=F32)
        x = recur[at, :].astype(F32)
        ext[0:HALO, :] = halo[pl.ds(pl.multiple_of(s * HALO, HALO), HALO), :]
        ext[HALO : HALO + seg, :] = x

        def add(row, values):
            small_out[row : row + 1, :] += jnp.sum(values, axis=0, keepdims=True)

        add(0, grad_conv * x)
        for k in range(1, 4):
            add(k, grad_conv * ext[HALO - k : HALO - k + seg, :] * m[:, k - 1 : k])
        add(4, grad_conv)
        add(5, grad0)
        add(6, grad1)
        add(7, grad_log * recur_gate)
        return none

    lax.fori_loop(0, 2 * rows, gates, 0)
    small_out[7:8, :] = small_out[7:8, :] * vec[8:9]
    for r in range(rows):
        halo_send[r * HALO : (r + 1) * HALO, :] = get_tiles(tot, pl.ds(r * seg, HALO), width)
    halo_copy = pltpu.make_async_remote_copy(
        src_ref=halo_send,
        dst_ref=halo_recv,
        send_sem=halo_sems.at[0],
        recv_sem=halo_sems.at[1],
        device_id={"t": lax.rem(me + count - 1, count)},
        device_id_type=MESH,
    )
    halo_copy.start()
    halo_copy.wait()

    def back(s, none):
        at = pl.ds(pl.multiple_of(s * seg, seg), seg)
        m = mask[at, :]
        grad_conv = get_tiles(tot, at, width)
        ext[0:seg, :] = grad_conv
        result = vec[0:1] * grad_conv

        @pl.when(s < rows)
        def _():
            ext[seg : seg + HALO, :] = get_tiles(tot, pl.ds(pl.multiple_of((s + rows) * seg, seg), HALO), width)

        @pl.when(s >= rows)
        def _():
            ext[seg : seg + HALO, :] = halo_recv[pl.ds(pl.multiple_of((s - rows) * HALO, HALO), HALO), :]

        for k in range(1, 4):
            result = result + vec[k : k + 1] * ext[k : k + seg, :] * m[:, 2 + k : 3 + k]
        grad_recur_out[at, :] = result.astype(BF16)
        return none

    lax.fori_loop(0, 2 * rows, back, 0)
    scatter.run_third()

    def body(at):
        down_out[at, :] = scatter.rows(at)

    for_slices(0, down_out.shape[0], body)
    scatter.finish()


def whole(count):
    return [pl.BlockSpec(memory_space=pltpu.VMEM)] * count


def mixer_params(number):
    return pltpu.CompilerParams(collective_id=number, has_side_effects=True, vmem_limit_bytes=60 * 1024 * 1024)


def mixer_forward(count, seg, rows_here, recur, gate, ids, wg0, wg1, vec, cot, quarters):
    n, width = recur.shape
    full = functools.partial(jax.ShapeDtypeStruct, (n, width))
    tiles = -(-width // LANES)
    tiled = jax.ShapeDtypeStruct((tiles, n, LANES), F32)
    groups, kinds, part, depth = quarters.shape
    return pl.pallas_call(
        functools.partial(mixer_forward_kernel, count, seg, rows_here),
        name="mixer_forward",
        out_shape=(
            full(BF16), tiled, full(F32), full(BF16),
            jax.ShapeDtypeStruct((16 * HALO, width), F32), jax.ShapeDtypeStruct((16, width), F32),
            jax.ShapeDtypeStruct((n, 8), F32),
            jax.ShapeDtypeStruct((8 * cot.shape[0], cot.shape[1]), BF16),
            jax.ShapeDtypeStruct((kinds, groups, part, depth), BF16),
        ),
        in_specs=whole(8) + [ANYWHERE] * 2,
        out_specs=(*whole(7), ANYWHERE, ANYWHERE),
        scratch_shapes=[
            pltpu.VMEM((tiles, n, LANES), F32),
            pltpu.VMEM((tiles, n, LANES), F32),
            pltpu.VMEM((tiles, n, LANES), F32),
            pltpu.VMEM((seg + HALO, width), F32),
            pltpu.VMEM((8 * HALO, width), F32),
            pltpu.VMEM((8 * HALO, width), F32),
            pltpu.VMEM((16, width), F32),
            pltpu.VMEM((count, 16, width), F32),
            pltpu.SemaphoreType.DMA((count,)),
            pltpu.SemaphoreType.DMA((count,)),
            pltpu.SemaphoreType.DMA((2,)),
            *GATHER_SCRATCH,
            *swap_scratch(groups),
        ],
        compiler_params=mixer_params(1),
    )(recur, gate, *ids, wg0, wg1, vec, cot, quarters)


def mixer_backward(count, seg, grad_mixed, gate, states, decay, conv_low, recur, halo, cin, mask, wg0, wg1, wg0t, wg1t, vec, hidden, w_down):
    n, width = recur.shape
    tokens, depth = n // 8, w_down.shape[1]
    full = functools.partial(jax.ShapeDtypeStruct, (n, width))
    tiles = -(-width // LANES)
    tiled = jax.ShapeDtypeStruct((tiles, n, LANES), F32)
    return pl.pallas_call(
        functools.partial(mixer_backward_kernel, count, seg),
        name="mixer_backward",
        out_shape=(
            full(BF16), full(BF16),
            jax.ShapeDtypeStruct((width, width), F32), jax.ShapeDtypeStruct((width, width), F32),
            jax.ShapeDtypeStruct((8, width), F32), jax.ShapeDtypeStruct((tokens, depth), F32),
        ),
        in_specs=whole(16),
        out_specs=tuple(whole(6)),
        scratch_shapes=[
            pltpu.VMEM((tiles, n, LANES), F32),
            pltpu.VMEM((tiles, n, LANES), F32),
            pltpu.VMEM((seg + HALO, width), F32),
            pltpu.VMEM((8 * HALO, width), F32),
            pltpu.VMEM((8 * HALO, width), F32),
            pltpu.VMEM((16, width), F32),
            pltpu.VMEM((count, 16, width), F32),
            pltpu.VMEM((16, width), F32),
            pltpu.SemaphoreType.DMA((count,)),
            pltpu.SemaphoreType.DMA((count,)),
            pltpu.SemaphoreType.DMA((2,)),
            *Scatter.scratch(tokens, depth),
        ],
        compiler_params=mixer_params(2),
    )(grad_mixed, gate, states, decay, conv_low, recur, halo, cin, mask, wg0, wg1, wg0t, wg1t, vec, hidden, w_down)


class Place:
    def __init__(self):
        self.i, self.g, self.c = lax.axis_index("i"), lax.axis_index("g"), lax.axis_index("c")
        self.core, self.across, self.along = {"c": 1 - self.c}, {"g": 1 - self.g}, {"i": 1 - self.i}

    def chunk(self, di, dg, dc):
        i = 1 - self.i if di else self.i
        g = 1 - self.g if dg else self.g
        c = 1 - self.c if dc else self.c
        return (i * 2 + g) * 2 + c

    def peer(self, di, dg, dc):
        return {
            "i": 1 - self.i if di else self.i,
            "g": 1 - self.g if dg else self.g,
            "c": 1 - self.c if dc else self.c,
        }

    def greet(self, more=()):
        barrier = pltpu.get_barrier_semaphore()
        peers = [self.core, self.across, self.along, *more]
        for peer in peers:
            pl.semaphore_signal(barrier, inc=1, device_id=peer, device_id_type=MESH)
        pl.semaphore_wait(barrier, len(peers))


class Gather:
    COPIES = 11

    def __init__(self, place, block, out, send, recv):
        self.place, self.block, self.out, self.send, self.recv = place, block, out, send, recv
        self.tokens = block.shape[0]
        self.half = self.tokens // 2

    def rows(self, chunk, part):
        start = chunk * self.tokens + (self.half if part == 1 else 0)
        return self.out.at[pl.ds(pl.multiple_of(start, self.half), self.tokens if part == 2 else self.half)]

    def mine(self, part):
        if part == 2:
            return self.block
        return self.block.at[pl.ds(part * self.half, self.half)]

    def copy(self, number, source, chunk, part, peer):
        return pltpu.make_async_remote_copy(
            src_ref=source,
            dst_ref=self.rows(chunk, part),
            send_sem=self.send.at[number],
            recv_sem=self.recv.at[number],
            device_id=peer,
            device_id_type=MESH,
        )

    def begin(self, part):
        place = self.place
        own = place.chunk(0, 0, 0)
        self.kept = getattr(self, "kept", [])
        mine = self.mine(part)
        order = ((0 + part, place.across), (2 + part, place.along))
        for number, peer in order:
            self.kept.append((self.copy(number, mine, own, part, peer), None))
            self.kept[-1][0].start()
        self.kept.append((self.copy(4 + part, mine, own, part, place.core), None))
        self.kept[-1][0].start()
        keep = pltpu.make_async_copy(mine, self.rows(own, part), self.send.at[self.COPIES + part])
        keep.start()
        self.local = getattr(self, "local", []) + [keep]

    def arrived(self, number, chunk, part):
        self.copy(number, self.rows(chunk, part), chunk, part, self.place.core).wait_recv()

    def forward(self, number, chunk, part, peer):
        moved = self.copy(number, self.rows(chunk, part), chunk, part, peer)
        moved.start()
        self.kept.append((moved, None))

    def pass_first(self):
        place = self.place
        ax, al = place.chunk(0, 1, 0), place.chunk(1, 0, 0)
        self.arrived(0, ax, 0)
        self.forward(6, ax, 0, place.along)
        self.arrived(3, al, 1)
        self.forward(7, al, 1, place.across)

    def pass_second(self):
        place = self.place
        ax, al = place.chunk(0, 1, 0), place.chunk(1, 0, 0)
        self.arrived(1, ax, 1)
        self.forward(8, ax, 2, place.core)
        self.arrived(2, al, 0)
        self.forward(9, al, 2, place.core)

    def pass_third(self):
        dia = self.place.chunk(1, 1, 0)
        self.arrived(6, dia, 0)
        self.arrived(7, dia, 1)
        self.forward(10, dia, 2, self.place.core)

    def pass_on(self):
        self.pass_first()
        self.pass_second()
        self.pass_third()

    def finish(self):
        place = self.place
        self.arrived(4, place.chunk(0, 0, 1), 0)
        self.arrived(5, place.chunk(0, 0, 1), 1)
        self.arrived(8, place.chunk(0, 1, 1), 2)
        self.arrived(9, place.chunk(1, 0, 1), 2)
        self.arrived(10, place.chunk(1, 1, 1), 2)
        for moved, _ in self.kept:
            moved.wait_send()
        for keep in self.local:
            keep.wait()


OTHERS = [(di, dg, dc) for di in (0, 1) for dg in (0, 1) for dc in (0, 1) if di or dg or dc]


def first_gather_kernel(count, normed, ids, normed_out, ids_out, before_out, after_out, plane_ids, before, after, send, recv, ids_send, ids_recv):
    place = Place()
    me = lax.axis_index("t")
    up, down = {"t": lax.rem(me + 1, count)}, {"t": lax.rem(me + count - 1, count)}
    place.greet([place.peer(*offset) for offset in OTHERS if sum(offset) > 1] + [up, down])
    gather = Gather(place, normed, normed_out, send, recv)
    gather.begin(0)
    gather.begin(1)
    own = place.chunk(0, 0, 0)
    moved = []

    def move(number, source, target, peer):
        copy = pltpu.make_async_remote_copy(
            src_ref=source,
            dst_ref=target,
            send_sem=ids_send.at[number],
            recv_sem=ids_recv.at[number],
            device_id=peer,
            device_id_type=MESH,
        )
        copy.start()
        moved.append(copy)

    for number, offset in enumerate(OTHERS):
        move(number, ids, plane_ids.at[own], place.peer(*offset))
    plane_ids[own] = ids[...]
    for number, offset in enumerate(OTHERS):
        chunk = place.chunk(*offset)
        pltpu.make_async_remote_copy(
            src_ref=ids,
            dst_ref=plane_ids.at[chunk],
            send_sem=ids_send.at[number],
            recv_sem=ids_recv.at[number],
            device_id=place.peer(*offset),
            device_id_type=MESH,
        ).wait_recv()
    move(7, plane_ids, before, up)
    move(8, plane_ids, after, down)
    gather.pass_on()
    for copy in moved[7:]:
        copy.wait_recv()
    for copy in moved:
        copy.wait_send()
    ids_out[...] = plane_ids[...]
    before_out[...] = before[...]
    after_out[...] = after[...]
    gather.finish()


class Scatter:
    def __init__(self, place, product, core_send, core_recv, held, acc, across_recv, along_recv, second, second_recv, send, recv):
        self.place, self.product = place, product
        self.core_send, self.core_recv, self.held, self.acc = core_send, core_recv, held, acc
        self.across_recv, self.along_recv, self.second, self.second_recv = across_recv, along_recv, second, second_recv
        self.send, self.recv = send, recv
        self.kept = []

    def copy(self, number, source, target, peer):
        return pltpu.make_async_remote_copy(
            src_ref=source,
            dst_ref=target,
            send_sem=self.send.at[number],
            recv_sem=self.recv.at[number],
            device_id=peer,
            device_id_type=MESH,
        )

    def start(self, *parts):
        moved = self.copy(*parts)
        moved.start()
        self.kept.append(moved)

    def run(self):
        self.run_first()
        self.run_second()
        self.run_third()

    def run_first(self):
        place = self.place
        order = ((1, 1), (0, 1), (1, 0), (0, 0))
        tile = 256
        per_half = self.held.shape[3] // tile
        def give(di, dg):
            q = 2 * di + dg
            chunk = place.chunk(di, dg, 1)

            def send_tile(n, none):
                at = pl.ds(pl.multiple_of(n % per_half * tile, tile), tile)
                self.core_send[q, n // per_half, :, at] = self.product(chunk, n).astype(BF16)
                return none

            lax.fori_loop(0, 2 * per_half, send_tile, 0)
            self.start(q, self.core_send.at[q], self.core_recv.at[q], place.core)

        def take(di, dg):
            q = 2 * di + dg
            chunk = place.chunk(di, dg, 0)
            self.copy(q, self.core_send.at[q], self.core_recv.at[q], place.core).wait_recv()

            def sum_tile(n, none):
                at = pl.ds(pl.multiple_of(n % per_half * tile, tile), tile)
                value = self.product(chunk, n) + self.core_recv[q, n // per_half, :, at].astype(F32)
                if q:
                    self.held[q - 1, n // per_half, :, at] = value.astype(BF16)
                else:
                    self.acc[n // per_half, :, at] = value
                return none

            lax.fori_loop(0, 2 * per_half, sum_tile, 0)
            if dg:
                self.start(4 + di, self.held.at[q - 1, 0], self.across_recv.at[di], place.across)
            if di:
                self.start(6 + dg, self.held.at[q - 1, 1], self.along_recv.at[dg], place.along)

        give(*order[0])
        give(*order[1])
        take(*order[0])
        give(*order[2])
        take(*order[1])
        give(*order[3])
        take(*order[2])
        take(*order[3])

    def run_second(self):
        place = self.place
        for half, number, buffer, mine, peer, out in (
            (0, 5, self.across_recv, 2, place.along, 8),
            (1, 7, self.along_recv, 1, place.across, 9),
        ):
            self.copy(number, buffer.at[1], buffer.at[1], place.core).wait_recv()

            def add_rows(n, none):
                at = pl.ds(pl.multiple_of(n * SLICE, SLICE), SLICE)
                total = self.held[mine - 1, half, at, :].astype(F32) + buffer[1, at, :].astype(F32)
                self.second[half, at, :] = total.astype(BF16)
                return none

            lax.fori_loop(0, self.held.shape[2] // SLICE, add_rows, 0)
            self.start(out, self.second.at[half], self.second_recv.at[half], peer)

    def run_third(self):
        place = self.place
        for number, buffer in ((4, self.across_recv), (6, self.along_recv)):
            self.copy(number, buffer.at[0], buffer.at[0], place.core).wait_recv()
        for number, half in ((8, 0), (9, 1)):
            self.copy(number, self.second.at[half], self.second_recv.at[half], place.core).wait_recv()

    def rows(self, at):
        first = self.acc[0, at, :] + self.across_recv[0, at, :].astype(F32) + self.second_recv[0, at, :].astype(F32)
        last = self.acc[1, at, :] + self.along_recv[0, at, :].astype(F32) + self.second_recv[1, at, :].astype(F32)
        return jnp.concatenate([first, last], axis=1)

    def finish(self):
        for moved in self.kept:
            moved.wait_send()

    @staticmethod
    def scratch(tokens, width):
        half = width // 2
        return [
            pltpu.VMEM((4, 2, tokens, half), BF16),
            pltpu.VMEM((4, 2, tokens, half), BF16),
            pltpu.VMEM((3, 2, tokens, half), BF16),
            pltpu.VMEM((2, tokens, half), F32),
            pltpu.VMEM((2, tokens, half), BF16),
            pltpu.VMEM((2, tokens, half), BF16),
            pltpu.VMEM((2, tokens, half), BF16),
            pltpu.VMEM((2, tokens, half), BF16),
            pltpu.SemaphoreType.DMA((10,)),
            pltpu.SemaphoreType.DMA((10,)),
        ]


SCATTER_BUFFERS = 10


def pair_product(lefts, rights, tokens):
    def product(chunk, n):
        at = pl.ds(pl.multiple_of(chunk * tokens, tokens), tokens)
        cols = pl.ds(pl.multiple_of(n * 256, 256), 256)
        total = None
        for left, right in zip(lefts, rights):
            term = jnp.dot(left[at, :], right[:, cols], preferred_element_type=F32)
            total = term if total is None else total + term
        return total

    return product


def for_slices(start, stop, body):
    def step(n, none):
        body(pl.ds(pl.multiple_of(n * SLICE, SLICE), SLICE))
        return none

    lax.fori_loop(start // SLICE, stop // SLICE, step, 0)


def middle_kernel(left, right, own_in, gain, middle_out, gathered, *scratch):
    buffers, (block, send, recv) = scratch[:SCATTER_BUFFERS], scratch[SCATTER_BUFFERS:]
    tokens = own_in.shape[0]
    place = Place()
    place.greet()
    scatter = Scatter(place, pair_product([left], [right], tokens), *buffers)
    scatter.run()

    def body(at):
        middle = own_in[at, :].astype(F32) + scatter.rows(at)
        middle_out[at, :] = middle
        block[at, :] = (middle * rms(middle) * gain[...]).astype(BF16)

    gather = Gather(place, block, gathered, send, recv)
    for part in (0, 1):
        for_slices(part * tokens // 2, (part + 1) * tokens // 2, body)
        gather.begin(part)
    gather.pass_on()
    scatter.finish()
    gather.finish()


def turn_kernel(left0, left1, right0, right1, middle, gain, cot, grad_middle_out, gain_out, gathered, *scratch):
    buffers, (block, send, recv) = scratch[:SCATTER_BUFFERS], scratch[SCATTER_BUFFERS:]
    tokens = cot.shape[0]
    place = Place()
    place.greet()
    scatter = Scatter(place, pair_product([left0, left1], [right0, right1], tokens), *buffers)
    scatter.run()
    gain_out[...] = jnp.zeros_like(gain_out)

    def body(at):
        values = middle[at, :]
        grad = scatter.rows(at)
        scale = rms(values)
        weighted = grad * gain[...]
        inner = jnp.mean(values * weighted, axis=-1, keepdims=True)
        total = cot[at, :].astype(F32) + scale * weighted - values * (scale * scale * scale * inner)
        grad_middle_out[at, :] = total
        block[at, :] = total.astype(BF16)
        term = grad * values * scale
        gain_out[...] += term[0:8] + term[8:16]

    gather = Gather(place, block, gathered, send, recv)
    for part in (0, 1):
        for_slices(part * tokens // 2, (part + 1) * tokens // 2, body)
        gather.begin(part)
    gather.pass_on()
    scatter.finish()
    gather.finish()


class Owners:
    def __init__(self, place, reduced, out, send, recv):
        self.place, self.reduced, self.out, self.send, self.recv = place, reduced, out, send, recv
        self.own = place.chunk(0, 0, 0)

    def copy(self, number, offset, slot):
        return pltpu.make_async_remote_copy(
            src_ref=self.reduced.at[self.place.chunk(*offset)],
            dst_ref=self.out.at[slot],
            send_sem=self.send.at[number],
            recv_sem=self.recv.at[number],
            device_id=self.place.peer(*offset),
            device_id_type=MESH,
        )

    def begin(self):
        self.keep = pltpu.make_async_copy(self.reduced.at[self.own], self.out.at[self.own], self.send.at[7])
        self.keep.start()
        self.moved = [self.copy(number, offset, self.own) for number, offset in enumerate(OTHERS)]
        for copy in self.moved:
            copy.start()

    def finish(self):
        for number, offset in enumerate(OTHERS):
            self.copy(number, offset, self.place.chunk(*offset)).wait_recv()
        for copy in self.moved:
            copy.wait_send()
        self.keep.wait()


OWNERS_SCRATCH = [pltpu.SemaphoreType.DMA((8,))] * 2
BEYOND = [offset for offset in OTHERS if sum(offset) > 1]


class GateSums:
    def __init__(self, place, count, pieces, rows_recv, gates_all, send, recv):
        self.place, self.count, self.pieces = place, count, pieces
        self.rows_recv, self.gates_all, self.send, self.recv = rows_recv, gates_all, send, recv
        self.me = lax.axis_index("t")
        self.rank = place.g * 2 + place.c
        self.near = [offset for offset in OTHERS if not offset[0]]
        self.moved = []

    def copy(self, number, source, target, peer):
        return pltpu.make_async_remote_copy(
            src_ref=source,
            dst_ref=target,
            send_sem=self.send.at[number],
            recv_sem=self.recv.at[number],
            device_id=peer,
            device_id_type=MESH,
        )

    def begin(self):
        for number, offset in enumerate(self.near):
            other = lax.rem(self.place.chunk(*offset), 4)
            self.moved.append(self.copy(number, self.pieces.at[other], self.rows_recv.at[self.rank], self.place.peer(*offset)))
            self.moved[-1].start()
        self.rows_recv[self.rank] = self.pieces[self.rank]

    def pass_on(self):
        for number, offset in enumerate(self.near):
            other = lax.rem(self.place.chunk(*offset), 4)
            self.copy(number, self.pieces.at[other], self.rows_recv.at[other], self.place.peer(*offset)).wait_recv()
        for step in range(1, self.count):
            to = lax.rem(self.me + step, self.count)
            self.moved.append(self.copy(2 + step, self.rows_recv.at[to], self.gates_all.at[self.me], {"t": to}))
            self.moved[-1].start()
        self.gates_all[self.me] = self.rows_recv[self.me]

    def finish(self, out):
        for step in range(1, self.count):
            other = lax.rem(self.me + self.count - step, self.count)
            self.copy(2 + step, self.rows_recv.at[other], self.gates_all.at[other], {"t": other}).wait_recv()
        total = self.gates_all[0].astype(F32)
        for z in range(1, self.count):
            total = total + self.gates_all[z].astype(F32)
        out[...] = total
        for copy in self.moved:
            copy.wait_send()


def sum_everywhere(place, count, values, inbox, plane_box, send, recv):
    me = lax.axis_index("t")
    moved = []

    def copy(number, target, peer):
        return pltpu.make_async_remote_copy(
            src_ref=values.at[min(number, 3)],
            dst_ref=target,
            send_sem=send.at[number],
            recv_sem=recv.at[number],
            device_id=peer,
            device_id_type=MESH,
        )

    for number, peer in enumerate((place.core, place.across, place.along)):
        moved.append(copy(number, inbox.at[number], peer))
        moved[-1].start()
        copy(number, inbox.at[number], peer).wait_recv()
        values[number + 1] = values[number] + inbox[number]
    for step in range(1, count):
        moved.append(copy(2 + step, plane_box.at[me], {"t": lax.rem(me + step, count)}))
        moved[-1].start()
    plane_box[me] = values[3]
    for step in range(1, count):
        other = lax.rem(me + count - step, count)
        copy(2 + step, plane_box.at[other], {"t": other}).wait_recv()
    total = plane_box[0]
    for z in range(1, count):
        total = total + plane_box[z]
    for sent in moved:
        sent.wait_send()
    return total


def final_kernel(
    count, with_gates, left0, left1, right0, right1, own_in, gain, mlp_gains, pieces, reduced0, reduced1,
    grad_out, gains_out, gates_out, owned0, owned1,
    gain_sum, values, inbox, plane_box, sum_send, sum_recv, rows_recv, gates_all, gates_send, gates_recv,
    send0, recv0, send1, recv1, *buffers,
):
    tokens, width = own_in.shape
    place = Place()
    me = lax.axis_index("t")
    place.greet([place.peer(*offset) for offset in BEYOND] + [{"t": lax.rem(me + step, count)} for step in range(1, count)])
    scatter = Scatter(place, pair_product([left0, left1], [right0, right1], tokens), *buffers)
    owners = [Owners(place, reduced0, owned0, send0, recv0), Owners(place, reduced1, owned1, send1, recv1)]
    gates = GateSums(place, count, pieces, rows_recv, gates_all, gates_send, gates_recv)
    scatter.run_first()
    if with_gates:
        gates.begin()
    owners[0].begin()
    owners[1].begin()
    scatter.run_second()
    if with_gates:
        gates.pass_on()
    scatter.run_third()
    gain_sum[...] = jnp.zeros_like(gain_sum)

    def body(at):
        x = own_in[at, :].astype(F32)
        grad = scatter.rows(at)
        scale = rms(x)
        weighted = grad * gain[...]
        inner = jnp.mean(x * weighted, axis=-1, keepdims=True)
        grad_out[at, :] = scale * weighted - x * (scale * scale * scale * inner)
        term = grad * x * scale
        gain_sum[...] += term[0:8] + term[8:16]

    for_slices(0, tokens, body)
    lines = width // LANES
    for base, row in ((0, jnp.sum(mlp_gains[...], axis=0, keepdims=True)), (lines, jnp.sum(gain_sum[...], axis=0, keepdims=True))):
        for n in range(lines):
            values[0, base + n : base + n + 1, :] = row[:, n * LANES : (n + 1) * LANES]
    gains_out[...] = sum_everywhere(place, count, values, inbox, plane_box, sum_send, sum_recv)
    if with_gates:
        gates.finish(gates_out)
    else:
        gates_out[...] = jnp.zeros_like(gates_out)
    owners[0].finish()
    owners[1].finish()
    scatter.finish()


def final_step(planes, lefts, rights, own_in, gain, mlp_gains, pieces, reduced):
    tokens, width = own_in.shape
    with_gates = pieces.shape[0] == planes
    block = pieces.shape[1:] if with_gates else (16, LANES)
    slots = planes if with_gates else 1
    pieces = pieces if with_gates else jnp.zeros((1, *block), BF16)
    sums = (2 * width // LANES, LANES)
    return pl.pallas_call(
        functools.partial(final_kernel, planes, with_gates),
        name="final_step",
        out_shape=(
            jax.ShapeDtypeStruct((tokens, width), F32),
            jax.ShapeDtypeStruct(sums, F32),
            jax.ShapeDtypeStruct(block, F32),
            *[jax.ShapeDtypeStruct(part.shape, part.dtype) for part in reduced],
        ),
        in_specs=whole(8) + [ANYWHERE] * 2,
        out_specs=(*whole(3), ANYWHERE, ANYWHERE),
        scratch_shapes=[
            pltpu.VMEM((8, width), F32),
            pltpu.VMEM((4, *sums), F32),
            pltpu.VMEM((3, *sums), F32),
            pltpu.VMEM((planes, *sums), F32),
            pltpu.SemaphoreType.DMA((planes + 2,)),
            pltpu.SemaphoreType.DMA((planes + 2,)),
            pltpu.VMEM((slots, *block), BF16),
            pltpu.VMEM((slots, *block), BF16),
            pltpu.SemaphoreType.DMA((planes + 2,)),
            pltpu.SemaphoreType.DMA((planes + 2,)),
            *OWNERS_SCRATCH,
            *OWNERS_SCRATCH,
            *Scatter.scratch(tokens, width),
        ],
        compiler_params=mixer_params(7),
    )(*lefts, *rights, own_in, gain[None], mlp_gains, pieces, *reduced)


def owners_kernel(reduced0, reduced1, out0, out1, send0, recv0, send1, recv1):
    place = Place()
    place.greet([place.peer(*offset) for offset in BEYOND])
    owners = [Owners(place, reduced0, out0, send0, recv0), Owners(place, reduced1, out1, send1, recv1)]
    for part in owners:
        part.begin()
    for part in owners:
        part.finish()


def owners_step(reduced):
    return pl.pallas_call(
        owners_kernel,
        name="owners_step",
        out_shape=tuple(jax.ShapeDtypeStruct(part.shape, part.dtype) for part in reduced),
        in_specs=[ANYWHERE] * 2,
        out_specs=(ANYWHERE,) * 2,
        scratch_shapes=[*OWNERS_SCRATCH, *OWNERS_SCRATCH],
        compiler_params=mixer_params(8),
    )(*reduced)


def place_kernel(planes, hidden, pairs, sources, out):
    piece = sources.shape[2] // (len(pairs) * (planes if hidden else 1))
    for k in pairs:
        if hidden:
            groups = [
                ((t * 2 + i) * 4 * piece, [(i * 4 + r, (k * planes + t) * piece) for r in range(4)])
                for t in range(planes)
                for i in range(2)
            ]
        else:
            groups = [(r * 2 * piece, [(i * 4 + r, k * piece) for i in range(2)]) for r in range(4)]
        for start, parts in groups:
            row = jnp.concatenate([sources[p, :, at : at + piece].astype(F32) for p, at in parts], axis=1)
            if len(pairs) > 1:
                out[:, k, start : start + row.shape[1]] = row
            else:
                out[:, start : start + row.shape[1]] = row


def place_columns(planes, hidden, kinds, owned):
    members, own_rows, columns = owned.shape
    total = columns * members // kinds
    shape = (own_rows, kinds, total) if kinds > 1 else (own_rows, total)
    return pl.pallas_call(
        functools.partial(place_kernel, planes, hidden, tuple(range(kinds))),
        name="place_columns",
        out_shape=jax.ShapeDtypeStruct(shape, F32),
        in_specs=whole(1),
        out_specs=pl.BlockSpec(memory_space=pltpu.VMEM),
        compiler_params=pltpu.CompilerParams(vmem_limit_bytes=60 * 1024 * 1024),
    )(owned)


def first_gather(planes, normed, ids):
    tokens, width = normed.shape
    every = (8, *ids.shape)
    return pl.pallas_call(
        functools.partial(first_gather_kernel, planes),
        name="first_gather",
        out_shape=(jax.ShapeDtypeStruct((8 * tokens, width), BF16), *[jax.ShapeDtypeStruct(every, F32)] * 3),
        in_specs=[ANYWHERE, *whole(1)],
        out_specs=(ANYWHERE, *whole(3)),
        scratch_shapes=[pltpu.VMEM(every, F32)] * 3 + GATHER_SCRATCH + [pltpu.SemaphoreType.DMA((9,))] * 2,
        compiler_params=mixer_params(3),
    )(normed, ids)


def middle_step(mixed, w_out, own_in, gain):
    tokens, width = own_in.shape
    return pl.pallas_call(
        middle_kernel,
        name="middle_step",
        out_shape=(jax.ShapeDtypeStruct((tokens, width), F32), jax.ShapeDtypeStruct((8 * tokens, width), BF16)),
        in_specs=whole(4),
        out_specs=(pl.BlockSpec(memory_space=pltpu.VMEM), ANYWHERE),
        scratch_shapes=Scatter.scratch(tokens, width) + [pltpu.VMEM((tokens, width), BF16)] + GATHER_SCRATCH,
        compiler_params=mixer_params(4),
    )(mixed, w_out, own_in, gain[None])


def turn_step(left0, left1, right0, right1, middle, gain, cot):
    tokens, width = cot.shape
    return pl.pallas_call(
        turn_kernel,
        name="turn_step",
        out_shape=(
            jax.ShapeDtypeStruct((tokens, width), F32),
            jax.ShapeDtypeStruct((8, width), F32),
            jax.ShapeDtypeStruct((8 * tokens, width), BF16),
        ),
        in_specs=whole(7),
        out_specs=(*whole(2), ANYWHERE),
        scratch_shapes=Scatter.scratch(tokens, width) + [pltpu.VMEM((tokens, width), BF16)] + GATHER_SCRATCH,
        compiler_params=mixer_params(5),
    )(left0, left1, right0, right1, middle, gain[None], cot)


class Swap:
    def __init__(self, quarters, out, send, recv):
        self.quarters, self.out, self.send, self.recv = quarters, out, send, recv
        self.groups = quarters.shape[0]
        self.me = lax.axis_index("g") * 2 + lax.axis_index("c")

    def copy(self, step, other, slot):
        return pltpu.make_async_remote_copy(
            src_ref=self.quarters.at[other],
            dst_ref=self.out.at[:, slot],
            send_sem=self.send.at[step],
            recv_sem=self.recv.at[step],
            device_id={"g": other // 2, "c": other % 2},
            device_id_type=MESH,
        )

    def peers(self):
        others = [lax.rem(self.me + step, self.groups) for step in range(1, self.groups)]
        return [{"g": other // 2, "c": other % 2} for other in others]

    def begin(self):
        self.keep = pltpu.make_async_copy(self.quarters.at[self.me], self.out.at[:, self.me], self.send.at[0])
        self.keep.start()
        self.moved = []
        for step in range(1, self.groups):
            self.moved.append(self.copy(step, lax.rem(self.me + step, self.groups), self.me))
            self.moved[-1].start()

    def finish(self):
        for step in range(1, self.groups):
            other = lax.rem(self.me + self.groups - step, self.groups)
            self.copy(step, other, other).wait_recv()
        for copy in self.moved:
            copy.wait_send()
        self.keep.wait()


def swap_scratch(groups):
    return [pltpu.SemaphoreType.DMA((groups,)), pltpu.SemaphoreType.DMA((groups,))]


def swap_kernel(quarters, out, send, recv):
    move = Swap(quarters, out, send, recv)
    barrier = pltpu.get_barrier_semaphore()
    for peer in move.peers():
        pl.semaphore_signal(barrier, inc=1, device_id=peer, device_id_type=MESH)
    pl.semaphore_wait(barrier, move.groups - 1)
    move.begin()
    move.finish()


def swap(quarters):
    groups, kinds, part, width = quarters.shape
    return pl.pallas_call(
        swap_kernel,
        name="swap",
        out_shape=jax.ShapeDtypeStruct((kinds, groups, part, width), quarters.dtype),
        in_specs=[ANYWHERE],
        out_specs=ANYWHERE,
        scratch_shapes=swap_scratch(groups),
        compiler_params=mixer_params(6),
    )(quarters)


def rms(values):
    return lax.rsqrt(jnp.mean(values * values, axis=-1, keepdims=True) + EPS)


def nt(left, right, out):
    return lax.dot_general(left, right, (((1,), (1,)), ((), ())), preferred_element_type=F32).astype(out)


def tn(left, right, out):
    return lax.dot_general(left, right, (((0,), (0,)), ((), ())), preferred_element_type=F32).astype(out)


def nn(left, right, out):
    return jnp.dot(left, right, preferred_element_type=F32).astype(out)


def per_device(
    inputs, segment_ids, mix_gain, in_weight, conv_weight, conv_bias, gate_weight, gate_bias, decay_param, out_weight,
    mlp_gain, mlp_in, down_weight, cotangent,
):
    planes = lax.axis_size("t")
    rows_here, seg, width = inputs.shape
    row_groups = lax.axis_size("g") * lax.axis_size("c")
    own_tokens = rows_here * seg
    recur_width = conv_weight.shape[1]
    block_width = gate_weight.shape[0]
    members = 2 * row_groups
    channels = recur_width // members
    t, i = lax.axis_index("t"), lax.axis_index("i")
    r = lax.axis_index("g") * lax.axis_size("c") + lax.axis_index("c")
    member = 2 * r + i
    first = member * channels

    own_in = inputs.reshape(own_tokens, width)
    flat_in = own_in.astype(F32)
    scale_in = rms(flat_in)
    cot_own = cotangent.reshape(own_tokens, width)
    own_ids = jnp.pad((segment_ids + 1).astype(F32), ((0, 8 - rows_here), (0, 0)))

    normed, *ids = first_gather(planes, (flat_in * scale_in * mix_gain).astype(BF16), own_ids)
    late_r, ids[0] = lax.optimization_barrier((r, ids[0]))

    direct = planes == row_groups
    in_own = in_weight.transpose(1, 2, 0)
    out_own = out_weight.T[None]
    part = channels // row_groups if direct else 0

    def quarter(weight, part, rank=r):
        return lax.dynamic_slice_in_dim(weight, rank * part, part, weight.ndim - 1)

    def spread_units(weight):
        return lax.all_gather(weight, "t", axis=0, tiled=False)

    def whole_units(weight):
        every = lax.all_gather(weight, ("t", "i"), axis=1, tiled=True)
        return lax.dynamic_slice_in_dim(every, first, channels, 1)

    if direct:
        in_w = swap(spread_units(quarter(in_weight, part).transpose(1, 2, 0)))
        out_quarters = spread_units(quarter(out_weight, part).T[None])
    else:
        in_w = whole_units(in_own)
        out_quarters = jnp.zeros((row_groups, 1, 16, width), BF16)
    w_gate, w_recur = in_w.reshape(2, channels, width)
    hidden_part = mlp_in.shape[2] // row_groups
    mlp_w = spread_units(quarter(mlp_in, hidden_part, late_r).transpose(1, 2, 0))
    w_left = mlp_w[:, 0].reshape(-1, width)
    w_right = mlp_w[:, 1].reshape(-1, width)
    w_down = spread_units(quarter(down_weight, hidden_part, late_r).T).reshape(-1, width)

    def own(values):
        return lax.dynamic_slice_in_dim(values, first, channels, values.ndim - 1)

    decay_own = own(decay_param)
    vec = jnp.concatenate(
        [
            own(conv_weight),
            own(conv_bias)[None],
            own(gate_bias),
            8.0 * jax.nn.softplus(-decay_own)[None],
            8.0 * jax.nn.sigmoid(-decay_own)[None],
            jnp.zeros((7, channels), F32),
        ]
    )
    blocks = channels // block_width
    gate_own = own(gate_weight).reshape(block_width, 2, blocks, block_width)
    spread = jnp.zeros((2, blocks, block_width, blocks, block_width), BF16)
    for n in range(blocks):
        spread = spread.at[:, n, :, n, :].set(gate_own[:, :, n, :].transpose(1, 0, 2))
    spread = spread.reshape(2, channels, channels)
    wg0, wg1 = spread[0], spread[1]

    gate_branch = nt(normed, w_gate, F32)
    recur = nt(normed, w_recur, BF16)
    conv_low, decay, states, mixed, halo, cin, mask, cot, w_out = mixer_forward(
        planes, seg, rows_here, recur, gate_branch, ids, wg0, wg1, vec, cot_own, out_quarters
    )
    w_out = (w_out if direct else whole_units(out_own)).reshape(channels, width)
    middle, normed_two = middle_step(mixed, w_out, own_in, mlp_gain)
    left = nt(normed_two, w_left, F32)
    right = nt(normed_two, w_right, F32)
    act, slope = gelu_parts(left)
    hidden = (act * right).astype(BF16)

    def over_planes(grad):
        return lax.psum_scatter(grad, "t", scatter_dimension=0, tiled=True)

    grad_down = tn(cot, hidden, BF16)
    grad_down, hidden, w_down = lax.optimization_barrier((grad_down, hidden, w_down))
    grad_down = over_planes(grad_down)
    grad_hidden = nt(cot, w_down, F32)
    grad_left = (grad_hidden * right * slope).astype(BF16)
    grad_right = (grad_hidden * act).astype(BF16)
    grad_mlp_in = jnp.concatenate([tn(normed_two, grad_left, BF16), tn(normed_two, grad_right, BF16)], axis=1)
    grad_mlp_in, grad_left, grad_right = lax.optimization_barrier((grad_mlp_in, grad_left, grad_right))
    grad_mlp_in = over_planes(grad_mlp_in)
    grad_middle, grad_mlp_gain, grad_mid = turn_step(grad_left, grad_right, w_left, w_right, middle, mlp_gain, cot_own)
    grad_down, grad_mid = lax.optimization_barrier((grad_down, grad_mid))
    grad_out = tn(grad_mid, mixed, BF16)
    grad_mixed = nt(grad_mid, w_out, F32)
    grad_out, grad_mixed = lax.optimization_barrier((grad_out, grad_mixed))
    grad_out = over_planes(grad_out)
    grad_gate, grad_recur, gw0, gw1, small, down = mixer_backward(
        planes, seg, grad_mixed, gate_branch, states, decay, conv_low, recur, halo, cin, mask, wg0, wg1, wg0.T, wg1.T, vec,
        hidden, w_down,
    )
    grad_mlp_in, grad_gate, grad_recur = lax.optimization_barrier((grad_mlp_in, grad_gate, grad_recur))
    grad_in = jnp.concatenate([tn(normed, grad_gate, BF16), tn(normed, grad_recur, BF16)], axis=1)
    grad_in, grad_gate, grad_recur = lax.optimization_barrier((grad_in, grad_gate, grad_recur))
    grad_in = over_planes(grad_in)
    outputs = (middle + down).astype(BF16).reshape(inputs.shape)
    own_rows = width // (planes * members)

    column_block = lax.broadcasted_iota(jnp.int32, (block_width, channels), 1) // block_width

    def diagonal(gw):
        return sum(
            jnp.where(column_block == n, gw[n * block_width : (n + 1) * block_width], 0.0) for n in range(blocks)
        )

    gate_grads = jnp.concatenate([diagonal(gw0), diagonal(gw1), small], axis=0)
    pieces = jnp.zeros((0, 8, LANES), F32)
    if direct:
        pieces = gate_grads.reshape(gate_grads.shape[0], row_groups, -1).transpose(1, 0, 2)
        pieces = jnp.pad(pieces.astype(BF16), ((0, 0), (0, -pieces.shape[1] % 16), (0, LANES - part)))
    reduced = [part.reshape(members, own_rows, -1) for part in (grad_mlp_in, grad_down)]
    grad_in_norm, gains, gate_sums, owned_mlp_in, owned_down = final_step(
        planes, [grad_gate, grad_recur], [w_gate, w_recur], own_in, mix_gain, grad_mlp_gain, pieces, reduced
    )
    grad_inputs = (grad_middle + grad_in_norm).reshape(inputs.shape)
    index = ((t * 2 + i) * row_groups + r) * own_rows
    gains = lax.dynamic_slice_in_dim(gains.reshape(2, width), index, own_rows, 1)
    owned_in, owned_out = owners_step([part.reshape(members, own_rows, -1) for part in (grad_in, grad_out)])

    def columns(owned, kinds, hidden):
        if direct:
            return place_columns(planes, hidden, kinds, owned)
        owned = owned.reshape(2, row_groups, own_rows, kinds, planes if hidden else 1, -1).astype(F32)
        order = (2, 3, 4, 0, 1, 5) if hidden else (2, 3, 1, 0, 4, 5)
        owned = owned.transpose(order).reshape(own_rows, kinds, -1)
        return owned if kinds > 1 else owned[:, 0]

    if direct:
        gate_grads = gate_sums[:, :part]
    else:
        placed = jnp.zeros((gate_grads.shape[0], recur_width), F32)
        placed = lax.dynamic_update_slice_in_dim(placed, gate_grads, first, 1)
        gate_grads = lax.psum_scatter(placed, EVERY, scatter_dimension=1, tiled=True)
    grad_gate_weight = jnp.stack([gate_grads[:block_width], gate_grads[block_width : 2 * block_width]], axis=1)
    small = gate_grads[2 * block_width : 2 * block_width + 8]
    return (
        outputs,
        grad_inputs,
        gains[1],
        columns(owned_in, 2, False),
        small[0:4],
        small[4],
        grad_gate_weight,
        small[5:7],
        small[7],
        columns(owned_out, 1, False),
        gains[0],
        columns(owned_mlp_in, 2, True),
        columns(owned_down, 1, True),
    )


def solution(mesh):
    seq, rows = mesh.shape["seq"], mesh.shape["rows"]
    grid = Mesh(mesh.devices.reshape(seq // 2, 2, rows // 2, 2), EVERY)
    row_axes, seq_axes = ("g", "c"), ("t", "i")
    tokens = P(row_axes, seq_axes, None)
    return jax.shard_map(
        per_device,
        mesh=grid,
        in_specs=(
            tokens,
            P(row_axes, seq_axes),
            P(),
            P(None, None, seq_axes),
            P(),
            P(),
            P(),
            P(),
            P(),
            P(None, seq_axes),
            P(),
            P(None, None, seq_axes),
            P(None, seq_axes),
            tokens,
        ),
        out_specs=(
            tokens,
            tokens,
            P(EVERY),
            P(EVERY, None, None),
            P(None, EVERY),
            P(EVERY),
            P(None, None, EVERY),
            P(None, EVERY),
            P(EVERY),
            P(EVERY, None),
            P(EVERY),
            P(EVERY, None, None),
            P(EVERY, None),
        ),
        check_vma=False,
    )
```

```python
import functools

import jax
import jax.numpy as jnp
from jax import lax
from jax.experimental import pallas as pl
from jax.experimental.pallas import tpu as pltpu
from jax.sharding import Mesh
from jax.sharding import PartitionSpec as P

EPS = 1e-06
MESH = pl.DeviceIdType.MESH
PLANE = ("i", "g", "c")
EVERY = ("t", "i", "g", "c")
F32 = jnp.float32
BF16 = jnp.bfloat16
GELU_A = 0.7978845608028654
GELU_B = 0.044715
HALO = 8
LANES = 128
SLICE = 16
ANYWHERE = pl.BlockSpec(memory_space=pl.ANY)
GATHER_SCRATCH = [pltpu.SemaphoreType.DMA((13,))] * 2


def gelu_parts(x):
    square = x * x
    th = jnp.tanh(GELU_A * x * (1.0 + GELU_B * square))
    half = 0.5 * (1.0 + th)
    slope = half + 0.5 * x * (1.0 - th * th) * (GELU_A * (1.0 + 3.0 * GELU_B * square))
    return x * half, slope


def one_minus_exp(y):
    series = 1.0 + y * (-1.0 / 2 + y * (1.0 / 6 + y * (-1.0 / 24 + y * (1.0 / 120 + y * (-1.0 / 720 + y * (1.0 / 5040))))))
    return jnp.where(y < 0.35, y * series, 1.0 - jnp.exp(-y))


def sigmoid(x):
    return 1.0 / (1.0 + jnp.exp(-x))


def gate_values(conv_low, wg0, wg1, vec):
    logits0 = jnp.dot(conv_low, wg0, preferred_element_type=F32) + vec[5:6]
    logits1 = jnp.dot(conv_low, wg1, preferred_element_type=F32) + vec[6:7]
    recur_gate = sigmoid(logits0)
    input_gate = sigmoid(logits1)
    log_decay = -vec[7:8] * recur_gate
    return recur_gate, input_gate, log_decay


def put_tiles(ref, at, values):
    tiles, lanes = ref.shape[0], ref.shape[2]
    short = tiles * lanes - values.shape[1]
    if short:
        values = jnp.concatenate([values, jnp.zeros((values.shape[0], short), values.dtype)], axis=1)
    for j in range(tiles):
        ref[j, at, :] = values[:, j * lanes : (j + 1) * lanes]


def get_tiles(ref, at, width):
    joined = jnp.concatenate([ref[j, at, :] for j in range(ref.shape[0])], axis=1)
    return joined[:, :width]


def join_tiles(parts, width):
    return jnp.concatenate(parts, axis=1)[:, :width]


def exchange_copy(step, send, target, other, send_sem, recv_sem):
    return pltpu.make_async_remote_copy(
        src_ref=send,
        dst_ref=target,
        send_sem=send_sem.at[step],
        recv_sem=recv_sem.at[step],
        device_id={"t": other},
        device_id_type=MESH,
    )


def exchange_start(count, me, send, slots, send_sem, recv_sem):
    for step in range(1, count):
        exchange_copy(step, send, slots.at[me], lax.rem(me + step, count), send_sem, recv_sem).start()


def exchange_wait(count, me, send, slots, send_sem, recv_sem):
    for step in range(1, count):
        other = lax.rem(me + count - step, count)
        exchange_copy(step, send, slots.at[other], other, send_sem, recv_sem).wait()


def mixer_forward_kernel(
    count, seg, rows_here, branches, ids, ids_before, ids_after, wg0, wg1, vec_ref, cot, quarters,
    conv_out, decay_out, states_out, mixed_out, halo_out, cin_out, mask, cot_out, swapped,
    drive, h_ref, a_ref, ext, halo_send, halo_recv, summary, slots, send_sem, recv_sem, halo_sems,
    gather_send, gather_recv, swap_send, swap_recv,
):
    place = Place()
    me = lax.axis_index("t")
    place.greet([place.peer(0, 1, 1)] + [{"t": lax.rem(me + step, count)} for step in range(1, count)])
    gather = Gather(place, cot, cot_out, gather_send, gather_recv)
    move = Swap(quarters, swapped, swap_send, swap_recv)
    rows = 8
    width = branches.shape[1] // 2

    def recur_at(at):
        return branches[at, width:].astype(BF16).astype(F32)

    for r in range(rows):
        halo_send[r * HALO : (r + 1) * HALO, :] = recur_at(pl.ds((rows + r + 1) * seg - HALO, HALO))
    halo_copy = pltpu.make_async_remote_copy(
        src_ref=halo_send,
        dst_ref=halo_recv,
        send_sem=halo_sems.at[0],
        recv_sem=halo_sems.at[1],
        device_id={"t": lax.rem(me + 1, count)},
        device_id_type=MESH,
    )
    halo_copy.start()
    gather.begin(0)
    gather.begin(1)
    move.begin()
    for r in range(rows):
        halo_out[(rows + r) * HALO : (rows + r + 1) * HALO, :] = recur_at(pl.ds((r + 1) * seg - HALO, HALO))
    vec = vec_ref[...]

    def ids_of(ref, s):
        chunk = s // rows_here
        return ref[chunk, s % rows_here : s % rows_here + 1, :]

    nothing = jnp.zeros((1, LANES), F32)
    for s in range(2 * rows):
        here = ids_of(ids, s)
        back = ids_of(ids, s - rows) if s >= rows else jnp.where(me > 0, ids_of(ids_before, s + rows), nothing)
        ahead = ids_of(ids, s + rows) if s < rows else jnp.where(me < count - 1, ids_of(ids_after, s - rows), nothing)
        lines = [jnp.concatenate([back[:, seg - k :], here[:, : seg - k]], axis=1) for k in (1, 2, 3)]
        lines += [jnp.concatenate([here[:, k:], ahead[:, :k]], axis=1) for k in (1, 2, 3)]
        lines = [jnp.where(line == here, 1.0, 0.0) for line in lines] + [nothing] * 2
        mask[s * seg : (s + 1) * seg, :] = jnp.concatenate(lines, axis=0).T

    def local(s, none):
        at = pl.ds(pl.multiple_of(s * seg, seg), seg)
        x = recur_at(at)
        ext[0:HALO, :] = halo_out[pl.ds(pl.multiple_of(s * HALO, HALO), HALO), :]
        ext[HALO : HALO + seg, :] = x
        m = mask[at, :]
        conv = vec[4:5] + vec[0:1] * x
        for k in range(1, 4):
            conv = conv + vec[k : k + 1] * ext[HALO - k : HALO - k + seg, :] * m[:, k - 1 : k]
        conv_low = conv.astype(BF16)
        conv_out[at, :] = conv_low
        recur_gate, input_gate, log_decay = gate_values(conv_low, wg0[...], wg1[...], vec)
        keep = m[:, 0:1]
        put_tiles(decay_out, at, jnp.exp(log_decay) * keep)
        scale = (1.0 - keep) + keep * jnp.sqrt(one_minus_exp(-2.0 * log_decay))
        put_tiles(drive, at, scale * input_gate * conv_low.astype(F32))
        return none

    lax.fori_loop(rows, 2 * rows, local, 0)
    halo_copy.wait()
    for r in range(rows):
        halo_out[r * HALO : (r + 1) * HALO, :] = halo_recv[r * HALO : (r + 1) * HALO, :]
    gather.pass_first()
    lax.fori_loop(0, rows, local, 0)
    tiles, lanes = drive.shape[0], drive.shape[2]

    def scan(k, carried):
        at = pl.ds(k, 2 * rows, stride=seg)
        after = []
        for j in range(tiles):
            h, a = carried[j]
            d = decay_out[j, at, :]
            h = d * h + drive[j, at, :]
            a = a * d
            h_ref[j, at, :] = h
            a_ref[j, at, :] = a
            after.append((h, a))
        return tuple(after)

    start = (jnp.zeros((2 * rows, lanes), F32), jnp.ones((2 * rows, lanes), F32))
    last = lax.fori_loop(0, seg, scan, (start,) * tiles, unroll=4)
    last_h = join_tiles([part[0] for part in last], width)
    last_a = join_tiles([part[1] for part in last], width)
    summary[0:rows, :] = last_a[rows:] * last_a[:rows]
    summary[rows : 2 * rows, :] = last_a[rows:] * last_h[:rows] + last_h[rows:]
    exchange_start(count, me, summary, slots, send_sem, recv_sem)
    gather.pass_second()

    def activate(s, none):
        at = pl.ds(pl.multiple_of(s * seg, seg), seg)
        act, _ = gelu_parts(branches[at, :width])
        states_out[at, :] = act
        return none

    lax.fori_loop(0, 2 * rows, activate, 0)
    exchange_wait(count, me, summary, slots, send_sem, recv_sem)
    carry = jnp.zeros((rows, width), F32)
    for z in range(count - 1):
        carry = jnp.where(z < me, slots[z, 0:rows, :] * carry + slots[z, rows : 2 * rows, :], carry)
    cin_out[0:rows, :] = carry
    cin_out[rows : 2 * rows, :] = last_a[:rows] * carry + last_h[:rows]

    def finish(s, none):
        at = pl.ds(pl.multiple_of(s * seg, seg), seg)
        states = get_tiles(h_ref, at, width) + get_tiles(a_ref, at, width) * cin_out[pl.ds(s, 1), :]
        act = states_out[at, :]
        states_out[at, :] = states
        mixed_out[at, :] = (act * states.astype(BF16).astype(F32)).astype(BF16)
        return none

    lax.fori_loop(0, 2 * rows, finish, 0)
    gather.pass_third()
    gather.finish()
    move.finish()


def mixer_backward_kernel(
    count, seg, grad_mixed, branches, states, decay, conv_low_ref, halo, cin, mask, wg0, wg1, wg0t, wg1t, vec_ref,
    hidden, w_down, grad_out, gw0_out, gw1_out, small_out, down_out,
    tot, prod, ext, halo_send, halo_recv, summary, slots, uin, send_sem, recv_sem, halo_sems, *buffers,
):
    place = Place()
    me = lax.axis_index("t")
    place.greet([{"t": lax.rem(me + step, count)} for step in range(1, count)])
    scatter = Scatter(place, pair_product([hidden], [w_down], down_out.shape[0]), *buffers)
    scatter.run_first()
    rows = 8
    width = branches.shape[1] // 2
    vec = vec_ref[...]

    def local(s, none):
        at = pl.ds(pl.multiple_of(s * seg, seg), seg)
        act, slope = gelu_parts(branches[at, :width])
        gm = grad_mixed[at, :].astype(F32)
        grad_out[at, :width] = (gm * states[at, :].astype(BF16).astype(F32) * slope).astype(BF16)
        put_tiles(tot, at, (gm * act).astype(BF16).astype(F32))
        return none

    lax.fori_loop(0, 2 * rows, local, 0)

    tiles, lanes = tot.shape[0], tot.shape[2]

    def scan(k, carried):
        at = pl.ds(seg - 1 - k, 2 * rows, stride=seg)
        after = []
        for j in range(tiles):
            u, p = carried[j]
            d = decay[j, at, :]
            total = tot[j, at, :] + u
            tot[j, at, :] = total
            prod[j, at, :] = p
            after.append((d * total, d * p))
        return tuple(after)

    start = (jnp.zeros((2 * rows, lanes), F32), jnp.ones((2 * rows, lanes), F32))
    last = lax.fori_loop(0, seg, scan, (start,) * tiles, unroll=4)
    u = join_tiles([part[0] for part in last], width)
    p = join_tiles([part[1] for part in last], width)
    summary[0:rows, :] = p[:rows] * p[rows:]
    summary[rows : 2 * rows, :] = p[:rows] * u[rows:] + u[:rows]
    exchange_start(count, me, summary, slots, send_sem, recv_sem)
    scatter.run_second()
    exchange_wait(count, me, summary, slots, send_sem, recv_sem)
    carry = jnp.zeros((rows, width), F32)
    for z in range(count - 1, 0, -1):
        carry = jnp.where(z > me, slots[z, 0:rows, :] * carry + slots[z, rows : 2 * rows, :], carry)
    uin[rows : 2 * rows, :] = carry
    uin[0:rows, :] = p[rows:] * carry + u[rows:]
    gw0_out[...] = jnp.zeros_like(gw0_out)
    gw1_out[...] = jnp.zeros_like(gw1_out)
    small_out[...] = jnp.zeros_like(small_out)

    def gates(s, none):
        at = pl.ds(pl.multiple_of(s * seg, seg), seg)
        total = get_tiles(tot, at, width) + get_tiles(prod, at, width) * uin[pl.ds(s, 1), :]
        ext[HALO - 1 : HALO, :] = cin[pl.ds(s, 1), :]
        ext[HALO : HALO + seg, :] = states[at, :]
        before = ext[HALO - 1 : HALO - 1 + seg, :]
        conv_low = conv_low_ref[at, :]
        conv_vals = conv_low.astype(F32)
        m = mask[at, :]
        keep = m[:, 0:1]
        recur_gate, input_gate, log_decay = gate_values(conv_low, wg0[...], wg1[...], vec)
        root = jnp.sqrt(one_minus_exp(-2.0 * log_decay))
        scale = (1.0 - keep) + keep * root
        driven_in = total * conv_vals
        grad_log = total * before * get_tiles(decay, at, width) - driven_in * input_gate * keep * (jnp.exp(2.0 * log_decay) / root)
        grad0 = grad_log * log_decay * (1.0 - recur_gate)
        grad1 = driven_in * scale * input_gate * (1.0 - input_gate)
        low0 = grad0.astype(BF16)
        low1 = grad1.astype(BF16)
        grad_conv = (
            total * scale * input_gate
            + jnp.dot(low0, wg0t[...], preferred_element_type=F32)
            + jnp.dot(low1, wg1t[...], preferred_element_type=F32)
        )
        put_tiles(tot, at, grad_conv)
        turned = (((0,), (0,)), ((), ()))
        gw0_out[...] += lax.dot_general(conv_low, low0, turned, preferred_element_type=F32)
        gw1_out[...] += lax.dot_general(conv_low, low1, turned, preferred_element_type=F32)
        x = branches[at, width:].astype(BF16).astype(F32)
        ext[0:HALO, :] = halo[pl.ds(pl.multiple_of(s * HALO, HALO), HALO), :]
        ext[HALO : HALO + seg, :] = x

        def add(row, values):
            small_out[row : row + 1, :] += jnp.sum(values, axis=0, keepdims=True)

        add(0, grad_conv * x)
        for k in range(1, 4):
            add(k, grad_conv * ext[HALO - k : HALO - k + seg, :] * m[:, k - 1 : k])
        add(4, grad_conv)
        add(5, grad0)
        add(6, grad1)
        add(7, grad_log * recur_gate)
        return none

    lax.fori_loop(0, 2 * rows, gates, 0)
    small_out[7:8, :] = small_out[7:8, :] * vec[8:9]
    for r in range(rows):
        halo_send[r * HALO : (r + 1) * HALO, :] = get_tiles(tot, pl.ds(r * seg, HALO), width)
    halo_copy = pltpu.make_async_remote_copy(
        src_ref=halo_send,
        dst_ref=halo_recv,
        send_sem=halo_sems.at[0],
        recv_sem=halo_sems.at[1],
        device_id={"t": lax.rem(me + count - 1, count)},
        device_id_type=MESH,
    )
    halo_copy.start()

    def back(s, none):
        at = pl.ds(pl.multiple_of(s * seg, seg), seg)
        m = mask[at, :]
        grad_conv = get_tiles(tot, at, width)
        ext[0:seg, :] = grad_conv
        result = vec[0:1] * grad_conv

        @pl.when(s < rows)
        def _():
            ext[seg : seg + HALO, :] = get_tiles(tot, pl.ds(pl.multiple_of((s + rows) * seg, seg), HALO), width)

        @pl.when(s >= rows)
        def _():
            ext[seg : seg + HALO, :] = halo_recv[pl.ds(pl.multiple_of((s - rows) * HALO, HALO), HALO), :]

        for k in range(1, 4):
            result = result + vec[k : k + 1] * ext[k : k + seg, :] * m[:, 2 + k : 3 + k]
        grad_out[at, width:] = result.astype(BF16)
        return none

    lax.fori_loop(0, rows, back, 0)
    halo_copy.wait()
    lax.fori_loop(rows, 2 * rows, back, 0)
    scatter.run_third()

    def body(at):
        down_out[at, :] = scatter.rows(at)

    for_slices(0, down_out.shape[0], body)
    scatter.finish()


def whole(count):
    return [pl.BlockSpec(memory_space=pltpu.VMEM)] * count


def mixer_params(number):
    return pltpu.CompilerParams(collective_id=number, has_side_effects=True, vmem_limit_bytes=60 * 1024 * 1024)


def mixer_forward(count, seg, rows_here, branches, ids, wg0, wg1, vec, cot, quarters):
    n, width = branches.shape[0], branches.shape[1] // 2
    full = functools.partial(jax.ShapeDtypeStruct, (n, width))
    tiles = -(-width // LANES)
    tiled = jax.ShapeDtypeStruct((tiles, n, LANES), F32)
    groups, kinds, part, depth = quarters.shape
    return pl.pallas_call(
        functools.partial(mixer_forward_kernel, count, seg, rows_here),
        name="mixer_forward",
        out_shape=(
            full(BF16), tiled, full(F32), full(BF16),
            jax.ShapeDtypeStruct((16 * HALO, width), F32), jax.ShapeDtypeStruct((16, width), F32),
            jax.ShapeDtypeStruct((n, 8), F32),
            jax.ShapeDtypeStruct((8 * cot.shape[0], cot.shape[1]), BF16),
            jax.ShapeDtypeStruct((kinds, groups, part, depth), BF16),
        ),
        in_specs=whole(7) + [ANYWHERE] * 2,
        out_specs=(*whole(7), ANYWHERE, ANYWHERE),
        scratch_shapes=[
            pltpu.VMEM((tiles, n, LANES), F32),
            pltpu.VMEM((tiles, n, LANES), F32),
            pltpu.VMEM((tiles, n, LANES), F32),
            pltpu.VMEM((seg + HALO, width), F32),
            pltpu.VMEM((8 * HALO, width), F32),
            pltpu.VMEM((8 * HALO, width), F32),
            pltpu.VMEM((16, width), F32),
            pltpu.VMEM((count, 16, width), F32),
            pltpu.SemaphoreType.DMA((count,)),
            pltpu.SemaphoreType.DMA((count,)),
            pltpu.SemaphoreType.DMA((2,)),
            *GATHER_SCRATCH,
            *swap_scratch(groups),
        ],
        compiler_params=mixer_params(1),
    )(branches, *ids, wg0, wg1, vec, cot, quarters)


def mixer_backward(count, seg, grad_mixed, branches, states, decay, conv_low, halo, cin, mask, wg0, wg1, wg0t, wg1t, vec, hidden, w_down):
    n, width = branches.shape[0], branches.shape[1] // 2
    tokens, depth = n // 8, w_down.shape[1]
    full = functools.partial(jax.ShapeDtypeStruct, (n, width))
    tiles = -(-width // LANES)
    tiled = jax.ShapeDtypeStruct((tiles, n, LANES), F32)
    return pl.pallas_call(
        functools.partial(mixer_backward_kernel, count, seg),
        name="mixer_backward",
        out_shape=(
            jax.ShapeDtypeStruct((n, 2 * width), BF16),
            jax.ShapeDtypeStruct((width, width), F32), jax.ShapeDtypeStruct((width, width), F32),
            jax.ShapeDtypeStruct((8, width), F32), jax.ShapeDtypeStruct((tokens, depth), F32),
        ),
        in_specs=whole(15),
        out_specs=tuple(whole(5)),
        scratch_shapes=[
            pltpu.VMEM((tiles, n, LANES), F32),
            pltpu.VMEM((tiles, n, LANES), F32),
            pltpu.VMEM((seg + HALO, width), F32),
            pltpu.VMEM((8 * HALO, width), F32),
            pltpu.VMEM((8 * HALO, width), F32),
            pltpu.VMEM((16, width), F32),
            pltpu.VMEM((count, 16, width), F32),
            pltpu.VMEM((16, width), F32),
            pltpu.SemaphoreType.DMA((count,)),
            pltpu.SemaphoreType.DMA((count,)),
            pltpu.SemaphoreType.DMA((2,)),
            *Scatter.scratch(tokens, depth),
        ],
        compiler_params=mixer_params(2),
    )(grad_mixed, branches, states, decay, conv_low, halo, cin, mask, wg0, wg1, wg0t, wg1t, vec, hidden, w_down)


class Place:
    def __init__(self):
        self.i, self.g, self.c = lax.axis_index("i"), lax.axis_index("g"), lax.axis_index("c")
        self.core, self.across, self.along = {"c": 1 - self.c}, {"g": 1 - self.g}, {"i": 1 - self.i}

    def chunk(self, di, dg, dc):
        i = 1 - self.i if di else self.i
        g = 1 - self.g if dg else self.g
        c = 1 - self.c if dc else self.c
        return (i * 2 + g) * 2 + c

    def peer(self, di, dg, dc):
        return {
            "i": 1 - self.i if di else self.i,
            "g": 1 - self.g if dg else self.g,
            "c": 1 - self.c if dc else self.c,
        }

    def greet(self, more=()):
        barrier = pltpu.get_barrier_semaphore()
        peers = [self.core, self.across, self.along, *more]
        for peer in peers:
            pl.semaphore_signal(barrier, inc=1, device_id=peer, device_id_type=MESH)
        pl.semaphore_wait(barrier, len(peers))


class Gather:
    COPIES = 11

    def __init__(self, place, block, out, send, recv):
        self.place, self.block, self.out, self.send, self.recv = place, block, out, send, recv
        self.tokens = block.shape[0]
        self.half = self.tokens // 2

    def rows(self, chunk, part):
        start = chunk * self.tokens + (self.half if part == 1 else 0)
        return self.out.at[pl.ds(pl.multiple_of(start, self.half), self.tokens if part == 2 else self.half)]

    def mine(self, part):
        if part == 2:
            return self.block
        return self.block.at[pl.ds(part * self.half, self.half)]

    def copy(self, number, source, chunk, part, peer):
        return pltpu.make_async_remote_copy(
            src_ref=source,
            dst_ref=self.rows(chunk, part),
            send_sem=self.send.at[number],
            recv_sem=self.recv.at[number],
            device_id=peer,
            device_id_type=MESH,
        )

    def begin(self, part):
        place = self.place
        own = place.chunk(0, 0, 0)
        self.kept = getattr(self, "kept", [])
        mine = self.mine(part)
        order = ((0 + part, place.across), (2 + part, place.along))
        for number, peer in order:
            self.kept.append((self.copy(number, mine, own, part, peer), None))
            self.kept[-1][0].start()
        self.kept.append((self.copy(4 + part, mine, own, part, place.core), None))
        self.kept[-1][0].start()
        keep = pltpu.make_async_copy(mine, self.rows(own, part), self.send.at[self.COPIES + part])
        keep.start()
        self.local = getattr(self, "local", []) + [keep]

    def arrived(self, number, chunk, part):
        self.copy(number, self.rows(chunk, part), chunk, part, self.place.core).wait_recv()

    def forward(self, number, chunk, part, peer):
        moved = self.copy(number, self.rows(chunk, part), chunk, part, peer)
        moved.start()
        self.kept.append((moved, None))

    def pass_first(self):
        place = self.place
        ax, al = place.chunk(0, 1, 0), place.chunk(1, 0, 0)
        self.arrived(0, ax, 0)
        self.forward(6, ax, 0, place.along)
        self.arrived(3, al, 1)
        self.forward(7, al, 1, place.across)

    def pass_second(self):
        place = self.place
        ax, al = place.chunk(0, 1, 0), place.chunk(1, 0, 0)
        self.arrived(1, ax, 1)
        self.forward(8, ax, 2, place.core)
        self.arrived(2, al, 0)
        self.forward(9, al, 2, place.core)

    def pass_third(self):
        dia = self.place.chunk(1, 1, 0)
        self.arrived(6, dia, 0)
        self.arrived(7, dia, 1)
        self.forward(10, dia, 2, self.place.core)

    def pass_on(self):
        self.pass_first()
        self.pass_second()
        self.pass_third()

    def finish(self):
        place = self.place
        self.arrived(4, place.chunk(0, 0, 1), 0)
        self.arrived(5, place.chunk(0, 0, 1), 1)
        self.arrived(8, place.chunk(0, 1, 1), 2)
        self.arrived(9, place.chunk(1, 0, 1), 2)
        self.arrived(10, place.chunk(1, 1, 1), 2)
        for moved, _ in self.kept:
            moved.wait_send()
        for keep in self.local:
            keep.wait()


OTHERS = [(di, dg, dc) for di in (0, 1) for dg in (0, 1) for dc in (0, 1) if di or dg or dc]


def first_gather_kernel(count, normed, ids, normed_out, ids_out, before_out, after_out, plane_ids, before, after, send, recv, ids_send, ids_recv):
    place = Place()
    me = lax.axis_index("t")
    up, down = {"t": lax.rem(me + 1, count)}, {"t": lax.rem(me + count - 1, count)}
    place.greet([place.peer(*offset) for offset in OTHERS if sum(offset) > 1] + [up, down])
    gather = Gather(place, normed, normed_out, send, recv)
    own = place.chunk(0, 0, 0)
    moved = []

    def move(number, source, target, peer):
        copy = pltpu.make_async_remote_copy(
            src_ref=source,
            dst_ref=target,
            send_sem=ids_send.at[number],
            recv_sem=ids_recv.at[number],
            device_id=peer,
            device_id_type=MESH,
        )
        copy.start()
        moved.append(copy)

    for number, offset in enumerate(OTHERS):
        move(number, ids, plane_ids.at[own], place.peer(*offset))
    gather.begin(0)
    gather.begin(1)
    plane_ids[own] = ids[...]
    for number, offset in enumerate(OTHERS):
        chunk = place.chunk(*offset)
        pltpu.make_async_remote_copy(
            src_ref=ids,
            dst_ref=plane_ids.at[chunk],
            send_sem=ids_send.at[number],
            recv_sem=ids_recv.at[number],
            device_id=place.peer(*offset),
            device_id_type=MESH,
        ).wait_recv()
    move(7, plane_ids, before, up)
    move(8, plane_ids, after, down)
    gather.pass_on()
    for copy in moved[7:]:
        copy.wait_recv()
    for copy in moved:
        copy.wait_send()
    ids_out[...] = plane_ids[...]
    before_out[...] = before[...]
    after_out[...] = after[...]
    gather.finish()


class Scatter:
    def __init__(self, place, product, core_send, core_recv, held, acc, across_recv, along_recv, second, second_recv, send, recv):
        self.place, self.product = place, product
        self.core_send, self.core_recv, self.held, self.acc = core_send, core_recv, held, acc
        self.across_recv, self.along_recv, self.second, self.second_recv = across_recv, along_recv, second, second_recv
        self.send, self.recv = send, recv
        self.kept = []

    def copy(self, number, source, target, peer):
        return pltpu.make_async_remote_copy(
            src_ref=source,
            dst_ref=target,
            send_sem=self.send.at[number],
            recv_sem=self.recv.at[number],
            device_id=peer,
            device_id_type=MESH,
        )

    def start(self, *parts):
        moved = self.copy(*parts)
        moved.start()
        self.kept.append(moved)

    def run(self):
        self.run_first()
        self.run_second()
        self.run_third()

    def run_first(self):
        place = self.place
        order = ((1, 1), (0, 1), (1, 0), (0, 0))
        tile = 256
        per_half = self.held.shape[3] // tile
        def give(di, dg):
            q = 2 * di + dg
            chunk = place.chunk(di, dg, 1)

            def send_tile(n, none):
                at = pl.ds(pl.multiple_of(n % per_half * tile, tile), tile)
                self.core_send[q, n // per_half, :, at] = self.product(chunk, n).astype(BF16)
                return none

            lax.fori_loop(0, 2 * per_half, send_tile, 0)
            self.start(q, self.core_send.at[q], self.core_recv.at[q], place.core)

        def take(di, dg):
            q = 2 * di + dg
            chunk = place.chunk(di, dg, 0)
            self.copy(q, self.core_send.at[q], self.core_recv.at[q], place.core).wait_recv()

            def sum_tile(n, none):
                at = pl.ds(pl.multiple_of(n % per_half * tile, tile), tile)
                value = self.product(chunk, n) + self.core_recv[q, n // per_half, :, at].astype(F32)
                if q:
                    self.held[q - 1, n // per_half, :, at] = value.astype(BF16)
                else:
                    self.acc[n // per_half, :, at] = value
                return none

            lax.fori_loop(0, 2 * per_half, sum_tile, 0)
            if dg:
                self.start(4 + di, self.held.at[q - 1, 0], self.across_recv.at[di], place.across)
            if di:
                self.start(6 + dg, self.held.at[q - 1, 1], self.along_recv.at[dg], place.along)

        give(*order[0])
        give(*order[1])
        take(*order[0])
        give(*order[2])
        take(*order[1])
        give(*order[3])
        take(*order[2])
        take(*order[3])

    def run_second(self):
        place = self.place
        for half, number, buffer, mine, peer, out in (
            (0, 5, self.across_recv, 2, place.along, 8),
            (1, 7, self.along_recv, 1, place.across, 9),
        ):
            self.copy(number, buffer.at[1], buffer.at[1], place.core).wait_recv()

            def add_rows(n, none):
                at = pl.ds(pl.multiple_of(n * SLICE, SLICE), SLICE)
                total = self.held[mine - 1, half, at, :].astype(F32) + buffer[1, at, :].astype(F32)
                self.second[half, at, :] = total.astype(BF16)
                return none

            lax.fori_loop(0, self.held.shape[2] // SLICE, add_rows, 0)
            self.start(out, self.second.at[half], self.second_recv.at[half], peer)

    def run_third(self):
        place = self.place
        for number, buffer in ((4, self.across_recv), (6, self.along_recv)):
            self.copy(number, buffer.at[0], buffer.at[0], place.core).wait_recv()
        for number, half in ((8, 0), (9, 1)):
            self.copy(number, self.second.at[half], self.second_recv.at[half], place.core).wait_recv()

    def rows(self, at):
        first = self.acc[0, at, :] + self.across_recv[0, at, :].astype(F32) + self.second_recv[0, at, :].astype(F32)
        last = self.acc[1, at, :] + self.along_recv[0, at, :].astype(F32) + self.second_recv[1, at, :].astype(F32)
        return jnp.concatenate([first, last], axis=1)

    def finish(self):
        for moved in self.kept:
            moved.wait_send()

    @staticmethod
    def scratch(tokens, width):
        half = width // 2
        return [
            pltpu.VMEM((4, 2, tokens, half), BF16),
            pltpu.VMEM((4, 2, tokens, half), BF16),
            pltpu.VMEM((3, 2, tokens, half), BF16),
            pltpu.VMEM((2, tokens, half), F32),
            pltpu.VMEM((2, tokens, half), BF16),
            pltpu.VMEM((2, tokens, half), BF16),
            pltpu.VMEM((2, tokens, half), BF16),
            pltpu.VMEM((2, tokens, half), BF16),
            pltpu.SemaphoreType.DMA((10,)),
            pltpu.SemaphoreType.DMA((10,)),
        ]


SCATTER_BUFFERS = 10


def pair_product(lefts, rights, tokens):
    def product(chunk, n):
        at = pl.ds(pl.multiple_of(chunk * tokens, tokens), tokens)
        cols = pl.ds(pl.multiple_of(n * 256, 256), 256)
        total = None
        for left, right in zip(lefts, rights):
            term = jnp.dot(left[at, :], right[:, cols], preferred_element_type=F32)
            total = term if total is None else total + term
        return total

    return product


def for_slices(start, stop, body):
    def step(n, none):
        body(pl.ds(pl.multiple_of(n * SLICE, SLICE), SLICE))
        return none

    lax.fori_loop(start // SLICE, stop // SLICE, step, 0)


def middle_kernel(left, right, own_in, gain, middle_out, gathered, *scratch):
    buffers, (block, send, recv) = scratch[:SCATTER_BUFFERS], scratch[SCATTER_BUFFERS:]
    tokens = own_in.shape[0]
    place = Place()
    place.greet()
    scatter = Scatter(place, pair_product([left], [right], tokens), *buffers)
    scatter.run()

    def body(at):
        middle = own_in[at, :].astype(F32) + scatter.rows(at)
        middle_out[at, :] = middle
        block[at, :] = (middle * rms(middle) * gain[...]).astype(BF16)

    gather = Gather(place, block, gathered, send, recv)
    for part in (0, 1):
        for_slices(part * tokens // 2, (part + 1) * tokens // 2, body)
        gather.begin(part)
    gather.pass_on()
    scatter.finish()
    gather.finish()


def turn_kernel(left0, left1, right0, right1, middle, gain, cot, normed, grad_middle_out, gain_out, grads_out, gathered, *scratch):
    buffers, (block, send, recv) = scratch[:SCATTER_BUFFERS], scratch[SCATTER_BUFFERS:]
    tokens = cot.shape[0]
    place = Place()
    place.greet()
    scatter = Scatter(place, pair_product([left0, left1], [right0, right1], tokens), *buffers)
    hidden = left0.shape[1]

    def weight_grads(start, stop):
        def step(n, none):
            at = pl.ds(pl.multiple_of(n * 256, 256), 256)
            for k, part in enumerate((left0, left1)):
                value = lax.dot_general(normed[:, at], part[...], (((0,), (0,)), ((), ())), preferred_element_type=F32)
                grads_out[at, k * hidden : (k + 1) * hidden] = value.astype(BF16)
            return none

        lax.fori_loop(start, stop, step, 0)

    steps = normed.shape[1] // 256
    scatter.run_first()
    weight_grads(0, steps // 4)
    scatter.run_second()
    weight_grads(steps // 4, steps // 2)
    scatter.run_third()
    gain_out[...] = jnp.zeros_like(gain_out)

    def body(at):
        values = middle[at, :]
        grad = scatter.rows(at)
        scale = rms(values)
        weighted = grad * gain[...]
        inner = jnp.mean(values * weighted, axis=-1, keepdims=True)
        total = cot[at, :].astype(F32) + scale * weighted - values * (scale * scale * scale * inner)
        grad_middle_out[at, :] = total
        block[at, :] = total.astype(BF16)
        term = grad * values * scale
        gain_out[...] += term[0:8] + term[8:16]

    gather = Gather(place, block, gathered, send, recv)
    for part in (0, 1):
        for_slices(part * tokens // 2, (part + 1) * tokens // 2, body)
        gather.begin(part)
    weight_grads(steps // 2, 3 * steps // 4)
    gather.pass_first()
    weight_grads(3 * steps // 4, steps)
    gather.pass_second()
    gather.pass_third()
    scatter.finish()
    gather.finish()


class Owners:
    def __init__(self, place, reduced, out, send, recv):
        self.place, self.reduced, self.out, self.send, self.recv = place, reduced, out, send, recv
        self.own = place.chunk(0, 0, 0)

    def copy(self, number, offset, slot):
        return pltpu.make_async_remote_copy(
            src_ref=self.reduced.at[self.place.chunk(*offset)],
            dst_ref=self.out.at[slot],
            send_sem=self.send.at[number],
            recv_sem=self.recv.at[number],
            device_id=self.place.peer(*offset),
            device_id_type=MESH,
        )

    def begin(self):
        self.keep = pltpu.make_async_copy(self.reduced.at[self.own], self.out.at[self.own], self.send.at[7])
        self.keep.start()
        self.moved = [self.copy(number, offset, self.own) for number, offset in enumerate(OTHERS)]
        for copy in self.moved:
            copy.start()

    def finish(self):
        for number, offset in enumerate(OTHERS):
            self.copy(number, offset, self.place.chunk(*offset)).wait_recv()
        for copy in self.moved:
            copy.wait_send()
        self.keep.wait()


OWNERS_SCRATCH = [pltpu.SemaphoreType.DMA((8,))] * 2
BEYOND = [offset for offset in OTHERS if sum(offset) > 1]


class GateSums:
    def __init__(self, place, count, pieces, rows_recv, gates_all, send, recv):
        self.place, self.count, self.pieces = place, count, pieces
        self.rows_recv, self.gates_all, self.send, self.recv = rows_recv, gates_all, send, recv
        self.me = lax.axis_index("t")
        self.rank = place.g * 2 + place.c
        self.near = [offset for offset in OTHERS if not offset[0]]
        self.moved = []

    def copy(self, number, source, target, peer):
        return pltpu.make_async_remote_copy(
            src_ref=source,
            dst_ref=target,
            send_sem=self.send.at[number],
            recv_sem=self.recv.at[number],
            device_id=peer,
            device_id_type=MESH,
        )

    def begin(self):
        for number, offset in enumerate(self.near):
            other = lax.rem(self.place.chunk(*offset), 4)
            self.moved.append(self.copy(number, self.pieces.at[other], self.rows_recv.at[self.rank], self.place.peer(*offset)))
            self.moved[-1].start()
        self.rows_recv[self.rank] = self.pieces[self.rank]

    def pass_on(self):
        for number, offset in enumerate(self.near):
            other = lax.rem(self.place.chunk(*offset), 4)
            self.copy(number, self.pieces.at[other], self.rows_recv.at[other], self.place.peer(*offset)).wait_recv()
        for step in range(1, self.count):
            to = lax.rem(self.me + step, self.count)
            self.moved.append(self.copy(2 + step, self.rows_recv.at[to], self.gates_all.at[self.me], {"t": to}))
            self.moved[-1].start()
        self.gates_all[self.me] = self.rows_recv[self.me]

    def finish(self, out):
        for step in range(1, self.count):
            other = lax.rem(self.me + self.count - step, self.count)
            self.copy(2 + step, self.rows_recv.at[other], self.gates_all.at[other], {"t": other}).wait_recv()
        total = self.gates_all[0].astype(F32)
        for z in range(1, self.count):
            total = total + self.gates_all[z].astype(F32)
        out[...] = total
        for copy in self.moved:
            copy.wait_send()


def sum_everywhere(place, count, values, inbox, plane_box, send, recv):
    me = lax.axis_index("t")
    moved = []

    def copy(number, target, peer):
        return pltpu.make_async_remote_copy(
            src_ref=values.at[min(number, 3)],
            dst_ref=target,
            send_sem=send.at[number],
            recv_sem=recv.at[number],
            device_id=peer,
            device_id_type=MESH,
        )

    for number, peer in enumerate((place.core, place.across, place.along)):
        moved.append(copy(number, inbox.at[number], peer))
        moved[-1].start()
        copy(number, inbox.at[number], peer).wait_recv()
        values[number + 1] = values[number] + inbox[number]
    for step in range(1, count):
        moved.append(copy(2 + step, plane_box.at[me], {"t": lax.rem(me + step, count)}))
        moved[-1].start()
    plane_box[me] = values[3]
    for step in range(1, count):
        other = lax.rem(me + count - step, count)
        copy(2 + step, plane_box.at[other], {"t": other}).wait_recv()
    total = plane_box[0]
    for z in range(1, count):
        total = total + plane_box[z]
    for sent in moved:
        sent.wait_send()
    return total


def final_kernel(
    count, with_gates, left, right, own_in, gain, mlp_gains, pieces, grad_out, gains_out, gates_out,
    gain_sum, values, inbox, plane_box, sum_send, sum_recv, rows_recv, gates_all, gates_send, gates_recv,
    *buffers,
):
    tokens, width = own_in.shape
    place = Place()
    me = lax.axis_index("t")
    place.greet([place.peer(*offset) for offset in BEYOND] + [{"t": lax.rem(me + step, count)} for step in range(1, count)])
    scatter = Scatter(place, pair_product([left], [right], tokens), *buffers)
    gates = GateSums(place, count, pieces, rows_recv, gates_all, gates_send, gates_recv)
    scatter.run_first()
    if with_gates:
        gates.begin()
    scatter.run_second()
    if with_gates:
        gates.pass_on()
    scatter.run_third()
    gain_sum[...] = jnp.zeros_like(gain_sum)

    def body(at):
        x = own_in[at, :].astype(F32)
        grad = scatter.rows(at)
        scale = rms(x)
        weighted = grad * gain[...]
        inner = jnp.mean(x * weighted, axis=-1, keepdims=True)
        grad_out[at, :] = scale * weighted - x * (scale * scale * scale * inner)
        term = grad * x * scale
        gain_sum[...] += term[0:8] + term[8:16]

    for_slices(0, tokens, body)
    lines = width // LANES
    for base, row in ((0, jnp.sum(mlp_gains[...], axis=0, keepdims=True)), (lines, jnp.sum(gain_sum[...], axis=0, keepdims=True))):
        for n in range(lines):
            values[0, base + n : base + n + 1, :] = row[:, n * LANES : (n + 1) * LANES]
    gains_out[...] = sum_everywhere(place, count, values, inbox, plane_box, sum_send, sum_recv)
    if with_gates:
        gates.finish(gates_out)
    else:
        gates_out[...] = jnp.zeros_like(gates_out)
    scatter.finish()


def final_step(planes, left, right, own_in, gain, mlp_gains, pieces):
    tokens, width = own_in.shape
    with_gates = pieces.shape[0] == planes
    block = pieces.shape[1:] if with_gates else (16, LANES)
    slots = planes if with_gates else 1
    pieces = pieces if with_gates else jnp.zeros((1, *block), BF16)
    sums = (2 * width // LANES, LANES)
    return pl.pallas_call(
        functools.partial(final_kernel, planes, with_gates),
        name="final_step",
        out_shape=(
            jax.ShapeDtypeStruct((tokens, width), F32),
            jax.ShapeDtypeStruct(sums, F32),
            jax.ShapeDtypeStruct(block, F32),
        ),
        in_specs=whole(6),
        out_specs=tuple(whole(3)),
        scratch_shapes=[
            pltpu.VMEM((8, width), F32),
            pltpu.VMEM((4, *sums), F32),
            pltpu.VMEM((3, *sums), F32),
            pltpu.VMEM((planes, *sums), F32),
            pltpu.SemaphoreType.DMA((planes + 2,)),
            pltpu.SemaphoreType.DMA((planes + 2,)),
            pltpu.VMEM((slots, *block), BF16),
            pltpu.VMEM((slots, *block), BF16),
            pltpu.SemaphoreType.DMA((planes + 2,)),
            pltpu.SemaphoreType.DMA((planes + 2,)),
            *Scatter.scratch(tokens, width),
        ],
        compiler_params=mixer_params(7),
    )(left, right, own_in, gain[None], mlp_gains, pieces)


def owners_kernel(reduced0, reduced1, out0, out1, send0, recv0, send1, recv1):
    place = Place()
    place.greet([place.peer(*offset) for offset in BEYOND])
    owners = [Owners(place, reduced0, out0, send0, recv0), Owners(place, reduced1, out1, send1, recv1)]
    for part in owners:
        part.begin()
    for part in owners:
        part.finish()


def owners_step(number, reduced):
    return pl.pallas_call(
        owners_kernel,
        name="owners_step",
        out_shape=tuple(jax.ShapeDtypeStruct(part.shape, part.dtype) for part in reduced),
        in_specs=[ANYWHERE] * 2,
        out_specs=(ANYWHERE,) * 2,
        scratch_shapes=[*OWNERS_SCRATCH, *OWNERS_SCRATCH],
        compiler_params=mixer_params(number),
    )(*reduced)


def place_kernel(planes, hidden, pairs, sources, out):
    piece = sources.shape[2] // (len(pairs) * (planes if hidden else 1))
    for k in pairs:
        if hidden:
            groups = [
                ((t * 2 + i) * 4 * piece, [(i * 4 + r, (k * planes + t) * piece) for r in range(4)])
                for t in range(planes)
                for i in range(2)
            ]
        else:
            groups = [(r * 2 * piece, [(i * 4 + r, k * piece) for i in range(2)]) for r in range(4)]
        for start, parts in groups:
            row = jnp.concatenate([sources[p, :, at : at + piece].astype(F32) for p, at in parts], axis=1)
            if len(pairs) > 1:
                out[:, k, start : start + row.shape[1]] = row
            else:
                out[:, start : start + row.shape[1]] = row


def place_columns(planes, hidden, kinds, owned):
    members, own_rows, columns = owned.shape
    total = columns * members // kinds
    shape = (own_rows, kinds, total) if kinds > 1 else (own_rows, total)
    return pl.pallas_call(
        functools.partial(place_kernel, planes, hidden, tuple(range(kinds))),
        name="place_columns",
        out_shape=jax.ShapeDtypeStruct(shape, F32),
        in_specs=whole(1),
        out_specs=pl.BlockSpec(memory_space=pltpu.VMEM),
        compiler_params=pltpu.CompilerParams(vmem_limit_bytes=60 * 1024 * 1024),
    )(owned)


def first_gather(planes, normed, ids):
    tokens, width = normed.shape
    every = (8, *ids.shape)
    return pl.pallas_call(
        functools.partial(first_gather_kernel, planes),
        name="first_gather",
        out_shape=(jax.ShapeDtypeStruct((8 * tokens, width), BF16), *[jax.ShapeDtypeStruct(every, F32)] * 3),
        in_specs=[ANYWHERE, *whole(1)],
        out_specs=(ANYWHERE, *whole(3)),
        scratch_shapes=[pltpu.VMEM(every, F32)] * 3 + GATHER_SCRATCH + [pltpu.SemaphoreType.DMA((9,))] * 2,
        compiler_params=mixer_params(3),
    )(normed, ids)


def middle_step(mixed, w_out, own_in, gain):
    tokens, width = own_in.shape
    return pl.pallas_call(
        middle_kernel,
        name="middle_step",
        out_shape=(jax.ShapeDtypeStruct((tokens, width), F32), jax.ShapeDtypeStruct((8 * tokens, width), BF16)),
        in_specs=whole(4),
        out_specs=(pl.BlockSpec(memory_space=pltpu.VMEM), ANYWHERE),
        scratch_shapes=Scatter.scratch(tokens, width) + [pltpu.VMEM((tokens, width), BF16)] + GATHER_SCRATCH,
        compiler_params=mixer_params(4),
    )(mixed, w_out, own_in, gain[None])


def turn_step(left0, left1, right0, right1, middle, gain, cot, normed):
    tokens, width = cot.shape
    return pl.pallas_call(
        turn_kernel,
        name="turn_step",
        out_shape=(
            jax.ShapeDtypeStruct((tokens, width), F32),
            jax.ShapeDtypeStruct((8, width), F32),
            jax.ShapeDtypeStruct((width, 2 * left0.shape[1]), BF16),
            jax.ShapeDtypeStruct((8 * tokens, width), BF16),
        ),
        in_specs=whole(8),
        out_specs=(*whole(3), ANYWHERE),
        scratch_shapes=Scatter.scratch(tokens, width) + [pltpu.VMEM((tokens, width), BF16)] + GATHER_SCRATCH,
        compiler_params=mixer_params(5),
    )(left0, left1, right0, right1, middle, gain[None], cot, normed)


class Swap:
    def __init__(self, quarters, out, send, recv):
        self.quarters, self.out, self.send, self.recv = quarters, out, send, recv
        self.groups = quarters.shape[0]
        self.me = lax.axis_index("g") * 2 + lax.axis_index("c")

    def copy(self, step, other, slot):
        return pltpu.make_async_remote_copy(
            src_ref=self.quarters.at[other],
            dst_ref=self.out.at[:, slot],
            send_sem=self.send.at[step],
            recv_sem=self.recv.at[step],
            device_id={"g": other // 2, "c": other % 2},
            device_id_type=MESH,
        )

    def peers(self):
        others = [lax.rem(self.me + step, self.groups) for step in range(1, self.groups)]
        return [{"g": other // 2, "c": other % 2} for other in others]

    def begin(self):
        self.keep = pltpu.make_async_copy(self.quarters.at[self.me], self.out.at[:, self.me], self.send.at[0])
        self.keep.start()
        self.moved = []
        for step in range(1, self.groups):
            self.moved.append(self.copy(step, lax.rem(self.me + step, self.groups), self.me))
            self.moved[-1].start()

    def finish(self):
        for step in range(1, self.groups):
            other = lax.rem(self.me + self.groups - step, self.groups)
            self.copy(step, other, other).wait_recv()
        for copy in self.moved:
            copy.wait_send()
        self.keep.wait()


def swap_scratch(groups):
    return [pltpu.SemaphoreType.DMA((groups,)), pltpu.SemaphoreType.DMA((groups,))]


def swap_kernel(quarters, out, send, recv):
    move = Swap(quarters, out, send, recv)
    barrier = pltpu.get_barrier_semaphore()
    for peer in move.peers():
        pl.semaphore_signal(barrier, inc=1, device_id=peer, device_id_type=MESH)
    pl.semaphore_wait(barrier, move.groups - 1)
    move.begin()
    move.finish()


def swap(quarters):
    groups, kinds, part, width = quarters.shape
    return pl.pallas_call(
        swap_kernel,
        name="swap",
        out_shape=jax.ShapeDtypeStruct((kinds, groups, part, width), quarters.dtype),
        in_specs=[ANYWHERE],
        out_specs=ANYWHERE,
        scratch_shapes=swap_scratch(groups),
        compiler_params=mixer_params(6),
    )(quarters)


def rms(values):
    return lax.rsqrt(jnp.mean(values * values, axis=-1, keepdims=True) + EPS)


def nt(left, right, out):
    return lax.dot_general(left, right, (((1,), (1,)), ((), ())), preferred_element_type=F32).astype(out)


def tn(left, right, out):
    return lax.dot_general(left, right, (((0,), (0,)), ((), ())), preferred_element_type=F32).astype(out)


def nn(left, right, out):
    return jnp.dot(left, right, preferred_element_type=F32).astype(out)


def per_device(
    inputs, segment_ids, mix_gain, in_weight, conv_weight, conv_bias, gate_weight, gate_bias, decay_param, out_weight,
    mlp_gain, mlp_in, down_weight, cotangent,
):
    planes = lax.axis_size("t")
    rows_here, seg, width = inputs.shape
    row_groups = lax.axis_size("g") * lax.axis_size("c")
    own_tokens = rows_here * seg
    recur_width = conv_weight.shape[1]
    block_width = gate_weight.shape[0]
    members = 2 * row_groups
    channels = recur_width // members
    t, i = lax.axis_index("t"), lax.axis_index("i")
    r = lax.axis_index("g") * lax.axis_size("c") + lax.axis_index("c")
    member = 2 * r + i
    first = member * channels

    own_in = inputs.reshape(own_tokens, width)
    flat_in = own_in.astype(F32)
    scale_in = rms(flat_in)
    cot_own = cotangent.reshape(own_tokens, width)
    own_ids = jnp.pad((segment_ids + 1).astype(F32), ((0, 8 - rows_here), (0, 0)))

    normed, *ids = first_gather(planes, (flat_in * scale_in * mix_gain).astype(BF16), own_ids)
    late_r, ids[0] = lax.optimization_barrier((r, ids[0]))

    direct = planes == row_groups
    in_own = in_weight.transpose(1, 2, 0)
    out_own = out_weight.T[None]
    part = channels // row_groups if direct else 0

    def quarter(weight, part, rank=r):
        return lax.dynamic_slice_in_dim(weight, rank * part, part, weight.ndim - 1)

    def spread_units(weight):
        return lax.all_gather(weight, "t", axis=0, tiled=False)

    def whole_units(weight):
        every = lax.all_gather(weight, ("t", "i"), axis=1, tiled=True)
        return lax.dynamic_slice_in_dim(every, first, channels, 1)

    if direct:
        in_w = swap(spread_units(quarter(in_weight, part).transpose(1, 2, 0)))
        out_quarters = spread_units(quarter(out_weight, part).T[None])
    else:
        in_w = whole_units(in_own)
        out_quarters = jnp.zeros((row_groups, 1, 16, width), BF16)
    in_w = in_w.reshape(2 * channels, width)
    hidden_part = mlp_in.shape[2] // row_groups
    w_left, w_right, w_down = [
        spread_units(quarter(weight, hidden_part, late_r).T).reshape(-1, width)
        for weight in (mlp_in[:, 0], mlp_in[:, 1], down_weight)
    ]

    def own(values):
        return lax.dynamic_slice_in_dim(values, first, channels, values.ndim - 1)

    decay_own = own(decay_param)
    vec = jnp.concatenate(
        [
            own(conv_weight),
            own(conv_bias)[None],
            own(gate_bias),
            8.0 * jax.nn.softplus(-decay_own)[None],
            8.0 * jax.nn.sigmoid(-decay_own)[None],
            jnp.zeros((7, channels), F32),
        ]
    )
    blocks = channels // block_width
    gate_own = own(gate_weight).reshape(block_width, 2, blocks, block_width)
    spread = jnp.zeros((2, blocks, block_width, blocks, block_width), BF16)
    for n in range(blocks):
        spread = spread.at[:, n, :, n, :].set(gate_own[:, :, n, :].transpose(1, 0, 2))
    spread = spread.reshape(2, channels, channels)
    wg0, wg1 = spread[0], spread[1]

    branches = nt(normed, in_w, F32)
    conv_low, decay, states, mixed, halo, cin, mask, cot, w_out = mixer_forward(
        planes, seg, rows_here, branches, ids, wg0, wg1, vec, cot_own, out_quarters
    )
    w_out = (w_out if direct else whole_units(out_own)).reshape(channels, width)
    middle, normed_two = middle_step(mixed, w_out, own_in, mlp_gain)
    left = nt(normed_two, w_left, F32)
    right = nt(normed_two, w_right, F32)
    act, slope = gelu_parts(left)
    hidden = (act * right).astype(BF16)

    def over_planes(grad):
        return lax.psum_scatter(grad, "t", scatter_dimension=0, tiled=True)

    grad_down = tn(cot, hidden, BF16)
    grad_down, hidden, w_down = lax.optimization_barrier((grad_down, hidden, w_down))
    grad_down = over_planes(grad_down)
    grad_hidden = nt(cot, w_down, F32)
    grad_left = (grad_hidden * right * slope).astype(BF16)
    grad_right = (grad_hidden * act).astype(BF16)
    grad_middle, grad_mlp_gain, grad_mlp_in, grad_mid = turn_step(
        grad_left, grad_right, w_left, w_right, middle, mlp_gain, cot_own, normed_two
    )
    grad_mlp_in = over_planes(grad_mlp_in)
    grad_down, grad_mid = lax.optimization_barrier((grad_down, grad_mid))
    grad_out = tn(grad_mid, mixed, BF16)
    grad_mixed = nt(grad_mid, w_out, F32)
    grad_out, grad_mixed = lax.optimization_barrier((grad_out, grad_mixed))
    grad_out = over_planes(grad_out)
    grad_branches, gw0, gw1, small, down = mixer_backward(
        planes, seg, grad_mixed, branches, states, decay, conv_low, halo, cin, mask, wg0, wg1, wg0.T, wg1.T, vec,
        hidden, w_down,
    )
    grad_in = tn(normed, grad_branches, BF16)
    grad_mlp_in, grad_in, grad_branches = lax.optimization_barrier((grad_mlp_in, grad_in, grad_branches))
    grad_in = over_planes(grad_in)
    outputs = (middle + down).astype(BF16).reshape(inputs.shape)
    own_rows = width // (planes * members)

    column_block = lax.broadcasted_iota(jnp.int32, (block_width, channels), 1) // block_width

    def diagonal(gw):
        return sum(
            jnp.where(column_block == n, gw[n * block_width : (n + 1) * block_width], 0.0) for n in range(blocks)
        )

    gate_grads = jnp.concatenate([diagonal(gw0), diagonal(gw1), small], axis=0)
    pieces = jnp.zeros((0, 8, LANES), F32)
    if direct:
        pieces = gate_grads.reshape(gate_grads.shape[0], row_groups, -1).transpose(1, 0, 2)
        pieces = jnp.pad(pieces.astype(BF16), ((0, 0), (0, -pieces.shape[1] % 16), (0, LANES - part)))
    grad_in_norm, gains, gate_sums = final_step(planes, grad_branches, in_w, own_in, mix_gain, grad_mlp_gain, pieces)
    grad_inputs = (grad_middle + grad_in_norm).reshape(inputs.shape)
    index = ((t * 2 + i) * row_groups + r) * own_rows
    gains = lax.dynamic_slice_in_dim(gains.reshape(2, width), index, own_rows, 1)


    def exchanged(number, *grads):
        return owners_step(number, [grad.reshape(members, own_rows, -1) for grad in grads])

    owned_mlp_in, owned_down = exchanged(8, grad_mlp_in, grad_down)
    owned_in, owned_out = exchanged(9, grad_in, grad_out)

    def columns(owned, kinds, hidden):
        if direct:
            return place_columns(planes, hidden, kinds, owned)
        owned = owned.reshape(2, row_groups, own_rows, kinds, planes if hidden else 1, -1).astype(F32)
        order = (2, 3, 4, 0, 1, 5) if hidden else (2, 3, 1, 0, 4, 5)
        owned = owned.transpose(order).reshape(own_rows, kinds, -1)
        return owned if kinds > 1 else owned[:, 0]

    if direct:
        gate_grads = gate_sums[:, :part]
    else:
        placed = jnp.zeros((gate_grads.shape[0], recur_width), F32)
        placed = lax.dynamic_update_slice_in_dim(placed, gate_grads, first, 1)
        gate_grads = lax.psum_scatter(placed, EVERY, scatter_dimension=1, tiled=True)
    grad_gate_weight = jnp.stack([gate_grads[:block_width], gate_grads[block_width : 2 * block_width]], axis=1)
    small = gate_grads[2 * block_width : 2 * block_width + 8]
    return (
        outputs,
        grad_inputs,
        gains[1],
        columns(owned_in, 2, False),
        small[0:4],
        small[4],
        grad_gate_weight,
        small[5:7],
        small[7],
        columns(owned_out, 1, False),
        gains[0],
        columns(owned_mlp_in, 2, True),
        columns(owned_down, 1, True),
    )


def solution(mesh):
    seq, rows = mesh.shape["seq"], mesh.shape["rows"]
    grid = Mesh(mesh.devices.reshape(seq // 2, 2, rows // 2, 2), EVERY)
    row_axes, seq_axes = ("g", "c"), ("t", "i")
    tokens = P(row_axes, seq_axes, None)
    return jax.shard_map(
        per_device,
        mesh=grid,
        in_specs=(
            tokens,
            P(row_axes, seq_axes),
            P(),
            P(None, None, seq_axes),
            P(),
            P(),
            P(),
            P(),
            P(),
            P(None, seq_axes),
            P(),
            P(None, None, seq_axes),
            P(None, seq_axes),
            tokens,
        ),
        out_specs=(
            tokens,
            tokens,
            P(EVERY),
            P(EVERY, None, None),
            P(None, EVERY),
            P(EVERY),
            P(None, None, EVERY),
            P(None, EVERY),
            P(EVERY),
            P(EVERY, None),
            P(EVERY),
            P(EVERY, None, None),
            P(EVERY, None),
        ),
        check_vma=False,
    )
```

```python
import functools

import jax
import jax.numpy as jnp
from jax import lax
from jax.experimental import pallas as pl
from jax.experimental.pallas import tpu as pltpu
from jax.sharding import Mesh
from jax.sharding import PartitionSpec as P

EPS = 1e-06
MESH = pl.DeviceIdType.MESH
PLANE = ("i", "g", "c")
EVERY = ("t", "i", "g", "c")
F32 = jnp.float32
BF16 = jnp.bfloat16
GELU_A = 0.7978845608028654
GELU_B = 0.044715
HALO = 8
LANES = 128
SLICE = 16
ANYWHERE = pl.BlockSpec(memory_space=pl.ANY)
GATHER_SCRATCH = [pltpu.SemaphoreType.DMA((14,))] * 2


def gelu_parts(x):
    square = x * x
    th = jnp.tanh(GELU_A * x * (1.0 + GELU_B * square))
    half = 0.5 * (1.0 + th)
    slope = half + 0.5 * x * (1.0 - th * th) * (GELU_A * (1.0 + 3.0 * GELU_B * square))
    return x * half, slope


def one_minus_exp(y):
    series = 1.0 + y * (-1.0 / 2 + y * (1.0 / 6 + y * (-1.0 / 24 + y * (1.0 / 120 + y * (-1.0 / 720 + y * (1.0 / 5040))))))
    return jnp.where(y < 0.35, y * series, 1.0 - jnp.exp(-y))


def sigmoid(x):
    return 1.0 / (1.0 + jnp.exp(-x))


def gate_values(conv_low, wg0, wg1, vec):
    logits0 = jnp.dot(conv_low, wg0, preferred_element_type=F32) + vec[5:6]
    logits1 = jnp.dot(conv_low, wg1, preferred_element_type=F32) + vec[6:7]
    recur_gate = sigmoid(logits0)
    input_gate = sigmoid(logits1)
    log_decay = -vec[7:8] * recur_gate
    return recur_gate, input_gate, log_decay


def spread_blocks(gates, out):
    size, width = gates.shape[1], gates.shape[2]
    column = lax.broadcasted_iota(jnp.int32, (size, width), 1) // size
    for k in range(2):
        block = gates[k].astype(F32)
        for n in range(width // size):
            out[k, n * size : (n + 1) * size, :] = jnp.where(column == n, block, 0.0).astype(BF16)


def put_tiles(ref, at, values):
    tiles, lanes = ref.shape[0], ref.shape[2]
    short = tiles * lanes - values.shape[1]
    if short:
        values = jnp.concatenate([values, jnp.zeros((values.shape[0], short), values.dtype)], axis=1)
    for j in range(tiles):
        ref[j, at, :] = values[:, j * lanes : (j + 1) * lanes]


def get_tiles(ref, at, width):
    joined = jnp.concatenate([ref[j, at, :] for j in range(ref.shape[0])], axis=1)
    return joined[:, :width]


def join_tiles(parts, width):
    return jnp.concatenate(parts, axis=1)[:, :width]


def exchange_copy(step, send, target, other, send_sem, recv_sem):
    return pltpu.make_async_remote_copy(
        src_ref=send,
        dst_ref=target,
        send_sem=send_sem.at[step],
        recv_sem=recv_sem.at[step],
        device_id={"t": other},
        device_id_type=MESH,
    )


def exchange_start(count, me, send, slots, send_sem, recv_sem):
    for step in range(1, count):
        exchange_copy(step, send, slots.at[me], lax.rem(me + step, count), send_sem, recv_sem).start()


def exchange_wait(count, me, send, slots, send_sem, recv_sem):
    for step in range(1, count):
        other = lax.rem(me + count - step, count)
        exchange_copy(step, send, slots.at[other], other, send_sem, recv_sem).wait()


def mixer_forward_kernel(
    count, seg, rows_here, branches_far, ids, ids_before, ids_after, gate_blocks, vec_ref, cot, quarters,
    conv_out, decay_out, states_out, mixed_out, halo_out, cin_out, mask, cot_out, swapped,
    drive, h_ref, a_ref, ext, halo_send, halo_recv, summary, slots, send_sem, recv_sem, halo_sems,
    gather_send, gather_recv, swap_send, swap_recv, branches, wg, load,
):
    place = Place()
    me = lax.axis_index("t")
    loaded = pltpu.make_async_copy(branches_far, branches, load.at[0])
    loaded.start()
    place.greet([place.peer(0, 1, 1)] + [{"t": lax.rem(me + step, count)} for step in range(1, count)])
    gather = Gather(place, cot, cot_out, gather_send, gather_recv)
    move = Swap(quarters, swapped, swap_send, swap_recv)
    gather.begin_whole()
    move.begin()
    spread_blocks(gate_blocks, wg)
    rows = 8
    width = branches.shape[1] // 2
    loaded.wait()

    def recur_at(at):
        return branches[at, width:].astype(BF16).astype(F32)

    for r in range(rows):
        halo_send[r * HALO : (r + 1) * HALO, :] = recur_at(pl.ds((rows + r + 1) * seg - HALO, HALO))
    halo_copy = pltpu.make_async_remote_copy(
        src_ref=halo_send,
        dst_ref=halo_recv,
        send_sem=halo_sems.at[0],
        recv_sem=halo_sems.at[1],
        device_id={"t": lax.rem(me + 1, count)},
        device_id_type=MESH,
    )
    halo_copy.start()
    for r in range(rows):
        halo_out[(rows + r) * HALO : (rows + r + 1) * HALO, :] = recur_at(pl.ds((r + 1) * seg - HALO, HALO))
    vec = vec_ref[...]

    def ids_of(ref, s):
        chunk = s // rows_here
        return ref[chunk, s % rows_here : s % rows_here + 1, :]

    nothing = jnp.zeros((1, LANES), F32)
    for s in range(2 * rows):
        here = ids_of(ids, s)
        back = ids_of(ids, s - rows) if s >= rows else jnp.where(me > 0, ids_of(ids_before, s + rows), nothing)
        ahead = ids_of(ids, s + rows) if s < rows else jnp.where(me < count - 1, ids_of(ids_after, s - rows), nothing)
        lines = [jnp.concatenate([back[:, seg - k :], here[:, : seg - k]], axis=1) for k in (1, 2, 3)]
        lines += [jnp.concatenate([here[:, k:], ahead[:, :k]], axis=1) for k in (1, 2, 3)]
        lines = [jnp.where(line == here, 1.0, 0.0) for line in lines] + [nothing] * 2
        mask[s * seg : (s + 1) * seg, :] = jnp.concatenate(lines, axis=0).T

    def local(s, none):
        at = pl.ds(pl.multiple_of(s * seg, seg), seg)
        x = recur_at(at)
        ext[0:HALO, :] = halo_out[pl.ds(pl.multiple_of(s * HALO, HALO), HALO), :]
        ext[HALO : HALO + seg, :] = x
        m = mask[at, :]
        conv = vec[4:5] + vec[0:1] * x
        for k in range(1, 4):
            conv = conv + vec[k : k + 1] * ext[HALO - k : HALO - k + seg, :] * m[:, k - 1 : k]
        conv_low = conv.astype(BF16)
        conv_out[at, :] = conv_low
        recur_gate, input_gate, log_decay = gate_values(conv_low, wg[0], wg[1], vec)
        keep = m[:, 0:1]
        put_tiles(decay_out, at, jnp.exp(log_decay) * keep)
        scale = (1.0 - keep) + keep * jnp.sqrt(one_minus_exp(-2.0 * log_decay))
        put_tiles(drive, at, scale * input_gate * conv_low.astype(F32))
        return none

    lax.fori_loop(rows, 2 * rows, local, 0)
    halo_copy.wait()
    for r in range(rows):
        halo_out[r * HALO : (r + 1) * HALO, :] = halo_recv[r * HALO : (r + 1) * HALO, :]
    gather.pass_first()
    lax.fori_loop(0, rows, local, 0)
    tiles, lanes = drive.shape[0], drive.shape[2]

    def scan(k, carried):
        at = pl.ds(k, 2 * rows, stride=seg)
        after = []
        for j in range(tiles):
            h, a = carried[j]
            d = decay_out[j, at, :]
            h = d * h + drive[j, at, :]
            a = a * d
            h_ref[j, at, :] = h
            a_ref[j, at, :] = a
            after.append((h, a))
        return tuple(after)

    start = (jnp.zeros((2 * rows, lanes), F32), jnp.ones((2 * rows, lanes), F32))
    last = lax.fori_loop(0, seg, scan, (start,) * tiles, unroll=4)
    last_h = join_tiles([part[0] for part in last], width)
    last_a = join_tiles([part[1] for part in last], width)
    summary[0:rows, :] = last_a[rows:] * last_a[:rows]
    summary[rows : 2 * rows, :] = last_a[rows:] * last_h[:rows] + last_h[rows:]
    exchange_start(count, me, summary, slots, send_sem, recv_sem)
    gather.pass_second()

    def activate(s, none):
        at = pl.ds(pl.multiple_of(s * seg, seg), seg)
        act, _ = gelu_parts(branches[at, :width])
        states_out[at, :] = act
        return none

    lax.fori_loop(0, 2 * rows, activate, 0)
    exchange_wait(count, me, summary, slots, send_sem, recv_sem)
    carry = jnp.zeros((rows, width), F32)
    for z in range(count - 1):
        carry = jnp.where(z < me, slots[z, 0:rows, :] * carry + slots[z, rows : 2 * rows, :], carry)
    cin_out[0:rows, :] = carry
    cin_out[rows : 2 * rows, :] = last_a[:rows] * carry + last_h[:rows]

    def finish(s, none):
        at = pl.ds(pl.multiple_of(s * seg, seg), seg)
        states = get_tiles(h_ref, at, width) + get_tiles(a_ref, at, width) * cin_out[pl.ds(s, 1), :]
        act = states_out[at, :]
        states_out[at, :] = states
        mixed_out[at, :] = (act * states.astype(BF16).astype(F32)).astype(BF16)
        return none

    lax.fori_loop(0, 2 * rows, finish, 0)
    gather.pass_third()
    gather.finish()
    move.finish()


def mixer_backward_kernel(
    count, seg, grad_mixed_far, branches_far, states_far, decay_far, conv_far, mask_far, halo, cin, gate_blocks, vec_ref,
    hidden, w_down, middle_far, grad_out, gw0_out, gw1_out, small_out, outputs,
    tot, prod, ext, halo_send, halo_recv, summary, slots, uin, send_sem, recv_sem, halo_sems,
    grad_mixed, branches, states, decay, conv_low_ref, mask, middle, wg, load, *buffers,
):
    place = Place()
    pairs = (
        (grad_mixed_far, grad_mixed),
        (branches_far, branches),
        (states_far, states),
        (decay_far, decay),
        (conv_far, conv_low_ref),
        (mask_far, mask),
        (middle_far, middle),
    )
    loads = [pltpu.make_async_copy(far, near, load.at[n]) for n, (far, near) in enumerate(pairs)]
    for part in loads:
        part.start()
    me = lax.axis_index("t")
    place.greet([{"t": lax.rem(me + step, count)} for step in range(1, count)])
    scatter = Scatter(place, pair_product([hidden], [w_down], outputs.shape[0]), *buffers)
    spread_blocks(gate_blocks, wg)
    scatter.run_first()
    for part in loads:
        part.wait()
    rows = 8
    width = branches.shape[1] // 2
    vec = vec_ref[...]

    def local(s, none):
        at = pl.ds(pl.multiple_of(s * seg, seg), seg)
        act, slope = gelu_parts(branches[at, :width])
        gm = grad_mixed[at, :].astype(F32)
        grad_out[at, :width] = (gm * states[at, :].astype(BF16).astype(F32) * slope).astype(BF16)
        put_tiles(tot, at, (gm * act).astype(BF16).astype(F32))
        return none

    lax.fori_loop(0, 2 * rows, local, 0)

    tiles, lanes = tot.shape[0], tot.shape[2]

    def scan(k, carried):
        at = pl.ds(seg - 1 - k, 2 * rows, stride=seg)
        after = []
        for j in range(tiles):
            u, p = carried[j]
            d = decay[j, at, :]
            total = tot[j, at, :] + u
            tot[j, at, :] = total
            prod[j, at, :] = p
            after.append((d * total, d * p))
        return tuple(after)

    start = (jnp.zeros((2 * rows, lanes), F32), jnp.ones((2 * rows, lanes), F32))
    last = lax.fori_loop(0, seg, scan, (start,) * tiles, unroll=4)
    u = join_tiles([part[0] for part in last], width)
    p = join_tiles([part[1] for part in last], width)
    summary[0:rows, :] = p[:rows] * p[rows:]
    summary[rows : 2 * rows, :] = p[:rows] * u[rows:] + u[:rows]
    exchange_start(count, me, summary, slots, send_sem, recv_sem)
    scatter.run_second()
    exchange_wait(count, me, summary, slots, send_sem, recv_sem)
    carry = jnp.zeros((rows, width), F32)
    for z in range(count - 1, 0, -1):
        carry = jnp.where(z > me, slots[z, 0:rows, :] * carry + slots[z, rows : 2 * rows, :], carry)
    uin[rows : 2 * rows, :] = carry
    uin[0:rows, :] = p[rows:] * carry + u[rows:]
    gw0_out[...] = jnp.zeros_like(gw0_out)
    gw1_out[...] = jnp.zeros_like(gw1_out)
    small_out[...] = jnp.zeros_like(small_out)

    def gates(s, none):
        at = pl.ds(pl.multiple_of(s * seg, seg), seg)
        total = get_tiles(tot, at, width) + get_tiles(prod, at, width) * uin[pl.ds(s, 1), :]
        ext[HALO - 1 : HALO, :] = cin[pl.ds(s, 1), :]
        ext[HALO : HALO + seg, :] = states[at, :]
        before = ext[HALO - 1 : HALO - 1 + seg, :]
        conv_low = conv_low_ref[at, :]
        conv_vals = conv_low.astype(F32)
        m = mask[at, :]
        keep = m[:, 0:1]
        recur_gate, input_gate, log_decay = gate_values(conv_low, wg[0], wg[1], vec)
        root = jnp.sqrt(one_minus_exp(-2.0 * log_decay))
        scale = (1.0 - keep) + keep * root
        driven_in = total * conv_vals
        grad_log = total * before * get_tiles(decay, at, width) - driven_in * input_gate * keep * (jnp.exp(2.0 * log_decay) / root)
        grad0 = grad_log * log_decay * (1.0 - recur_gate)
        grad1 = driven_in * scale * input_gate * (1.0 - input_gate)
        low0 = grad0.astype(BF16)
        low1 = grad1.astype(BF16)
        inputs_of = (((1,), (1,)), ((), ()))
        grad_conv = (
            total * scale * input_gate
            + lax.dot_general(low0, wg[0], inputs_of, preferred_element_type=F32)
            + lax.dot_general(low1, wg[1], inputs_of, preferred_element_type=F32)
        )
        put_tiles(tot, at, grad_conv)
        turned = (((0,), (0,)), ((), ()))
        gw0_out[...] += lax.dot_general(conv_low, low0, turned, preferred_element_type=F32)
        gw1_out[...] += lax.dot_general(conv_low, low1, turned, preferred_element_type=F32)
        x = branches[at, width:].astype(BF16).astype(F32)
        ext[0:HALO, :] = halo[pl.ds(pl.multiple_of(s * HALO, HALO), HALO), :]
        ext[HALO : HALO + seg, :] = x

        def add(row, values):
            small_out[row : row + 1, :] += jnp.sum(values, axis=0, keepdims=True)

        add(0, grad_conv * x)
        for k in range(1, 4):
            add(k, grad_conv * ext[HALO - k : HALO - k + seg, :] * m[:, k - 1 : k])
        add(4, grad_conv)
        add(5, grad0)
        add(6, grad1)
        add(7, grad_log * recur_gate)
        return none

    lax.fori_loop(0, 2 * rows, gates, 0)
    small_out[7:8, :] = small_out[7:8, :] * vec[8:9]
    for r in range(rows):
        halo_send[r * HALO : (r + 1) * HALO, :] = get_tiles(tot, pl.ds(r * seg, HALO), width)
    halo_copy = pltpu.make_async_remote_copy(
        src_ref=halo_send,
        dst_ref=halo_recv,
        send_sem=halo_sems.at[0],
        recv_sem=halo_sems.at[1],
        device_id={"t": lax.rem(me + count - 1, count)},
        device_id_type=MESH,
    )
    halo_copy.start()

    def back(s, none):
        at = pl.ds(pl.multiple_of(s * seg, seg), seg)
        m = mask[at, :]
        grad_conv = get_tiles(tot, at, width)
        ext[0:seg, :] = grad_conv
        result = vec[0:1] * grad_conv

        @pl.when(s < rows)
        def _():
            ext[seg : seg + HALO, :] = get_tiles(tot, pl.ds(pl.multiple_of((s + rows) * seg, seg), HALO), width)

        @pl.when(s >= rows)
        def _():
            ext[seg : seg + HALO, :] = halo_recv[pl.ds(pl.multiple_of((s - rows) * HALO, HALO), HALO), :]

        for k in range(1, 4):
            result = result + vec[k : k + 1] * ext[k : k + seg, :] * m[:, 2 + k : 3 + k]
        grad_out[at, width:] = result.astype(BF16)
        return none

    lax.fori_loop(0, rows, back, 0)
    halo_copy.wait()
    lax.fori_loop(rows, 2 * rows, back, 0)
    scatter.run_third(0)
    scatter.run_third(1)

    def body(at):
        outputs[at, :] = (middle[at, :] + scatter.rows(at)).astype(BF16)

    for_slices(0, outputs.shape[0], body)
    scatter.finish()


def whole(count):
    return [pl.BlockSpec(memory_space=pltpu.VMEM)] * count


def mixer_params(number):
    return pltpu.CompilerParams(collective_id=number, has_side_effects=True, vmem_limit_bytes=60 * 1024 * 1024)


def mixer_forward(count, seg, rows_here, branches, ids, gate_blocks, vec, cot, quarters):
    n, width = branches.shape[0], branches.shape[1] // 2
    full = functools.partial(jax.ShapeDtypeStruct, (n, width))
    tiles = -(-width // LANES)
    tiled = jax.ShapeDtypeStruct((tiles, n, LANES), F32)
    groups, kinds, part, depth = quarters.shape
    return pl.pallas_call(
        functools.partial(mixer_forward_kernel, count, seg, rows_here),
        name="mixer_forward",
        out_shape=(
            full(BF16), tiled, full(F32), full(BF16),
            jax.ShapeDtypeStruct((16 * HALO, width), F32), jax.ShapeDtypeStruct((16, width), F32),
            jax.ShapeDtypeStruct((n, 8), F32),
            jax.ShapeDtypeStruct((8 * cot.shape[0], cot.shape[1]), BF16),
            jax.ShapeDtypeStruct((kinds, groups, part, depth), BF16),
        ),
        in_specs=[ANYWHERE, *whole(5), ANYWHERE, ANYWHERE],
        out_specs=(*whole(7), ANYWHERE, ANYWHERE),
        scratch_shapes=[
            pltpu.VMEM((tiles, n, LANES), F32),
            pltpu.VMEM((tiles, n, LANES), F32),
            pltpu.VMEM((tiles, n, LANES), F32),
            pltpu.VMEM((seg + HALO, width), F32),
            pltpu.VMEM((8 * HALO, width), F32),
            pltpu.VMEM((8 * HALO, width), F32),
            pltpu.VMEM((16, width), F32),
            pltpu.VMEM((count, 16, width), F32),
            pltpu.SemaphoreType.DMA((count,)),
            pltpu.SemaphoreType.DMA((count,)),
            pltpu.SemaphoreType.DMA((2,)),
            *GATHER_SCRATCH,
            *swap_scratch(groups),
            pltpu.VMEM(branches.shape, F32),
            pltpu.VMEM((2, width, width), BF16),
            pltpu.SemaphoreType.DMA((1,)),
        ],
        compiler_params=mixer_params(1),
    )(branches, *ids, gate_blocks, vec, cot, quarters)


def mixer_backward(count, seg, grad_mixed, branches, states, decay, conv_low, mask, halo, cin, gate_blocks, vec, hidden, w_down, middle):
    n, width = branches.shape[0], branches.shape[1] // 2
    tokens, depth = n // 8, w_down.shape[1]
    full = functools.partial(jax.ShapeDtypeStruct, (n, width))
    tiles = -(-width // LANES)
    tiled = jax.ShapeDtypeStruct((tiles, n, LANES), F32)
    return pl.pallas_call(
        functools.partial(mixer_backward_kernel, count, seg),
        name="mixer_backward",
        out_shape=(
            jax.ShapeDtypeStruct((n, 2 * width), BF16),
            jax.ShapeDtypeStruct((width, width), F32), jax.ShapeDtypeStruct((width, width), F32),
            jax.ShapeDtypeStruct((8, width), F32), jax.ShapeDtypeStruct((tokens, depth), BF16),
        ),
        in_specs=[*[ANYWHERE] * 6, *whole(6), ANYWHERE],
        out_specs=tuple(whole(5)),
        scratch_shapes=[
            pltpu.VMEM((tiles, n, LANES), F32),
            pltpu.VMEM((tiles, n, LANES), F32),
            pltpu.VMEM((seg + HALO, width), F32),
            pltpu.VMEM((8 * HALO, width), F32),
            pltpu.VMEM((8 * HALO, width), F32),
            pltpu.VMEM((16, width), F32),
            pltpu.VMEM((count, 16, width), F32),
            pltpu.VMEM((16, width), F32),
            pltpu.SemaphoreType.DMA((count,)),
            pltpu.SemaphoreType.DMA((count,)),
            pltpu.SemaphoreType.DMA((2,)),
            *[pltpu.VMEM(part.shape, part.dtype) for part in (grad_mixed, branches, states, decay, conv_low, mask, middle)],
            pltpu.VMEM((2, width, width), BF16),
            pltpu.SemaphoreType.DMA((7,)),
            *Scatter.scratch(tokens, depth),
        ],
        compiler_params=mixer_params(2),
    )(grad_mixed, branches, states, decay, conv_low, mask, halo, cin, gate_blocks, vec, hidden, w_down, middle)


class Place:
    def __init__(self):
        self.i, self.g, self.c = lax.axis_index("i"), lax.axis_index("g"), lax.axis_index("c")
        self.core, self.across, self.along = {"c": 1 - self.c}, {"g": 1 - self.g}, {"i": 1 - self.i}

    def chunk(self, di, dg, dc):
        i = 1 - self.i if di else self.i
        g = 1 - self.g if dg else self.g
        c = 1 - self.c if dc else self.c
        return (i * 2 + g) * 2 + c

    def peer(self, di, dg, dc):
        return {
            "i": 1 - self.i if di else self.i,
            "g": 1 - self.g if dg else self.g,
            "c": 1 - self.c if dc else self.c,
        }

    def greet(self, more=()):
        barrier = pltpu.get_barrier_semaphore()
        peers = [self.core, self.across, self.along, *more]
        for peer in peers:
            pl.semaphore_signal(barrier, inc=1, device_id=peer, device_id_type=MESH)
        pl.semaphore_wait(barrier, len(peers))


class Gather:
    COPIES = 12

    def __init__(self, place, block, out, send, recv):
        self.place, self.block, self.out, self.send, self.recv = place, block, out, send, recv
        self.tokens = block.shape[0]
        self.half = self.tokens // 2

    def rows(self, chunk, part):
        start = chunk * self.tokens + (self.half if part == 1 else 0)
        return self.out.at[pl.ds(pl.multiple_of(start, self.half), self.tokens if part == 2 else self.half)]

    def mine(self, part):
        if part == 2:
            return self.block
        return self.block.at[pl.ds(part * self.half, self.half)]

    def copy(self, number, source, chunk, part, peer):
        return pltpu.make_async_remote_copy(
            src_ref=source,
            dst_ref=self.rows(chunk, part),
            send_sem=self.send.at[number],
            recv_sem=self.recv.at[number],
            device_id=peer,
            device_id_type=MESH,
        )

    def begin(self, part, whole=False):
        place = self.place
        own = place.chunk(0, 0, 0)
        other = 1 - part if whole else part
        self.give(0 + part, own, part, place.across)
        self.give(2 + other, own, other, place.along)
        self.give(4 + part, own, part, place.core)
        keep = pltpu.make_async_copy(self.mine(part), self.rows(own, part), self.send.at[self.COPIES + part])
        keep.start()
        self.local = getattr(self, "local", []) + [keep]

    def begin_whole(self):
        self.begin(0, True)
        self.begin(1, True)

    def give(self, number, chunk, part, peer):
        moved = self.copy(number, self.mine(part), chunk, part, peer)
        moved.start()
        self.kept = getattr(self, "kept", []) + [moved]

    def arrived(self, number, chunk, part):
        self.copy(number, self.rows(chunk, part), chunk, part, self.place.core).wait_recv()

    def forward(self, number, chunk, part, peer):
        moved = self.copy(number, self.rows(chunk, part), chunk, part, peer)
        moved.start()
        self.kept.append(moved)

    def pass_first(self):
        place = self.place
        ax, al = place.chunk(0, 1, 0), place.chunk(1, 0, 0)
        self.arrived(0, ax, 0)
        self.forward(6, ax, 0, place.along)
        self.arrived(3, al, 1)
        self.forward(7, al, 1, place.across)

    def pass_second(self):
        place = self.place
        ax, al = place.chunk(0, 1, 0), place.chunk(1, 0, 0)
        self.arrived(1, ax, 1)
        self.forward(8, ax, 2, place.core)
        self.arrived(2, al, 0)
        self.forward(9, al, 2, place.core)

    def pass_third(self):
        dia = self.place.chunk(1, 1, 0)
        self.arrived(6, dia, 0)
        self.forward(10, dia, 0, self.place.core)
        self.arrived(7, dia, 1)
        self.forward(11, dia, 1, self.place.core)

    def pass_on(self):
        self.pass_first()
        self.pass_second()
        self.pass_third()

    def finish(self):
        place = self.place
        self.arrived(4, place.chunk(0, 0, 1), 0)
        self.arrived(5, place.chunk(0, 0, 1), 1)
        self.arrived(8, place.chunk(0, 1, 1), 2)
        self.arrived(9, place.chunk(1, 0, 1), 2)
        self.arrived(10, place.chunk(1, 1, 1), 0)
        self.arrived(11, place.chunk(1, 1, 1), 1)
        for moved in self.kept:
            moved.wait_send()
        for keep in self.local:
            keep.wait()


OTHERS = [(di, dg, dc) for di in (0, 1) for dg in (0, 1) for dc in (0, 1) if di or dg or dc]


def first_gather_kernel(count, normed, ids, normed_out, ids_out, before_out, after_out, plane_ids, before, after, send, recv, ids_send, ids_recv):
    place = Place()
    me = lax.axis_index("t")
    up, down = {"t": lax.rem(me + 1, count)}, {"t": lax.rem(me + count - 1, count)}
    place.greet([place.peer(*offset) for offset in OTHERS if sum(offset) > 1] + [up, down])
    gather = Gather(place, normed, normed_out, send, recv)
    own = place.chunk(0, 0, 0)
    moved = []

    def move(number, source, target, peer):
        copy = pltpu.make_async_remote_copy(
            src_ref=source,
            dst_ref=target,
            send_sem=ids_send.at[number],
            recv_sem=ids_recv.at[number],
            device_id=peer,
            device_id_type=MESH,
        )
        copy.start()
        moved.append(copy)

    for number, offset in enumerate(OTHERS):
        move(number, ids, plane_ids.at[own], place.peer(*offset))
    gather.begin_whole()
    plane_ids[own] = ids[...]
    for number, offset in enumerate(OTHERS):
        chunk = place.chunk(*offset)
        pltpu.make_async_remote_copy(
            src_ref=ids,
            dst_ref=plane_ids.at[chunk],
            send_sem=ids_send.at[number],
            recv_sem=ids_recv.at[number],
            device_id=place.peer(*offset),
            device_id_type=MESH,
        ).wait_recv()
    move(7, plane_ids, before, up)
    move(8, plane_ids, after, down)
    gather.pass_on()
    for copy in moved[7:]:
        copy.wait_recv()
    for copy in moved:
        copy.wait_send()
    ids_out[...] = plane_ids[...]
    before_out[...] = before[...]
    after_out[...] = after[...]
    gather.finish()


class Scatter:
    def __init__(self, place, product, core_send, core_recv, held, acc, across_recv, along_recv, second, second_recv, send, recv):
        self.place, self.product = place, product
        self.core_send, self.core_recv, self.held, self.acc = core_send, core_recv, held, acc
        self.across_recv, self.along_recv, self.second, self.second_recv = across_recv, along_recv, second, second_recv
        self.send, self.recv = send, recv
        self.kept = []

    def copy(self, number, source, target, peer):
        return pltpu.make_async_remote_copy(
            src_ref=source,
            dst_ref=target,
            send_sem=self.send.at[number],
            recv_sem=self.recv.at[number],
            device_id=peer,
            device_id_type=MESH,
        )

    def start(self, *parts):
        moved = self.copy(*parts)
        moved.start()
        self.kept.append(moved)

    def run_first(self):
        place = self.place
        order = ((1, 1), (0, 1), (1, 0), (0, 0))
        tile = 256
        per_half = self.held.shape[3] // tile
        def give(di, dg):
            q = 2 * di + dg
            chunk = place.chunk(di, dg, 1)

            def send_tile(n, none):
                at = pl.ds(pl.multiple_of(n % per_half * tile, tile), tile)
                self.core_send[q, n // per_half, :, at] = self.product(chunk, n).astype(BF16)
                return none

            lax.fori_loop(0, 2 * per_half, send_tile, 0)
            self.start(q, self.core_send.at[q], self.core_recv.at[q], place.core)

        def take(di, dg):
            q = 2 * di + dg
            chunk = place.chunk(di, dg, 0)
            self.copy(q, self.core_send.at[q], self.core_recv.at[q], place.core).wait_recv()

            def sum_tile(n, none):
                at = pl.ds(pl.multiple_of(n % per_half * tile, tile), tile)
                value = self.product(chunk, n) + self.core_recv[q, n // per_half, :, at].astype(F32)
                if q:
                    self.held[q - 1, n // per_half, :, at] = value.astype(BF16)
                else:
                    self.acc[n // per_half, :, at] = value
                return none

            lax.fori_loop(0, 2 * per_half, sum_tile, 0)
            if dg:
                self.start(4 + di, self.held.at[q - 1, 0], self.across_recv.at[di], place.across)
            if di:
                self.start(6 + dg, self.held.at[q - 1, 1], self.along_recv.at[dg], place.along)

        give(*order[0])
        give(*order[1])
        take(*order[0])
        give(*order[2])
        take(*order[1])
        give(*order[3])
        take(*order[2])
        take(*order[3])

    def second_copy(self, half, part):
        tokens = self.second.shape[1] // 2
        at = pl.ds(part * tokens, tokens)
        peer = self.place.across if half else self.place.along
        return 8 + 2 * part + half, self.second.at[half, at], self.second_recv.at[half, at], peer

    def run_second(self):
        place = self.place
        tokens = self.second.shape[1] // 2
        for part in (0, 1):
            for half, number, buffer, mine in ((0, 5, self.across_recv, 2), (1, 7, self.along_recv, 1)):
                if part == 0:
                    self.copy(number, buffer.at[1], buffer.at[1], place.core).wait_recv()

                def add_rows(at):
                    total = self.held[mine - 1, half, at, :].astype(F32) + buffer[1, at, :].astype(F32)
                    self.second[half, at, :] = total.astype(BF16)

                for_slices(part * tokens, (part + 1) * tokens, add_rows)
                self.start(*self.second_copy(half, part))

    def run_third(self, part):
        place = self.place
        if part == 0:
            for number, buffer in ((4, self.across_recv), (6, self.along_recv)):
                self.copy(number, buffer.at[0], buffer.at[0], place.core).wait_recv()
        for half in (0, 1):
            self.copy(*self.second_copy(half, part)).wait_recv()

    def rows(self, at):
        first = self.acc[0, at, :] + self.across_recv[0, at, :].astype(F32) + self.second_recv[0, at, :].astype(F32)
        last = self.acc[1, at, :] + self.along_recv[0, at, :].astype(F32) + self.second_recv[1, at, :].astype(F32)
        return jnp.concatenate([first, last], axis=1)

    def finish(self):
        for moved in self.kept:
            moved.wait_send()

    @staticmethod
    def scratch(tokens, width):
        half = width // 2
        return [
            pltpu.VMEM((4, 2, tokens, half), BF16),
            pltpu.VMEM((4, 2, tokens, half), BF16),
            pltpu.VMEM((3, 2, tokens, half), BF16),
            pltpu.VMEM((2, tokens, half), F32),
            pltpu.VMEM((2, tokens, half), BF16),
            pltpu.VMEM((2, tokens, half), BF16),
            pltpu.VMEM((2, tokens, half), BF16),
            pltpu.VMEM((2, tokens, half), BF16),
            pltpu.SemaphoreType.DMA((12,)),
            pltpu.SemaphoreType.DMA((12,)),
        ]


SCATTER_BUFFERS = 10


def pair_product(lefts, rights, tokens):
    def product(chunk, n):
        at = pl.ds(pl.multiple_of(chunk * tokens, tokens), tokens)
        cols = pl.ds(pl.multiple_of(n * 256, 256), 256)
        total = None
        for left, right in zip(lefts, rights):
            term = jnp.dot(left[at, :], right[:, cols], preferred_element_type=F32)
            total = term if total is None else total + term
        return total

    return product


def for_slices(start, stop, body):
    def step(n, none):
        body(pl.ds(pl.multiple_of(n * SLICE, SLICE), SLICE))
        return none

    lax.fori_loop(start // SLICE, stop // SLICE, step, 0)


def middle_kernel(left, right, own_in, gain, middle_out, gathered, *scratch):
    buffers, (block, send, recv) = scratch[:SCATTER_BUFFERS], scratch[SCATTER_BUFFERS:]
    tokens = own_in.shape[0]
    place = Place()
    place.greet()
    scatter = Scatter(place, pair_product([left], [right], tokens), *buffers)
    scatter.run_first()
    scatter.run_second()

    def body(at):
        middle = own_in[at, :].astype(F32) + scatter.rows(at)
        middle_out[at, :] = middle
        block[at, :] = (middle * rms(middle) * gain[...]).astype(BF16)

    gather = Gather(place, block, gathered, send, recv)
    for part in (0, 1):
        scatter.run_third(part)
        for_slices(part * tokens // 2, (part + 1) * tokens // 2, body)
        gather.begin(part)
    gather.pass_on()
    scatter.finish()
    gather.finish()


def turn_kernel(left0, left1, right0, right1, middle, gain, cot, normed_far, grad_middle_out, gain_out, grads_out, gathered, *scratch):
    buffers, (block, send, recv, normed, load) = scratch[:SCATTER_BUFFERS], scratch[SCATTER_BUFFERS:]
    loaded = pltpu.make_async_copy(normed_far, normed, load.at[0])
    loaded.start()
    tokens = cot.shape[0]
    place = Place()
    place.greet()
    scatter = Scatter(place, pair_product([left0, left1], [right0, right1], tokens), *buffers)
    hidden = left0.shape[1]

    def weight_grads(start, stop):
        def step(n, none):
            at = pl.ds(pl.multiple_of(n * 256, 256), 256)
            for k, part in enumerate((left0, left1)):
                value = lax.dot_general(normed[:, at], part[...], (((0,), (0,)), ((), ())), preferred_element_type=F32)
                grads_out[at, k * hidden : (k + 1) * hidden] = value.astype(BF16)
            return none

        lax.fori_loop(start, stop, step, 0)

    steps = normed.shape[1] // 256
    scatter.run_first()
    loaded.wait()
    weight_grads(0, steps // 4)
    scatter.run_second()
    weight_grads(steps // 4, steps // 2)
    gain_out[...] = jnp.zeros_like(gain_out)

    def body(at):
        values = middle[at, :]
        grad = scatter.rows(at)
        scale = rms(values)
        weighted = grad * gain[...]
        inner = jnp.mean(values * weighted, axis=-1, keepdims=True)
        total = cot[at, :].astype(F32) + scale * weighted - values * (scale * scale * scale * inner)
        grad_middle_out[at, :] = total
        block[at, :] = total.astype(BF16)
        term = grad * values * scale
        gain_out[...] += term[0:8] + term[8:16]

    gather = Gather(place, block, gathered, send, recv)
    for part in (0, 1):
        scatter.run_third(part)
        for_slices(part * tokens // 2, (part + 1) * tokens // 2, body)
        gather.begin(part)
    weight_grads(steps // 2, 3 * steps // 4)
    gather.pass_first()
    weight_grads(3 * steps // 4, steps)
    gather.pass_second()
    gather.pass_third()
    scatter.finish()
    gather.finish()


class Owners:
    def __init__(self, place, reduced, out, send, recv):
        self.place, self.reduced, self.out, self.send, self.recv = place, reduced, out, send, recv
        self.own = place.chunk(0, 0, 0)

    def copy(self, number, offset, slot):
        return pltpu.make_async_remote_copy(
            src_ref=self.reduced.at[self.place.chunk(*offset)],
            dst_ref=self.out.at[slot],
            send_sem=self.send.at[number],
            recv_sem=self.recv.at[number],
            device_id=self.place.peer(*offset),
            device_id_type=MESH,
        )

    def begin(self):
        self.keep = pltpu.make_async_copy(self.reduced.at[self.own], self.out.at[self.own], self.send.at[7])
        self.keep.start()
        self.moved = [self.copy(number, offset, self.own) for number, offset in enumerate(OTHERS)]
        for copy in self.moved:
            copy.start()

    def finish(self):
        for number, offset in enumerate(OTHERS):
            self.copy(number, offset, self.place.chunk(*offset)).wait_recv()
        for copy in self.moved:
            copy.wait_send()
        self.keep.wait()


OWNERS_SCRATCH = [pltpu.SemaphoreType.DMA((8,))] * 2
BEYOND = [offset for offset in OTHERS if sum(offset) > 1]


class GateSums:
    def __init__(self, place, count, pieces, rows_recv, gates_all, send, recv):
        self.place, self.count, self.pieces = place, count, pieces
        self.rows_recv, self.gates_all, self.send, self.recv = rows_recv, gates_all, send, recv
        self.me = lax.axis_index("t")
        self.rank = place.g * 2 + place.c
        self.near = [offset for offset in OTHERS if not offset[0]]
        self.moved = []

    def copy(self, number, source, target, peer):
        return pltpu.make_async_remote_copy(
            src_ref=source,
            dst_ref=target,
            send_sem=self.send.at[number],
            recv_sem=self.recv.at[number],
            device_id=peer,
            device_id_type=MESH,
        )

    def begin(self):
        for number, offset in enumerate(self.near):
            other = lax.rem(self.place.chunk(*offset), 4)
            self.moved.append(self.copy(number, self.pieces.at[other], self.rows_recv.at[self.rank], self.place.peer(*offset)))
            self.moved[-1].start()
        self.rows_recv[self.rank] = self.pieces[self.rank]

    def pass_on(self):
        for number, offset in enumerate(self.near):
            other = lax.rem(self.place.chunk(*offset), 4)
            self.copy(number, self.pieces.at[other], self.rows_recv.at[other], self.place.peer(*offset)).wait_recv()
        for step in range(1, self.count):
            to = lax.rem(self.me + step, self.count)
            self.moved.append(self.copy(2 + step, self.rows_recv.at[to], self.gates_all.at[self.me], {"t": to}))
            self.moved[-1].start()
        self.gates_all[self.me] = self.rows_recv[self.me]

    def finish(self, out):
        for step in range(1, self.count):
            other = lax.rem(self.me + self.count - step, self.count)
            self.copy(2 + step, self.rows_recv.at[other], self.gates_all.at[other], {"t": other}).wait_recv()
        total = self.gates_all[0].astype(F32)
        for z in range(1, self.count):
            total = total + self.gates_all[z].astype(F32)
        out[...] = total
        for copy in self.moved:
            copy.wait_send()


def sum_everywhere(place, count, values, inbox, plane_box, send, recv):
    me = lax.axis_index("t")
    moved = []

    def copy(number, target, peer):
        return pltpu.make_async_remote_copy(
            src_ref=values.at[min(number, 3)],
            dst_ref=target,
            send_sem=send.at[number],
            recv_sem=recv.at[number],
            device_id=peer,
            device_id_type=MESH,
        )

    for number, peer in enumerate((place.core, place.across, place.along)):
        moved.append(copy(number, inbox.at[number], peer))
        moved[-1].start()
        copy(number, inbox.at[number], peer).wait_recv()
        values[number + 1] = values[number] + inbox[number]
    for step in range(1, count):
        moved.append(copy(2 + step, plane_box.at[me], {"t": lax.rem(me + step, count)}))
        moved[-1].start()
    plane_box[me] = values[3]
    for step in range(1, count):
        other = lax.rem(me + count - step, count)
        copy(2 + step, plane_box.at[other], {"t": other}).wait_recv()
    total = plane_box[0]
    for z in range(1, count):
        total = total + plane_box[z]
    for sent in moved:
        sent.wait_send()
    return total


def final_kernel(
    count, with_gates, left, right, own_in, gain, mlp_gains, pieces, grad_middle, grad_out, gains_out, gates_out,
    gain_sum, values, inbox, plane_box, sum_send, sum_recv, rows_recv, gates_all, gates_send, gates_recv,
    *buffers,
):
    tokens, width = own_in.shape
    place = Place()
    me = lax.axis_index("t")
    place.greet([place.peer(*offset) for offset in BEYOND] + [{"t": lax.rem(me + step, count)} for step in range(1, count)])
    scatter = Scatter(place, pair_product([left], [right], tokens), *buffers)
    gates = GateSums(place, count, pieces, rows_recv, gates_all, gates_send, gates_recv)
    scatter.run_first()
    if with_gates:
        gates.begin()
    scatter.run_second()
    if with_gates:
        gates.pass_on()
    scatter.run_third(0)
    scatter.run_third(1)
    gain_sum[...] = jnp.zeros_like(gain_sum)

    def body(at):
        x = own_in[at, :].astype(F32)
        grad = scatter.rows(at)
        scale = rms(x)
        weighted = grad * gain[...]
        inner = jnp.mean(x * weighted, axis=-1, keepdims=True)
        grad_out[at, :] = grad_middle[at, :] + scale * weighted - x * (scale * scale * scale * inner)
        term = grad * x * scale
        gain_sum[...] += term[0:8] + term[8:16]

    for_slices(0, tokens, body)
    lines = width // LANES
    for base, row in ((0, jnp.sum(mlp_gains[...], axis=0, keepdims=True)), (lines, jnp.sum(gain_sum[...], axis=0, keepdims=True))):
        for n in range(lines):
            values[0, base + n : base + n + 1, :] = row[:, n * LANES : (n + 1) * LANES]
    gains_out[...] = sum_everywhere(place, count, values, inbox, plane_box, sum_send, sum_recv)
    if with_gates:
        gates.finish(gates_out)
    else:
        gates_out[...] = jnp.zeros_like(gates_out)
    scatter.finish()


def final_step(planes, left, right, own_in, gain, mlp_gains, pieces, grad_middle):
    tokens, width = own_in.shape
    with_gates = pieces.shape[0] == planes
    block = pieces.shape[1:] if with_gates else (16, LANES)
    slots = planes if with_gates else 1
    pieces = pieces if with_gates else jnp.zeros((1, *block), BF16)
    sums = (2 * width // LANES, LANES)
    return pl.pallas_call(
        functools.partial(final_kernel, planes, with_gates),
        name="final_step",
        out_shape=(
            jax.ShapeDtypeStruct((tokens, width), F32),
            jax.ShapeDtypeStruct(sums, F32),
            jax.ShapeDtypeStruct(block, F32),
        ),
        in_specs=whole(7),
        out_specs=tuple(whole(3)),
        scratch_shapes=[
            pltpu.VMEM((8, width), F32),
            pltpu.VMEM((4, *sums), F32),
            pltpu.VMEM((3, *sums), F32),
            pltpu.VMEM((planes, *sums), F32),
            pltpu.SemaphoreType.DMA((planes + 2,)),
            pltpu.SemaphoreType.DMA((planes + 2,)),
            pltpu.VMEM((slots, *block), BF16),
            pltpu.VMEM((slots, *block), BF16),
            pltpu.SemaphoreType.DMA((planes + 2,)),
            pltpu.SemaphoreType.DMA((planes + 2,)),
            *Scatter.scratch(tokens, width),
        ],
        compiler_params=mixer_params(7),
    )(left, right, own_in, gain[None], mlp_gains, pieces, grad_middle)


def owners_kernel(reduced0, reduced1, out0, out1, send0, recv0, send1, recv1):
    place = Place()
    place.greet([place.peer(*offset) for offset in BEYOND])
    owners = [Owners(place, reduced0, out0, send0, recv0), Owners(place, reduced1, out1, send1, recv1)]
    for part in owners:
        part.begin()
    for part in owners:
        part.finish()


def owners_step(number, reduced):
    return pl.pallas_call(
        owners_kernel,
        name="owners_step",
        out_shape=tuple(jax.ShapeDtypeStruct(part.shape, part.dtype) for part in reduced),
        in_specs=[ANYWHERE] * 2,
        out_specs=(ANYWHERE,) * 2,
        scratch_shapes=[*OWNERS_SCRATCH, *OWNERS_SCRATCH],
        compiler_params=mixer_params(number),
    )(*reduced)


def place_kernel(planes, hidden, pairs, sources, out):
    piece = sources.shape[2] // (len(pairs) * (planes if hidden else 1))
    for k in pairs:
        if hidden:
            groups = [
                ((t * 2 + i) * 4 * piece, [(i * 4 + r, (k * planes + t) * piece) for r in range(4)])
                for t in range(planes)
                for i in range(2)
            ]
        else:
            groups = [(r * 2 * piece, [(i * 4 + r, k * piece) for i in range(2)]) for r in range(4)]
        for start, parts in groups:
            row = jnp.concatenate([sources[p, :, at : at + piece].astype(F32) for p, at in parts], axis=1)
            if len(pairs) > 1:
                out[:, k, start : start + row.shape[1]] = row
            else:
                out[:, start : start + row.shape[1]] = row


def place_columns(planes, hidden, kinds, owned):
    members, own_rows, columns = owned.shape
    total = columns * members // kinds
    shape = (own_rows, kinds, total) if kinds > 1 else (own_rows, total)
    return pl.pallas_call(
        functools.partial(place_kernel, planes, hidden, tuple(range(kinds))),
        name="place_columns",
        out_shape=jax.ShapeDtypeStruct(shape, F32),
        in_specs=whole(1),
        out_specs=pl.BlockSpec(memory_space=pltpu.VMEM),
        compiler_params=pltpu.CompilerParams(vmem_limit_bytes=60 * 1024 * 1024),
    )(owned)


def first_gather(planes, normed, ids):
    tokens, width = normed.shape
    every = (8, *ids.shape)
    return pl.pallas_call(
        functools.partial(first_gather_kernel, planes),
        name="first_gather",
        out_shape=(jax.ShapeDtypeStruct((8 * tokens, width), BF16), *[jax.ShapeDtypeStruct(every, F32)] * 3),
        in_specs=[ANYWHERE, *whole(1)],
        out_specs=(ANYWHERE, *whole(3)),
        scratch_shapes=[pltpu.VMEM(every, F32)] * 3 + GATHER_SCRATCH + [pltpu.SemaphoreType.DMA((9,))] * 2,
        compiler_params=mixer_params(3),
    )(normed, ids)


def middle_step(mixed, w_out, own_in, gain):
    tokens, width = own_in.shape
    return pl.pallas_call(
        middle_kernel,
        name="middle_step",
        out_shape=(jax.ShapeDtypeStruct((tokens, width), F32), jax.ShapeDtypeStruct((8 * tokens, width), BF16)),
        in_specs=whole(4),
        out_specs=(pl.BlockSpec(memory_space=pltpu.VMEM), ANYWHERE),
        scratch_shapes=Scatter.scratch(tokens, width) + [pltpu.VMEM((tokens, width), BF16)] + GATHER_SCRATCH,
        compiler_params=mixer_params(4),
    )(mixed, w_out, own_in, gain[None])


def turn_step(left0, left1, right0, right1, middle, gain, cot, normed):
    tokens, width = cot.shape
    return pl.pallas_call(
        turn_kernel,
        name="turn_step",
        out_shape=(
            jax.ShapeDtypeStruct((tokens, width), F32),
            jax.ShapeDtypeStruct((8, width), F32),
            jax.ShapeDtypeStruct((width, 2 * left0.shape[1]), BF16),
            jax.ShapeDtypeStruct((8 * tokens, width), BF16),
        ),
        in_specs=[*whole(7), ANYWHERE],
        out_specs=(*whole(3), ANYWHERE),
        scratch_shapes=Scatter.scratch(tokens, width)
        + [pltpu.VMEM((tokens, width), BF16)]
        + GATHER_SCRATCH
        + [pltpu.VMEM(normed.shape, BF16), pltpu.SemaphoreType.DMA((1,))],
        compiler_params=mixer_params(5),
    )(left0, left1, right0, right1, middle, gain[None], cot, normed)


class Swap:
    def __init__(self, quarters, out, send, recv):
        self.quarters, self.out, self.send, self.recv = quarters, out, send, recv
        self.groups = quarters.shape[0]
        self.me = lax.axis_index("g") * 2 + lax.axis_index("c")

    def copy(self, step, other, slot):
        return pltpu.make_async_remote_copy(
            src_ref=self.quarters.at[other],
            dst_ref=self.out.at[:, slot],
            send_sem=self.send.at[step],
            recv_sem=self.recv.at[step],
            device_id={"g": other // 2, "c": other % 2},
            device_id_type=MESH,
        )

    def peers(self):
        others = [lax.rem(self.me + step, self.groups) for step in range(1, self.groups)]
        return [{"g": other // 2, "c": other % 2} for other in others]

    def begin(self):
        self.keep = pltpu.make_async_copy(self.quarters.at[self.me], self.out.at[:, self.me], self.send.at[0])
        self.keep.start()
        self.moved = []
        for step in range(1, self.groups):
            self.moved.append(self.copy(step, lax.rem(self.me + step, self.groups), self.me))
            self.moved[-1].start()

    def finish(self):
        for step in range(1, self.groups):
            other = lax.rem(self.me + self.groups - step, self.groups)
            self.copy(step, other, other).wait_recv()
        for copy in self.moved:
            copy.wait_send()
        self.keep.wait()


def swap_scratch(groups):
    return [pltpu.SemaphoreType.DMA((groups,)), pltpu.SemaphoreType.DMA((groups,))]


def swap_kernel(quarters, out, send, recv):
    move = Swap(quarters, out, send, recv)
    barrier = pltpu.get_barrier_semaphore()
    for peer in move.peers():
        pl.semaphore_signal(barrier, inc=1, device_id=peer, device_id_type=MESH)
    pl.semaphore_wait(barrier, move.groups - 1)
    move.begin()
    move.finish()


def swap(quarters):
    groups, kinds, part, width = quarters.shape
    return pl.pallas_call(
        swap_kernel,
        name="swap",
        out_shape=jax.ShapeDtypeStruct((kinds, groups, part, width), quarters.dtype),
        in_specs=[ANYWHERE],
        out_specs=ANYWHERE,
        scratch_shapes=swap_scratch(groups),
        compiler_params=mixer_params(6),
    )(quarters)


def rms(values):
    return lax.rsqrt(jnp.mean(values * values, axis=-1, keepdims=True) + EPS)


def nt(left, right, out):
    return lax.dot_general(left, right, (((1,), (1,)), ((), ())), preferred_element_type=F32).astype(out)


def tn(left, right, out):
    return lax.dot_general(left, right, (((0,), (0,)), ((), ())), preferred_element_type=F32).astype(out)


def nn(left, right, out):
    return jnp.dot(left, right, preferred_element_type=F32).astype(out)


def per_device(
    inputs, segment_ids, mix_gain, in_weight, conv_weight, conv_bias, gate_weight, gate_bias, decay_param, out_weight,
    mlp_gain, mlp_in, down_weight, cotangent,
):
    planes = lax.axis_size("t")
    rows_here, seg, width = inputs.shape
    row_groups = lax.axis_size("g") * lax.axis_size("c")
    own_tokens = rows_here * seg
    recur_width = conv_weight.shape[1]
    block_width = gate_weight.shape[0]
    members = 2 * row_groups
    channels = recur_width // members
    t, i = lax.axis_index("t"), lax.axis_index("i")
    r = lax.axis_index("g") * lax.axis_size("c") + lax.axis_index("c")
    member = 2 * r + i
    first = member * channels

    own_in = inputs.reshape(own_tokens, width)
    flat_in = own_in.astype(F32)
    scale_in = rms(flat_in)
    cot_own = cotangent.reshape(own_tokens, width)
    own_ids = jnp.pad((segment_ids + 1).astype(F32), ((0, 8 - rows_here), (0, 0)))

    normed, *ids = first_gather(planes, (flat_in * scale_in * mix_gain).astype(BF16), own_ids)
    late_r, ids[0] = lax.optimization_barrier((r, ids[0]))

    direct = planes == row_groups
    in_own = in_weight.transpose(1, 2, 0)
    out_own = out_weight.T[None]
    part = channels // row_groups if direct else 0

    def quarter(weight, part, rank=r):
        return lax.dynamic_slice_in_dim(weight, rank * part, part, weight.ndim - 1)

    def spread_units(weight):
        return lax.all_gather(weight, "t", axis=0, tiled=False)

    def whole_units(weight):
        every = lax.all_gather(weight, ("t", "i"), axis=1, tiled=True)
        return lax.dynamic_slice_in_dim(every, first, channels, 1)

    if direct:
        in_w = swap(spread_units(quarter(in_weight, part).transpose(1, 2, 0)))
        out_quarters = spread_units(quarter(out_weight, part).T[None])
    else:
        in_w = whole_units(in_own)
        out_quarters = jnp.zeros((row_groups, 1, 16, width), BF16)
    in_w = in_w.reshape(2 * channels, width)
    hidden_part = mlp_in.shape[2] // row_groups
    gated = quarter(mlp_in, hidden_part, late_r).transpose(1, 2, 0)
    w_left, w_right, w_down = [
        spread_units(part).reshape(-1, width)
        for part in (gated[0], gated[1], quarter(down_weight, hidden_part, late_r).T)
    ]

    def own(values):
        return lax.dynamic_slice_in_dim(values, first, channels, values.ndim - 1)

    vec = own(
        jnp.concatenate(
            [
                conv_weight,
                conv_bias[None],
                gate_bias,
                8.0 * jax.nn.softplus(-decay_param)[None],
                8.0 * jax.nn.sigmoid(-decay_param)[None],
                jnp.zeros((7, recur_width), F32),
            ]
        )
    )
    gate_blocks = own(gate_weight).transpose(1, 0, 2)
    blocks = channels // block_width

    branches = nt(normed, in_w, F32)
    conv_low, decay, states, mixed, halo, cin, mask, cot, w_out = mixer_forward(
        planes, seg, rows_here, branches, ids, gate_blocks, vec, cot_own, out_quarters
    )
    w_out = (w_out if direct else whole_units(out_own)).reshape(channels, width)
    middle, normed_two = middle_step(mixed, w_out, own_in, mlp_gain)
    left = nt(normed_two, w_left, F32)
    right = nt(normed_two, w_right, F32)
    act, slope = gelu_parts(left)
    hidden = (act * right).astype(BF16)

    def over_planes(grad):
        return lax.psum_scatter(grad, "t", scatter_dimension=0, tiled=True)

    grad_down = tn(cot, hidden, BF16)
    grad_down, hidden, w_down = lax.optimization_barrier((grad_down, hidden, w_down))
    grad_down = over_planes(grad_down)
    grad_hidden = nt(cot, w_down, F32)
    grad_left = (grad_hidden * right * slope).astype(BF16)
    grad_right = (grad_hidden * act).astype(BF16)
    grad_middle, grad_mlp_gain, grad_mlp_in, grad_mid = turn_step(
        grad_left, grad_right, w_left, w_right, middle, mlp_gain, cot_own, normed_two
    )
    grad_mlp_in = over_planes(grad_mlp_in)
    grad_down, grad_mid = lax.optimization_barrier((grad_down, grad_mid))
    grad_out = tn(grad_mid, mixed, BF16)
    grad_mixed = nt(grad_mid, w_out, F32)
    grad_branches, gw0, gw1, small, outputs = mixer_backward(
        planes, seg, grad_mixed, branches, states, decay, conv_low, mask, halo, cin, gate_blocks, vec, hidden, w_down, middle
    )
    grad_in = jnp.concatenate([tn(normed, grad_branches, BF16), grad_out], axis=1)
    grad_mlp_in, grad_in, grad_branches = lax.optimization_barrier((grad_mlp_in, grad_in, grad_branches))
    grad_in = over_planes(grad_in)
    outputs = outputs.reshape(inputs.shape)
    own_rows = width // (planes * members)

    column_block = lax.broadcasted_iota(jnp.int32, (block_width, channels), 1) // block_width

    def diagonal(gw):
        return sum(
            jnp.where(column_block == n, gw[n * block_width : (n + 1) * block_width], 0.0) for n in range(blocks)
        )

    gate_grads = jnp.concatenate([diagonal(gw0), diagonal(gw1), small], axis=0)
    pieces = jnp.zeros((0, 8, LANES), F32)
    if direct:
        pieces = gate_grads.reshape(gate_grads.shape[0], row_groups, -1).transpose(1, 0, 2)
        pieces = jnp.pad(pieces.astype(BF16), ((0, 0), (0, -pieces.shape[1] % 16), (0, LANES - part)))
    grad_inputs, gains, gate_sums = final_step(
        planes, grad_branches, in_w, own_in, mix_gain, grad_mlp_gain, pieces, grad_middle
    )
    grad_inputs = grad_inputs.reshape(inputs.shape)
    index = ((t * 2 + i) * row_groups + r) * own_rows
    gains = lax.dynamic_slice_in_dim(gains.reshape(2, width), index, own_rows, 1)


    def exchanged(number, *grads):
        return owners_step(number, [grad.reshape(members, own_rows, -1) for grad in grads])

    owned_mlp_in, owned_down = exchanged(8, grad_mlp_in, grad_down)
    split = 2 * channels
    owned_in, owned_out = exchanged(9, grad_in[:, :split], grad_in[:, split:])

    def columns(owned, kinds, hidden):
        if direct:
            return place_columns(planes, hidden, kinds, owned)
        owned = owned.reshape(2, row_groups, own_rows, kinds, planes if hidden else 1, -1).astype(F32)
        order = (2, 3, 4, 0, 1, 5) if hidden else (2, 3, 1, 0, 4, 5)
        owned = owned.transpose(order).reshape(own_rows, kinds, -1)
        return owned if kinds > 1 else owned[:, 0]

    if direct:
        gate_grads = gate_sums[:, :part]
    else:
        placed = jnp.zeros((gate_grads.shape[0], recur_width), F32)
        placed = lax.dynamic_update_slice_in_dim(placed, gate_grads, first, 1)
        gate_grads = lax.psum_scatter(placed, EVERY, scatter_dimension=1, tiled=True)
    grad_gate_weight = jnp.stack([gate_grads[:block_width], gate_grads[block_width : 2 * block_width]], axis=1)
    small = gate_grads[2 * block_width : 2 * block_width + 8]
    return (
        outputs,
        grad_inputs,
        gains[1],
        columns(owned_in, 2, False),
        small[0:4],
        small[4],
        grad_gate_weight,
        small[5:7],
        small[7],
        columns(owned_out, 1, False),
        gains[0],
        columns(owned_mlp_in, 2, True),
        columns(owned_down, 1, True),
    )


def solution(mesh):
    seq, rows = mesh.shape["seq"], mesh.shape["rows"]
    grid = Mesh(mesh.devices.reshape(seq // 2, 2, rows // 2, 2), EVERY)
    row_axes, seq_axes = ("g", "c"), ("t", "i")
    tokens = P(row_axes, seq_axes, None)
    return jax.shard_map(
        per_device,
        mesh=grid,
        in_specs=(
            tokens,
            P(row_axes, seq_axes),
            P(),
            P(None, None, seq_axes),
            P(),
            P(),
            P(),
            P(),
            P(),
            P(None, seq_axes),
            P(),
            P(None, None, seq_axes),
            P(None, seq_axes),
            tokens,
        ),
        out_specs=(
            tokens,
            tokens,
            P(EVERY),
            P(EVERY, None, None),
            P(None, EVERY),
            P(EVERY),
            P(None, None, EVERY),
            P(None, EVERY),
            P(EVERY),
            P(EVERY, None),
            P(EVERY),
            P(EVERY, None, None),
            P(EVERY, None),
        ),
        check_vma=False,
    )
```

```python
import functools

import jax
import jax.numpy as jnp
from jax import lax
from jax.experimental import pallas as pl
from jax.experimental.pallas import tpu as pltpu
from jax.sharding import Mesh
from jax.sharding import PartitionSpec as P

EPS = 1e-06
MESH = pl.DeviceIdType.MESH
PLANE = ("i", "g", "c")
EVERY = ("t", "i", "g", "c")
F32 = jnp.float32
BF16 = jnp.bfloat16
GELU_A = 0.7978845608028654
GELU_B = 0.044715
HALO = 8
LANES = 128
SLICE = 16
ANYWHERE = pl.BlockSpec(memory_space=pl.ANY)
GATHER_SCRATCH = [pltpu.SemaphoreType.DMA((14,))] * 2


def gelu_parts(x):
    square = x * x
    th = jnp.tanh(GELU_A * x * (1.0 + GELU_B * square))
    half = 0.5 * (1.0 + th)
    slope = half + 0.5 * x * (1.0 - th * th) * (GELU_A * (1.0 + 3.0 * GELU_B * square))
    return x * half, slope


def one_minus_exp(y, power):
    series = 1.0 + y * (-1.0 / 2 + y * (1.0 / 6 + y * (-1.0 / 24 + y * (1.0 / 120 + y * (-1.0 / 720 + y * (1.0 / 5040))))))
    return jnp.where(y < 0.35, y * series, 1.0 - power)


def sigmoid(x):
    return 1.0 / (1.0 + jnp.exp(-x))


def gate_values(conv_low, wg0, wg1, vec):
    logits0 = jnp.dot(conv_low, wg0, preferred_element_type=F32) + vec[5:6]
    logits1 = jnp.dot(conv_low, wg1, preferred_element_type=F32) + vec[6:7]
    recur_gate = sigmoid(logits0)
    input_gate = sigmoid(logits1)
    log_decay = -vec[7:8] * recur_gate
    return recur_gate, input_gate, log_decay


def spread_blocks(gates, out):
    size, width = gates.shape[1], gates.shape[2]
    column = lax.broadcasted_iota(jnp.int32, (size, width), 1) // size
    for k in range(2):
        block = gates[k].astype(F32)
        for n in range(width // size):
            out[k, n * size : (n + 1) * size, :] = jnp.where(column == n, block, 0.0).astype(BF16)


def put_tiles(ref, at, values):
    tiles, lanes = ref.shape[0], ref.shape[2]
    short = tiles * lanes - values.shape[1]
    if short:
        values = jnp.concatenate([values, jnp.zeros((values.shape[0], short), values.dtype)], axis=1)
    for j in range(tiles):
        ref[j, at, :] = values[:, j * lanes : (j + 1) * lanes]


def get_tiles(ref, at, width):
    joined = jnp.concatenate([ref[j, at, :] for j in range(ref.shape[0])], axis=1)
    return joined[:, :width]


def join_tiles(parts, width):
    return jnp.concatenate(parts, axis=1)[:, :width]


def exchange_copy(step, send, target, other, send_sem, recv_sem):
    return pltpu.make_async_remote_copy(
        src_ref=send,
        dst_ref=target,
        send_sem=send_sem.at[step],
        recv_sem=recv_sem.at[step],
        device_id={"t": other},
        device_id_type=MESH,
    )


def exchange_start(count, me, send, slots, send_sem, recv_sem):
    for step in range(1, count):
        exchange_copy(step, send, slots.at[me], lax.rem(me + step, count), send_sem, recv_sem).start()


def exchange_wait(count, me, send, slots, send_sem, recv_sem):
    for step in range(1, count):
        other = lax.rem(me + count - step, count)
        exchange_copy(step, send, slots.at[other], other, send_sem, recv_sem).wait()


def mixer_forward_kernel(
    count, seg, rows_here, branches_far, ids, ids_before, ids_after, gate_blocks, vec_ref, cot, quarters,
    conv_out, decay_out, states_out, mixed_out, halo_out, cin_out, mask, cot_out, swapped,
    drive, h_ref, a_ref, ext, halo_send, halo_recv, summary, slots, send_sem, recv_sem, halo_sems,
    gather_send, gather_recv, swap_send, swap_recv, branches, wg, load,
):
    place = Place()
    me = lax.axis_index("t")
    loaded = pltpu.make_async_copy(branches_far, branches, load.at[0])
    loaded.start()
    place.greet([place.peer(0, 1, 1)] + [{"t": lax.rem(me + step, count)} for step in range(1, count)])
    gather = Gather(place, cot, cot_out, gather_send, gather_recv)
    move = Swap(quarters, swapped, swap_send, swap_recv)
    gather.begin_whole()
    move.begin()
    spread_blocks(gate_blocks, wg)
    rows = 8
    width = branches.shape[1] // 2
    loaded.wait()

    def recur_at(at):
        return branches[at, width:].astype(BF16).astype(F32)

    for r in range(rows):
        halo_send[r * HALO : (r + 1) * HALO, :] = recur_at(pl.ds((rows + r + 1) * seg - HALO, HALO))
    halo_copy = pltpu.make_async_remote_copy(
        src_ref=halo_send,
        dst_ref=halo_recv,
        send_sem=halo_sems.at[0],
        recv_sem=halo_sems.at[1],
        device_id={"t": lax.rem(me + 1, count)},
        device_id_type=MESH,
    )
    halo_copy.start()
    for r in range(rows):
        halo_out[(rows + r) * HALO : (rows + r + 1) * HALO, :] = recur_at(pl.ds((r + 1) * seg - HALO, HALO))
    vec = vec_ref[...]

    def ids_of(ref, s):
        chunk = s // rows_here
        return ref[chunk, s % rows_here : s % rows_here + 1, :]

    nothing = jnp.zeros((1, LANES), F32)
    for s in range(2 * rows):
        here = ids_of(ids, s)
        back = ids_of(ids, s - rows) if s >= rows else jnp.where(me > 0, ids_of(ids_before, s + rows), nothing)
        ahead = ids_of(ids, s + rows) if s < rows else jnp.where(me < count - 1, ids_of(ids_after, s - rows), nothing)
        lines = [jnp.concatenate([back[:, seg - k :], here[:, : seg - k]], axis=1) for k in (1, 2, 3)]
        lines += [jnp.concatenate([here[:, k:], ahead[:, :k]], axis=1) for k in (1, 2, 3)]
        lines = [jnp.where(line == here, 1.0, 0.0) for line in lines] + [nothing] * 2
        mask[s * seg : (s + 1) * seg, :] = jnp.concatenate(lines, axis=0).T

    def local(s, none):
        at = pl.ds(pl.multiple_of(s * seg, seg), seg)
        x = recur_at(at)
        ext[0:HALO, :] = halo_out[pl.ds(pl.multiple_of(s * HALO, HALO), HALO), :]
        ext[HALO : HALO + seg, :] = x
        m = mask[at, :]
        conv = vec[4:5] + vec[0:1] * x
        for k in range(1, 4):
            conv = conv + vec[k : k + 1] * ext[HALO - k : HALO - k + seg, :] * m[:, k - 1 : k]
        conv_low = conv.astype(BF16)
        conv_out[at, :] = conv_low
        recur_gate, input_gate, log_decay = gate_values(conv_low, wg[0], wg[1], vec)
        keep = m[:, 0:1]
        kept = jnp.exp(log_decay)
        put_tiles(decay_out, at, kept * keep)
        scale = (1.0 - keep) + keep * jnp.sqrt(one_minus_exp(-2.0 * log_decay, kept * kept))
        put_tiles(drive, at, scale * input_gate * conv_low.astype(F32))
        return none

    lax.fori_loop(rows, 2 * rows, local, 0)
    halo_copy.wait()
    for r in range(rows):
        halo_out[r * HALO : (r + 1) * HALO, :] = halo_recv[r * HALO : (r + 1) * HALO, :]
    gather.pass_first()
    lax.fori_loop(0, rows, local, 0)
    tiles, lanes = drive.shape[0], drive.shape[2]

    def scan(k, carried):
        at = pl.ds(k, 2 * rows, stride=seg)
        after = []
        for j in range(tiles):
            h, a = carried[j]
            d = decay_out[j, at, :]
            h = d * h + drive[j, at, :]
            a = a * d
            h_ref[j, at, :] = h
            a_ref[j, at, :] = a
            after.append((h, a))
        return tuple(after)

    start = (jnp.zeros((2 * rows, lanes), F32), jnp.ones((2 * rows, lanes), F32))
    last = lax.fori_loop(0, seg, scan, (start,) * tiles, unroll=4)
    last_h = join_tiles([part[0] for part in last], width)
    last_a = join_tiles([part[1] for part in last], width)
    summary[0:rows, :] = last_a[rows:] * last_a[:rows]
    summary[rows : 2 * rows, :] = last_a[rows:] * last_h[:rows] + last_h[rows:]
    exchange_start(count, me, summary, slots, send_sem, recv_sem)
    gather.pass_second()

    def activate(s, none):
        at = pl.ds(pl.multiple_of(s * seg, seg), seg)
        act, _ = gelu_parts(branches[at, :width])
        states_out[at, :] = act
        return none

    lax.fori_loop(0, 2 * rows, activate, 0)
    exchange_wait(count, me, summary, slots, send_sem, recv_sem)
    carry = jnp.zeros((rows, width), F32)
    for z in range(count - 1):
        carry = jnp.where(z < me, slots[z, 0:rows, :] * carry + slots[z, rows : 2 * rows, :], carry)
    cin_out[0:rows, :] = carry
    cin_out[rows : 2 * rows, :] = last_a[:rows] * carry + last_h[:rows]

    def finish(s, none):
        at = pl.ds(pl.multiple_of(s * seg, seg), seg)
        states = get_tiles(h_ref, at, width) + get_tiles(a_ref, at, width) * cin_out[pl.ds(s, 1), :]
        act = states_out[at, :]
        states_out[at, :] = states
        mixed_out[at, :] = (act * states.astype(BF16).astype(F32)).astype(BF16)
        return none

    lax.fori_loop(0, 2 * rows, finish, 0)
    gather.pass_third()
    gather.finish()
    move.finish()


def mixer_backward_kernel(
    count, seg, grad_mixed_far, branches_far, states_far, decay_far, conv_far, mask_far, halo, cin, gate_blocks, vec_ref,
    hidden, w_down, middle_far, reduced0, reduced1, grad_out, gw0_out, gw1_out, small_out, outputs, owned0, owned1,
    tot, prod, ext, halo_send, halo_recv, summary, slots, uin, send_sem, recv_sem, halo_sems,
    grad_mixed, branches, states, decay, conv_low_ref, mask, middle, wg, load, own0, own1, own2, own3, *buffers,
):
    place = Place()
    pairs = (
        (grad_mixed_far, grad_mixed),
        (branches_far, branches),
        (states_far, states),
        (decay_far, decay),
        (conv_far, conv_low_ref),
        (mask_far, mask),
        (middle_far, middle),
    )
    loads = [pltpu.make_async_copy(far, near, load.at[n]) for n, (far, near) in enumerate(pairs)]
    for part in loads:
        part.start()
    me = lax.axis_index("t")
    place.greet([place.peer(*offset) for offset in BEYOND] + [{"t": lax.rem(me + step, count)} for step in range(1, count)])
    scatter = Scatter(place, pair_product([hidden], [w_down], outputs.shape[0]), *buffers)
    owners = [Owners(place, reduced0, owned0, own0, own1), Owners(place, reduced1, owned1, own2, own3)]
    spread_blocks(gate_blocks, wg)
    scatter.run_first()
    for part in owners:
        part.begin()
    for part in loads:
        part.wait()
    rows = 8
    width = branches.shape[1] // 2
    vec = vec_ref[...]

    def local(s, none):
        at = pl.ds(pl.multiple_of(s * seg, seg), seg)
        act, slope = gelu_parts(branches[at, :width])
        gm = grad_mixed[at, :].astype(F32)
        grad_out[at, :width] = (gm * states[at, :].astype(BF16).astype(F32) * slope).astype(BF16)
        put_tiles(tot, at, (gm * act).astype(BF16).astype(F32))
        return none

    lax.fori_loop(0, 2 * rows, local, 0)

    tiles, lanes = tot.shape[0], tot.shape[2]

    def scan(k, carried):
        at = pl.ds(seg - 1 - k, 2 * rows, stride=seg)
        after = []
        for j in range(tiles):
            u, p = carried[j]
            d = decay[j, at, :]
            total = tot[j, at, :] + u
            tot[j, at, :] = total
            prod[j, at, :] = p
            after.append((d * total, d * p))
        return tuple(after)

    start = (jnp.zeros((2 * rows, lanes), F32), jnp.ones((2 * rows, lanes), F32))
    last = lax.fori_loop(0, seg, scan, (start,) * tiles, unroll=4)
    u = join_tiles([part[0] for part in last], width)
    p = join_tiles([part[1] for part in last], width)
    summary[0:rows, :] = p[:rows] * p[rows:]
    summary[rows : 2 * rows, :] = p[:rows] * u[rows:] + u[:rows]
    exchange_start(count, me, summary, slots, send_sem, recv_sem)
    scatter.run_second()
    exchange_wait(count, me, summary, slots, send_sem, recv_sem)
    carry = jnp.zeros((rows, width), F32)
    for z in range(count - 1, 0, -1):
        carry = jnp.where(z > me, slots[z, 0:rows, :] * carry + slots[z, rows : 2 * rows, :], carry)
    uin[rows : 2 * rows, :] = carry
    uin[0:rows, :] = p[rows:] * carry + u[rows:]
    gw0_out[...] = jnp.zeros_like(gw0_out)
    gw1_out[...] = jnp.zeros_like(gw1_out)
    small_out[...] = jnp.zeros_like(small_out)

    def gates(s, none):
        at = pl.ds(pl.multiple_of(s * seg, seg), seg)
        total = get_tiles(tot, at, width) + get_tiles(prod, at, width) * uin[pl.ds(s, 1), :]
        ext[HALO - 1 : HALO, :] = cin[pl.ds(s, 1), :]
        ext[HALO : HALO + seg, :] = states[at, :]
        before = ext[HALO - 1 : HALO - 1 + seg, :]
        conv_low = conv_low_ref[at, :]
        conv_vals = conv_low.astype(F32)
        m = mask[at, :]
        keep = m[:, 0:1]
        recur_gate, input_gate, log_decay = gate_values(conv_low, wg[0], wg[1], vec)
        power = jnp.exp(2.0 * log_decay)
        root = jnp.sqrt(one_minus_exp(-2.0 * log_decay, power))
        scale = (1.0 - keep) + keep * root
        driven_in = total * conv_vals
        grad_log = total * before * get_tiles(decay, at, width) - driven_in * input_gate * keep * (power / root)
        grad0 = grad_log * log_decay * (1.0 - recur_gate)
        grad1 = driven_in * scale * input_gate * (1.0 - input_gate)
        low0 = grad0.astype(BF16)
        low1 = grad1.astype(BF16)
        inputs_of = (((1,), (1,)), ((), ()))
        grad_conv = (
            total * scale * input_gate
            + lax.dot_general(low0, wg[0], inputs_of, preferred_element_type=F32)
            + lax.dot_general(low1, wg[1], inputs_of, preferred_element_type=F32)
        )
        put_tiles(tot, at, grad_conv)
        turned = (((0,), (0,)), ((), ()))
        gw0_out[...] += lax.dot_general(conv_low, low0, turned, preferred_element_type=F32)
        gw1_out[...] += lax.dot_general(conv_low, low1, turned, preferred_element_type=F32)
        x = branches[at, width:].astype(BF16).astype(F32)
        ext[0:HALO, :] = halo[pl.ds(pl.multiple_of(s * HALO, HALO), HALO), :]
        ext[HALO : HALO + seg, :] = x

        def add(row, values):
            small_out[row : row + 1, :] += jnp.sum(values, axis=0, keepdims=True)

        add(0, grad_conv * x)
        for k in range(1, 4):
            add(k, grad_conv * ext[HALO - k : HALO - k + seg, :] * m[:, k - 1 : k])
        add(4, grad_conv)
        add(5, grad0)
        add(6, grad1)
        add(7, grad_log * recur_gate)
        return none

    lax.fori_loop(0, 2 * rows, gates, 0)
    small_out[7:8, :] = small_out[7:8, :] * vec[8:9]
    for r in range(rows):
        halo_send[r * HALO : (r + 1) * HALO, :] = get_tiles(tot, pl.ds(r * seg, HALO), width)
    halo_copy = pltpu.make_async_remote_copy(
        src_ref=halo_send,
        dst_ref=halo_recv,
        send_sem=halo_sems.at[0],
        recv_sem=halo_sems.at[1],
        device_id={"t": lax.rem(me + count - 1, count)},
        device_id_type=MESH,
    )
    halo_copy.start()

    def back(s, none):
        at = pl.ds(pl.multiple_of(s * seg, seg), seg)
        m = mask[at, :]
        grad_conv = get_tiles(tot, at, width)
        ext[0:seg, :] = grad_conv
        result = vec[0:1] * grad_conv

        @pl.when(s < rows)
        def _():
            ext[seg : seg + HALO, :] = get_tiles(tot, pl.ds(pl.multiple_of((s + rows) * seg, seg), HALO), width)

        @pl.when(s >= rows)
        def _():
            ext[seg : seg + HALO, :] = halo_recv[pl.ds(pl.multiple_of((s - rows) * HALO, HALO), HALO), :]

        for k in range(1, 4):
            result = result + vec[k : k + 1] * ext[k : k + seg, :] * m[:, 2 + k : 3 + k]
        grad_out[at, width:] = result.astype(BF16)
        return none

    lax.fori_loop(0, rows, back, 0)
    halo_copy.wait()
    lax.fori_loop(rows, 2 * rows, back, 0)
    scatter.run_third(0)
    scatter.run_third(1)

    def body(at):
        outputs[at, :] = (middle[at, :] + scatter.rows(at)).astype(BF16)

    for_slices(0, outputs.shape[0], body)
    scatter.finish()
    for part in owners:
        part.finish()


def whole(count):
    return [pl.BlockSpec(memory_space=pltpu.VMEM)] * count


def mixer_params(number):
    return pltpu.CompilerParams(collective_id=number, has_side_effects=True, vmem_limit_bytes=60 * 1024 * 1024)


def mixer_forward(count, seg, rows_here, branches, ids, gate_blocks, vec, cot, quarters):
    n, width = branches.shape[0], branches.shape[1] // 2
    full = functools.partial(jax.ShapeDtypeStruct, (n, width))
    tiles = -(-width // LANES)
    tiled = jax.ShapeDtypeStruct((tiles, n, LANES), F32)
    groups, kinds, part, depth = quarters.shape
    return pl.pallas_call(
        functools.partial(mixer_forward_kernel, count, seg, rows_here),
        name="mixer_forward",
        out_shape=(
            full(BF16), tiled, full(F32), full(BF16),
            jax.ShapeDtypeStruct((16 * HALO, width), F32), jax.ShapeDtypeStruct((16, width), F32),
            jax.ShapeDtypeStruct((n, 8), F32),
            jax.ShapeDtypeStruct((8 * cot.shape[0], cot.shape[1]), BF16),
            jax.ShapeDtypeStruct((kinds, groups, part, depth), BF16),
        ),
        in_specs=[ANYWHERE, *whole(5), ANYWHERE, ANYWHERE],
        out_specs=(*whole(7), ANYWHERE, ANYWHERE),
        scratch_shapes=[
            pltpu.VMEM((tiles, n, LANES), F32),
            pltpu.VMEM((tiles, n, LANES), F32),
            pltpu.VMEM((tiles, n, LANES), F32),
            pltpu.VMEM((seg + HALO, width), F32),
            pltpu.VMEM((8 * HALO, width), F32),
            pltpu.VMEM((8 * HALO, width), F32),
            pltpu.VMEM((16, width), F32),
            pltpu.VMEM((count, 16, width), F32),
            pltpu.SemaphoreType.DMA((count,)),
            pltpu.SemaphoreType.DMA((count,)),
            pltpu.SemaphoreType.DMA((2,)),
            *GATHER_SCRATCH,
            *swap_scratch(groups),
            pltpu.VMEM(branches.shape, F32),
            pltpu.VMEM((2, width, width), BF16),
            pltpu.SemaphoreType.DMA((1,)),
        ],
        compiler_params=mixer_params(1),
    )(branches, *ids, gate_blocks, vec, cot, quarters)


def mixer_backward(count, seg, grad_mixed, branches, states, decay, conv_low, mask, halo, cin, gate_blocks, vec, hidden, w_down, middle, reduced):
    n, width = branches.shape[0], branches.shape[1] // 2
    tokens, depth = n // 8, w_down.shape[1]
    full = functools.partial(jax.ShapeDtypeStruct, (n, width))
    tiles = -(-width // LANES)
    tiled = jax.ShapeDtypeStruct((tiles, n, LANES), F32)
    return pl.pallas_call(
        functools.partial(mixer_backward_kernel, count, seg),
        name="mixer_backward",
        out_shape=(
            jax.ShapeDtypeStruct((n, 2 * width), BF16),
            jax.ShapeDtypeStruct((width, width), F32), jax.ShapeDtypeStruct((width, width), F32),
            jax.ShapeDtypeStruct((8, width), F32), jax.ShapeDtypeStruct((tokens, depth), BF16),
            *[jax.ShapeDtypeStruct(part.shape, BF16) for part in reduced],
        ),
        in_specs=[*[ANYWHERE] * 6, *whole(6), *[ANYWHERE] * 3],
        out_specs=(*whole(5), *[ANYWHERE] * 2),
        scratch_shapes=[
            pltpu.VMEM((tiles, n, LANES), F32),
            pltpu.VMEM((tiles, n, LANES), F32),
            pltpu.VMEM((seg + HALO, width), F32),
            pltpu.VMEM((8 * HALO, width), F32),
            pltpu.VMEM((8 * HALO, width), F32),
            pltpu.VMEM((16, width), F32),
            pltpu.VMEM((count, 16, width), F32),
            pltpu.VMEM((16, width), F32),
            pltpu.SemaphoreType.DMA((count,)),
            pltpu.SemaphoreType.DMA((count,)),
            pltpu.SemaphoreType.DMA((2,)),
            *[pltpu.VMEM(part.shape, part.dtype) for part in (grad_mixed, branches, states, decay, conv_low, mask, middle)],
            pltpu.VMEM((2, width, width), BF16),
            pltpu.SemaphoreType.DMA((7,)),
            *[pltpu.SemaphoreType.DMA((8,))] * 4,
            *Scatter.scratch(tokens, depth),
        ],
        compiler_params=mixer_params(2),
    )(grad_mixed, branches, states, decay, conv_low, mask, halo, cin, gate_blocks, vec, hidden, w_down, middle, *reduced)


class Place:
    def __init__(self):
        self.i, self.g, self.c = lax.axis_index("i"), lax.axis_index("g"), lax.axis_index("c")
        self.core, self.across, self.along = {"c": 1 - self.c}, {"g": 1 - self.g}, {"i": 1 - self.i}

    def chunk(self, di, dg, dc):
        i = 1 - self.i if di else self.i
        g = 1 - self.g if dg else self.g
        c = 1 - self.c if dc else self.c
        return (i * 2 + g) * 2 + c

    def peer(self, di, dg, dc):
        return {
            "i": 1 - self.i if di else self.i,
            "g": 1 - self.g if dg else self.g,
            "c": 1 - self.c if dc else self.c,
        }

    def greet(self, more=()):
        barrier = pltpu.get_barrier_semaphore()
        peers = [self.core, self.across, self.along, *more]
        for peer in peers:
            pl.semaphore_signal(barrier, inc=1, device_id=peer, device_id_type=MESH)
        pl.semaphore_wait(barrier, len(peers))


class Gather:
    COPIES = 12

    def __init__(self, place, block, out, send, recv):
        self.place, self.block, self.out, self.send, self.recv = place, block, out, send, recv
        self.tokens = block.shape[0]
        self.half = self.tokens // 2

    def rows(self, chunk, part):
        start = chunk * self.tokens + (self.half if part == 1 else 0)
        return self.out.at[pl.ds(pl.multiple_of(start, self.half), self.tokens if part == 2 else self.half)]

    def mine(self, part):
        if part == 2:
            return self.block
        return self.block.at[pl.ds(part * self.half, self.half)]

    def copy(self, number, source, chunk, part, peer):
        return pltpu.make_async_remote_copy(
            src_ref=source,
            dst_ref=self.rows(chunk, part),
            send_sem=self.send.at[number],
            recv_sem=self.recv.at[number],
            device_id=peer,
            device_id_type=MESH,
        )

    def begin(self, part, whole=False):
        place = self.place
        own = place.chunk(0, 0, 0)
        other = 1 - part if whole else part
        self.give(0 + part, own, part, place.across)
        self.give(2 + other, own, other, place.along)
        self.give(4 + part, own, part, place.core)
        keep = pltpu.make_async_copy(self.mine(part), self.rows(own, part), self.send.at[self.COPIES + part])
        keep.start()
        self.local = getattr(self, "local", []) + [keep]

    def begin_whole(self):
        self.begin(0, True)
        self.begin(1, True)

    def give(self, number, chunk, part, peer):
        moved = self.copy(number, self.mine(part), chunk, part, peer)
        moved.start()
        self.kept = getattr(self, "kept", []) + [moved]

    def arrived(self, number, chunk, part):
        self.copy(number, self.rows(chunk, part), chunk, part, self.place.core).wait_recv()

    def forward(self, number, chunk, part, peer):
        moved = self.copy(number, self.rows(chunk, part), chunk, part, peer)
        moved.start()
        self.kept.append(moved)

    def pass_first(self):
        place = self.place
        ax, al = place.chunk(0, 1, 0), place.chunk(1, 0, 0)
        self.arrived(0, ax, 0)
        self.forward(6, ax, 0, place.along)
        self.arrived(3, al, 1)
        self.forward(7, al, 1, place.across)

    def pass_second(self):
        place = self.place
        ax, al = place.chunk(0, 1, 0), place.chunk(1, 0, 0)
        self.arrived(1, ax, 1)
        self.forward(8, ax, 2, place.core)
        self.arrived(2, al, 0)
        self.forward(9, al, 2, place.core)

    def pass_third(self):
        dia = self.place.chunk(1, 1, 0)
        self.arrived(6, dia, 0)
        self.forward(10, dia, 0, self.place.core)
        self.arrived(7, dia, 1)
        self.forward(11, dia, 1, self.place.core)

    def pass_on(self):
        self.pass_first()
        self.pass_second()
        self.pass_third()

    def finish_core(self):
        for part in (0, 1):
            self.arrived(4 + part, self.place.chunk(0, 0, 1), part)

    def finish_near(self):
        self.arrived(8, self.place.chunk(0, 1, 1), 2)
        self.arrived(9, self.place.chunk(1, 0, 1), 2)

    def finish_far(self):
        for part in (0, 1):
            self.arrived(10 + part, self.place.chunk(1, 1, 1), part)

    def finish(self):
        self.finish_core()
        self.finish_near()
        self.finish_far()
        self.finish_sends()

    def finish_sends(self):
        for moved in self.kept:
            moved.wait_send()
        for keep in self.local:
            keep.wait()


OTHERS = [(di, dg, dc) for di in (0, 1) for dg in (0, 1) for dc in (0, 1) if di or dg or dc]


def first_gather_kernel(count, normed, ids, normed_out, ids_out, before_out, after_out, plane_ids, before, after, send, recv, ids_send, ids_recv):
    place = Place()
    me = lax.axis_index("t")
    up, down = {"t": lax.rem(me + 1, count)}, {"t": lax.rem(me + count - 1, count)}
    place.greet([place.peer(*offset) for offset in OTHERS if sum(offset) > 1] + [up, down])
    gather = Gather(place, normed, normed_out, send, recv)
    own = place.chunk(0, 0, 0)
    moved = []

    def move(number, source, target, peer):
        copy = pltpu.make_async_remote_copy(
            src_ref=source,
            dst_ref=target,
            send_sem=ids_send.at[number],
            recv_sem=ids_recv.at[number],
            device_id=peer,
            device_id_type=MESH,
        )
        copy.start()
        moved.append(copy)

    for number, offset in enumerate(OTHERS):
        move(number, ids, plane_ids.at[own], place.peer(*offset))
    gather.begin_whole()
    plane_ids[own] = ids[...]
    for number, offset in enumerate(OTHERS):
        chunk = place.chunk(*offset)
        pltpu.make_async_remote_copy(
            src_ref=ids,
            dst_ref=plane_ids.at[chunk],
            send_sem=ids_send.at[number],
            recv_sem=ids_recv.at[number],
            device_id=place.peer(*offset),
            device_id_type=MESH,
        ).wait_recv()
    move(7, plane_ids, before, up)
    move(8, plane_ids, after, down)
    gather.pass_on()
    for copy in moved[7:]:
        copy.wait_recv()
    for copy in moved:
        copy.wait_send()
    ids_out[...] = plane_ids[...]
    before_out[...] = before[...]
    after_out[...] = after[...]
    gather.finish()


class Scatter:
    def __init__(self, place, product, core_send, core_recv, held, acc, across_recv, along_recv, second, second_recv, send, recv):
        self.place, self.product = place, product
        self.core_send, self.core_recv, self.held, self.acc = core_send, core_recv, held, acc
        self.across_recv, self.along_recv, self.second, self.second_recv = across_recv, along_recv, second, second_recv
        self.send, self.recv = send, recv
        self.kept = []

    def copy(self, number, source, target, peer):
        return pltpu.make_async_remote_copy(
            src_ref=source,
            dst_ref=target,
            send_sem=self.send.at[number],
            recv_sem=self.recv.at[number],
            device_id=peer,
            device_id_type=MESH,
        )

    def start(self, *parts):
        moved = self.copy(*parts)
        moved.start()
        self.kept.append(moved)

    def run_first(self):
        place = self.place
        order = ((1, 1), (0, 1), (1, 0), (0, 0))
        tile = 256
        per_half = self.held.shape[3] // tile
        def give(di, dg):
            q = 2 * di + dg
            chunk = place.chunk(di, dg, 1)

            def send_tile(n, none):
                at = pl.ds(pl.multiple_of(n % per_half * tile, tile), tile)
                self.core_send[q, n // per_half, :, at] = self.product(chunk, n).astype(BF16)
                return none

            lax.fori_loop(0, 2 * per_half, send_tile, 0)
            self.start(q, self.core_send.at[q], self.core_recv.at[q], place.core)

        def take(di, dg):
            q = 2 * di + dg
            chunk = place.chunk(di, dg, 0)
            self.copy(q, self.core_send.at[q], self.core_recv.at[q], place.core).wait_recv()

            def sum_tile(n, none):
                at = pl.ds(pl.multiple_of(n % per_half * tile, tile), tile)
                value = self.product(chunk, n) + self.core_recv[q, n // per_half, :, at].astype(F32)
                if q:
                    self.held[q - 1, n // per_half, :, at] = value.astype(BF16)
                else:
                    self.acc[n // per_half, :, at] = value
                return none

            lax.fori_loop(0, 2 * per_half, sum_tile, 0)
            if dg:
                self.start(4 + di, self.held.at[q - 1, 0], self.across_recv.at[di], place.across)
            if di:
                self.start(6 + dg, self.held.at[q - 1, 1], self.along_recv.at[dg], place.along)

        give(*order[0])
        give(*order[1])
        take(*order[0])
        give(*order[2])
        take(*order[1])
        give(*order[3])
        take(*order[2])
        take(*order[3])

    def second_copy(self, half, part):
        tokens = self.second.shape[1] // 2
        at = pl.ds(part * tokens, tokens)
        peer = self.place.across if half else self.place.along
        return 8 + 2 * part + half, self.second.at[half, at], self.second_recv.at[half, at], peer

    def run_second(self):
        place = self.place
        tokens = self.second.shape[1] // 2
        for part in (0, 1):
            for half, number, buffer, mine in ((0, 5, self.across_recv, 2), (1, 7, self.along_recv, 1)):
                if part == 0:
                    self.copy(number, buffer.at[1], buffer.at[1], place.core).wait_recv()

                def add_rows(at):
                    total = self.held[mine - 1, half, at, :].astype(F32) + buffer[1, at, :].astype(F32)
                    self.second[half, at, :] = total.astype(BF16)

                for_slices(part * tokens, (part + 1) * tokens, add_rows)
                self.start(*self.second_copy(half, part))

    def run_third(self, part):
        place = self.place
        if part == 0:
            for number, buffer in ((4, self.across_recv), (6, self.along_recv)):
                self.copy(number, buffer.at[0], buffer.at[0], place.core).wait_recv()
        for half in (0, 1):
            self.copy(*self.second_copy(half, part)).wait_recv()

    def rows(self, at):
        first = self.acc[0, at, :] + self.across_recv[0, at, :].astype(F32) + self.second_recv[0, at, :].astype(F32)
        last = self.acc[1, at, :] + self.along_recv[0, at, :].astype(F32) + self.second_recv[1, at, :].astype(F32)
        return jnp.concatenate([first, last], axis=1)

    def finish(self):
        for moved in self.kept:
            moved.wait_send()

    @staticmethod
    def scratch(tokens, width):
        half = width // 2
        return [
            pltpu.VMEM((4, 2, tokens, half), BF16),
            pltpu.VMEM((4, 2, tokens, half), BF16),
            pltpu.VMEM((3, 2, tokens, half), BF16),
            pltpu.VMEM((2, tokens, half), F32),
            pltpu.VMEM((2, tokens, half), BF16),
            pltpu.VMEM((2, tokens, half), BF16),
            pltpu.VMEM((2, tokens, half), BF16),
            pltpu.VMEM((2, tokens, half), BF16),
            pltpu.SemaphoreType.DMA((12,)),
            pltpu.SemaphoreType.DMA((12,)),
        ]


SCATTER_BUFFERS = 10


def pair_product(lefts, rights, tokens):
    def product(chunk, n):
        at = pl.ds(pl.multiple_of(chunk * tokens, tokens), tokens)
        cols = pl.ds(pl.multiple_of(n * 256, 256), 256)
        total = None
        for left, right in zip(lefts, rights):
            term = jnp.dot(left[at, :], right[:, cols], preferred_element_type=F32)
            total = term if total is None else total + term
        return total

    return product


def for_slices(start, stop, body):
    def step(n, none):
        body(pl.ds(pl.multiple_of(n * SLICE, SLICE), SLICE))
        return none

    lax.fori_loop(start // SLICE, stop // SLICE, step, 0)


def middle_kernel(left, right, own_in, gain, middle_out, gathered, *scratch):
    buffers, (block, send, recv) = scratch[:SCATTER_BUFFERS], scratch[SCATTER_BUFFERS:]
    tokens = own_in.shape[0]
    place = Place()
    place.greet()
    scatter = Scatter(place, pair_product([left], [right], tokens), *buffers)
    scatter.run_first()
    scatter.run_second()

    def body(at):
        middle = own_in[at, :].astype(F32) + scatter.rows(at)
        middle_out[at, :] = middle
        block[at, :] = (middle * rms(middle) * gain[...]).astype(BF16)

    gather = Gather(place, block, gathered, send, recv)
    for part in (0, 1):
        scatter.run_third(part)
        for_slices(part * tokens // 2, (part + 1) * tokens // 2, body)
        gather.begin(part)
    gather.pass_on()
    scatter.finish()
    gather.finish()


def turn_kernel(
    left0, left1, right0, right1, middle, gain, cot, w_out, normed_far,
    grad_middle_out, gain_out, grads_out, mixed_out, gathered, *scratch,
):
    buffers, (block, send, recv, normed, chunk_ref, load) = scratch[:SCATTER_BUFFERS], scratch[SCATTER_BUFFERS:]
    loaded = pltpu.make_async_copy(normed_far, normed, load.at[0])
    loaded.start()
    tokens = cot.shape[0]
    place = Place()
    place.greet()
    scatter = Scatter(place, pair_product([left0, left1], [right0, right1], tokens), *buffers)
    def weight_grads(start, stop):
        def step(n, none):
            at = pl.ds(pl.multiple_of(n * 256, 256), 256)
            value = lax.dot_general(normed[:, at], left1[...], (((0,), (0,)), ((), ())), preferred_element_type=F32)
            grads_out[at, :] = value.astype(BF16)
            return none

        lax.fori_loop(start, stop, step, 0)

    steps = normed.shape[1] // 256
    scatter.run_first()
    loaded.wait()
    weight_grads(0, steps // 4)
    scatter.run_second()
    weight_grads(steps // 4, steps // 2)
    gain_out[...] = jnp.zeros_like(gain_out)

    def body(at):
        values = middle[at, :]
        grad = scatter.rows(at)
        scale = rms(values)
        weighted = grad * gain[...]
        inner = jnp.mean(values * weighted, axis=-1, keepdims=True)
        total = cot[at, :].astype(F32) + scale * weighted - values * (scale * scale * scale * inner)
        grad_middle_out[at, :] = total
        block[at, :] = total.astype(BF16)
        term = grad * values * scale
        gain_out[...] += term[0:8] + term[8:16]

    gather = Gather(place, block, gathered, send, recv)
    for part in (0, 1):
        scatter.run_third(part)
        for_slices(part * tokens // 2, (part + 1) * tokens // 2, body)
        gather.begin(part)
    weight_grads(steps // 2, 3 * steps // 4)
    gather.pass_first()
    weight_grads(3 * steps // 4, steps)
    gather.pass_second()

    def mixed_back(source, chunk):
        at = pl.ds(pl.multiple_of(chunk * tokens, tokens), tokens)
        if source is None:
            fetch = pltpu.make_async_copy(gathered.at[at], chunk_ref, load.at[0])
            fetch.start()
            fetch.wait()
            source = chunk_ref
        value = lax.dot_general(source[...], w_out[...], (((1,), (1,)), ((), ())), preferred_element_type=F32)
        mixed_out[at, :] = value

    mixed_back(block, place.chunk(0, 0, 0))
    mixed_back(None, place.chunk(0, 1, 0))
    mixed_back(None, place.chunk(1, 0, 0))
    gather.finish_core()
    mixed_back(None, place.chunk(0, 0, 1))
    gather.pass_third()
    mixed_back(None, place.chunk(1, 1, 0))
    gather.finish_near()
    mixed_back(None, place.chunk(0, 1, 1))
    mixed_back(None, place.chunk(1, 0, 1))
    gather.finish_far()
    mixed_back(None, place.chunk(1, 1, 1))
    scatter.finish()
    gather.finish_sends()


class Owners:
    def __init__(self, place, reduced, out, send, recv):
        self.place, self.reduced, self.out, self.send, self.recv = place, reduced, out, send, recv
        self.own = place.chunk(0, 0, 0)

    def copy(self, number, offset, slot):
        return pltpu.make_async_remote_copy(
            src_ref=self.reduced.at[self.place.chunk(*offset)],
            dst_ref=self.out.at[slot],
            send_sem=self.send.at[number],
            recv_sem=self.recv.at[number],
            device_id=self.place.peer(*offset),
            device_id_type=MESH,
        )

    def begin(self):
        self.keep = pltpu.make_async_copy(self.reduced.at[self.own], self.out.at[self.own], self.send.at[7])
        self.keep.start()
        self.moved = [self.copy(number, offset, self.own) for number, offset in enumerate(OTHERS)]
        for copy in self.moved:
            copy.start()

    def finish(self):
        for number, offset in enumerate(OTHERS):
            self.copy(number, offset, self.place.chunk(*offset)).wait_recv()
        for copy in self.moved:
            copy.wait_send()
        self.keep.wait()


OWNERS_SCRATCH = [pltpu.SemaphoreType.DMA((8,))] * 2
BEYOND = [offset for offset in OTHERS if sum(offset) > 1]


class GateSums:
    def __init__(self, place, count, pieces, rows_recv, gates_all, send, recv):
        self.place, self.count, self.pieces = place, count, pieces
        self.rows_recv, self.gates_all, self.send, self.recv = rows_recv, gates_all, send, recv
        self.me = lax.axis_index("t")
        self.rank = place.g * 2 + place.c
        self.near = [offset for offset in OTHERS if not offset[0]]
        self.moved = []

    def copy(self, number, source, target, peer):
        return pltpu.make_async_remote_copy(
            src_ref=source,
            dst_ref=target,
            send_sem=self.send.at[number],
            recv_sem=self.recv.at[number],
            device_id=peer,
            device_id_type=MESH,
        )

    def begin(self):
        for number, offset in enumerate(self.near):
            other = lax.rem(self.place.chunk(*offset), 4)
            self.moved.append(self.copy(number, self.pieces.at[other], self.rows_recv.at[self.rank], self.place.peer(*offset)))
            self.moved[-1].start()
        self.rows_recv[self.rank] = self.pieces[self.rank]

    def pass_on(self):
        for number, offset in enumerate(self.near):
            other = lax.rem(self.place.chunk(*offset), 4)
            self.copy(number, self.pieces.at[other], self.rows_recv.at[other], self.place.peer(*offset)).wait_recv()
        for step in range(1, self.count):
            to = lax.rem(self.me + step, self.count)
            self.moved.append(self.copy(2 + step, self.rows_recv.at[to], self.gates_all.at[self.me], {"t": to}))
            self.moved[-1].start()
        self.gates_all[self.me] = self.rows_recv[self.me]

    def finish(self, out):
        for step in range(1, self.count):
            other = lax.rem(self.me + self.count - step, self.count)
            self.copy(2 + step, self.rows_recv.at[other], self.gates_all.at[other], {"t": other}).wait_recv()
        total = self.gates_all[0].astype(F32)
        for z in range(1, self.count):
            total = total + self.gates_all[z].astype(F32)
        out[...] = total
        for copy in self.moved:
            copy.wait_send()


def sum_everywhere(place, count, values, inbox, plane_sum, plane_box, send, recv):
    me = lax.axis_index("t")
    own = place.chunk(0, 0, 0)
    moved = []

    def copy(number, source, target, peer):
        return pltpu.make_async_remote_copy(
            src_ref=source,
            dst_ref=target,
            send_sem=send.at[number],
            recv_sem=recv.at[number],
            device_id=peer,
            device_id_type=MESH,
        )

    for number, offset in enumerate(OTHERS):
        moved.append(copy(number, values, inbox.at[own], place.peer(*offset)))
        moved[-1].start()
    inbox[own] = values[...]
    for number, offset in enumerate(OTHERS):
        copy(number, values, inbox.at[place.chunk(*offset)], place.peer(*offset)).wait_recv()
    total = inbox[0]
    for n in range(1, 8):
        total = total + inbox[n]
    plane_sum[...] = total
    for step in range(1, count):
        moved.append(copy(6 + step, plane_sum, plane_box.at[me], {"t": lax.rem(me + step, count)}))
        moved[-1].start()
    plane_box[me] = total
    for step in range(1, count):
        other = lax.rem(me + count - step, count)
        copy(6 + step, plane_sum, plane_box.at[other], {"t": other}).wait_recv()
    total = plane_box[0]
    for z in range(1, count):
        total = total + plane_box[z]
    for sent in moved:
        sent.wait_send()
    return total


def final_kernel(
    count, with_gates, left, right, own_in, gain, mlp_gains, pieces, grad_middle, reduced,
    grad_out, gains_out, gates_out, owned,
    gain_sum, values, inbox, plane_sum, plane_box, sum_send, sum_recv, rows_recv, gates_all, gates_send, gates_recv,
    own_send, own_recv, *buffers,
):
    tokens, width = own_in.shape
    place = Place()
    me = lax.axis_index("t")
    place.greet([place.peer(*offset) for offset in BEYOND] + [{"t": lax.rem(me + step, count)} for step in range(1, count)])
    scatter = Scatter(place, pair_product([left], [right], tokens), *buffers)
    owners = Owners(place, reduced, owned, own_send, own_recv)
    gates = GateSums(place, count, pieces, rows_recv, gates_all, gates_send, gates_recv)
    scatter.run_first()
    if with_gates:
        gates.begin()
    owners.begin()
    scatter.run_second()
    if with_gates:
        gates.pass_on()
    scatter.run_third(0)
    scatter.run_third(1)
    gain_sum[...] = jnp.zeros_like(gain_sum)

    def body(at):
        x = own_in[at, :].astype(F32)
        grad = scatter.rows(at)
        scale = rms(x)
        weighted = grad * gain[...]
        inner = jnp.mean(x * weighted, axis=-1, keepdims=True)
        grad_out[at, :] = grad_middle[at, :] + scale * weighted - x * (scale * scale * scale * inner)
        term = grad * x * scale
        gain_sum[...] += term[0:8] + term[8:16]

    for_slices(0, tokens, body)
    lines = width // LANES
    for base, row in ((0, jnp.sum(mlp_gains[...], axis=0, keepdims=True)), (lines, jnp.sum(gain_sum[...], axis=0, keepdims=True))):
        for n in range(lines):
            values[base + n : base + n + 1, :] = row[:, n * LANES : (n + 1) * LANES]
    gains_out[...] = sum_everywhere(place, count, values, inbox, plane_sum, plane_box, sum_send, sum_recv)
    if with_gates:
        gates.finish(gates_out)
    else:
        gates_out[...] = jnp.zeros_like(gates_out)
    owners.finish()
    scatter.finish()


def final_step(planes, left, right, own_in, gain, mlp_gains, pieces, grad_middle, reduced):
    tokens, width = own_in.shape
    with_gates = pieces.shape[0] == planes
    block = pieces.shape[1:] if with_gates else (16, LANES)
    slots = planes if with_gates else 1
    pieces = pieces if with_gates else jnp.zeros((1, *block), BF16)
    sums = (2 * width // LANES, LANES)
    return pl.pallas_call(
        functools.partial(final_kernel, planes, with_gates),
        name="final_step",
        out_shape=(
            jax.ShapeDtypeStruct((tokens, width), F32),
            jax.ShapeDtypeStruct(sums, F32),
            jax.ShapeDtypeStruct(block, F32),
            jax.ShapeDtypeStruct(reduced.shape, reduced.dtype),
        ),
        in_specs=[*whole(7), ANYWHERE],
        out_specs=(*whole(3), ANYWHERE),
        scratch_shapes=[
            pltpu.VMEM((8, width), F32),
            pltpu.VMEM(sums, F32),
            pltpu.VMEM((8, *sums), F32),
            pltpu.VMEM(sums, F32),
            pltpu.VMEM((planes, *sums), F32),
            pltpu.SemaphoreType.DMA((planes + 6,)),
            pltpu.SemaphoreType.DMA((planes + 6,)),
            pltpu.VMEM((slots, *block), BF16),
            pltpu.VMEM((slots, *block), BF16),
            pltpu.SemaphoreType.DMA((planes + 2,)),
            pltpu.SemaphoreType.DMA((planes + 2,)),
            *OWNERS_SCRATCH,
            *Scatter.scratch(tokens, width),
        ],
        compiler_params=mixer_params(7),
    )(left, right, own_in, gain[None], mlp_gains, pieces, grad_middle, reduced)


def owners_kernel(reduced0, reduced1, out0, out1, send0, recv0, send1, recv1):
    place = Place()
    place.greet([place.peer(*offset) for offset in BEYOND])
    owners = [Owners(place, reduced0, out0, send0, recv0), Owners(place, reduced1, out1, send1, recv1)]
    for part in owners:
        part.begin()
    for part in owners:
        part.finish()


def owners_step(number, reduced):
    return pl.pallas_call(
        owners_kernel,
        name="owners_step",
        out_shape=tuple(jax.ShapeDtypeStruct(part.shape, part.dtype) for part in reduced),
        in_specs=[ANYWHERE] * 2,
        out_specs=(ANYWHERE,) * 2,
        scratch_shapes=[*OWNERS_SCRATCH, *OWNERS_SCRATCH],
        compiler_params=mixer_params(number),
    )(*reduced)


def place_kernel(planes, hidden, kinds, *refs):
    given, out = refs[:-1], refs[-1]
    each = kinds // len(given)
    piece = given[0].shape[2] // (each * (planes if hidden else 1))
    for kind in range(kinds):
        sources, k = given[kind // each], kind % each
        if hidden:
            groups = [
                ((t * 2 + i) * 4 * piece, [(i * 4 + r, (k * planes + t) * piece) for r in range(4)])
                for t in range(planes)
                for i in range(2)
            ]
        else:
            groups = [(r * 2 * piece, [(i * 4 + r, k * piece) for i in range(2)]) for r in range(4)]
        for start, parts in groups:
            row = jnp.concatenate([sources[p, :, at : at + piece].astype(F32) for p, at in parts], axis=1)
            if kinds > 1:
                out[:, kind, start : start + row.shape[1]] = row
            else:
                out[:, start : start + row.shape[1]] = row


def place_columns(planes, hidden, kinds, *owned):
    members, own_rows, columns = owned[0].shape
    total = columns * len(owned) * members // kinds
    shape = (own_rows, kinds, total) if kinds > 1 else (own_rows, total)
    return pl.pallas_call(
        functools.partial(place_kernel, planes, hidden, kinds),
        name="place_columns",
        out_shape=jax.ShapeDtypeStruct(shape, F32),
        in_specs=whole(len(owned)),
        out_specs=pl.BlockSpec(memory_space=pltpu.VMEM),
        compiler_params=pltpu.CompilerParams(vmem_limit_bytes=60 * 1024 * 1024),
    )(*owned)


def first_gather(planes, normed, ids):
    tokens, width = normed.shape
    every = (8, *ids.shape)
    return pl.pallas_call(
        functools.partial(first_gather_kernel, planes),
        name="first_gather",
        out_shape=(jax.ShapeDtypeStruct((8 * tokens, width), BF16), *[jax.ShapeDtypeStruct(every, F32)] * 3),
        in_specs=[ANYWHERE, *whole(1)],
        out_specs=(ANYWHERE, *whole(3)),
        scratch_shapes=[pltpu.VMEM(every, F32)] * 3 + GATHER_SCRATCH + [pltpu.SemaphoreType.DMA((9,))] * 2,
        compiler_params=mixer_params(3),
    )(normed, ids)


def middle_step(mixed, w_out, own_in, gain):
    tokens, width = own_in.shape
    return pl.pallas_call(
        middle_kernel,
        name="middle_step",
        out_shape=(jax.ShapeDtypeStruct((tokens, width), F32), jax.ShapeDtypeStruct((8 * tokens, width), BF16)),
        in_specs=whole(4),
        out_specs=(pl.BlockSpec(memory_space=pltpu.VMEM), ANYWHERE),
        scratch_shapes=Scatter.scratch(tokens, width) + [pltpu.VMEM((tokens, width), BF16)] + GATHER_SCRATCH,
        compiler_params=mixer_params(4),
    )(mixed, w_out, own_in, gain[None])


def turn_step(left0, left1, right0, right1, middle, gain, cot, w_out, normed):
    tokens, width = cot.shape
    return pl.pallas_call(
        turn_kernel,
        name="turn_step",
        out_shape=(
            jax.ShapeDtypeStruct((tokens, width), F32),
            jax.ShapeDtypeStruct((8, width), F32),
            jax.ShapeDtypeStruct((width, left1.shape[1]), BF16),
            jax.ShapeDtypeStruct((8 * tokens, w_out.shape[0]), F32),
            jax.ShapeDtypeStruct((8 * tokens, width), BF16),
        ),
        in_specs=[*whole(8), ANYWHERE],
        out_specs=(*whole(4), ANYWHERE),
        scratch_shapes=Scatter.scratch(tokens, width)
        + [pltpu.VMEM((tokens, width), BF16)]
        + GATHER_SCRATCH
        + [pltpu.VMEM(normed.shape, BF16), pltpu.VMEM((tokens, width), BF16), pltpu.SemaphoreType.DMA((1,))],
        compiler_params=mixer_params(5),
    )(left0, left1, right0, right1, middle, gain[None], cot, w_out, normed)


class Swap:
    def __init__(self, quarters, out, send, recv):
        self.quarters, self.out, self.send, self.recv = quarters, out, send, recv
        self.groups = quarters.shape[0]
        self.me = lax.axis_index("g") * 2 + lax.axis_index("c")

    def copy(self, step, other, slot):
        return pltpu.make_async_remote_copy(
            src_ref=self.quarters.at[other],
            dst_ref=self.out.at[:, slot],
            send_sem=self.send.at[step],
            recv_sem=self.recv.at[step],
            device_id={"g": other // 2, "c": other % 2},
            device_id_type=MESH,
        )

    def peers(self):
        others = [lax.rem(self.me + step, self.groups) for step in range(1, self.groups)]
        return [{"g": other // 2, "c": other % 2} for other in others]

    def begin(self):
        self.keep = pltpu.make_async_copy(self.quarters.at[self.me], self.out.at[:, self.me], self.send.at[0])
        self.keep.start()
        self.moved = []
        for step in range(1, self.groups):
            self.moved.append(self.copy(step, lax.rem(self.me + step, self.groups), self.me))
            self.moved[-1].start()

    def finish(self):
        for step in range(1, self.groups):
            other = lax.rem(self.me + self.groups - step, self.groups)
            self.copy(step, other, other).wait_recv()
        for copy in self.moved:
            copy.wait_send()
        self.keep.wait()


def swap_scratch(groups):
    return [pltpu.SemaphoreType.DMA((groups,)), pltpu.SemaphoreType.DMA((groups,))]


def swap_kernel(quarters, out, send, recv):
    move = Swap(quarters, out, send, recv)
    barrier = pltpu.get_barrier_semaphore()
    for peer in move.peers():
        pl.semaphore_signal(barrier, inc=1, device_id=peer, device_id_type=MESH)
    pl.semaphore_wait(barrier, move.groups - 1)
    move.begin()
    move.finish()


def swap(quarters):
    groups, kinds, part, width = quarters.shape
    return pl.pallas_call(
        swap_kernel,
        name="swap",
        out_shape=jax.ShapeDtypeStruct((kinds, groups, part, width), quarters.dtype),
        in_specs=[ANYWHERE],
        out_specs=ANYWHERE,
        scratch_shapes=swap_scratch(groups),
        compiler_params=mixer_params(6),
    )(quarters)


def rms(values):
    return lax.rsqrt(jnp.mean(values * values, axis=-1, keepdims=True) + EPS)


def nt(left, right, out):
    return lax.dot_general(left, right, (((1,), (1,)), ((), ())), preferred_element_type=F32).astype(out)


def tn(left, right, out):
    return lax.dot_general(left, right, (((0,), (0,)), ((), ())), preferred_element_type=F32).astype(out)


def nn(left, right, out):
    return jnp.dot(left, right, preferred_element_type=F32).astype(out)


def per_device(
    inputs, segment_ids, mix_gain, in_weight, conv_weight, conv_bias, gate_weight, gate_bias, decay_param, out_weight,
    mlp_gain, mlp_in, down_weight, cotangent,
):
    planes = lax.axis_size("t")
    rows_here, seg, width = inputs.shape
    row_groups = lax.axis_size("g") * lax.axis_size("c")
    own_tokens = rows_here * seg
    recur_width = conv_weight.shape[1]
    block_width = gate_weight.shape[0]
    members = 2 * row_groups
    channels = recur_width // members
    t, i = lax.axis_index("t"), lax.axis_index("i")
    r = lax.axis_index("g") * lax.axis_size("c") + lax.axis_index("c")
    member = 2 * r + i
    first = member * channels
    own_rows = width // (planes * members)

    own_in = inputs.reshape(own_tokens, width)
    flat_in = own_in.astype(F32)
    scale_in = rms(flat_in)
    cot_own = cotangent.reshape(own_tokens, width)
    own_ids = jnp.pad((segment_ids + 1).astype(F32), ((0, 8 - rows_here), (0, 0)))

    normed, *ids = first_gather(planes, (flat_in * scale_in * mix_gain).astype(BF16), own_ids)
    late_r, ids[0] = lax.optimization_barrier((r, ids[0]))

    direct = planes == row_groups
    in_own = in_weight.transpose(1, 2, 0)
    out_own = out_weight.T[None]
    part = channels // row_groups if direct else 0

    def quarter(weight, part, rank=r):
        return lax.dynamic_slice_in_dim(weight, rank * part, part, weight.ndim - 1)

    def spread_units(weight):
        return lax.all_gather(weight, "t", axis=0, tiled=False)

    def whole_units(weight):
        every = lax.all_gather(weight, ("t", "i"), axis=1, tiled=True)
        return lax.dynamic_slice_in_dim(every, first, channels, 1)

    if direct:
        in_w = swap(spread_units(quarter(in_weight, part).transpose(1, 2, 0)))
        out_quarters = spread_units(quarter(out_weight, part).T[None])
    else:
        in_w = whole_units(in_own)
        out_quarters = jnp.zeros((row_groups, 1, 16, width), BF16)
    in_w = in_w.reshape(2 * channels, width)
    hidden_part = mlp_in.shape[2] // row_groups
    gated = quarter(mlp_in, hidden_part, late_r).transpose(1, 2, 0)
    w_left, w_right, w_down = [
        spread_units(part).reshape(-1, width)
        for part in (gated[0], gated[1], quarter(down_weight, hidden_part, late_r).T)
    ]

    def own(values):
        return lax.dynamic_slice_in_dim(values, first, channels, values.ndim - 1)

    vec = own(
        jnp.concatenate(
            [
                conv_weight,
                conv_bias[None],
                gate_bias,
                8.0 * jax.nn.softplus(-decay_param)[None],
                8.0 * jax.nn.sigmoid(-decay_param)[None],
                jnp.zeros((7, recur_width), F32),
            ]
        )
    )
    gate_blocks = own(gate_weight).transpose(1, 0, 2)
    blocks = channels // block_width

    branches = nt(normed, in_w, F32)
    conv_low, decay, states, mixed, halo, cin, mask, cot, w_out = mixer_forward(
        planes, seg, rows_here, branches, ids, gate_blocks, vec, cot_own, out_quarters
    )
    w_out = (w_out if direct else whole_units(out_own)).reshape(channels, width)
    middle, normed_two = middle_step(mixed, w_out, own_in, mlp_gain)
    left = nt(normed_two, w_left, F32)
    right = nt(normed_two, w_right, F32)
    act, slope = gelu_parts(left)
    hidden = (act * right).astype(BF16)

    def over_planes(grad):
        return lax.psum_scatter(grad, "t", scatter_dimension=0, tiled=True)

    grad_down = tn(cot, hidden, BF16)
    grad_down, hidden, w_down = lax.optimization_barrier((grad_down, hidden, w_down))
    grad_down = over_planes(grad_down)
    grad_hidden = nt(cot, w_down, F32)
    grad_left = (grad_hidden * right * slope).astype(BF16)
    grad_right = (grad_hidden * act).astype(BF16)
    grad_left_w = tn(normed_two, grad_left, BF16)
    grad_left_w, grad_left, grad_right = lax.optimization_barrier((grad_left_w, grad_left, grad_right))
    grad_left_w = over_planes(grad_left_w)
    grad_middle, grad_mlp_gain, grad_right_w, grad_mixed, grad_mid = turn_step(
        grad_left, grad_right, w_left, w_right, middle, mlp_gain, cot_own, w_out, normed_two
    )
    grad_right_w = over_planes(grad_right_w)
    grad_out = tn(grad_mid, mixed, BF16)

    def by_owner(grad):
        return grad.reshape(members, own_rows, -1)

    grad_branches, gw0, gw1, small, outputs, owned_down, owned_left = mixer_backward(
        planes, seg, grad_mixed, branches, states, decay, conv_low, mask, halo, cin, gate_blocks, vec, hidden, w_down, middle,
        [by_owner(grad_down), by_owner(grad_left_w)],
    )
    grad_in = jnp.concatenate([tn(normed, grad_branches, BF16), grad_out], axis=1)
    grad_right_w, grad_in, grad_branches = lax.optimization_barrier((grad_right_w, grad_in, grad_branches))
    grad_in = over_planes(grad_in)
    outputs = outputs.reshape(inputs.shape)

    column_block = lax.broadcasted_iota(jnp.int32, (block_width, channels), 1) // block_width

    def diagonal(gw):
        return sum(
            jnp.where(column_block == n, gw[n * block_width : (n + 1) * block_width], 0.0) for n in range(blocks)
        )

    gate_grads = jnp.concatenate([diagonal(gw0), diagonal(gw1), small], axis=0)
    pieces = jnp.zeros((0, 8, LANES), F32)
    if direct:
        pieces = gate_grads.reshape(gate_grads.shape[0], row_groups, -1).transpose(1, 0, 2)
        pieces = jnp.pad(pieces.astype(BF16), ((0, 0), (0, -pieces.shape[1] % 16), (0, LANES - part)))
    grad_inputs, gains, gate_sums, owned_right = final_step(
        planes, grad_branches, in_w, own_in, mix_gain, grad_mlp_gain, pieces, grad_middle, by_owner(grad_right_w)
    )
    grad_inputs = grad_inputs.reshape(inputs.shape)
    index = ((t * 2 + i) * row_groups + r) * own_rows
    gains = lax.dynamic_slice_in_dim(gains.reshape(2, width), index, own_rows, 1)


    split = 2 * channels
    owned_in, owned_out = owners_step(8, [by_owner(grad_in[:, :split]), by_owner(grad_in[:, split:])])

    def columns(kinds, hidden, *owned):
        if direct:
            return place_columns(planes, hidden, kinds, *owned)
        owned = jnp.concatenate(owned, axis=2).reshape(2, row_groups, own_rows, kinds, planes if hidden else 1, -1).astype(F32)
        order = (2, 3, 4, 0, 1, 5) if hidden else (2, 3, 1, 0, 4, 5)
        owned = owned.transpose(order).reshape(own_rows, kinds, -1)
        return owned if kinds > 1 else owned[:, 0]

    if direct:
        gate_grads = gate_sums[:, :part]
    else:
        placed = jnp.zeros((gate_grads.shape[0], recur_width), F32)
        placed = lax.dynamic_update_slice_in_dim(placed, gate_grads, first, 1)
        gate_grads = lax.psum_scatter(placed, EVERY, scatter_dimension=1, tiled=True)
    grad_gate_weight = jnp.stack([gate_grads[:block_width], gate_grads[block_width : 2 * block_width]], axis=1)
    small = gate_grads[2 * block_width : 2 * block_width + 8]
    return (
        outputs,
        grad_inputs,
        gains[1],
        columns(2, False, owned_in),
        small[0:4],
        small[4],
        grad_gate_weight,
        small[5:7],
        small[7],
        columns(1, False, owned_out),
        gains[0],
        columns(2, True, owned_left, owned_right),
        columns(1, True, owned_down),
    )


def solution(mesh):
    seq, rows = mesh.shape["seq"], mesh.shape["rows"]
    grid = Mesh(mesh.devices.reshape(seq // 2, 2, rows // 2, 2), EVERY)
    row_axes, seq_axes = ("g", "c"), ("t", "i")
    tokens = P(row_axes, seq_axes, None)
    return jax.shard_map(
        per_device,
        mesh=grid,
        in_specs=(
            tokens,
            P(row_axes, seq_axes),
            P(),
            P(None, None, seq_axes),
            P(),
            P(),
            P(),
            P(),
            P(),
            P(None, seq_axes),
            P(),
            P(None, None, seq_axes),
            P(None, seq_axes),
            tokens,
        ),
        out_specs=(
            tokens,
            tokens,
            P(EVERY),
            P(EVERY, None, None),
            P(None, EVERY),
            P(EVERY),
            P(None, None, EVERY),
            P(None, EVERY),
            P(EVERY),
            P(EVERY, None),
            P(EVERY),
            P(EVERY, None, None),
            P(EVERY, None),
        ),
        check_vma=False,
    )
```

```python
import functools

import jax
import jax.numpy as jnp
from jax import lax
from jax.experimental import pallas as pl
from jax.experimental.pallas import tpu as pltpu
from jax.sharding import Mesh
from jax.sharding import PartitionSpec as P

EPS = 1e-06
MESH = pl.DeviceIdType.MESH
PLANE = ("i", "g", "c")
EVERY = ("t", "i", "g", "c")
F32 = jnp.float32
BF16 = jnp.bfloat16
GELU_A = 0.7978845608028654
GELU_B = 0.044715
HALO = 8
LANES = 128
SLICE = 16
ANYWHERE = pl.BlockSpec(memory_space=pl.ANY)
GATHER_SCRATCH = [pltpu.SemaphoreType.DMA((14,))] * 2


def gelu_parts(x):
    square = x * x
    th = jnp.tanh(GELU_A * x * (1.0 + GELU_B * square))
    half = 0.5 * (1.0 + th)
    slope = half + 0.5 * x * (1.0 - th * th) * (GELU_A * (1.0 + 3.0 * GELU_B * square))
    return x * half, slope


def one_minus_exp(y, power):
    series = 1.0 + y * (-1.0 / 2 + y * (1.0 / 6 + y * (-1.0 / 24 + y * (1.0 / 120 + y * (-1.0 / 720 + y * (1.0 / 5040))))))
    return jnp.where(y < 0.35, y * series, 1.0 - power)


def sigmoid(x):
    return 1.0 / (1.0 + jnp.exp(-x))


def gate_values(conv_low, wg0, wg1, vec):
    logits0 = jnp.dot(conv_low, wg0, preferred_element_type=F32) + vec[5:6]
    logits1 = jnp.dot(conv_low, wg1, preferred_element_type=F32) + vec[6:7]
    recur_gate = sigmoid(logits0)
    input_gate = sigmoid(logits1)
    log_decay = -vec[7:8] * recur_gate
    return recur_gate, input_gate, log_decay


def spread_blocks(gates, out):
    size, width = gates.shape[1], gates.shape[2]
    column = lax.broadcasted_iota(jnp.int32, (size, width), 1) // size
    for k in range(2):
        block = gates[k].astype(F32)
        for n in range(width // size):
            out[k, n * size : (n + 1) * size, :] = jnp.where(column == n, block, 0.0).astype(BF16)


def put_tiles(ref, at, values):
    tiles, lanes = ref.shape[0], ref.shape[2]
    short = tiles * lanes - values.shape[1]
    if short:
        values = jnp.concatenate([values, jnp.zeros((values.shape[0], short), values.dtype)], axis=1)
    for j in range(tiles):
        ref[j, at, :] = values[:, j * lanes : (j + 1) * lanes]


def get_tiles(ref, at, width):
    joined = jnp.concatenate([ref[j, at, :] for j in range(ref.shape[0])], axis=1)
    return joined[:, :width]


def join_tiles(parts, width):
    return jnp.concatenate(parts, axis=1)[:, :width]


def exchange_copy(step, send, target, other, send_sem, recv_sem):
    return pltpu.make_async_remote_copy(
        src_ref=send,
        dst_ref=target,
        send_sem=send_sem.at[step],
        recv_sem=recv_sem.at[step],
        device_id={"t": other},
        device_id_type=MESH,
    )


def exchange_start(count, me, send, slots, send_sem, recv_sem):
    for step in range(1, count):
        exchange_copy(step, send, slots.at[me], lax.rem(me + step, count), send_sem, recv_sem).start()


def exchange_wait(count, me, send, slots, send_sem, recv_sem):
    for step in range(1, count):
        other = lax.rem(me + count - step, count)
        exchange_copy(step, send, slots.at[other], other, send_sem, recv_sem).wait()


def mixer_forward_kernel(
    count, seg, rows_here, branches_far, ids, ids_before, ids_after, gate_blocks, vec_ref, cot, quarters,
    conv_out, decay_out, states_out, mixed_out, halo_out, cin_out, mask, cot_out, swapped,
    drive, h_ref, a_ref, ext, halo_send, halo_recv, summary, slots, send_sem, recv_sem, halo_sems,
    gather_send, gather_recv, swap_send, swap_recv, branches, wg, load,
):
    place = Place()
    me = lax.axis_index("t")
    loaded = pltpu.make_async_copy(branches_far, branches, load.at[0])
    loaded.start()
    place.greet([place.peer(0, 1, 1)] + [{"t": lax.rem(me + step, count)} for step in range(1, count)])
    gather = Gather(place, cot, cot_out, gather_send, gather_recv)
    move = Swap(quarters, swapped, swap_send, swap_recv)
    gather.begin_whole()
    move.begin()
    spread_blocks(gate_blocks, wg)
    rows = 8
    width = branches.shape[1] // 2
    loaded.wait()

    def recur_at(at):
        return branches[at, width:].astype(BF16).astype(F32)

    for r in range(rows):
        halo_send[r * HALO : (r + 1) * HALO, :] = recur_at(pl.ds((rows + r + 1) * seg - HALO, HALO))
    halo_copy = pltpu.make_async_remote_copy(
        src_ref=halo_send,
        dst_ref=halo_recv,
        send_sem=halo_sems.at[0],
        recv_sem=halo_sems.at[1],
        device_id={"t": lax.rem(me + 1, count)},
        device_id_type=MESH,
    )
    halo_copy.start()
    for r in range(rows):
        halo_out[(rows + r) * HALO : (rows + r + 1) * HALO, :] = recur_at(pl.ds((r + 1) * seg - HALO, HALO))
    vec = vec_ref[...]

    def ids_of(ref, s):
        chunk = s // rows_here
        return ref[chunk, s % rows_here : s % rows_here + 1, :]

    nothing = jnp.zeros((1, LANES), F32)
    for s in range(2 * rows):
        here = ids_of(ids, s)
        back = ids_of(ids, s - rows) if s >= rows else jnp.where(me > 0, ids_of(ids_before, s + rows), nothing)
        ahead = ids_of(ids, s + rows) if s < rows else jnp.where(me < count - 1, ids_of(ids_after, s - rows), nothing)
        lines = [jnp.concatenate([back[:, seg - k :], here[:, : seg - k]], axis=1) for k in (1, 2, 3)]
        lines += [jnp.concatenate([here[:, k:], ahead[:, :k]], axis=1) for k in (1, 2, 3)]
        lines = [jnp.where(line == here, 1.0, 0.0) for line in lines] + [nothing] * 2
        mask[s * seg : (s + 1) * seg, :] = jnp.concatenate(lines, axis=0).T

    def local(s, none):
        at = pl.ds(pl.multiple_of(s * seg, seg), seg)
        x = recur_at(at)
        ext[0:HALO, :] = halo_out[pl.ds(pl.multiple_of(s * HALO, HALO), HALO), :]
        ext[HALO : HALO + seg, :] = x
        m = mask[at, :]
        conv = vec[4:5] + vec[0:1] * x
        for k in range(1, 4):
            conv = conv + vec[k : k + 1] * ext[HALO - k : HALO - k + seg, :] * m[:, k - 1 : k]
        conv_low = conv.astype(BF16)
        conv_out[at, :] = conv_low
        recur_gate, input_gate, log_decay = gate_values(conv_low, wg[0], wg[1], vec)
        keep = m[:, 0:1]
        kept = jnp.exp(log_decay)
        put_tiles(decay_out, at, kept * keep)
        scale = (1.0 - keep) + keep * jnp.sqrt(one_minus_exp(-2.0 * log_decay, kept * kept))
        put_tiles(drive, at, scale * input_gate * conv_low.astype(F32))
        return none

    lax.fori_loop(rows, 2 * rows, local, 0)
    halo_copy.wait()
    for r in range(rows):
        halo_out[r * HALO : (r + 1) * HALO, :] = halo_recv[r * HALO : (r + 1) * HALO, :]
    gather.pass_first()
    lax.fori_loop(0, rows, local, 0)
    tiles, lanes = drive.shape[0], drive.shape[2]

    def scan(k, carried):
        at = pl.ds(k, 2 * rows, stride=seg)
        after = []
        for j in range(tiles):
            h, a = carried[j]
            d = decay_out[j, at, :]
            h = d * h + drive[j, at, :]
            a = a * d
            h_ref[j, at, :] = h
            a_ref[j, at, :] = a
            after.append((h, a))
        return tuple(after)

    start = (jnp.zeros((2 * rows, lanes), F32), jnp.ones((2 * rows, lanes), F32))
    last = lax.fori_loop(0, seg, scan, (start,) * tiles, unroll=4)
    last_h = join_tiles([part[0] for part in last], width)
    last_a = join_tiles([part[1] for part in last], width)
    summary[0:rows, :] = last_a[rows:] * last_a[:rows]
    summary[rows : 2 * rows, :] = last_a[rows:] * last_h[:rows] + last_h[rows:]
    exchange_start(count, me, summary, slots, send_sem, recv_sem)
    gather.pass_second()

    def activate(s, none):
        at = pl.ds(pl.multiple_of(s * seg, seg), seg)
        act, _ = gelu_parts(branches[at, :width])
        states_out[at, :] = act
        return none

    lax.fori_loop(0, 2 * rows, activate, 0)
    exchange_wait(count, me, summary, slots, send_sem, recv_sem)
    carry = jnp.zeros((rows, width), F32)
    for z in range(count - 1):
        carry = jnp.where(z < me, slots[z, 0:rows, :] * carry + slots[z, rows : 2 * rows, :], carry)
    cin_out[0:rows, :] = carry
    cin_out[rows : 2 * rows, :] = last_a[:rows] * carry + last_h[:rows]

    def finish(s, none):
        at = pl.ds(pl.multiple_of(s * seg, seg), seg)
        states = get_tiles(h_ref, at, width) + get_tiles(a_ref, at, width) * cin_out[pl.ds(s, 1), :]
        act = states_out[at, :]
        states_out[at, :] = states
        mixed_out[at, :] = (act * states.astype(BF16).astype(F32)).astype(BF16)
        return none

    lax.fori_loop(0, 2 * rows, finish, 0)
    gather.pass_third()
    gather.finish()
    move.finish()


def mixer_backward_kernel(
    count, seg, grad_mixed_far, branches_far, states_far, decay_far, conv_far, mask_far, halo, cin, gate_blocks, vec_ref,
    hidden, w_down, middle_far, reduced, grad_out, gw0_out, gw1_out, small_out, pieces_out, outputs, owned,
    tot, prod, ext, halo_send, halo_recv, summary, slots, uin, send_sem, recv_sem, halo_sems,
    grad_mixed, branches, states, decay, conv_low_ref, mask, middle, wg, load, own_send, own_recv, *buffers,
):
    place = Place()
    pairs = (
        (grad_mixed_far, grad_mixed),
        (branches_far, branches),
        (states_far, states),
        (decay_far, decay),
        (conv_far, conv_low_ref),
        (mask_far, mask),
        (middle_far, middle),
    )
    loads = [pltpu.make_async_copy(far, near, load.at[n]) for n, (far, near) in enumerate(pairs)]
    for part in loads:
        part.start()
    me = lax.axis_index("t")
    place.greet([place.peer(*offset) for offset in BEYOND] + [{"t": lax.rem(me + step, count)} for step in range(1, count)])
    scatter = Scatter(place, pair_product([hidden], [w_down], outputs.shape[0]), *buffers)
    owners = Owners(place, reduced, owned, own_send, own_recv)
    spread_blocks(gate_blocks, wg)
    scatter.run_first()
    owners.begin()
    for part in loads:
        part.wait()
    rows = 8
    width = branches.shape[1] // 2
    vec = vec_ref[...]

    def local(s, none):
        at = pl.ds(pl.multiple_of(s * seg, seg), seg)
        act, slope = gelu_parts(branches[at, :width])
        gm = grad_mixed[at, :].astype(F32)
        grad_out[at, :width] = (gm * states[at, :].astype(BF16).astype(F32) * slope).astype(BF16)
        put_tiles(tot, at, (gm * act).astype(BF16).astype(F32))
        return none

    lax.fori_loop(0, 2 * rows, local, 0)

    tiles, lanes = tot.shape[0], tot.shape[2]

    def scan(k, carried):
        at = pl.ds(seg - 1 - k, 2 * rows, stride=seg)
        after = []
        for j in range(tiles):
            u, p = carried[j]
            d = decay[j, at, :]
            total = tot[j, at, :] + u
            tot[j, at, :] = total
            prod[j, at, :] = p
            after.append((d * total, d * p))
        return tuple(after)

    start = (jnp.zeros((2 * rows, lanes), F32), jnp.ones((2 * rows, lanes), F32))
    last = lax.fori_loop(0, seg, scan, (start,) * tiles, unroll=4)
    u = join_tiles([part[0] for part in last], width)
    p = join_tiles([part[1] for part in last], width)
    summary[0:rows, :] = p[:rows] * p[rows:]
    summary[rows : 2 * rows, :] = p[:rows] * u[rows:] + u[:rows]
    exchange_start(count, me, summary, slots, send_sem, recv_sem)
    scatter.run_second()
    exchange_wait(count, me, summary, slots, send_sem, recv_sem)
    carry = jnp.zeros((rows, width), F32)
    for z in range(count - 1, 0, -1):
        carry = jnp.where(z > me, slots[z, 0:rows, :] * carry + slots[z, rows : 2 * rows, :], carry)
    uin[rows : 2 * rows, :] = carry
    uin[0:rows, :] = p[rows:] * carry + u[rows:]
    gw0_out[...] = jnp.zeros_like(gw0_out)
    gw1_out[...] = jnp.zeros_like(gw1_out)
    small_out[...] = jnp.zeros_like(small_out)

    def gates(s, none):
        at = pl.ds(pl.multiple_of(s * seg, seg), seg)
        total = get_tiles(tot, at, width) + get_tiles(prod, at, width) * uin[pl.ds(s, 1), :]
        ext[HALO - 1 : HALO, :] = cin[pl.ds(s, 1), :]
        ext[HALO : HALO + seg, :] = states[at, :]
        before = ext[HALO - 1 : HALO - 1 + seg, :]
        conv_low = conv_low_ref[at, :]
        conv_vals = conv_low.astype(F32)
        m = mask[at, :]
        keep = m[:, 0:1]
        recur_gate, input_gate, log_decay = gate_values(conv_low, wg[0], wg[1], vec)
        power = jnp.exp(2.0 * log_decay)
        gone = one_minus_exp(-2.0 * log_decay, power)
        inverse = lax.rsqrt(gone)
        root = gone * inverse
        scale = (1.0 - keep) + keep * root
        driven_in = total * conv_vals
        grad_log = total * before * get_tiles(decay, at, width) - driven_in * input_gate * keep * (power * inverse)
        grad0 = grad_log * log_decay * (1.0 - recur_gate)
        grad1 = driven_in * scale * input_gate * (1.0 - input_gate)
        low0 = grad0.astype(BF16)
        low1 = grad1.astype(BF16)
        inputs_of = (((1,), (1,)), ((), ()))
        grad_conv = (
            total * scale * input_gate
            + lax.dot_general(low0, wg[0], inputs_of, preferred_element_type=F32)
            + lax.dot_general(low1, wg[1], inputs_of, preferred_element_type=F32)
        )
        put_tiles(tot, at, grad_conv)
        turned = (((0,), (0,)), ((), ()))
        gw0_out[...] += lax.dot_general(conv_low, low0, turned, preferred_element_type=F32)
        gw1_out[...] += lax.dot_general(conv_low, low1, turned, preferred_element_type=F32)
        x = branches[at, width:].astype(BF16).astype(F32)
        ext[0:HALO, :] = halo[pl.ds(pl.multiple_of(s * HALO, HALO), HALO), :]
        ext[HALO : HALO + seg, :] = x

        def add(row, values):
            small_out[row : row + 1, :] += jnp.sum(values, axis=0, keepdims=True)

        add(0, grad_conv * x)
        for k in range(1, 4):
            add(k, grad_conv * ext[HALO - k : HALO - k + seg, :] * m[:, k - 1 : k])
        add(4, grad_conv)
        add(5, grad0)
        add(6, grad1)
        add(7, grad_log * recur_gate)
        return none

    lax.fori_loop(0, 2 * rows, gates, 0)
    small_out[7:8, :] = small_out[7:8, :] * vec[8:9]
    size, part = gate_blocks.shape[1], width // 4

    def padded(values):
        short = [values, jnp.zeros((values.shape[0], LANES - part), F32)]
        return jnp.concatenate(short, axis=1)

    for r in range(4):
        first = r * part // size * size
        at = slice(r * part, (r + 1) * part)
        for k, square in enumerate((gw0_out, gw1_out)):
            pieces_out[r, k * size : (k + 1) * size, :] = padded(square[first : first + size, at]).astype(BF16)
        rest = jnp.concatenate([padded(small_out[:, at]), jnp.zeros((8, LANES), F32)], axis=0)
        pieces_out[r, 2 * size :, :] = rest.astype(BF16)
    for r in range(rows):
        halo_send[r * HALO : (r + 1) * HALO, :] = get_tiles(tot, pl.ds(r * seg, HALO), width)
    halo_copy = pltpu.make_async_remote_copy(
        src_ref=halo_send,
        dst_ref=halo_recv,
        send_sem=halo_sems.at[0],
        recv_sem=halo_sems.at[1],
        device_id={"t": lax.rem(me + count - 1, count)},
        device_id_type=MESH,
    )
    halo_copy.start()

    def back(s, none):
        at = pl.ds(pl.multiple_of(s * seg, seg), seg)
        m = mask[at, :]
        grad_conv = get_tiles(tot, at, width)
        ext[0:seg, :] = grad_conv
        result = vec[0:1] * grad_conv

        @pl.when(s < rows)
        def _():
            ext[seg : seg + HALO, :] = get_tiles(tot, pl.ds(pl.multiple_of((s + rows) * seg, seg), HALO), width)

        @pl.when(s >= rows)
        def _():
            ext[seg : seg + HALO, :] = halo_recv[pl.ds(pl.multiple_of((s - rows) * HALO, HALO), HALO), :]

        for k in range(1, 4):
            result = result + vec[k : k + 1] * ext[k : k + seg, :] * m[:, 2 + k : 3 + k]
        grad_out[at, width:] = result.astype(BF16)
        return none

    lax.fori_loop(0, rows, back, 0)
    halo_copy.wait()
    lax.fori_loop(rows, 2 * rows, back, 0)
    scatter.run_third(0)
    scatter.run_third(1)

    def body(at):
        outputs[at, :] = (middle[at, :] + scatter.rows(at)).astype(BF16)

    for_slices(0, outputs.shape[0], body)
    scatter.finish()
    owners.finish()


def whole(count):
    return [pl.BlockSpec(memory_space=pltpu.VMEM)] * count


def mixer_params(number):
    return pltpu.CompilerParams(collective_id=number, has_side_effects=True, vmem_limit_bytes=60 * 1024 * 1024)


def mixer_forward(count, seg, rows_here, branches, ids, gate_blocks, vec, cot, quarters):
    n, width = branches.shape[0], branches.shape[1] // 2
    full = functools.partial(jax.ShapeDtypeStruct, (n, width))
    tiles = -(-width // LANES)
    tiled = jax.ShapeDtypeStruct((tiles, n, LANES), F32)
    groups, kinds, part, depth = quarters.shape
    return pl.pallas_call(
        functools.partial(mixer_forward_kernel, count, seg, rows_here),
        name="mixer_forward",
        out_shape=(
            full(BF16), tiled, full(F32), full(BF16),
            jax.ShapeDtypeStruct((16 * HALO, width), F32), jax.ShapeDtypeStruct((16, width), F32),
            jax.ShapeDtypeStruct((n, 8), F32),
            jax.ShapeDtypeStruct((8 * cot.shape[0], cot.shape[1]), BF16),
            jax.ShapeDtypeStruct((kinds, groups, part, depth), BF16),
        ),
        in_specs=[ANYWHERE, *whole(5), ANYWHERE, ANYWHERE],
        out_specs=(*whole(7), ANYWHERE, ANYWHERE),
        scratch_shapes=[
            pltpu.VMEM((tiles, n, LANES), F32),
            pltpu.VMEM((tiles, n, LANES), F32),
            pltpu.VMEM((tiles, n, LANES), F32),
            pltpu.VMEM((seg + HALO, width), F32),
            pltpu.VMEM((8 * HALO, width), F32),
            pltpu.VMEM((8 * HALO, width), F32),
            pltpu.VMEM((16, width), F32),
            pltpu.VMEM((count, 16, width), F32),
            pltpu.SemaphoreType.DMA((count,)),
            pltpu.SemaphoreType.DMA((count,)),
            pltpu.SemaphoreType.DMA((2,)),
            *GATHER_SCRATCH,
            *swap_scratch(groups),
            pltpu.VMEM(branches.shape, F32),
            pltpu.VMEM((2, width, width), BF16),
            pltpu.SemaphoreType.DMA((1,)),
        ],
        compiler_params=mixer_params(1),
    )(branches, *ids, gate_blocks, vec, cot, quarters)


def mixer_backward(count, seg, grad_mixed, branches, states, decay, conv_low, mask, halo, cin, gate_blocks, vec, hidden, w_down, middle, reduced):
    n, width = branches.shape[0], branches.shape[1] // 2
    tokens, depth = n // 8, w_down.shape[1]
    full = functools.partial(jax.ShapeDtypeStruct, (n, width))
    tiles = -(-width // LANES)
    tiled = jax.ShapeDtypeStruct((tiles, n, LANES), F32)
    return pl.pallas_call(
        functools.partial(mixer_backward_kernel, count, seg),
        name="mixer_backward",
        out_shape=(
            jax.ShapeDtypeStruct((n, 2 * width), BF16),
            jax.ShapeDtypeStruct((width, width), F32), jax.ShapeDtypeStruct((width, width), F32),
            jax.ShapeDtypeStruct((8, width), F32),
            jax.ShapeDtypeStruct((4, 2 * gate_blocks.shape[1] + 16, LANES), BF16),
            jax.ShapeDtypeStruct((tokens, depth), BF16),
            jax.ShapeDtypeStruct(reduced.shape, BF16),
        ),
        in_specs=[*[ANYWHERE] * 6, *whole(6), *[ANYWHERE] * 2],
        out_specs=(*whole(6), ANYWHERE),
        scratch_shapes=[
            pltpu.VMEM((tiles, n, LANES), F32),
            pltpu.VMEM((tiles, n, LANES), F32),
            pltpu.VMEM((seg + HALO, width), F32),
            pltpu.VMEM((8 * HALO, width), F32),
            pltpu.VMEM((8 * HALO, width), F32),
            pltpu.VMEM((16, width), F32),
            pltpu.VMEM((count, 16, width), F32),
            pltpu.VMEM((16, width), F32),
            pltpu.SemaphoreType.DMA((count,)),
            pltpu.SemaphoreType.DMA((count,)),
            pltpu.SemaphoreType.DMA((2,)),
            *[pltpu.VMEM(part.shape, part.dtype) for part in (grad_mixed, branches, states, decay, conv_low, mask, middle)],
            pltpu.VMEM((2, width, width), BF16),
            pltpu.SemaphoreType.DMA((7,)),
            *[pltpu.SemaphoreType.DMA((8,))] * 2,
            *Scatter.scratch(tokens, depth),
        ],
        compiler_params=mixer_params(2),
    )(grad_mixed, branches, states, decay, conv_low, mask, halo, cin, gate_blocks, vec, hidden, w_down, middle, reduced)


class Place:
    def __init__(self):
        self.i, self.g, self.c = lax.axis_index("i"), lax.axis_index("g"), lax.axis_index("c")
        self.core, self.across, self.along = {"c": 1 - self.c}, {"g": 1 - self.g}, {"i": 1 - self.i}

    def chunk(self, di, dg, dc):
        i = 1 - self.i if di else self.i
        g = 1 - self.g if dg else self.g
        c = 1 - self.c if dc else self.c
        return (i * 2 + g) * 2 + c

    def peer(self, di, dg, dc):
        return {
            "i": 1 - self.i if di else self.i,
            "g": 1 - self.g if dg else self.g,
            "c": 1 - self.c if dc else self.c,
        }

    def greet(self, more=()):
        barrier = pltpu.get_barrier_semaphore()
        peers = [self.core, self.across, self.along, *more]
        for peer in peers:
            pl.semaphore_signal(barrier, inc=1, device_id=peer, device_id_type=MESH)
        pl.semaphore_wait(barrier, len(peers))


class Gather:
    COPIES = 12

    def __init__(self, place, block, out, send, recv):
        self.place, self.block, self.out, self.send, self.recv = place, block, out, send, recv
        self.tokens = block.shape[0]
        self.half = self.tokens // 2

    def rows(self, chunk, part):
        start = chunk * self.tokens + (self.half if part == 1 else 0)
        return self.out.at[pl.ds(pl.multiple_of(start, self.half), self.tokens if part == 2 else self.half)]

    def mine(self, part):
        if part == 2:
            return self.block
        return self.block.at[pl.ds(part * self.half, self.half)]

    def copy(self, number, source, chunk, part, peer):
        return pltpu.make_async_remote_copy(
            src_ref=source,
            dst_ref=self.rows(chunk, part),
            send_sem=self.send.at[number],
            recv_sem=self.recv.at[number],
            device_id=peer,
            device_id_type=MESH,
        )

    def begin(self, part, whole=False):
        place = self.place
        own = place.chunk(0, 0, 0)
        other = 1 - part if whole else part
        self.give(0 + part, own, part, place.across)
        self.give(2 + other, own, other, place.along)
        self.give(4 + part, own, part, place.core)
        keep = pltpu.make_async_copy(self.mine(part), self.rows(own, part), self.send.at[self.COPIES + part])
        keep.start()
        self.local = getattr(self, "local", []) + [keep]

    def begin_whole(self):
        self.begin(0, True)
        self.begin(1, True)

    def give(self, number, chunk, part, peer):
        moved = self.copy(number, self.mine(part), chunk, part, peer)
        moved.start()
        self.kept = getattr(self, "kept", []) + [moved]

    def arrived(self, number, chunk, part):
        self.copy(number, self.rows(chunk, part), chunk, part, self.place.core).wait_recv()

    def forward(self, number, chunk, part, peer):
        moved = self.copy(number, self.rows(chunk, part), chunk, part, peer)
        moved.start()
        self.kept.append(moved)

    def pass_first(self):
        place = self.place
        ax, al = place.chunk(0, 1, 0), place.chunk(1, 0, 0)
        self.arrived(0, ax, 0)
        self.forward(6, ax, 0, place.along)
        self.arrived(3, al, 1)
        self.forward(7, al, 1, place.across)

    def pass_second(self):
        place = self.place
        ax, al = place.chunk(0, 1, 0), place.chunk(1, 0, 0)
        self.arrived(1, ax, 1)
        self.forward(8, ax, 2, place.core)
        self.arrived(2, al, 0)
        self.forward(9, al, 2, place.core)

    def pass_third(self):
        dia = self.place.chunk(1, 1, 0)
        self.arrived(6, dia, 0)
        self.forward(10, dia, 0, self.place.core)
        self.arrived(7, dia, 1)
        self.forward(11, dia, 1, self.place.core)

    def pass_on(self):
        self.pass_first()
        self.pass_second()
        self.pass_third()

    def finish_core(self):
        for part in (0, 1):
            self.arrived(4 + part, self.place.chunk(0, 0, 1), part)

    def finish_near(self):
        self.arrived(8, self.place.chunk(0, 1, 1), 2)
        self.arrived(9, self.place.chunk(1, 0, 1), 2)

    def finish_far(self):
        for part in (0, 1):
            self.arrived(10 + part, self.place.chunk(1, 1, 1), part)

    def finish(self):
        self.finish_core()
        self.finish_near()
        self.finish_far()
        self.finish_sends()

    def finish_sends(self):
        for moved in self.kept:
            moved.wait_send()
        for keep in self.local:
            keep.wait()


OTHERS = [(di, dg, dc) for di in (0, 1) for dg in (0, 1) for dc in (0, 1) if di or dg or dc]


def first_gather_kernel(count, normed, ids, normed_out, ids_out, before_out, after_out, plane_ids, before, after, send, recv, ids_send, ids_recv):
    place = Place()
    me = lax.axis_index("t")
    up, down = {"t": lax.rem(me + 1, count)}, {"t": lax.rem(me + count - 1, count)}
    place.greet([place.peer(*offset) for offset in OTHERS if sum(offset) > 1] + [up, down])
    gather = Gather(place, normed, normed_out, send, recv)
    own = place.chunk(0, 0, 0)
    moved = []

    def move(number, source, target, peer):
        copy = pltpu.make_async_remote_copy(
            src_ref=source,
            dst_ref=target,
            send_sem=ids_send.at[number],
            recv_sem=ids_recv.at[number],
            device_id=peer,
            device_id_type=MESH,
        )
        copy.start()
        moved.append(copy)

    for number, offset in enumerate(OTHERS):
        move(number, ids, plane_ids.at[own], place.peer(*offset))
    gather.begin_whole()
    plane_ids[own] = ids[...]
    for number, offset in enumerate(OTHERS):
        chunk = place.chunk(*offset)
        pltpu.make_async_remote_copy(
            src_ref=ids,
            dst_ref=plane_ids.at[chunk],
            send_sem=ids_send.at[number],
            recv_sem=ids_recv.at[number],
            device_id=place.peer(*offset),
            device_id_type=MESH,
        ).wait_recv()
    move(7, plane_ids, before, up)
    move(8, plane_ids, after, down)
    gather.pass_on()
    for copy in moved[7:]:
        copy.wait_recv()
    for copy in moved:
        copy.wait_send()
    ids_out[...] = plane_ids[...]
    before_out[...] = before[...]
    after_out[...] = after[...]
    gather.finish()


class Scatter:
    def __init__(self, place, product, core_send, core_recv, held, acc, across_recv, along_recv, second, second_recv, send, recv):
        self.place, self.product = place, product
        self.core_send, self.core_recv, self.held, self.acc = core_send, core_recv, held, acc
        self.across_recv, self.along_recv, self.second, self.second_recv = across_recv, along_recv, second, second_recv
        self.send, self.recv = send, recv
        self.kept = []

    def copy(self, number, source, target, peer):
        return pltpu.make_async_remote_copy(
            src_ref=source,
            dst_ref=target,
            send_sem=self.send.at[number],
            recv_sem=self.recv.at[number],
            device_id=peer,
            device_id_type=MESH,
        )

    def start(self, *parts):
        moved = self.copy(*parts)
        moved.start()
        self.kept.append(moved)

    def run_first(self):
        place = self.place
        order = ((1, 1), (0, 1), (1, 0), (0, 0))
        tile = 256
        per_half = self.held.shape[3] // tile
        def give(di, dg):
            q = 2 * di + dg
            chunk = place.chunk(di, dg, 1)

            def send_tile(n, none):
                at = pl.ds(pl.multiple_of(n % per_half * tile, tile), tile)
                self.core_send[q, n // per_half, :, at] = self.product(chunk, n).astype(BF16)
                return none

            lax.fori_loop(0, 2 * per_half, send_tile, 0)
            self.start(q, self.core_send.at[q], self.core_recv.at[q], place.core)

        def take(di, dg):
            q = 2 * di + dg
            chunk = place.chunk(di, dg, 0)
            self.copy(q, self.core_send.at[q], self.core_recv.at[q], place.core).wait_recv()

            def sum_tile(n, none):
                at = pl.ds(pl.multiple_of(n % per_half * tile, tile), tile)
                value = self.product(chunk, n) + self.core_recv[q, n // per_half, :, at].astype(F32)
                if q:
                    self.held[q - 1, n // per_half, :, at] = value.astype(BF16)
                else:
                    self.acc[n // per_half, :, at] = value
                return none

            lax.fori_loop(0, 2 * per_half, sum_tile, 0)
            if dg:
                self.start(4 + di, self.held.at[q - 1, 0], self.across_recv.at[di], place.across)
            if di:
                self.start(6 + dg, self.held.at[q - 1, 1], self.along_recv.at[dg], place.along)

        give(*order[0])
        give(*order[1])
        take(*order[0])
        give(*order[2])
        take(*order[1])
        give(*order[3])
        take(*order[2])
        take(*order[3])

    def second_copy(self, half, part):
        tokens = self.second.shape[1] // 2
        at = pl.ds(part * tokens, tokens)
        peer = self.place.across if half else self.place.along
        return 8 + 2 * part + half, self.second.at[half, at], self.second_recv.at[half, at], peer

    def run_second(self):
        place = self.place
        tokens = self.second.shape[1] // 2
        for part in (0, 1):
            for half, number, buffer, mine in ((0, 5, self.across_recv, 2), (1, 7, self.along_recv, 1)):
                if part == 0:
                    self.copy(number, buffer.at[1], buffer.at[1], place.core).wait_recv()

                def add_rows(at):
                    total = self.held[mine - 1, half, at, :].astype(F32) + buffer[1, at, :].astype(F32)
                    self.second[half, at, :] = total.astype(BF16)

                for_slices(part * tokens, (part + 1) * tokens, add_rows)
                self.start(*self.second_copy(half, part))

    def run_third(self, part):
        place = self.place
        if part == 0:
            for number, buffer in ((4, self.across_recv), (6, self.along_recv)):
                self.copy(number, buffer.at[0], buffer.at[0], place.core).wait_recv()
        for half in (0, 1):
            self.copy(*self.second_copy(half, part)).wait_recv()

    def rows(self, at):
        first = self.acc[0, at, :] + self.across_recv[0, at, :].astype(F32) + self.second_recv[0, at, :].astype(F32)
        last = self.acc[1, at, :] + self.along_recv[0, at, :].astype(F32) + self.second_recv[1, at, :].astype(F32)
        return jnp.concatenate([first, last], axis=1)

    def finish(self):
        for moved in self.kept:
            moved.wait_send()

    @staticmethod
    def scratch(tokens, width):
        half = width // 2
        return [
            pltpu.VMEM((4, 2, tokens, half), BF16),
            pltpu.VMEM((4, 2, tokens, half), BF16),
            pltpu.VMEM((3, 2, tokens, half), BF16),
            pltpu.VMEM((2, tokens, half), F32),
            pltpu.VMEM((2, tokens, half), BF16),
            pltpu.VMEM((2, tokens, half), BF16),
            pltpu.VMEM((2, tokens, half), BF16),
            pltpu.VMEM((2, tokens, half), BF16),
            pltpu.SemaphoreType.DMA((12,)),
            pltpu.SemaphoreType.DMA((12,)),
        ]


SCATTER_BUFFERS = 10


def pair_product(lefts, rights, tokens):
    def product(chunk, n):
        at = pl.ds(pl.multiple_of(chunk * tokens, tokens), tokens)
        cols = pl.ds(pl.multiple_of(n * 256, 256), 256)
        total = None
        for left, right in zip(lefts, rights):
            term = jnp.dot(left[at, :], right[:, cols], preferred_element_type=F32)
            total = term if total is None else total + term
        return total

    return product


def for_slices(start, stop, body):
    def step(n, none):
        body(pl.ds(pl.multiple_of(n * SLICE, SLICE), SLICE))
        return none

    lax.fori_loop(start // SLICE, stop // SLICE, step, 0)


def middle_kernel(left, right, own_in, gain, middle_out, gathered, *scratch):
    buffers, (block, send, recv) = scratch[:SCATTER_BUFFERS], scratch[SCATTER_BUFFERS:]
    tokens = own_in.shape[0]
    place = Place()
    place.greet()
    scatter = Scatter(place, pair_product([left], [right], tokens), *buffers)
    scatter.run_first()
    scatter.run_second()

    def body(at):
        middle = own_in[at, :].astype(F32) + scatter.rows(at)
        middle_out[at, :] = middle
        block[at, :] = (middle * rms(middle) * gain[...]).astype(BF16)

    gather = Gather(place, block, gathered, send, recv)
    for part in (0, 1):
        scatter.run_third(part)
        for_slices(part * tokens // 2, (part + 1) * tokens // 2, body)
        gather.begin(part)
    gather.pass_on()
    scatter.finish()
    gather.finish()


def turn_kernel(
    left0, left1, right0, right1, middle, gain, cot, w_out, normed_far,
    grad_middle_out, gain_out, grads_out, mixed_out, gathered, *scratch,
):
    buffers, (block, send, recv, normed, chunk_ref, load) = scratch[:SCATTER_BUFFERS], scratch[SCATTER_BUFFERS:]
    loaded = pltpu.make_async_copy(normed_far, normed, load.at[0])
    loaded.start()
    tokens = cot.shape[0]
    place = Place()
    place.greet()
    scatter = Scatter(place, pair_product([left0, left1], [right0, right1], tokens), *buffers)
    def weight_grads(start, stop):
        def step(n, none):
            at = pl.ds(pl.multiple_of(n * 256, 256), 256)
            value = lax.dot_general(normed[:, at], left1[...], (((0,), (0,)), ((), ())), preferred_element_type=F32)
            grads_out[at, :] = value.astype(BF16)
            return none

        lax.fori_loop(start, stop, step, 0)

    steps = normed.shape[1] // 256
    scatter.run_first()
    loaded.wait()
    weight_grads(0, steps // 4)
    scatter.run_second()
    weight_grads(steps // 4, steps // 2)
    gain_out[...] = jnp.zeros_like(gain_out)

    def body(at):
        values = middle[at, :]
        grad = scatter.rows(at)
        scale = rms(values)
        weighted = grad * gain[...]
        inner = jnp.mean(values * weighted, axis=-1, keepdims=True)
        total = cot[at, :].astype(F32) + scale * weighted - values * (scale * scale * scale * inner)
        grad_middle_out[at, :] = total
        block[at, :] = total.astype(BF16)
        term = grad * values * scale
        gain_out[...] += term[0:8] + term[8:16]

    gather = Gather(place, block, gathered, send, recv)
    for part in (0, 1):
        scatter.run_third(part)
        for_slices(part * tokens // 2, (part + 1) * tokens // 2, body)
        gather.begin(part)
    weight_grads(steps // 2, 3 * steps // 4)
    gather.pass_first()
    weight_grads(3 * steps // 4, steps)
    gather.pass_second()

    def fetch(slot, chunk):
        at = pl.ds(pl.multiple_of(chunk * tokens, tokens), tokens)
        copy = pltpu.make_async_copy(gathered.at[at], chunk_ref.at[slot], load.at[slot])
        copy.start()
        return copy, slot, chunk

    def mixed_back(fetched):
        copy, slot, chunk = fetched
        copy.wait()
        mixed_of(chunk_ref[slot], chunk)

    def mixed_of(values, chunk):
        at = pl.ds(pl.multiple_of(chunk * tokens, tokens), tokens)
        mixed_out[at, :] = lax.dot_general(values, w_out[...], (((1,), (1,)), ((), ())), preferred_element_type=F32)

    ahead = fetch(0, place.chunk(0, 1, 0))
    mixed_of(block[...], place.chunk(0, 0, 0))
    after = fetch(1, place.chunk(1, 0, 0))
    mixed_back(ahead)
    gather.finish_core()
    ahead = fetch(0, place.chunk(0, 0, 1))
    mixed_back(after)
    gather.pass_third()
    after = fetch(1, place.chunk(1, 1, 0))
    mixed_back(ahead)
    gather.finish_near()
    ahead = fetch(0, place.chunk(0, 1, 1))
    mixed_back(after)
    after = fetch(1, place.chunk(1, 0, 1))
    mixed_back(ahead)
    gather.finish_far()
    ahead = fetch(0, place.chunk(1, 1, 1))
    mixed_back(after)
    mixed_back(ahead)
    scatter.finish()
    gather.finish_sends()


class Owners:
    def __init__(self, place, reduced, out, send, recv):
        self.place, self.reduced, self.out, self.send, self.recv = place, reduced, out, send, recv
        self.own = place.chunk(0, 0, 0)

    def copy(self, number, offset, slot):
        return pltpu.make_async_remote_copy(
            src_ref=self.reduced.at[self.place.chunk(*offset)],
            dst_ref=self.out.at[slot],
            send_sem=self.send.at[number],
            recv_sem=self.recv.at[number],
            device_id=self.place.peer(*offset),
            device_id_type=MESH,
        )

    def begin(self):
        self.keep = pltpu.make_async_copy(self.reduced.at[self.own], self.out.at[self.own], self.send.at[7])
        self.keep.start()
        self.moved = [self.copy(number, offset, self.own) for number, offset in enumerate(OTHERS)]
        for copy in self.moved:
            copy.start()

    def finish(self):
        for number, offset in enumerate(OTHERS):
            self.copy(number, offset, self.place.chunk(*offset)).wait_recv()
        for copy in self.moved:
            copy.wait_send()
        self.keep.wait()


OWNERS_SCRATCH = [pltpu.SemaphoreType.DMA((8,))] * 2
BEYOND = [offset for offset in OTHERS if sum(offset) > 1]


class GateSums:
    def __init__(self, place, count, pieces, rows_recv, gates_all, send, recv):
        self.place, self.count, self.pieces = place, count, pieces
        self.rows_recv, self.gates_all, self.send, self.recv = rows_recv, gates_all, send, recv
        self.me = lax.axis_index("t")
        self.rank = place.g * 2 + place.c
        self.near = [offset for offset in OTHERS if not offset[0]]
        self.moved = []

    def copy(self, number, source, target, peer):
        return pltpu.make_async_remote_copy(
            src_ref=source,
            dst_ref=target,
            send_sem=self.send.at[number],
            recv_sem=self.recv.at[number],
            device_id=peer,
            device_id_type=MESH,
        )

    def begin(self):
        for number, offset in enumerate(self.near):
            other = lax.rem(self.place.chunk(*offset), 4)
            self.moved.append(self.copy(number, self.pieces.at[other], self.rows_recv.at[self.rank], self.place.peer(*offset)))
            self.moved[-1].start()
        self.rows_recv[self.rank] = self.pieces[self.rank]

    def pass_on(self):
        for number, offset in enumerate(self.near):
            other = lax.rem(self.place.chunk(*offset), 4)
            self.copy(number, self.pieces.at[other], self.rows_recv.at[other], self.place.peer(*offset)).wait_recv()
        for step in range(1, self.count):
            to = lax.rem(self.me + step, self.count)
            self.moved.append(self.copy(2 + step, self.rows_recv.at[to], self.gates_all.at[self.me], {"t": to}))
            self.moved[-1].start()
        self.gates_all[self.me] = self.rows_recv[self.me]

    def finish(self, out):
        for step in range(1, self.count):
            other = lax.rem(self.me + self.count - step, self.count)
            self.copy(2 + step, self.rows_recv.at[other], self.gates_all.at[other], {"t": other}).wait_recv()
        total = self.gates_all[0].astype(F32)
        for z in range(1, self.count):
            total = total + self.gates_all[z].astype(F32)
        out[...] = total
        for copy in self.moved:
            copy.wait_send()


def sum_everywhere(place, count, values, inbox, plane_sum, plane_box, send, recv):
    me = lax.axis_index("t")
    own = place.chunk(0, 0, 0)
    moved = []

    def copy(number, source, target, peer):
        return pltpu.make_async_remote_copy(
            src_ref=source,
            dst_ref=target,
            send_sem=send.at[number],
            recv_sem=recv.at[number],
            device_id=peer,
            device_id_type=MESH,
        )

    for number, offset in enumerate(OTHERS):
        moved.append(copy(number, values, inbox.at[own], place.peer(*offset)))
        moved[-1].start()
    inbox[own] = values[...]
    for number, offset in enumerate(OTHERS):
        copy(number, values, inbox.at[place.chunk(*offset)], place.peer(*offset)).wait_recv()
    total = inbox[0]
    for n in range(1, 8):
        total = total + inbox[n]
    plane_sum[...] = total
    for step in range(1, count):
        moved.append(copy(6 + step, plane_sum, plane_box.at[me], {"t": lax.rem(me + step, count)}))
        moved[-1].start()
    plane_box[me] = total
    for step in range(1, count):
        other = lax.rem(me + count - step, count)
        copy(6 + step, plane_sum, plane_box.at[other], {"t": other}).wait_recv()
    total = plane_box[0]
    for z in range(1, count):
        total = total + plane_box[z]
    for sent in moved:
        sent.wait_send()
    return total


def final_kernel(
    count, with_gates, left, right, own_in, gain, mlp_gains, pieces, grad_middle, reduced0, reduced1,
    grad_out, gains_out, gates_out, owned0, owned1,
    gain_sum, values, inbox, plane_sum, plane_box, sum_send, sum_recv, rows_recv, gates_all, gates_send, gates_recv,
    send0, recv0, send1, recv1, *buffers,
):
    tokens, width = own_in.shape
    place = Place()
    me = lax.axis_index("t")
    place.greet([place.peer(*offset) for offset in BEYOND] + [{"t": lax.rem(me + step, count)} for step in range(1, count)])
    scatter = Scatter(place, pair_product([left], [right], tokens), *buffers)
    owners = [Owners(place, reduced0, owned0, send0, recv0), Owners(place, reduced1, owned1, send1, recv1)]
    gates = GateSums(place, count, pieces, rows_recv, gates_all, gates_send, gates_recv)
    scatter.run_first()
    if with_gates:
        gates.begin()
    for part in owners:
        part.begin()
    scatter.run_second()
    if with_gates:
        gates.pass_on()
    scatter.run_third(0)
    scatter.run_third(1)
    gain_sum[...] = jnp.zeros_like(gain_sum)

    def body(at):
        x = own_in[at, :].astype(F32)
        grad = scatter.rows(at)
        scale = rms(x)
        weighted = grad * gain[...]
        inner = jnp.mean(x * weighted, axis=-1, keepdims=True)
        grad_out[at, :] = grad_middle[at, :] + scale * weighted - x * (scale * scale * scale * inner)
        term = grad * x * scale
        gain_sum[...] += term[0:8] + term[8:16]

    for_slices(0, tokens, body)
    lines = width // LANES
    for base, row in ((0, jnp.sum(mlp_gains[...], axis=0, keepdims=True)), (lines, jnp.sum(gain_sum[...], axis=0, keepdims=True))):
        for n in range(lines):
            values[base + n : base + n + 1, :] = row[:, n * LANES : (n + 1) * LANES]
    gains_out[...] = sum_everywhere(place, count, values, inbox, plane_sum, plane_box, sum_send, sum_recv)
    if with_gates:
        gates.finish(gates_out)
    else:
        gates_out[...] = jnp.zeros_like(gates_out)
    for part in owners:
        part.finish()
    scatter.finish()


def final_step(planes, with_gates, left, right, own_in, gain, mlp_gains, pieces, grad_middle, reduced):
    tokens, width = own_in.shape
    block = pieces.shape[1:] if with_gates else (16, LANES)
    slots = planes if with_gates else 1
    sums = (2 * width // LANES, LANES)
    return pl.pallas_call(
        functools.partial(final_kernel, planes, with_gates),
        name="final_step",
        out_shape=(
            jax.ShapeDtypeStruct((tokens, width), F32),
            jax.ShapeDtypeStruct(sums, F32),
            jax.ShapeDtypeStruct(block, F32),
            *[jax.ShapeDtypeStruct(part.shape, part.dtype) for part in reduced],
        ),
        in_specs=[*whole(7), ANYWHERE, ANYWHERE],
        out_specs=(*whole(3), ANYWHERE, ANYWHERE),
        scratch_shapes=[
            pltpu.VMEM((8, width), F32),
            pltpu.VMEM(sums, F32),
            pltpu.VMEM((8, *sums), F32),
            pltpu.VMEM(sums, F32),
            pltpu.VMEM((planes, *sums), F32),
            pltpu.SemaphoreType.DMA((planes + 6,)),
            pltpu.SemaphoreType.DMA((planes + 6,)),
            pltpu.VMEM((slots, *block), BF16),
            pltpu.VMEM((slots, *block), BF16),
            pltpu.SemaphoreType.DMA((planes + 2,)),
            pltpu.SemaphoreType.DMA((planes + 2,)),
            *OWNERS_SCRATCH,
            *OWNERS_SCRATCH,
            *Scatter.scratch(tokens, width),
        ],
        compiler_params=mixer_params(7),
    )(left, right, own_in, gain[None], mlp_gains, pieces, grad_middle, *reduced)


def owners_kernel(reduced, out, send, recv):
    place = Place()
    place.greet([place.peer(*offset) for offset in BEYOND])
    owners = Owners(place, reduced, out, send, recv)
    owners.begin()
    owners.finish()


def owners_step(reduced):
    return pl.pallas_call(
        owners_kernel,
        name="owners_step",
        out_shape=jax.ShapeDtypeStruct(reduced.shape, reduced.dtype),
        in_specs=[ANYWHERE],
        out_specs=ANYWHERE,
        scratch_shapes=OWNERS_SCRATCH,
        compiler_params=mixer_params(8),
    )(reduced)


def place_kernel(planes, hidden, outs, *refs):
    given, results = refs[: -len(outs)], refs[-len(outs) :]
    each = sum(outs) // len(given)
    piece = given[0].shape[2] // (each * (planes if hidden else 1))
    kind = 0
    for count, out in zip(outs, results):
        for slot in range(count):
            sources, k = given[kind // each], kind % each
            kind += 1
            if hidden:
                groups = [
                    ((t * 2 + i) * 4 * piece, [(i * 4 + r, (k * planes + t) * piece) for r in range(4)])
                    for t in range(planes)
                    for i in range(2)
                ]
            else:
                groups = [(r * 2 * piece, [(i * 4 + r, k * piece) for i in range(2)]) for r in range(4)]
            for start, parts in groups:
                row = jnp.concatenate([sources[p, :, at : at + piece].astype(F32) for p, at in parts], axis=1)
                if count > 1:
                    out[:, slot, start : start + row.shape[1]] = row
                else:
                    out[:, start : start + row.shape[1]] = row


def place_columns(planes, hidden, outs, *owned):
    members, own_rows, columns = owned[0].shape
    total = columns * len(owned) * members // sum(outs)
    shapes = [(own_rows, count, total) if count > 1 else (own_rows, total) for count in outs]
    return pl.pallas_call(
        functools.partial(place_kernel, planes, hidden, outs),
        name="place_columns",
        out_shape=tuple(jax.ShapeDtypeStruct(shape, F32) for shape in shapes),
        in_specs=whole(len(owned)),
        out_specs=tuple(whole(len(outs))),
        compiler_params=pltpu.CompilerParams(vmem_limit_bytes=60 * 1024 * 1024),
    )(*owned)


def first_gather(planes, normed, ids):
    tokens, width = normed.shape
    every = (8, *ids.shape)
    return pl.pallas_call(
        functools.partial(first_gather_kernel, planes),
        name="first_gather",
        out_shape=(jax.ShapeDtypeStruct((8 * tokens, width), BF16), *[jax.ShapeDtypeStruct(every, F32)] * 3),
        in_specs=[ANYWHERE, *whole(1)],
        out_specs=(ANYWHERE, *whole(3)),
        scratch_shapes=[pltpu.VMEM(every, F32)] * 3 + GATHER_SCRATCH + [pltpu.SemaphoreType.DMA((9,))] * 2,
        compiler_params=mixer_params(3),
    )(normed, ids)


def middle_step(mixed, w_out, own_in, gain):
    tokens, width = own_in.shape
    return pl.pallas_call(
        middle_kernel,
        name="middle_step",
        out_shape=(jax.ShapeDtypeStruct((tokens, width), F32), jax.ShapeDtypeStruct((8 * tokens, width), BF16)),
        in_specs=whole(4),
        out_specs=(pl.BlockSpec(memory_space=pltpu.VMEM), ANYWHERE),
        scratch_shapes=Scatter.scratch(tokens, width) + [pltpu.VMEM((tokens, width), BF16)] + GATHER_SCRATCH,
        compiler_params=mixer_params(4),
    )(mixed, w_out, own_in, gain[None])


def turn_step(left0, left1, right0, right1, middle, gain, cot, w_out, normed):
    tokens, width = cot.shape
    return pl.pallas_call(
        turn_kernel,
        name="turn_step",
        out_shape=(
            jax.ShapeDtypeStruct((tokens, width), F32),
            jax.ShapeDtypeStruct((8, width), F32),
            jax.ShapeDtypeStruct((width, left1.shape[1]), BF16),
            jax.ShapeDtypeStruct((8 * tokens, w_out.shape[0]), F32),
            jax.ShapeDtypeStruct((8 * tokens, width), BF16),
        ),
        in_specs=[*whole(8), ANYWHERE],
        out_specs=(*whole(4), ANYWHERE),
        scratch_shapes=Scatter.scratch(tokens, width)
        + [pltpu.VMEM((tokens, width), BF16)]
        + GATHER_SCRATCH
        + [pltpu.VMEM(normed.shape, BF16), pltpu.VMEM((2, tokens, width), BF16), pltpu.SemaphoreType.DMA((2,))],
        compiler_params=mixer_params(5),
    )(left0, left1, right0, right1, middle, gain[None], cot, w_out, normed)


class Swap:
    def __init__(self, quarters, out, send, recv):
        self.quarters, self.out, self.send, self.recv = quarters, out, send, recv
        self.groups = quarters.shape[0]
        self.me = lax.axis_index("g") * 2 + lax.axis_index("c")

    def copy(self, step, other, slot):
        return pltpu.make_async_remote_copy(
            src_ref=self.quarters.at[other],
            dst_ref=self.out.at[:, slot],
            send_sem=self.send.at[step],
            recv_sem=self.recv.at[step],
            device_id={"g": other // 2, "c": other % 2},
            device_id_type=MESH,
        )

    def peers(self):
        others = [lax.rem(self.me + step, self.groups) for step in range(1, self.groups)]
        return [{"g": other // 2, "c": other % 2} for other in others]

    def begin(self):
        self.keep = pltpu.make_async_copy(self.quarters.at[self.me], self.out.at[:, self.me], self.send.at[0])
        self.keep.start()
        self.moved = []
        for step in range(1, self.groups):
            self.moved.append(self.copy(step, lax.rem(self.me + step, self.groups), self.me))
            self.moved[-1].start()

    def finish(self):
        for step in range(1, self.groups):
            other = lax.rem(self.me + self.groups - step, self.groups)
            self.copy(step, other, other).wait_recv()
        for copy in self.moved:
            copy.wait_send()
        self.keep.wait()


def swap_scratch(groups):
    return [pltpu.SemaphoreType.DMA((groups,)), pltpu.SemaphoreType.DMA((groups,))]


def swap_kernel(quarters, out, send, recv):
    move = Swap(quarters, out, send, recv)
    barrier = pltpu.get_barrier_semaphore()
    for peer in move.peers():
        pl.semaphore_signal(barrier, inc=1, device_id=peer, device_id_type=MESH)
    pl.semaphore_wait(barrier, move.groups - 1)
    move.begin()
    move.finish()


def swap(quarters):
    groups, kinds, part, width = quarters.shape
    return pl.pallas_call(
        swap_kernel,
        name="swap",
        out_shape=jax.ShapeDtypeStruct((kinds, groups, part, width), quarters.dtype),
        in_specs=[ANYWHERE],
        out_specs=ANYWHERE,
        scratch_shapes=swap_scratch(groups),
        compiler_params=mixer_params(6),
    )(quarters)


def rms(values):
    return lax.rsqrt(jnp.mean(values * values, axis=-1, keepdims=True) + EPS)


def nt(left, right, out):
    return lax.dot_general(left, right, (((1,), (1,)), ((), ())), preferred_element_type=F32).astype(out)


def tn(left, right, out):
    return lax.dot_general(left, right, (((0,), (0,)), ((), ())), preferred_element_type=F32).astype(out)


def nn(left, right, out):
    return jnp.dot(left, right, preferred_element_type=F32).astype(out)


def per_device(
    inputs, segment_ids, mix_gain, in_weight, conv_weight, conv_bias, gate_weight, gate_bias, decay_param, out_weight,
    mlp_gain, mlp_in, down_weight, cotangent,
):
    planes = lax.axis_size("t")
    rows_here, seg, width = inputs.shape
    row_groups = lax.axis_size("g") * lax.axis_size("c")
    own_tokens = rows_here * seg
    recur_width = conv_weight.shape[1]
    block_width = gate_weight.shape[0]
    members = 2 * row_groups
    channels = recur_width // members
    t, i = lax.axis_index("t"), lax.axis_index("i")
    r = lax.axis_index("g") * lax.axis_size("c") + lax.axis_index("c")
    member = 2 * r + i
    first = member * channels
    own_rows = width // (planes * members)

    own_in = inputs.reshape(own_tokens, width)
    flat_in = own_in.astype(F32)
    scale_in = rms(flat_in)
    cot_own = cotangent.reshape(own_tokens, width)
    own_ids = jnp.pad((segment_ids + 1).astype(F32), ((0, 8 - rows_here), (0, 0)))

    normed, *ids = first_gather(planes, (flat_in * scale_in * mix_gain).astype(BF16), own_ids)
    late_r, ids[0] = lax.optimization_barrier((r, ids[0]))

    direct = planes == row_groups
    in_own = in_weight.transpose(1, 2, 0)
    out_own = out_weight.T[None]
    part = channels // row_groups if direct else 0

    def quarter(weight, part, rank=r):
        return lax.dynamic_slice_in_dim(weight, rank * part, part, weight.ndim - 1)

    def spread_units(weight):
        return lax.all_gather(weight, "t", axis=0, tiled=False)

    def whole_units(weight):
        every = lax.all_gather(weight, ("t", "i"), axis=1, tiled=True)
        return lax.dynamic_slice_in_dim(every, first, channels, 1)

    if direct:
        in_w = swap(spread_units(quarter(in_weight, part).transpose(1, 2, 0)))
        out_quarters = spread_units(quarter(out_weight, part).T[None])
    else:
        in_w = whole_units(in_own)
        out_quarters = jnp.zeros((row_groups, 1, 16, width), BF16)
    in_w = in_w.reshape(2 * channels, width)
    hidden_part = mlp_in.shape[2] // row_groups
    gated = quarter(mlp_in, hidden_part, late_r).transpose(1, 2, 0)
    w_left, w_right, w_down = [
        spread_units(part).reshape(-1, width)
        for part in (gated[0], gated[1], quarter(down_weight, hidden_part, late_r).T)
    ]

    def own(values):
        return lax.dynamic_slice_in_dim(values, first, channels, values.ndim - 1)

    vec = own(
        jnp.concatenate(
            [
                conv_weight,
                conv_bias[None],
                gate_bias,
                8.0 * jax.nn.softplus(-decay_param)[None],
                8.0 * jax.nn.sigmoid(-decay_param)[None],
                jnp.zeros((7, recur_width), F32),
            ]
        )
    )
    gate_blocks = own(gate_weight).transpose(1, 0, 2)
    blocks = channels // block_width

    branches = nt(normed, in_w, F32)
    conv_low, decay, states, mixed, halo, cin, mask, cot, w_out = mixer_forward(
        planes, seg, rows_here, branches, ids, gate_blocks, vec, cot_own, out_quarters
    )
    w_out = (w_out if direct else whole_units(out_own)).reshape(channels, width)
    middle, normed_two = middle_step(mixed, w_out, own_in, mlp_gain)
    left = nt(normed_two, w_left, F32)
    right = nt(normed_two, w_right, F32)
    act, slope = gelu_parts(left)
    hidden = (act * right).astype(BF16)

    def over_planes(grad):
        return lax.psum_scatter(grad, "t", scatter_dimension=0, tiled=True)

    grad_down = tn(cot, hidden, BF16)
    grad_down, hidden, w_down = lax.optimization_barrier((grad_down, hidden, w_down))
    grad_down = over_planes(grad_down)
    grad_hidden = nt(cot, w_down, F32)
    grad_left = (grad_hidden * right * slope).astype(BF16)
    grad_right = (grad_hidden * act).astype(BF16)
    grad_left_w = tn(normed_two, grad_left, BF16)
    grad_left_w, grad_left, grad_right = lax.optimization_barrier((grad_left_w, grad_left, grad_right))
    grad_left_w = over_planes(grad_left_w)
    grad_middle, grad_mlp_gain, grad_right_w, grad_mixed, grad_mid = turn_step(
        grad_left, grad_right, w_left, w_right, middle, mlp_gain, cot_own, w_out, normed_two
    )
    grad_right_w = over_planes(grad_right_w)
    grad_out = tn(grad_mid, mixed, BF16)

    def by_owner(grad):
        return grad.reshape(members, own_rows, -1)

    grad_branches, gw0, gw1, small, pieces, outputs, owned_down = mixer_backward(
        planes, seg, grad_mixed, branches, states, decay, conv_low, mask, halo, cin, gate_blocks, vec, hidden, w_down, middle,
        by_owner(grad_down),
    )
    grad_in = jnp.concatenate([tn(normed, grad_branches, BF16), grad_out], axis=1)
    grad_right_w, grad_in, grad_branches = lax.optimization_barrier((grad_right_w, grad_in, grad_branches))
    grad_in = over_planes(grad_in)
    outputs = outputs.reshape(inputs.shape)

    grad_inputs, gains, gate_grads, owned_left, owned_right = final_step(
        planes, direct, grad_branches, in_w, own_in, mix_gain, grad_mlp_gain, pieces, grad_middle,
        [by_owner(grad_left_w), by_owner(grad_right_w)],
    )
    grad_inputs = grad_inputs.reshape(inputs.shape)
    index = ((t * 2 + i) * row_groups + r) * own_rows
    gains = lax.dynamic_slice_in_dim(gains.reshape(2, width), index, own_rows, 1)


    owned_in = owners_step(by_owner(grad_in))

    def columns(hidden, outs, *owned):
        if direct:
            return place_columns(planes, hidden, outs, *owned)
        owned = jnp.concatenate(owned, axis=2)
        owned = owned.reshape(2, row_groups, own_rows, sum(outs), planes if hidden else 1, -1).astype(F32)
        order = (2, 3, 4, 0, 1, 5) if hidden else (2, 3, 1, 0, 4, 5)
        owned = owned.transpose(order).reshape(own_rows, sum(outs), -1)
        return (owned[:, :2], owned[:, 2])

    grad_in_weight, grad_out_weight = columns(False, (2, 1), owned_in)
    grad_mlp_in, grad_down_weight = columns(True, (2, 1), owned_left, owned_right, owned_down)
    if direct:
        gate_grads = gate_grads[:, :part]
    else:
        column_block = lax.broadcasted_iota(jnp.int32, (block_width, channels), 1) // block_width

        def diagonal(gw):
            return sum(
                jnp.where(column_block == n, gw[n * block_width : (n + 1) * block_width], 0.0) for n in range(blocks)
            )

        gate_grads = jnp.concatenate([diagonal(gw0), diagonal(gw1), small], axis=0)
        placed = jnp.zeros((gate_grads.shape[0], recur_width), F32)
        placed = lax.dynamic_update_slice_in_dim(placed, gate_grads, first, 1)
        gate_grads = lax.psum_scatter(placed, EVERY, scatter_dimension=1, tiled=True)
    grad_gate_weight = jnp.stack([gate_grads[:block_width], gate_grads[block_width : 2 * block_width]], axis=1)
    small = gate_grads[2 * block_width : 2 * block_width + 8]
    return (
        outputs,
        grad_inputs,
        gains[1],
        grad_in_weight,
        small[0:4],
        small[4],
        grad_gate_weight,
        small[5:7],
        small[7],
        grad_out_weight,
        gains[0],
        grad_mlp_in,
        grad_down_weight,
    )


def solution(mesh):
    seq, rows = mesh.shape["seq"], mesh.shape["rows"]
    grid = Mesh(mesh.devices.reshape(seq // 2, 2, rows // 2, 2), EVERY)
    row_axes, seq_axes = ("g", "c"), ("t", "i")
    tokens = P(row_axes, seq_axes, None)
    return jax.shard_map(
        per_device,
        mesh=grid,
        in_specs=(
            tokens,
            P(row_axes, seq_axes),
            P(),
            P(None, None, seq_axes),
            P(),
            P(),
            P(),
            P(),
            P(),
            P(None, seq_axes),
            P(),
            P(None, None, seq_axes),
            P(None, seq_axes),
            tokens,
        ),
        out_specs=(
            tokens,
            tokens,
            P(EVERY),
            P(EVERY, None, None),
            P(None, EVERY),
            P(EVERY),
            P(None, None, EVERY),
            P(None, EVERY),
            P(EVERY),
            P(EVERY, None),
            P(EVERY),
            P(EVERY, None, None),
            P(EVERY, None),
        ),
        check_vma=False,
    )
```

```python
import functools

import jax
import jax.numpy as jnp
from jax import lax
from jax.experimental import pallas as pl
from jax.experimental.pallas import tpu as pltpu
from jax.sharding import Mesh
from jax.sharding import PartitionSpec as P

EPS = 1e-06
MESH = pl.DeviceIdType.MESH
PLANE = ("i", "g", "c")
EVERY = ("t", "i", "g", "c")
F32 = jnp.float32
BF16 = jnp.bfloat16
GELU_A = 0.7978845608028654
GELU_B = 0.044715
HALO = 8
LANES = 128
SLICE = 16
ANYWHERE = pl.BlockSpec(memory_space=pl.ANY)
GATHER_SCRATCH = [pltpu.SemaphoreType.DMA((14,))] * 2


def gelu_parts(x):
    square = x * x
    th = jnp.tanh(GELU_A * x * (1.0 + GELU_B * square))
    half = 0.5 * (1.0 + th)
    slope = half + 0.5 * x * (1.0 - th * th) * (GELU_A * (1.0 + 3.0 * GELU_B * square))
    return x * half, slope


def one_minus_exp(y, power):
    series = 1.0 + y * (-1.0 / 2 + y * (1.0 / 6 + y * (-1.0 / 24 + y * (1.0 / 120 + y * (-1.0 / 720 + y * (1.0 / 5040))))))
    return jnp.where(y < 0.35, y * series, 1.0 - power)


def sigmoid(x):
    return 1.0 / (1.0 + jnp.exp(-x))


def gate_values(conv_low, wg0, wg1, vec):
    logits0 = jnp.dot(conv_low, wg0, preferred_element_type=F32) + vec[5:6]
    logits1 = jnp.dot(conv_low, wg1, preferred_element_type=F32) + vec[6:7]
    recur_gate = sigmoid(logits0)
    input_gate = sigmoid(logits1)
    log_decay = -vec[7:8] * recur_gate
    return recur_gate, input_gate, log_decay


def spread_blocks(gates, out):
    size, width = gates.shape[1], gates.shape[2]
    column = lax.broadcasted_iota(jnp.int32, (size, width), 1) // size
    for k in range(2):
        block = gates[k].astype(F32)
        for n in range(width // size):
            out[k, n * size : (n + 1) * size, :] = jnp.where(column == n, block, 0.0).astype(BF16)


def put_tiles(ref, at, values):
    tiles, lanes = ref.shape[0], ref.shape[2]
    short = tiles * lanes - values.shape[1]
    if short:
        values = jnp.concatenate([values, jnp.zeros((values.shape[0], short), values.dtype)], axis=1)
    for j in range(tiles):
        ref[j, at, :] = values[:, j * lanes : (j + 1) * lanes]


def get_tiles(ref, at, width):
    joined = jnp.concatenate([ref[j, at, :] for j in range(ref.shape[0])], axis=1)
    return joined[:, :width]


def join_tiles(parts, width):
    return jnp.concatenate(parts, axis=1)[:, :width]


def exchange_copy(step, send, target, other, send_sem, recv_sem):
    return pltpu.make_async_remote_copy(
        src_ref=send,
        dst_ref=target,
        send_sem=send_sem.at[step],
        recv_sem=recv_sem.at[step],
        device_id={"t": other},
        device_id_type=MESH,
    )


def exchange_start(count, me, send, slots, send_sem, recv_sem):
    for step in range(1, count):
        exchange_copy(step, send, slots.at[me], lax.rem(me + step, count), send_sem, recv_sem).start()


def exchange_wait(count, me, send, slots, send_sem, recv_sem):
    for step in range(1, count):
        other = lax.rem(me + count - step, count)
        exchange_copy(step, send, slots.at[other], other, send_sem, recv_sem).wait()


def mixer_forward_kernel(
    count, seg, rows_here, branches_far, ids, ids_before, ids_after, gate_blocks, vec_ref, cot, quarters,
    conv_out, decay_out, states_out, mixed_out, halo_out, cin_out, mask, cot_out, swapped,
    drive, h_ref, a_ref, ext, halo_send, halo_recv, summary, slots, send_sem, recv_sem, halo_sems,
    gather_send, gather_recv, swap_send, swap_recv, branches, wg, load,
):
    place = Place()
    me = lax.axis_index("t")
    loaded = pltpu.make_async_copy(branches_far, branches, load.at[0])
    loaded.start()
    place.greet([place.peer(0, 1, 1)] + [{"t": lax.rem(me + step, count)} for step in range(1, count)])
    gather = Gather(place, cot, cot_out, gather_send, gather_recv)
    move = Swap(quarters, swapped, swap_send, swap_recv)
    gather.begin_whole()
    move.begin()
    spread_blocks(gate_blocks, wg)
    rows = 8
    width = branches.shape[1] // 2
    loaded.wait()

    def recur_at(at):
        return branches[at, width:].astype(BF16).astype(F32)

    for r in range(rows):
        halo_send[r * HALO : (r + 1) * HALO, :] = recur_at(pl.ds((rows + r + 1) * seg - HALO, HALO))
    halo_copy = pltpu.make_async_remote_copy(
        src_ref=halo_send,
        dst_ref=halo_recv,
        send_sem=halo_sems.at[0],
        recv_sem=halo_sems.at[1],
        device_id={"t": lax.rem(me + 1, count)},
        device_id_type=MESH,
    )
    halo_copy.start()
    for r in range(rows):
        halo_out[(rows + r) * HALO : (rows + r + 1) * HALO, :] = recur_at(pl.ds((r + 1) * seg - HALO, HALO))
    vec = vec_ref[...]

    def ids_of(ref, s):
        chunk = s // rows_here
        return ref[chunk, s % rows_here : s % rows_here + 1, :]

    nothing = jnp.zeros((1, LANES), F32)
    for s in range(2 * rows):
        here = ids_of(ids, s)
        back = ids_of(ids, s - rows) if s >= rows else jnp.where(me > 0, ids_of(ids_before, s + rows), nothing)
        ahead = ids_of(ids, s + rows) if s < rows else jnp.where(me < count - 1, ids_of(ids_after, s - rows), nothing)
        lines = [jnp.concatenate([back[:, seg - k :], here[:, : seg - k]], axis=1) for k in (1, 2, 3)]
        lines += [jnp.concatenate([here[:, k:], ahead[:, :k]], axis=1) for k in (1, 2, 3)]
        lines = [jnp.where(line == here, 1.0, 0.0) for line in lines] + [nothing] * 2
        mask[s * seg : (s + 1) * seg, :] = jnp.concatenate(lines, axis=0).T

    def local(s, none):
        at = pl.ds(pl.multiple_of(s * seg, seg), seg)
        x = recur_at(at)
        ext[0:HALO, :] = halo_out[pl.ds(pl.multiple_of(s * HALO, HALO), HALO), :]
        ext[HALO : HALO + seg, :] = x
        m = mask[at, :]
        conv = vec[4:5] + vec[0:1] * x
        for k in range(1, 4):
            conv = conv + vec[k : k + 1] * ext[HALO - k : HALO - k + seg, :] * m[:, k - 1 : k]
        conv_low = conv.astype(BF16)
        conv_out[at, :] = conv_low
        recur_gate, input_gate, log_decay = gate_values(conv_low, wg[0], wg[1], vec)
        keep = m[:, 0:1]
        kept = jnp.exp(log_decay)
        put_tiles(decay_out, at, kept * keep)
        scale = (1.0 - keep) + keep * jnp.sqrt(one_minus_exp(-2.0 * log_decay, kept * kept))
        put_tiles(drive, at, scale * input_gate * conv_low.astype(F32))
        return none

    lax.fori_loop(rows, 2 * rows, local, 0)
    halo_copy.wait()
    for r in range(rows):
        halo_out[r * HALO : (r + 1) * HALO, :] = halo_recv[r * HALO : (r + 1) * HALO, :]
    gather.pass_first()
    lax.fori_loop(0, rows, local, 0)
    tiles, lanes = drive.shape[0], drive.shape[2]

    def scan(k, carried):
        at = pl.ds(k, 2 * rows, stride=seg)
        after = []
        for j in range(tiles):
            h, a = carried[j]
            d = decay_out[j, at, :]
            h = d * h + drive[j, at, :]
            a = a * d
            h_ref[j, at, :] = h
            a_ref[j, at, :] = a
            after.append((h, a))
        return tuple(after)

    start = (jnp.zeros((2 * rows, lanes), F32), jnp.ones((2 * rows, lanes), F32))
    last = lax.fori_loop(0, seg, scan, (start,) * tiles, unroll=4)
    last_h = join_tiles([part[0] for part in last], width)
    last_a = join_tiles([part[1] for part in last], width)
    summary[0:rows, :] = last_a[rows:] * last_a[:rows]
    summary[rows : 2 * rows, :] = last_a[rows:] * last_h[:rows] + last_h[rows:]
    exchange_start(count, me, summary, slots, send_sem, recv_sem)
    gather.pass_second()

    def activate(s, none):
        at = pl.ds(pl.multiple_of(s * seg, seg), seg)
        act, _ = gelu_parts(branches[at, :width])
        states_out[at, :] = act
        return none

    lax.fori_loop(0, 2 * rows, activate, 0)
    exchange_wait(count, me, summary, slots, send_sem, recv_sem)
    carry = jnp.zeros((rows, width), F32)
    for z in range(count - 1):
        carry = jnp.where(z < me, slots[z, 0:rows, :] * carry + slots[z, rows : 2 * rows, :], carry)
    cin_out[0:rows, :] = carry
    cin_out[rows : 2 * rows, :] = last_a[:rows] * carry + last_h[:rows]

    def finish(s, none):
        at = pl.ds(pl.multiple_of(s * seg, seg), seg)
        states = get_tiles(h_ref, at, width) + get_tiles(a_ref, at, width) * cin_out[pl.ds(s, 1), :]
        act = states_out[at, :]
        states_out[at, :] = states
        mixed_out[at, :] = (act * states.astype(BF16).astype(F32)).astype(BF16)
        return none

    lax.fori_loop(0, 2 * rows, finish, 0)
    gather.pass_third()
    gather.finish()
    move.finish()


def mixer_backward_kernel(
    count, seg, grad_mixed_far, branches_far, states_far, decay_far, conv_far, mask_far, halo, cin, gate_blocks, vec_ref,
    hidden, w_down, middle_far, reduced, grad_out, gw0_out, gw1_out, small_out, pieces_out, outputs, owned,
    tot, prod, ext, halo_send, halo_recv, summary, slots, uin, send_sem, recv_sem, halo_sems,
    grad_mixed, branches, states, decay, conv_low_ref, mask, middle, wg, load, own_send, own_recv, *buffers,
):
    place = Place()
    pairs = (
        (grad_mixed_far, grad_mixed),
        (branches_far, branches),
        (states_far, states),
        (decay_far, decay),
        (conv_far, conv_low_ref),
        (mask_far, mask),
        (middle_far, middle),
    )
    loads = [pltpu.make_async_copy(far, near, load.at[n]) for n, (far, near) in enumerate(pairs)]
    for part in loads:
        part.start()
    me = lax.axis_index("t")
    place.greet([place.peer(*offset) for offset in BEYOND] + [{"t": lax.rem(me + step, count)} for step in range(1, count)])
    scatter = Scatter(place, pair_product([hidden], [w_down], outputs.shape[0]), *buffers)
    owners = Owners(place, reduced, owned, own_send, own_recv)
    spread_blocks(gate_blocks, wg)
    scatter.run_first()
    owners.begin()
    for part in loads:
        part.wait()
    rows = 8
    width = branches.shape[1] // 2
    vec = vec_ref[...]

    def local(s, none):
        at = pl.ds(pl.multiple_of(s * seg, seg), seg)
        act, slope = gelu_parts(branches[at, :width])
        gm = grad_mixed[at, :].astype(F32)
        grad_out[at, :width] = (gm * states[at, :].astype(BF16).astype(F32) * slope).astype(BF16)
        put_tiles(tot, at, (gm * act).astype(BF16).astype(F32))
        return none

    lax.fori_loop(0, 2 * rows, local, 0)

    tiles, lanes = tot.shape[0], tot.shape[2]

    def scan(k, carried):
        at = pl.ds(seg - 1 - k, 2 * rows, stride=seg)
        after = []
        for j in range(tiles):
            u, p = carried[j]
            d = decay[j, at, :]
            total = tot[j, at, :] + u
            tot[j, at, :] = total
            prod[j, at, :] = p
            after.append((d * total, d * p))
        return tuple(after)

    start = (jnp.zeros((2 * rows, lanes), F32), jnp.ones((2 * rows, lanes), F32))
    last = lax.fori_loop(0, seg, scan, (start,) * tiles, unroll=4)
    u = join_tiles([part[0] for part in last], width)
    p = join_tiles([part[1] for part in last], width)
    summary[0:rows, :] = p[:rows] * p[rows:]
    summary[rows : 2 * rows, :] = p[:rows] * u[rows:] + u[:rows]
    exchange_start(count, me, summary, slots, send_sem, recv_sem)
    scatter.run_second()
    exchange_wait(count, me, summary, slots, send_sem, recv_sem)
    carry = jnp.zeros((rows, width), F32)
    for z in range(count - 1, 0, -1):
        carry = jnp.where(z > me, slots[z, 0:rows, :] * carry + slots[z, rows : 2 * rows, :], carry)
    uin[rows : 2 * rows, :] = carry
    uin[0:rows, :] = p[rows:] * carry + u[rows:]
    gw0_out[...] = jnp.zeros_like(gw0_out)
    gw1_out[...] = jnp.zeros_like(gw1_out)
    small_out[...] = jnp.zeros_like(small_out)

    def gates(s, none):
        at = pl.ds(pl.multiple_of(s * seg, seg), seg)
        total = get_tiles(tot, at, width) + get_tiles(prod, at, width) * uin[pl.ds(s, 1), :]
        ext[HALO - 1 : HALO, :] = cin[pl.ds(s, 1), :]
        ext[HALO : HALO + seg, :] = states[at, :]
        before = ext[HALO - 1 : HALO - 1 + seg, :]
        conv_low = conv_low_ref[at, :]
        conv_vals = conv_low.astype(F32)
        m = mask[at, :]
        keep = m[:, 0:1]
        recur_gate, input_gate, log_decay = gate_values(conv_low, wg[0], wg[1], vec)
        power = jnp.exp(2.0 * log_decay)
        gone = one_minus_exp(-2.0 * log_decay, power)
        inverse = lax.rsqrt(gone)
        root = gone * inverse
        scale = (1.0 - keep) + keep * root
        driven_in = total * conv_vals
        grad_log = total * before * get_tiles(decay, at, width) - driven_in * input_gate * keep * (power * inverse)
        grad0 = grad_log * log_decay * (1.0 - recur_gate)
        grad1 = driven_in * scale * input_gate * (1.0 - input_gate)
        low0 = grad0.astype(BF16)
        low1 = grad1.astype(BF16)
        inputs_of = (((1,), (1,)), ((), ()))
        grad_conv = (
            total * scale * input_gate
            + lax.dot_general(low0, wg[0], inputs_of, preferred_element_type=F32)
            + lax.dot_general(low1, wg[1], inputs_of, preferred_element_type=F32)
        )
        put_tiles(tot, at, grad_conv)
        turned = (((0,), (0,)), ((), ()))
        gw0_out[...] += lax.dot_general(conv_low, low0, turned, preferred_element_type=F32)
        gw1_out[...] += lax.dot_general(conv_low, low1, turned, preferred_element_type=F32)
        x = branches[at, width:].astype(BF16).astype(F32)
        ext[0:HALO, :] = halo[pl.ds(pl.multiple_of(s * HALO, HALO), HALO), :]
        ext[HALO : HALO + seg, :] = x

        def add(row, values):
            small_out[row : row + 1, :] += jnp.sum(values, axis=0, keepdims=True)

        add(0, grad_conv * x)
        for k in range(1, 4):
            add(k, grad_conv * ext[HALO - k : HALO - k + seg, :] * m[:, k - 1 : k])
        add(4, grad_conv)
        add(5, grad0)
        add(6, grad1)
        add(7, grad_log * recur_gate)
        return none

    lax.fori_loop(0, 2 * rows, gates, 0)
    small_out[7:8, :] = small_out[7:8, :] * vec[8:9]
    size, part = gate_blocks.shape[1], width // 4

    def padded(values):
        short = [values, jnp.zeros((values.shape[0], LANES - part), F32)]
        return jnp.concatenate(short, axis=1)

    for r in range(4):
        first = r * part // size * size
        at = slice(r * part, (r + 1) * part)
        for k, square in enumerate((gw0_out, gw1_out)):
            pieces_out[r, k * size : (k + 1) * size, :] = padded(square[first : first + size, at]).astype(BF16)
        rest = jnp.concatenate([padded(small_out[:, at]), jnp.zeros((8, LANES), F32)], axis=0)
        pieces_out[r, 2 * size :, :] = rest.astype(BF16)
    for r in range(rows):
        halo_send[r * HALO : (r + 1) * HALO, :] = get_tiles(tot, pl.ds(r * seg, HALO), width)
    halo_copy = pltpu.make_async_remote_copy(
        src_ref=halo_send,
        dst_ref=halo_recv,
        send_sem=halo_sems.at[0],
        recv_sem=halo_sems.at[1],
        device_id={"t": lax.rem(me + count - 1, count)},
        device_id_type=MESH,
    )
    halo_copy.start()

    def back(s, none):
        at = pl.ds(pl.multiple_of(s * seg, seg), seg)
        m = mask[at, :]
        grad_conv = get_tiles(tot, at, width)
        ext[0:seg, :] = grad_conv
        result = vec[0:1] * grad_conv

        @pl.when(s < rows)
        def _():
            ext[seg : seg + HALO, :] = get_tiles(tot, pl.ds(pl.multiple_of((s + rows) * seg, seg), HALO), width)

        @pl.when(s >= rows)
        def _():
            ext[seg : seg + HALO, :] = halo_recv[pl.ds(pl.multiple_of((s - rows) * HALO, HALO), HALO), :]

        for k in range(1, 4):
            result = result + vec[k : k + 1] * ext[k : k + seg, :] * m[:, 2 + k : 3 + k]
        grad_out[at, width:] = result.astype(BF16)
        return none

    lax.fori_loop(0, rows, back, 0)
    halo_copy.wait()
    lax.fori_loop(rows, 2 * rows, back, 0)
    scatter.run_third(0)
    scatter.run_third(1)

    def body(at):
        outputs[at, :] = (middle[at, :] + scatter.rows(at)).astype(BF16)

    for_slices(0, outputs.shape[0], body)
    scatter.finish()
    owners.finish()


def whole(count):
    return [pl.BlockSpec(memory_space=pltpu.VMEM)] * count


def mixer_params(number):
    return pltpu.CompilerParams(collective_id=number, has_side_effects=True, vmem_limit_bytes=60 * 1024 * 1024)


def mixer_forward(count, seg, rows_here, branches, ids, gate_blocks, vec, cot, quarters):
    n, width = branches.shape[0], branches.shape[1] // 2
    full = functools.partial(jax.ShapeDtypeStruct, (n, width))
    tiles = -(-width // LANES)
    tiled = jax.ShapeDtypeStruct((tiles, n, LANES), F32)
    groups, kinds, part, depth = quarters.shape
    return pl.pallas_call(
        functools.partial(mixer_forward_kernel, count, seg, rows_here),
        name="mixer_forward",
        out_shape=(
            full(BF16), tiled, full(F32), full(BF16),
            jax.ShapeDtypeStruct((16 * HALO, width), F32), jax.ShapeDtypeStruct((16, width), F32),
            jax.ShapeDtypeStruct((n, 8), F32),
            jax.ShapeDtypeStruct((8 * cot.shape[0], cot.shape[1]), BF16),
            jax.ShapeDtypeStruct((kinds, groups, part, depth), BF16),
        ),
        in_specs=[ANYWHERE, *whole(5), ANYWHERE, ANYWHERE],
        out_specs=(*whole(7), ANYWHERE, ANYWHERE),
        scratch_shapes=[
            pltpu.VMEM((tiles, n, LANES), F32),
            pltpu.VMEM((tiles, n, LANES), F32),
            pltpu.VMEM((tiles, n, LANES), F32),
            pltpu.VMEM((seg + HALO, width), F32),
            pltpu.VMEM((8 * HALO, width), F32),
            pltpu.VMEM((8 * HALO, width), F32),
            pltpu.VMEM((16, width), F32),
            pltpu.VMEM((count, 16, width), F32),
            pltpu.SemaphoreType.DMA((count,)),
            pltpu.SemaphoreType.DMA((count,)),
            pltpu.SemaphoreType.DMA((2,)),
            *GATHER_SCRATCH,
            *swap_scratch(groups),
            pltpu.VMEM(branches.shape, F32),
            pltpu.VMEM((2, width, width), BF16),
            pltpu.SemaphoreType.DMA((1,)),
        ],
        compiler_params=mixer_params(1),
    )(branches, *ids, gate_blocks, vec, cot, quarters)


def mixer_backward(count, seg, grad_mixed, branches, states, decay, conv_low, mask, halo, cin, gate_blocks, vec, hidden, w_down, middle, reduced):
    n, width = branches.shape[0], branches.shape[1] // 2
    tokens, depth = n // 8, w_down.shape[1]
    full = functools.partial(jax.ShapeDtypeStruct, (n, width))
    tiles = -(-width // LANES)
    tiled = jax.ShapeDtypeStruct((tiles, n, LANES), F32)
    return pl.pallas_call(
        functools.partial(mixer_backward_kernel, count, seg),
        name="mixer_backward",
        out_shape=(
            jax.ShapeDtypeStruct((n, 2 * width), BF16),
            jax.ShapeDtypeStruct((width, width), F32), jax.ShapeDtypeStruct((width, width), F32),
            jax.ShapeDtypeStruct((8, width), F32),
            jax.ShapeDtypeStruct((4, 2 * gate_blocks.shape[1] + 16, LANES), BF16),
            jax.ShapeDtypeStruct((tokens, depth), BF16),
            jax.ShapeDtypeStruct(reduced.shape, BF16),
        ),
        in_specs=[*[ANYWHERE] * 6, *whole(6), *[ANYWHERE] * 2],
        out_specs=(*whole(6), ANYWHERE),
        scratch_shapes=[
            pltpu.VMEM((tiles, n, LANES), F32),
            pltpu.VMEM((tiles, n, LANES), F32),
            pltpu.VMEM((seg + HALO, width), F32),
            pltpu.VMEM((8 * HALO, width), F32),
            pltpu.VMEM((8 * HALO, width), F32),
            pltpu.VMEM((16, width), F32),
            pltpu.VMEM((count, 16, width), F32),
            pltpu.VMEM((16, width), F32),
            pltpu.SemaphoreType.DMA((count,)),
            pltpu.SemaphoreType.DMA((count,)),
            pltpu.SemaphoreType.DMA((2,)),
            *[pltpu.VMEM(part.shape, part.dtype) for part in (grad_mixed, branches, states, decay, conv_low, mask, middle)],
            pltpu.VMEM((2, width, width), BF16),
            pltpu.SemaphoreType.DMA((7,)),
            *[pltpu.SemaphoreType.DMA((8,))] * 2,
            *Scatter.scratch(tokens, depth),
        ],
        compiler_params=mixer_params(2),
    )(grad_mixed, branches, states, decay, conv_low, mask, halo, cin, gate_blocks, vec, hidden, w_down, middle, reduced)


class Place:
    def __init__(self):
        self.i, self.g, self.c = lax.axis_index("i"), lax.axis_index("g"), lax.axis_index("c")
        self.core, self.across, self.along = {"c": 1 - self.c}, {"g": 1 - self.g}, {"i": 1 - self.i}

    def chunk(self, di, dg, dc):
        i = 1 - self.i if di else self.i
        g = 1 - self.g if dg else self.g
        c = 1 - self.c if dc else self.c
        return (i * 2 + g) * 2 + c

    def peer(self, di, dg, dc):
        return {
            "i": 1 - self.i if di else self.i,
            "g": 1 - self.g if dg else self.g,
            "c": 1 - self.c if dc else self.c,
        }

    def greet(self, more=()):
        barrier = pltpu.get_barrier_semaphore()
        peers = [self.core, self.across, self.along, *more]
        for peer in peers:
            pl.semaphore_signal(barrier, inc=1, device_id=peer, device_id_type=MESH)
        pl.semaphore_wait(barrier, len(peers))


class Gather:
    COPIES = 12

    def __init__(self, place, block, out, send, recv):
        self.place, self.block, self.out, self.send, self.recv = place, block, out, send, recv
        self.tokens = block.shape[0]
        self.half = self.tokens // 2

    def rows(self, chunk, part):
        start = chunk * self.tokens + (self.half if part == 1 else 0)
        return self.out.at[pl.ds(pl.multiple_of(start, self.half), self.tokens if part == 2 else self.half)]

    def mine(self, part):
        if part == 2:
            return self.block
        return self.block.at[pl.ds(part * self.half, self.half)]

    def copy(self, number, source, chunk, part, peer):
        return pltpu.make_async_remote_copy(
            src_ref=source,
            dst_ref=self.rows(chunk, part),
            send_sem=self.send.at[number],
            recv_sem=self.recv.at[number],
            device_id=peer,
            device_id_type=MESH,
        )

    def begin(self, part, whole=False):
        place = self.place
        own = place.chunk(0, 0, 0)
        other = 1 - part if whole else part
        self.give(0 + part, own, part, place.across)
        self.give(2 + other, own, other, place.along)
        self.give(4 + part, own, part, place.core)
        keep = pltpu.make_async_copy(self.mine(part), self.rows(own, part), self.send.at[self.COPIES + part])
        keep.start()
        self.local = getattr(self, "local", []) + [keep]

    def begin_whole(self):
        self.begin(0, True)
        self.begin(1, True)

    def give(self, number, chunk, part, peer):
        moved = self.copy(number, self.mine(part), chunk, part, peer)
        moved.start()
        self.kept = getattr(self, "kept", []) + [moved]

    def arrived(self, number, chunk, part):
        self.copy(number, self.rows(chunk, part), chunk, part, self.place.core).wait_recv()

    def forward(self, number, chunk, part, peer):
        moved = self.copy(number, self.rows(chunk, part), chunk, part, peer)
        moved.start()
        self.kept.append(moved)

    def pass_first(self):
        place = self.place
        ax, al = place.chunk(0, 1, 0), place.chunk(1, 0, 0)
        self.arrived(0, ax, 0)
        self.forward(6, ax, 0, place.along)
        self.arrived(3, al, 1)
        self.forward(7, al, 1, place.across)

    def pass_second(self):
        place = self.place
        ax, al = place.chunk(0, 1, 0), place.chunk(1, 0, 0)
        self.arrived(1, ax, 1)
        self.forward(8, ax, 2, place.core)
        self.arrived(2, al, 0)
        self.forward(9, al, 2, place.core)

    def pass_third(self):
        dia = self.place.chunk(1, 1, 0)
        self.arrived(6, dia, 0)
        self.forward(10, dia, 0, self.place.core)
        self.arrived(7, dia, 1)
        self.forward(11, dia, 1, self.place.core)

    def pass_on(self):
        self.pass_first()
        self.pass_second()
        self.pass_third()

    def finish_core(self):
        for part in (0, 1):
            self.arrived(4 + part, self.place.chunk(0, 0, 1), part)

    def finish_near(self):
        self.arrived(8, self.place.chunk(0, 1, 1), 2)
        self.arrived(9, self.place.chunk(1, 0, 1), 2)

    def finish_far(self):
        for part in (0, 1):
            self.arrived(10 + part, self.place.chunk(1, 1, 1), part)

    def finish(self):
        self.finish_core()
        self.finish_near()
        self.finish_far()
        self.finish_sends()

    def finish_sends(self):
        for moved in self.kept:
            moved.wait_send()
        for keep in self.local:
            keep.wait()


OTHERS = [(di, dg, dc) for di in (0, 1) for dg in (0, 1) for dc in (0, 1) if di or dg or dc]


def first_gather_kernel(count, normed, ids, normed_out, ids_out, before_out, after_out, plane_ids, before, after, send, recv, ids_send, ids_recv):
    place = Place()
    me = lax.axis_index("t")
    up, down = {"t": lax.rem(me + 1, count)}, {"t": lax.rem(me + count - 1, count)}
    place.greet([place.peer(*offset) for offset in OTHERS if sum(offset) > 1] + [up, down])
    gather = Gather(place, normed, normed_out, send, recv)
    own = place.chunk(0, 0, 0)
    moved = []

    def move(number, source, target, peer):
        copy = pltpu.make_async_remote_copy(
            src_ref=source,
            dst_ref=target,
            send_sem=ids_send.at[number],
            recv_sem=ids_recv.at[number],
            device_id=peer,
            device_id_type=MESH,
        )
        copy.start()
        moved.append(copy)

    for number, offset in enumerate(OTHERS):
        move(number, ids, plane_ids.at[own], place.peer(*offset))
    gather.begin_whole()
    plane_ids[own] = ids[...]
    for number, offset in enumerate(OTHERS):
        chunk = place.chunk(*offset)
        pltpu.make_async_remote_copy(
            src_ref=ids,
            dst_ref=plane_ids.at[chunk],
            send_sem=ids_send.at[number],
            recv_sem=ids_recv.at[number],
            device_id=place.peer(*offset),
            device_id_type=MESH,
        ).wait_recv()
    move(7, plane_ids, before, up)
    move(8, plane_ids, after, down)
    gather.pass_on()
    for copy in moved[7:]:
        copy.wait_recv()
    for copy in moved:
        copy.wait_send()
    ids_out[...] = plane_ids[...]
    before_out[...] = before[...]
    after_out[...] = after[...]
    gather.finish()


class Scatter:
    def __init__(self, place, product, core_send, core_recv, held, acc, across_recv, along_recv, second, second_recv, send, recv):
        self.place, self.product = place, product
        self.core_send, self.core_recv, self.held, self.acc = core_send, core_recv, held, acc
        self.across_recv, self.along_recv, self.second, self.second_recv = across_recv, along_recv, second, second_recv
        self.send, self.recv = send, recv
        self.kept = []

    def copy(self, number, source, target, peer):
        return pltpu.make_async_remote_copy(
            src_ref=source,
            dst_ref=target,
            send_sem=self.send.at[number],
            recv_sem=self.recv.at[number],
            device_id=peer,
            device_id_type=MESH,
        )

    def start(self, *parts):
        moved = self.copy(*parts)
        moved.start()
        self.kept.append(moved)

    def run_first(self):
        place = self.place
        order = ((1, 1), (0, 1), (1, 0), (0, 0))
        tile = 256
        per_half = self.held.shape[3] // tile
        def give(di, dg):
            q = 2 * di + dg
            chunk = place.chunk(di, dg, 1)

            def send_tile(n, none):
                at = pl.ds(pl.multiple_of(n % per_half * tile, tile), tile)
                self.core_send[q, n // per_half, :, at] = self.product(chunk, n).astype(BF16)
                return none

            lax.fori_loop(0, 2 * per_half, send_tile, 0)
            self.start(q, self.core_send.at[q], self.core_recv.at[q], place.core)

        def take(di, dg):
            q = 2 * di + dg
            chunk = place.chunk(di, dg, 0)
            self.copy(q, self.core_send.at[q], self.core_recv.at[q], place.core).wait_recv()

            def sum_tile(n, none):
                at = pl.ds(pl.multiple_of(n % per_half * tile, tile), tile)
                value = self.product(chunk, n) + self.core_recv[q, n // per_half, :, at].astype(F32)
                if q:
                    self.held[q - 1, n // per_half, :, at] = value.astype(BF16)
                else:
                    self.acc[n // per_half, :, at] = value
                return none

            lax.fori_loop(0, 2 * per_half, sum_tile, 0)
            if dg:
                self.start(4 + di, self.held.at[q - 1, 0], self.across_recv.at[di], place.across)
            if di:
                self.start(6 + dg, self.held.at[q - 1, 1], self.along_recv.at[dg], place.along)

        give(*order[0])
        give(*order[1])
        take(*order[0])
        give(*order[2])
        take(*order[1])
        give(*order[3])
        take(*order[2])
        take(*order[3])

    def second_copy(self, half, part):
        tokens = self.second.shape[1] // 2
        at = pl.ds(part * tokens, tokens)
        peer = self.place.across if half else self.place.along
        return 8 + 2 * part + half, self.second.at[half, at], self.second_recv.at[half, at], peer

    def run_second(self):
        place = self.place
        tokens = self.second.shape[1] // 2
        for part in (0, 1):
            for half, number, buffer, mine in ((0, 5, self.across_recv, 2), (1, 7, self.along_recv, 1)):
                if part == 0:
                    self.copy(number, buffer.at[1], buffer.at[1], place.core).wait_recv()

                def add_rows(at):
                    total = self.held[mine - 1, half, at, :].astype(F32) + buffer[1, at, :].astype(F32)
                    self.second[half, at, :] = total.astype(BF16)

                for_slices(part * tokens, (part + 1) * tokens, add_rows)
                self.start(*self.second_copy(half, part))

    def run_third(self, part):
        place = self.place
        if part == 0:
            for number, buffer in ((4, self.across_recv), (6, self.along_recv)):
                self.copy(number, buffer.at[0], buffer.at[0], place.core).wait_recv()
        for half in (0, 1):
            self.copy(*self.second_copy(half, part)).wait_recv()

    def rows(self, at):
        first = self.acc[0, at, :] + self.across_recv[0, at, :].astype(F32) + self.second_recv[0, at, :].astype(F32)
        last = self.acc[1, at, :] + self.along_recv[0, at, :].astype(F32) + self.second_recv[1, at, :].astype(F32)
        return jnp.concatenate([first, last], axis=1)

    def finish(self):
        for moved in self.kept:
            moved.wait_send()

    @staticmethod
    def scratch(tokens, width):
        half = width // 2
        return [
            pltpu.VMEM((4, 2, tokens, half), BF16),
            pltpu.VMEM((4, 2, tokens, half), BF16),
            pltpu.VMEM((3, 2, tokens, half), BF16),
            pltpu.VMEM((2, tokens, half), F32),
            pltpu.VMEM((2, tokens, half), BF16),
            pltpu.VMEM((2, tokens, half), BF16),
            pltpu.VMEM((2, tokens, half), BF16),
            pltpu.VMEM((2, tokens, half), BF16),
            pltpu.SemaphoreType.DMA((12,)),
            pltpu.SemaphoreType.DMA((12,)),
        ]


SCATTER_BUFFERS = 10


def pair_product(lefts, rights, tokens):
    def product(chunk, n):
        at = pl.ds(pl.multiple_of(chunk * tokens, tokens), tokens)
        cols = pl.ds(pl.multiple_of(n * 256, 256), 256)
        total = None
        for left, right in zip(lefts, rights):
            term = jnp.dot(left[at, :], right[:, cols], preferred_element_type=F32)
            total = term if total is None else total + term
        return total

    return product


def for_slices(start, stop, body):
    def step(n, none):
        body(pl.ds(pl.multiple_of(n * SLICE, SLICE), SLICE))
        return none

    lax.fori_loop(start // SLICE, stop // SLICE, step, 0)


def middle_kernel(left, right, own_in, gain, middle_out, gathered, *scratch):
    buffers, (block, send, recv) = scratch[:SCATTER_BUFFERS], scratch[SCATTER_BUFFERS:]
    tokens = own_in.shape[0]
    place = Place()
    place.greet()
    scatter = Scatter(place, pair_product([left], [right], tokens), *buffers)
    scatter.run_first()
    scatter.run_second()

    def body(at):
        middle = own_in[at, :].astype(F32) + scatter.rows(at)
        middle_out[at, :] = middle
        block[at, :] = (middle * rms(middle) * gain[...]).astype(BF16)

    gather = Gather(place, block, gathered, send, recv)
    for part in (0, 1):
        scatter.run_third(part)
        for_slices(part * tokens // 2, (part + 1) * tokens // 2, body)
        gather.begin(part)
    gather.pass_on()
    scatter.finish()
    gather.finish()


def turn_kernel(
    left0, left1, right0, right1, middle, gain, cot, normed_far, grad_middle_out, gain_out, grads_out, block_out, *scratch
):
    buffers, (normed, load) = scratch[:SCATTER_BUFFERS], scratch[SCATTER_BUFFERS:]
    loaded = pltpu.make_async_copy(normed_far, normed, load.at[0])
    loaded.start()
    tokens, hidden = cot.shape[0], left0.shape[1]
    place = Place()
    place.greet()
    scatter = Scatter(place, pair_product([left0, left1], [right0, right1], tokens), *buffers)
    scatter.run_first()
    scatter.run_second()
    loaded.wait()

    def weight_grads(n, none):
        at = pl.ds(pl.multiple_of(n * 256, 256), 256)
        for k, part in enumerate((left0, left1)):
            value = lax.dot_general(normed[:, at], part[...], (((0,), (0,)), ((), ())), preferred_element_type=F32)
            grads_out[at, k * hidden : (k + 1) * hidden] = value.astype(BF16)
        return none

    lax.fori_loop(0, normed.shape[1] // 256, weight_grads, 0)
    gain_out[...] = jnp.zeros_like(gain_out)

    def body(at):
        values = middle[at, :]
        grad = scatter.rows(at)
        scale = rms(values)
        weighted = grad * gain[...]
        inner = jnp.mean(values * weighted, axis=-1, keepdims=True)
        total = cot[at, :].astype(F32) + scale * weighted - values * (scale * scale * scale * inner)
        grad_middle_out[at, :] = total
        block_out[at, :] = total.astype(BF16)
        term = grad * values * scale
        gain_out[...] += term[0:8] + term[8:16]

    for part in (0, 1):
        scatter.run_third(part)
        for_slices(part * tokens // 2, (part + 1) * tokens // 2, body)
    scatter.finish()


def spread_kernel(block, w_out, mixed, mixed_out, out_grad, gathered, send, recv, chunk_ref, total, load):
    tokens = block.shape[0]
    place = Place()
    place.greet()
    gather = Gather(place, block, gathered, send, recv)
    gather.begin_whole()
    total[...] = jnp.zeros_like(total)

    def fetch(slot, chunk):
        at = pl.ds(pl.multiple_of(chunk * tokens, tokens), tokens)
        copy = pltpu.make_async_copy(gathered.at[at], chunk_ref.at[slot], load.at[slot])
        copy.start()
        return copy, slot, chunk

    def use(fetched):
        copy, slot, chunk = fetched
        copy.wait()
        use_chunk(chunk_ref.at[slot], chunk)

    def use_chunk(values, chunk):
        at = pl.ds(pl.multiple_of(chunk * tokens, tokens), tokens)
        mixed_out[at, :] = lax.dot_general(values[...], w_out[...], (((1,), (1,)), ((), ())), preferred_element_type=F32)
        part = mixed[at, :]

        def rows(n, none):
            columns = pl.ds(pl.multiple_of(n * 256, 256), 256)
            turned = (((0,), (0,)), ((), ()))
            total[columns, :] += lax.dot_general(values[:, columns], part, turned, preferred_element_type=F32)
            return none

        lax.fori_loop(0, values.shape[1] // 256, rows, 0)

    use_chunk(block, place.chunk(0, 0, 0))
    gather.pass_first()
    gather.finish_core()
    ahead = fetch(0, place.chunk(0, 0, 1))
    use(ahead)
    gather.pass_second()
    ahead = fetch(0, place.chunk(0, 1, 0))
    after = fetch(1, place.chunk(1, 0, 0))
    use(ahead)
    gather.finish_near()
    ahead = fetch(0, place.chunk(0, 1, 1))
    use(after)
    gather.pass_third()
    after = fetch(1, place.chunk(1, 0, 1))
    use(ahead)
    ahead = fetch(0, place.chunk(1, 1, 0))
    use(after)
    gather.finish_far()
    after = fetch(1, place.chunk(1, 1, 1))
    use(ahead)
    use(after)
    out_grad[...] = total[...].astype(BF16)
    gather.finish_sends()


class Owners:
    def __init__(self, place, reduced, out, send, recv):
        self.place, self.reduced, self.out, self.send, self.recv = place, reduced, out, send, recv
        self.own = place.chunk(0, 0, 0)

    def copy(self, number, offset, slot):
        return pltpu.make_async_remote_copy(
            src_ref=self.reduced.at[self.place.chunk(*offset)],
            dst_ref=self.out.at[slot],
            send_sem=self.send.at[number],
            recv_sem=self.recv.at[number],
            device_id=self.place.peer(*offset),
            device_id_type=MESH,
        )

    def begin(self):
        self.keep = pltpu.make_async_copy(self.reduced.at[self.own], self.out.at[self.own], self.send.at[7])
        self.keep.start()
        self.moved = [self.copy(number, offset, self.own) for number, offset in enumerate(OTHERS)]
        for copy in self.moved:
            copy.start()

    def finish(self):
        for number, offset in enumerate(OTHERS):
            self.copy(number, offset, self.place.chunk(*offset)).wait_recv()
        for copy in self.moved:
            copy.wait_send()
        self.keep.wait()


OWNERS_SCRATCH = [pltpu.SemaphoreType.DMA((8,))] * 2
BEYOND = [offset for offset in OTHERS if sum(offset) > 1]


class GateSums:
    def __init__(self, place, count, pieces, rows_recv, gates_all, send, recv):
        self.place, self.count, self.pieces = place, count, pieces
        self.rows_recv, self.gates_all, self.send, self.recv = rows_recv, gates_all, send, recv
        self.me = lax.axis_index("t")
        self.rank = place.g * 2 + place.c
        self.near = [offset for offset in OTHERS if not offset[0]]
        self.moved = []

    def copy(self, number, source, target, peer):
        return pltpu.make_async_remote_copy(
            src_ref=source,
            dst_ref=target,
            send_sem=self.send.at[number],
            recv_sem=self.recv.at[number],
            device_id=peer,
            device_id_type=MESH,
        )

    def begin(self):
        for number, offset in enumerate(self.near):
            other = lax.rem(self.place.chunk(*offset), 4)
            self.moved.append(self.copy(number, self.pieces.at[other], self.rows_recv.at[self.rank], self.place.peer(*offset)))
            self.moved[-1].start()
        self.rows_recv[self.rank] = self.pieces[self.rank]

    def pass_on(self):
        for number, offset in enumerate(self.near):
            other = lax.rem(self.place.chunk(*offset), 4)
            self.copy(number, self.pieces.at[other], self.rows_recv.at[other], self.place.peer(*offset)).wait_recv()
        for step in range(1, self.count):
            to = lax.rem(self.me + step, self.count)
            self.moved.append(self.copy(2 + step, self.rows_recv.at[to], self.gates_all.at[self.me], {"t": to}))
            self.moved[-1].start()
        self.gates_all[self.me] = self.rows_recv[self.me]

    def finish(self, out):
        for step in range(1, self.count):
            other = lax.rem(self.me + self.count - step, self.count)
            self.copy(2 + step, self.rows_recv.at[other], self.gates_all.at[other], {"t": other}).wait_recv()
        total = self.gates_all[0].astype(F32)
        for z in range(1, self.count):
            total = total + self.gates_all[z].astype(F32)
        out[...] = total
        for copy in self.moved:
            copy.wait_send()


def sum_everywhere(place, count, values, inbox, plane_sum, plane_box, send, recv):
    me = lax.axis_index("t")
    own = place.chunk(0, 0, 0)
    moved = []

    def copy(number, source, target, peer):
        return pltpu.make_async_remote_copy(
            src_ref=source,
            dst_ref=target,
            send_sem=send.at[number],
            recv_sem=recv.at[number],
            device_id=peer,
            device_id_type=MESH,
        )

    for number, offset in enumerate(OTHERS):
        moved.append(copy(number, values, inbox.at[own], place.peer(*offset)))
        moved[-1].start()
    inbox[own] = values[...]
    for number, offset in enumerate(OTHERS):
        copy(number, values, inbox.at[place.chunk(*offset)], place.peer(*offset)).wait_recv()
    total = inbox[0]
    for n in range(1, 8):
        total = total + inbox[n]
    plane_sum[...] = total
    for step in range(1, count):
        moved.append(copy(6 + step, plane_sum, plane_box.at[me], {"t": lax.rem(me + step, count)}))
        moved[-1].start()
    plane_box[me] = total
    for step in range(1, count):
        other = lax.rem(me + count - step, count)
        copy(6 + step, plane_sum, plane_box.at[other], {"t": other}).wait_recv()
    total = plane_box[0]
    for z in range(1, count):
        total = total + plane_box[z]
    for sent in moved:
        sent.wait_send()
    return total


def final_kernel(
    count, with_gates, left, right, own_in, gain, mlp_gains, pieces, grad_middle, reduced,
    grad_out, gains_out, gates_out, owned,
    gain_sum, values, inbox, plane_sum, plane_box, sum_send, sum_recv, rows_recv, gates_all, gates_send, gates_recv,
    own_send, own_recv, *buffers,
):
    tokens, width = own_in.shape
    place = Place()
    me = lax.axis_index("t")
    place.greet([place.peer(*offset) for offset in BEYOND] + [{"t": lax.rem(me + step, count)} for step in range(1, count)])
    scatter = Scatter(place, pair_product([left], [right], tokens), *buffers)
    owners = Owners(place, reduced, owned, own_send, own_recv)
    gates = GateSums(place, count, pieces, rows_recv, gates_all, gates_send, gates_recv)
    scatter.run_first()
    if with_gates:
        gates.begin()
    owners.begin()
    scatter.run_second()
    if with_gates:
        gates.pass_on()
    scatter.run_third(0)
    scatter.run_third(1)
    gain_sum[...] = jnp.zeros_like(gain_sum)

    def body(at):
        x = own_in[at, :].astype(F32)
        grad = scatter.rows(at)
        scale = rms(x)
        weighted = grad * gain[...]
        inner = jnp.mean(x * weighted, axis=-1, keepdims=True)
        grad_out[at, :] = grad_middle[at, :] + scale * weighted - x * (scale * scale * scale * inner)
        term = grad * x * scale
        gain_sum[...] += term[0:8] + term[8:16]

    for_slices(0, tokens, body)
    lines = width // LANES
    for base, row in ((0, jnp.sum(mlp_gains[...], axis=0, keepdims=True)), (lines, jnp.sum(gain_sum[...], axis=0, keepdims=True))):
        for n in range(lines):
            values[base + n : base + n + 1, :] = row[:, n * LANES : (n + 1) * LANES]
    gains_out[...] = sum_everywhere(place, count, values, inbox, plane_sum, plane_box, sum_send, sum_recv)
    if with_gates:
        gates.finish(gates_out)
    else:
        gates_out[...] = jnp.zeros_like(gates_out)
    owners.finish()
    scatter.finish()


def final_step(planes, with_gates, left, right, own_in, gain, mlp_gains, pieces, grad_middle, reduced):
    tokens, width = own_in.shape
    block = pieces.shape[1:] if with_gates else (16, LANES)
    slots = planes if with_gates else 1
    sums = (2 * width // LANES, LANES)
    return pl.pallas_call(
        functools.partial(final_kernel, planes, with_gates),
        name="final_step",
        out_shape=(
            jax.ShapeDtypeStruct((tokens, width), F32),
            jax.ShapeDtypeStruct(sums, F32),
            jax.ShapeDtypeStruct(block, F32),
            jax.ShapeDtypeStruct(reduced.shape, reduced.dtype),
        ),
        in_specs=[*whole(7), ANYWHERE],
        out_specs=(*whole(3), ANYWHERE),
        scratch_shapes=[
            pltpu.VMEM((8, width), F32),
            pltpu.VMEM(sums, F32),
            pltpu.VMEM((8, *sums), F32),
            pltpu.VMEM(sums, F32),
            pltpu.VMEM((planes, *sums), F32),
            pltpu.SemaphoreType.DMA((planes + 6,)),
            pltpu.SemaphoreType.DMA((planes + 6,)),
            pltpu.VMEM((slots, *block), BF16),
            pltpu.VMEM((slots, *block), BF16),
            pltpu.SemaphoreType.DMA((planes + 2,)),
            pltpu.SemaphoreType.DMA((planes + 2,)),
            *OWNERS_SCRATCH,
            *Scatter.scratch(tokens, width),
        ],
        compiler_params=mixer_params(7),
    )(left, right, own_in, gain[None], mlp_gains, pieces, grad_middle, reduced)


def owners_kernel(reduced0, reduced1, out0, out1, send0, recv0, send1, recv1):
    place = Place()
    place.greet([place.peer(*offset) for offset in BEYOND])
    owners = [Owners(place, reduced0, out0, send0, recv0), Owners(place, reduced1, out1, send1, recv1)]
    for part in owners:
        part.begin()
    for part in owners:
        part.finish()


def owners_step(reduced):
    return pl.pallas_call(
        owners_kernel,
        name="owners_step",
        out_shape=tuple(jax.ShapeDtypeStruct(part.shape, part.dtype) for part in reduced),
        in_specs=[ANYWHERE] * 2,
        out_specs=(ANYWHERE,) * 2,
        scratch_shapes=[*OWNERS_SCRATCH, *OWNERS_SCRATCH],
        compiler_params=mixer_params(8),
    )(*reduced)


def place_kernel(planes, hidden, outs, *refs):
    given, results = refs[: -len(outs)], refs[-len(outs) :]
    for count, sources, out in zip(outs, given, results):
        piece = sources.shape[2] // (count * (planes if hidden else 1))
        for k in range(count):
            if hidden:
                groups = [
                    ((t * 2 + i) * 4 * piece, [(i * 4 + r, (k * planes + t) * piece) for r in range(4)])
                    for t in range(planes)
                    for i in range(2)
                ]
            else:
                groups = [(r * 2 * piece, [(i * 4 + r, k * piece) for i in range(2)]) for r in range(4)]
            for start, parts in groups:
                row = jnp.concatenate([sources[p, :, at : at + piece].astype(F32) for p, at in parts], axis=1)
                if count > 1:
                    out[:, k, start : start + row.shape[1]] = row
                else:
                    out[:, start : start + row.shape[1]] = row


def place_columns(planes, hidden, outs, *owned):
    members, own_rows, columns = owned[0].shape
    total = columns * members // outs[0]
    shapes = [(own_rows, count, total) if count > 1 else (own_rows, total) for count in outs]
    return pl.pallas_call(
        functools.partial(place_kernel, planes, hidden, outs),
        name="place_columns",
        out_shape=tuple(jax.ShapeDtypeStruct(shape, F32) for shape in shapes),
        in_specs=whole(len(owned)),
        out_specs=tuple(whole(len(outs))),
        compiler_params=pltpu.CompilerParams(vmem_limit_bytes=60 * 1024 * 1024),
    )(*owned)


def first_gather(planes, normed, ids):
    tokens, width = normed.shape
    every = (8, *ids.shape)
    return pl.pallas_call(
        functools.partial(first_gather_kernel, planes),
        name="first_gather",
        out_shape=(jax.ShapeDtypeStruct((8 * tokens, width), BF16), *[jax.ShapeDtypeStruct(every, F32)] * 3),
        in_specs=[ANYWHERE, *whole(1)],
        out_specs=(ANYWHERE, *whole(3)),
        scratch_shapes=[pltpu.VMEM(every, F32)] * 3 + GATHER_SCRATCH + [pltpu.SemaphoreType.DMA((9,))] * 2,
        compiler_params=mixer_params(3),
    )(normed, ids)


def middle_step(mixed, w_out, own_in, gain):
    tokens, width = own_in.shape
    return pl.pallas_call(
        middle_kernel,
        name="middle_step",
        out_shape=(jax.ShapeDtypeStruct((tokens, width), F32), jax.ShapeDtypeStruct((8 * tokens, width), BF16)),
        in_specs=whole(4),
        out_specs=(pl.BlockSpec(memory_space=pltpu.VMEM), ANYWHERE),
        scratch_shapes=Scatter.scratch(tokens, width) + [pltpu.VMEM((tokens, width), BF16)] + GATHER_SCRATCH,
        compiler_params=mixer_params(4),
    )(mixed, w_out, own_in, gain[None])


def turn_step(left0, left1, right0, right1, middle, gain, cot, normed):
    tokens, width = cot.shape
    return pl.pallas_call(
        turn_kernel,
        name="turn_step",
        out_shape=(
            jax.ShapeDtypeStruct((tokens, width), F32),
            jax.ShapeDtypeStruct((8, width), F32),
            jax.ShapeDtypeStruct((width, 2 * left1.shape[1]), BF16),
            jax.ShapeDtypeStruct((tokens, width), BF16),
        ),
        in_specs=[*whole(7), ANYWHERE],
        out_specs=tuple(whole(4)),
        scratch_shapes=Scatter.scratch(tokens, width)
        + [pltpu.VMEM(normed.shape, BF16), pltpu.SemaphoreType.DMA((1,))],
        compiler_params=mixer_params(5),
    )(left0, left1, right0, right1, middle, gain[None], cot, normed)


def spread_step(block, w_out, mixed):
    tokens, width = block.shape
    return pl.pallas_call(
        spread_kernel,
        name="turn_spread",
        out_shape=(
            jax.ShapeDtypeStruct((8 * tokens, w_out.shape[0]), F32),
            jax.ShapeDtypeStruct((width, w_out.shape[0]), BF16),
            jax.ShapeDtypeStruct((8 * tokens, width), BF16),
        ),
        in_specs=whole(3),
        out_specs=(*whole(2), ANYWHERE),
        scratch_shapes=GATHER_SCRATCH
        + [
            pltpu.VMEM((2, tokens, width), BF16),
            pltpu.VMEM((width, w_out.shape[0]), F32),
            pltpu.SemaphoreType.DMA((2,)),
        ],
        compiler_params=mixer_params(10),
    )(block, w_out, mixed)


class Swap:
    def __init__(self, quarters, out, send, recv):
        self.quarters, self.out, self.send, self.recv = quarters, out, send, recv
        self.groups = quarters.shape[0]
        self.me = lax.axis_index("g") * 2 + lax.axis_index("c")

    def copy(self, step, other, slot):
        return pltpu.make_async_remote_copy(
            src_ref=self.quarters.at[other],
            dst_ref=self.out.at[:, slot],
            send_sem=self.send.at[step],
            recv_sem=self.recv.at[step],
            device_id={"g": other // 2, "c": other % 2},
            device_id_type=MESH,
        )

    def peers(self):
        others = [lax.rem(self.me + step, self.groups) for step in range(1, self.groups)]
        return [{"g": other // 2, "c": other % 2} for other in others]

    def begin(self):
        self.keep = pltpu.make_async_copy(self.quarters.at[self.me], self.out.at[:, self.me], self.send.at[0])
        self.keep.start()
        self.moved = []
        for step in range(1, self.groups):
            self.moved.append(self.copy(step, lax.rem(self.me + step, self.groups), self.me))
            self.moved[-1].start()

    def finish(self):
        for step in range(1, self.groups):
            other = lax.rem(self.me + self.groups - step, self.groups)
            self.copy(step, other, other).wait_recv()
        for copy in self.moved:
            copy.wait_send()
        self.keep.wait()


def swap_scratch(groups):
    return [pltpu.SemaphoreType.DMA((groups,)), pltpu.SemaphoreType.DMA((groups,))]


def swap_kernel(quarters, out, send, recv):
    move = Swap(quarters, out, send, recv)
    barrier = pltpu.get_barrier_semaphore()
    for peer in move.peers():
        pl.semaphore_signal(barrier, inc=1, device_id=peer, device_id_type=MESH)
    pl.semaphore_wait(barrier, move.groups - 1)
    move.begin()
    move.finish()


def swap(quarters):
    groups, kinds, part, width = quarters.shape
    return pl.pallas_call(
        swap_kernel,
        name="swap",
        out_shape=jax.ShapeDtypeStruct((kinds, groups, part, width), quarters.dtype),
        in_specs=[ANYWHERE],
        out_specs=ANYWHERE,
        scratch_shapes=swap_scratch(groups),
        compiler_params=mixer_params(6),
    )(quarters)


def rms(values):
    return lax.rsqrt(jnp.mean(values * values, axis=-1, keepdims=True) + EPS)


def nt(left, right, out):
    return lax.dot_general(left, right, (((1,), (1,)), ((), ())), preferred_element_type=F32).astype(out)


def tn(left, right, out):
    return lax.dot_general(left, right, (((0,), (0,)), ((), ())), preferred_element_type=F32).astype(out)


def nn(left, right, out):
    return jnp.dot(left, right, preferred_element_type=F32).astype(out)


def per_device(
    inputs, segment_ids, mix_gain, in_weight, conv_weight, conv_bias, gate_weight, gate_bias, decay_param, out_weight,
    mlp_gain, mlp_in, down_weight, cotangent,
):
    planes = lax.axis_size("t")
    rows_here, seg, width = inputs.shape
    row_groups = lax.axis_size("g") * lax.axis_size("c")
    own_tokens = rows_here * seg
    recur_width = conv_weight.shape[1]
    block_width = gate_weight.shape[0]
    members = 2 * row_groups
    channels = recur_width // members
    t, i = lax.axis_index("t"), lax.axis_index("i")
    r = lax.axis_index("g") * lax.axis_size("c") + lax.axis_index("c")
    member = 2 * r + i
    first = member * channels
    own_rows = width // (planes * members)

    own_in = inputs.reshape(own_tokens, width)
    flat_in = own_in.astype(F32)
    scale_in = rms(flat_in)
    cot_own = cotangent.reshape(own_tokens, width)
    own_ids = jnp.pad((segment_ids + 1).astype(F32), ((0, 8 - rows_here), (0, 0)))

    normed, *ids = first_gather(planes, (flat_in * scale_in * mix_gain).astype(BF16), own_ids)
    late_r, ids[0] = lax.optimization_barrier((r, ids[0]))

    direct = planes == row_groups
    in_own = in_weight.transpose(1, 2, 0)
    out_own = out_weight.T[None]
    part = channels // row_groups if direct else 0

    def quarter(weight, part, rank=r):
        return lax.dynamic_slice_in_dim(weight, rank * part, part, weight.ndim - 1)

    def spread_units(weight):
        return lax.all_gather(weight, "t", axis=0, tiled=False)

    def whole_units(weight):
        every = lax.all_gather(weight, ("t", "i"), axis=1, tiled=True)
        return lax.dynamic_slice_in_dim(every, first, channels, 1)

    if direct:
        in_w = swap(spread_units(quarter(in_weight, part).transpose(1, 2, 0)))
        out_quarters = spread_units(quarter(out_weight, part).T[None])
    else:
        in_w = whole_units(in_own)
        out_quarters = jnp.zeros((row_groups, 1, 16, width), BF16)
    in_w = in_w.reshape(2 * channels, width)
    hidden_part = mlp_in.shape[2] // row_groups
    gated = quarter(mlp_in, hidden_part, late_r).transpose(1, 2, 0)
    w_left, w_right, w_down = [
        spread_units(part).reshape(-1, width)
        for part in (gated[0], gated[1], quarter(down_weight, hidden_part, late_r).T)
    ]

    def own(values):
        return lax.dynamic_slice_in_dim(values, first, channels, values.ndim - 1)

    vec = own(
        jnp.concatenate(
            [
                conv_weight,
                conv_bias[None],
                gate_bias,
                8.0 * jax.nn.softplus(-decay_param)[None],
                8.0 * jax.nn.sigmoid(-decay_param)[None],
                jnp.zeros((7, recur_width), F32),
            ]
        )
    )
    gate_blocks = own(gate_weight).transpose(1, 0, 2)
    blocks = channels // block_width

    branches = nt(normed, in_w, F32)
    conv_low, decay, states, mixed, halo, cin, mask, cot, w_out = mixer_forward(
        planes, seg, rows_here, branches, ids, gate_blocks, vec, cot_own, out_quarters
    )
    w_out = (w_out if direct else whole_units(out_own)).reshape(channels, width)
    middle, normed_two = middle_step(mixed, w_out, own_in, mlp_gain)
    left = nt(normed_two, w_left, F32)
    right = nt(normed_two, w_right, F32)
    act, slope = gelu_parts(left)
    hidden = (act * right).astype(BF16)

    def over_planes(grad):
        return lax.psum_scatter(grad, "t", scatter_dimension=0, tiled=True)

    grad_down = tn(cot, hidden, BF16)
    grad_down, hidden, w_down = lax.optimization_barrier((grad_down, hidden, w_down))
    grad_down = over_planes(grad_down)
    grad_hidden = nt(cot, w_down, F32)
    grad_left = (grad_hidden * right * slope).astype(BF16)
    grad_right = (grad_hidden * act).astype(BF16)
    grad_middle, grad_mlp_gain, grad_mlp_in, grad_mid_own = turn_step(
        grad_left, grad_right, w_left, w_right, middle, mlp_gain, cot_own, normed_two
    )
    grad_down, grad_mid_own = lax.optimization_barrier((grad_down, grad_mid_own))
    grad_mlp_in = over_planes(grad_mlp_in)
    grad_mixed, grad_out, _ = spread_step(grad_mid_own, w_out, mixed)
    grad_out = over_planes(grad_out)

    def by_owner(grad):
        return grad.reshape(members, own_rows, -1)

    grad_branches, gw0, gw1, small, pieces, outputs, owned_down = mixer_backward(
        planes, seg, grad_mixed, branches, states, decay, conv_low, mask, halo, cin, gate_blocks, vec, hidden, w_down, middle,
        by_owner(grad_down),
    )
    grad_in = tn(normed, grad_branches, BF16)
    grad_in, grad_branches = lax.optimization_barrier((grad_in, grad_branches))
    grad_in = over_planes(grad_in)
    outputs = outputs.reshape(inputs.shape)

    grad_inputs, gains, gate_grads, owned_mlp_in = final_step(
        planes, direct, grad_branches, in_w, own_in, mix_gain, grad_mlp_gain, pieces, grad_middle,
        by_owner(grad_mlp_in),
    )
    grad_inputs = grad_inputs.reshape(inputs.shape)
    index = ((t * 2 + i) * row_groups + r) * own_rows
    gains = lax.dynamic_slice_in_dim(gains.reshape(2, width), index, own_rows, 1)


    owned_in, owned_out = owners_step([by_owner(grad_in), by_owner(grad_out)])

    def columns(hidden, outs, *owned):
        if direct:
            return place_columns(planes, hidden, outs, *owned)
        owned = jnp.concatenate(owned, axis=2)
        owned = owned.reshape(2, row_groups, own_rows, sum(outs), planes if hidden else 1, -1).astype(F32)
        order = (2, 3, 4, 0, 1, 5) if hidden else (2, 3, 1, 0, 4, 5)
        owned = owned.transpose(order).reshape(own_rows, sum(outs), -1)
        return (owned[:, :2], owned[:, 2])

    grad_in_weight, grad_out_weight = columns(False, (2, 1), owned_in, owned_out)
    grad_mlp_in, grad_down_weight = columns(True, (2, 1), owned_mlp_in, owned_down)
    if direct:
        gate_grads = gate_grads[:, :part]
    else:
        column_block = lax.broadcasted_iota(jnp.int32, (block_width, channels), 1) // block_width

        def diagonal(gw):
            return sum(
                jnp.where(column_block == n, gw[n * block_width : (n + 1) * block_width], 0.0) for n in range(blocks)
            )

        gate_grads = jnp.concatenate([diagonal(gw0), diagonal(gw1), small], axis=0)
        placed = jnp.zeros((gate_grads.shape[0], recur_width), F32)
        placed = lax.dynamic_update_slice_in_dim(placed, gate_grads, first, 1)
        gate_grads = lax.psum_scatter(placed, EVERY, scatter_dimension=1, tiled=True)
    grad_gate_weight = jnp.stack([gate_grads[:block_width], gate_grads[block_width : 2 * block_width]], axis=1)
    small = gate_grads[2 * block_width : 2 * block_width + 8]
    return (
        outputs,
        grad_inputs,
        gains[1],
        grad_in_weight,
        small[0:4],
        small[4],
        grad_gate_weight,
        small[5:7],
        small[7],
        grad_out_weight,
        gains[0],
        grad_mlp_in,
        grad_down_weight,
    )


def solution(mesh):
    seq, rows = mesh.shape["seq"], mesh.shape["rows"]
    grid = Mesh(mesh.devices.reshape(seq // 2, 2, rows // 2, 2), EVERY)
    row_axes, seq_axes = ("g", "c"), ("t", "i")
    tokens = P(row_axes, seq_axes, None)
    return jax.shard_map(
        per_device,
        mesh=grid,
        in_specs=(
            tokens,
            P(row_axes, seq_axes),
            P(),
            P(None, None, seq_axes),
            P(),
            P(),
            P(),
            P(),
            P(),
            P(None, seq_axes),
            P(),
            P(None, None, seq_axes),
            P(None, seq_axes),
            tokens,
        ),
        out_specs=(
            tokens,
            tokens,
            P(EVERY),
            P(EVERY, None, None),
            P(None, EVERY),
            P(EVERY),
            P(None, None, EVERY),
            P(None, EVERY),
            P(EVERY),
            P(EVERY, None),
            P(EVERY),
            P(EVERY, None, None),
            P(EVERY, None),
        ),
        check_vma=False,
    )
```

```python
import functools

import jax
import jax.numpy as jnp
from jax import lax
from jax.experimental import pallas as pl
from jax.experimental.pallas import tpu as pltpu
from jax.sharding import Mesh
from jax.sharding import PartitionSpec as P

EPS = 1e-06
MESH = pl.DeviceIdType.MESH
PLANE = ("i", "g", "c")
EVERY = ("t", "i", "g", "c")
F32 = jnp.float32
BF16 = jnp.bfloat16
GELU_A = 0.7978845608028654
GELU_B = 0.044715
HALO = 8
LANES = 128
SLICE = 16
ANYWHERE = pl.BlockSpec(memory_space=pl.ANY)
GATHER_SCRATCH = [pltpu.SemaphoreType.DMA((14,))] * 2


def gelu_parts(x):
    square = x * x
    th = jnp.tanh(GELU_A * x * (1.0 + GELU_B * square))
    half = 0.5 * (1.0 + th)
    slope = half + 0.5 * x * (1.0 - th * th) * (GELU_A * (1.0 + 3.0 * GELU_B * square))
    return x * half, slope


def one_minus_exp(y, power):
    series = 1.0 + y * (-1.0 / 2 + y * (1.0 / 6 + y * (-1.0 / 24 + y * (1.0 / 120 + y * (-1.0 / 720 + y * (1.0 / 5040))))))
    return jnp.where(y < 0.35, y * series, 1.0 - power)


def sigmoid(x):
    return 1.0 / (1.0 + jnp.exp(-x))


def gate_values(conv_low, wg0, wg1, vec):
    logits0 = jnp.dot(conv_low, wg0, preferred_element_type=F32) + vec[5:6]
    logits1 = jnp.dot(conv_low, wg1, preferred_element_type=F32) + vec[6:7]
    recur_gate = sigmoid(logits0)
    input_gate = sigmoid(logits1)
    log_decay = -vec[7:8] * recur_gate
    return recur_gate, input_gate, log_decay


def spread_blocks(gates, out):
    size, width = gates.shape[1], gates.shape[2]
    column = lax.broadcasted_iota(jnp.int32, (size, width), 1) // size
    for k in range(2):
        block = gates[k].astype(F32)
        for n in range(width // size):
            out[k, n * size : (n + 1) * size, :] = jnp.where(column == n, block, 0.0).astype(BF16)


def put_tiles(ref, at, values):
    tiles, lanes = ref.shape[0], ref.shape[2]
    short = tiles * lanes - values.shape[1]
    if short:
        values = jnp.concatenate([values, jnp.zeros((values.shape[0], short), values.dtype)], axis=1)
    for j in range(tiles):
        ref[j, at, :] = values[:, j * lanes : (j + 1) * lanes]


def get_tiles(ref, at, width):
    joined = jnp.concatenate([ref[j, at, :] for j in range(ref.shape[0])], axis=1)
    return joined[:, :width]


def join_tiles(parts, width):
    return jnp.concatenate(parts, axis=1)[:, :width]


def exchange_copy(step, send, target, other, send_sem, recv_sem):
    return pltpu.make_async_remote_copy(
        src_ref=send,
        dst_ref=target,
        send_sem=send_sem.at[step],
        recv_sem=recv_sem.at[step],
        device_id={"t": other},
        device_id_type=MESH,
    )


def exchange_start(count, me, send, slots, send_sem, recv_sem):
    for step in range(1, count):
        exchange_copy(step, send, slots.at[me], lax.rem(me + step, count), send_sem, recv_sem).start()


def exchange_wait(count, me, send, slots, send_sem, recv_sem):
    for step in range(1, count):
        other = lax.rem(me + count - step, count)
        exchange_copy(step, send, slots.at[other], other, send_sem, recv_sem).wait()


def mixer_forward_kernel(
    count, seg, rows_here, branches_far, ids, ids_before, ids_after, gate_blocks, vec_ref, cot, quarters,
    conv_out, decay_out, states_out, mixed_out, halo_out, cin_out, mask, cot_out, swapped,
    drive, h_ref, a_ref, ext, halo_send, halo_recv, summary, slots, send_sem, recv_sem, halo_sems,
    gather_send, gather_recv, swap_send, swap_recv, branches, wg, load,
):
    place = Place()
    me = lax.axis_index("t")
    loaded = pltpu.make_async_copy(branches_far, branches, load.at[0])
    loaded.start()
    place.greet([place.peer(0, 1, 1)] + [{"t": lax.rem(me + step, count)} for step in range(1, count)])
    gather = Gather(place, cot, cot_out, gather_send, gather_recv)
    move = Swap(quarters, swapped, swap_send, swap_recv)
    gather.begin_whole()
    move.begin()
    spread_blocks(gate_blocks, wg)
    rows = 8
    width = branches.shape[1] // 2
    loaded.wait()

    def recur_at(at):
        return branches[at, width:].astype(BF16).astype(F32)

    for r in range(rows):
        halo_send[r * HALO : (r + 1) * HALO, :] = recur_at(pl.ds((rows + r + 1) * seg - HALO, HALO))
    halo_copy = pltpu.make_async_remote_copy(
        src_ref=halo_send,
        dst_ref=halo_recv,
        send_sem=halo_sems.at[0],
        recv_sem=halo_sems.at[1],
        device_id={"t": lax.rem(me + 1, count)},
        device_id_type=MESH,
    )
    halo_copy.start()
    for r in range(rows):
        halo_out[(rows + r) * HALO : (rows + r + 1) * HALO, :] = recur_at(pl.ds((r + 1) * seg - HALO, HALO))
    vec = vec_ref[...]

    def ids_of(ref, s):
        chunk = s // rows_here
        return ref[chunk, s % rows_here : s % rows_here + 1, :]

    nothing = jnp.zeros((1, LANES), F32)
    for s in range(2 * rows):
        here = ids_of(ids, s)
        back = ids_of(ids, s - rows) if s >= rows else jnp.where(me > 0, ids_of(ids_before, s + rows), nothing)
        ahead = ids_of(ids, s + rows) if s < rows else jnp.where(me < count - 1, ids_of(ids_after, s - rows), nothing)
        lines = [jnp.concatenate([back[:, seg - k :], here[:, : seg - k]], axis=1) for k in (1, 2, 3)]
        lines += [jnp.concatenate([here[:, k:], ahead[:, :k]], axis=1) for k in (1, 2, 3)]
        lines = [jnp.where(line == here, 1.0, 0.0) for line in lines] + [nothing] * 2
        mask[s * seg : (s + 1) * seg, :] = jnp.concatenate(lines, axis=0).T

    def local(s, none):
        at = pl.ds(pl.multiple_of(s * seg, seg), seg)
        x = recur_at(at)
        ext[0:HALO, :] = halo_out[pl.ds(pl.multiple_of(s * HALO, HALO), HALO), :]
        ext[HALO : HALO + seg, :] = x
        m = mask[at, :]
        conv = vec[4:5] + vec[0:1] * x
        for k in range(1, 4):
            conv = conv + vec[k : k + 1] * ext[HALO - k : HALO - k + seg, :] * m[:, k - 1 : k]
        conv_low = conv.astype(BF16)
        conv_out[at, :] = conv_low
        recur_gate, input_gate, log_decay = gate_values(conv_low, wg[0], wg[1], vec)
        keep = m[:, 0:1]
        kept = jnp.exp(log_decay)
        put_tiles(decay_out, at, kept * keep)
        scale = (1.0 - keep) + keep * jnp.sqrt(one_minus_exp(-2.0 * log_decay, kept * kept))
        put_tiles(drive, at, scale * input_gate * conv_low.astype(F32))
        return none

    lax.fori_loop(rows, 2 * rows, local, 0)
    halo_copy.wait()
    for r in range(rows):
        halo_out[r * HALO : (r + 1) * HALO, :] = halo_recv[r * HALO : (r + 1) * HALO, :]
    gather.pass_first()
    lax.fori_loop(0, rows, local, 0)
    tiles, lanes = drive.shape[0], drive.shape[2]

    def scan(k, carried):
        at = pl.ds(k, 2 * rows, stride=seg)
        after = []
        for j in range(tiles):
            h, a = carried[j]
            d = decay_out[j, at, :]
            h = d * h + drive[j, at, :]
            a = a * d
            h_ref[j, at, :] = h
            a_ref[j, at, :] = a
            after.append((h, a))
        return tuple(after)

    start = (jnp.zeros((2 * rows, lanes), F32), jnp.ones((2 * rows, lanes), F32))
    last = lax.fori_loop(0, seg, scan, (start,) * tiles, unroll=4)
    last_h = join_tiles([part[0] for part in last], width)
    last_a = join_tiles([part[1] for part in last], width)
    summary[0:rows, :] = last_a[rows:] * last_a[:rows]
    summary[rows : 2 * rows, :] = last_a[rows:] * last_h[:rows] + last_h[rows:]
    exchange_start(count, me, summary, slots, send_sem, recv_sem)
    gather.pass_second()

    def activate(s, none):
        at = pl.ds(pl.multiple_of(s * seg, seg), seg)
        act, _ = gelu_parts(branches[at, :width])
        states_out[at, :] = act
        return none

    lax.fori_loop(0, 2 * rows, activate, 0)
    exchange_wait(count, me, summary, slots, send_sem, recv_sem)
    carry = jnp.zeros((rows, width), F32)
    for z in range(count - 1):
        carry = jnp.where(z < me, slots[z, 0:rows, :] * carry + slots[z, rows : 2 * rows, :], carry)
    cin_out[0:rows, :] = carry
    cin_out[rows : 2 * rows, :] = last_a[:rows] * carry + last_h[:rows]

    def finish(s, none):
        at = pl.ds(pl.multiple_of(s * seg, seg), seg)
        states = get_tiles(h_ref, at, width) + get_tiles(a_ref, at, width) * cin_out[pl.ds(s, 1), :]
        act = states_out[at, :]
        states_out[at, :] = states
        mixed_out[at, :] = (act * states.astype(BF16).astype(F32)).astype(BF16)
        return none

    lax.fori_loop(0, 2 * rows, finish, 0)
    gather.pass_third()
    gather.finish()
    move.finish()


def mixer_backward_kernel(
    count, seg, grad_mixed_far, branches_far, states_far, decay_far, conv_far, mask_far, halo, cin, gate_blocks, vec_ref,
    hidden, w_down, middle_far, reduced, grad_out, gw0_out, gw1_out, small_out, pieces_out, outputs, owned,
    tot, prod, ext, halo_send, halo_recv, summary, slots, uin, send_sem, recv_sem, halo_sems,
    grad_mixed, branches, states, decay, conv_low_ref, mask, middle, wg, load, own_send, own_recv, *buffers,
):
    place = Place()
    pairs = (
        (grad_mixed_far, grad_mixed),
        (branches_far, branches),
        (states_far, states),
        (decay_far, decay),
        (conv_far, conv_low_ref),
        (mask_far, mask),
        (middle_far, middle),
    )
    loads = [pltpu.make_async_copy(far, near, load.at[n]) for n, (far, near) in enumerate(pairs)]
    for part in loads:
        part.start()
    me = lax.axis_index("t")
    place.greet([place.peer(*offset) for offset in BEYOND] + [{"t": lax.rem(me + step, count)} for step in range(1, count)])
    scatter = Scatter(place, pair_product([hidden], [w_down], outputs.shape[0]), *buffers)
    owners = Owners(place, reduced, owned, own_send, own_recv)
    spread_blocks(gate_blocks, wg)
    scatter.run_first()
    owners.begin()
    for part in loads:
        part.wait()
    rows = 8
    width = branches.shape[1] // 2
    vec = vec_ref[...]

    def local(s, none):
        at = pl.ds(pl.multiple_of(s * seg, seg), seg)
        act, slope = gelu_parts(branches[at, :width])
        gm = grad_mixed[at, :].astype(F32)
        grad_out[at, :width] = (gm * states[at, :].astype(BF16).astype(F32) * slope).astype(BF16)
        put_tiles(tot, at, (gm * act).astype(BF16).astype(F32))
        return none

    lax.fori_loop(0, 2 * rows, local, 0)

    tiles, lanes = tot.shape[0], tot.shape[2]

    def scan(k, carried):
        at = pl.ds(seg - 1 - k, 2 * rows, stride=seg)
        after = []
        for j in range(tiles):
            u, p = carried[j]
            d = decay[j, at, :]
            total = tot[j, at, :] + u
            tot[j, at, :] = total
            prod[j, at, :] = p
            after.append((d * total, d * p))
        return tuple(after)

    start = (jnp.zeros((2 * rows, lanes), F32), jnp.ones((2 * rows, lanes), F32))
    last = lax.fori_loop(0, seg, scan, (start,) * tiles, unroll=4)
    u = join_tiles([part[0] for part in last], width)
    p = join_tiles([part[1] for part in last], width)
    summary[0:rows, :] = p[:rows] * p[rows:]
    summary[rows : 2 * rows, :] = p[:rows] * u[rows:] + u[:rows]
    exchange_start(count, me, summary, slots, send_sem, recv_sem)
    scatter.run_second()
    exchange_wait(count, me, summary, slots, send_sem, recv_sem)
    carry = jnp.zeros((rows, width), F32)
    for z in range(count - 1, 0, -1):
        carry = jnp.where(z > me, slots[z, 0:rows, :] * carry + slots[z, rows : 2 * rows, :], carry)
    uin[rows : 2 * rows, :] = carry
    uin[0:rows, :] = p[rows:] * carry + u[rows:]
    gw0_out[...] = jnp.zeros_like(gw0_out)
    gw1_out[...] = jnp.zeros_like(gw1_out)
    small_out[...] = jnp.zeros_like(small_out)

    def gates(s, none):
        at = pl.ds(pl.multiple_of(s * seg, seg), seg)
        total = get_tiles(tot, at, width) + get_tiles(prod, at, width) * uin[pl.ds(s, 1), :]
        ext[HALO - 1 : HALO, :] = cin[pl.ds(s, 1), :]
        ext[HALO : HALO + seg, :] = states[at, :]
        before = ext[HALO - 1 : HALO - 1 + seg, :]
        conv_low = conv_low_ref[at, :]
        conv_vals = conv_low.astype(F32)
        m = mask[at, :]
        keep = m[:, 0:1]
        recur_gate, input_gate, log_decay = gate_values(conv_low, wg[0], wg[1], vec)
        power = jnp.exp(2.0 * log_decay)
        gone = one_minus_exp(-2.0 * log_decay, power)
        inverse = lax.rsqrt(gone)
        root = gone * inverse
        scale = (1.0 - keep) + keep * root
        driven_in = total * conv_vals
        grad_log = total * before * get_tiles(decay, at, width) - driven_in * input_gate * keep * (power * inverse)
        grad0 = grad_log * log_decay * (1.0 - recur_gate)
        grad1 = driven_in * scale * input_gate * (1.0 - input_gate)
        low0 = grad0.astype(BF16)
        low1 = grad1.astype(BF16)
        inputs_of = (((1,), (1,)), ((), ()))
        grad_conv = (
            total * scale * input_gate
            + lax.dot_general(low0, wg[0], inputs_of, preferred_element_type=F32)
            + lax.dot_general(low1, wg[1], inputs_of, preferred_element_type=F32)
        )
        put_tiles(tot, at, grad_conv)
        turned = (((0,), (0,)), ((), ()))
        gw0_out[...] += lax.dot_general(conv_low, low0, turned, preferred_element_type=F32)
        gw1_out[...] += lax.dot_general(conv_low, low1, turned, preferred_element_type=F32)
        x = branches[at, width:].astype(BF16).astype(F32)
        ext[0:HALO, :] = halo[pl.ds(pl.multiple_of(s * HALO, HALO), HALO), :]
        ext[HALO : HALO + seg, :] = x

        def add(row, values):
            small_out[row : row + 1, :] += jnp.sum(values, axis=0, keepdims=True)

        add(0, grad_conv * x)
        for k in range(1, 4):
            add(k, grad_conv * ext[HALO - k : HALO - k + seg, :] * m[:, k - 1 : k])
        add(4, grad_conv)
        add(5, grad0)
        add(6, grad1)
        add(7, grad_log * recur_gate)
        return none

    lax.fori_loop(0, 2 * rows, gates, 0)
    small_out[7:8, :] = small_out[7:8, :] * vec[8:9]
    size, part = gate_blocks.shape[1], width // 4

    def padded(values):
        short = [values, jnp.zeros((values.shape[0], LANES - part), F32)]
        return jnp.concatenate(short, axis=1)

    for r in range(4):
        first = r * part // size * size
        at = slice(r * part, (r + 1) * part)
        for k, square in enumerate((gw0_out, gw1_out)):
            pieces_out[r, k * size : (k + 1) * size, :] = padded(square[first : first + size, at]).astype(BF16)
        rest = jnp.concatenate([padded(small_out[:, at]), jnp.zeros((8, LANES), F32)], axis=0)
        pieces_out[r, 2 * size :, :] = rest.astype(BF16)
    for r in range(rows):
        halo_send[r * HALO : (r + 1) * HALO, :] = get_tiles(tot, pl.ds(r * seg, HALO), width)
    halo_copy = pltpu.make_async_remote_copy(
        src_ref=halo_send,
        dst_ref=halo_recv,
        send_sem=halo_sems.at[0],
        recv_sem=halo_sems.at[1],
        device_id={"t": lax.rem(me + count - 1, count)},
        device_id_type=MESH,
    )
    halo_copy.start()

    def back(s, none):
        at = pl.ds(pl.multiple_of(s * seg, seg), seg)
        m = mask[at, :]
        grad_conv = get_tiles(tot, at, width)
        ext[0:seg, :] = grad_conv
        result = vec[0:1] * grad_conv

        @pl.when(s < rows)
        def _():
            ext[seg : seg + HALO, :] = get_tiles(tot, pl.ds(pl.multiple_of((s + rows) * seg, seg), HALO), width)

        @pl.when(s >= rows)
        def _():
            ext[seg : seg + HALO, :] = halo_recv[pl.ds(pl.multiple_of((s - rows) * HALO, HALO), HALO), :]

        for k in range(1, 4):
            result = result + vec[k : k + 1] * ext[k : k + seg, :] * m[:, 2 + k : 3 + k]
        grad_out[at, width:] = result.astype(BF16)
        return none

    lax.fori_loop(0, rows, back, 0)
    halo_copy.wait()
    lax.fori_loop(rows, 2 * rows, back, 0)
    scatter.run_third(0)
    scatter.run_third(1)

    def body(at):
        outputs[at, :] = (middle[at, :] + scatter.rows(at)).astype(BF16)

    for_slices(0, outputs.shape[0], body)
    scatter.finish()
    owners.finish()


def whole(count):
    return [pl.BlockSpec(memory_space=pltpu.VMEM)] * count


def mixer_params(number):
    return pltpu.CompilerParams(collective_id=number, has_side_effects=True, vmem_limit_bytes=60 * 1024 * 1024)


def mixer_forward(count, seg, rows_here, branches, ids, gate_blocks, vec, cot, quarters):
    n, width = branches.shape[0], branches.shape[1] // 2
    full = functools.partial(jax.ShapeDtypeStruct, (n, width))
    tiles = -(-width // LANES)
    tiled = jax.ShapeDtypeStruct((tiles, n, LANES), F32)
    groups, kinds, part, depth = quarters.shape
    return pl.pallas_call(
        functools.partial(mixer_forward_kernel, count, seg, rows_here),
        name="mixer_forward",
        out_shape=(
            full(BF16), tiled, full(F32), full(BF16),
            jax.ShapeDtypeStruct((16 * HALO, width), F32), jax.ShapeDtypeStruct((16, width), F32),
            jax.ShapeDtypeStruct((n, 8), F32),
            jax.ShapeDtypeStruct((8 * cot.shape[0], cot.shape[1]), BF16),
            jax.ShapeDtypeStruct((kinds, groups, part, depth), BF16),
        ),
        in_specs=[ANYWHERE, *whole(5), ANYWHERE, ANYWHERE],
        out_specs=(*whole(7), ANYWHERE, ANYWHERE),
        scratch_shapes=[
            pltpu.VMEM((tiles, n, LANES), F32),
            pltpu.VMEM((tiles, n, LANES), F32),
            pltpu.VMEM((tiles, n, LANES), F32),
            pltpu.VMEM((seg + HALO, width), F32),
            pltpu.VMEM((8 * HALO, width), F32),
            pltpu.VMEM((8 * HALO, width), F32),
            pltpu.VMEM((16, width), F32),
            pltpu.VMEM((count, 16, width), F32),
            pltpu.SemaphoreType.DMA((count,)),
            pltpu.SemaphoreType.DMA((count,)),
            pltpu.SemaphoreType.DMA((2,)),
            *GATHER_SCRATCH,
            *swap_scratch(groups),
            pltpu.VMEM(branches.shape, F32),
            pltpu.VMEM((2, width, width), BF16),
            pltpu.SemaphoreType.DMA((1,)),
        ],
        compiler_params=mixer_params(1),
    )(branches, *ids, gate_blocks, vec, cot, quarters)


def mixer_backward(count, seg, grad_mixed, branches, states, decay, conv_low, mask, halo, cin, gate_blocks, vec, hidden, w_down, middle, reduced):
    n, width = branches.shape[0], branches.shape[1] // 2
    tokens, depth = n // 8, w_down.shape[1]
    full = functools.partial(jax.ShapeDtypeStruct, (n, width))
    tiles = -(-width // LANES)
    tiled = jax.ShapeDtypeStruct((tiles, n, LANES), F32)
    return pl.pallas_call(
        functools.partial(mixer_backward_kernel, count, seg),
        name="mixer_backward",
        out_shape=(
            jax.ShapeDtypeStruct((n, 2 * width), BF16),
            jax.ShapeDtypeStruct((width, width), F32), jax.ShapeDtypeStruct((width, width), F32),
            jax.ShapeDtypeStruct((8, width), F32),
            jax.ShapeDtypeStruct((4, 2 * gate_blocks.shape[1] + 16, LANES), BF16),
            jax.ShapeDtypeStruct((tokens, depth), BF16),
            jax.ShapeDtypeStruct(reduced.shape, BF16),
        ),
        in_specs=[*[ANYWHERE] * 6, *whole(6), *[ANYWHERE] * 2],
        out_specs=(*whole(6), ANYWHERE),
        scratch_shapes=[
            pltpu.VMEM((tiles, n, LANES), F32),
            pltpu.VMEM((tiles, n, LANES), F32),
            pltpu.VMEM((seg + HALO, width), F32),
            pltpu.VMEM((8 * HALO, width), F32),
            pltpu.VMEM((8 * HALO, width), F32),
            pltpu.VMEM((16, width), F32),
            pltpu.VMEM((count, 16, width), F32),
            pltpu.VMEM((16, width), F32),
            pltpu.SemaphoreType.DMA((count,)),
            pltpu.SemaphoreType.DMA((count,)),
            pltpu.SemaphoreType.DMA((2,)),
            *[pltpu.VMEM(part.shape, part.dtype) for part in (grad_mixed, branches, states, decay, conv_low, mask, middle)],
            pltpu.VMEM((2, width, width), BF16),
            pltpu.SemaphoreType.DMA((7,)),
            *[pltpu.SemaphoreType.DMA((8,))] * 2,
            *Scatter.scratch(tokens, depth),
        ],
        compiler_params=mixer_params(2),
    )(grad_mixed, branches, states, decay, conv_low, mask, halo, cin, gate_blocks, vec, hidden, w_down, middle, reduced)


class Place:
    def __init__(self):
        self.i, self.g, self.c = lax.axis_index("i"), lax.axis_index("g"), lax.axis_index("c")
        self.core, self.across, self.along = {"c": 1 - self.c}, {"g": 1 - self.g}, {"i": 1 - self.i}

    def chunk(self, di, dg, dc):
        i = 1 - self.i if di else self.i
        g = 1 - self.g if dg else self.g
        c = 1 - self.c if dc else self.c
        return (i * 2 + g) * 2 + c

    def peer(self, di, dg, dc):
        return {
            "i": 1 - self.i if di else self.i,
            "g": 1 - self.g if dg else self.g,
            "c": 1 - self.c if dc else self.c,
        }

    def greet(self, more=()):
        barrier = pltpu.get_barrier_semaphore()
        peers = [self.core, self.across, self.along, *more]
        for peer in peers:
            pl.semaphore_signal(barrier, inc=1, device_id=peer, device_id_type=MESH)
        pl.semaphore_wait(barrier, len(peers))


class Gather:
    COPIES = 12

    def __init__(self, place, block, out, send, recv):
        self.place, self.block, self.out, self.send, self.recv = place, block, out, send, recv
        self.tokens = block.shape[0]
        self.half = self.tokens // 2

    def rows(self, chunk, part):
        start = chunk * self.tokens + (self.half if part == 1 else 0)
        return self.out.at[pl.ds(pl.multiple_of(start, self.half), self.tokens if part == 2 else self.half)]

    def mine(self, part):
        if part == 2:
            return self.block
        return self.block.at[pl.ds(part * self.half, self.half)]

    def copy(self, number, source, chunk, part, peer):
        return pltpu.make_async_remote_copy(
            src_ref=source,
            dst_ref=self.rows(chunk, part),
            send_sem=self.send.at[number],
            recv_sem=self.recv.at[number],
            device_id=peer,
            device_id_type=MESH,
        )

    def begin(self, part, whole=False):
        place = self.place
        own = place.chunk(0, 0, 0)
        other = 1 - part if whole else part
        self.give(0 + part, own, part, place.across)
        self.give(2 + other, own, other, place.along)
        self.give(4 + part, own, part, place.core)
        keep = pltpu.make_async_copy(self.mine(part), self.rows(own, part), self.send.at[self.COPIES + part])
        keep.start()
        self.local = getattr(self, "local", []) + [keep]

    def begin_whole(self):
        self.begin(0, True)
        self.begin(1, True)

    def give(self, number, chunk, part, peer):
        moved = self.copy(number, self.mine(part), chunk, part, peer)
        moved.start()
        self.kept = getattr(self, "kept", []) + [moved]

    def arrived(self, number, chunk, part):
        self.copy(number, self.rows(chunk, part), chunk, part, self.place.core).wait_recv()

    def forward(self, number, chunk, part, peer):
        moved = self.copy(number, self.rows(chunk, part), chunk, part, peer)
        moved.start()
        self.kept.append(moved)

    def pass_first(self):
        place = self.place
        ax, al = place.chunk(0, 1, 0), place.chunk(1, 0, 0)
        self.arrived(0, ax, 0)
        self.forward(6, ax, 0, place.along)
        self.arrived(3, al, 1)
        self.forward(7, al, 1, place.across)

    def pass_second(self):
        place = self.place
        ax, al = place.chunk(0, 1, 0), place.chunk(1, 0, 0)
        self.arrived(1, ax, 1)
        self.forward(8, ax, 2, place.core)
        self.arrived(2, al, 0)
        self.forward(9, al, 2, place.core)

    def pass_third(self):
        dia = self.place.chunk(1, 1, 0)
        self.arrived(6, dia, 0)
        self.forward(10, dia, 0, self.place.core)
        self.arrived(7, dia, 1)
        self.forward(11, dia, 1, self.place.core)

    def pass_on(self):
        self.pass_first()
        self.pass_second()
        self.pass_third()

    def finish_core(self):
        for part in (0, 1):
            self.arrived(4 + part, self.place.chunk(0, 0, 1), part)

    def finish_near(self):
        self.arrived(8, self.place.chunk(0, 1, 1), 2)
        self.arrived(9, self.place.chunk(1, 0, 1), 2)

    def finish_far(self):
        for part in (0, 1):
            self.arrived(10 + part, self.place.chunk(1, 1, 1), part)

    def finish(self):
        self.finish_core()
        self.finish_near()
        self.finish_far()
        self.finish_sends()

    def finish_sends(self):
        for moved in self.kept:
            moved.wait_send()
        for keep in self.local:
            keep.wait()


OTHERS = [(di, dg, dc) for di in (0, 1) for dg in (0, 1) for dc in (0, 1) if di or dg or dc]


def first_gather_kernel(count, normed, ids, normed_out, ids_out, before_out, after_out, plane_ids, before, after, send, recv, ids_send, ids_recv):
    place = Place()
    me = lax.axis_index("t")
    up, down = {"t": lax.rem(me + 1, count)}, {"t": lax.rem(me + count - 1, count)}
    place.greet([place.peer(*offset) for offset in OTHERS if sum(offset) > 1] + [up, down])
    gather = Gather(place, normed, normed_out, send, recv)
    own = place.chunk(0, 0, 0)
    moved = []

    def move(number, source, target, peer):
        copy = pltpu.make_async_remote_copy(
            src_ref=source,
            dst_ref=target,
            send_sem=ids_send.at[number],
            recv_sem=ids_recv.at[number],
            device_id=peer,
            device_id_type=MESH,
        )
        copy.start()
        moved.append(copy)

    for number, offset in enumerate(OTHERS):
        move(number, ids, plane_ids.at[own], place.peer(*offset))
    gather.begin_whole()
    plane_ids[own] = ids[...]
    for number, offset in enumerate(OTHERS):
        chunk = place.chunk(*offset)
        pltpu.make_async_remote_copy(
            src_ref=ids,
            dst_ref=plane_ids.at[chunk],
            send_sem=ids_send.at[number],
            recv_sem=ids_recv.at[number],
            device_id=place.peer(*offset),
            device_id_type=MESH,
        ).wait_recv()
    move(7, plane_ids, before, up)
    move(8, plane_ids, after, down)
    gather.pass_on()
    for copy in moved[7:]:
        copy.wait_recv()
    for copy in moved:
        copy.wait_send()
    ids_out[...] = plane_ids[...]
    before_out[...] = before[...]
    after_out[...] = after[...]
    gather.finish()


class Scatter:
    def __init__(self, place, product, core_send, core_recv, held, acc, across_recv, along_recv, second, second_recv, send, recv):
        self.place, self.product = place, product
        self.core_send, self.core_recv, self.held, self.acc = core_send, core_recv, held, acc
        self.across_recv, self.along_recv, self.second, self.second_recv = across_recv, along_recv, second, second_recv
        self.send, self.recv = send, recv
        self.kept = []

    def copy(self, number, source, target, peer):
        return pltpu.make_async_remote_copy(
            src_ref=source,
            dst_ref=target,
            send_sem=self.send.at[number],
            recv_sem=self.recv.at[number],
            device_id=peer,
            device_id_type=MESH,
        )

    def start(self, *parts):
        moved = self.copy(*parts)
        moved.start()
        self.kept.append(moved)

    def run_first(self):
        place = self.place
        order = ((1, 1), (0, 1), (1, 0), (0, 0))
        tile = 256
        per_half = self.held.shape[3] // tile
        def give(di, dg):
            q = 2 * di + dg
            chunk = place.chunk(di, dg, 1)

            def send_tile(n, none):
                at = pl.ds(pl.multiple_of(n % per_half * tile, tile), tile)
                self.core_send[q, n // per_half, :, at] = self.product(chunk, n).astype(BF16)
                return none

            lax.fori_loop(0, 2 * per_half, send_tile, 0)
            self.start(q, self.core_send.at[q], self.core_recv.at[q], place.core)

        def take(di, dg):
            q = 2 * di + dg
            chunk = place.chunk(di, dg, 0)
            self.copy(q, self.core_send.at[q], self.core_recv.at[q], place.core).wait_recv()

            def sum_tile(n, none):
                at = pl.ds(pl.multiple_of(n % per_half * tile, tile), tile)
                value = self.product(chunk, n) + self.core_recv[q, n // per_half, :, at].astype(F32)
                if q:
                    self.held[q - 1, n // per_half, :, at] = value.astype(BF16)
                else:
                    self.acc[n // per_half, :, at] = value
                return none

            lax.fori_loop(0, 2 * per_half, sum_tile, 0)
            if dg:
                self.start(4 + di, self.held.at[q - 1, 0], self.across_recv.at[di], place.across)
            if di:
                self.start(6 + dg, self.held.at[q - 1, 1], self.along_recv.at[dg], place.along)

        give(*order[0])
        give(*order[1])
        take(*order[0])
        give(*order[2])
        take(*order[1])
        give(*order[3])
        take(*order[2])
        take(*order[3])

    def second_copy(self, half, part):
        tokens = self.second.shape[1] // 2
        at = pl.ds(part * tokens, tokens)
        peer = self.place.across if half else self.place.along
        return 8 + 2 * part + half, self.second.at[half, at], self.second_recv.at[half, at], peer

    def run_second(self):
        place = self.place
        tokens = self.second.shape[1] // 2
        for part in (0, 1):
            for half, number, buffer, mine in ((0, 5, self.across_recv, 2), (1, 7, self.along_recv, 1)):
                if part == 0:
                    self.copy(number, buffer.at[1], buffer.at[1], place.core).wait_recv()

                def add_rows(at):
                    total = self.held[mine - 1, half, at, :].astype(F32) + buffer[1, at, :].astype(F32)
                    self.second[half, at, :] = total.astype(BF16)

                for_slices(part * tokens, (part + 1) * tokens, add_rows)
                self.start(*self.second_copy(half, part))

    def run_third(self, part):
        place = self.place
        if part == 0:
            for number, buffer in ((4, self.across_recv), (6, self.along_recv)):
                self.copy(number, buffer.at[0], buffer.at[0], place.core).wait_recv()
        for half in (0, 1):
            self.copy(*self.second_copy(half, part)).wait_recv()

    def rows(self, at):
        first = self.acc[0, at, :] + self.across_recv[0, at, :].astype(F32) + self.second_recv[0, at, :].astype(F32)
        last = self.acc[1, at, :] + self.along_recv[0, at, :].astype(F32) + self.second_recv[1, at, :].astype(F32)
        return jnp.concatenate([first, last], axis=1)

    def finish(self):
        for moved in self.kept:
            moved.wait_send()

    @staticmethod
    def scratch(tokens, width):
        half = width // 2
        return [
            pltpu.VMEM((4, 2, tokens, half), BF16),
            pltpu.VMEM((4, 2, tokens, half), BF16),
            pltpu.VMEM((3, 2, tokens, half), BF16),
            pltpu.VMEM((2, tokens, half), F32),
            pltpu.VMEM((2, tokens, half), BF16),
            pltpu.VMEM((2, tokens, half), BF16),
            pltpu.VMEM((2, tokens, half), BF16),
            pltpu.VMEM((2, tokens, half), BF16),
            pltpu.SemaphoreType.DMA((12,)),
            pltpu.SemaphoreType.DMA((12,)),
        ]


SCATTER_BUFFERS = 10


def pair_product(lefts, rights, tokens):
    def product(chunk, n):
        at = pl.ds(pl.multiple_of(chunk * tokens, tokens), tokens)
        cols = pl.ds(pl.multiple_of(n * 256, 256), 256)
        total = None
        for left, right in zip(lefts, rights):
            term = jnp.dot(left[at, :], right[:, cols], preferred_element_type=F32)
            total = term if total is None else total + term
        return total

    return product


def for_slices(start, stop, body):
    def step(n, none):
        body(pl.ds(pl.multiple_of(n * SLICE, SLICE), SLICE))
        return none

    lax.fori_loop(start // SLICE, stop // SLICE, step, 0)


def middle_kernel(left, right, own_in, gain, middle_out, gathered, *scratch):
    buffers, (block, send, recv) = scratch[:SCATTER_BUFFERS], scratch[SCATTER_BUFFERS:]
    tokens = own_in.shape[0]
    place = Place()
    place.greet()
    scatter = Scatter(place, pair_product([left], [right], tokens), *buffers)
    scatter.run_first()
    scatter.run_second()

    def body(at):
        middle = own_in[at, :].astype(F32) + scatter.rows(at)
        middle_out[at, :] = middle
        block[at, :] = (middle * rms(middle) * gain[...]).astype(BF16)

    gather = Gather(place, block, gathered, send, recv)
    for part in (0, 1):
        scatter.run_third(part)
        for_slices(part * tokens // 2, (part + 1) * tokens // 2, body)
        gather.begin(part)
    gather.pass_on()
    scatter.finish()
    gather.finish()


def turn_kernel(
    left0, left1, right0, right1, middle, gain, cot, normed_far, grad_middle_out, gain_out, grads_out, block_out, *scratch
):
    buffers, (normed, load) = scratch[:SCATTER_BUFFERS], scratch[SCATTER_BUFFERS:]
    loaded = pltpu.make_async_copy(normed_far, normed, load.at[0])
    loaded.start()
    tokens, hidden = cot.shape[0], left0.shape[1]
    place = Place()
    place.greet()
    scatter = Scatter(place, pair_product([left0, left1], [right0, right1], tokens), *buffers)
    scatter.run_first()
    scatter.run_second()
    loaded.wait()

    def weight_grads(n, none):
        at = pl.ds(pl.multiple_of(n * 256, 256), 256)
        for k, part in enumerate((left0, left1)):
            value = lax.dot_general(normed[:, at], part[...], (((0,), (0,)), ((), ())), preferred_element_type=F32)
            grads_out[at, k * hidden : (k + 1) * hidden] = value.astype(BF16)
        return none

    lax.fori_loop(0, normed.shape[1] // 256, weight_grads, 0)
    gain_out[...] = jnp.zeros_like(gain_out)

    def body(at):
        values = middle[at, :]
        grad = scatter.rows(at)
        scale = rms(values)
        weighted = grad * gain[...]
        inner = jnp.mean(values * weighted, axis=-1, keepdims=True)
        total = cot[at, :].astype(F32) + scale * weighted - values * (scale * scale * scale * inner)
        grad_middle_out[at, :] = total
        block_out[at, :] = total.astype(BF16)
        term = grad * values * scale
        gain_out[...] += term[0:8] + term[8:16]

    for part in (0, 1):
        scatter.run_third(part)
        for_slices(part * tokens // 2, (part + 1) * tokens // 2, body)
    scatter.finish()


def spread_kernel(block, w_out, mixed, mixed_out, out_grad, gathered, send, recv, chunk_ref, total, load):
    tokens = block.shape[0]
    place = Place()
    place.greet()
    gather = Gather(place, block, gathered, send, recv)
    gather.begin_whole()
    total[...] = jnp.zeros_like(total)

    def fetch(slot, chunk):
        at = pl.ds(pl.multiple_of(chunk * tokens, tokens), tokens)
        copy = pltpu.make_async_copy(gathered.at[at], chunk_ref.at[slot], load.at[slot])
        copy.start()
        return copy, slot, chunk

    def use(fetched):
        copy, slot, chunk = fetched
        copy.wait()
        use_chunk(chunk_ref.at[slot], chunk)

    def use_chunk(values, chunk):
        at = pl.ds(pl.multiple_of(chunk * tokens, tokens), tokens)
        mixed_out[at, :] = lax.dot_general(values[...], w_out[...], (((1,), (1,)), ((), ())), preferred_element_type=F32)
        part = mixed[at, :]

        def rows(n, none):
            columns = pl.ds(pl.multiple_of(n * 256, 256), 256)
            turned = (((0,), (0,)), ((), ()))
            total[columns, :] += lax.dot_general(values[:, columns], part, turned, preferred_element_type=F32)
            return none

        lax.fori_loop(0, values.shape[1] // 256, rows, 0)

    use_chunk(block, place.chunk(0, 0, 0))
    gather.pass_first()
    gather.finish_core()
    ahead = fetch(0, place.chunk(0, 0, 1))
    use(ahead)
    gather.pass_second()
    ahead = fetch(0, place.chunk(0, 1, 0))
    after = fetch(1, place.chunk(1, 0, 0))
    use(ahead)
    gather.finish_near()
    ahead = fetch(0, place.chunk(0, 1, 1))
    use(after)
    gather.pass_third()
    after = fetch(1, place.chunk(1, 0, 1))
    use(ahead)
    ahead = fetch(0, place.chunk(1, 1, 0))
    use(after)
    gather.finish_far()
    after = fetch(1, place.chunk(1, 1, 1))
    use(ahead)
    use(after)
    out_grad[...] = total[...].astype(BF16)
    gather.finish_sends()


class Owners:
    def __init__(self, place, reduced, out, send, recv):
        self.place, self.reduced, self.out, self.send, self.recv = place, reduced, out, send, recv
        self.own = place.chunk(0, 0, 0)

    def copy(self, number, offset, slot):
        return pltpu.make_async_remote_copy(
            src_ref=self.reduced.at[self.place.chunk(*offset)],
            dst_ref=self.out.at[slot],
            send_sem=self.send.at[number],
            recv_sem=self.recv.at[number],
            device_id=self.place.peer(*offset),
            device_id_type=MESH,
        )

    def begin(self):
        self.keep = pltpu.make_async_copy(self.reduced.at[self.own], self.out.at[self.own], self.send.at[7])
        self.keep.start()
        self.moved = [self.copy(number, offset, self.own) for number, offset in enumerate(OTHERS)]
        for copy in self.moved:
            copy.start()

    def finish(self):
        for number, offset in enumerate(OTHERS):
            self.copy(number, offset, self.place.chunk(*offset)).wait_recv()
        for copy in self.moved:
            copy.wait_send()
        self.keep.wait()


OWNERS_SCRATCH = [pltpu.SemaphoreType.DMA((8,))] * 2
BEYOND = [offset for offset in OTHERS if sum(offset) > 1]


class GateSums:
    def __init__(self, place, count, pieces, rows_recv, gates_all, send, recv):
        self.place, self.count, self.pieces = place, count, pieces
        self.rows_recv, self.gates_all, self.send, self.recv = rows_recv, gates_all, send, recv
        self.me = lax.axis_index("t")
        self.rank = place.g * 2 + place.c
        self.near = [offset for offset in OTHERS if not offset[0]]
        self.moved = []

    def copy(self, number, source, target, peer):
        return pltpu.make_async_remote_copy(
            src_ref=source,
            dst_ref=target,
            send_sem=self.send.at[number],
            recv_sem=self.recv.at[number],
            device_id=peer,
            device_id_type=MESH,
        )

    def begin(self):
        for number, offset in enumerate(self.near):
            other = lax.rem(self.place.chunk(*offset), 4)
            self.moved.append(self.copy(number, self.pieces.at[other], self.rows_recv.at[self.rank], self.place.peer(*offset)))
            self.moved[-1].start()
        self.rows_recv[self.rank] = self.pieces[self.rank]

    def pass_on(self):
        for number, offset in enumerate(self.near):
            other = lax.rem(self.place.chunk(*offset), 4)
            self.copy(number, self.pieces.at[other], self.rows_recv.at[other], self.place.peer(*offset)).wait_recv()
        for step in range(1, self.count):
            to = lax.rem(self.me + step, self.count)
            self.moved.append(self.copy(2 + step, self.rows_recv.at[to], self.gates_all.at[self.me], {"t": to}))
            self.moved[-1].start()
        self.gates_all[self.me] = self.rows_recv[self.me]

    def finish(self, out):
        for step in range(1, self.count):
            other = lax.rem(self.me + self.count - step, self.count)
            self.copy(2 + step, self.rows_recv.at[other], self.gates_all.at[other], {"t": other}).wait_recv()
        total = self.gates_all[0].astype(F32)
        for z in range(1, self.count):
            total = total + self.gates_all[z].astype(F32)
        out[...] = total
        for copy in self.moved:
            copy.wait_send()


def sum_everywhere(place, count, values, inbox, plane_sum, plane_box, send, recv):
    me = lax.axis_index("t")
    own = place.chunk(0, 0, 0)
    moved = []

    def copy(number, source, target, peer):
        return pltpu.make_async_remote_copy(
            src_ref=source,
            dst_ref=target,
            send_sem=send.at[number],
            recv_sem=recv.at[number],
            device_id=peer,
            device_id_type=MESH,
        )

    for number, offset in enumerate(OTHERS):
        moved.append(copy(number, values, inbox.at[own], place.peer(*offset)))
        moved[-1].start()
    inbox[own] = values[...]
    for number, offset in enumerate(OTHERS):
        copy(number, values, inbox.at[place.chunk(*offset)], place.peer(*offset)).wait_recv()
    total = inbox[0]
    for n in range(1, 8):
        total = total + inbox[n]
    plane_sum[...] = total
    for step in range(1, count):
        moved.append(copy(6 + step, plane_sum, plane_box.at[me], {"t": lax.rem(me + step, count)}))
        moved[-1].start()
    plane_box[me] = total
    for step in range(1, count):
        other = lax.rem(me + count - step, count)
        copy(6 + step, plane_sum, plane_box.at[other], {"t": other}).wait_recv()
    total = plane_box[0]
    for z in range(1, count):
        total = total + plane_box[z]
    for sent in moved:
        sent.wait_send()
    return total


def final_kernel(
    count, with_gates, left, right, own_in, gain, mlp_gains, pieces, grad_middle, reduced,
    grad_out, gains_out, gates_out, owned,
    gain_sum, values, inbox, plane_sum, plane_box, sum_send, sum_recv, rows_recv, gates_all, gates_send, gates_recv,
    own_send, own_recv, *buffers,
):
    tokens, width = own_in.shape
    place = Place()
    me = lax.axis_index("t")
    place.greet([place.peer(*offset) for offset in BEYOND] + [{"t": lax.rem(me + step, count)} for step in range(1, count)])
    scatter = Scatter(place, pair_product([left], [right], tokens), *buffers)
    owners = Owners(place, reduced, owned, own_send, own_recv)
    gates = GateSums(place, count, pieces, rows_recv, gates_all, gates_send, gates_recv)
    scatter.run_first()
    if with_gates:
        gates.begin()
    owners.begin()
    scatter.run_second()
    if with_gates:
        gates.pass_on()
    scatter.run_third(0)
    scatter.run_third(1)
    gain_sum[...] = jnp.zeros_like(gain_sum)

    def body(at):
        x = own_in[at, :].astype(F32)
        grad = scatter.rows(at)
        scale = rms(x)
        weighted = grad * gain[...]
        inner = jnp.mean(x * weighted, axis=-1, keepdims=True)
        grad_out[at, :] = grad_middle[at, :] + scale * weighted - x * (scale * scale * scale * inner)
        term = grad * x * scale
        gain_sum[...] += term[0:8] + term[8:16]

    for_slices(0, tokens, body)
    lines = width // LANES
    for base, row in ((0, jnp.sum(mlp_gains[...], axis=0, keepdims=True)), (lines, jnp.sum(gain_sum[...], axis=0, keepdims=True))):
        for n in range(lines):
            values[base + n : base + n + 1, :] = row[:, n * LANES : (n + 1) * LANES]
    gains_out[...] = sum_everywhere(place, count, values, inbox, plane_sum, plane_box, sum_send, sum_recv)
    if with_gates:
        gates.finish(gates_out)
    else:
        gates_out[...] = jnp.zeros_like(gates_out)
    owners.finish()
    scatter.finish()


def final_step(planes, with_gates, left, right, own_in, gain, mlp_gains, pieces, grad_middle, reduced):
    tokens, width = own_in.shape
    block = pieces.shape[1:] if with_gates else (16, LANES)
    slots = planes if with_gates else 1
    sums = (2 * width // LANES, LANES)
    return pl.pallas_call(
        functools.partial(final_kernel, planes, with_gates),
        name="final_step",
        out_shape=(
            jax.ShapeDtypeStruct((tokens, width), F32),
            jax.ShapeDtypeStruct(sums, F32),
            jax.ShapeDtypeStruct(block, F32),
            jax.ShapeDtypeStruct(reduced.shape, reduced.dtype),
        ),
        in_specs=[*whole(7), ANYWHERE],
        out_specs=(*whole(3), ANYWHERE),
        scratch_shapes=[
            pltpu.VMEM((8, width), F32),
            pltpu.VMEM(sums, F32),
            pltpu.VMEM((8, *sums), F32),
            pltpu.VMEM(sums, F32),
            pltpu.VMEM((planes, *sums), F32),
            pltpu.SemaphoreType.DMA((planes + 6,)),
            pltpu.SemaphoreType.DMA((planes + 6,)),
            pltpu.VMEM((slots, *block), BF16),
            pltpu.VMEM((slots, *block), BF16),
            pltpu.SemaphoreType.DMA((planes + 2,)),
            pltpu.SemaphoreType.DMA((planes + 2,)),
            *OWNERS_SCRATCH,
            *Scatter.scratch(tokens, width),
        ],
        compiler_params=mixer_params(7),
    )(left, right, own_in, gain[None], mlp_gains, pieces, grad_middle, reduced)


def owners_kernel(reduced0, reduced1, out0, out1, send0, recv0, send1, recv1):
    place = Place()
    place.greet([place.peer(*offset) for offset in BEYOND])
    owners = [Owners(place, reduced0, out0, send0, recv0), Owners(place, reduced1, out1, send1, recv1)]
    for part in owners:
        part.begin()
    for part in owners:
        part.finish()


def owners_step(reduced):
    return pl.pallas_call(
        owners_kernel,
        name="owners_step",
        out_shape=tuple(jax.ShapeDtypeStruct(part.shape, part.dtype) for part in reduced),
        in_specs=[ANYWHERE] * 2,
        out_specs=(ANYWHERE,) * 2,
        scratch_shapes=[*OWNERS_SCRATCH, *OWNERS_SCRATCH],
        compiler_params=mixer_params(8),
    )(*reduced)


def place_kernel(planes, hidden, outs, *refs):
    given, results = refs[: -len(outs)], refs[-len(outs) :]
    for count, sources, out in zip(outs, given, results):
        piece = sources.shape[2] // (count * (planes if hidden else 1))
        for k in range(count):
            if hidden:
                groups = [
                    ((t * 2 + i) * 4 * piece, [(i * 4 + r, (k * planes + t) * piece) for r in range(4)])
                    for t in range(planes)
                    for i in range(2)
                ]
            else:
                groups = [(r * 2 * piece, [(i * 4 + r, k * piece) for i in range(2)]) for r in range(4)]
            for start, parts in groups:
                row = jnp.concatenate([sources[p, :, at : at + piece].astype(F32) for p, at in parts], axis=1)
                if count > 1:
                    out[:, k, start : start + row.shape[1]] = row
                else:
                    out[:, start : start + row.shape[1]] = row


def place_columns(planes, hidden, outs, *owned):
    members, own_rows, columns = owned[0].shape
    total = columns * members // outs[0]
    shapes = [(own_rows, count, total) if count > 1 else (own_rows, total) for count in outs]
    return pl.pallas_call(
        functools.partial(place_kernel, planes, hidden, outs),
        name="place_columns",
        out_shape=tuple(jax.ShapeDtypeStruct(shape, F32) for shape in shapes),
        in_specs=whole(len(owned)),
        out_specs=tuple(whole(len(outs))),
        compiler_params=pltpu.CompilerParams(vmem_limit_bytes=60 * 1024 * 1024),
    )(*owned)


def first_gather(planes, normed, ids):
    tokens, width = normed.shape
    every = (8, *ids.shape)
    return pl.pallas_call(
        functools.partial(first_gather_kernel, planes),
        name="first_gather",
        out_shape=(jax.ShapeDtypeStruct((8 * tokens, width), BF16), *[jax.ShapeDtypeStruct(every, F32)] * 3),
        in_specs=[ANYWHERE, *whole(1)],
        out_specs=(ANYWHERE, *whole(3)),
        scratch_shapes=[pltpu.VMEM(every, F32)] * 3 + GATHER_SCRATCH + [pltpu.SemaphoreType.DMA((9,))] * 2,
        compiler_params=mixer_params(3),
    )(normed, ids)


def middle_step(mixed, w_out, own_in, gain):
    tokens, width = own_in.shape
    return pl.pallas_call(
        middle_kernel,
        name="middle_step",
        out_shape=(jax.ShapeDtypeStruct((tokens, width), F32), jax.ShapeDtypeStruct((8 * tokens, width), BF16)),
        in_specs=whole(4),
        out_specs=(pl.BlockSpec(memory_space=pltpu.VMEM), ANYWHERE),
        scratch_shapes=Scatter.scratch(tokens, width) + [pltpu.VMEM((tokens, width), BF16)] + GATHER_SCRATCH,
        compiler_params=mixer_params(4),
    )(mixed, w_out, own_in, gain[None])


def turn_step(left0, left1, right0, right1, middle, gain, cot, normed):
    tokens, width = cot.shape
    return pl.pallas_call(
        turn_kernel,
        name="turn_step",
        out_shape=(
            jax.ShapeDtypeStruct((tokens, width), F32),
            jax.ShapeDtypeStruct((8, width), F32),
            jax.ShapeDtypeStruct((width, 2 * left1.shape[1]), BF16),
            jax.ShapeDtypeStruct((tokens, width), BF16),
        ),
        in_specs=[*whole(7), ANYWHERE],
        out_specs=tuple(whole(4)),
        scratch_shapes=Scatter.scratch(tokens, width)
        + [pltpu.VMEM(normed.shape, BF16), pltpu.SemaphoreType.DMA((1,))],
        compiler_params=mixer_params(5),
    )(left0, left1, right0, right1, middle, gain[None], cot, normed)


def spread_step(block, w_out, mixed):
    tokens, width = block.shape
    return pl.pallas_call(
        spread_kernel,
        name="turn_spread",
        out_shape=(
            jax.ShapeDtypeStruct((8 * tokens, w_out.shape[0]), F32),
            jax.ShapeDtypeStruct((width, w_out.shape[0]), BF16),
            jax.ShapeDtypeStruct((8 * tokens, width), BF16),
        ),
        in_specs=whole(3),
        out_specs=(*whole(2), ANYWHERE),
        scratch_shapes=GATHER_SCRATCH
        + [
            pltpu.VMEM((2, tokens, width), BF16),
            pltpu.VMEM((width, w_out.shape[0]), F32),
            pltpu.SemaphoreType.DMA((2,)),
        ],
        compiler_params=mixer_params(10),
    )(block, w_out, mixed)


class Swap:
    def __init__(self, quarters, out, send, recv):
        self.quarters, self.out, self.send, self.recv = quarters, out, send, recv
        self.groups = quarters.shape[0]
        self.me = lax.axis_index("g") * 2 + lax.axis_index("c")

    def copy(self, step, other, slot):
        return pltpu.make_async_remote_copy(
            src_ref=self.quarters.at[other],
            dst_ref=self.out.at[:, slot],
            send_sem=self.send.at[step],
            recv_sem=self.recv.at[step],
            device_id={"g": other // 2, "c": other % 2},
            device_id_type=MESH,
        )

    def peers(self):
        others = [lax.rem(self.me + step, self.groups) for step in range(1, self.groups)]
        return [{"g": other // 2, "c": other % 2} for other in others]

    def begin(self):
        self.keep = pltpu.make_async_copy(self.quarters.at[self.me], self.out.at[:, self.me], self.send.at[0])
        self.keep.start()
        self.moved = []
        for step in range(1, self.groups):
            self.moved.append(self.copy(step, lax.rem(self.me + step, self.groups), self.me))
            self.moved[-1].start()

    def finish(self):
        for step in range(1, self.groups):
            other = lax.rem(self.me + self.groups - step, self.groups)
            self.copy(step, other, other).wait_recv()
        for copy in self.moved:
            copy.wait_send()
        self.keep.wait()


def swap_scratch(groups):
    return [pltpu.SemaphoreType.DMA((groups,)), pltpu.SemaphoreType.DMA((groups,))]


def swap_kernel(quarters, out, send, recv):
    move = Swap(quarters, out, send, recv)
    barrier = pltpu.get_barrier_semaphore()
    for peer in move.peers():
        pl.semaphore_signal(barrier, inc=1, device_id=peer, device_id_type=MESH)
    pl.semaphore_wait(barrier, move.groups - 1)
    move.begin()
    move.finish()


def swap(quarters):
    groups, kinds, part, width = quarters.shape
    return pl.pallas_call(
        swap_kernel,
        name="swap",
        out_shape=jax.ShapeDtypeStruct((kinds, groups, part, width), quarters.dtype),
        in_specs=[ANYWHERE],
        out_specs=ANYWHERE,
        scratch_shapes=swap_scratch(groups),
        compiler_params=mixer_params(6),
    )(quarters)


def rms(values):
    return lax.rsqrt(jnp.mean(values * values, axis=-1, keepdims=True) + EPS)


def nt(left, right, out):
    return lax.dot_general(left, right, (((1,), (1,)), ((), ())), preferred_element_type=F32).astype(out)


def tn(left, right, out):
    return lax.dot_general(left, right, (((0,), (0,)), ((), ())), preferred_element_type=F32).astype(out)


def nn(left, right, out):
    return jnp.dot(left, right, preferred_element_type=F32).astype(out)


def per_device(
    inputs, segment_ids, mix_gain, in_weight, conv_weight, conv_bias, gate_weight, gate_bias, decay_param, out_weight,
    mlp_gain, mlp_in, down_weight, cotangent,
):
    planes = lax.axis_size("t")
    rows_here, seg, width = inputs.shape
    row_groups = lax.axis_size("g") * lax.axis_size("c")
    own_tokens = rows_here * seg
    recur_width = conv_weight.shape[1]
    block_width = gate_weight.shape[0]
    members = 2 * row_groups
    channels = recur_width // members
    t, i = lax.axis_index("t"), lax.axis_index("i")
    r = lax.axis_index("g") * lax.axis_size("c") + lax.axis_index("c")
    member = 2 * r + i
    first = member * channels
    own_rows = width // (planes * members)

    own_in = inputs.reshape(own_tokens, width)
    flat_in = own_in.astype(F32)
    scale_in = rms(flat_in)
    cot_own = cotangent.reshape(own_tokens, width)
    own_ids = jnp.pad((segment_ids + 1).astype(F32), ((0, 8 - rows_here), (0, 0)))

    normed, *ids = first_gather(planes, (flat_in * scale_in * mix_gain).astype(BF16), own_ids)
    late_r, ids[0] = lax.optimization_barrier((r, ids[0]))

    direct = planes == row_groups
    in_own = in_weight.transpose(1, 2, 0)
    out_own = out_weight.T[None]
    part = channels // row_groups if direct else 0

    def quarter(weight, part, rank=r):
        return lax.dynamic_slice_in_dim(weight, rank * part, part, weight.ndim - 1)

    def spread_units(weight):
        return lax.all_gather(weight, "t", axis=0, tiled=False)

    def whole_units(weight):
        every = lax.all_gather(weight, ("t", "i"), axis=1, tiled=True)
        return lax.dynamic_slice_in_dim(every, first, channels, 1)

    if direct:
        in_w = swap(spread_units(quarter(in_weight, part).transpose(1, 2, 0)))
        out_quarters = spread_units(quarter(out_weight, part).T[None])
    else:
        in_w = whole_units(in_own)
        out_quarters = jnp.zeros((row_groups, 1, 16, width), BF16)
    in_w = in_w.reshape(2 * channels, width)
    hidden_part = mlp_in.shape[2] // row_groups
    gated = quarter(mlp_in, hidden_part, late_r).transpose(1, 2, 0)
    w_left, w_right, w_down = [
        spread_units(part).reshape(-1, width)
        for part in (gated[0], gated[1], quarter(down_weight, hidden_part, late_r).T)
    ]

    def own(values):
        return lax.dynamic_slice_in_dim(values, first, channels, values.ndim - 1)

    vec = own(
        jnp.concatenate(
            [
                conv_weight,
                conv_bias[None],
                gate_bias,
                8.0 * jax.nn.softplus(-decay_param)[None],
                8.0 * jax.nn.sigmoid(-decay_param)[None],
                jnp.zeros((7, recur_width), F32),
            ]
        )
    )
    gate_blocks = own(gate_weight).transpose(1, 0, 2)
    blocks = channels // block_width

    branches = nt(normed, in_w, F32)
    conv_low, decay, states, mixed, halo, cin, mask, cot, w_out = mixer_forward(
        planes, seg, rows_here, branches, ids, gate_blocks, vec, cot_own, out_quarters
    )
    w_out = (w_out if direct else whole_units(out_own)).reshape(channels, width)
    middle, normed_two = middle_step(mixed, w_out, own_in, mlp_gain)
    left = nt(normed_two, w_left, F32)
    right = nt(normed_two, w_right, F32)
    act, slope = gelu_parts(left)
    hidden = (act * right).astype(BF16)

    def over_planes(grad):
        return lax.psum_scatter(grad, "t", scatter_dimension=0, tiled=True)

    grad_down = tn(cot, hidden, BF16)
    grad_down, hidden, w_down = lax.optimization_barrier((grad_down, hidden, w_down))
    grad_down = over_planes(grad_down)
    grad_hidden = nt(cot, w_down, F32)
    grad_left = (grad_hidden * right * slope).astype(BF16)
    grad_right = (grad_hidden * act).astype(BF16)
    grad_middle, grad_mlp_gain, grad_mlp_in, grad_mid_own = turn_step(
        grad_left, grad_right, w_left, w_right, middle, mlp_gain, cot_own, normed_two
    )
    grad_down, grad_mid_own = lax.optimization_barrier((grad_down, grad_mid_own))
    grad_mlp_in = over_planes(grad_mlp_in)
    grad_mixed, grad_out, _ = spread_step(grad_mid_own, w_out, mixed)

    def by_owner(grad):
        return grad.reshape(members, own_rows, -1)

    grad_branches, gw0, gw1, small, pieces, outputs, owned_down = mixer_backward(
        planes, seg, grad_mixed, branches, states, decay, conv_low, mask, halo, cin, gate_blocks, vec, hidden, w_down, middle,
        by_owner(grad_down),
    )
    grad_mlp_in, grad_out, grad_branches = lax.optimization_barrier((grad_mlp_in, grad_out, grad_branches))
    grad_out = over_planes(grad_out)
    grad_in = tn(normed, grad_branches, BF16)
    grad_in, grad_branches = lax.optimization_barrier((grad_in, grad_branches))
    grad_in = over_planes(grad_in)
    outputs = outputs.reshape(inputs.shape)

    grad_inputs, gains, gate_grads, owned_mlp_in = final_step(
        planes, direct, grad_branches, in_w, own_in, mix_gain, grad_mlp_gain, pieces, grad_middle,
        by_owner(grad_mlp_in),
    )
    grad_inputs = grad_inputs.reshape(inputs.shape)
    index = ((t * 2 + i) * row_groups + r) * own_rows
    gains = lax.dynamic_slice_in_dim(gains.reshape(2, width), index, own_rows, 1)


    owned_in, owned_out = owners_step([by_owner(grad_in), by_owner(grad_out)])

    def columns(hidden, outs, *owned):
        if direct:
            return place_columns(planes, hidden, outs, *owned)
        owned = jnp.concatenate(owned, axis=2)
        owned = owned.reshape(2, row_groups, own_rows, sum(outs), planes if hidden else 1, -1).astype(F32)
        order = (2, 3, 4, 0, 1, 5) if hidden else (2, 3, 1, 0, 4, 5)
        owned = owned.transpose(order).reshape(own_rows, sum(outs), -1)
        return (owned[:, :2], owned[:, 2])

    grad_in_weight, grad_out_weight = columns(False, (2, 1), owned_in, owned_out)
    grad_mlp_in, grad_down_weight = columns(True, (2, 1), owned_mlp_in, owned_down)
    if direct:
        gate_grads = gate_grads[:, :part]
    else:
        column_block = lax.broadcasted_iota(jnp.int32, (block_width, channels), 1) // block_width

        def diagonal(gw):
            return sum(
                jnp.where(column_block == n, gw[n * block_width : (n + 1) * block_width], 0.0) for n in range(blocks)
            )

        gate_grads = jnp.concatenate([diagonal(gw0), diagonal(gw1), small], axis=0)
        placed = jnp.zeros((gate_grads.shape[0], recur_width), F32)
        placed = lax.dynamic_update_slice_in_dim(placed, gate_grads, first, 1)
        gate_grads = lax.psum_scatter(placed, EVERY, scatter_dimension=1, tiled=True)
    grad_gate_weight = jnp.stack([gate_grads[:block_width], gate_grads[block_width : 2 * block_width]], axis=1)
    small = gate_grads[2 * block_width : 2 * block_width + 8]
    return (
        outputs,
        grad_inputs,
        gains[1],
        grad_in_weight,
        small[0:4],
        small[4],
        grad_gate_weight,
        small[5:7],
        small[7],
        grad_out_weight,
        gains[0],
        grad_mlp_in,
        grad_down_weight,
    )


def solution(mesh):
    seq, rows = mesh.shape["seq"], mesh.shape["rows"]
    grid = Mesh(mesh.devices.reshape(seq // 2, 2, rows // 2, 2), EVERY)
    row_axes, seq_axes = ("g", "c"), ("t", "i")
    tokens = P(row_axes, seq_axes, None)
    return jax.shard_map(
        per_device,
        mesh=grid,
        in_specs=(
            tokens,
            P(row_axes, seq_axes),
            P(),
            P(None, None, seq_axes),
            P(),
            P(),
            P(),
            P(),
            P(),
            P(None, seq_axes),
            P(),
            P(None, None, seq_axes),
            P(None, seq_axes),
            tokens,
        ),
        out_specs=(
            tokens,
            tokens,
            P(EVERY),
            P(EVERY, None, None),
            P(None, EVERY),
            P(EVERY),
            P(None, None, EVERY),
            P(None, EVERY),
            P(EVERY),
            P(EVERY, None),
            P(EVERY),
            P(EVERY, None, None),
            P(EVERY, None),
        ),
        check_vma=False,
    )
```

```python
import functools

import jax
import jax.numpy as jnp
from jax import lax
from jax.experimental import pallas as pl
from jax.experimental.pallas import tpu as pltpu
from jax.sharding import Mesh
from jax.sharding import PartitionSpec as P

EPS = 1e-06
MESH = pl.DeviceIdType.MESH
PLANE = ("i", "g", "c")
EVERY = ("t", "i", "g", "c")
F32 = jnp.float32
BF16 = jnp.bfloat16
GELU_A = 0.7978845608028654
GELU_B = 0.044715
HALO = 8
LANES = 128
SLICE = 16
ANYWHERE = pl.BlockSpec(memory_space=pl.ANY)
GATHER_SCRATCH = [pltpu.SemaphoreType.DMA((14,))] * 2


def gelu_parts(x):
    square = x * x
    th = jnp.tanh(GELU_A * x * (1.0 + GELU_B * square))
    half = 0.5 * (1.0 + th)
    slope = half + 0.5 * x * (1.0 - th * th) * (GELU_A * (1.0 + 3.0 * GELU_B * square))
    return x * half, slope


def one_minus_exp(y, power):
    series = 1.0 + y * (-1.0 / 2 + y * (1.0 / 6 + y * (-1.0 / 24 + y * (1.0 / 120 + y * (-1.0 / 720 + y * (1.0 / 5040))))))
    return jnp.where(y < 0.35, y * series, 1.0 - power)


def sigmoid(x):
    return 1.0 / (1.0 + jnp.exp(-x))


def gate_values(conv_low, wg0, wg1, vec):
    logits0 = jnp.dot(conv_low, wg0, preferred_element_type=F32) + vec[5:6]
    logits1 = jnp.dot(conv_low, wg1, preferred_element_type=F32) + vec[6:7]
    recur_gate = sigmoid(logits0)
    input_gate = sigmoid(logits1)
    log_decay = -vec[7:8] * recur_gate
    return recur_gate, input_gate, log_decay


def spread_blocks(gates, out):
    size, width = gates.shape[1], gates.shape[2]
    column = lax.broadcasted_iota(jnp.int32, (size, width), 1) // size
    for k in range(2):
        block = gates[k].astype(F32)
        for n in range(width // size):
            out[k, n * size : (n + 1) * size, :] = jnp.where(column == n, block, 0.0).astype(BF16)


def put_tiles(ref, at, values):
    tiles, lanes = ref.shape[0], ref.shape[2]
    short = tiles * lanes - values.shape[1]
    if short:
        values = jnp.concatenate([values, jnp.zeros((values.shape[0], short), values.dtype)], axis=1)
    for j in range(tiles):
        ref[j, at, :] = values[:, j * lanes : (j + 1) * lanes]


def get_tiles(ref, at, width):
    joined = jnp.concatenate([ref[j, at, :] for j in range(ref.shape[0])], axis=1)
    return joined[:, :width]


def join_tiles(parts, width):
    return jnp.concatenate(parts, axis=1)[:, :width]


def exchange_copy(step, send, target, other, send_sem, recv_sem):
    return pltpu.make_async_remote_copy(
        src_ref=send,
        dst_ref=target,
        send_sem=send_sem.at[step],
        recv_sem=recv_sem.at[step],
        device_id={"t": other},
        device_id_type=MESH,
    )


def exchange_start(count, me, send, slots, send_sem, recv_sem):
    for step in range(1, count):
        exchange_copy(step, send, slots.at[me], lax.rem(me + step, count), send_sem, recv_sem).start()


def exchange_wait(count, me, send, slots, send_sem, recv_sem):
    for step in range(1, count):
        other = lax.rem(me + count - step, count)
        exchange_copy(step, send, slots.at[other], other, send_sem, recv_sem).wait()


def mixer_forward_kernel(
    count, seg, rows_here, branches_far, ids, ids_before, ids_after, gate_blocks, vec_ref, cot, quarters,
    conv_out, decay_out, states_out, mixed_out, halo_out, cin_out, mask, cot_out, swapped,
    drive, h_ref, a_ref, ext, halo_send, halo_recv, summary, slots, send_sem, recv_sem, halo_sems,
    gather_send, gather_recv, swap_send, swap_recv, branches, wg, load,
):
    place = Place()
    me = lax.axis_index("t")
    loaded = pltpu.make_async_copy(branches_far, branches, load.at[0])
    loaded.start()
    place.greet([place.peer(0, 1, 1)] + [{"t": lax.rem(me + step, count)} for step in range(1, count)])
    gather = Gather(place, cot, cot_out, gather_send, gather_recv)
    move = Swap(quarters, swapped, swap_send, swap_recv)
    gather.begin_whole()
    move.begin()
    spread_blocks(gate_blocks, wg)
    rows = 8
    width = branches.shape[1] // 2
    loaded.wait()

    def recur_at(at):
        return branches[at, width:].astype(BF16).astype(F32)

    for r in range(rows):
        halo_send[r * HALO : (r + 1) * HALO, :] = recur_at(pl.ds((rows + r + 1) * seg - HALO, HALO))
    halo_copy = pltpu.make_async_remote_copy(
        src_ref=halo_send,
        dst_ref=halo_recv,
        send_sem=halo_sems.at[0],
        recv_sem=halo_sems.at[1],
        device_id={"t": lax.rem(me + 1, count)},
        device_id_type=MESH,
    )
    halo_copy.start()
    for r in range(rows):
        halo_out[(rows + r) * HALO : (rows + r + 1) * HALO, :] = recur_at(pl.ds((r + 1) * seg - HALO, HALO))
    vec = vec_ref[...]

    def ids_of(ref, s):
        chunk = s // rows_here
        return ref[chunk, s % rows_here : s % rows_here + 1, :]

    nothing = jnp.zeros((1, LANES), F32)
    for s in range(2 * rows):
        here = ids_of(ids, s)
        back = ids_of(ids, s - rows) if s >= rows else jnp.where(me > 0, ids_of(ids_before, s + rows), nothing)
        ahead = ids_of(ids, s + rows) if s < rows else jnp.where(me < count - 1, ids_of(ids_after, s - rows), nothing)
        lines = [jnp.concatenate([back[:, seg - k :], here[:, : seg - k]], axis=1) for k in (1, 2, 3)]
        lines += [jnp.concatenate([here[:, k:], ahead[:, :k]], axis=1) for k in (1, 2, 3)]
        lines = [jnp.where(line == here, 1.0, 0.0) for line in lines] + [nothing] * 2
        mask[s * seg : (s + 1) * seg, :] = jnp.concatenate(lines, axis=0).T

    def local(s, none):
        at = pl.ds(pl.multiple_of(s * seg, seg), seg)
        x = recur_at(at)
        ext[0:HALO, :] = halo_out[pl.ds(pl.multiple_of(s * HALO, HALO), HALO), :]
        ext[HALO : HALO + seg, :] = x
        m = mask[at, :]
        conv = vec[4:5] + vec[0:1] * x
        for k in range(1, 4):
            conv = conv + vec[k : k + 1] * ext[HALO - k : HALO - k + seg, :] * m[:, k - 1 : k]
        conv_low = conv.astype(BF16)
        conv_out[at, :] = conv_low
        recur_gate, input_gate, log_decay = gate_values(conv_low, wg[0], wg[1], vec)
        keep = m[:, 0:1]
        kept = jnp.exp(log_decay)
        put_tiles(decay_out, at, kept * keep)
        scale = (1.0 - keep) + keep * jnp.sqrt(one_minus_exp(-2.0 * log_decay, kept * kept))
        put_tiles(drive, at, scale * input_gate * conv_low.astype(F32))
        return none

    lax.fori_loop(rows, 2 * rows, local, 0)
    halo_copy.wait()
    for r in range(rows):
        halo_out[r * HALO : (r + 1) * HALO, :] = halo_recv[r * HALO : (r + 1) * HALO, :]
    gather.pass_first()
    lax.fori_loop(0, rows, local, 0)
    tiles, lanes = drive.shape[0], drive.shape[2]

    def scan(k, carried):
        at = pl.ds(k, 2 * rows, stride=seg)
        after = []
        for j in range(tiles):
            h, a = carried[j]
            d = decay_out[j, at, :]
            h = d * h + drive[j, at, :]
            a = a * d
            h_ref[j, at, :] = h
            a_ref[j, at, :] = a
            after.append((h, a))
        return tuple(after)

    start = (jnp.zeros((2 * rows, lanes), F32), jnp.ones((2 * rows, lanes), F32))
    last = lax.fori_loop(0, seg, scan, (start,) * tiles, unroll=4)
    last_h = join_tiles([part[0] for part in last], width)
    last_a = join_tiles([part[1] for part in last], width)
    summary[0:rows, :] = last_a[rows:] * last_a[:rows]
    summary[rows : 2 * rows, :] = last_a[rows:] * last_h[:rows] + last_h[rows:]
    exchange_start(count, me, summary, slots, send_sem, recv_sem)
    gather.pass_second()

    def activate(s, none):
        at = pl.ds(pl.multiple_of(s * seg, seg), seg)
        act, _ = gelu_parts(branches[at, :width])
        states_out[at, :] = act
        return none

    lax.fori_loop(0, 2 * rows, activate, 0)
    exchange_wait(count, me, summary, slots, send_sem, recv_sem)
    carry = jnp.zeros((rows, width), F32)
    for z in range(count - 1):
        carry = jnp.where(z < me, slots[z, 0:rows, :] * carry + slots[z, rows : 2 * rows, :], carry)
    cin_out[0:rows, :] = carry
    cin_out[rows : 2 * rows, :] = last_a[:rows] * carry + last_h[:rows]

    def finish(s, none):
        at = pl.ds(pl.multiple_of(s * seg, seg), seg)
        states = get_tiles(h_ref, at, width) + get_tiles(a_ref, at, width) * cin_out[pl.ds(s, 1), :]
        act = states_out[at, :]
        states_out[at, :] = states
        mixed_out[at, :] = (act * states.astype(BF16).astype(F32)).astype(BF16)
        return none

    lax.fori_loop(0, 2 * rows, finish, 0)
    gather.pass_third()
    gather.finish()
    move.finish()


def mixer_backward_kernel(
    count, seg, grad_mixed_far, branches_far, states_far, decay_far, conv_far, mask_far, halo, cin, gate_blocks, vec_ref,
    hidden, w_down, middle_far, reduced, grad_out, gw0_out, gw1_out, small_out, pieces_out, outputs, owned,
    tot, prod, ext, halo_send, halo_recv, summary, slots, uin, send_sem, recv_sem, halo_sems,
    grad_mixed, branches, states, decay, conv_low_ref, mask, middle, wg, load, own_send, own_recv, *buffers,
):
    place = Place()
    pairs = (
        (grad_mixed_far, grad_mixed),
        (branches_far, branches),
        (states_far, states),
        (decay_far, decay),
        (conv_far, conv_low_ref),
        (mask_far, mask),
        (middle_far, middle),
    )
    loads = [pltpu.make_async_copy(far, near, load.at[n]) for n, (far, near) in enumerate(pairs)]
    for part in loads:
        part.start()
    me = lax.axis_index("t")
    place.greet([place.peer(*offset) for offset in BEYOND] + [{"t": lax.rem(me + step, count)} for step in range(1, count)])
    scatter = Scatter(place, pair_product([hidden], [w_down], outputs.shape[0]), *buffers)
    owners = Owners(place, reduced, owned, own_send, own_recv)
    spread_blocks(gate_blocks, wg)
    scatter.run_first()
    owners.begin()
    for part in loads:
        part.wait()
    rows = 8
    width = branches.shape[1] // 2
    vec = vec_ref[...]

    def local(s, none):
        at = pl.ds(pl.multiple_of(s * seg, seg), seg)
        act, slope = gelu_parts(branches[at, :width])
        gm = grad_mixed[at, :].astype(F32)
        grad_out[at, :width] = (gm * states[at, :].astype(BF16).astype(F32) * slope).astype(BF16)
        put_tiles(tot, at, (gm * act).astype(BF16).astype(F32))
        return none

    lax.fori_loop(0, 2 * rows, local, 0)

    tiles, lanes = tot.shape[0], tot.shape[2]

    def scan(k, carried):
        at = pl.ds(seg - 1 - k, 2 * rows, stride=seg)
        after = []
        for j in range(tiles):
            u, p = carried[j]
            d = decay[j, at, :]
            total = tot[j, at, :] + u
            tot[j, at, :] = total
            prod[j, at, :] = p
            after.append((d * total, d * p))
        return tuple(after)

    start = (jnp.zeros((2 * rows, lanes), F32), jnp.ones((2 * rows, lanes), F32))
    last = lax.fori_loop(0, seg, scan, (start,) * tiles, unroll=4)
    u = join_tiles([part[0] for part in last], width)
    p = join_tiles([part[1] for part in last], width)
    summary[0:rows, :] = p[:rows] * p[rows:]
    summary[rows : 2 * rows, :] = p[:rows] * u[rows:] + u[:rows]
    exchange_start(count, me, summary, slots, send_sem, recv_sem)
    scatter.run_second()
    exchange_wait(count, me, summary, slots, send_sem, recv_sem)
    carry = jnp.zeros((rows, width), F32)
    for z in range(count - 1, 0, -1):
        carry = jnp.where(z > me, slots[z, 0:rows, :] * carry + slots[z, rows : 2 * rows, :], carry)
    uin[rows : 2 * rows, :] = carry
    uin[0:rows, :] = p[rows:] * carry + u[rows:]
    gw0_out[...] = jnp.zeros_like(gw0_out)
    gw1_out[...] = jnp.zeros_like(gw1_out)
    small_out[...] = jnp.zeros_like(small_out)

    def gates(s, none):
        at = pl.ds(pl.multiple_of(s * seg, seg), seg)
        total = get_tiles(tot, at, width) + get_tiles(prod, at, width) * uin[pl.ds(s, 1), :]
        ext[HALO - 1 : HALO, :] = cin[pl.ds(s, 1), :]
        ext[HALO : HALO + seg, :] = states[at, :]
        before = ext[HALO - 1 : HALO - 1 + seg, :]
        conv_low = conv_low_ref[at, :]
        conv_vals = conv_low.astype(F32)
        m = mask[at, :]
        keep = m[:, 0:1]
        recur_gate, input_gate, log_decay = gate_values(conv_low, wg[0], wg[1], vec)
        power = jnp.exp(2.0 * log_decay)
        gone = one_minus_exp(-2.0 * log_decay, power)
        inverse = lax.rsqrt(gone)
        root = gone * inverse
        scale = (1.0 - keep) + keep * root
        driven_in = total * conv_vals
        grad_log = total * before * get_tiles(decay, at, width) - driven_in * input_gate * keep * (power * inverse)
        grad0 = grad_log * log_decay * (1.0 - recur_gate)
        grad1 = driven_in * scale * input_gate * (1.0 - input_gate)
        low0 = grad0.astype(BF16)
        low1 = grad1.astype(BF16)
        inputs_of = (((1,), (1,)), ((), ()))
        grad_conv = (
            total * scale * input_gate
            + lax.dot_general(low0, wg[0], inputs_of, preferred_element_type=F32)
            + lax.dot_general(low1, wg[1], inputs_of, preferred_element_type=F32)
        )
        put_tiles(tot, at, grad_conv)
        turned = (((0,), (0,)), ((), ()))
        gw0_out[...] += lax.dot_general(conv_low, low0, turned, preferred_element_type=F32)
        gw1_out[...] += lax.dot_general(conv_low, low1, turned, preferred_element_type=F32)
        x = branches[at, width:].astype(BF16).astype(F32)
        ext[0:HALO, :] = halo[pl.ds(pl.multiple_of(s * HALO, HALO), HALO), :]
        ext[HALO : HALO + seg, :] = x

        def add(row, values):
            small_out[row : row + 1, :] += jnp.sum(values, axis=0, keepdims=True)

        add(0, grad_conv * x)
        for k in range(1, 4):
            add(k, grad_conv * ext[HALO - k : HALO - k + seg, :] * m[:, k - 1 : k])
        add(4, grad_conv)
        add(5, grad0)
        add(6, grad1)
        add(7, grad_log * recur_gate)
        return none

    lax.fori_loop(0, 2 * rows, gates, 0)
    small_out[7:8, :] = small_out[7:8, :] * vec[8:9]
    size, part = gate_blocks.shape[1], width // 4

    def padded(values):
        short = [values, jnp.zeros((values.shape[0], LANES - part), F32)]
        return jnp.concatenate(short, axis=1)

    for r in range(4):
        first = r * part // size * size
        at = slice(r * part, (r + 1) * part)
        for k, square in enumerate((gw0_out, gw1_out)):
            pieces_out[r, k * size : (k + 1) * size, :] = padded(square[first : first + size, at]).astype(BF16)
        rest = jnp.concatenate([padded(small_out[:, at]), jnp.zeros((8, LANES), F32)], axis=0)
        pieces_out[r, 2 * size :, :] = rest.astype(BF16)
    for r in range(rows):
        halo_send[r * HALO : (r + 1) * HALO, :] = get_tiles(tot, pl.ds(r * seg, HALO), width)
    halo_copy = pltpu.make_async_remote_copy(
        src_ref=halo_send,
        dst_ref=halo_recv,
        send_sem=halo_sems.at[0],
        recv_sem=halo_sems.at[1],
        device_id={"t": lax.rem(me + count - 1, count)},
        device_id_type=MESH,
    )
    halo_copy.start()

    def back(s, none):
        at = pl.ds(pl.multiple_of(s * seg, seg), seg)
        m = mask[at, :]
        grad_conv = get_tiles(tot, at, width)
        ext[0:seg, :] = grad_conv
        result = vec[0:1] * grad_conv

        @pl.when(s < rows)
        def _():
            ext[seg : seg + HALO, :] = get_tiles(tot, pl.ds(pl.multiple_of((s + rows) * seg, seg), HALO), width)

        @pl.when(s >= rows)
        def _():
            ext[seg : seg + HALO, :] = halo_recv[pl.ds(pl.multiple_of((s - rows) * HALO, HALO), HALO), :]

        for k in range(1, 4):
            result = result + vec[k : k + 1] * ext[k : k + seg, :] * m[:, 2 + k : 3 + k]
        grad_out[at, width:] = result.astype(BF16)
        return none

    lax.fori_loop(0, rows, back, 0)
    halo_copy.wait()
    lax.fori_loop(rows, 2 * rows, back, 0)
    scatter.run_third(0)
    scatter.run_third(1)

    def body(at):
        outputs[at, :] = (middle[at, :] + scatter.rows(at)).astype(BF16)

    for_slices(0, outputs.shape[0], body)
    scatter.finish()
    owners.finish()


def whole(count):
    return [pl.BlockSpec(memory_space=pltpu.VMEM)] * count


def mixer_params(number):
    return pltpu.CompilerParams(collective_id=number, has_side_effects=True, vmem_limit_bytes=60 * 1024 * 1024)


def mixer_forward(count, seg, rows_here, branches, ids, gate_blocks, vec, cot, quarters):
    n, width = branches.shape[0], branches.shape[1] // 2
    full = functools.partial(jax.ShapeDtypeStruct, (n, width))
    tiles = -(-width // LANES)
    tiled = jax.ShapeDtypeStruct((tiles, n, LANES), F32)
    groups, kinds, part, depth = quarters.shape
    return pl.pallas_call(
        functools.partial(mixer_forward_kernel, count, seg, rows_here),
        name="mixer_forward",
        out_shape=(
            full(BF16), tiled, full(F32), full(BF16),
            jax.ShapeDtypeStruct((16 * HALO, width), F32), jax.ShapeDtypeStruct((16, width), F32),
            jax.ShapeDtypeStruct((n, 8), F32),
            jax.ShapeDtypeStruct((8 * cot.shape[0], cot.shape[1]), BF16),
            jax.ShapeDtypeStruct((kinds, groups, part, depth), BF16),
        ),
        in_specs=[ANYWHERE, *whole(5), ANYWHERE, ANYWHERE],
        out_specs=(*whole(7), ANYWHERE, ANYWHERE),
        scratch_shapes=[
            pltpu.VMEM((tiles, n, LANES), F32),
            pltpu.VMEM((tiles, n, LANES), F32),
            pltpu.VMEM((tiles, n, LANES), F32),
            pltpu.VMEM((seg + HALO, width), F32),
            pltpu.VMEM((8 * HALO, width), F32),
            pltpu.VMEM((8 * HALO, width), F32),
            pltpu.VMEM((16, width), F32),
            pltpu.VMEM((count, 16, width), F32),
            pltpu.SemaphoreType.DMA((count,)),
            pltpu.SemaphoreType.DMA((count,)),
            pltpu.SemaphoreType.DMA((2,)),
            *GATHER_SCRATCH,
            *swap_scratch(groups),
            pltpu.VMEM(branches.shape, F32),
            pltpu.VMEM((2, width, width), BF16),
            pltpu.SemaphoreType.DMA((1,)),
        ],
        compiler_params=mixer_params(1),
    )(branches, *ids, gate_blocks, vec, cot, quarters)


def mixer_backward(count, seg, grad_mixed, branches, states, decay, conv_low, mask, halo, cin, gate_blocks, vec, hidden, w_down, middle, reduced):
    n, width = branches.shape[0], branches.shape[1] // 2
    tokens, depth = n // 8, w_down.shape[1]
    full = functools.partial(jax.ShapeDtypeStruct, (n, width))
    tiles = -(-width // LANES)
    tiled = jax.ShapeDtypeStruct((tiles, n, LANES), F32)
    return pl.pallas_call(
        functools.partial(mixer_backward_kernel, count, seg),
        name="mixer_backward",
        out_shape=(
            jax.ShapeDtypeStruct((n, 2 * width), BF16),
            jax.ShapeDtypeStruct((width, width), F32), jax.ShapeDtypeStruct((width, width), F32),
            jax.ShapeDtypeStruct((8, width), F32),
            jax.ShapeDtypeStruct((4, 2 * gate_blocks.shape[1] + 16, LANES), BF16),
            jax.ShapeDtypeStruct((tokens, depth), BF16),
            jax.ShapeDtypeStruct(reduced.shape, BF16),
        ),
        in_specs=[*[ANYWHERE] * 6, *whole(6), *[ANYWHERE] * 2],
        out_specs=(*whole(6), ANYWHERE),
        scratch_shapes=[
            pltpu.VMEM((tiles, n, LANES), F32),
            pltpu.VMEM((tiles, n, LANES), F32),
            pltpu.VMEM((seg + HALO, width), F32),
            pltpu.VMEM((8 * HALO, width), F32),
            pltpu.VMEM((8 * HALO, width), F32),
            pltpu.VMEM((16, width), F32),
            pltpu.VMEM((count, 16, width), F32),
            pltpu.VMEM((16, width), F32),
            pltpu.SemaphoreType.DMA((count,)),
            pltpu.SemaphoreType.DMA((count,)),
            pltpu.SemaphoreType.DMA((2,)),
            *[pltpu.VMEM(part.shape, part.dtype) for part in (grad_mixed, branches, states, decay, conv_low, mask, middle)],
            pltpu.VMEM((2, width, width), BF16),
            pltpu.SemaphoreType.DMA((7,)),
            *[pltpu.SemaphoreType.DMA((8,))] * 2,
            *Scatter.scratch(tokens, depth),
        ],
        compiler_params=mixer_params(2),
    )(grad_mixed, branches, states, decay, conv_low, mask, halo, cin, gate_blocks, vec, hidden, w_down, middle, reduced)


class Place:
    def __init__(self):
        self.i, self.g, self.c = lax.axis_index("i"), lax.axis_index("g"), lax.axis_index("c")
        self.core, self.across, self.along = {"c": 1 - self.c}, {"g": 1 - self.g}, {"i": 1 - self.i}

    def chunk(self, di, dg, dc):
        i = 1 - self.i if di else self.i
        g = 1 - self.g if dg else self.g
        c = 1 - self.c if dc else self.c
        return (i * 2 + g) * 2 + c

    def peer(self, di, dg, dc):
        return {
            "i": 1 - self.i if di else self.i,
            "g": 1 - self.g if dg else self.g,
            "c": 1 - self.c if dc else self.c,
        }

    def greet(self, more=()):
        barrier = pltpu.get_barrier_semaphore()
        peers = [self.core, self.across, self.along, *more]
        for peer in peers:
            pl.semaphore_signal(barrier, inc=1, device_id=peer, device_id_type=MESH)
        pl.semaphore_wait(barrier, len(peers))


class Gather:
    COPIES = 12

    def __init__(self, place, block, out, send, recv):
        self.place, self.block, self.out, self.send, self.recv = place, block, out, send, recv
        self.tokens = block.shape[0]
        self.half = self.tokens // 2

    def rows(self, chunk, part):
        start = chunk * self.tokens + (self.half if part == 1 else 0)
        return self.out.at[pl.ds(pl.multiple_of(start, self.half), self.tokens if part == 2 else self.half)]

    def mine(self, part):
        if part == 2:
            return self.block
        return self.block.at[pl.ds(part * self.half, self.half)]

    def copy(self, number, source, chunk, part, peer):
        return pltpu.make_async_remote_copy(
            src_ref=source,
            dst_ref=self.rows(chunk, part),
            send_sem=self.send.at[number],
            recv_sem=self.recv.at[number],
            device_id=peer,
            device_id_type=MESH,
        )

    def begin(self, part, whole=False):
        place = self.place
        own = place.chunk(0, 0, 0)
        other = 1 - part if whole else part
        self.give(0 + part, own, part, place.across)
        self.give(2 + other, own, other, place.along)
        self.give(4 + part, own, part, place.core)
        keep = pltpu.make_async_copy(self.mine(part), self.rows(own, part), self.send.at[self.COPIES + part])
        keep.start()
        self.local = getattr(self, "local", []) + [keep]

    def begin_whole(self):
        self.begin(0, True)
        self.begin(1, True)

    def give(self, number, chunk, part, peer):
        moved = self.copy(number, self.mine(part), chunk, part, peer)
        moved.start()
        self.kept = getattr(self, "kept", []) + [moved]

    def arrived(self, number, chunk, part):
        self.copy(number, self.rows(chunk, part), chunk, part, self.place.core).wait_recv()

    def forward(self, number, chunk, part, peer):
        moved = self.copy(number, self.rows(chunk, part), chunk, part, peer)
        moved.start()
        self.kept.append(moved)

    def pass_first(self):
        place = self.place
        ax, al = place.chunk(0, 1, 0), place.chunk(1, 0, 0)
        self.arrived(0, ax, 0)
        self.forward(6, ax, 0, place.along)
        self.arrived(3, al, 1)
        self.forward(7, al, 1, place.across)

    def pass_second(self):
        place = self.place
        ax, al = place.chunk(0, 1, 0), place.chunk(1, 0, 0)
        self.arrived(1, ax, 1)
        self.forward(8, ax, 2, place.core)
        self.arrived(2, al, 0)
        self.forward(9, al, 2, place.core)

    def pass_third(self):
        dia = self.place.chunk(1, 1, 0)
        self.arrived(6, dia, 0)
        self.forward(10, dia, 0, self.place.core)
        self.arrived(7, dia, 1)
        self.forward(11, dia, 1, self.place.core)

    def pass_on(self):
        self.pass_first()
        self.pass_second()
        self.pass_third()

    def finish_core(self):
        for part in (0, 1):
            self.arrived(4 + part, self.place.chunk(0, 0, 1), part)

    def finish_near(self):
        self.arrived(8, self.place.chunk(0, 1, 1), 2)
        self.arrived(9, self.place.chunk(1, 0, 1), 2)

    def finish_far(self):
        for part in (0, 1):
            self.arrived(10 + part, self.place.chunk(1, 1, 1), part)

    def finish(self):
        self.finish_core()
        self.finish_near()
        self.finish_far()
        self.finish_sends()

    def finish_sends(self):
        for moved in self.kept:
            moved.wait_send()
        for keep in self.local:
            keep.wait()


OTHERS = [(di, dg, dc) for di in (0, 1) for dg in (0, 1) for dc in (0, 1) if di or dg or dc]


def first_gather_kernel(count, normed, ids, normed_out, ids_out, before_out, after_out, plane_ids, before, after, send, recv, ids_send, ids_recv):
    place = Place()
    me = lax.axis_index("t")
    up, down = {"t": lax.rem(me + 1, count)}, {"t": lax.rem(me + count - 1, count)}
    place.greet([place.peer(*offset) for offset in OTHERS if sum(offset) > 1] + [up, down])
    gather = Gather(place, normed, normed_out, send, recv)
    own = place.chunk(0, 0, 0)
    moved = []

    def move(number, source, target, peer):
        copy = pltpu.make_async_remote_copy(
            src_ref=source,
            dst_ref=target,
            send_sem=ids_send.at[number],
            recv_sem=ids_recv.at[number],
            device_id=peer,
            device_id_type=MESH,
        )
        copy.start()
        moved.append(copy)

    for number, offset in enumerate(OTHERS):
        move(number, ids, plane_ids.at[own], place.peer(*offset))
    gather.begin_whole()
    plane_ids[own] = ids[...]
    for number, offset in enumerate(OTHERS):
        chunk = place.chunk(*offset)
        pltpu.make_async_remote_copy(
            src_ref=ids,
            dst_ref=plane_ids.at[chunk],
            send_sem=ids_send.at[number],
            recv_sem=ids_recv.at[number],
            device_id=place.peer(*offset),
            device_id_type=MESH,
        ).wait_recv()
    move(7, plane_ids, before, up)
    move(8, plane_ids, after, down)
    gather.pass_on()
    for copy in moved[7:]:
        copy.wait_recv()
    for copy in moved:
        copy.wait_send()
    ids_out[...] = plane_ids[...]
    before_out[...] = before[...]
    after_out[...] = after[...]
    gather.finish()


class Scatter:
    def __init__(self, place, product, core_send, core_recv, held, acc, across_recv, along_recv, second, second_recv, send, recv):
        self.place, self.product = place, product
        self.core_send, self.core_recv, self.held, self.acc = core_send, core_recv, held, acc
        self.across_recv, self.along_recv, self.second, self.second_recv = across_recv, along_recv, second, second_recv
        self.send, self.recv = send, recv
        self.kept = []

    def copy(self, number, source, target, peer):
        return pltpu.make_async_remote_copy(
            src_ref=source,
            dst_ref=target,
            send_sem=self.send.at[number],
            recv_sem=self.recv.at[number],
            device_id=peer,
            device_id_type=MESH,
        )

    def start(self, *parts):
        moved = self.copy(*parts)
        moved.start()
        self.kept.append(moved)

    def run_first(self):
        place = self.place
        order = ((1, 1), (0, 1), (1, 0), (0, 0))
        tile = 256
        per_half = self.held.shape[3] // tile
        def give(di, dg):
            q = 2 * di + dg
            chunk = place.chunk(di, dg, 1)

            def send_tile(n, none):
                at = pl.ds(pl.multiple_of(n % per_half * tile, tile), tile)
                self.core_send[q, n // per_half, :, at] = self.product(chunk, n).astype(BF16)
                return none

            lax.fori_loop(0, 2 * per_half, send_tile, 0)
            self.start(q, self.core_send.at[q], self.core_recv.at[q], place.core)

        def take(di, dg):
            q = 2 * di + dg
            chunk = place.chunk(di, dg, 0)
            self.copy(q, self.core_send.at[q], self.core_recv.at[q], place.core).wait_recv()

            def sum_tile(n, none):
                at = pl.ds(pl.multiple_of(n % per_half * tile, tile), tile)
                value = self.product(chunk, n) + self.core_recv[q, n // per_half, :, at].astype(F32)
                if q:
                    self.held[q - 1, n // per_half, :, at] = value.astype(BF16)
                else:
                    self.acc[n // per_half, :, at] = value
                return none

            lax.fori_loop(0, 2 * per_half, sum_tile, 0)
            if dg:
                self.start(4 + di, self.held.at[q - 1, 0], self.across_recv.at[di], place.across)
            if di:
                self.start(6 + dg, self.held.at[q - 1, 1], self.along_recv.at[dg], place.along)

        give(*order[0])
        give(*order[1])
        take(*order[0])
        give(*order[2])
        take(*order[1])
        give(*order[3])
        take(*order[2])
        take(*order[3])

    def second_copy(self, half, part):
        tokens = self.second.shape[1] // 2
        at = pl.ds(part * tokens, tokens)
        peer = self.place.across if half else self.place.along
        return 8 + 2 * part + half, self.second.at[half, at], self.second_recv.at[half, at], peer

    def run_second(self):
        place = self.place
        tokens = self.second.shape[1] // 2
        for part in (0, 1):
            for half, number, buffer, mine in ((0, 5, self.across_recv, 2), (1, 7, self.along_recv, 1)):
                if part == 0:
                    self.copy(number, buffer.at[1], buffer.at[1], place.core).wait_recv()

                def add_rows(at):
                    total = self.held[mine - 1, half, at, :].astype(F32) + buffer[1, at, :].astype(F32)
                    self.second[half, at, :] = total.astype(BF16)

                for_slices(part * tokens, (part + 1) * tokens, add_rows)
                self.start(*self.second_copy(half, part))

    def run_third(self, part):
        place = self.place
        if part == 0:
            for number, buffer in ((4, self.across_recv), (6, self.along_recv)):
                self.copy(number, buffer.at[0], buffer.at[0], place.core).wait_recv()
        for half in (0, 1):
            self.copy(*self.second_copy(half, part)).wait_recv()

    def rows(self, at):
        first = self.acc[0, at, :] + self.across_recv[0, at, :].astype(F32) + self.second_recv[0, at, :].astype(F32)
        last = self.acc[1, at, :] + self.along_recv[0, at, :].astype(F32) + self.second_recv[1, at, :].astype(F32)
        return jnp.concatenate([first, last], axis=1)

    def finish(self):
        for moved in self.kept:
            moved.wait_send()

    @staticmethod
    def scratch(tokens, width):
        half = width // 2
        return [
            pltpu.VMEM((4, 2, tokens, half), BF16),
            pltpu.VMEM((4, 2, tokens, half), BF16),
            pltpu.VMEM((3, 2, tokens, half), BF16),
            pltpu.VMEM((2, tokens, half), F32),
            pltpu.VMEM((2, tokens, half), BF16),
            pltpu.VMEM((2, tokens, half), BF16),
            pltpu.VMEM((2, tokens, half), BF16),
            pltpu.VMEM((2, tokens, half), BF16),
            pltpu.SemaphoreType.DMA((12,)),
            pltpu.SemaphoreType.DMA((12,)),
        ]


SCATTER_BUFFERS = 10


def pair_product(lefts, rights, tokens):
    def product(chunk, n):
        at = pl.ds(pl.multiple_of(chunk * tokens, tokens), tokens)
        cols = pl.ds(pl.multiple_of(n * 256, 256), 256)
        total = None
        for left, right in zip(lefts, rights):
            term = jnp.dot(left[at, :], right[:, cols], preferred_element_type=F32)
            total = term if total is None else total + term
        return total

    return product


def for_slices(start, stop, body):
    def step(n, none):
        body(pl.ds(pl.multiple_of(n * SLICE, SLICE), SLICE))
        return none

    lax.fori_loop(start // SLICE, stop // SLICE, step, 0)


def middle_kernel(left, right, own_in, gain, middle_out, gathered, *scratch):
    buffers, (block, send, recv) = scratch[:SCATTER_BUFFERS], scratch[SCATTER_BUFFERS:]
    tokens = own_in.shape[0]
    place = Place()
    place.greet()
    scatter = Scatter(place, pair_product([left], [right], tokens), *buffers)
    scatter.run_first()
    scatter.run_second()

    def body(at):
        middle = own_in[at, :].astype(F32) + scatter.rows(at)
        middle_out[at, :] = middle
        block[at, :] = (middle * rms(middle) * gain[...]).astype(BF16)

    gather = Gather(place, block, gathered, send, recv)
    for part in (0, 1):
        scatter.run_third(part)
        for_slices(part * tokens // 2, (part + 1) * tokens // 2, body)
        gather.begin(part)
    gather.pass_on()
    scatter.finish()
    gather.finish()


def turn_kernel(
    left0, left1, right0, right1, middle, gain, cot, normed_far, grad_middle_out, gain_out, grads_out, block_out, *scratch
):
    buffers, (normed, load) = scratch[:SCATTER_BUFFERS], scratch[SCATTER_BUFFERS:]
    loaded = pltpu.make_async_copy(normed_far, normed, load.at[0])
    loaded.start()
    tokens, hidden = cot.shape[0], left0.shape[1]
    place = Place()
    place.greet()
    scatter = Scatter(place, pair_product([left0, left1], [right0, right1], tokens), *buffers)
    scatter.run_first()
    scatter.run_second()
    loaded.wait()

    def weight_grads(n, none):
        at = pl.ds(pl.multiple_of(n * 256, 256), 256)
        for k, part in enumerate((left0, left1)):
            value = lax.dot_general(normed[:, at], part[...], (((0,), (0,)), ((), ())), preferred_element_type=F32)
            grads_out[at, k * hidden : (k + 1) * hidden] = value.astype(BF16)
        return none

    lax.fori_loop(0, normed.shape[1] // 256, weight_grads, 0)
    gain_out[...] = jnp.zeros_like(gain_out)

    def body(at):
        values = middle[at, :]
        grad = scatter.rows(at)
        scale = rms(values)
        weighted = grad * gain[...]
        inner = jnp.mean(values * weighted, axis=-1, keepdims=True)
        total = cot[at, :].astype(F32) + scale * weighted - values * (scale * scale * scale * inner)
        grad_middle_out[at, :] = total
        block_out[at, :] = total.astype(BF16)
        term = grad * values * scale
        gain_out[...] += term[0:8] + term[8:16]

    for part in (0, 1):
        scatter.run_third(part)
        for_slices(part * tokens // 2, (part + 1) * tokens // 2, body)
    scatter.finish()


def spread_kernel(block, w_out, mixed, mixed_out, out_grad, gathered, send, recv, chunk_ref, total, load):
    tokens = block.shape[0]
    place = Place()
    place.greet()
    gather = Gather(place, block, gathered, send, recv)
    gather.begin_whole()
    total[...] = jnp.zeros_like(total)

    def fetch(slot, chunk):
        at = pl.ds(pl.multiple_of(chunk * tokens, tokens), tokens)
        copy = pltpu.make_async_copy(gathered.at[at], chunk_ref.at[slot], load.at[slot])
        copy.start()
        return copy, slot, chunk

    def use(fetched):
        copy, slot, chunk = fetched
        copy.wait()
        use_chunk(chunk_ref.at[slot], chunk)

    def use_chunk(values, chunk):
        at = pl.ds(pl.multiple_of(chunk * tokens, tokens), tokens)
        mixed_out[at, :] = lax.dot_general(values[...], w_out[...], (((1,), (1,)), ((), ())), preferred_element_type=F32)
        part = mixed[at, :]

        def rows(n, none):
            columns = pl.ds(pl.multiple_of(n * 256, 256), 256)
            turned = (((0,), (0,)), ((), ()))
            total[columns, :] += lax.dot_general(values[:, columns], part, turned, preferred_element_type=F32)
            return none

        lax.fori_loop(0, values.shape[1] // 256, rows, 0)

    use_chunk(block, place.chunk(0, 0, 0))
    gather.pass_first()
    gather.finish_core()
    ahead = fetch(0, place.chunk(0, 0, 1))
    use(ahead)
    gather.pass_second()
    ahead = fetch(0, place.chunk(0, 1, 0))
    after = fetch(1, place.chunk(1, 0, 0))
    use(ahead)
    gather.finish_near()
    ahead = fetch(0, place.chunk(0, 1, 1))
    use(after)
    gather.pass_third()
    after = fetch(1, place.chunk(1, 0, 1))
    use(ahead)
    ahead = fetch(0, place.chunk(1, 1, 0))
    use(after)
    gather.finish_far()
    after = fetch(1, place.chunk(1, 1, 1))
    use(ahead)
    use(after)
    out_grad[...] = total[...].astype(BF16)
    gather.finish_sends()


class Owners:
    def __init__(self, place, reduced, out, send, recv):
        self.place, self.reduced, self.out, self.send, self.recv = place, reduced, out, send, recv
        self.own = place.chunk(0, 0, 0)

    def copy(self, number, offset, slot):
        return pltpu.make_async_remote_copy(
            src_ref=self.reduced.at[self.place.chunk(*offset)],
            dst_ref=self.out.at[slot],
            send_sem=self.send.at[number],
            recv_sem=self.recv.at[number],
            device_id=self.place.peer(*offset),
            device_id_type=MESH,
        )

    def begin(self):
        self.keep = pltpu.make_async_copy(self.reduced.at[self.own], self.out.at[self.own], self.send.at[7])
        self.keep.start()
        self.moved = [self.copy(number, offset, self.own) for number, offset in enumerate(OTHERS)]
        for copy in self.moved:
            copy.start()

    def finish(self):
        for number, offset in enumerate(OTHERS):
            self.copy(number, offset, self.place.chunk(*offset)).wait_recv()
        for copy in self.moved:
            copy.wait_send()
        self.keep.wait()


OWNERS_SCRATCH = [pltpu.SemaphoreType.DMA((8,))] * 2
BEYOND = [offset for offset in OTHERS if sum(offset) > 1]


class GateSums:
    def __init__(self, place, count, pieces, rows_recv, gates_all, send, recv):
        self.place, self.count, self.pieces = place, count, pieces
        self.rows_recv, self.gates_all, self.send, self.recv = rows_recv, gates_all, send, recv
        self.me = lax.axis_index("t")
        self.rank = place.g * 2 + place.c
        self.near = [offset for offset in OTHERS if not offset[0]]
        self.moved = []

    def copy(self, number, source, target, peer):
        return pltpu.make_async_remote_copy(
            src_ref=source,
            dst_ref=target,
            send_sem=self.send.at[number],
            recv_sem=self.recv.at[number],
            device_id=peer,
            device_id_type=MESH,
        )

    def begin(self):
        for number, offset in enumerate(self.near):
            other = lax.rem(self.place.chunk(*offset), 4)
            self.moved.append(self.copy(number, self.pieces.at[other], self.rows_recv.at[self.rank], self.place.peer(*offset)))
            self.moved[-1].start()
        self.rows_recv[self.rank] = self.pieces[self.rank]

    def pass_on(self):
        for number, offset in enumerate(self.near):
            other = lax.rem(self.place.chunk(*offset), 4)
            self.copy(number, self.pieces.at[other], self.rows_recv.at[other], self.place.peer(*offset)).wait_recv()
        for step in range(1, self.count):
            to = lax.rem(self.me + step, self.count)
            self.moved.append(self.copy(2 + step, self.rows_recv.at[to], self.gates_all.at[self.me], {"t": to}))
            self.moved[-1].start()
        self.gates_all[self.me] = self.rows_recv[self.me]

    def finish(self, out):
        for step in range(1, self.count):
            other = lax.rem(self.me + self.count - step, self.count)
            self.copy(2 + step, self.rows_recv.at[other], self.gates_all.at[other], {"t": other}).wait_recv()
        total = self.gates_all[0].astype(F32)
        for z in range(1, self.count):
            total = total + self.gates_all[z].astype(F32)
        out[...] = total
        for copy in self.moved:
            copy.wait_send()


class SmallSum:
    def __init__(self, place, count, values, inbox, plane_sum, plane_box, send, recv):
        self.place, self.count, self.values, self.inbox = place, count, values, inbox
        self.plane_sum, self.plane_box, self.send, self.recv = plane_sum, plane_box, send, recv
        self.me = lax.axis_index("t")
        self.moved = []

    def copy(self, number, source, target, peer):
        return pltpu.make_async_remote_copy(
            src_ref=source,
            dst_ref=target,
            send_sem=self.send.at[number],
            recv_sem=self.recv.at[number],
            device_id=peer,
            device_id_type=MESH,
        )

    def begin(self):
        own = self.place.chunk(0, 0, 0)
        for number, offset in enumerate(OTHERS):
            self.moved.append(self.copy(number, self.values, self.inbox.at[own], self.place.peer(*offset)))
            self.moved[-1].start()
        self.inbox[own] = self.values[...]

    def pass_on(self):
        for number, offset in enumerate(OTHERS):
            slot = self.inbox.at[self.place.chunk(*offset)]
            self.copy(number, self.values, slot, self.place.peer(*offset)).wait_recv()
        total = self.inbox[0]
        for n in range(1, 8):
            total = total + self.inbox[n]
        self.plane_sum[...] = total
        self.plane_box[self.me] = total
        for step in range(1, self.count):
            to = {"t": lax.rem(self.me + step, self.count)}
            self.moved.append(self.copy(6 + step, self.plane_sum, self.plane_box.at[self.me], to))
            self.moved[-1].start()

    def finish(self, out):
        for step in range(1, self.count):
            other = lax.rem(self.me + self.count - step, self.count)
            self.copy(6 + step, self.plane_sum, self.plane_box.at[other], {"t": other}).wait_recv()
        total = self.plane_box[0]
        for z in range(1, self.count):
            total = total + self.plane_box[z]
        out[...] = total
        for sent in self.moved:
            sent.wait_send()


def final_kernel(
    left, right, own_in, gain, mlp_gains, grad_middle, reduced, grad_out, values_out, owned,
    gain_sum, own_send, own_recv, *buffers,
):
    tokens, width = own_in.shape
    place = Place()
    place.greet([place.peer(*offset) for offset in BEYOND])
    scatter = Scatter(place, pair_product([left], [right], tokens), *buffers)
    owners = Owners(place, reduced, owned, own_send, own_recv)
    scatter.run_first()
    owners.begin()
    scatter.run_second()
    gain_sum[...] = jnp.zeros_like(gain_sum)

    def body(at):
        x = own_in[at, :].astype(F32)
        grad = scatter.rows(at)
        scale = rms(x)
        weighted = grad * gain[...]
        inner = jnp.mean(x * weighted, axis=-1, keepdims=True)
        grad_out[at, :] = grad_middle[at, :] + scale * weighted - x * (scale * scale * scale * inner)
        term = grad * x * scale
        gain_sum[...] += term[0:8] + term[8:16]

    for part in (0, 1):
        scatter.run_third(part)
        for_slices(part * tokens // 2, (part + 1) * tokens // 2, body)
    lines = width // LANES
    for base, row in ((0, jnp.sum(mlp_gains[...], axis=0, keepdims=True)), (lines, jnp.sum(gain_sum[...], axis=0, keepdims=True))):
        for n in range(lines):
            values_out[base + n : base + n + 1, :] = row[:, n * LANES : (n + 1) * LANES]
    owners.finish()
    scatter.finish()


def final_step(left, right, own_in, gain, mlp_gains, grad_middle, reduced):
    tokens, width = own_in.shape
    return pl.pallas_call(
        final_kernel,
        name="final_step",
        out_shape=(
            jax.ShapeDtypeStruct((tokens, width), F32),
            jax.ShapeDtypeStruct((2 * width // LANES, LANES), F32),
            jax.ShapeDtypeStruct(reduced.shape, reduced.dtype),
        ),
        in_specs=[*whole(6), ANYWHERE],
        out_specs=(*whole(2), ANYWHERE),
        scratch_shapes=[pltpu.VMEM((8, width), F32), *OWNERS_SCRATCH, *Scatter.scratch(tokens, width)],
        compiler_params=mixer_params(7),
    )(left, right, own_in, gain[None], mlp_gains, grad_middle, reduced)


def owners_kernel(
    count, with_gates, pieces, values, reduced0, reduced1, gates_out, gains_out, out0, out1,
    inbox, plane_sum, plane_box, sum_send, sum_recv, rows_recv, gates_all, gates_send, gates_recv,
    send0, recv0, send1, recv1,
):
    place = Place()
    me = lax.axis_index("t")
    place.greet([place.peer(*offset) for offset in BEYOND] + [{"t": lax.rem(me + step, count)} for step in range(1, count)])
    owners = [Owners(place, reduced0, out0, send0, recv0), Owners(place, reduced1, out1, send1, recv1)]
    gates = GateSums(place, count, pieces, rows_recv, gates_all, gates_send, gates_recv)
    gains = SmallSum(place, count, values, inbox, plane_sum, plane_box, sum_send, sum_recv)
    gains.begin()
    if with_gates:
        gates.begin()
    for part in owners:
        part.begin()
    gains.pass_on()
    if with_gates:
        gates.pass_on()
    gains.finish(gains_out)
    if with_gates:
        gates.finish(gates_out)
    else:
        gates_out[...] = jnp.zeros_like(gates_out)
    for part in owners:
        part.finish()


def owners_step(planes, with_gates, pieces, values, reduced):
    block = pieces.shape[1:]
    slots = planes if with_gates else 1
    return pl.pallas_call(
        functools.partial(owners_kernel, planes, with_gates),
        name="owners_step",
        out_shape=(
            jax.ShapeDtypeStruct(block, F32),
            jax.ShapeDtypeStruct(values.shape, F32),
            *[jax.ShapeDtypeStruct(part.shape, part.dtype) for part in reduced],
        ),
        in_specs=[*whole(2), ANYWHERE, ANYWHERE],
        out_specs=(*whole(2), ANYWHERE, ANYWHERE),
        scratch_shapes=[
            pltpu.VMEM((8, *values.shape), F32),
            pltpu.VMEM(values.shape, F32),
            pltpu.VMEM((planes, *values.shape), F32),
            pltpu.SemaphoreType.DMA((planes + 6,)),
            pltpu.SemaphoreType.DMA((planes + 6,)),
            pltpu.VMEM((slots, *block), BF16),
            pltpu.VMEM((slots, *block), BF16),
            pltpu.SemaphoreType.DMA((planes + 2,)),
            pltpu.SemaphoreType.DMA((planes + 2,)),
            *OWNERS_SCRATCH,
            *OWNERS_SCRATCH,
        ],
        compiler_params=mixer_params(8),
    )(pieces, values, *reduced)


def place_kernel(planes, hidden, outs, through, *refs):
    count = len(outs)
    given, passed, results, copied = refs[:count], refs[count : count + through], refs[count + through : 2 * count + through], refs[2 * count + through :]
    copies = [pltpu.make_async_copy(passed[n], copied[n], copied[-1].at[n]) for n in range(through)]
    for copy in copies:
        copy.start()
    for count, sources, out in zip(outs, given, results):
        piece = sources.shape[2] // (count * (planes if hidden else 1))
        for k in range(count):
            if hidden:
                groups = [
                    ((t * 2 + i) * 4 * piece, [(i * 4 + r, (k * planes + t) * piece) for r in range(4)])
                    for t in range(planes)
                    for i in range(2)
                ]
            else:
                groups = [(r * 2 * piece, [(i * 4 + r, k * piece) for i in range(2)]) for r in range(4)]
            for start, parts in groups:
                row = jnp.concatenate([sources[p, :, at : at + piece].astype(F32) for p, at in parts], axis=1)
                if count > 1:
                    out[:, k, start : start + row.shape[1]] = row
                else:
                    out[:, start : start + row.shape[1]] = row
    for copy in copies:
        copy.wait()


def place_columns(planes, hidden, outs, owned, through=()):
    members, own_rows, columns = owned[0].shape
    total = columns * members // outs[0]
    shapes = [(own_rows, count, total) if count > 1 else (own_rows, total) for count in outs]
    return pl.pallas_call(
        functools.partial(place_kernel, planes, hidden, outs, len(through)),
        name="place_columns",
        out_shape=(
            *[jax.ShapeDtypeStruct(shape, F32) for shape in shapes],
            *[jax.ShapeDtypeStruct(part.shape, part.dtype) for part in through],
        ),
        in_specs=[*whole(len(owned)), *[ANYWHERE] * len(through)],
        out_specs=(*whole(len(outs)), *[ANYWHERE] * len(through)),
        scratch_shapes=[pltpu.SemaphoreType.DMA((len(through),))] if through else [],
        compiler_params=pltpu.CompilerParams(vmem_limit_bytes=60 * 1024 * 1024),
    )(*owned, *through)


def first_gather(planes, normed, ids):
    tokens, width = normed.shape
    every = (8, *ids.shape)
    return pl.pallas_call(
        functools.partial(first_gather_kernel, planes),
        name="first_gather",
        out_shape=(jax.ShapeDtypeStruct((8 * tokens, width), BF16), *[jax.ShapeDtypeStruct(every, F32)] * 3),
        in_specs=[ANYWHERE, *whole(1)],
        out_specs=(ANYWHERE, *whole(3)),
        scratch_shapes=[pltpu.VMEM(every, F32)] * 3 + GATHER_SCRATCH + [pltpu.SemaphoreType.DMA((9,))] * 2,
        compiler_params=mixer_params(3),
    )(normed, ids)


def middle_step(mixed, w_out, own_in, gain):
    tokens, width = own_in.shape
    return pl.pallas_call(
        middle_kernel,
        name="middle_step",
        out_shape=(jax.ShapeDtypeStruct((tokens, width), F32), jax.ShapeDtypeStruct((8 * tokens, width), BF16)),
        in_specs=whole(4),
        out_specs=(pl.BlockSpec(memory_space=pltpu.VMEM), ANYWHERE),
        scratch_shapes=Scatter.scratch(tokens, width) + [pltpu.VMEM((tokens, width), BF16)] + GATHER_SCRATCH,
        compiler_params=mixer_params(4),
    )(mixed, w_out, own_in, gain[None])


def turn_step(left0, left1, right0, right1, middle, gain, cot, normed):
    tokens, width = cot.shape
    return pl.pallas_call(
        turn_kernel,
        name="turn_step",
        out_shape=(
            jax.ShapeDtypeStruct((tokens, width), F32),
            jax.ShapeDtypeStruct((8, width), F32),
            jax.ShapeDtypeStruct((width, 2 * left1.shape[1]), BF16),
            jax.ShapeDtypeStruct((tokens, width), BF16),
        ),
        in_specs=[*whole(7), ANYWHERE],
        out_specs=tuple(whole(4)),
        scratch_shapes=Scatter.scratch(tokens, width)
        + [pltpu.VMEM(normed.shape, BF16), pltpu.SemaphoreType.DMA((1,))],
        compiler_params=mixer_params(5),
    )(left0, left1, right0, right1, middle, gain[None], cot, normed)


def spread_step(block, w_out, mixed):
    tokens, width = block.shape
    return pl.pallas_call(
        spread_kernel,
        name="turn_spread",
        out_shape=(
            jax.ShapeDtypeStruct((8 * tokens, w_out.shape[0]), F32),
            jax.ShapeDtypeStruct((width, w_out.shape[0]), BF16),
            jax.ShapeDtypeStruct((8 * tokens, width), BF16),
        ),
        in_specs=whole(3),
        out_specs=(*whole(2), ANYWHERE),
        scratch_shapes=GATHER_SCRATCH
        + [
            pltpu.VMEM((2, tokens, width), BF16),
            pltpu.VMEM((width, w_out.shape[0]), F32),
            pltpu.SemaphoreType.DMA((2,)),
        ],
        compiler_params=mixer_params(10),
    )(block, w_out, mixed)


class Swap:
    def __init__(self, quarters, out, send, recv):
        self.quarters, self.out, self.send, self.recv = quarters, out, send, recv
        self.groups = quarters.shape[0]
        self.me = lax.axis_index("g") * 2 + lax.axis_index("c")

    def copy(self, step, other, slot):
        return pltpu.make_async_remote_copy(
            src_ref=self.quarters.at[other],
            dst_ref=self.out.at[:, slot],
            send_sem=self.send.at[step],
            recv_sem=self.recv.at[step],
            device_id={"g": other // 2, "c": other % 2},
            device_id_type=MESH,
        )

    def peers(self):
        others = [lax.rem(self.me + step, self.groups) for step in range(1, self.groups)]
        return [{"g": other // 2, "c": other % 2} for other in others]

    def begin(self):
        self.keep = pltpu.make_async_copy(self.quarters.at[self.me], self.out.at[:, self.me], self.send.at[0])
        self.keep.start()
        self.moved = []
        for step in range(1, self.groups):
            self.moved.append(self.copy(step, lax.rem(self.me + step, self.groups), self.me))
            self.moved[-1].start()

    def finish(self):
        for step in range(1, self.groups):
            other = lax.rem(self.me + self.groups - step, self.groups)
            self.copy(step, other, other).wait_recv()
        for copy in self.moved:
            copy.wait_send()
        self.keep.wait()


def swap_scratch(groups):
    return [pltpu.SemaphoreType.DMA((groups,)), pltpu.SemaphoreType.DMA((groups,))]


def swap_kernel(quarters, out, send, recv):
    move = Swap(quarters, out, send, recv)
    barrier = pltpu.get_barrier_semaphore()
    for peer in move.peers():
        pl.semaphore_signal(barrier, inc=1, device_id=peer, device_id_type=MESH)
    pl.semaphore_wait(barrier, move.groups - 1)
    move.begin()
    move.finish()


def swap(quarters):
    groups, kinds, part, width = quarters.shape
    return pl.pallas_call(
        swap_kernel,
        name="swap",
        out_shape=jax.ShapeDtypeStruct((kinds, groups, part, width), quarters.dtype),
        in_specs=[ANYWHERE],
        out_specs=ANYWHERE,
        scratch_shapes=swap_scratch(groups),
        compiler_params=mixer_params(6),
    )(quarters)


def rms(values):
    return lax.rsqrt(jnp.mean(values * values, axis=-1, keepdims=True) + EPS)


def nt(left, right, out):
    return lax.dot_general(left, right, (((1,), (1,)), ((), ())), preferred_element_type=F32).astype(out)


def tn(left, right, out):
    return lax.dot_general(left, right, (((0,), (0,)), ((), ())), preferred_element_type=F32).astype(out)


def nn(left, right, out):
    return jnp.dot(left, right, preferred_element_type=F32).astype(out)


def per_device(
    inputs, segment_ids, mix_gain, in_weight, conv_weight, conv_bias, gate_weight, gate_bias, decay_param, out_weight,
    mlp_gain, mlp_in, down_weight, cotangent,
):
    planes = lax.axis_size("t")
    rows_here, seg, width = inputs.shape
    row_groups = lax.axis_size("g") * lax.axis_size("c")
    own_tokens = rows_here * seg
    recur_width = conv_weight.shape[1]
    block_width = gate_weight.shape[0]
    members = 2 * row_groups
    channels = recur_width // members
    t, i = lax.axis_index("t"), lax.axis_index("i")
    r = lax.axis_index("g") * lax.axis_size("c") + lax.axis_index("c")
    member = 2 * r + i
    first = member * channels
    own_rows = width // (planes * members)

    own_in = inputs.reshape(own_tokens, width)
    flat_in = own_in.astype(F32)
    scale_in = rms(flat_in)
    cot_own = cotangent.reshape(own_tokens, width)
    own_ids = jnp.pad((segment_ids + 1).astype(F32), ((0, 8 - rows_here), (0, 0)))

    normed, *ids = first_gather(planes, (flat_in * scale_in * mix_gain).astype(BF16), own_ids)
    late_r, ids[0] = lax.optimization_barrier((r, ids[0]))

    direct = planes == row_groups
    in_own = in_weight.transpose(1, 2, 0)
    out_own = out_weight.T[None]
    part = channels // row_groups if direct else 0

    def quarter(weight, part, rank=r):
        return lax.dynamic_slice_in_dim(weight, rank * part, part, weight.ndim - 1)

    def spread_units(weight):
        return lax.all_gather(weight, "t", axis=0, tiled=False)

    def whole_units(weight):
        every = lax.all_gather(weight, ("t", "i"), axis=1, tiled=True)
        return lax.dynamic_slice_in_dim(every, first, channels, 1)

    if direct:
        in_w = swap(spread_units(quarter(in_weight, part).transpose(1, 2, 0)))
        out_quarters = spread_units(quarter(out_weight, part).T[None])
    else:
        in_w = whole_units(in_own)
        out_quarters = jnp.zeros((row_groups, 1, 16, width), BF16)
    in_w = in_w.reshape(2 * channels, width)
    hidden_part = mlp_in.shape[2] // row_groups
    gated = quarter(mlp_in, hidden_part, late_r).transpose(1, 2, 0)
    w_left, w_right, w_down = [
        spread_units(part).reshape(-1, width)
        for part in (gated[0], gated[1], quarter(down_weight, hidden_part, late_r).T)
    ]

    def own(values):
        return lax.dynamic_slice_in_dim(values, first, channels, values.ndim - 1)

    vec = own(
        jnp.concatenate(
            [
                conv_weight,
                conv_bias[None],
                gate_bias,
                8.0 * jax.nn.softplus(-decay_param)[None],
                8.0 * jax.nn.sigmoid(-decay_param)[None],
                jnp.zeros((7, recur_width), F32),
            ]
        )
    )
    gate_blocks = own(gate_weight).transpose(1, 0, 2)
    blocks = channels // block_width

    branches = nt(normed, in_w, F32)
    conv_low, decay, states, mixed, halo, cin, mask, cot, w_out = mixer_forward(
        planes, seg, rows_here, branches, ids, gate_blocks, vec, cot_own, out_quarters
    )
    w_out = (w_out if direct else whole_units(out_own)).reshape(channels, width)
    middle, normed_two = middle_step(mixed, w_out, own_in, mlp_gain)
    left = nt(normed_two, w_left, F32)
    right = nt(normed_two, w_right, F32)
    act, slope = gelu_parts(left)
    hidden = (act * right).astype(BF16)

    def over_planes(grad):
        return lax.psum_scatter(grad, "t", scatter_dimension=0, tiled=True)

    grad_down = tn(cot, hidden, BF16)
    grad_down, hidden, w_down = lax.optimization_barrier((grad_down, hidden, w_down))
    grad_down = over_planes(grad_down)
    grad_hidden = nt(cot, w_down, F32)
    grad_left = (grad_hidden * right * slope).astype(BF16)
    grad_right = (grad_hidden * act).astype(BF16)
    grad_middle, grad_mlp_gain, grad_mlp_in, grad_mid_own = turn_step(
        grad_left, grad_right, w_left, w_right, middle, mlp_gain, cot_own, normed_two
    )
    grad_down, grad_mid_own = lax.optimization_barrier((grad_down, grad_mid_own))
    grad_mlp_in = over_planes(grad_mlp_in)
    grad_mixed, grad_out, _ = spread_step(grad_mid_own, w_out, mixed)

    def by_owner(grad):
        return grad.reshape(members, own_rows, -1)

    grad_branches, gw0, gw1, small, pieces, outputs, owned_down = mixer_backward(
        planes, seg, grad_mixed, branches, states, decay, conv_low, mask, halo, cin, gate_blocks, vec, hidden, w_down, middle,
        by_owner(grad_down),
    )
    grad_mlp_in, grad_branches = lax.optimization_barrier((grad_mlp_in, grad_branches))
    grad_out = over_planes(grad_out)
    grad_in = tn(normed, grad_branches, BF16)
    grad_in, grad_branches = lax.optimization_barrier((grad_in, grad_branches))
    grad_in = over_planes(grad_in)
    outputs = outputs.reshape(inputs.shape)

    grad_inputs, values, owned_mlp_in = final_step(
        grad_branches, in_w, own_in, mix_gain, grad_mlp_gain, grad_middle, by_owner(grad_mlp_in)
    )
    gate_grads, gains, owned_in, owned_out = owners_step(planes, direct, pieces, values, [by_owner(grad_in), by_owner(grad_out)])
    grad_inputs = grad_inputs.reshape(inputs.shape)
    index = ((t * 2 + i) * row_groups + r) * own_rows
    gains = lax.dynamic_slice_in_dim(gains.reshape(2, width), index, own_rows, 1)


    def columns(hidden, outs, owned, through=()):
        if direct:
            return place_columns(planes, hidden, outs, owned, through)
        owned = jnp.concatenate(owned, axis=2)
        owned = owned.reshape(2, row_groups, own_rows, sum(outs), planes if hidden else 1, -1).astype(F32)
        order = (2, 3, 4, 0, 1, 5) if hidden else (2, 3, 1, 0, 4, 5)
        owned = owned.transpose(order).reshape(own_rows, sum(outs), -1)
        return (owned[:, :2], owned[:, 2], *through)

    grad_in_weight, grad_out_weight = columns(False, (2, 1), [owned_in, owned_out])
    grad_mlp_in, grad_down_weight, outputs, grad_inputs = columns(
        True, (2, 1), [owned_mlp_in, owned_down], [outputs, grad_inputs]
    )
    if direct:
        gate_grads = gate_grads[:, :part]
    else:
        column_block = lax.broadcasted_iota(jnp.int32, (block_width, channels), 1) // block_width

        def diagonal(gw):
            return sum(
                jnp.where(column_block == n, gw[n * block_width : (n + 1) * block_width], 0.0) for n in range(blocks)
            )

        gate_grads = jnp.concatenate([diagonal(gw0), diagonal(gw1), small], axis=0)
        placed = jnp.zeros((gate_grads.shape[0], recur_width), F32)
        placed = lax.dynamic_update_slice_in_dim(placed, gate_grads, first, 1)
        gate_grads = lax.psum_scatter(placed, EVERY, scatter_dimension=1, tiled=True)
    grad_gate_weight = jnp.stack([gate_grads[:block_width], gate_grads[block_width : 2 * block_width]], axis=1)
    small = gate_grads[2 * block_width : 2 * block_width + 8]
    return (
        outputs,
        grad_inputs,
        gains[1],
        grad_in_weight,
        small[0:4],
        small[4],
        grad_gate_weight,
        small[5:7],
        small[7],
        grad_out_weight,
        gains[0],
        grad_mlp_in,
        grad_down_weight,
    )


def solution(mesh):
    seq, rows = mesh.shape["seq"], mesh.shape["rows"]
    grid = Mesh(mesh.devices.reshape(seq // 2, 2, rows // 2, 2), EVERY)
    row_axes, seq_axes = ("g", "c"), ("t", "i")
    tokens = P(row_axes, seq_axes, None)
    return jax.shard_map(
        per_device,
        mesh=grid,
        in_specs=(
            tokens,
            P(row_axes, seq_axes),
            P(),
            P(None, None, seq_axes),
            P(),
            P(),
            P(),
            P(),
            P(),
            P(None, seq_axes),
            P(),
            P(None, None, seq_axes),
            P(None, seq_axes),
            tokens,
        ),
        out_specs=(
            tokens,
            tokens,
            P(EVERY),
            P(EVERY, None, None),
            P(None, EVERY),
            P(EVERY),
            P(None, None, EVERY),
            P(None, EVERY),
            P(EVERY),
            P(EVERY, None),
            P(EVERY),
            P(EVERY, None, None),
            P(EVERY, None),
        ),
        check_vma=False,
    )
```

```python
import functools

import jax
import jax.numpy as jnp
from jax import lax
from jax.experimental import pallas as pl
from jax.experimental.pallas import tpu as pltpu
from jax.sharding import Mesh
from jax.sharding import PartitionSpec as P

EPS = 1e-06
MESH = pl.DeviceIdType.MESH
PLANE = ("i", "g", "c")
EVERY = ("t", "i", "g", "c")
F32 = jnp.float32
BF16 = jnp.bfloat16
GELU_A = 0.7978845608028654
GELU_B = 0.044715
HALO = 8
LANES = 128
SLICE = 16
ANYWHERE = pl.BlockSpec(memory_space=pl.ANY)
GATHER_SCRATCH = [pltpu.SemaphoreType.DMA((14,))] * 2


def gelu_parts(x):
    square = x * x
    th = jnp.tanh(GELU_A * x * (1.0 + GELU_B * square))
    half = 0.5 * (1.0 + th)
    slope = half + 0.5 * x * (1.0 - th * th) * (GELU_A * (1.0 + 3.0 * GELU_B * square))
    return x * half, slope


def one_minus_exp(y, power):
    series = 1.0 + y * (-1.0 / 2 + y * (1.0 / 6 + y * (-1.0 / 24 + y * (1.0 / 120 + y * (-1.0 / 720 + y * (1.0 / 5040))))))
    return jnp.where(y < 0.35, y * series, 1.0 - power)


def sigmoid(x):
    return 1.0 / (1.0 + jnp.exp(-x))


def gate_values(conv_low, wg0, wg1, vec):
    logits0 = jnp.dot(conv_low, wg0, preferred_element_type=F32) + vec[5:6]
    logits1 = jnp.dot(conv_low, wg1, preferred_element_type=F32) + vec[6:7]
    recur_gate = sigmoid(logits0)
    input_gate = sigmoid(logits1)
    log_decay = -vec[7:8] * recur_gate
    return recur_gate, input_gate, log_decay


def spread_blocks(gates, out):
    size, width = gates.shape[1], gates.shape[2]
    column = lax.broadcasted_iota(jnp.int32, (size, width), 1) // size
    for k in range(2):
        block = gates[k].astype(F32)
        for n in range(width // size):
            out[k, n * size : (n + 1) * size, :] = jnp.where(column == n, block, 0.0).astype(BF16)


def put_tiles(ref, at, values):
    tiles, lanes = ref.shape[0], ref.shape[2]
    short = tiles * lanes - values.shape[1]
    if short:
        values = jnp.concatenate([values, jnp.zeros((values.shape[0], short), values.dtype)], axis=1)
    for j in range(tiles):
        ref[j, at, :] = values[:, j * lanes : (j + 1) * lanes]


def get_tiles(ref, at, width):
    joined = jnp.concatenate([ref[j, at, :] for j in range(ref.shape[0])], axis=1)
    return joined[:, :width]


def join_tiles(parts, width):
    return jnp.concatenate(parts, axis=1)[:, :width]


def exchange_copy(step, send, target, other, send_sem, recv_sem):
    return pltpu.make_async_remote_copy(
        src_ref=send,
        dst_ref=target,
        send_sem=send_sem.at[step],
        recv_sem=recv_sem.at[step],
        device_id={"t": other},
        device_id_type=MESH,
    )


def exchange_start(count, me, send, slots, send_sem, recv_sem):
    for step in range(1, count):
        exchange_copy(step, send, slots.at[me], lax.rem(me + step, count), send_sem, recv_sem).start()


def exchange_wait(count, me, send, slots, send_sem, recv_sem):
    for step in range(1, count):
        other = lax.rem(me + count - step, count)
        exchange_copy(step, send, slots.at[other], other, send_sem, recv_sem).wait()


def mixer_forward_kernel(
    count, seg, rows_here, branches_far, ids, ids_before, ids_after, gate_blocks, vec_ref, cot, quarters,
    conv_out, decay_out, states_out, mixed_out, halo_out, cin_out, mask, cot_out, swapped,
    drive, h_ref, a_ref, ext, halo_send, halo_recv, summary, slots, send_sem, recv_sem, halo_sems,
    gather_send, gather_recv, swap_send, swap_recv, branches, wg, load,
):
    place = Place()
    me = lax.axis_index("t")
    loaded = pltpu.make_async_copy(branches_far, branches, load.at[0])
    loaded.start()
    place.greet([place.peer(0, 1, 1)] + [{"t": lax.rem(me + step, count)} for step in range(1, count)])
    gather = Gather(place, cot, cot_out, gather_send, gather_recv)
    move = Swap(quarters, swapped, swap_send, swap_recv)
    gather.begin_whole()
    move.begin()
    spread_blocks(gate_blocks, wg)
    rows = 8
    width = branches.shape[1] // 2
    loaded.wait()

    def recur_at(at):
        return branches[at, width:].astype(BF16).astype(F32)

    for r in range(rows):
        halo_send[r * HALO : (r + 1) * HALO, :] = recur_at(pl.ds((rows + r + 1) * seg - HALO, HALO))
    halo_copy = pltpu.make_async_remote_copy(
        src_ref=halo_send,
        dst_ref=halo_recv,
        send_sem=halo_sems.at[0],
        recv_sem=halo_sems.at[1],
        device_id={"t": lax.rem(me + 1, count)},
        device_id_type=MESH,
    )
    halo_copy.start()
    for r in range(rows):
        halo_out[(rows + r) * HALO : (rows + r + 1) * HALO, :] = recur_at(pl.ds((r + 1) * seg - HALO, HALO))
    vec = vec_ref[...]

    def ids_of(ref, s):
        chunk = s // rows_here
        return ref[chunk, s % rows_here : s % rows_here + 1, :]

    nothing = jnp.zeros((1, LANES), F32)
    for s in range(2 * rows):
        here = ids_of(ids, s)
        back = ids_of(ids, s - rows) if s >= rows else jnp.where(me > 0, ids_of(ids_before, s + rows), nothing)
        ahead = ids_of(ids, s + rows) if s < rows else jnp.where(me < count - 1, ids_of(ids_after, s - rows), nothing)
        lines = [jnp.concatenate([back[:, seg - k :], here[:, : seg - k]], axis=1) for k in (1, 2, 3)]
        lines += [jnp.concatenate([here[:, k:], ahead[:, :k]], axis=1) for k in (1, 2, 3)]
        lines = [jnp.where(line == here, 1.0, 0.0) for line in lines] + [nothing] * 2
        mask[s * seg : (s + 1) * seg, :] = jnp.concatenate(lines, axis=0).T

    def local(s, none):
        at = pl.ds(pl.multiple_of(s * seg, seg), seg)
        x = recur_at(at)
        ext[0:HALO, :] = halo_out[pl.ds(pl.multiple_of(s * HALO, HALO), HALO), :]
        ext[HALO : HALO + seg, :] = x
        m = mask[at, :]
        conv = vec[4:5] + vec[0:1] * x
        for k in range(1, 4):
            conv = conv + vec[k : k + 1] * ext[HALO - k : HALO - k + seg, :] * m[:, k - 1 : k]
        conv_low = conv.astype(BF16)
        conv_out[at, :] = conv_low
        recur_gate, input_gate, log_decay = gate_values(conv_low, wg[0], wg[1], vec)
        keep = m[:, 0:1]
        kept = jnp.exp(log_decay)
        put_tiles(decay_out, at, kept * keep)
        scale = (1.0 - keep) + keep * jnp.sqrt(one_minus_exp(-2.0 * log_decay, kept * kept))
        put_tiles(drive, at, scale * input_gate * conv_low.astype(F32))
        return none

    lax.fori_loop(rows, 2 * rows, local, 0)
    halo_copy.wait()
    for r in range(rows):
        halo_out[r * HALO : (r + 1) * HALO, :] = halo_recv[r * HALO : (r + 1) * HALO, :]
    gather.pass_first()
    lax.fori_loop(0, rows, local, 0)
    tiles, lanes = drive.shape[0], drive.shape[2]

    def scan(k, carried):
        at = pl.ds(k, 2 * rows, stride=seg)
        after = []
        for j in range(tiles):
            h, a = carried[j]
            d = decay_out[j, at, :]
            h = d * h + drive[j, at, :]
            a = a * d
            h_ref[j, at, :] = h
            a_ref[j, at, :] = a
            after.append((h, a))
        return tuple(after)

    start = (jnp.zeros((2 * rows, lanes), F32), jnp.ones((2 * rows, lanes), F32))
    last = lax.fori_loop(0, seg, scan, (start,) * tiles, unroll=4)
    last_h = join_tiles([part[0] for part in last], width)
    last_a = join_tiles([part[1] for part in last], width)
    summary[0:rows, :] = last_a[rows:] * last_a[:rows]
    summary[rows : 2 * rows, :] = last_a[rows:] * last_h[:rows] + last_h[rows:]
    exchange_start(count, me, summary, slots, send_sem, recv_sem)
    gather.pass_second()

    def activate(s, none):
        at = pl.ds(pl.multiple_of(s * seg, seg), seg)
        act, _ = gelu_parts(branches[at, :width])
        states_out[at, :] = act
        return none

    lax.fori_loop(0, 2 * rows, activate, 0)
    exchange_wait(count, me, summary, slots, send_sem, recv_sem)
    carry = jnp.zeros((rows, width), F32)
    for z in range(count - 1):
        carry = jnp.where(z < me, slots[z, 0:rows, :] * carry + slots[z, rows : 2 * rows, :], carry)
    cin_out[0:rows, :] = carry
    cin_out[rows : 2 * rows, :] = last_a[:rows] * carry + last_h[:rows]

    def finish(s, none):
        at = pl.ds(pl.multiple_of(s * seg, seg), seg)
        states = get_tiles(h_ref, at, width) + get_tiles(a_ref, at, width) * cin_out[pl.ds(s, 1), :]
        act = states_out[at, :]
        states_out[at, :] = states
        mixed_out[at, :] = (act * states.astype(BF16).astype(F32)).astype(BF16)
        return none

    lax.fori_loop(0, 2 * rows, finish, 0)
    gather.pass_third()
    gather.finish()
    move.finish()


def mixer_backward_kernel(
    count, seg, grad_mixed_far, branches_far, states_far, decay_far, conv_far, mask_far, halo, cin, gate_blocks, vec_ref,
    hidden, w_down, middle_far, reduced, grad_out, gw0_out, gw1_out, small_out, pieces_out, outputs, owned,
    tot, prod, ext, halo_send, halo_recv, summary, slots, uin, send_sem, recv_sem, halo_sems,
    grad_mixed, branches, states, decay, conv_low_ref, mask, middle, wg, load, own_send, own_recv, *buffers,
):
    place = Place()
    pairs = (
        (grad_mixed_far, grad_mixed),
        (branches_far, branches),
        (states_far, states),
        (decay_far, decay),
        (conv_far, conv_low_ref),
        (mask_far, mask),
        (middle_far, middle),
    )
    loads = [pltpu.make_async_copy(far, near, load.at[n]) for n, (far, near) in enumerate(pairs)]
    for part in loads:
        part.start()
    me = lax.axis_index("t")
    place.greet([place.peer(*offset) for offset in BEYOND] + [{"t": lax.rem(me + step, count)} for step in range(1, count)])
    scatter = Scatter(place, pair_product([hidden], [w_down], outputs.shape[0]), *buffers)
    owners = Owners(place, reduced, owned, own_send, own_recv)
    spread_blocks(gate_blocks, wg)
    scatter.run_first()
    owners.begin()
    for part in loads:
        part.wait()
    rows = 8
    width = branches.shape[1] // 2
    vec = vec_ref[...]

    def local(s, none):
        at = pl.ds(pl.multiple_of(s * seg, seg), seg)
        act, slope = gelu_parts(branches[at, :width])
        gm = grad_mixed[at, :].astype(F32)
        grad_out[at, :width] = (gm * states[at, :].astype(BF16).astype(F32) * slope).astype(BF16)
        put_tiles(tot, at, (gm * act).astype(BF16).astype(F32))
        return none

    lax.fori_loop(0, 2 * rows, local, 0)

    tiles, lanes = tot.shape[0], tot.shape[2]

    def scan(k, carried):
        at = pl.ds(seg - 1 - k, 2 * rows, stride=seg)
        after = []
        for j in range(tiles):
            u, p = carried[j]
            d = decay[j, at, :]
            total = tot[j, at, :] + u
            tot[j, at, :] = total
            prod[j, at, :] = p
            after.append((d * total, d * p))
        return tuple(after)

    start = (jnp.zeros((2 * rows, lanes), F32), jnp.ones((2 * rows, lanes), F32))
    last = lax.fori_loop(0, seg, scan, (start,) * tiles, unroll=4)
    u = join_tiles([part[0] for part in last], width)
    p = join_tiles([part[1] for part in last], width)
    summary[0:rows, :] = p[:rows] * p[rows:]
    summary[rows : 2 * rows, :] = p[:rows] * u[rows:] + u[:rows]
    exchange_start(count, me, summary, slots, send_sem, recv_sem)
    scatter.run_second()
    exchange_wait(count, me, summary, slots, send_sem, recv_sem)
    carry = jnp.zeros((rows, width), F32)
    for z in range(count - 1, 0, -1):
        carry = jnp.where(z > me, slots[z, 0:rows, :] * carry + slots[z, rows : 2 * rows, :], carry)
    uin[rows : 2 * rows, :] = carry
    uin[0:rows, :] = p[rows:] * carry + u[rows:]
    gw0_out[...] = jnp.zeros_like(gw0_out)
    gw1_out[...] = jnp.zeros_like(gw1_out)
    small_out[...] = jnp.zeros_like(small_out)

    def gates(s, none):
        at = pl.ds(pl.multiple_of(s * seg, seg), seg)
        total = get_tiles(tot, at, width) + get_tiles(prod, at, width) * uin[pl.ds(s, 1), :]
        ext[HALO - 1 : HALO, :] = cin[pl.ds(s, 1), :]
        ext[HALO : HALO + seg, :] = states[at, :]
        before = ext[HALO - 1 : HALO - 1 + seg, :]
        conv_low = conv_low_ref[at, :]
        conv_vals = conv_low.astype(F32)
        m = mask[at, :]
        keep = m[:, 0:1]
        recur_gate, input_gate, log_decay = gate_values(conv_low, wg[0], wg[1], vec)
        power = jnp.exp(2.0 * log_decay)
        gone = one_minus_exp(-2.0 * log_decay, power)
        inverse = lax.rsqrt(gone)
        root = gone * inverse
        scale = (1.0 - keep) + keep * root
        driven_in = total * conv_vals
        grad_log = total * before * get_tiles(decay, at, width) - driven_in * input_gate * keep * (power * inverse)
        grad0 = grad_log * log_decay * (1.0 - recur_gate)
        grad1 = driven_in * scale * input_gate * (1.0 - input_gate)
        low0 = grad0.astype(BF16)
        low1 = grad1.astype(BF16)
        inputs_of = (((1,), (1,)), ((), ()))
        grad_conv = (
            total * scale * input_gate
            + lax.dot_general(low0, wg[0], inputs_of, preferred_element_type=F32)
            + lax.dot_general(low1, wg[1], inputs_of, preferred_element_type=F32)
        )
        put_tiles(tot, at, grad_conv)
        turned = (((0,), (0,)), ((), ()))
        gw0_out[...] += lax.dot_general(conv_low, low0, turned, preferred_element_type=F32)
        gw1_out[...] += lax.dot_general(conv_low, low1, turned, preferred_element_type=F32)
        x = branches[at, width:].astype(BF16).astype(F32)
        ext[0:HALO, :] = halo[pl.ds(pl.multiple_of(s * HALO, HALO), HALO), :]
        ext[HALO : HALO + seg, :] = x

        def add(row, values):
            small_out[row : row + 1, :] += jnp.sum(values, axis=0, keepdims=True)

        add(0, grad_conv * x)
        for k in range(1, 4):
            add(k, grad_conv * ext[HALO - k : HALO - k + seg, :] * m[:, k - 1 : k])
        add(4, grad_conv)
        add(5, grad0)
        add(6, grad1)
        add(7, grad_log * recur_gate)
        return none

    lax.fori_loop(0, 2 * rows, gates, 0)
    small_out[7:8, :] = small_out[7:8, :] * vec[8:9]
    size, part = gate_blocks.shape[1], width // 4

    def padded(values):
        short = [values, jnp.zeros((values.shape[0], LANES - part), F32)]
        return jnp.concatenate(short, axis=1)

    for r in range(4):
        first = r * part // size * size
        at = slice(r * part, (r + 1) * part)
        for k, square in enumerate((gw0_out, gw1_out)):
            pieces_out[r, k * size : (k + 1) * size, :] = padded(square[first : first + size, at]).astype(BF16)
        rest = jnp.concatenate([padded(small_out[:, at]), jnp.zeros((8, LANES), F32)], axis=0)
        pieces_out[r, 2 * size :, :] = rest.astype(BF16)
    for r in range(rows):
        halo_send[r * HALO : (r + 1) * HALO, :] = get_tiles(tot, pl.ds(r * seg, HALO), width)
    halo_copy = pltpu.make_async_remote_copy(
        src_ref=halo_send,
        dst_ref=halo_recv,
        send_sem=halo_sems.at[0],
        recv_sem=halo_sems.at[1],
        device_id={"t": lax.rem(me + count - 1, count)},
        device_id_type=MESH,
    )
    halo_copy.start()

    def back(s, none):
        at = pl.ds(pl.multiple_of(s * seg, seg), seg)
        m = mask[at, :]
        grad_conv = get_tiles(tot, at, width)
        ext[0:seg, :] = grad_conv
        result = vec[0:1] * grad_conv

        @pl.when(s < rows)
        def _():
            ext[seg : seg + HALO, :] = get_tiles(tot, pl.ds(pl.multiple_of((s + rows) * seg, seg), HALO), width)

        @pl.when(s >= rows)
        def _():
            ext[seg : seg + HALO, :] = halo_recv[pl.ds(pl.multiple_of((s - rows) * HALO, HALO), HALO), :]

        for k in range(1, 4):
            result = result + vec[k : k + 1] * ext[k : k + seg, :] * m[:, 2 + k : 3 + k]
        grad_out[at, width:] = result.astype(BF16)
        return none

    lax.fori_loop(0, rows, back, 0)
    halo_copy.wait()
    lax.fori_loop(rows, 2 * rows, back, 0)
    scatter.run_third(0)
    scatter.run_third(1)

    def body(at):
        outputs[at, :] = (middle[at, :] + scatter.rows(at)).astype(BF16)

    for_slices(0, outputs.shape[0], body)
    scatter.finish()
    owners.finish()


def whole(count):
    return [pl.BlockSpec(memory_space=pltpu.VMEM)] * count


def mixer_params(number):
    return pltpu.CompilerParams(collective_id=number, has_side_effects=True, vmem_limit_bytes=60 * 1024 * 1024)


def mixer_forward(count, seg, rows_here, branches, ids, gate_blocks, vec, cot, quarters):
    n, width = branches.shape[0], branches.shape[1] // 2
    full = functools.partial(jax.ShapeDtypeStruct, (n, width))
    tiles = -(-width // LANES)
    tiled = jax.ShapeDtypeStruct((tiles, n, LANES), F32)
    groups, kinds, part, depth = quarters.shape
    return pl.pallas_call(
        functools.partial(mixer_forward_kernel, count, seg, rows_here),
        name="mixer_forward",
        out_shape=(
            full(BF16), tiled, full(F32), full(BF16),
            jax.ShapeDtypeStruct((16 * HALO, width), F32), jax.ShapeDtypeStruct((16, width), F32),
            jax.ShapeDtypeStruct((n, 8), F32),
            jax.ShapeDtypeStruct((8 * cot.shape[0], cot.shape[1]), BF16),
            jax.ShapeDtypeStruct((kinds, groups, part, depth), BF16),
        ),
        in_specs=[ANYWHERE, *whole(5), ANYWHERE, ANYWHERE],
        out_specs=(*whole(7), ANYWHERE, ANYWHERE),
        scratch_shapes=[
            pltpu.VMEM((tiles, n, LANES), F32),
            pltpu.VMEM((tiles, n, LANES), F32),
            pltpu.VMEM((tiles, n, LANES), F32),
            pltpu.VMEM((seg + HALO, width), F32),
            pltpu.VMEM((8 * HALO, width), F32),
            pltpu.VMEM((8 * HALO, width), F32),
            pltpu.VMEM((16, width), F32),
            pltpu.VMEM((count, 16, width), F32),
            pltpu.SemaphoreType.DMA((count,)),
            pltpu.SemaphoreType.DMA((count,)),
            pltpu.SemaphoreType.DMA((2,)),
            *GATHER_SCRATCH,
            *swap_scratch(groups),
            pltpu.VMEM(branches.shape, F32),
            pltpu.VMEM((2, width, width), BF16),
            pltpu.SemaphoreType.DMA((1,)),
        ],
        compiler_params=mixer_params(1),
    )(branches, *ids, gate_blocks, vec, cot, quarters)


def mixer_backward(count, seg, grad_mixed, branches, states, decay, conv_low, mask, halo, cin, gate_blocks, vec, hidden, w_down, middle, reduced):
    n, width = branches.shape[0], branches.shape[1] // 2
    tokens, depth = n // 8, w_down.shape[1]
    full = functools.partial(jax.ShapeDtypeStruct, (n, width))
    tiles = -(-width // LANES)
    tiled = jax.ShapeDtypeStruct((tiles, n, LANES), F32)
    return pl.pallas_call(
        functools.partial(mixer_backward_kernel, count, seg),
        name="mixer_backward",
        out_shape=(
            jax.ShapeDtypeStruct((n, 2 * width), BF16),
            jax.ShapeDtypeStruct((width, width), F32), jax.ShapeDtypeStruct((width, width), F32),
            jax.ShapeDtypeStruct((8, width), F32),
            jax.ShapeDtypeStruct((4, 2 * gate_blocks.shape[1] + 16, LANES), BF16),
            jax.ShapeDtypeStruct((tokens, depth), BF16),
            jax.ShapeDtypeStruct(reduced.shape, BF16),
        ),
        in_specs=[*[ANYWHERE] * 6, *whole(6), *[ANYWHERE] * 2],
        out_specs=(*whole(6), ANYWHERE),
        scratch_shapes=[
            pltpu.VMEM((tiles, n, LANES), F32),
            pltpu.VMEM((tiles, n, LANES), F32),
            pltpu.VMEM((seg + HALO, width), F32),
            pltpu.VMEM((8 * HALO, width), F32),
            pltpu.VMEM((8 * HALO, width), F32),
            pltpu.VMEM((16, width), F32),
            pltpu.VMEM((count, 16, width), F32),
            pltpu.VMEM((16, width), F32),
            pltpu.SemaphoreType.DMA((count,)),
            pltpu.SemaphoreType.DMA((count,)),
            pltpu.SemaphoreType.DMA((2,)),
            *[pltpu.VMEM(part.shape, part.dtype) for part in (grad_mixed, branches, states, decay, conv_low, mask, middle)],
            pltpu.VMEM((2, width, width), BF16),
            pltpu.SemaphoreType.DMA((7,)),
            *[pltpu.SemaphoreType.DMA((8,))] * 2,
            *Scatter.scratch(tokens, depth),
        ],
        compiler_params=mixer_params(2),
    )(grad_mixed, branches, states, decay, conv_low, mask, halo, cin, gate_blocks, vec, hidden, w_down, middle, reduced)


class Place:
    def __init__(self):
        self.i, self.g, self.c = lax.axis_index("i"), lax.axis_index("g"), lax.axis_index("c")
        self.core, self.across, self.along = {"c": 1 - self.c}, {"g": 1 - self.g}, {"i": 1 - self.i}

    def chunk(self, di, dg, dc):
        i = 1 - self.i if di else self.i
        g = 1 - self.g if dg else self.g
        c = 1 - self.c if dc else self.c
        return (i * 2 + g) * 2 + c

    def peer(self, di, dg, dc):
        return {
            "i": 1 - self.i if di else self.i,
            "g": 1 - self.g if dg else self.g,
            "c": 1 - self.c if dc else self.c,
        }

    def greet(self, more=()):
        barrier = pltpu.get_barrier_semaphore()
        peers = [self.core, self.across, self.along, *more]
        for peer in peers:
            pl.semaphore_signal(barrier, inc=1, device_id=peer, device_id_type=MESH)
        pl.semaphore_wait(barrier, len(peers))


class Gather:
    COPIES = 12

    def __init__(self, place, block, out, send, recv):
        self.place, self.block, self.out, self.send, self.recv = place, block, out, send, recv
        self.tokens = block.shape[0]
        self.half = self.tokens // 2

    def rows(self, chunk, part):
        start = chunk * self.tokens + (self.half if part == 1 else 0)
        return self.out.at[pl.ds(pl.multiple_of(start, self.half), self.tokens if part == 2 else self.half)]

    def mine(self, part):
        if part == 2:
            return self.block
        return self.block.at[pl.ds(part * self.half, self.half)]

    def copy(self, number, source, chunk, part, peer):
        return pltpu.make_async_remote_copy(
            src_ref=source,
            dst_ref=self.rows(chunk, part),
            send_sem=self.send.at[number],
            recv_sem=self.recv.at[number],
            device_id=peer,
            device_id_type=MESH,
        )

    def begin(self, part, whole=False):
        place = self.place
        own = place.chunk(0, 0, 0)
        other = 1 - part if whole else part
        self.give(0 + part, own, part, place.across)
        self.give(2 + other, own, other, place.along)
        self.give(4 + part, own, part, place.core)
        keep = pltpu.make_async_copy(self.mine(part), self.rows(own, part), self.send.at[self.COPIES + part])
        keep.start()
        self.local = getattr(self, "local", []) + [keep]

    def begin_whole(self):
        self.begin(0, True)
        self.begin(1, True)

    def give(self, number, chunk, part, peer):
        moved = self.copy(number, self.mine(part), chunk, part, peer)
        moved.start()
        self.kept = getattr(self, "kept", []) + [moved]

    def arrived(self, number, chunk, part):
        self.copy(number, self.rows(chunk, part), chunk, part, self.place.core).wait_recv()

    def forward(self, number, chunk, part, peer):
        moved = self.copy(number, self.rows(chunk, part), chunk, part, peer)
        moved.start()
        self.kept.append(moved)

    def pass_first(self):
        place = self.place
        ax, al = place.chunk(0, 1, 0), place.chunk(1, 0, 0)
        self.arrived(0, ax, 0)
        self.forward(6, ax, 0, place.along)
        self.arrived(3, al, 1)
        self.forward(7, al, 1, place.across)

    def pass_second(self):
        place = self.place
        ax, al = place.chunk(0, 1, 0), place.chunk(1, 0, 0)
        self.arrived(1, ax, 1)
        self.forward(8, ax, 2, place.core)
        self.arrived(2, al, 0)
        self.forward(9, al, 2, place.core)

    def pass_third(self):
        dia = self.place.chunk(1, 1, 0)
        self.arrived(6, dia, 0)
        self.forward(10, dia, 0, self.place.core)
        self.arrived(7, dia, 1)
        self.forward(11, dia, 1, self.place.core)

    def pass_on(self):
        self.pass_first()
        self.pass_second()
        self.pass_third()

    def finish_core(self):
        for part in (0, 1):
            self.arrived(4 + part, self.place.chunk(0, 0, 1), part)

    def finish_near(self):
        self.arrived(8, self.place.chunk(0, 1, 1), 2)
        self.arrived(9, self.place.chunk(1, 0, 1), 2)

    def finish_far(self):
        for part in (0, 1):
            self.arrived(10 + part, self.place.chunk(1, 1, 1), part)

    def finish(self):
        self.finish_core()
        self.finish_near()
        self.finish_far()
        self.finish_sends()

    def finish_sends(self):
        for moved in self.kept:
            moved.wait_send()
        for keep in self.local:
            keep.wait()


OTHERS = [(di, dg, dc) for di in (0, 1) for dg in (0, 1) for dc in (0, 1) if di or dg or dc]


def first_gather_kernel(count, normed, ids, normed_out, ids_out, before_out, after_out, plane_ids, before, after, send, recv, ids_send, ids_recv):
    place = Place()
    me = lax.axis_index("t")
    up, down = {"t": lax.rem(me + 1, count)}, {"t": lax.rem(me + count - 1, count)}
    place.greet([place.peer(*offset) for offset in OTHERS if sum(offset) > 1] + [up, down])
    gather = Gather(place, normed, normed_out, send, recv)
    own = place.chunk(0, 0, 0)
    moved = []

    def move(number, source, target, peer):
        copy = pltpu.make_async_remote_copy(
            src_ref=source,
            dst_ref=target,
            send_sem=ids_send.at[number],
            recv_sem=ids_recv.at[number],
            device_id=peer,
            device_id_type=MESH,
        )
        copy.start()
        moved.append(copy)

    for number, offset in enumerate(OTHERS):
        move(number, ids, plane_ids.at[own], place.peer(*offset))
    gather.begin_whole()
    plane_ids[own] = ids[...]
    for number, offset in enumerate(OTHERS):
        chunk = place.chunk(*offset)
        pltpu.make_async_remote_copy(
            src_ref=ids,
            dst_ref=plane_ids.at[chunk],
            send_sem=ids_send.at[number],
            recv_sem=ids_recv.at[number],
            device_id=place.peer(*offset),
            device_id_type=MESH,
        ).wait_recv()
    move(7, plane_ids, before, up)
    move(8, plane_ids, after, down)
    gather.pass_on()
    for copy in moved[7:]:
        copy.wait_recv()
    for copy in moved:
        copy.wait_send()
    ids_out[...] = plane_ids[...]
    before_out[...] = before[...]
    after_out[...] = after[...]
    gather.finish()


class Scatter:
    def __init__(self, place, product, core_send, core_recv, held, acc, across_recv, along_recv, second, second_recv, send, recv):
        self.place, self.product = place, product
        self.core_send, self.core_recv, self.held, self.acc = core_send, core_recv, held, acc
        self.across_recv, self.along_recv, self.second, self.second_recv = across_recv, along_recv, second, second_recv
        self.send, self.recv = send, recv
        self.kept = []

    def copy(self, number, source, target, peer):
        return pltpu.make_async_remote_copy(
            src_ref=source,
            dst_ref=target,
            send_sem=self.send.at[number],
            recv_sem=self.recv.at[number],
            device_id=peer,
            device_id_type=MESH,
        )

    def start(self, *parts):
        moved = self.copy(*parts)
        moved.start()
        self.kept.append(moved)

    def run_first(self):
        place = self.place
        order = ((1, 1), (0, 1), (1, 0), (0, 0))
        tile = 256
        per_half = self.held.shape[3] // tile
        def give(di, dg):
            q = 2 * di + dg
            chunk = place.chunk(di, dg, 1)

            def send_tile(n, none):
                at = pl.ds(pl.multiple_of(n % per_half * tile, tile), tile)
                self.core_send[q, n // per_half, :, at] = self.product(chunk, n).astype(BF16)
                return none

            lax.fori_loop(0, 2 * per_half, send_tile, 0)
            self.start(q, self.core_send.at[q], self.core_recv.at[q], place.core)

        def take(di, dg):
            q = 2 * di + dg
            chunk = place.chunk(di, dg, 0)
            self.copy(q, self.core_send.at[q], self.core_recv.at[q], place.core).wait_recv()

            def sum_tile(n, none):
                at = pl.ds(pl.multiple_of(n % per_half * tile, tile), tile)
                value = self.product(chunk, n) + self.core_recv[q, n // per_half, :, at].astype(F32)
                if q:
                    self.held[q - 1, n // per_half, :, at] = value.astype(BF16)
                else:
                    self.acc[n // per_half, :, at] = value
                return none

            lax.fori_loop(0, 2 * per_half, sum_tile, 0)
            if dg:
                self.start(4 + di, self.held.at[q - 1, 0], self.across_recv.at[di], place.across)
            if di:
                self.start(6 + dg, self.held.at[q - 1, 1], self.along_recv.at[dg], place.along)

        give(*order[0])
        give(*order[1])
        take(*order[0])
        give(*order[2])
        take(*order[1])
        give(*order[3])
        take(*order[2])
        take(*order[3])

    def second_copy(self, half, part):
        tokens = self.second.shape[1] // 2
        at = pl.ds(part * tokens, tokens)
        peer = self.place.across if half else self.place.along
        return 8 + 2 * part + half, self.second.at[half, at], self.second_recv.at[half, at], peer

    def run_second(self):
        place = self.place
        tokens = self.second.shape[1] // 2
        for part in (0, 1):
            for half, number, buffer, mine in ((0, 5, self.across_recv, 2), (1, 7, self.along_recv, 1)):
                if part == 0:
                    self.copy(number, buffer.at[1], buffer.at[1], place.core).wait_recv()

                def add_rows(at):
                    total = self.held[mine - 1, half, at, :].astype(F32) + buffer[1, at, :].astype(F32)
                    self.second[half, at, :] = total.astype(BF16)

                for_slices(part * tokens, (part + 1) * tokens, add_rows)
                self.start(*self.second_copy(half, part))

    def run_third(self, part):
        place = self.place
        if part == 0:
            for number, buffer in ((4, self.across_recv), (6, self.along_recv)):
                self.copy(number, buffer.at[0], buffer.at[0], place.core).wait_recv()
        for half in (0, 1):
            self.copy(*self.second_copy(half, part)).wait_recv()

    def rows(self, at):
        first = self.acc[0, at, :] + self.across_recv[0, at, :].astype(F32) + self.second_recv[0, at, :].astype(F32)
        last = self.acc[1, at, :] + self.along_recv[0, at, :].astype(F32) + self.second_recv[1, at, :].astype(F32)
        return jnp.concatenate([first, last], axis=1)

    def finish(self):
        for moved in self.kept:
            moved.wait_send()

    @staticmethod
    def scratch(tokens, width):
        half = width // 2
        return [
            pltpu.VMEM((4, 2, tokens, half), BF16),
            pltpu.VMEM((4, 2, tokens, half), BF16),
            pltpu.VMEM((3, 2, tokens, half), BF16),
            pltpu.VMEM((2, tokens, half), F32),
            pltpu.VMEM((2, tokens, half), BF16),
            pltpu.VMEM((2, tokens, half), BF16),
            pltpu.VMEM((2, tokens, half), BF16),
            pltpu.VMEM((2, tokens, half), BF16),
            pltpu.SemaphoreType.DMA((12,)),
            pltpu.SemaphoreType.DMA((12,)),
        ]


SCATTER_BUFFERS = 10


def pair_product(lefts, rights, tokens):
    def product(chunk, n):
        at = pl.ds(pl.multiple_of(chunk * tokens, tokens), tokens)
        cols = pl.ds(pl.multiple_of(n * 256, 256), 256)
        total = None
        for left, right in zip(lefts, rights):
            term = jnp.dot(left[at, :], right[:, cols], preferred_element_type=F32)
            total = term if total is None else total + term
        return total

    return product


def for_slices(start, stop, body):
    def step(n, none):
        body(pl.ds(pl.multiple_of(n * SLICE, SLICE), SLICE))
        return none

    lax.fori_loop(start // SLICE, stop // SLICE, step, 0)


def middle_kernel(left, right, own_in, gain, middle_out, gathered, *scratch):
    buffers, (block, send, recv) = scratch[:SCATTER_BUFFERS], scratch[SCATTER_BUFFERS:]
    tokens = own_in.shape[0]
    place = Place()
    place.greet()
    scatter = Scatter(place, pair_product([left], [right], tokens), *buffers)
    scatter.run_first()
    scatter.run_second()

    def body(at):
        middle = own_in[at, :].astype(F32) + scatter.rows(at)
        middle_out[at, :] = middle
        block[at, :] = (middle * rms(middle) * gain[...]).astype(BF16)

    gather = Gather(place, block, gathered, send, recv)
    for part in (0, 1):
        scatter.run_third(part)
        for_slices(part * tokens // 2, (part + 1) * tokens // 2, body)
        gather.begin(part)
    gather.pass_on()
    scatter.finish()
    gather.finish()


def turn_kernel(
    left0, left1, right0, right1, middle, gain, cot, normed_far, grad_middle_out, gain_out, grads_out, block_out, *scratch
):
    buffers, (normed, load) = scratch[:SCATTER_BUFFERS], scratch[SCATTER_BUFFERS:]
    loaded = pltpu.make_async_copy(normed_far, normed, load.at[0])
    loaded.start()
    tokens, hidden = cot.shape[0], left0.shape[1]
    place = Place()
    place.greet()
    scatter = Scatter(place, pair_product([left0, left1], [right0, right1], tokens), *buffers)
    scatter.run_first()
    scatter.run_second()
    loaded.wait()

    def weight_grads(n, none):
        at = pl.ds(pl.multiple_of(n * 256, 256), 256)
        for k, part in enumerate((left0, left1)):
            value = lax.dot_general(normed[:, at], part[...], (((0,), (0,)), ((), ())), preferred_element_type=F32)
            grads_out[at, k * hidden : (k + 1) * hidden] = value.astype(BF16)
        return none

    lax.fori_loop(0, normed.shape[1] // 256, weight_grads, 0)
    gain_out[...] = jnp.zeros_like(gain_out)

    def body(at):
        values = middle[at, :]
        grad = scatter.rows(at)
        scale = rms(values)
        weighted = grad * gain[...]
        inner = jnp.mean(values * weighted, axis=-1, keepdims=True)
        total = cot[at, :].astype(F32) + scale * weighted - values * (scale * scale * scale * inner)
        grad_middle_out[at, :] = total
        block_out[at, :] = total.astype(BF16)
        term = grad * values * scale
        gain_out[...] += term[0:8] + term[8:16]

    for part in (0, 1):
        scatter.run_third(part)
        for_slices(part * tokens // 2, (part + 1) * tokens // 2, body)
    scatter.finish()


def spread_kernel(block, w_out, mixed, mixed_out, out_grad, gathered, send, recv, chunk_ref, total, load):
    tokens = block.shape[0]
    place = Place()
    place.greet()
    gather = Gather(place, block, gathered, send, recv)
    gather.begin_whole()
    total[...] = jnp.zeros_like(total)

    def fetch(slot, chunk):
        at = pl.ds(pl.multiple_of(chunk * tokens, tokens), tokens)
        copy = pltpu.make_async_copy(gathered.at[at], chunk_ref.at[slot], load.at[slot])
        copy.start()
        return copy, slot, chunk

    def use(fetched):
        copy, slot, chunk = fetched
        copy.wait()
        use_chunk(chunk_ref.at[slot], chunk)

    def use_chunk(values, chunk):
        at = pl.ds(pl.multiple_of(chunk * tokens, tokens), tokens)
        mixed_out[at, :] = lax.dot_general(values[...], w_out[...], (((1,), (1,)), ((), ())), preferred_element_type=F32)
        part = mixed[at, :]

        def rows(n, none):
            columns = pl.ds(pl.multiple_of(n * 256, 256), 256)
            turned = (((0,), (0,)), ((), ()))
            total[columns, :] += lax.dot_general(values[:, columns], part, turned, preferred_element_type=F32)
            return none

        lax.fori_loop(0, values.shape[1] // 256, rows, 0)

    use_chunk(block, place.chunk(0, 0, 0))
    gather.pass_first()
    gather.finish_core()
    ahead = fetch(0, place.chunk(0, 0, 1))
    use(ahead)
    gather.pass_second()
    ahead = fetch(0, place.chunk(0, 1, 0))
    after = fetch(1, place.chunk(1, 0, 0))
    use(ahead)
    gather.finish_near()
    ahead = fetch(0, place.chunk(0, 1, 1))
    use(after)
    gather.pass_third()
    after = fetch(1, place.chunk(1, 0, 1))
    use(ahead)
    ahead = fetch(0, place.chunk(1, 1, 0))
    use(after)
    gather.finish_far()
    after = fetch(1, place.chunk(1, 1, 1))
    use(ahead)
    use(after)
    out_grad[...] = total[...].astype(BF16)
    gather.finish_sends()


class Owners:
    def __init__(self, place, reduced, out, send, recv):
        self.place, self.reduced, self.out, self.send, self.recv = place, reduced, out, send, recv
        self.own = place.chunk(0, 0, 0)

    def copy(self, number, offset, slot):
        return pltpu.make_async_remote_copy(
            src_ref=self.reduced.at[self.place.chunk(*offset)],
            dst_ref=self.out.at[slot],
            send_sem=self.send.at[number],
            recv_sem=self.recv.at[number],
            device_id=self.place.peer(*offset),
            device_id_type=MESH,
        )

    def begin(self):
        self.keep = pltpu.make_async_copy(self.reduced.at[self.own], self.out.at[self.own], self.send.at[7])
        self.keep.start()
        self.moved = [self.copy(number, offset, self.own) for number, offset in enumerate(OTHERS)]
        for copy in self.moved:
            copy.start()

    def finish(self):
        for number, offset in enumerate(OTHERS):
            self.copy(number, offset, self.place.chunk(*offset)).wait_recv()
        for copy in self.moved:
            copy.wait_send()
        self.keep.wait()


OWNERS_SCRATCH = [pltpu.SemaphoreType.DMA((8,))] * 2
BEYOND = [offset for offset in OTHERS if sum(offset) > 1]


class GateSums:
    def __init__(self, place, count, pieces, rows_recv, gates_all, send, recv):
        self.place, self.count, self.pieces = place, count, pieces
        self.rows_recv, self.gates_all, self.send, self.recv = rows_recv, gates_all, send, recv
        self.me = lax.axis_index("t")
        self.rank = place.g * 2 + place.c
        self.near = [offset for offset in OTHERS if not offset[0]]
        self.moved = []

    def copy(self, number, source, target, peer):
        return pltpu.make_async_remote_copy(
            src_ref=source,
            dst_ref=target,
            send_sem=self.send.at[number],
            recv_sem=self.recv.at[number],
            device_id=peer,
            device_id_type=MESH,
        )

    def begin(self):
        for number, offset in enumerate(self.near):
            other = lax.rem(self.place.chunk(*offset), 4)
            self.moved.append(self.copy(number, self.pieces.at[other], self.rows_recv.at[self.rank], self.place.peer(*offset)))
            self.moved[-1].start()
        self.rows_recv[self.rank] = self.pieces[self.rank]

    def pass_on(self):
        for number, offset in enumerate(self.near):
            other = lax.rem(self.place.chunk(*offset), 4)
            self.copy(number, self.pieces.at[other], self.rows_recv.at[other], self.place.peer(*offset)).wait_recv()
        for step in range(1, self.count):
            to = lax.rem(self.me + step, self.count)
            self.moved.append(self.copy(2 + step, self.rows_recv.at[to], self.gates_all.at[self.me], {"t": to}))
            self.moved[-1].start()
        self.gates_all[self.me] = self.rows_recv[self.me]

    def finish(self, out):
        for step in range(1, self.count):
            other = lax.rem(self.me + self.count - step, self.count)
            self.copy(2 + step, self.rows_recv.at[other], self.gates_all.at[other], {"t": other}).wait_recv()
        total = self.gates_all[0].astype(F32)
        for z in range(1, self.count):
            total = total + self.gates_all[z].astype(F32)
        out[...] = total
        for copy in self.moved:
            copy.wait_send()


class SmallSum:
    def __init__(self, place, count, values, inbox, plane_sum, plane_box, send, recv):
        self.place, self.count, self.values, self.inbox = place, count, values, inbox
        self.plane_sum, self.plane_box, self.send, self.recv = plane_sum, plane_box, send, recv
        self.me = lax.axis_index("t")
        self.moved = []

    def copy(self, number, source, target, peer):
        return pltpu.make_async_remote_copy(
            src_ref=source,
            dst_ref=target,
            send_sem=self.send.at[number],
            recv_sem=self.recv.at[number],
            device_id=peer,
            device_id_type=MESH,
        )

    def begin(self):
        own = self.place.chunk(0, 0, 0)
        for number, offset in enumerate(OTHERS):
            self.moved.append(self.copy(number, self.values, self.inbox.at[own], self.place.peer(*offset)))
            self.moved[-1].start()
        self.inbox[own] = self.values[...]

    def pass_on(self):
        for number, offset in enumerate(OTHERS):
            slot = self.inbox.at[self.place.chunk(*offset)]
            self.copy(number, self.values, slot, self.place.peer(*offset)).wait_recv()
        total = self.inbox[0]
        for n in range(1, 8):
            total = total + self.inbox[n]
        self.plane_sum[...] = total
        self.plane_box[self.me] = total
        for step in range(1, self.count):
            to = {"t": lax.rem(self.me + step, self.count)}
            self.moved.append(self.copy(6 + step, self.plane_sum, self.plane_box.at[self.me], to))
            self.moved[-1].start()

    def finish(self, out):
        for step in range(1, self.count):
            other = lax.rem(self.me + self.count - step, self.count)
            self.copy(6 + step, self.plane_sum, self.plane_box.at[other], {"t": other}).wait_recv()
        total = self.plane_box[0]
        for z in range(1, self.count):
            total = total + self.plane_box[z]
        out[...] = total
        for sent in self.moved:
            sent.wait_send()


def final_kernel(
    left, right, own_in, gain, mlp_gains, grad_middle, reduced, grad_out, values_out, owned,
    gain_sum, own_send, own_recv, *buffers,
):
    tokens, width = own_in.shape
    place = Place()
    place.greet([place.peer(*offset) for offset in BEYOND])
    scatter = Scatter(place, pair_product([left], [right], tokens), *buffers)
    owners = Owners(place, reduced, owned, own_send, own_recv)
    scatter.run_first()
    owners.begin()
    scatter.run_second()
    gain_sum[...] = jnp.zeros_like(gain_sum)

    def body(at):
        x = own_in[at, :].astype(F32)
        grad = scatter.rows(at)
        scale = rms(x)
        weighted = grad * gain[...]
        inner = jnp.mean(x * weighted, axis=-1, keepdims=True)
        grad_out[at, :] = grad_middle[at, :] + scale * weighted - x * (scale * scale * scale * inner)
        term = grad * x * scale
        gain_sum[...] += term[0:8] + term[8:16]

    for part in (0, 1):
        scatter.run_third(part)
        for_slices(part * tokens // 2, (part + 1) * tokens // 2, body)
    lines = width // LANES
    for base, row in ((0, jnp.sum(mlp_gains[...], axis=0, keepdims=True)), (lines, jnp.sum(gain_sum[...], axis=0, keepdims=True))):
        for n in range(lines):
            values_out[base + n : base + n + 1, :] = row[:, n * LANES : (n + 1) * LANES]
    owners.finish()
    scatter.finish()


def final_step(left, right, own_in, gain, mlp_gains, grad_middle, reduced):
    tokens, width = own_in.shape
    return pl.pallas_call(
        final_kernel,
        name="final_step",
        out_shape=(
            jax.ShapeDtypeStruct((tokens, width), F32),
            jax.ShapeDtypeStruct((2 * width // LANES, LANES), F32),
            jax.ShapeDtypeStruct(reduced.shape, reduced.dtype),
        ),
        in_specs=[*whole(6), ANYWHERE],
        out_specs=(*whole(2), ANYWHERE),
        scratch_shapes=[pltpu.VMEM((8, width), F32), *OWNERS_SCRATCH, *Scatter.scratch(tokens, width)],
        compiler_params=mixer_params(7),
    )(left, right, own_in, gain[None], mlp_gains, grad_middle, reduced)


def owners_kernel(
    count, with_gates, pieces, values, reduced0, reduced1, gates_out, gains_out, out0, out1,
    inbox, plane_sum, plane_box, sum_send, sum_recv, rows_recv, gates_all, gates_send, gates_recv,
    send0, recv0, send1, recv1,
):
    place = Place()
    me = lax.axis_index("t")
    place.greet([place.peer(*offset) for offset in BEYOND] + [{"t": lax.rem(me + step, count)} for step in range(1, count)])
    owners = [Owners(place, reduced0, out0, send0, recv0), Owners(place, reduced1, out1, send1, recv1)]
    gates = GateSums(place, count, pieces, rows_recv, gates_all, gates_send, gates_recv)
    gains = SmallSum(place, count, values, inbox, plane_sum, plane_box, sum_send, sum_recv)
    gains.begin()
    if with_gates:
        gates.begin()
    for part in owners:
        part.begin()
    gains.pass_on()
    if with_gates:
        gates.pass_on()
    gains.finish(gains_out)
    if with_gates:
        gates.finish(gates_out)
    else:
        gates_out[...] = jnp.zeros_like(gates_out)
    for part in owners:
        part.finish()


def owners_step(planes, with_gates, pieces, values, reduced):
    block = pieces.shape[1:]
    slots = planes if with_gates else 1
    return pl.pallas_call(
        functools.partial(owners_kernel, planes, with_gates),
        name="owners_step",
        out_shape=(
            jax.ShapeDtypeStruct(block, F32),
            jax.ShapeDtypeStruct(values.shape, F32),
            *[jax.ShapeDtypeStruct(part.shape, part.dtype) for part in reduced],
        ),
        in_specs=[*whole(2), ANYWHERE, ANYWHERE],
        out_specs=(*whole(2), ANYWHERE, ANYWHERE),
        scratch_shapes=[
            pltpu.VMEM((8, *values.shape), F32),
            pltpu.VMEM(values.shape, F32),
            pltpu.VMEM((planes, *values.shape), F32),
            pltpu.SemaphoreType.DMA((planes + 6,)),
            pltpu.SemaphoreType.DMA((planes + 6,)),
            pltpu.VMEM((slots, *block), BF16),
            pltpu.VMEM((slots, *block), BF16),
            pltpu.SemaphoreType.DMA((planes + 2,)),
            pltpu.SemaphoreType.DMA((planes + 2,)),
            *OWNERS_SCRATCH,
            *OWNERS_SCRATCH,
        ],
        compiler_params=mixer_params(8),
    )(pieces, values, *reduced)


def place_kernel(planes, hidden, outs, through, *refs):
    count = len(outs)
    given, passed, results, copied = refs[:count], refs[count : count + through], refs[count + through : 2 * count + through], refs[2 * count + through :]
    for source, target in zip(passed, copied):
        target[...] = source[...]
    for count, sources, out in zip(outs, given, results):
        piece = sources.shape[2] // (count * (planes if hidden else 1))
        for k in range(count):
            if hidden:
                groups = [
                    ((t * 2 + i) * 4 * piece, [(i * 4 + r, (k * planes + t) * piece) for r in range(4)])
                    for t in range(planes)
                    for i in range(2)
                ]
            else:
                groups = [(r * 2 * piece, [(i * 4 + r, k * piece) for i in range(2)]) for r in range(4)]
            for start, parts in groups:
                row = jnp.concatenate([sources[p, :, at : at + piece].astype(F32) for p, at in parts], axis=1)
                if count > 1:
                    out[:, k, start : start + row.shape[1]] = row
                else:
                    out[:, start : start + row.shape[1]] = row


def place_columns(planes, hidden, outs, owned, through=()):
    members, own_rows, columns = owned[0].shape
    total = columns * members // outs[0]
    shapes = [(own_rows, count, total) if count > 1 else (own_rows, total) for count in outs]
    return pl.pallas_call(
        functools.partial(place_kernel, planes, hidden, outs, len(through)),
        name="place_columns",
        out_shape=(
            *[jax.ShapeDtypeStruct(shape, F32) for shape in shapes],
            *[jax.ShapeDtypeStruct(part.shape, part.dtype) for part in through],
        ),
        in_specs=whole(len(owned) + len(through)),
        out_specs=tuple(whole(len(outs) + len(through))),
        compiler_params=pltpu.CompilerParams(vmem_limit_bytes=60 * 1024 * 1024),
    )(*owned, *through)


def last_kernel(planes, own_in, own_out, gates, gains, in_out, out_out, gate_out, taps_out, bias_out, logit_out, decay_out, mlp_out, mix_out):
    place_kernel(planes, False, (2, 1), 0, own_in, own_out, in_out, out_out)
    size, part = gate_out.shape[0], gate_out.shape[2]
    for k in range(2):
        gate_out[:, k, :] = gates[k * size : (k + 1) * size, :part]
    rest = gates[2 * size : 2 * size + 8, :part]
    taps_out[...] = rest[0:4]
    bias_out[...] = rest[4:5]
    logit_out[...] = rest[5:7]
    decay_out[...] = rest[7:8]
    own_rows = mlp_out.shape[1]
    per_line = LANES // own_rows
    index = lax.axis_index("t") * 8 + Place().chunk(0, 0, 0)
    for base, out in ((0, mlp_out), (gains.shape[0] // 2, mix_out)):
        line = gains[pl.ds(base + index // per_line, 1), :]
        value = line[:, :own_rows]
        for n in range(1, per_line):
            value = jnp.where(index % per_line == n, line[:, n * own_rows : (n + 1) * own_rows], value)
        out[...] = value


def last_step(planes, own_in, own_out, gates, gains, size, part):
    members, own_rows, columns = own_out.shape
    shapes = [
        (own_rows, 2, columns * members), (own_rows, columns * members),
        (size, 2, part), (4, part), (1, part), (2, part), (1, part), (1, own_rows), (1, own_rows),
    ]
    return pl.pallas_call(
        functools.partial(last_kernel, planes),
        name="place_last",
        out_shape=tuple(jax.ShapeDtypeStruct(shape, F32) for shape in shapes),
        in_specs=whole(4),
        out_specs=tuple(whole(9)),
        compiler_params=pltpu.CompilerParams(vmem_limit_bytes=60 * 1024 * 1024),
    )(own_in, own_out, gates, gains)


def first_gather(planes, normed, ids):
    tokens, width = normed.shape
    every = (8, *ids.shape)
    return pl.pallas_call(
        functools.partial(first_gather_kernel, planes),
        name="first_gather",
        out_shape=(jax.ShapeDtypeStruct((8 * tokens, width), BF16), *[jax.ShapeDtypeStruct(every, F32)] * 3),
        in_specs=[ANYWHERE, *whole(1)],
        out_specs=(ANYWHERE, *whole(3)),
        scratch_shapes=[pltpu.VMEM(every, F32)] * 3 + GATHER_SCRATCH + [pltpu.SemaphoreType.DMA((9,))] * 2,
        compiler_params=mixer_params(3),
    )(normed, ids)


def middle_step(mixed, w_out, own_in, gain):
    tokens, width = own_in.shape
    return pl.pallas_call(
        middle_kernel,
        name="middle_step",
        out_shape=(jax.ShapeDtypeStruct((tokens, width), F32), jax.ShapeDtypeStruct((8 * tokens, width), BF16)),
        in_specs=whole(4),
        out_specs=(pl.BlockSpec(memory_space=pltpu.VMEM), ANYWHERE),
        scratch_shapes=Scatter.scratch(tokens, width) + [pltpu.VMEM((tokens, width), BF16)] + GATHER_SCRATCH,
        compiler_params=mixer_params(4),
    )(mixed, w_out, own_in, gain[None])


def turn_step(left0, left1, right0, right1, middle, gain, cot, normed):
    tokens, width = cot.shape
    return pl.pallas_call(
        turn_kernel,
        name="turn_step",
        out_shape=(
            jax.ShapeDtypeStruct((tokens, width), F32),
            jax.ShapeDtypeStruct((8, width), F32),
            jax.ShapeDtypeStruct((width, 2 * left1.shape[1]), BF16),
            jax.ShapeDtypeStruct((tokens, width), BF16),
        ),
        in_specs=[*whole(7), ANYWHERE],
        out_specs=tuple(whole(4)),
        scratch_shapes=Scatter.scratch(tokens, width)
        + [pltpu.VMEM(normed.shape, BF16), pltpu.SemaphoreType.DMA((1,))],
        compiler_params=mixer_params(5),
    )(left0, left1, right0, right1, middle, gain[None], cot, normed)


def spread_step(block, w_out, mixed):
    tokens, width = block.shape
    return pl.pallas_call(
        spread_kernel,
        name="turn_spread",
        out_shape=(
            jax.ShapeDtypeStruct((8 * tokens, w_out.shape[0]), F32),
            jax.ShapeDtypeStruct((width, w_out.shape[0]), BF16),
            jax.ShapeDtypeStruct((8 * tokens, width), BF16),
        ),
        in_specs=whole(3),
        out_specs=(*whole(2), ANYWHERE),
        scratch_shapes=GATHER_SCRATCH
        + [
            pltpu.VMEM((2, tokens, width), BF16),
            pltpu.VMEM((width, w_out.shape[0]), F32),
            pltpu.SemaphoreType.DMA((2,)),
        ],
        compiler_params=mixer_params(10),
    )(block, w_out, mixed)


class Swap:
    def __init__(self, quarters, out, send, recv):
        self.quarters, self.out, self.send, self.recv = quarters, out, send, recv
        self.groups = quarters.shape[0]
        self.me = lax.axis_index("g") * 2 + lax.axis_index("c")

    def copy(self, step, other, slot):
        return pltpu.make_async_remote_copy(
            src_ref=self.quarters.at[other],
            dst_ref=self.out.at[:, slot],
            send_sem=self.send.at[step],
            recv_sem=self.recv.at[step],
            device_id={"g": other // 2, "c": other % 2},
            device_id_type=MESH,
        )

    def peers(self):
        others = [lax.rem(self.me + step, self.groups) for step in range(1, self.groups)]
        return [{"g": other // 2, "c": other % 2} for other in others]

    def begin(self):
        self.keep = pltpu.make_async_copy(self.quarters.at[self.me], self.out.at[:, self.me], self.send.at[0])
        self.keep.start()
        self.moved = []
        for step in range(1, self.groups):
            self.moved.append(self.copy(step, lax.rem(self.me + step, self.groups), self.me))
            self.moved[-1].start()

    def finish(self):
        for step in range(1, self.groups):
            other = lax.rem(self.me + self.groups - step, self.groups)
            self.copy(step, other, other).wait_recv()
        for copy in self.moved:
            copy.wait_send()
        self.keep.wait()


def swap_scratch(groups):
    return [pltpu.SemaphoreType.DMA((groups,)), pltpu.SemaphoreType.DMA((groups,))]


def swap_kernel(quarters, out, send, recv):
    move = Swap(quarters, out, send, recv)
    barrier = pltpu.get_barrier_semaphore()
    for peer in move.peers():
        pl.semaphore_signal(barrier, inc=1, device_id=peer, device_id_type=MESH)
    pl.semaphore_wait(barrier, move.groups - 1)
    move.begin()
    move.finish()


def swap(quarters):
    groups, kinds, part, width = quarters.shape
    return pl.pallas_call(
        swap_kernel,
        name="swap",
        out_shape=jax.ShapeDtypeStruct((kinds, groups, part, width), quarters.dtype),
        in_specs=[ANYWHERE],
        out_specs=ANYWHERE,
        scratch_shapes=swap_scratch(groups),
        compiler_params=mixer_params(6),
    )(quarters)


def rms(values):
    return lax.rsqrt(jnp.mean(values * values, axis=-1, keepdims=True) + EPS)


def nt(left, right, out):
    return lax.dot_general(left, right, (((1,), (1,)), ((), ())), preferred_element_type=F32).astype(out)


def tn(left, right, out):
    return lax.dot_general(left, right, (((0,), (0,)), ((), ())), preferred_element_type=F32).astype(out)


def nn(left, right, out):
    return jnp.dot(left, right, preferred_element_type=F32).astype(out)


def per_device(
    inputs, segment_ids, mix_gain, in_weight, conv_weight, conv_bias, gate_weight, gate_bias, decay_param, out_weight,
    mlp_gain, mlp_in, down_weight, cotangent,
):
    planes = lax.axis_size("t")
    rows_here, seg, width = inputs.shape
    row_groups = lax.axis_size("g") * lax.axis_size("c")
    own_tokens = rows_here * seg
    recur_width = conv_weight.shape[1]
    block_width = gate_weight.shape[0]
    members = 2 * row_groups
    channels = recur_width // members
    t, i = lax.axis_index("t"), lax.axis_index("i")
    r = lax.axis_index("g") * lax.axis_size("c") + lax.axis_index("c")
    member = 2 * r + i
    first = member * channels
    own_rows = width // (planes * members)

    own_in = inputs.reshape(own_tokens, width)
    flat_in = own_in.astype(F32)
    scale_in = rms(flat_in)
    cot_own = cotangent.reshape(own_tokens, width)
    own_ids = jnp.pad((segment_ids + 1).astype(F32), ((0, 8 - rows_here), (0, 0)))

    normed, *ids = first_gather(planes, (flat_in * scale_in * mix_gain).astype(BF16), own_ids)
    late_r, ids[0] = lax.optimization_barrier((r, ids[0]))

    direct = planes == row_groups
    in_own = in_weight.transpose(1, 2, 0)
    out_own = out_weight.T[None]
    part = channels // row_groups if direct else 0

    def quarter(weight, part, rank=r):
        return lax.dynamic_slice_in_dim(weight, rank * part, part, weight.ndim - 1)

    def spread_units(weight):
        return lax.all_gather(weight, "t", axis=0, tiled=False)

    def whole_units(weight):
        every = lax.all_gather(weight, ("t", "i"), axis=1, tiled=True)
        return lax.dynamic_slice_in_dim(every, first, channels, 1)

    if direct:
        in_w = swap(spread_units(quarter(in_weight, part).transpose(1, 2, 0)))
        out_quarters = spread_units(quarter(out_weight, part).T[None])
    else:
        in_w = whole_units(in_own)
        out_quarters = jnp.zeros((row_groups, 1, 16, width), BF16)
    in_w = in_w.reshape(2 * channels, width)
    hidden_part = mlp_in.shape[2] // row_groups
    gated = quarter(mlp_in, hidden_part, late_r).transpose(1, 2, 0)
    w_left, w_right, w_down = [
        spread_units(part).reshape(-1, width)
        for part in (gated[0], gated[1], quarter(down_weight, hidden_part, late_r).T)
    ]

    def own(values):
        return lax.dynamic_slice_in_dim(values, first, channels, values.ndim - 1)

    vec = own(
        jnp.concatenate(
            [
                conv_weight,
                conv_bias[None],
                gate_bias,
                8.0 * jax.nn.softplus(-decay_param)[None],
                8.0 * jax.nn.sigmoid(-decay_param)[None],
                jnp.zeros((7, recur_width), F32),
            ]
        )
    )
    gate_blocks = own(gate_weight).transpose(1, 0, 2)
    blocks = channels // block_width

    branches = nt(normed, in_w, F32)
    conv_low, decay, states, mixed, halo, cin, mask, cot, w_out = mixer_forward(
        planes, seg, rows_here, branches, ids, gate_blocks, vec, cot_own, out_quarters
    )
    w_out = (w_out if direct else whole_units(out_own)).reshape(channels, width)
    middle, normed_two = middle_step(mixed, w_out, own_in, mlp_gain)
    left = nt(normed_two, w_left, F32)
    right = nt(normed_two, w_right, F32)
    act, slope = gelu_parts(left)
    hidden = (act * right).astype(BF16)

    def over_planes(grad):
        return lax.psum_scatter(grad, "t", scatter_dimension=0, tiled=True)

    grad_down = tn(cot, hidden, BF16)
    grad_down, hidden, w_down = lax.optimization_barrier((grad_down, hidden, w_down))
    grad_down = over_planes(grad_down)
    grad_hidden = nt(cot, w_down, F32)
    grad_left = (grad_hidden * right * slope).astype(BF16)
    grad_right = (grad_hidden * act).astype(BF16)
    grad_middle, grad_mlp_gain, grad_mlp_in, grad_mid_own = turn_step(
        grad_left, grad_right, w_left, w_right, middle, mlp_gain, cot_own, normed_two
    )
    grad_down, grad_mid_own = lax.optimization_barrier((grad_down, grad_mid_own))
    grad_mlp_in = over_planes(grad_mlp_in)
    grad_mixed, grad_out, _ = spread_step(grad_mid_own, w_out, mixed)

    def by_owner(grad):
        return grad.reshape(members, own_rows, -1)

    grad_branches, gw0, gw1, small, pieces, outputs, owned_down = mixer_backward(
        planes, seg, grad_mixed, branches, states, decay, conv_low, mask, halo, cin, gate_blocks, vec, hidden, w_down, middle,
        by_owner(grad_down),
    )
    grad_mlp_in, grad_branches = lax.optimization_barrier((grad_mlp_in, grad_branches))
    grad_out = over_planes(grad_out)
    grad_in = tn(normed, grad_branches, BF16)
    grad_in, grad_branches = lax.optimization_barrier((grad_in, grad_branches))
    grad_in = over_planes(grad_in)
    outputs = outputs.reshape(inputs.shape)

    grad_inputs, values, owned_mlp_in = final_step(
        grad_branches, in_w, own_in, mix_gain, grad_mlp_gain, grad_middle, by_owner(grad_mlp_in)
    )
    gate_grads, gains, owned_in, owned_out = owners_step(planes, direct, pieces, values, [by_owner(grad_in), by_owner(grad_out)])
    grad_inputs = grad_inputs.reshape(inputs.shape)
    def columns(hidden, outs, owned, through=()):
        if direct:
            return place_columns(planes, hidden, outs, owned, through)
        owned = jnp.concatenate(owned, axis=2)
        owned = owned.reshape(2, row_groups, own_rows, sum(outs), planes if hidden else 1, -1).astype(F32)
        order = (2, 3, 4, 0, 1, 5) if hidden else (2, 3, 1, 0, 4, 5)
        owned = owned.transpose(order).reshape(own_rows, sum(outs), -1)
        return (owned[:, :2], owned[:, 2], *through)

    grad_mlp_in, grad_down_weight, outputs, grad_inputs = columns(
        True, (2, 1), [owned_mlp_in, owned_down], [outputs, grad_inputs]
    )
    if direct:
        grad_in_weight, grad_out_weight, grad_gate_weight, taps, bias, logit_bias, decay_grad, mlp_sum, mix_sum = last_step(
            planes, owned_in, owned_out, gate_grads, gains, block_width, part
        )
        bias, decay_grad, mlp_sum, mix_sum = bias[0], decay_grad[0], mlp_sum[0], mix_sum[0]
    else:
        grad_in_weight, grad_out_weight = columns(False, (2, 1), [owned_in, owned_out])
        index = ((t * 2 + i) * row_groups + r) * own_rows
        mlp_sum, mix_sum = lax.dynamic_slice_in_dim(gains.reshape(2, width), index, own_rows, 1)
        column_block = lax.broadcasted_iota(jnp.int32, (block_width, channels), 1) // block_width

        def diagonal(gw):
            return sum(
                jnp.where(column_block == n, gw[n * block_width : (n + 1) * block_width], 0.0) for n in range(blocks)
            )

        gate_grads = jnp.concatenate([diagonal(gw0), diagonal(gw1), small], axis=0)
        placed = jnp.zeros((gate_grads.shape[0], recur_width), F32)
        placed = lax.dynamic_update_slice_in_dim(placed, gate_grads, first, 1)
        gate_grads = lax.psum_scatter(placed, EVERY, scatter_dimension=1, tiled=True)
        grad_gate_weight = jnp.stack([gate_grads[:block_width], gate_grads[block_width : 2 * block_width]], axis=1)
        rest = gate_grads[2 * block_width :]
        taps, bias, logit_bias, decay_grad = rest[0:4], rest[4], rest[5:7], rest[7]
    return (
        outputs,
        grad_inputs,
        mix_sum,
        grad_in_weight,
        taps,
        bias,
        grad_gate_weight,
        logit_bias,
        decay_grad,
        grad_out_weight,
        mlp_sum,
        grad_mlp_in,
        grad_down_weight,
    )


def solution(mesh):
    seq, rows = mesh.shape["seq"], mesh.shape["rows"]
    grid = Mesh(mesh.devices.reshape(seq // 2, 2, rows // 2, 2), EVERY)
    row_axes, seq_axes = ("g", "c"), ("t", "i")
    tokens = P(row_axes, seq_axes, None)
    return jax.shard_map(
        per_device,
        mesh=grid,
        in_specs=(
            tokens,
            P(row_axes, seq_axes),
            P(),
            P(None, None, seq_axes),
            P(),
            P(),
            P(),
            P(),
            P(),
            P(None, seq_axes),
            P(),
            P(None, None, seq_axes),
            P(None, seq_axes),
            tokens,
        ),
        out_specs=(
            tokens,
            tokens,
            P(EVERY),
            P(EVERY, None, None),
            P(None, EVERY),
            P(EVERY),
            P(None, None, EVERY),
            P(None, EVERY),
            P(EVERY),
            P(EVERY, None),
            P(EVERY),
            P(EVERY, None, None),
            P(EVERY, None),
        ),
        check_vma=False,
    )
```

```python
import functools

import jax
import jax.numpy as jnp
from jax import lax
from jax.experimental import pallas as pl
from jax.experimental.pallas import tpu as pltpu
from jax.sharding import Mesh
from jax.sharding import PartitionSpec as P

EPS = 1e-06
MESH = pl.DeviceIdType.MESH
PLANE = ("i", "g", "c")
EVERY = ("t", "i", "g", "c")
F32 = jnp.float32
BF16 = jnp.bfloat16
GELU_A = 0.7978845608028654
GELU_B = 0.044715
HALO = 8
LANES = 128
SLICE = 16
ANYWHERE = pl.BlockSpec(memory_space=pl.ANY)
GATHER_SCRATCH = [pltpu.SemaphoreType.DMA((14,))] * 2


def gelu_parts(x):
    square = x * x
    th = jnp.tanh(GELU_A * x * (1.0 + GELU_B * square))
    half = 0.5 * (1.0 + th)
    slope = half + 0.5 * x * (1.0 - th * th) * (GELU_A * (1.0 + 3.0 * GELU_B * square))
    return x * half, slope


def one_minus_exp(y, power):
    series = 1.0 + y * (-1.0 / 2 + y * (1.0 / 6 + y * (-1.0 / 24 + y * (1.0 / 120 + y * (-1.0 / 720 + y * (1.0 / 5040))))))
    return jnp.where(y < 0.35, y * series, 1.0 - power)


def sigmoid(x):
    return 1.0 / (1.0 + jnp.exp(-x))


def gate_values(conv_low, wg0, wg1, vec):
    logits0 = jnp.dot(conv_low, wg0, preferred_element_type=F32) + vec[5:6]
    logits1 = jnp.dot(conv_low, wg1, preferred_element_type=F32) + vec[6:7]
    recur_gate = sigmoid(logits0)
    input_gate = sigmoid(logits1)
    log_decay = -vec[7:8] * recur_gate
    return recur_gate, input_gate, log_decay


def spread_blocks(gates, out):
    size, width = gates.shape[1], gates.shape[2]
    column = lax.broadcasted_iota(jnp.int32, (size, width), 1) // size
    for k in range(2):
        block = gates[k].astype(F32)
        for n in range(width // size):
            out[k, n * size : (n + 1) * size, :] = jnp.where(column == n, block, 0.0).astype(BF16)


def put_tiles(ref, at, values):
    tiles, lanes = ref.shape[0], ref.shape[2]
    short = tiles * lanes - values.shape[1]
    if short:
        values = jnp.concatenate([values, jnp.zeros((values.shape[0], short), values.dtype)], axis=1)
    for j in range(tiles):
        ref[j, at, :] = values[:, j * lanes : (j + 1) * lanes]


def get_tiles(ref, at, width):
    joined = jnp.concatenate([ref[j, at, :] for j in range(ref.shape[0])], axis=1)
    return joined[:, :width]


def join_tiles(parts, width):
    return jnp.concatenate(parts, axis=1)[:, :width]


def exchange_copy(step, send, target, other, send_sem, recv_sem):
    return pltpu.make_async_remote_copy(
        src_ref=send,
        dst_ref=target,
        send_sem=send_sem.at[step],
        recv_sem=recv_sem.at[step],
        device_id={"t": other},
        device_id_type=MESH,
    )


def exchange_start(count, me, send, slots, send_sem, recv_sem):
    for step in range(1, count):
        exchange_copy(step, send, slots.at[me], lax.rem(me + step, count), send_sem, recv_sem).start()


def exchange_wait(count, me, send, slots, send_sem, recv_sem):
    for step in range(1, count):
        other = lax.rem(me + count - step, count)
        exchange_copy(step, send, slots.at[other], other, send_sem, recv_sem).wait()


def mixer_forward_kernel(
    count, seg, rows_here, branches_far, ids, ids_before, ids_after, gate_blocks, vec_ref, cot, quarters,
    conv_out, decay_out, states_out, mixed_out, halo_out, cin_out, mask, cot_out, swapped,
    drive, h_ref, a_ref, ext, halo_send, halo_recv, summary, slots, send_sem, recv_sem, halo_sems,
    gather_send, gather_recv, swap_send, swap_recv, branches, wg, load,
):
    place = Place()
    me = lax.axis_index("t")
    loaded = pltpu.make_async_copy(branches_far, branches, load.at[0])
    loaded.start()
    place.greet([place.peer(0, 1, 1)] + [{"t": lax.rem(me + step, count)} for step in range(1, count)])
    gather = Gather(place, cot, cot_out, gather_send, gather_recv)
    move = Swap(quarters, swapped, swap_send, swap_recv)
    gather.begin_whole()
    move.begin()
    spread_blocks(gate_blocks, wg)
    rows = 8
    width = branches.shape[1] // 2
    loaded.wait()

    def recur_at(at):
        return branches[at, width:].astype(BF16).astype(F32)

    for r in range(rows):
        halo_send[r * HALO : (r + 1) * HALO, :] = recur_at(pl.ds((rows + r + 1) * seg - HALO, HALO))
    halo_copy = pltpu.make_async_remote_copy(
        src_ref=halo_send,
        dst_ref=halo_recv,
        send_sem=halo_sems.at[0],
        recv_sem=halo_sems.at[1],
        device_id={"t": lax.rem(me + 1, count)},
        device_id_type=MESH,
    )
    halo_copy.start()
    for r in range(rows):
        halo_out[(rows + r) * HALO : (rows + r + 1) * HALO, :] = recur_at(pl.ds((r + 1) * seg - HALO, HALO))
    vec = vec_ref[...]

    def ids_of(ref, s):
        chunk = s // rows_here
        return ref[chunk, s % rows_here : s % rows_here + 1, :]

    nothing = jnp.zeros((1, LANES), F32)
    for s in range(2 * rows):
        here = ids_of(ids, s)
        back = ids_of(ids, s - rows) if s >= rows else jnp.where(me > 0, ids_of(ids_before, s + rows), nothing)
        ahead = ids_of(ids, s + rows) if s < rows else jnp.where(me < count - 1, ids_of(ids_after, s - rows), nothing)
        lines = [jnp.concatenate([back[:, seg - k :], here[:, : seg - k]], axis=1) for k in (1, 2, 3)]
        lines += [jnp.concatenate([here[:, k:], ahead[:, :k]], axis=1) for k in (1, 2, 3)]
        lines = [jnp.where(line == here, 1.0, 0.0) for line in lines] + [nothing] * 2
        mask[s * seg : (s + 1) * seg, :] = jnp.concatenate(lines, axis=0).T

    def local(s, none):
        at = pl.ds(pl.multiple_of(s * seg, seg), seg)
        x = recur_at(at)
        ext[0:HALO, :] = halo_out[pl.ds(pl.multiple_of(s * HALO, HALO), HALO), :]
        ext[HALO : HALO + seg, :] = x
        m = mask[at, :]
        conv = vec[4:5] + vec[0:1] * x
        for k in range(1, 4):
            conv = conv + vec[k : k + 1] * ext[HALO - k : HALO - k + seg, :] * m[:, k - 1 : k]
        conv_low = conv.astype(BF16)
        conv_out[at, :] = conv_low
        recur_gate, input_gate, log_decay = gate_values(conv_low, wg[0], wg[1], vec)
        keep = m[:, 0:1]
        kept = jnp.exp(log_decay)
        put_tiles(decay_out, at, kept * keep)
        scale = (1.0 - keep) + keep * jnp.sqrt(one_minus_exp(-2.0 * log_decay, kept * kept))
        put_tiles(drive, at, scale * input_gate * conv_low.astype(F32))
        return none

    lax.fori_loop(rows, 2 * rows, local, 0)
    halo_copy.wait()
    for r in range(rows):
        halo_out[r * HALO : (r + 1) * HALO, :] = halo_recv[r * HALO : (r + 1) * HALO, :]
    gather.pass_first()
    lax.fori_loop(0, rows, local, 0)
    tiles, lanes = drive.shape[0], drive.shape[2]

    def scan(k, carried):
        at = pl.ds(k, 2 * rows, stride=seg)
        after = []
        for j in range(tiles):
            h, a = carried[j]
            d = decay_out[j, at, :]
            h = d * h + drive[j, at, :]
            a = a * d
            h_ref[j, at, :] = h
            a_ref[j, at, :] = a
            after.append((h, a))
        return tuple(after)

    start = (jnp.zeros((2 * rows, lanes), F32), jnp.ones((2 * rows, lanes), F32))
    last = lax.fori_loop(0, seg, scan, (start,) * tiles, unroll=4)
    last_h = join_tiles([part[0] for part in last], width)
    last_a = join_tiles([part[1] for part in last], width)
    summary[0:rows, :] = last_a[rows:] * last_a[:rows]
    summary[rows : 2 * rows, :] = last_a[rows:] * last_h[:rows] + last_h[rows:]
    exchange_start(count, me, summary, slots, send_sem, recv_sem)
    gather.pass_second()

    def activate(s, none):
        at = pl.ds(pl.multiple_of(s * seg, seg), seg)
        act, _ = gelu_parts(branches[at, :width])
        states_out[at, :] = act
        return none

    lax.fori_loop(0, 2 * rows, activate, 0)
    exchange_wait(count, me, summary, slots, send_sem, recv_sem)
    carry = jnp.zeros((rows, width), F32)
    for z in range(count - 1):
        carry = jnp.where(z < me, slots[z, 0:rows, :] * carry + slots[z, rows : 2 * rows, :], carry)
    cin_out[0:rows, :] = carry
    cin_out[rows : 2 * rows, :] = last_a[:rows] * carry + last_h[:rows]

    def finish(s, none):
        at = pl.ds(pl.multiple_of(s * seg, seg), seg)
        states = get_tiles(h_ref, at, width) + get_tiles(a_ref, at, width) * cin_out[pl.ds(s, 1), :]
        act = states_out[at, :]
        states_out[at, :] = states
        mixed_out[at, :] = (act * states.astype(BF16).astype(F32)).astype(BF16)
        return none

    lax.fori_loop(0, 2 * rows, finish, 0)
    gather.pass_third()
    gather.finish()
    move.finish()


def mixer_backward_kernel(
    count, seg, grad_mixed_far, branches_far, states_far, decay_far, conv_far, mask_far, halo, cin, gate_blocks, vec_ref,
    hidden, w_down, middle_far, reduced, grad_out, gw0_out, gw1_out, small_out, pieces_out, outputs, owned,
    tot, prod, ext, halo_send, halo_recv, summary, slots, uin, send_sem, recv_sem, halo_sems,
    grad_mixed, branches, states, decay, conv_low_ref, mask, middle, wg, load, own_send, own_recv, *buffers,
):
    place = Place()
    pairs = (
        (grad_mixed_far, grad_mixed),
        (branches_far, branches),
        (states_far, states),
        (decay_far, decay),
        (conv_far, conv_low_ref),
        (mask_far, mask),
        (middle_far, middle),
    )
    loads = [pltpu.make_async_copy(far, near, load.at[n]) for n, (far, near) in enumerate(pairs)]
    for part in loads:
        part.start()
    me = lax.axis_index("t")
    place.greet([place.peer(*offset) for offset in BEYOND] + [{"t": lax.rem(me + step, count)} for step in range(1, count)])
    scatter = Scatter(place, pair_product([hidden], [w_down], outputs.shape[0]), *buffers)
    owners = Owners(place, reduced, owned, own_send, own_recv)
    spread_blocks(gate_blocks, wg)
    scatter.run_first()
    owners.begin()
    for part in loads:
        part.wait()
    rows = 8
    width = branches.shape[1] // 2
    vec = vec_ref[...]

    def local(s, none):
        at = pl.ds(pl.multiple_of(s * seg, seg), seg)
        act, slope = gelu_parts(branches[at, :width])
        gm = grad_mixed[at, :].astype(F32)
        grad_out[at, :width] = (gm * states[at, :].astype(BF16).astype(F32) * slope).astype(BF16)
        put_tiles(tot, at, (gm * act).astype(BF16).astype(F32))
        return none

    lax.fori_loop(0, 2 * rows, local, 0)

    tiles, lanes = tot.shape[0], tot.shape[2]

    def scan(k, carried):
        at = pl.ds(seg - 1 - k, 2 * rows, stride=seg)
        after = []
        for j in range(tiles):
            u, p = carried[j]
            d = decay[j, at, :]
            total = tot[j, at, :] + u
            tot[j, at, :] = total
            prod[j, at, :] = p
            after.append((d * total, d * p))
        return tuple(after)

    start = (jnp.zeros((2 * rows, lanes), F32), jnp.ones((2 * rows, lanes), F32))
    last = lax.fori_loop(0, seg, scan, (start,) * tiles, unroll=4)
    u = join_tiles([part[0] for part in last], width)
    p = join_tiles([part[1] for part in last], width)
    summary[0:rows, :] = p[:rows] * p[rows:]
    summary[rows : 2 * rows, :] = p[:rows] * u[rows:] + u[:rows]
    exchange_start(count, me, summary, slots, send_sem, recv_sem)
    scatter.run_second()
    exchange_wait(count, me, summary, slots, send_sem, recv_sem)
    carry = jnp.zeros((rows, width), F32)
    for z in range(count - 1, 0, -1):
        carry = jnp.where(z > me, slots[z, 0:rows, :] * carry + slots[z, rows : 2 * rows, :], carry)
    uin[rows : 2 * rows, :] = carry
    uin[0:rows, :] = p[rows:] * carry + u[rows:]
    gw0_out[...] = jnp.zeros_like(gw0_out)
    gw1_out[...] = jnp.zeros_like(gw1_out)
    small_out[...] = jnp.zeros_like(small_out)

    def gates(s, none):
        at = pl.ds(pl.multiple_of(s * seg, seg), seg)
        total = get_tiles(tot, at, width) + get_tiles(prod, at, width) * uin[pl.ds(s, 1), :]
        ext[HALO - 1 : HALO, :] = cin[pl.ds(s, 1), :]
        ext[HALO : HALO + seg, :] = states[at, :]
        before = ext[HALO - 1 : HALO - 1 + seg, :]
        conv_low = conv_low_ref[at, :]
        conv_vals = conv_low.astype(F32)
        m = mask[at, :]
        keep = m[:, 0:1]
        recur_gate, input_gate, log_decay = gate_values(conv_low, wg[0], wg[1], vec)
        power = jnp.exp(2.0 * log_decay)
        gone = one_minus_exp(-2.0 * log_decay, power)
        inverse = lax.rsqrt(gone)
        root = gone * inverse
        scale = (1.0 - keep) + keep * root
        driven_in = total * conv_vals
        grad_log = total * before * get_tiles(decay, at, width) - driven_in * input_gate * keep * (power * inverse)
        grad0 = grad_log * log_decay * (1.0 - recur_gate)
        grad1 = driven_in * scale * input_gate * (1.0 - input_gate)
        low0 = grad0.astype(BF16)
        low1 = grad1.astype(BF16)
        inputs_of = (((1,), (1,)), ((), ()))
        grad_conv = (
            total * scale * input_gate
            + lax.dot_general(low0, wg[0], inputs_of, preferred_element_type=F32)
            + lax.dot_general(low1, wg[1], inputs_of, preferred_element_type=F32)
        )
        put_tiles(tot, at, grad_conv)
        turned = (((0,), (0,)), ((), ()))
        gw0_out[...] += lax.dot_general(conv_low, low0, turned, preferred_element_type=F32)
        gw1_out[...] += lax.dot_general(conv_low, low1, turned, preferred_element_type=F32)
        x = branches[at, width:].astype(BF16).astype(F32)
        ext[0:HALO, :] = halo[pl.ds(pl.multiple_of(s * HALO, HALO), HALO), :]
        ext[HALO : HALO + seg, :] = x

        def add(row, values):
            small_out[row : row + 1, :] += jnp.sum(values, axis=0, keepdims=True)

        add(0, grad_conv * x)
        for k in range(1, 4):
            add(k, grad_conv * ext[HALO - k : HALO - k + seg, :] * m[:, k - 1 : k])
        add(4, grad_conv)
        add(5, grad0)
        add(6, grad1)
        add(7, grad_log * recur_gate)
        return none

    lax.fori_loop(0, 2 * rows, gates, 0)
    small_out[7:8, :] = small_out[7:8, :] * vec[8:9]
    size, part = gate_blocks.shape[1], width // 4

    def padded(values):
        short = [values, jnp.zeros((values.shape[0], LANES - part), F32)]
        return jnp.concatenate(short, axis=1)

    for r in range(4):
        first = r * part // size * size
        at = slice(r * part, (r + 1) * part)
        for k, square in enumerate((gw0_out, gw1_out)):
            pieces_out[r, k * size : (k + 1) * size, :] = padded(square[first : first + size, at]).astype(BF16)
        rest = jnp.concatenate([padded(small_out[:, at]), jnp.zeros((8, LANES), F32)], axis=0)
        pieces_out[r, 2 * size :, :] = rest.astype(BF16)
    for r in range(rows):
        halo_send[r * HALO : (r + 1) * HALO, :] = get_tiles(tot, pl.ds(r * seg, HALO), width)
    halo_copy = pltpu.make_async_remote_copy(
        src_ref=halo_send,
        dst_ref=halo_recv,
        send_sem=halo_sems.at[0],
        recv_sem=halo_sems.at[1],
        device_id={"t": lax.rem(me + count - 1, count)},
        device_id_type=MESH,
    )
    halo_copy.start()

    def back(s, none):
        at = pl.ds(pl.multiple_of(s * seg, seg), seg)
        m = mask[at, :]
        grad_conv = get_tiles(tot, at, width)
        ext[0:seg, :] = grad_conv
        result = vec[0:1] * grad_conv

        @pl.when(s < rows)
        def _():
            ext[seg : seg + HALO, :] = get_tiles(tot, pl.ds(pl.multiple_of((s + rows) * seg, seg), HALO), width)

        @pl.when(s >= rows)
        def _():
            ext[seg : seg + HALO, :] = halo_recv[pl.ds(pl.multiple_of((s - rows) * HALO, HALO), HALO), :]

        for k in range(1, 4):
            result = result + vec[k : k + 1] * ext[k : k + seg, :] * m[:, 2 + k : 3 + k]
        grad_out[at, width:] = result.astype(BF16)
        return none

    lax.fori_loop(0, rows, back, 0)
    halo_copy.wait()
    lax.fori_loop(rows, 2 * rows, back, 0)
    scatter.run_third(0)
    scatter.run_third(1)

    def body(at):
        outputs[at, :] = (middle[at, :] + scatter.rows(at)).astype(BF16)

    for_slices(0, outputs.shape[0], body)
    scatter.finish()
    owners.finish()


def whole(count):
    return [pl.BlockSpec(memory_space=pltpu.VMEM)] * count


def mixer_params(number):
    return pltpu.CompilerParams(collective_id=number, has_side_effects=True, vmem_limit_bytes=60 * 1024 * 1024)


def mixer_forward(count, seg, rows_here, branches, ids, gate_blocks, vec, cot, quarters):
    n, width = branches.shape[0], branches.shape[1] // 2
    full = functools.partial(jax.ShapeDtypeStruct, (n, width))
    tiles = -(-width // LANES)
    tiled = jax.ShapeDtypeStruct((tiles, n, LANES), F32)
    groups, kinds, part, depth = quarters.shape
    return pl.pallas_call(
        functools.partial(mixer_forward_kernel, count, seg, rows_here),
        name="mixer_forward",
        out_shape=(
            full(BF16), tiled, full(F32), full(BF16),
            jax.ShapeDtypeStruct((16 * HALO, width), F32), jax.ShapeDtypeStruct((16, width), F32),
            jax.ShapeDtypeStruct((n, 8), F32),
            jax.ShapeDtypeStruct((8 * cot.shape[0], cot.shape[1]), BF16),
            jax.ShapeDtypeStruct((kinds, groups, part, depth), BF16),
        ),
        in_specs=[ANYWHERE, *whole(5), ANYWHERE, ANYWHERE],
        out_specs=(*whole(7), ANYWHERE, ANYWHERE),
        scratch_shapes=[
            pltpu.VMEM((tiles, n, LANES), F32),
            pltpu.VMEM((tiles, n, LANES), F32),
            pltpu.VMEM((tiles, n, LANES), F32),
            pltpu.VMEM((seg + HALO, width), F32),
            pltpu.VMEM((8 * HALO, width), F32),
            pltpu.VMEM((8 * HALO, width), F32),
            pltpu.VMEM((16, width), F32),
            pltpu.VMEM((count, 16, width), F32),
            pltpu.SemaphoreType.DMA((count,)),
            pltpu.SemaphoreType.DMA((count,)),
            pltpu.SemaphoreType.DMA((2,)),
            *GATHER_SCRATCH,
            *swap_scratch(groups),
            pltpu.VMEM(branches.shape, F32),
            pltpu.VMEM((2, width, width), BF16),
            pltpu.SemaphoreType.DMA((1,)),
        ],
        compiler_params=mixer_params(1),
    )(branches, *ids, gate_blocks, vec, cot, quarters)


def mixer_backward(count, seg, grad_mixed, branches, states, decay, conv_low, mask, halo, cin, gate_blocks, vec, hidden, w_down, middle, reduced):
    n, width = branches.shape[0], branches.shape[1] // 2
    tokens, depth = n // 8, w_down.shape[1]
    full = functools.partial(jax.ShapeDtypeStruct, (n, width))
    tiles = -(-width // LANES)
    tiled = jax.ShapeDtypeStruct((tiles, n, LANES), F32)
    return pl.pallas_call(
        functools.partial(mixer_backward_kernel, count, seg),
        name="mixer_backward",
        out_shape=(
            jax.ShapeDtypeStruct((n, 2 * width), BF16),
            jax.ShapeDtypeStruct((width, width), F32), jax.ShapeDtypeStruct((width, width), F32),
            jax.ShapeDtypeStruct((8, width), F32),
            jax.ShapeDtypeStruct((4, 2 * gate_blocks.shape[1] + 16, LANES), BF16),
            jax.ShapeDtypeStruct((tokens, depth), BF16),
            jax.ShapeDtypeStruct(reduced.shape, BF16),
        ),
        in_specs=[*[ANYWHERE] * 6, *whole(6), *[ANYWHERE] * 2],
        out_specs=(*whole(6), ANYWHERE),
        scratch_shapes=[
            pltpu.VMEM((tiles, n, LANES), F32),
            pltpu.VMEM((tiles, n, LANES), F32),
            pltpu.VMEM((seg + HALO, width), F32),
            pltpu.VMEM((8 * HALO, width), F32),
            pltpu.VMEM((8 * HALO, width), F32),
            pltpu.VMEM((16, width), F32),
            pltpu.VMEM((count, 16, width), F32),
            pltpu.VMEM((16, width), F32),
            pltpu.SemaphoreType.DMA((count,)),
            pltpu.SemaphoreType.DMA((count,)),
            pltpu.SemaphoreType.DMA((2,)),
            *[pltpu.VMEM(part.shape, part.dtype) for part in (grad_mixed, branches, states, decay, conv_low, mask, middle)],
            pltpu.VMEM((2, width, width), BF16),
            pltpu.SemaphoreType.DMA((7,)),
            *[pltpu.SemaphoreType.DMA((8,))] * 2,
            *Scatter.scratch(tokens, depth),
        ],
        compiler_params=mixer_params(2),
    )(grad_mixed, branches, states, decay, conv_low, mask, halo, cin, gate_blocks, vec, hidden, w_down, middle, reduced)


class Place:
    def __init__(self):
        self.i, self.g, self.c = lax.axis_index("i"), lax.axis_index("g"), lax.axis_index("c")
        self.core, self.across, self.along = {"c": 1 - self.c}, {"g": 1 - self.g}, {"i": 1 - self.i}

    def chunk(self, di, dg, dc):
        i = 1 - self.i if di else self.i
        g = 1 - self.g if dg else self.g
        c = 1 - self.c if dc else self.c
        return (i * 2 + g) * 2 + c

    def peer(self, di, dg, dc):
        return {
            "i": 1 - self.i if di else self.i,
            "g": 1 - self.g if dg else self.g,
            "c": 1 - self.c if dc else self.c,
        }

    def greet(self, more=()):
        barrier = pltpu.get_barrier_semaphore()
        peers = [self.core, self.across, self.along, *more]
        for peer in peers:
            pl.semaphore_signal(barrier, inc=1, device_id=peer, device_id_type=MESH)
        pl.semaphore_wait(barrier, len(peers))


class Gather:
    COPIES = 12

    def __init__(self, place, block, out, send, recv):
        self.place, self.block, self.out, self.send, self.recv = place, block, out, send, recv
        self.tokens = block.shape[0]
        self.half = self.tokens // 2

    def rows(self, chunk, part):
        start = chunk * self.tokens + (self.half if part == 1 else 0)
        return self.out.at[pl.ds(pl.multiple_of(start, self.half), self.tokens if part == 2 else self.half)]

    def mine(self, part):
        if part == 2:
            return self.block
        return self.block.at[pl.ds(part * self.half, self.half)]

    def copy(self, number, source, chunk, part, peer):
        return pltpu.make_async_remote_copy(
            src_ref=source,
            dst_ref=self.rows(chunk, part),
            send_sem=self.send.at[number],
            recv_sem=self.recv.at[number],
            device_id=peer,
            device_id_type=MESH,
        )

    def begin(self, part, whole=False):
        place = self.place
        own = place.chunk(0, 0, 0)
        other = 1 - part if whole else part
        self.give(0 + part, own, part, place.across)
        self.give(2 + other, own, other, place.along)
        self.give(4 + part, own, part, place.core)
        keep = pltpu.make_async_copy(self.mine(part), self.rows(own, part), self.send.at[self.COPIES + part])
        keep.start()
        self.local = getattr(self, "local", []) + [keep]

    def begin_whole(self):
        self.begin(0, True)
        self.begin(1, True)

    def give(self, number, chunk, part, peer):
        moved = self.copy(number, self.mine(part), chunk, part, peer)
        moved.start()
        self.kept = getattr(self, "kept", []) + [moved]

    def arrived(self, number, chunk, part):
        self.copy(number, self.rows(chunk, part), chunk, part, self.place.core).wait_recv()

    def forward(self, number, chunk, part, peer):
        moved = self.copy(number, self.rows(chunk, part), chunk, part, peer)
        moved.start()
        self.kept.append(moved)

    def pass_first(self):
        place = self.place
        ax, al = place.chunk(0, 1, 0), place.chunk(1, 0, 0)
        self.arrived(0, ax, 0)
        self.forward(6, ax, 0, place.along)
        self.arrived(3, al, 1)
        self.forward(7, al, 1, place.across)

    def pass_second(self):
        place = self.place
        ax, al = place.chunk(0, 1, 0), place.chunk(1, 0, 0)
        self.arrived(1, ax, 1)
        self.forward(8, ax, 2, place.core)
        self.arrived(2, al, 0)
        self.forward(9, al, 2, place.core)

    def pass_third(self):
        dia = self.place.chunk(1, 1, 0)
        self.arrived(6, dia, 0)
        self.forward(10, dia, 0, self.place.core)
        self.arrived(7, dia, 1)
        self.forward(11, dia, 1, self.place.core)

    def pass_on(self):
        self.pass_first()
        self.pass_second()
        self.pass_third()

    def finish_core(self):
        for part in (0, 1):
            self.arrived(4 + part, self.place.chunk(0, 0, 1), part)

    def finish_near(self):
        self.arrived(8, self.place.chunk(0, 1, 1), 2)
        self.arrived(9, self.place.chunk(1, 0, 1), 2)

    def finish_far(self):
        for part in (0, 1):
            self.arrived(10 + part, self.place.chunk(1, 1, 1), part)

    def finish(self):
        self.finish_core()
        self.finish_near()
        self.finish_far()
        self.finish_sends()

    def finish_sends(self):
        for moved in self.kept:
            moved.wait_send()
        for keep in self.local:
            keep.wait()


OTHERS = [(di, dg, dc) for di in (0, 1) for dg in (0, 1) for dc in (0, 1) if di or dg or dc]


def first_gather_kernel(count, normed, ids, normed_out, ids_out, before_out, after_out, plane_ids, before, after, send, recv, ids_send, ids_recv):
    place = Place()
    me = lax.axis_index("t")
    up, down = {"t": lax.rem(me + 1, count)}, {"t": lax.rem(me + count - 1, count)}
    place.greet([place.peer(*offset) for offset in OTHERS if sum(offset) > 1] + [up, down])
    gather = Gather(place, normed, normed_out, send, recv)
    own = place.chunk(0, 0, 0)
    moved = []

    def move(number, source, target, peer):
        copy = pltpu.make_async_remote_copy(
            src_ref=source,
            dst_ref=target,
            send_sem=ids_send.at[number],
            recv_sem=ids_recv.at[number],
            device_id=peer,
            device_id_type=MESH,
        )
        copy.start()
        moved.append(copy)

    for number, offset in enumerate(OTHERS):
        move(number, ids, plane_ids.at[own], place.peer(*offset))
    gather.begin_whole()
    plane_ids[own] = ids[...]
    for number, offset in enumerate(OTHERS):
        chunk = place.chunk(*offset)
        pltpu.make_async_remote_copy(
            src_ref=ids,
            dst_ref=plane_ids.at[chunk],
            send_sem=ids_send.at[number],
            recv_sem=ids_recv.at[number],
            device_id=place.peer(*offset),
            device_id_type=MESH,
        ).wait_recv()
    move(7, plane_ids, before, up)
    move(8, plane_ids, after, down)
    gather.pass_on()
    for copy in moved[7:]:
        copy.wait_recv()
    for copy in moved:
        copy.wait_send()
    ids_out[...] = plane_ids[...]
    before_out[...] = before[...]
    after_out[...] = after[...]
    gather.finish()


class Scatter:
    def __init__(self, place, product, core_send, core_recv, held, acc, across_recv, along_recv, second, second_recv, send, recv):
        self.place, self.product = place, product
        self.core_send, self.core_recv, self.held, self.acc = core_send, core_recv, held, acc
        self.across_recv, self.along_recv, self.second, self.second_recv = across_recv, along_recv, second, second_recv
        self.send, self.recv = send, recv
        self.kept = []

    def copy(self, number, source, target, peer):
        return pltpu.make_async_remote_copy(
            src_ref=source,
            dst_ref=target,
            send_sem=self.send.at[number],
            recv_sem=self.recv.at[number],
            device_id=peer,
            device_id_type=MESH,
        )

    def start(self, *parts):
        moved = self.copy(*parts)
        moved.start()
        self.kept.append(moved)

    def run_first(self):
        place = self.place
        order = ((1, 1), (0, 1), (1, 0), (0, 0))
        tile = 256
        per_half = self.held.shape[3] // tile
        def give(di, dg):
            q = 2 * di + dg
            chunk = place.chunk(di, dg, 1)

            def send_tile(n, none):
                at = pl.ds(pl.multiple_of(n % per_half * tile, tile), tile)
                self.core_send[q, n // per_half, :, at] = self.product(chunk, n).astype(BF16)
                return none

            lax.fori_loop(0, 2 * per_half, send_tile, 0)
            self.start(q, self.core_send.at[q], self.core_recv.at[q], place.core)

        def take(di, dg):
            q = 2 * di + dg
            chunk = place.chunk(di, dg, 0)
            self.copy(q, self.core_send.at[q], self.core_recv.at[q], place.core).wait_recv()

            def sum_tile(n, none):
                at = pl.ds(pl.multiple_of(n % per_half * tile, tile), tile)
                value = self.product(chunk, n) + self.core_recv[q, n // per_half, :, at].astype(F32)
                if q:
                    self.held[q - 1, n // per_half, :, at] = value.astype(BF16)
                else:
                    self.acc[n // per_half, :, at] = value
                return none

            lax.fori_loop(0, 2 * per_half, sum_tile, 0)
            if dg:
                self.start(4 + di, self.held.at[q - 1, 0], self.across_recv.at[di], place.across)
            if di:
                self.start(6 + dg, self.held.at[q - 1, 1], self.along_recv.at[dg], place.along)

        give(*order[0])
        give(*order[1])
        take(*order[0])
        give(*order[2])
        take(*order[1])
        give(*order[3])
        take(*order[2])
        take(*order[3])

    def second_copy(self, half, part):
        tokens = self.second.shape[1] // 2
        at = pl.ds(part * tokens, tokens)
        peer = self.place.across if half else self.place.along
        return 8 + 2 * part + half, self.second.at[half, at], self.second_recv.at[half, at], peer

    def run_second(self):
        place = self.place
        tokens = self.second.shape[1] // 2
        for part in (0, 1):
            for half, number, buffer, mine in ((0, 5, self.across_recv, 2), (1, 7, self.along_recv, 1)):
                if part == 0:
                    self.copy(number, buffer.at[1], buffer.at[1], place.core).wait_recv()

                def add_rows(at):
                    total = self.held[mine - 1, half, at, :].astype(F32) + buffer[1, at, :].astype(F32)
                    self.second[half, at, :] = total.astype(BF16)

                for_slices(part * tokens, (part + 1) * tokens, add_rows)
                self.start(*self.second_copy(half, part))

    def run_third(self, part):
        place = self.place
        if part == 0:
            for number, buffer in ((4, self.across_recv), (6, self.along_recv)):
                self.copy(number, buffer.at[0], buffer.at[0], place.core).wait_recv()
        for half in (0, 1):
            self.copy(*self.second_copy(half, part)).wait_recv()

    def rows(self, at):
        first = self.acc[0, at, :] + self.across_recv[0, at, :].astype(F32) + self.second_recv[0, at, :].astype(F32)
        last = self.acc[1, at, :] + self.along_recv[0, at, :].astype(F32) + self.second_recv[1, at, :].astype(F32)
        return jnp.concatenate([first, last], axis=1)

    def finish(self):
        for moved in self.kept:
            moved.wait_send()

    @staticmethod
    def scratch(tokens, width):
        half = width // 2
        return [
            pltpu.VMEM((4, 2, tokens, half), BF16),
            pltpu.VMEM((4, 2, tokens, half), BF16),
            pltpu.VMEM((3, 2, tokens, half), BF16),
            pltpu.VMEM((2, tokens, half), F32),
            pltpu.VMEM((2, tokens, half), BF16),
            pltpu.VMEM((2, tokens, half), BF16),
            pltpu.VMEM((2, tokens, half), BF16),
            pltpu.VMEM((2, tokens, half), BF16),
            pltpu.SemaphoreType.DMA((12,)),
            pltpu.SemaphoreType.DMA((12,)),
        ]


SCATTER_BUFFERS = 10


def pair_product(lefts, rights, tokens):
    def product(chunk, n):
        at = pl.ds(pl.multiple_of(chunk * tokens, tokens), tokens)
        cols = pl.ds(pl.multiple_of(n * 256, 256), 256)
        total = None
        for left, right in zip(lefts, rights):
            term = jnp.dot(left[at, :], right[:, cols], preferred_element_type=F32)
            total = term if total is None else total + term
        return total

    return product


def for_slices(start, stop, body):
    def step(n, none):
        body(pl.ds(pl.multiple_of(n * SLICE, SLICE), SLICE))
        return none

    lax.fori_loop(start // SLICE, stop // SLICE, step, 0)


def middle_kernel(left, right, own_in, gain, middle_out, gathered, *scratch):
    buffers, (block, send, recv) = scratch[:SCATTER_BUFFERS], scratch[SCATTER_BUFFERS:]
    tokens = own_in.shape[0]
    place = Place()
    place.greet()
    scatter = Scatter(place, pair_product([left], [right], tokens), *buffers)
    scatter.run_first()
    scatter.run_second()

    def body(at):
        middle = own_in[at, :].astype(F32) + scatter.rows(at)
        middle_out[at, :] = middle
        block[at, :] = (middle * rms(middle) * gain[...]).astype(BF16)

    gather = Gather(place, block, gathered, send, recv)
    for part in (0, 1):
        scatter.run_third(part)
        for_slices(part * tokens // 2, (part + 1) * tokens // 2, body)
        gather.begin(part)
    gather.pass_on()
    scatter.finish()
    gather.finish()


def turn_kernel(
    left0, left1, right0, right1, middle, gain, cot, normed_far, grad_middle_out, gain_out, grads_out, block_out, *scratch
):
    buffers, (normed, load) = scratch[:SCATTER_BUFFERS], scratch[SCATTER_BUFFERS:]
    loaded = pltpu.make_async_copy(normed_far, normed, load.at[0])
    loaded.start()
    tokens, hidden = cot.shape[0], left0.shape[1]
    place = Place()
    place.greet()
    scatter = Scatter(place, pair_product([left0, left1], [right0, right1], tokens), *buffers)
    scatter.run_first()
    scatter.run_second()
    loaded.wait()

    def weight_grads(n, none):
        at = pl.ds(pl.multiple_of(n * 256, 256), 256)
        for k, part in enumerate((left0, left1)):
            value = lax.dot_general(normed[:, at], part[...], (((0,), (0,)), ((), ())), preferred_element_type=F32)
            grads_out[at, k * hidden : (k + 1) * hidden] = value.astype(BF16)
        return none

    lax.fori_loop(0, normed.shape[1] // 256, weight_grads, 0)
    gain_out[...] = jnp.zeros_like(gain_out)

    def body(at):
        values = middle[at, :]
        grad = scatter.rows(at)
        scale = rms(values)
        weighted = grad * gain[...]
        inner = jnp.mean(values * weighted, axis=-1, keepdims=True)
        total = cot[at, :].astype(F32) + scale * weighted - values * (scale * scale * scale * inner)
        grad_middle_out[at, :] = total
        block_out[at, :] = total.astype(BF16)
        term = grad * values * scale
        gain_out[...] += term[0:8] + term[8:16]

    for part in (0, 1):
        scatter.run_third(part)
        for_slices(part * tokens // 2, (part + 1) * tokens // 2, body)
    scatter.finish()


def spread_kernel(block, w_out, mixed, mixed_out, out_grad, gathered, send, recv, chunk_ref, total, load):
    tokens = block.shape[0]
    place = Place()
    place.greet()
    gather = Gather(place, block, gathered, send, recv)
    gather.begin_whole()
    total[...] = jnp.zeros_like(total)

    def fetch(slot, chunk):
        at = pl.ds(pl.multiple_of(chunk * tokens, tokens), tokens)
        copy = pltpu.make_async_copy(gathered.at[at], chunk_ref.at[slot], load.at[slot])
        copy.start()
        return copy, slot, chunk

    def use(fetched):
        copy, slot, chunk = fetched
        copy.wait()
        use_chunk(chunk_ref.at[slot], chunk)

    def use_chunk(values, chunk):
        at = pl.ds(pl.multiple_of(chunk * tokens, tokens), tokens)
        mixed_out[at, :] = lax.dot_general(values[...], w_out[...], (((1,), (1,)), ((), ())), preferred_element_type=F32)
        part = mixed[at, :]

        def rows(n, none):
            columns = pl.ds(pl.multiple_of(n * 256, 256), 256)
            turned = (((0,), (0,)), ((), ()))
            total[columns, :] += lax.dot_general(values[:, columns], part, turned, preferred_element_type=F32)
            return none

        lax.fori_loop(0, values.shape[1] // 256, rows, 0)

    use_chunk(block, place.chunk(0, 0, 0))
    gather.pass_first()
    gather.finish_core()
    ahead = fetch(0, place.chunk(0, 0, 1))
    use(ahead)
    gather.pass_second()
    ahead = fetch(0, place.chunk(0, 1, 0))
    after = fetch(1, place.chunk(1, 0, 0))
    use(ahead)
    gather.finish_near()
    ahead = fetch(0, place.chunk(0, 1, 1))
    use(after)
    gather.pass_third()
    after = fetch(1, place.chunk(1, 0, 1))
    use(ahead)
    ahead = fetch(0, place.chunk(1, 1, 0))
    use(after)
    gather.finish_far()
    after = fetch(1, place.chunk(1, 1, 1))
    use(ahead)
    use(after)
    out_grad[...] = total[...].astype(BF16)
    gather.finish_sends()


class Owners:
    def __init__(self, place, reduced, out, send, recv):
        self.place, self.reduced, self.out, self.send, self.recv = place, reduced, out, send, recv
        self.own = place.chunk(0, 0, 0)

    def copy(self, number, offset, slot):
        return pltpu.make_async_remote_copy(
            src_ref=self.reduced.at[self.place.chunk(*offset)],
            dst_ref=self.out.at[slot],
            send_sem=self.send.at[number],
            recv_sem=self.recv.at[number],
            device_id=self.place.peer(*offset),
            device_id_type=MESH,
        )

    def begin(self):
        self.keep = pltpu.make_async_copy(self.reduced.at[self.own], self.out.at[self.own], self.send.at[7])
        self.keep.start()
        self.moved = [self.copy(number, offset, self.own) for number, offset in enumerate(OTHERS)]
        for copy in self.moved:
            copy.start()

    def finish(self):
        for number, offset in enumerate(OTHERS):
            self.copy(number, offset, self.place.chunk(*offset)).wait_recv()
        for copy in self.moved:
            copy.wait_send()
        self.keep.wait()


OWNERS_SCRATCH = [pltpu.SemaphoreType.DMA((8,))] * 2
BEYOND = [offset for offset in OTHERS if sum(offset) > 1]


class GateSums:
    def __init__(self, place, count, pieces, rows_recv, gates_all, send, recv):
        self.place, self.count, self.pieces = place, count, pieces
        self.rows_recv, self.gates_all, self.send, self.recv = rows_recv, gates_all, send, recv
        self.me = lax.axis_index("t")
        self.rank = place.g * 2 + place.c
        self.near = [offset for offset in OTHERS if not offset[0]]
        self.moved = []

    def copy(self, number, source, target, peer):
        return pltpu.make_async_remote_copy(
            src_ref=source,
            dst_ref=target,
            send_sem=self.send.at[number],
            recv_sem=self.recv.at[number],
            device_id=peer,
            device_id_type=MESH,
        )

    def begin(self):
        for number, offset in enumerate(self.near):
            other = lax.rem(self.place.chunk(*offset), 4)
            self.moved.append(self.copy(number, self.pieces.at[other], self.rows_recv.at[self.rank], self.place.peer(*offset)))
            self.moved[-1].start()
        self.rows_recv[self.rank] = self.pieces[self.rank]

    def pass_on(self):
        for number, offset in enumerate(self.near):
            other = lax.rem(self.place.chunk(*offset), 4)
            self.copy(number, self.pieces.at[other], self.rows_recv.at[other], self.place.peer(*offset)).wait_recv()
        for step in range(1, self.count):
            to = lax.rem(self.me + step, self.count)
            self.moved.append(self.copy(2 + step, self.rows_recv.at[to], self.gates_all.at[self.me], {"t": to}))
            self.moved[-1].start()
        self.gates_all[self.me] = self.rows_recv[self.me]

    def finish(self, out):
        for step in range(1, self.count):
            other = lax.rem(self.me + self.count - step, self.count)
            self.copy(2 + step, self.rows_recv.at[other], self.gates_all.at[other], {"t": other}).wait_recv()
        total = self.gates_all[0].astype(F32)
        for z in range(1, self.count):
            total = total + self.gates_all[z].astype(F32)
        out[...] = total
        for copy in self.moved:
            copy.wait_send()


class SmallSum:
    def __init__(self, place, count, values, inbox, plane_sum, plane_box, send, recv):
        self.place, self.count, self.values, self.inbox = place, count, values, inbox
        self.plane_sum, self.plane_box, self.send, self.recv = plane_sum, plane_box, send, recv
        self.me = lax.axis_index("t")
        self.moved = []

    def copy(self, number, source, target, peer):
        return pltpu.make_async_remote_copy(
            src_ref=source,
            dst_ref=target,
            send_sem=self.send.at[number],
            recv_sem=self.recv.at[number],
            device_id=peer,
            device_id_type=MESH,
        )

    def begin(self):
        own = self.place.chunk(0, 0, 0)
        for number, offset in enumerate(OTHERS):
            self.moved.append(self.copy(number, self.values, self.inbox.at[own], self.place.peer(*offset)))
            self.moved[-1].start()
        self.inbox[own] = self.values[...]

    def pass_on(self):
        for number, offset in enumerate(OTHERS):
            slot = self.inbox.at[self.place.chunk(*offset)]
            self.copy(number, self.values, slot, self.place.peer(*offset)).wait_recv()
        total = self.inbox[0]
        for n in range(1, 8):
            total = total + self.inbox[n]
        self.plane_sum[...] = total
        self.plane_box[self.me] = total
        for step in range(1, self.count):
            to = {"t": lax.rem(self.me + step, self.count)}
            self.moved.append(self.copy(6 + step, self.plane_sum, self.plane_box.at[self.me], to))
            self.moved[-1].start()

    def finish(self, out):
        for step in range(1, self.count):
            other = lax.rem(self.me + self.count - step, self.count)
            self.copy(6 + step, self.plane_sum, self.plane_box.at[other], {"t": other}).wait_recv()
        total = self.plane_box[0]
        for z in range(1, self.count):
            total = total + self.plane_box[z]
        out[...] = total
        for sent in self.moved:
            sent.wait_send()


def final_kernel(
    left, right, own_in, gain, mlp_gains, grad_middle, reduced, grad_out, values_out, owned,
    gain_sum, own_send, own_recv, *buffers,
):
    tokens, width = own_in.shape
    place = Place()
    place.greet([place.peer(*offset) for offset in BEYOND])
    scatter = Scatter(place, pair_product([left], [right], tokens), *buffers)
    owners = Owners(place, reduced, owned, own_send, own_recv)
    scatter.run_first()
    owners.begin()
    scatter.run_second()
    gain_sum[...] = jnp.zeros_like(gain_sum)

    def body(at):
        x = own_in[at, :].astype(F32)
        grad = scatter.rows(at)
        scale = rms(x)
        weighted = grad * gain[...]
        inner = jnp.mean(x * weighted, axis=-1, keepdims=True)
        grad_out[at, :] = grad_middle[at, :] + scale * weighted - x * (scale * scale * scale * inner)
        term = grad * x * scale
        gain_sum[...] += term[0:8] + term[8:16]

    for part in (0, 1):
        scatter.run_third(part)
        for_slices(part * tokens // 2, (part + 1) * tokens // 2, body)
    lines = width // LANES
    for base, row in ((0, jnp.sum(mlp_gains[...], axis=0, keepdims=True)), (lines, jnp.sum(gain_sum[...], axis=0, keepdims=True))):
        for n in range(lines):
            values_out[base + n : base + n + 1, :] = row[:, n * LANES : (n + 1) * LANES]
    owners.finish()
    scatter.finish()


def final_step(left, right, own_in, gain, mlp_gains, grad_middle, reduced):
    tokens, width = own_in.shape
    return pl.pallas_call(
        final_kernel,
        name="final_step",
        out_shape=(
            jax.ShapeDtypeStruct((tokens, width), F32),
            jax.ShapeDtypeStruct((2 * width // LANES, LANES), F32),
            jax.ShapeDtypeStruct(reduced.shape, reduced.dtype),
        ),
        in_specs=[*whole(6), ANYWHERE],
        out_specs=(*whole(2), ANYWHERE),
        scratch_shapes=[pltpu.VMEM((8, width), F32), *OWNERS_SCRATCH, *Scatter.scratch(tokens, width)],
        compiler_params=mixer_params(7),
    )(left, right, own_in, gain[None], mlp_gains, grad_middle, reduced)


def owners_kernel(
    count, with_gates, pieces, values, reduced0, reduced1, gates_out, gains_out, out0, out1,
    inbox, plane_sum, plane_box, sum_send, sum_recv, rows_recv, gates_all, gates_send, gates_recv,
    send0, recv0, send1, recv1,
):
    place = Place()
    me = lax.axis_index("t")
    place.greet([place.peer(*offset) for offset in BEYOND] + [{"t": lax.rem(me + step, count)} for step in range(1, count)])
    owners = [Owners(place, reduced0, out0, send0, recv0), Owners(place, reduced1, out1, send1, recv1)]
    gates = GateSums(place, count, pieces, rows_recv, gates_all, gates_send, gates_recv)
    gains = SmallSum(place, count, values, inbox, plane_sum, plane_box, sum_send, sum_recv)
    gains.begin()
    if with_gates:
        gates.begin()
    for part in owners:
        part.begin()
    gains.pass_on()
    if with_gates:
        gates.pass_on()
    gains.finish(gains_out)
    if with_gates:
        gates.finish(gates_out)
    else:
        gates_out[...] = jnp.zeros_like(gates_out)
    for part in owners:
        part.finish()


def owners_step(planes, with_gates, pieces, values, reduced):
    block = pieces.shape[1:]
    slots = planes if with_gates else 1
    return pl.pallas_call(
        functools.partial(owners_kernel, planes, with_gates),
        name="owners_step",
        out_shape=(
            jax.ShapeDtypeStruct(block, F32),
            jax.ShapeDtypeStruct(values.shape, F32),
            *[jax.ShapeDtypeStruct(part.shape, part.dtype) for part in reduced],
        ),
        in_specs=[*whole(2), ANYWHERE, ANYWHERE],
        out_specs=(*whole(2), ANYWHERE, ANYWHERE),
        scratch_shapes=[
            pltpu.VMEM((8, *values.shape), F32),
            pltpu.VMEM(values.shape, F32),
            pltpu.VMEM((planes, *values.shape), F32),
            pltpu.SemaphoreType.DMA((planes + 6,)),
            pltpu.SemaphoreType.DMA((planes + 6,)),
            pltpu.VMEM((slots, *block), BF16),
            pltpu.VMEM((slots, *block), BF16),
            pltpu.SemaphoreType.DMA((planes + 2,)),
            pltpu.SemaphoreType.DMA((planes + 2,)),
            *OWNERS_SCRATCH,
            *OWNERS_SCRATCH,
        ],
        compiler_params=mixer_params(8),
    )(pieces, values, *reduced)


def place_kernel(planes, hidden, outs, through, *refs):
    count = len(outs)
    given, passed, results, copied = refs[:count], refs[count : count + through], refs[count + through : 2 * count + through], refs[2 * count + through :]
    for source, target in zip(passed, copied):
        target[...] = source[...]
    for count, sources, out in zip(outs, given, results):
        piece = sources.shape[2] // (count * (planes if hidden else 1))
        for k in range(count):
            if hidden:
                groups = [
                    ((t * 2 + i) * 4 * piece, [(i * 4 + r, (k * planes + t) * piece) for r in range(4)])
                    for t in range(planes)
                    for i in range(2)
                ]
            else:
                groups = [(r * 2 * piece, [(i * 4 + r, k * piece) for i in range(2)]) for r in range(4)]
            for start, parts in groups:
                row = jnp.concatenate([sources[p, :, at : at + piece].astype(F32) for p, at in parts], axis=1)
                if count > 1:
                    out[:, k, start : start + row.shape[1]] = row
                else:
                    out[:, start : start + row.shape[1]] = row


def place_columns(planes, hidden, outs, owned, through=()):
    members, own_rows, columns = owned[0].shape
    total = columns * members // outs[0]
    shapes = [(own_rows, count, total) if count > 1 else (own_rows, total) for count in outs]
    return pl.pallas_call(
        functools.partial(place_kernel, planes, hidden, outs, len(through)),
        name="place_columns",
        out_shape=(
            *[jax.ShapeDtypeStruct(shape, F32) for shape in shapes],
            *[jax.ShapeDtypeStruct(part.shape, part.dtype) for part in through],
        ),
        in_specs=whole(len(owned) + len(through)),
        out_specs=tuple(whole(len(outs) + len(through))),
        compiler_params=pltpu.CompilerParams(vmem_limit_bytes=60 * 1024 * 1024),
    )(*owned, *through)


def last_kernel(planes, own_in, own_out, gates, gains, in_out, out_out, gate_out, taps_out, bias_out, logit_out, decay_out, mlp_out, mix_out):
    place_kernel(planes, False, (2, 1), 0, own_in, own_out, in_out, out_out)
    size, part = gate_out.shape[0], gate_out.shape[2]
    for k in range(2):
        gate_out[:, k, :] = gates[k * size : (k + 1) * size, :part]
    rest = gates[2 * size : 2 * size + 8, :part]
    taps_out[...] = rest[0:4]
    bias_out[...] = rest[4:5]
    logit_out[...] = rest[5:7]
    decay_out[...] = rest[7:8]
    own_rows = mlp_out.shape[1]
    per_line = LANES // own_rows
    index = lax.axis_index("t") * 8 + Place().chunk(0, 0, 0)
    for base, out in ((0, mlp_out), (gains.shape[0] // 2, mix_out)):
        line = gains[pl.ds(base + index // per_line, 1), :]
        value = line[:, :own_rows]
        for n in range(1, per_line):
            value = jnp.where(index % per_line == n, line[:, n * own_rows : (n + 1) * own_rows], value)
        out[...] = value


def last_step(planes, own_in, own_out, gates, gains, size, part):
    members, own_rows, columns = own_out.shape
    shapes = [
        (own_rows, 2, columns * members), (own_rows, columns * members),
        (size, 2, part), (4, part), (1, part), (2, part), (1, part), (1, own_rows), (1, own_rows),
    ]
    return pl.pallas_call(
        functools.partial(last_kernel, planes),
        name="place_last",
        out_shape=tuple(jax.ShapeDtypeStruct(shape, F32) for shape in shapes),
        in_specs=whole(4),
        out_specs=tuple(whole(9)),
        compiler_params=pltpu.CompilerParams(vmem_limit_bytes=60 * 1024 * 1024),
    )(own_in, own_out, gates, gains)


def first_gather(planes, normed, ids):
    tokens, width = normed.shape
    every = (8, *ids.shape)
    return pl.pallas_call(
        functools.partial(first_gather_kernel, planes),
        name="first_gather",
        out_shape=(jax.ShapeDtypeStruct((8 * tokens, width), BF16), *[jax.ShapeDtypeStruct(every, F32)] * 3),
        in_specs=[ANYWHERE, *whole(1)],
        out_specs=(ANYWHERE, *whole(3)),
        scratch_shapes=[pltpu.VMEM(every, F32)] * 3 + GATHER_SCRATCH + [pltpu.SemaphoreType.DMA((9,))] * 2,
        compiler_params=mixer_params(3),
    )(normed, ids)


def middle_step(mixed, w_out, own_in, gain):
    tokens, width = own_in.shape
    return pl.pallas_call(
        middle_kernel,
        name="middle_step",
        out_shape=(jax.ShapeDtypeStruct((tokens, width), F32), jax.ShapeDtypeStruct((8 * tokens, width), BF16)),
        in_specs=whole(4),
        out_specs=(pl.BlockSpec(memory_space=pltpu.VMEM), ANYWHERE),
        scratch_shapes=Scatter.scratch(tokens, width) + [pltpu.VMEM((tokens, width), BF16)] + GATHER_SCRATCH,
        compiler_params=mixer_params(4),
    )(mixed, w_out, own_in, gain[None])


def turn_step(left0, left1, right0, right1, middle, gain, cot, normed):
    tokens, width = cot.shape
    return pl.pallas_call(
        turn_kernel,
        name="turn_step",
        out_shape=(
            jax.ShapeDtypeStruct((tokens, width), F32),
            jax.ShapeDtypeStruct((8, width), F32),
            jax.ShapeDtypeStruct((width, 2 * left1.shape[1]), BF16),
            jax.ShapeDtypeStruct((tokens, width), BF16),
        ),
        in_specs=[*whole(7), ANYWHERE],
        out_specs=tuple(whole(4)),
        scratch_shapes=Scatter.scratch(tokens, width)
        + [pltpu.VMEM(normed.shape, BF16), pltpu.SemaphoreType.DMA((1,))],
        compiler_params=mixer_params(5),
    )(left0, left1, right0, right1, middle, gain[None], cot, normed)


def spread_step(block, w_out, mixed):
    tokens, width = block.shape
    return pl.pallas_call(
        spread_kernel,
        name="turn_spread",
        out_shape=(
            jax.ShapeDtypeStruct((8 * tokens, w_out.shape[0]), F32),
            jax.ShapeDtypeStruct((width, w_out.shape[0]), BF16),
            jax.ShapeDtypeStruct((8 * tokens, width), BF16),
        ),
        in_specs=whole(3),
        out_specs=(*whole(2), ANYWHERE),
        scratch_shapes=GATHER_SCRATCH
        + [
            pltpu.VMEM((2, tokens, width), BF16),
            pltpu.VMEM((width, w_out.shape[0]), F32),
            pltpu.SemaphoreType.DMA((2,)),
        ],
        compiler_params=mixer_params(10),
    )(block, w_out, mixed)


class Swap:
    def __init__(self, quarters, out, send, recv):
        self.quarters, self.out, self.send, self.recv = quarters, out, send, recv
        self.groups = quarters.shape[0]
        self.me = lax.axis_index("g") * 2 + lax.axis_index("c")

    def copy(self, step, other, slot):
        return pltpu.make_async_remote_copy(
            src_ref=self.quarters.at[other],
            dst_ref=self.out.at[:, slot],
            send_sem=self.send.at[step],
            recv_sem=self.recv.at[step],
            device_id={"g": other // 2, "c": other % 2},
            device_id_type=MESH,
        )

    def peers(self):
        others = [lax.rem(self.me + step, self.groups) for step in range(1, self.groups)]
        return [{"g": other // 2, "c": other % 2} for other in others]

    def begin(self):
        self.keep = pltpu.make_async_copy(self.quarters.at[self.me], self.out.at[:, self.me], self.send.at[0])
        self.keep.start()
        self.moved = []
        for step in range(1, self.groups):
            self.moved.append(self.copy(step, lax.rem(self.me + step, self.groups), self.me))
            self.moved[-1].start()

    def finish(self):
        for step in range(1, self.groups):
            other = lax.rem(self.me + self.groups - step, self.groups)
            self.copy(step, other, other).wait_recv()
        for copy in self.moved:
            copy.wait_send()
        self.keep.wait()


def swap_scratch(groups):
    return [pltpu.SemaphoreType.DMA((groups,)), pltpu.SemaphoreType.DMA((groups,))]


def swap_kernel(quarters, out, send, recv):
    move = Swap(quarters, out, send, recv)
    barrier = pltpu.get_barrier_semaphore()
    for peer in move.peers():
        pl.semaphore_signal(barrier, inc=1, device_id=peer, device_id_type=MESH)
    pl.semaphore_wait(barrier, move.groups - 1)
    move.begin()
    move.finish()


def swap(quarters):
    groups, kinds, part, width = quarters.shape
    return pl.pallas_call(
        swap_kernel,
        name="swap",
        out_shape=jax.ShapeDtypeStruct((kinds, groups, part, width), quarters.dtype),
        in_specs=[ANYWHERE],
        out_specs=ANYWHERE,
        scratch_shapes=swap_scratch(groups),
        compiler_params=mixer_params(6),
    )(quarters)


def rms(values):
    return lax.rsqrt(jnp.mean(values * values, axis=-1, keepdims=True) + EPS)


def nt(left, right, out):
    return lax.dot_general(left, right, (((1,), (1,)), ((), ())), preferred_element_type=F32).astype(out)


def tn(left, right, out):
    return lax.dot_general(left, right, (((0,), (0,)), ((), ())), preferred_element_type=F32).astype(out)


def nn(left, right, out):
    return jnp.dot(left, right, preferred_element_type=F32).astype(out)


def per_device(
    inputs, segment_ids, mix_gain, in_weight, conv_weight, conv_bias, gate_weight, gate_bias, decay_param, out_weight,
    mlp_gain, mlp_in, down_weight, cotangent,
):
    planes = lax.axis_size("t")
    rows_here, seg, width = inputs.shape
    row_groups = lax.axis_size("g") * lax.axis_size("c")
    own_tokens = rows_here * seg
    recur_width = conv_weight.shape[1]
    block_width = gate_weight.shape[0]
    members = 2 * row_groups
    channels = recur_width // members
    t, i = lax.axis_index("t"), lax.axis_index("i")
    r = lax.axis_index("g") * lax.axis_size("c") + lax.axis_index("c")
    member = 2 * r + i
    first = member * channels
    own_rows = width // (planes * members)

    own_in = inputs.reshape(own_tokens, width)
    flat_in = own_in.astype(F32)
    scale_in = rms(flat_in)
    cot_own = cotangent.reshape(own_tokens, width)
    own_ids = jnp.pad((segment_ids + 1).astype(F32), ((0, 8 - rows_here), (0, 0)))

    normed, *ids = first_gather(planes, (flat_in * scale_in * mix_gain).astype(BF16), own_ids)
    late_r, ids[0] = lax.optimization_barrier((r, ids[0]))

    direct = planes == row_groups
    in_own = in_weight.transpose(1, 2, 0)
    out_own = out_weight.T[None]
    part = channels // row_groups if direct else 0

    def quarter(weight, part, rank=r):
        return lax.dynamic_slice_in_dim(weight, rank * part, part, weight.ndim - 1)

    def spread_units(weight):
        return lax.all_gather(weight, "t", axis=0, tiled=False)

    def whole_units(weight):
        every = lax.all_gather(weight, ("t", "i"), axis=1, tiled=True)
        return lax.dynamic_slice_in_dim(every, first, channels, 1)

    if direct:
        in_w = swap(spread_units(quarter(in_weight, part).transpose(1, 2, 0)))
        out_quarters = spread_units(quarter(out_weight, part).T[None])
    else:
        in_w = whole_units(in_own)
        out_quarters = jnp.zeros((row_groups, 1, 16, width), BF16)
    in_w = in_w.reshape(2 * channels, width)
    hidden_part = mlp_in.shape[2] // row_groups
    gated = quarter(mlp_in, hidden_part, late_r).transpose(1, 2, 0)
    w_left, w_right, w_down = [
        spread_units(part).reshape(-1, width)
        for part in (gated[0], gated[1], quarter(down_weight, hidden_part, late_r).T)
    ]

    def own(values):
        return lax.dynamic_slice_in_dim(values, first, channels, values.ndim - 1)

    vec = own(
        jnp.concatenate(
            [
                conv_weight,
                conv_bias[None],
                gate_bias,
                8.0 * jax.nn.softplus(-decay_param)[None],
                8.0 * jax.nn.sigmoid(-decay_param)[None],
                jnp.zeros((7, recur_width), F32),
            ]
        )
    )
    gate_blocks = own(gate_weight).transpose(1, 0, 2)
    blocks = channels // block_width

    branches = nt(normed, in_w, F32)
    conv_low, decay, states, mixed, halo, cin, mask, cot, w_out = mixer_forward(
        planes, seg, rows_here, branches, ids, gate_blocks, vec, cot_own, out_quarters
    )
    w_out = (w_out if direct else whole_units(out_own)).reshape(channels, width)
    middle, normed_two = middle_step(mixed, w_out, own_in, mlp_gain)
    left = nt(normed_two, w_left, F32)
    right = nt(normed_two, w_right, F32)
    act, slope = gelu_parts(left)
    hidden = (act * right).astype(BF16)
    hidden, act, slope = lax.optimization_barrier((hidden, act.astype(BF16), (right * slope).astype(BF16)))

    def over_planes(grad):
        return lax.psum_scatter(grad, "t", scatter_dimension=0, tiled=True)

    grad_down = tn(cot, hidden, BF16)
    grad_down, hidden, w_down = lax.optimization_barrier((grad_down, hidden, w_down))
    grad_down = over_planes(grad_down)
    grad_hidden = nt(cot, w_down, F32)
    grad_left = (grad_hidden * slope.astype(F32)).astype(BF16)
    grad_right = (grad_hidden * act.astype(F32)).astype(BF16)
    grad_middle, grad_mlp_gain, grad_mlp_in, grad_mid_own = turn_step(
        grad_left, grad_right, w_left, w_right, middle, mlp_gain, cot_own, normed_two
    )
    grad_down, grad_mid_own = lax.optimization_barrier((grad_down, grad_mid_own))
    grad_mlp_in = over_planes(grad_mlp_in)
    grad_mixed, grad_out, _ = spread_step(grad_mid_own, w_out, mixed)

    def by_owner(grad):
        return grad.reshape(members, own_rows, -1)

    grad_branches, gw0, gw1, small, pieces, outputs, owned_down = mixer_backward(
        planes, seg, grad_mixed, branches, states, decay, conv_low, mask, halo, cin, gate_blocks, vec, hidden, w_down, middle,
        by_owner(grad_down),
    )
    grad_mlp_in, grad_branches = lax.optimization_barrier((grad_mlp_in, grad_branches))
    grad_out = over_planes(grad_out)
    grad_in = tn(normed, grad_branches, BF16)
    grad_in, grad_branches = lax.optimization_barrier((grad_in, grad_branches))
    grad_in = over_planes(grad_in)
    outputs = outputs.reshape(inputs.shape)

    grad_inputs, values, owned_mlp_in = final_step(
        grad_branches, in_w, own_in, mix_gain, grad_mlp_gain, grad_middle, by_owner(grad_mlp_in)
    )
    gate_grads, gains, owned_in, owned_out = owners_step(planes, direct, pieces, values, [by_owner(grad_in), by_owner(grad_out)])
    grad_inputs = grad_inputs.reshape(inputs.shape)
    def columns(hidden, outs, owned, through=()):
        if direct:
            return place_columns(planes, hidden, outs, owned, through)
        owned = jnp.concatenate(owned, axis=2)
        owned = owned.reshape(2, row_groups, own_rows, sum(outs), planes if hidden else 1, -1).astype(F32)
        order = (2, 3, 4, 0, 1, 5) if hidden else (2, 3, 1, 0, 4, 5)
        owned = owned.transpose(order).reshape(own_rows, sum(outs), -1)
        return (owned[:, :2], owned[:, 2], *through)

    grad_mlp_in, grad_down_weight, outputs, grad_inputs = columns(
        True, (2, 1), [owned_mlp_in, owned_down], [outputs, grad_inputs]
    )
    if direct:
        grad_in_weight, grad_out_weight, grad_gate_weight, taps, bias, logit_bias, decay_grad, mlp_sum, mix_sum = last_step(
            planes, owned_in, owned_out, gate_grads, gains, block_width, part
        )
        bias, decay_grad, mlp_sum, mix_sum = bias[0], decay_grad[0], mlp_sum[0], mix_sum[0]
    else:
        grad_in_weight, grad_out_weight = columns(False, (2, 1), [owned_in, owned_out])
        index = ((t * 2 + i) * row_groups + r) * own_rows
        mlp_sum, mix_sum = lax.dynamic_slice_in_dim(gains.reshape(2, width), index, own_rows, 1)
        column_block = lax.broadcasted_iota(jnp.int32, (block_width, channels), 1) // block_width

        def diagonal(gw):
            return sum(
                jnp.where(column_block == n, gw[n * block_width : (n + 1) * block_width], 0.0) for n in range(blocks)
            )

        gate_grads = jnp.concatenate([diagonal(gw0), diagonal(gw1), small], axis=0)
        placed = jnp.zeros((gate_grads.shape[0], recur_width), F32)
        placed = lax.dynamic_update_slice_in_dim(placed, gate_grads, first, 1)
        gate_grads = lax.psum_scatter(placed, EVERY, scatter_dimension=1, tiled=True)
        grad_gate_weight = jnp.stack([gate_grads[:block_width], gate_grads[block_width : 2 * block_width]], axis=1)
        rest = gate_grads[2 * block_width :]
        taps, bias, logit_bias, decay_grad = rest[0:4], rest[4], rest[5:7], rest[7]
    return (
        outputs,
        grad_inputs,
        mix_sum,
        grad_in_weight,
        taps,
        bias,
        grad_gate_weight,
        logit_bias,
        decay_grad,
        grad_out_weight,
        mlp_sum,
        grad_mlp_in,
        grad_down_weight,
    )


def solution(mesh):
    seq, rows = mesh.shape["seq"], mesh.shape["rows"]
    grid = Mesh(mesh.devices.reshape(seq // 2, 2, rows // 2, 2), EVERY)
    row_axes, seq_axes = ("g", "c"), ("t", "i")
    tokens = P(row_axes, seq_axes, None)
    return jax.shard_map(
        per_device,
        mesh=grid,
        in_specs=(
            tokens,
            P(row_axes, seq_axes),
            P(),
            P(None, None, seq_axes),
            P(),
            P(),
            P(),
            P(),
            P(),
            P(None, seq_axes),
            P(),
            P(None, None, seq_axes),
            P(None, seq_axes),
            tokens,
        ),
        out_specs=(
            tokens,
            tokens,
            P(EVERY),
            P(EVERY, None, None),
            P(None, EVERY),
            P(EVERY),
            P(None, None, EVERY),
            P(None, EVERY),
            P(EVERY),
            P(EVERY, None),
            P(EVERY),
            P(EVERY, None, None),
            P(EVERY, None),
        ),
        check_vma=False,
    )
```

```python
import functools

import jax
import jax.numpy as jnp
from jax import lax
from jax.experimental import pallas as pl
from jax.experimental.pallas import tpu as pltpu
from jax.sharding import Mesh
from jax.sharding import PartitionSpec as P

EPS = 1e-06
MESH = pl.DeviceIdType.MESH
PLANE = ("i", "g", "c")
EVERY = ("t", "i", "g", "c")
F32 = jnp.float32
BF16 = jnp.bfloat16
GELU_A = 0.7978845608028654
GELU_B = 0.044715
HALO = 8
LANES = 128
SLICE = 16
ANYWHERE = pl.BlockSpec(memory_space=pl.ANY)
GATHER_SCRATCH = [pltpu.SemaphoreType.DMA((14,))] * 2


def gelu_parts(x):
    square = x * x
    th = jnp.tanh(GELU_A * x * (1.0 + GELU_B * square))
    half = 0.5 * (1.0 + th)
    slope = half + 0.5 * x * (1.0 - th * th) * (GELU_A * (1.0 + 3.0 * GELU_B * square))
    return x * half, slope


def one_minus_exp(y, power):
    series = 1.0 + y * (-1.0 / 2 + y * (1.0 / 6 + y * (-1.0 / 24 + y * (1.0 / 120 + y * (-1.0 / 720 + y * (1.0 / 5040))))))
    return jnp.where(y < 0.35, y * series, 1.0 - power)


def sigmoid(x):
    return 1.0 / (1.0 + jnp.exp(-x))


def gate_values(conv_low, wg0, wg1, vec):
    logits0 = jnp.dot(conv_low, wg0, preferred_element_type=F32) + vec[5:6]
    logits1 = jnp.dot(conv_low, wg1, preferred_element_type=F32) + vec[6:7]
    recur_gate = sigmoid(logits0)
    input_gate = sigmoid(logits1)
    log_decay = -vec[7:8] * recur_gate
    return recur_gate, input_gate, log_decay


def spread_blocks(gates, out):
    size, width = gates.shape[1], gates.shape[2]
    column = lax.broadcasted_iota(jnp.int32, (size, width), 1) // size
    for k in range(2):
        block = gates[k].astype(F32)
        for n in range(width // size):
            out[k, n * size : (n + 1) * size, :] = jnp.where(column == n, block, 0.0).astype(BF16)


def put_tiles(ref, at, values):
    tiles, lanes = ref.shape[0], ref.shape[2]
    short = tiles * lanes - values.shape[1]
    if short:
        values = jnp.concatenate([values, jnp.zeros((values.shape[0], short), values.dtype)], axis=1)
    for j in range(tiles):
        ref[j, at, :] = values[:, j * lanes : (j + 1) * lanes]


def get_tiles(ref, at, width):
    joined = jnp.concatenate([ref[j, at, :] for j in range(ref.shape[0])], axis=1)
    return joined[:, :width]


def join_tiles(parts, width):
    return jnp.concatenate(parts, axis=1)[:, :width]


def exchange_copy(step, send, target, other, send_sem, recv_sem):
    return pltpu.make_async_remote_copy(
        src_ref=send,
        dst_ref=target,
        send_sem=send_sem.at[step],
        recv_sem=recv_sem.at[step],
        device_id={"t": other},
        device_id_type=MESH,
    )


def exchange_start(count, me, send, slots, send_sem, recv_sem):
    for step in range(1, count):
        exchange_copy(step, send, slots.at[me], lax.rem(me + step, count), send_sem, recv_sem).start()


def exchange_wait(count, me, send, slots, send_sem, recv_sem):
    for step in range(1, count):
        other = lax.rem(me + count - step, count)
        exchange_copy(step, send, slots.at[other], other, send_sem, recv_sem).wait()


def mixer_forward_kernel(
    count, seg, rows_here, branches_far, ids, ids_before, ids_after, gate_blocks, vec_ref, cot, quarters,
    conv_out, decay_out, states_out, mixed_out, halo_out, cin_out, mask, cot_out, swapped,
    drive, h_ref, a_ref, ext, halo_send, halo_recv, summary, slots, send_sem, recv_sem, halo_sems,
    gather_send, gather_recv, swap_send, swap_recv, branches, wg, load,
):
    place = Place()
    me = lax.axis_index("t")
    loaded = pltpu.make_async_copy(branches_far, branches, load.at[0])
    loaded.start()
    place.greet([place.peer(0, 1, 1)] + [{"t": lax.rem(me + step, count)} for step in range(1, count)])
    gather = Gather(place, cot, cot_out, gather_send, gather_recv)
    move = Swap(quarters, swapped, swap_send, swap_recv)
    gather.begin_whole()
    move.begin()
    spread_blocks(gate_blocks, wg)
    rows = 8
    width = branches.shape[1] // 2
    loaded.wait()

    def recur_at(at):
        return branches[at, width:].astype(BF16).astype(F32)

    for r in range(rows):
        halo_send[r * HALO : (r + 1) * HALO, :] = recur_at(pl.ds((rows + r + 1) * seg - HALO, HALO))
    halo_copy = pltpu.make_async_remote_copy(
        src_ref=halo_send,
        dst_ref=halo_recv,
        send_sem=halo_sems.at[0],
        recv_sem=halo_sems.at[1],
        device_id={"t": lax.rem(me + 1, count)},
        device_id_type=MESH,
    )
    halo_copy.start()
    for r in range(rows):
        halo_out[(rows + r) * HALO : (rows + r + 1) * HALO, :] = recur_at(pl.ds((r + 1) * seg - HALO, HALO))
    vec = vec_ref[...]

    def ids_of(ref, s):
        chunk = s // rows_here
        return ref[chunk, s % rows_here : s % rows_here + 1, :]

    nothing = jnp.zeros((1, LANES), F32)
    for s in range(2 * rows):
        here = ids_of(ids, s)
        back = ids_of(ids, s - rows) if s >= rows else jnp.where(me > 0, ids_of(ids_before, s + rows), nothing)
        ahead = ids_of(ids, s + rows) if s < rows else jnp.where(me < count - 1, ids_of(ids_after, s - rows), nothing)
        lines = [jnp.concatenate([back[:, seg - k :], here[:, : seg - k]], axis=1) for k in (1, 2, 3)]
        lines += [jnp.concatenate([here[:, k:], ahead[:, :k]], axis=1) for k in (1, 2, 3)]
        lines = [jnp.where(line == here, 1.0, 0.0) for line in lines] + [nothing] * 2
        mask[s * seg : (s + 1) * seg, :] = jnp.concatenate(lines, axis=0).T

    def local(s, none):
        at = pl.ds(pl.multiple_of(s * seg, seg), seg)
        x = recur_at(at)
        ext[0:HALO, :] = halo_out[pl.ds(pl.multiple_of(s * HALO, HALO), HALO), :]
        ext[HALO : HALO + seg, :] = x
        m = mask[at, :]
        conv = vec[4:5] + vec[0:1] * x
        for k in range(1, 4):
            conv = conv + vec[k : k + 1] * ext[HALO - k : HALO - k + seg, :] * m[:, k - 1 : k]
        conv_low = conv.astype(BF16)
        conv_out[at, :] = conv_low
        recur_gate, input_gate, log_decay = gate_values(conv_low, wg[0], wg[1], vec)
        keep = m[:, 0:1]
        kept = jnp.exp(log_decay)
        put_tiles(decay_out, at, kept * keep)
        scale = (1.0 - keep) + keep * jnp.sqrt(one_minus_exp(-2.0 * log_decay, kept * kept))
        put_tiles(drive, at, scale * input_gate * conv_low.astype(F32))
        return none

    lax.fori_loop(rows, 2 * rows, local, 0)
    halo_copy.wait()
    for r in range(rows):
        halo_out[r * HALO : (r + 1) * HALO, :] = halo_recv[r * HALO : (r + 1) * HALO, :]
    gather.pass_first()
    lax.fori_loop(0, rows, local, 0)
    tiles, lanes = drive.shape[0], drive.shape[2]

    def scan(k, carried):
        at = pl.ds(k, 2 * rows, stride=seg)
        after = []
        for j in range(tiles):
            h, a = carried[j]
            d = decay_out[j, at, :]
            h = d * h + drive[j, at, :]
            a = a * d
            h_ref[j, at, :] = h
            a_ref[j, at, :] = a
            after.append((h, a))
        return tuple(after)

    start = (jnp.zeros((2 * rows, lanes), F32), jnp.ones((2 * rows, lanes), F32))
    last = lax.fori_loop(0, seg, scan, (start,) * tiles, unroll=4)
    last_h = join_tiles([part[0] for part in last], width)
    last_a = join_tiles([part[1] for part in last], width)
    summary[0:rows, :] = last_a[rows:] * last_a[:rows]
    summary[rows : 2 * rows, :] = last_a[rows:] * last_h[:rows] + last_h[rows:]
    exchange_start(count, me, summary, slots, send_sem, recv_sem)
    gather.pass_second()

    def activate(s, none):
        at = pl.ds(pl.multiple_of(s * seg, seg), seg)
        act, _ = gelu_parts(branches[at, :width])
        states_out[at, :] = act
        return none

    lax.fori_loop(0, 2 * rows, activate, 0)
    exchange_wait(count, me, summary, slots, send_sem, recv_sem)
    carry = jnp.zeros((rows, width), F32)
    for z in range(count - 1):
        carry = jnp.where(z < me, slots[z, 0:rows, :] * carry + slots[z, rows : 2 * rows, :], carry)
    cin_out[0:rows, :] = carry
    cin_out[rows : 2 * rows, :] = last_a[:rows] * carry + last_h[:rows]

    def finish(s, none):
        at = pl.ds(pl.multiple_of(s * seg, seg), seg)
        states = get_tiles(h_ref, at, width) + get_tiles(a_ref, at, width) * cin_out[pl.ds(s, 1), :]
        act = states_out[at, :]
        states_out[at, :] = states
        mixed_out[at, :] = (act * states.astype(BF16).astype(F32)).astype(BF16)
        return none

    lax.fori_loop(0, 2 * rows, finish, 0)
    gather.pass_third()
    gather.finish()
    move.finish()


def mixer_backward_kernel(
    count, seg, grad_mixed_far, branches_far, states_far, decay_far, conv_far, mask_far, halo, cin, gate_blocks, vec_ref,
    hidden, w_down, middle_far, reduced, grad_out, gw0_out, gw1_out, small_out, pieces_out, outputs, owned,
    tot, prod, ext, halo_send, halo_recv, summary, slots, uin, send_sem, recv_sem, halo_sems,
    grad_mixed, branches, states, decay, conv_low_ref, mask, middle, wg, load, own_send, own_recv, *buffers,
):
    place = Place()
    pairs = (
        (grad_mixed_far, grad_mixed),
        (branches_far, branches),
        (states_far, states),
        (decay_far, decay),
        (conv_far, conv_low_ref),
        (mask_far, mask),
        (middle_far, middle),
    )
    loads = [pltpu.make_async_copy(far, near, load.at[n]) for n, (far, near) in enumerate(pairs)]
    for part in loads:
        part.start()
    me = lax.axis_index("t")
    place.greet([place.peer(*offset) for offset in BEYOND] + [{"t": lax.rem(me + step, count)} for step in range(1, count)])
    scatter = Scatter(place, pair_product([hidden], [w_down], outputs.shape[0]), *buffers)
    owners = Owners(place, reduced, owned, own_send, own_recv)
    spread_blocks(gate_blocks, wg)
    scatter.run_first()
    owners.begin()
    for part in loads:
        part.wait()
    rows = 8
    width = branches.shape[1] // 2
    vec = vec_ref[...]

    def local(s, none):
        at = pl.ds(pl.multiple_of(s * seg, seg), seg)
        act, slope = gelu_parts(branches[at, :width])
        gm = grad_mixed[at, :].astype(F32)
        grad_out[at, :width] = (gm * states[at, :].astype(BF16).astype(F32) * slope).astype(BF16)
        put_tiles(tot, at, (gm * act).astype(BF16).astype(F32))
        return none

    lax.fori_loop(0, 2 * rows, local, 0)

    tiles, lanes = tot.shape[0], tot.shape[2]

    def scan(k, carried):
        at = pl.ds(seg - 1 - k, 2 * rows, stride=seg)
        after = []
        for j in range(tiles):
            u, p = carried[j]
            d = decay[j, at, :]
            total = tot[j, at, :] + u
            tot[j, at, :] = total
            prod[j, at, :] = p
            after.append((d * total, d * p))
        return tuple(after)

    start = (jnp.zeros((2 * rows, lanes), F32), jnp.ones((2 * rows, lanes), F32))
    last = lax.fori_loop(0, seg, scan, (start,) * tiles, unroll=4)
    u = join_tiles([part[0] for part in last], width)
    p = join_tiles([part[1] for part in last], width)
    summary[0:rows, :] = p[:rows] * p[rows:]
    summary[rows : 2 * rows, :] = p[:rows] * u[rows:] + u[:rows]
    exchange_start(count, me, summary, slots, send_sem, recv_sem)
    scatter.run_second()
    exchange_wait(count, me, summary, slots, send_sem, recv_sem)
    carry = jnp.zeros((rows, width), F32)
    for z in range(count - 1, 0, -1):
        carry = jnp.where(z > me, slots[z, 0:rows, :] * carry + slots[z, rows : 2 * rows, :], carry)
    uin[rows : 2 * rows, :] = carry
    uin[0:rows, :] = p[rows:] * carry + u[rows:]
    gw0_out[...] = jnp.zeros_like(gw0_out)
    gw1_out[...] = jnp.zeros_like(gw1_out)
    small_out[...] = jnp.zeros_like(small_out)

    def gates(s, none):
        at = pl.ds(pl.multiple_of(s * seg, seg), seg)
        total = get_tiles(tot, at, width) + get_tiles(prod, at, width) * uin[pl.ds(s, 1), :]
        ext[HALO - 1 : HALO, :] = cin[pl.ds(s, 1), :]
        ext[HALO : HALO + seg, :] = states[at, :]
        before = ext[HALO - 1 : HALO - 1 + seg, :]
        conv_low = conv_low_ref[at, :]
        conv_vals = conv_low.astype(F32)
        m = mask[at, :]
        keep = m[:, 0:1]
        recur_gate, input_gate, log_decay = gate_values(conv_low, wg[0], wg[1], vec)
        power = jnp.exp(2.0 * log_decay)
        gone = one_minus_exp(-2.0 * log_decay, power)
        inverse = lax.rsqrt(gone)
        root = gone * inverse
        scale = (1.0 - keep) + keep * root
        driven_in = total * conv_vals
        grad_log = total * before * get_tiles(decay, at, width) - driven_in * input_gate * keep * (power * inverse)
        grad0 = grad_log * log_decay * (1.0 - recur_gate)
        grad1 = driven_in * scale * input_gate * (1.0 - input_gate)
        low0 = grad0.astype(BF16)
        low1 = grad1.astype(BF16)
        inputs_of = (((1,), (1,)), ((), ()))
        grad_conv = (
            total * scale * input_gate
            + lax.dot_general(low0, wg[0], inputs_of, preferred_element_type=F32)
            + lax.dot_general(low1, wg[1], inputs_of, preferred_element_type=F32)
        )
        put_tiles(tot, at, grad_conv)
        turned = (((0,), (0,)), ((), ()))
        gw0_out[...] += lax.dot_general(conv_low, low0, turned, preferred_element_type=F32)
        gw1_out[...] += lax.dot_general(conv_low, low1, turned, preferred_element_type=F32)
        x = branches[at, width:].astype(BF16).astype(F32)
        ext[0:HALO, :] = halo[pl.ds(pl.multiple_of(s * HALO, HALO), HALO), :]
        ext[HALO : HALO + seg, :] = x

        def add(row, values):
            small_out[row : row + 1, :] += jnp.sum(values, axis=0, keepdims=True)

        add(0, grad_conv * x)
        for k in range(1, 4):
            add(k, grad_conv * ext[HALO - k : HALO - k + seg, :] * m[:, k - 1 : k])
        add(4, grad_conv)
        add(5, grad0)
        add(6, grad1)
        add(7, grad_log * recur_gate)
        return none

    lax.fori_loop(0, 2 * rows, gates, 0)
    small_out[7:8, :] = small_out[7:8, :] * vec[8:9]
    size, part = gate_blocks.shape[1], width // 4

    def padded(values):
        short = [values, jnp.zeros((values.shape[0], LANES - part), F32)]
        return jnp.concatenate(short, axis=1)

    for r in range(4):
        first = r * part // size * size
        at = slice(r * part, (r + 1) * part)
        for k, square in enumerate((gw0_out, gw1_out)):
            pieces_out[r, k * size : (k + 1) * size, :] = padded(square[first : first + size, at]).astype(BF16)
        rest = jnp.concatenate([padded(small_out[:, at]), jnp.zeros((8, LANES), F32)], axis=0)
        pieces_out[r, 2 * size :, :] = rest.astype(BF16)
    for r in range(rows):
        halo_send[r * HALO : (r + 1) * HALO, :] = get_tiles(tot, pl.ds(r * seg, HALO), width)
    halo_copy = pltpu.make_async_remote_copy(
        src_ref=halo_send,
        dst_ref=halo_recv,
        send_sem=halo_sems.at[0],
        recv_sem=halo_sems.at[1],
        device_id={"t": lax.rem(me + count - 1, count)},
        device_id_type=MESH,
    )
    halo_copy.start()

    def back(s, none):
        at = pl.ds(pl.multiple_of(s * seg, seg), seg)
        m = mask[at, :]
        grad_conv = get_tiles(tot, at, width)
        ext[0:seg, :] = grad_conv
        result = vec[0:1] * grad_conv

        @pl.when(s < rows)
        def _():
            ext[seg : seg + HALO, :] = get_tiles(tot, pl.ds(pl.multiple_of((s + rows) * seg, seg), HALO), width)

        @pl.when(s >= rows)
        def _():
            ext[seg : seg + HALO, :] = halo_recv[pl.ds(pl.multiple_of((s - rows) * HALO, HALO), HALO), :]

        for k in range(1, 4):
            result = result + vec[k : k + 1] * ext[k : k + seg, :] * m[:, 2 + k : 3 + k]
        grad_out[at, width:] = result.astype(BF16)
        return none

    lax.fori_loop(0, rows, back, 0)
    halo_copy.wait()
    lax.fori_loop(rows, 2 * rows, back, 0)
    scatter.run_third(0)
    scatter.run_third(1)

    def body(at):
        outputs[at, :] = (middle[at, :] + scatter.rows(at)).astype(BF16)

    for_slices(0, outputs.shape[0], body)
    scatter.finish()
    owners.finish()


def whole(count):
    return [pl.BlockSpec(memory_space=pltpu.VMEM)] * count


def mixer_params(number):
    return pltpu.CompilerParams(collective_id=number, has_side_effects=True, vmem_limit_bytes=60 * 1024 * 1024)


def mixer_forward(count, seg, rows_here, branches, ids, gate_blocks, vec, cot, quarters):
    n, width = branches.shape[0], branches.shape[1] // 2
    full = functools.partial(jax.ShapeDtypeStruct, (n, width))
    tiles = -(-width // LANES)
    tiled = jax.ShapeDtypeStruct((tiles, n, LANES), F32)
    groups, kinds, part, depth = quarters.shape
    return pl.pallas_call(
        functools.partial(mixer_forward_kernel, count, seg, rows_here),
        name="mixer_forward",
        out_shape=(
            full(BF16), tiled, full(F32), full(BF16),
            jax.ShapeDtypeStruct((16 * HALO, width), F32), jax.ShapeDtypeStruct((16, width), F32),
            jax.ShapeDtypeStruct((n, 8), F32),
            jax.ShapeDtypeStruct((8 * cot.shape[0], cot.shape[1]), BF16),
            jax.ShapeDtypeStruct((kinds, groups, part, depth), BF16),
        ),
        in_specs=[ANYWHERE, *whole(5), ANYWHERE, ANYWHERE],
        out_specs=(*whole(7), ANYWHERE, ANYWHERE),
        scratch_shapes=[
            pltpu.VMEM((tiles, n, LANES), F32),
            pltpu.VMEM((tiles, n, LANES), F32),
            pltpu.VMEM((tiles, n, LANES), F32),
            pltpu.VMEM((seg + HALO, width), F32),
            pltpu.VMEM((8 * HALO, width), F32),
            pltpu.VMEM((8 * HALO, width), F32),
            pltpu.VMEM((16, width), F32),
            pltpu.VMEM((count, 16, width), F32),
            pltpu.SemaphoreType.DMA((count,)),
            pltpu.SemaphoreType.DMA((count,)),
            pltpu.SemaphoreType.DMA((2,)),
            *GATHER_SCRATCH,
            *swap_scratch(groups),
            pltpu.VMEM(branches.shape, F32),
            pltpu.VMEM((2, width, width), BF16),
            pltpu.SemaphoreType.DMA((1,)),
        ],
        compiler_params=mixer_params(1),
    )(branches, *ids, gate_blocks, vec, cot, quarters)


def mixer_backward(count, seg, grad_mixed, branches, states, decay, conv_low, mask, halo, cin, gate_blocks, vec, hidden, w_down, middle, reduced):
    n, width = branches.shape[0], branches.shape[1] // 2
    tokens, depth = n // 8, w_down.shape[1]
    full = functools.partial(jax.ShapeDtypeStruct, (n, width))
    tiles = -(-width // LANES)
    tiled = jax.ShapeDtypeStruct((tiles, n, LANES), F32)
    return pl.pallas_call(
        functools.partial(mixer_backward_kernel, count, seg),
        name="mixer_backward",
        out_shape=(
            jax.ShapeDtypeStruct((n, 2 * width), BF16),
            jax.ShapeDtypeStruct((width, width), F32), jax.ShapeDtypeStruct((width, width), F32),
            jax.ShapeDtypeStruct((8, width), F32),
            jax.ShapeDtypeStruct((4, 2 * gate_blocks.shape[1] + 16, LANES), BF16),
            jax.ShapeDtypeStruct((tokens, depth), BF16),
            jax.ShapeDtypeStruct(reduced.shape, BF16),
        ),
        in_specs=[*[ANYWHERE] * 6, *whole(6), *[ANYWHERE] * 2],
        out_specs=(*whole(6), ANYWHERE),
        scratch_shapes=[
            pltpu.VMEM((tiles, n, LANES), F32),
            pltpu.VMEM((tiles, n, LANES), F32),
            pltpu.VMEM((seg + HALO, width), F32),
            pltpu.VMEM((8 * HALO, width), F32),
            pltpu.VMEM((8 * HALO, width), F32),
            pltpu.VMEM((16, width), F32),
            pltpu.VMEM((count, 16, width), F32),
            pltpu.VMEM((16, width), F32),
            pltpu.SemaphoreType.DMA((count,)),
            pltpu.SemaphoreType.DMA((count,)),
            pltpu.SemaphoreType.DMA((2,)),
            *[pltpu.VMEM(part.shape, part.dtype) for part in (grad_mixed, branches, states, decay, conv_low, mask, middle)],
            pltpu.VMEM((2, width, width), BF16),
            pltpu.SemaphoreType.DMA((7,)),
            *[pltpu.SemaphoreType.DMA((8,))] * 2,
            *Scatter.scratch(tokens, depth),
        ],
        compiler_params=mixer_params(2),
    )(grad_mixed, branches, states, decay, conv_low, mask, halo, cin, gate_blocks, vec, hidden, w_down, middle, reduced)


class Place:
    def __init__(self):
        self.i, self.g, self.c = lax.axis_index("i"), lax.axis_index("g"), lax.axis_index("c")
        self.core, self.across, self.along = {"c": 1 - self.c}, {"g": 1 - self.g}, {"i": 1 - self.i}

    def chunk(self, di, dg, dc):
        i = 1 - self.i if di else self.i
        g = 1 - self.g if dg else self.g
        c = 1 - self.c if dc else self.c
        return (i * 2 + g) * 2 + c

    def peer(self, di, dg, dc):
        return {
            "i": 1 - self.i if di else self.i,
            "g": 1 - self.g if dg else self.g,
            "c": 1 - self.c if dc else self.c,
        }

    def greet(self, more=()):
        barrier = pltpu.get_barrier_semaphore()
        peers = [self.core, self.across, self.along, *more]
        for peer in peers:
            pl.semaphore_signal(barrier, inc=1, device_id=peer, device_id_type=MESH)
        pl.semaphore_wait(barrier, len(peers))


class Gather:
    COPIES = 12

    def __init__(self, place, block, out, send, recv):
        self.place, self.block, self.out, self.send, self.recv = place, block, out, send, recv
        self.tokens = block.shape[0]
        self.half = self.tokens // 2

    def rows(self, chunk, part):
        start = chunk * self.tokens + (self.half if part == 1 else 0)
        return self.out.at[pl.ds(pl.multiple_of(start, self.half), self.tokens if part == 2 else self.half)]

    def mine(self, part):
        if part == 2:
            return self.block
        return self.block.at[pl.ds(part * self.half, self.half)]

    def copy(self, number, source, chunk, part, peer):
        return pltpu.make_async_remote_copy(
            src_ref=source,
            dst_ref=self.rows(chunk, part),
            send_sem=self.send.at[number],
            recv_sem=self.recv.at[number],
            device_id=peer,
            device_id_type=MESH,
        )

    def begin(self, part, whole=False):
        place = self.place
        own = place.chunk(0, 0, 0)
        other = 1 - part if whole else part
        self.give(0 + part, own, part, place.across)
        self.give(2 + other, own, other, place.along)
        self.give(4 + part, own, part, place.core)
        keep = pltpu.make_async_copy(self.mine(part), self.rows(own, part), self.send.at[self.COPIES + part])
        keep.start()
        self.local = getattr(self, "local", []) + [keep]

    def begin_whole(self):
        self.begin(0, True)
        self.begin(1, True)

    def give(self, number, chunk, part, peer):
        moved = self.copy(number, self.mine(part), chunk, part, peer)
        moved.start()
        self.kept = getattr(self, "kept", []) + [moved]

    def arrived(self, number, chunk, part):
        self.copy(number, self.rows(chunk, part), chunk, part, self.place.core).wait_recv()

    def forward(self, number, chunk, part, peer):
        moved = self.copy(number, self.rows(chunk, part), chunk, part, peer)
        moved.start()
        self.kept.append(moved)

    def pass_first(self):
        place = self.place
        ax, al = place.chunk(0, 1, 0), place.chunk(1, 0, 0)
        self.arrived(0, ax, 0)
        self.forward(6, ax, 0, place.along)
        self.arrived(3, al, 1)
        self.forward(7, al, 1, place.across)

    def pass_second(self):
        place = self.place
        ax, al = place.chunk(0, 1, 0), place.chunk(1, 0, 0)
        self.arrived(1, ax, 1)
        self.forward(8, ax, 2, place.core)
        self.arrived(2, al, 0)
        self.forward(9, al, 2, place.core)

    def pass_third(self):
        dia = self.place.chunk(1, 1, 0)
        self.arrived(6, dia, 0)
        self.forward(10, dia, 0, self.place.core)
        self.arrived(7, dia, 1)
        self.forward(11, dia, 1, self.place.core)

    def pass_on(self):
        self.pass_first()
        self.pass_second()
        self.pass_third()

    def finish_core(self):
        for part in (0, 1):
            self.arrived(4 + part, self.place.chunk(0, 0, 1), part)

    def finish_near(self):
        self.arrived(8, self.place.chunk(0, 1, 1), 2)
        self.arrived(9, self.place.chunk(1, 0, 1), 2)

    def finish_far(self):
        for part in (0, 1):
            self.arrived(10 + part, self.place.chunk(1, 1, 1), part)

    def finish(self):
        self.finish_core()
        self.finish_near()
        self.finish_far()
        self.finish_sends()

    def finish_sends(self):
        for moved in self.kept:
            moved.wait_send()
        for keep in self.local:
            keep.wait()


OTHERS = [(di, dg, dc) for di in (0, 1) for dg in (0, 1) for dc in (0, 1) if di or dg or dc]


def first_gather_kernel(count, normed, ids, normed_out, ids_out, before_out, after_out, plane_ids, before, after, send, recv, ids_send, ids_recv):
    place = Place()
    me = lax.axis_index("t")
    up, down = {"t": lax.rem(me + 1, count)}, {"t": lax.rem(me + count - 1, count)}
    place.greet([place.peer(*offset) for offset in OTHERS if sum(offset) > 1] + [up, down])
    gather = Gather(place, normed, normed_out, send, recv)
    own = place.chunk(0, 0, 0)
    moved = []

    def move(number, source, target, peer):
        copy = pltpu.make_async_remote_copy(
            src_ref=source,
            dst_ref=target,
            send_sem=ids_send.at[number],
            recv_sem=ids_recv.at[number],
            device_id=peer,
            device_id_type=MESH,
        )
        copy.start()
        moved.append(copy)

    for number, offset in enumerate(OTHERS):
        move(number, ids, plane_ids.at[own], place.peer(*offset))
    gather.begin_whole()
    plane_ids[own] = ids[...]
    for number, offset in enumerate(OTHERS):
        chunk = place.chunk(*offset)
        pltpu.make_async_remote_copy(
            src_ref=ids,
            dst_ref=plane_ids.at[chunk],
            send_sem=ids_send.at[number],
            recv_sem=ids_recv.at[number],
            device_id=place.peer(*offset),
            device_id_type=MESH,
        ).wait_recv()
    move(7, plane_ids, before, up)
    move(8, plane_ids, after, down)
    gather.pass_on()
    for copy in moved[7:]:
        copy.wait_recv()
    for copy in moved:
        copy.wait_send()
    ids_out[...] = plane_ids[...]
    before_out[...] = before[...]
    after_out[...] = after[...]
    gather.finish()


class Scatter:
    def __init__(self, place, product, core_send, core_recv, held, acc, across_recv, along_recv, second, second_recv, send, recv):
        self.place, self.product = place, product
        self.core_send, self.core_recv, self.held, self.acc = core_send, core_recv, held, acc
        self.across_recv, self.along_recv, self.second, self.second_recv = across_recv, along_recv, second, second_recv
        self.send, self.recv = send, recv
        self.kept = []

    def copy(self, number, source, target, peer):
        return pltpu.make_async_remote_copy(
            src_ref=source,
            dst_ref=target,
            send_sem=self.send.at[number],
            recv_sem=self.recv.at[number],
            device_id=peer,
            device_id_type=MESH,
        )

    def start(self, *parts):
        moved = self.copy(*parts)
        moved.start()
        self.kept.append(moved)

    def run_first(self):
        place = self.place
        order = ((1, 1), (0, 1), (1, 0), (0, 0))
        tile = 256
        per_half = self.held.shape[3] // tile
        def give(di, dg):
            q = 2 * di + dg
            chunk = place.chunk(di, dg, 1)

            def send_tile(n, none):
                at = pl.ds(pl.multiple_of(n % per_half * tile, tile), tile)
                self.core_send[q, n // per_half, :, at] = self.product(chunk, n).astype(BF16)
                return none

            lax.fori_loop(0, 2 * per_half, send_tile, 0)
            self.start(q, self.core_send.at[q], self.core_recv.at[q], place.core)

        def take(di, dg):
            q = 2 * di + dg
            chunk = place.chunk(di, dg, 0)
            self.copy(q, self.core_send.at[q], self.core_recv.at[q], place.core).wait_recv()

            def sum_tile(n, none):
                at = pl.ds(pl.multiple_of(n % per_half * tile, tile), tile)
                value = self.product(chunk, n) + self.core_recv[q, n // per_half, :, at].astype(F32)
                if q:
                    self.held[q - 1, n // per_half, :, at] = value.astype(BF16)
                else:
                    self.acc[n // per_half, :, at] = value
                return none

            lax.fori_loop(0, 2 * per_half, sum_tile, 0)
            if dg:
                self.start(4 + di, self.held.at[q - 1, 0], self.across_recv.at[di], place.across)
            if di:
                self.start(6 + dg, self.held.at[q - 1, 1], self.along_recv.at[dg], place.along)

        give(*order[0])
        give(*order[1])
        take(*order[0])
        give(*order[2])
        take(*order[1])
        give(*order[3])
        take(*order[2])
        take(*order[3])

    def second_copy(self, half, part):
        tokens = self.second.shape[1] // 2
        at = pl.ds(part * tokens, tokens)
        peer = self.place.across if half else self.place.along
        return 8 + 2 * part + half, self.second.at[half, at], self.second_recv.at[half, at], peer

    def run_second(self):
        place = self.place
        tokens = self.second.shape[1] // 2
        for part in (0, 1):
            for half, number, buffer, mine in ((0, 5, self.across_recv, 2), (1, 7, self.along_recv, 1)):
                if part == 0:
                    self.copy(number, buffer.at[1], buffer.at[1], place.core).wait_recv()

                def add_rows(at):
                    total = self.held[mine - 1, half, at, :].astype(F32) + buffer[1, at, :].astype(F32)
                    self.second[half, at, :] = total.astype(BF16)

                for_slices(part * tokens, (part + 1) * tokens, add_rows)
                self.start(*self.second_copy(half, part))

    def run_third(self, part):
        place = self.place
        if part == 0:
            for number, buffer in ((4, self.across_recv), (6, self.along_recv)):
                self.copy(number, buffer.at[0], buffer.at[0], place.core).wait_recv()
        for half in (0, 1):
            self.copy(*self.second_copy(half, part)).wait_recv()

    def rows(self, at):
        first = self.acc[0, at, :] + self.across_recv[0, at, :].astype(F32) + self.second_recv[0, at, :].astype(F32)
        last = self.acc[1, at, :] + self.along_recv[0, at, :].astype(F32) + self.second_recv[1, at, :].astype(F32)
        return jnp.concatenate([first, last], axis=1)

    def finish(self):
        for moved in self.kept:
            moved.wait_send()

    @staticmethod
    def scratch(tokens, width):
        half = width // 2
        return [
            pltpu.VMEM((4, 2, tokens, half), BF16),
            pltpu.VMEM((4, 2, tokens, half), BF16),
            pltpu.VMEM((3, 2, tokens, half), BF16),
            pltpu.VMEM((2, tokens, half), F32),
            pltpu.VMEM((2, tokens, half), BF16),
            pltpu.VMEM((2, tokens, half), BF16),
            pltpu.VMEM((2, tokens, half), BF16),
            pltpu.VMEM((2, tokens, half), BF16),
            pltpu.SemaphoreType.DMA((12,)),
            pltpu.SemaphoreType.DMA((12,)),
        ]


SCATTER_BUFFERS = 10


def pair_product(lefts, rights, tokens):
    def product(chunk, n):
        at = pl.ds(pl.multiple_of(chunk * tokens, tokens), tokens)
        cols = pl.ds(pl.multiple_of(n * 256, 256), 256)
        total = None
        for left, right in zip(lefts, rights):
            term = jnp.dot(left[at, :], right[:, cols], preferred_element_type=F32)
            total = term if total is None else total + term
        return total

    return product


def for_slices(start, stop, body):
    def step(n, none):
        body(pl.ds(pl.multiple_of(n * SLICE, SLICE), SLICE))
        return none

    lax.fori_loop(start // SLICE, stop // SLICE, step, 0)


def middle_kernel(left, right, own_in, gain, middle_out, gathered, *scratch):
    buffers, (block, send, recv) = scratch[:SCATTER_BUFFERS], scratch[SCATTER_BUFFERS:]
    tokens = own_in.shape[0]
    place = Place()
    place.greet()
    scatter = Scatter(place, pair_product([left], [right], tokens), *buffers)
    scatter.run_first()
    scatter.run_second()

    def body(at):
        middle = own_in[at, :].astype(F32) + scatter.rows(at)
        middle_out[at, :] = middle
        block[at, :] = (middle * rms(middle) * gain[...]).astype(BF16)

    gather = Gather(place, block, gathered, send, recv)
    for part in (0, 1):
        scatter.run_third(part)
        for_slices(part * tokens // 2, (part + 1) * tokens // 2, body)
        gather.begin(part)
    gather.pass_on()
    scatter.finish()
    gather.finish()


def turn_kernel(
    left0, left1, right0, right1, middle, gain, cot, normed_far, grad_middle_out, gain_out, grads_out, block_out, *scratch
):
    buffers, (normed, load) = scratch[:SCATTER_BUFFERS], scratch[SCATTER_BUFFERS:]
    loaded = pltpu.make_async_copy(normed_far, normed, load.at[0])
    loaded.start()
    tokens, hidden = cot.shape[0], left0.shape[1]
    place = Place()
    place.greet()
    scatter = Scatter(place, pair_product([left0, left1], [right0, right1], tokens), *buffers)
    scatter.run_first()
    scatter.run_second()
    loaded.wait()

    def weight_grads(n, none):
        at = pl.ds(pl.multiple_of(n * 256, 256), 256)
        for k, part in enumerate((left0, left1)):
            value = lax.dot_general(normed[:, at], part[...], (((0,), (0,)), ((), ())), preferred_element_type=F32)
            grads_out[at, k * hidden : (k + 1) * hidden] = value.astype(BF16)
        return none

    lax.fori_loop(0, normed.shape[1] // 256, weight_grads, 0)
    gain_out[...] = jnp.zeros_like(gain_out)

    def body(at):
        values = middle[at, :]
        grad = scatter.rows(at)
        scale = rms(values)
        weighted = grad * gain[...]
        inner = jnp.mean(values * weighted, axis=-1, keepdims=True)
        total = cot[at, :].astype(F32) + scale * weighted - values * (scale * scale * scale * inner)
        grad_middle_out[at, :] = total
        block_out[at, :] = total.astype(BF16)
        term = grad * values * scale
        gain_out[...] += term[0:8] + term[8:16]

    for part in (0, 1):
        scatter.run_third(part)
        for_slices(part * tokens // 2, (part + 1) * tokens // 2, body)
    scatter.finish()


def spread_kernel(block, w_out, mixed, mixed_out, out_grad, gathered, send, recv, chunk_ref, total, load):
    tokens = block.shape[0]
    place = Place()
    place.greet()
    gather = Gather(place, block, gathered, send, recv)
    gather.begin_whole()
    total[...] = jnp.zeros_like(total)

    def fetch(slot, chunk):
        at = pl.ds(pl.multiple_of(chunk * tokens, tokens), tokens)
        copy = pltpu.make_async_copy(gathered.at[at], chunk_ref.at[slot], load.at[slot])
        copy.start()
        return copy, slot, chunk

    def use(fetched):
        copy, slot, chunk = fetched
        copy.wait()
        use_chunk(chunk_ref.at[slot], chunk)

    def use_chunk(values, chunk):
        at = pl.ds(pl.multiple_of(chunk * tokens, tokens), tokens)
        mixed_out[at, :] = lax.dot_general(values[...], w_out[...], (((1,), (1,)), ((), ())), preferred_element_type=F32)
        part = mixed[at, :]

        def rows(n, none):
            columns = pl.ds(pl.multiple_of(n * 256, 256), 256)
            turned = (((0,), (0,)), ((), ()))
            total[columns, :] += lax.dot_general(values[:, columns], part, turned, preferred_element_type=F32)
            return none

        lax.fori_loop(0, values.shape[1] // 256, rows, 0)

    use_chunk(block, place.chunk(0, 0, 0))
    gather.pass_first()
    gather.finish_core()
    ahead = fetch(0, place.chunk(0, 0, 1))
    use(ahead)
    gather.pass_second()
    ahead = fetch(0, place.chunk(0, 1, 0))
    after = fetch(1, place.chunk(1, 0, 0))
    use(ahead)
    gather.finish_near()
    ahead = fetch(0, place.chunk(0, 1, 1))
    use(after)
    gather.pass_third()
    after = fetch(1, place.chunk(1, 0, 1))
    use(ahead)
    ahead = fetch(0, place.chunk(1, 1, 0))
    use(after)
    gather.finish_far()
    after = fetch(1, place.chunk(1, 1, 1))
    use(ahead)
    use(after)
    out_grad[...] = total[...].astype(BF16)
    gather.finish_sends()


class Owners:
    def __init__(self, place, reduced, out, send, recv):
        self.place, self.reduced, self.out, self.send, self.recv = place, reduced, out, send, recv
        self.own = place.chunk(0, 0, 0)

    def copy(self, number, offset, slot):
        return pltpu.make_async_remote_copy(
            src_ref=self.reduced.at[self.place.chunk(*offset)],
            dst_ref=self.out.at[slot],
            send_sem=self.send.at[number],
            recv_sem=self.recv.at[number],
            device_id=self.place.peer(*offset),
            device_id_type=MESH,
        )

    def begin(self):
        self.keep = pltpu.make_async_copy(self.reduced.at[self.own], self.out.at[self.own], self.send.at[7])
        self.keep.start()
        self.moved = [self.copy(number, offset, self.own) for number, offset in enumerate(OTHERS)]
        for copy in self.moved:
            copy.start()

    def finish(self):
        for number, offset in enumerate(OTHERS):
            self.copy(number, offset, self.place.chunk(*offset)).wait_recv()
        for copy in self.moved:
            copy.wait_send()
        self.keep.wait()


OWNERS_SCRATCH = [pltpu.SemaphoreType.DMA((8,))] * 2
BEYOND = [offset for offset in OTHERS if sum(offset) > 1]


class GateSums:
    def __init__(self, place, count, pieces, rows_recv, gates_all, send, recv):
        self.place, self.count, self.pieces = place, count, pieces
        self.rows_recv, self.gates_all, self.send, self.recv = rows_recv, gates_all, send, recv
        self.me = lax.axis_index("t")
        self.rank = place.g * 2 + place.c
        self.near = [offset for offset in OTHERS if not offset[0]]
        self.moved = []

    def copy(self, number, source, target, peer):
        return pltpu.make_async_remote_copy(
            src_ref=source,
            dst_ref=target,
            send_sem=self.send.at[number],
            recv_sem=self.recv.at[number],
            device_id=peer,
            device_id_type=MESH,
        )

    def begin(self):
        for number, offset in enumerate(self.near):
            other = lax.rem(self.place.chunk(*offset), 4)
            self.moved.append(self.copy(number, self.pieces.at[other], self.rows_recv.at[self.rank], self.place.peer(*offset)))
            self.moved[-1].start()
        self.rows_recv[self.rank] = self.pieces[self.rank]

    def settle(self, out):
        for number, offset in enumerate(self.near):
            other = lax.rem(self.place.chunk(*offset), 4)
            self.copy(number, self.pieces.at[other], self.rows_recv.at[other], self.place.peer(*offset)).wait_recv()
        out[...] = self.rows_recv[...]
        for copy in self.moved:
            copy.wait_send()

    def pass_on(self):
        for step in range(1, self.count):
            to = lax.rem(self.me + step, self.count)
            self.moved.append(self.copy(2 + step, self.rows_recv.at[to], self.gates_all.at[self.me], {"t": to}))
            self.moved[-1].start()
        self.gates_all[self.me] = self.rows_recv[self.me]

    def finish(self, out):
        for step in range(1, self.count):
            other = lax.rem(self.me + self.count - step, self.count)
            self.copy(2 + step, self.rows_recv.at[other], self.gates_all.at[other], {"t": other}).wait_recv()
        total = self.gates_all[0].astype(F32)
        for z in range(1, self.count):
            total = total + self.gates_all[z].astype(F32)
        out[...] = total
        for copy in self.moved:
            copy.wait_send()


class SmallSum:
    def __init__(self, place, count, values, inbox, plane_sum, plane_box, send, recv):
        self.place, self.count, self.values, self.inbox = place, count, values, inbox
        self.plane_sum, self.plane_box, self.send, self.recv = plane_sum, plane_box, send, recv
        self.me = lax.axis_index("t")
        self.moved = []

    def copy(self, number, source, target, peer):
        return pltpu.make_async_remote_copy(
            src_ref=source,
            dst_ref=target,
            send_sem=self.send.at[number],
            recv_sem=self.recv.at[number],
            device_id=peer,
            device_id_type=MESH,
        )

    def begin(self):
        own = self.place.chunk(0, 0, 0)
        for number, offset in enumerate(OTHERS):
            self.moved.append(self.copy(number, self.values, self.inbox.at[own], self.place.peer(*offset)))
            self.moved[-1].start()
        self.inbox[own] = self.values[...]

    def pass_on(self):
        for number, offset in enumerate(OTHERS):
            slot = self.inbox.at[self.place.chunk(*offset)]
            self.copy(number, self.values, slot, self.place.peer(*offset)).wait_recv()
        total = self.inbox[0]
        for n in range(1, 8):
            total = total + self.inbox[n]
        self.plane_sum[...] = total
        self.plane_box[self.me] = total
        for step in range(1, self.count):
            to = {"t": lax.rem(self.me + step, self.count)}
            self.moved.append(self.copy(6 + step, self.plane_sum, self.plane_box.at[self.me], to))
            self.moved[-1].start()

    def finish(self, out):
        for step in range(1, self.count):
            other = lax.rem(self.me + self.count - step, self.count)
            self.copy(6 + step, self.plane_sum, self.plane_box.at[other], {"t": other}).wait_recv()
        total = self.plane_box[0]
        for z in range(1, self.count):
            total = total + self.plane_box[z]
        out[...] = total
        for sent in self.moved:
            sent.wait_send()


def final_kernel(
    left, right, own_in, gain, mlp_gains, grad_middle, pieces, reduced, grad_out, values_out, rows_out, owned,
    gain_sum, rows_recv, gates_send, gates_recv, own_send, own_recv, *buffers,
):
    tokens, width = own_in.shape
    place = Place()
    place.greet([place.peer(*offset) for offset in BEYOND])
    scatter = Scatter(place, pair_product([left], [right], tokens), *buffers)
    owners = Owners(place, reduced, owned, own_send, own_recv)
    gates = GateSums(place, 0, pieces, rows_recv, None, gates_send, gates_recv)
    scatter.run_first()
    gates.begin()
    owners.begin()
    scatter.run_second()
    gain_sum[...] = jnp.zeros_like(gain_sum)

    def body(at):
        x = own_in[at, :].astype(F32)
        grad = scatter.rows(at)
        scale = rms(x)
        weighted = grad * gain[...]
        inner = jnp.mean(x * weighted, axis=-1, keepdims=True)
        grad_out[at, :] = grad_middle[at, :] + scale * weighted - x * (scale * scale * scale * inner)
        term = grad * x * scale
        gain_sum[...] += term[0:8] + term[8:16]

    for part in (0, 1):
        scatter.run_third(part)
        for_slices(part * tokens // 2, (part + 1) * tokens // 2, body)
    lines = width // LANES
    for base, row in ((0, jnp.sum(mlp_gains[...], axis=0, keepdims=True)), (lines, jnp.sum(gain_sum[...], axis=0, keepdims=True))):
        for n in range(lines):
            values_out[base + n : base + n + 1, :] = row[:, n * LANES : (n + 1) * LANES]
    gates.settle(rows_out)
    owners.finish()
    scatter.finish()


def final_step(left, right, own_in, gain, mlp_gains, grad_middle, pieces, reduced):
    tokens, width = own_in.shape
    return pl.pallas_call(
        final_kernel,
        name="final_step",
        out_shape=(
            jax.ShapeDtypeStruct((tokens, width), F32),
            jax.ShapeDtypeStruct((2 * width // LANES, LANES), F32),
            jax.ShapeDtypeStruct(pieces.shape, pieces.dtype),
            jax.ShapeDtypeStruct(reduced.shape, reduced.dtype),
        ),
        in_specs=[*whole(7), ANYWHERE],
        out_specs=(*whole(3), ANYWHERE),
        scratch_shapes=[
            pltpu.VMEM((8, width), F32),
            pltpu.VMEM(pieces.shape, BF16),
            pltpu.SemaphoreType.DMA((3,)),
            pltpu.SemaphoreType.DMA((3,)),
            *OWNERS_SCRATCH,
            *Scatter.scratch(tokens, width),
        ],
        compiler_params=mixer_params(7),
    )(left, right, own_in, gain[None], mlp_gains, grad_middle, pieces, reduced)


def owners_kernel(
    count, with_gates, pieces, values, reduced0, reduced1, gates_out, gains_out, out0, out1,
    inbox, plane_sum, plane_box, sum_send, sum_recv, gates_all, gates_send, gates_recv,
    send0, recv0, send1, recv1,
):
    place = Place()
    me = lax.axis_index("t")
    place.greet([place.peer(*offset) for offset in BEYOND] + [{"t": lax.rem(me + step, count)} for step in range(1, count)])
    owners = [Owners(place, reduced0, out0, send0, recv0), Owners(place, reduced1, out1, send1, recv1)]
    gates = GateSums(place, count, None, pieces, gates_all, gates_send, gates_recv)
    gains = SmallSum(place, count, values, inbox, plane_sum, plane_box, sum_send, sum_recv)
    gains.begin()
    if with_gates:
        gates.pass_on()
    for part in owners:
        part.begin()
    gains.pass_on()
    gains.finish(gains_out)
    if with_gates:
        gates.finish(gates_out)
    else:
        gates_out[...] = jnp.zeros_like(gates_out)
    for part in owners:
        part.finish()


def owners_step(planes, with_gates, pieces, values, reduced):
    block = pieces.shape[1:]
    slots = planes if with_gates else 1
    return pl.pallas_call(
        functools.partial(owners_kernel, planes, with_gates),
        name="owners_step",
        out_shape=(
            jax.ShapeDtypeStruct(block, F32),
            jax.ShapeDtypeStruct(values.shape, F32),
            *[jax.ShapeDtypeStruct(part.shape, part.dtype) for part in reduced],
        ),
        in_specs=[*whole(2), ANYWHERE, ANYWHERE],
        out_specs=(*whole(2), ANYWHERE, ANYWHERE),
        scratch_shapes=[
            pltpu.VMEM((8, *values.shape), F32),
            pltpu.VMEM(values.shape, F32),
            pltpu.VMEM((planes, *values.shape), F32),
            pltpu.SemaphoreType.DMA((planes + 6,)),
            pltpu.SemaphoreType.DMA((planes + 6,)),
            pltpu.VMEM((slots, *block), BF16),
            pltpu.SemaphoreType.DMA((planes + 2,)),
            pltpu.SemaphoreType.DMA((planes + 2,)),
            *OWNERS_SCRATCH,
            *OWNERS_SCRATCH,
        ],
        compiler_params=mixer_params(8),
    )(pieces, values, *reduced)


def place_kernel(planes, hidden, outs, through, *refs):
    count = len(outs)
    given, passed, results, copied = refs[:count], refs[count : count + through], refs[count + through : 2 * count + through], refs[2 * count + through :]
    for source, target in zip(passed, copied):
        target[...] = source[...]
    for count, sources, out in zip(outs, given, results):
        piece = sources.shape[2] // (count * (planes if hidden else 1))
        for k in range(count):
            if hidden:
                groups = [
                    ((t * 2 + i) * 4 * piece, [(i * 4 + r, (k * planes + t) * piece) for r in range(4)])
                    for t in range(planes)
                    for i in range(2)
                ]
            else:
                groups = [(r * 2 * piece, [(i * 4 + r, k * piece) for i in range(2)]) for r in range(4)]
            for start, parts in groups:
                row = jnp.concatenate([sources[p, :, at : at + piece].astype(F32) for p, at in parts], axis=1)
                if count > 1:
                    out[:, k, start : start + row.shape[1]] = row
                else:
                    out[:, start : start + row.shape[1]] = row


def place_columns(planes, hidden, outs, owned, through=()):
    members, own_rows, columns = owned[0].shape
    total = columns * members // outs[0]
    shapes = [(own_rows, count, total) if count > 1 else (own_rows, total) for count in outs]
    return pl.pallas_call(
        functools.partial(place_kernel, planes, hidden, outs, len(through)),
        name="place_columns",
        out_shape=(
            *[jax.ShapeDtypeStruct(shape, F32) for shape in shapes],
            *[jax.ShapeDtypeStruct(part.shape, part.dtype) for part in through],
        ),
        in_specs=whole(len(owned) + len(through)),
        out_specs=tuple(whole(len(outs) + len(through))),
        compiler_params=pltpu.CompilerParams(vmem_limit_bytes=60 * 1024 * 1024),
    )(*owned, *through)


def last_kernel(planes, own_in, own_out, gates, gains, in_out, out_out, gate_out, taps_out, bias_out, logit_out, decay_out, mlp_out, mix_out):
    place_kernel(planes, False, (2, 1), 0, own_in, own_out, in_out, out_out)
    size, part = gate_out.shape[0], gate_out.shape[2]
    for k in range(2):
        gate_out[:, k, :] = gates[k * size : (k + 1) * size, :part]
    rest = gates[2 * size : 2 * size + 8, :part]
    taps_out[...] = rest[0:4]
    bias_out[...] = rest[4:5]
    logit_out[...] = rest[5:7]
    decay_out[...] = rest[7:8]
    own_rows = mlp_out.shape[1]
    per_line = LANES // own_rows
    index = lax.axis_index("t") * 8 + Place().chunk(0, 0, 0)
    for base, out in ((0, mlp_out), (gains.shape[0] // 2, mix_out)):
        line = gains[pl.ds(base + index // per_line, 1), :]
        value = line[:, :own_rows]
        for n in range(1, per_line):
            value = jnp.where(index % per_line == n, line[:, n * own_rows : (n + 1) * own_rows], value)
        out[...] = value


def last_step(planes, own_in, own_out, gates, gains, size, part):
    members, own_rows, columns = own_out.shape
    shapes = [
        (own_rows, 2, columns * members), (own_rows, columns * members),
        (size, 2, part), (4, part), (1, part), (2, part), (1, part), (1, own_rows), (1, own_rows),
    ]
    return pl.pallas_call(
        functools.partial(last_kernel, planes),
        name="place_last",
        out_shape=tuple(jax.ShapeDtypeStruct(shape, F32) for shape in shapes),
        in_specs=whole(4),
        out_specs=tuple(whole(9)),
        compiler_params=pltpu.CompilerParams(vmem_limit_bytes=60 * 1024 * 1024),
    )(own_in, own_out, gates, gains)


def first_gather(planes, normed, ids):
    tokens, width = normed.shape
    every = (8, *ids.shape)
    return pl.pallas_call(
        functools.partial(first_gather_kernel, planes),
        name="first_gather",
        out_shape=(jax.ShapeDtypeStruct((8 * tokens, width), BF16), *[jax.ShapeDtypeStruct(every, F32)] * 3),
        in_specs=[ANYWHERE, *whole(1)],
        out_specs=(ANYWHERE, *whole(3)),
        scratch_shapes=[pltpu.VMEM(every, F32)] * 3 + GATHER_SCRATCH + [pltpu.SemaphoreType.DMA((9,))] * 2,
        compiler_params=mixer_params(3),
    )(normed, ids)


def middle_step(mixed, w_out, own_in, gain):
    tokens, width = own_in.shape
    return pl.pallas_call(
        middle_kernel,
        name="middle_step",
        out_shape=(jax.ShapeDtypeStruct((tokens, width), F32), jax.ShapeDtypeStruct((8 * tokens, width), BF16)),
        in_specs=whole(4),
        out_specs=(pl.BlockSpec(memory_space=pltpu.VMEM), ANYWHERE),
        scratch_shapes=Scatter.scratch(tokens, width) + [pltpu.VMEM((tokens, width), BF16)] + GATHER_SCRATCH,
        compiler_params=mixer_params(4),
    )(mixed, w_out, own_in, gain[None])


def turn_step(left0, left1, right0, right1, middle, gain, cot, normed):
    tokens, width = cot.shape
    return pl.pallas_call(
        turn_kernel,
        name="turn_step",
        out_shape=(
            jax.ShapeDtypeStruct((tokens, width), F32),
            jax.ShapeDtypeStruct((8, width), F32),
            jax.ShapeDtypeStruct((width, 2 * left1.shape[1]), BF16),
            jax.ShapeDtypeStruct((tokens, width), BF16),
        ),
        in_specs=[*whole(7), ANYWHERE],
        out_specs=tuple(whole(4)),
        scratch_shapes=Scatter.scratch(tokens, width)
        + [pltpu.VMEM(normed.shape, BF16), pltpu.SemaphoreType.DMA((1,))],
        compiler_params=mixer_params(5),
    )(left0, left1, right0, right1, middle, gain[None], cot, normed)


def spread_step(block, w_out, mixed):
    tokens, width = block.shape
    return pl.pallas_call(
        spread_kernel,
        name="turn_spread",
        out_shape=(
            jax.ShapeDtypeStruct((8 * tokens, w_out.shape[0]), F32),
            jax.ShapeDtypeStruct((width, w_out.shape[0]), BF16),
            jax.ShapeDtypeStruct((8 * tokens, width), BF16),
        ),
        in_specs=whole(3),
        out_specs=(*whole(2), ANYWHERE),
        scratch_shapes=GATHER_SCRATCH
        + [
            pltpu.VMEM((2, tokens, width), BF16),
            pltpu.VMEM((width, w_out.shape[0]), F32),
            pltpu.SemaphoreType.DMA((2,)),
        ],
        compiler_params=mixer_params(10),
    )(block, w_out, mixed)


class Swap:
    def __init__(self, quarters, out, send, recv):
        self.quarters, self.out, self.send, self.recv = quarters, out, send, recv
        self.groups = quarters.shape[0]
        self.me = lax.axis_index("g") * 2 + lax.axis_index("c")

    def copy(self, step, other, slot):
        return pltpu.make_async_remote_copy(
            src_ref=self.quarters.at[other],
            dst_ref=self.out.at[:, slot],
            send_sem=self.send.at[step],
            recv_sem=self.recv.at[step],
            device_id={"g": other // 2, "c": other % 2},
            device_id_type=MESH,
        )

    def peers(self):
        others = [lax.rem(self.me + step, self.groups) for step in range(1, self.groups)]
        return [{"g": other // 2, "c": other % 2} for other in others]

    def begin(self):
        self.keep = pltpu.make_async_copy(self.quarters.at[self.me], self.out.at[:, self.me], self.send.at[0])
        self.keep.start()
        self.moved = []
        for step in range(1, self.groups):
            self.moved.append(self.copy(step, lax.rem(self.me + step, self.groups), self.me))
            self.moved[-1].start()

    def finish(self):
        for step in range(1, self.groups):
            other = lax.rem(self.me + self.groups - step, self.groups)
            self.copy(step, other, other).wait_recv()
        for copy in self.moved:
            copy.wait_send()
        self.keep.wait()


def swap_scratch(groups):
    return [pltpu.SemaphoreType.DMA((groups,)), pltpu.SemaphoreType.DMA((groups,))]


def swap_kernel(quarters, out, send, recv):
    move = Swap(quarters, out, send, recv)
    barrier = pltpu.get_barrier_semaphore()
    for peer in move.peers():
        pl.semaphore_signal(barrier, inc=1, device_id=peer, device_id_type=MESH)
    pl.semaphore_wait(barrier, move.groups - 1)
    move.begin()
    move.finish()


def swap(quarters):
    groups, kinds, part, width = quarters.shape
    return pl.pallas_call(
        swap_kernel,
        name="swap",
        out_shape=jax.ShapeDtypeStruct((kinds, groups, part, width), quarters.dtype),
        in_specs=[ANYWHERE],
        out_specs=ANYWHERE,
        scratch_shapes=swap_scratch(groups),
        compiler_params=mixer_params(6),
    )(quarters)


def rms(values):
    return lax.rsqrt(jnp.mean(values * values, axis=-1, keepdims=True) + EPS)


def nt(left, right, out):
    return lax.dot_general(left, right, (((1,), (1,)), ((), ())), preferred_element_type=F32).astype(out)


def tn(left, right, out):
    return lax.dot_general(left, right, (((0,), (0,)), ((), ())), preferred_element_type=F32).astype(out)


def nn(left, right, out):
    return jnp.dot(left, right, preferred_element_type=F32).astype(out)


def per_device(
    inputs, segment_ids, mix_gain, in_weight, conv_weight, conv_bias, gate_weight, gate_bias, decay_param, out_weight,
    mlp_gain, mlp_in, down_weight, cotangent,
):
    planes = lax.axis_size("t")
    rows_here, seg, width = inputs.shape
    row_groups = lax.axis_size("g") * lax.axis_size("c")
    own_tokens = rows_here * seg
    recur_width = conv_weight.shape[1]
    block_width = gate_weight.shape[0]
    members = 2 * row_groups
    channels = recur_width // members
    t, i = lax.axis_index("t"), lax.axis_index("i")
    r = lax.axis_index("g") * lax.axis_size("c") + lax.axis_index("c")
    member = 2 * r + i
    first = member * channels
    own_rows = width // (planes * members)

    own_in = inputs.reshape(own_tokens, width)
    flat_in = own_in.astype(F32)
    scale_in = rms(flat_in)
    cot_own = cotangent.reshape(own_tokens, width)
    own_ids = jnp.pad((segment_ids + 1).astype(F32), ((0, 8 - rows_here), (0, 0)))

    normed, *ids = first_gather(planes, (flat_in * scale_in * mix_gain).astype(BF16), own_ids)
    late_r, ids[0] = lax.optimization_barrier((r, ids[0]))

    direct = planes == row_groups
    in_own = in_weight.transpose(1, 2, 0)
    out_own = out_weight.T[None]
    part = channels // row_groups if direct else 0

    def quarter(weight, part, rank=r):
        return lax.dynamic_slice_in_dim(weight, rank * part, part, weight.ndim - 1)

    def spread_units(weight):
        return lax.all_gather(weight, "t", axis=0, tiled=False)

    def whole_units(weight):
        every = lax.all_gather(weight, ("t", "i"), axis=1, tiled=True)
        return lax.dynamic_slice_in_dim(every, first, channels, 1)

    if direct:
        in_w = swap(spread_units(quarter(in_weight, part).transpose(1, 2, 0)))
        out_quarters = spread_units(quarter(out_weight, part).T[None])
    else:
        in_w = whole_units(in_own)
        out_quarters = jnp.zeros((row_groups, 1, 16, width), BF16)
    in_w = in_w.reshape(2 * channels, width)
    hidden_part = mlp_in.shape[2] // row_groups
    gated = quarter(mlp_in, hidden_part, late_r).transpose(1, 2, 0)
    w_left, w_right, w_down = [
        spread_units(part).reshape(-1, width)
        for part in (gated[0], gated[1], quarter(down_weight, hidden_part, late_r).T)
    ]

    def own(values):
        return lax.dynamic_slice_in_dim(values, first, channels, values.ndim - 1)

    vec = own(
        jnp.concatenate(
            [
                conv_weight,
                conv_bias[None],
                gate_bias,
                8.0 * jax.nn.softplus(-decay_param)[None],
                8.0 * jax.nn.sigmoid(-decay_param)[None],
                jnp.zeros((7, recur_width), F32),
            ]
        )
    )
    gate_blocks = own(gate_weight).transpose(1, 0, 2)
    blocks = channels // block_width

    branches = nt(normed, in_w, F32)
    conv_low, decay, states, mixed, halo, cin, mask, cot, w_out = mixer_forward(
        planes, seg, rows_here, branches, ids, gate_blocks, vec, cot_own, out_quarters
    )
    w_out = (w_out if direct else whole_units(out_own)).reshape(channels, width)
    middle, normed_two = middle_step(mixed, w_out, own_in, mlp_gain)
    left = nt(normed_two, w_left, F32)
    right = nt(normed_two, w_right, F32)
    act, slope = gelu_parts(left)
    hidden = (act * right).astype(BF16)

    def over_planes(grad):
        return lax.psum_scatter(grad, "t", scatter_dimension=0, tiled=True)

    grad_down = tn(cot, hidden, BF16)
    grad_down, hidden, w_down = lax.optimization_barrier((grad_down, hidden, w_down))
    grad_down = over_planes(grad_down)
    grad_hidden = nt(cot, w_down, F32)
    grad_left = (grad_hidden * right * slope).astype(BF16)
    grad_right = (grad_hidden * act).astype(BF16)
    grad_middle, grad_mlp_gain, grad_mlp_in, grad_mid_own = turn_step(
        grad_left, grad_right, w_left, w_right, middle, mlp_gain, cot_own, normed_two
    )
    grad_down, grad_mid_own = lax.optimization_barrier((grad_down, grad_mid_own))
    grad_mlp_in = over_planes(grad_mlp_in)
    grad_mixed, grad_out, _ = spread_step(grad_mid_own, w_out, mixed)

    def by_owner(grad):
        return grad.reshape(members, own_rows, -1)

    grad_branches, gw0, gw1, small, pieces, outputs, owned_down = mixer_backward(
        planes, seg, grad_mixed, branches, states, decay, conv_low, mask, halo, cin, gate_blocks, vec, hidden, w_down, middle,
        by_owner(grad_down),
    )
    grad_mlp_in, grad_branches = lax.optimization_barrier((grad_mlp_in, grad_branches))
    grad_out = over_planes(grad_out)
    grad_in = tn(normed, grad_branches, BF16)
    grad_in, grad_branches = lax.optimization_barrier((grad_in, grad_branches))
    grad_in = over_planes(grad_in)
    outputs = outputs.reshape(inputs.shape)

    grad_inputs, values, pieces, owned_mlp_in = final_step(
        grad_branches, in_w, own_in, mix_gain, grad_mlp_gain, grad_middle, pieces, by_owner(grad_mlp_in)
    )
    gate_grads, gains, owned_in, owned_out = owners_step(planes, direct, pieces, values, [by_owner(grad_in), by_owner(grad_out)])
    grad_inputs = grad_inputs.reshape(inputs.shape)
    def columns(hidden, outs, owned, through=()):
        if direct:
            return place_columns(planes, hidden, outs, owned, through)
        owned = jnp.concatenate(owned, axis=2)
        owned = owned.reshape(2, row_groups, own_rows, sum(outs), planes if hidden else 1, -1).astype(F32)
        order = (2, 3, 4, 0, 1, 5) if hidden else (2, 3, 1, 0, 4, 5)
        owned = owned.transpose(order).reshape(own_rows, sum(outs), -1)
        return (owned[:, :2], owned[:, 2], *through)

    grad_mlp_in, grad_down_weight, outputs, grad_inputs = columns(
        True, (2, 1), [owned_mlp_in, owned_down], [outputs, grad_inputs]
    )
    if direct:
        grad_in_weight, grad_out_weight, grad_gate_weight, taps, bias, logit_bias, decay_grad, mlp_sum, mix_sum = last_step(
            planes, owned_in, owned_out, gate_grads, gains, block_width, part
        )
        bias, decay_grad, mlp_sum, mix_sum = bias[0], decay_grad[0], mlp_sum[0], mix_sum[0]
    else:
        grad_in_weight, grad_out_weight = columns(False, (2, 1), [owned_in, owned_out])
        index = ((t * 2 + i) * row_groups + r) * own_rows
        mlp_sum, mix_sum = lax.dynamic_slice_in_dim(gains.reshape(2, width), index, own_rows, 1)
        column_block = lax.broadcasted_iota(jnp.int32, (block_width, channels), 1) // block_width

        def diagonal(gw):
            return sum(
                jnp.where(column_block == n, gw[n * block_width : (n + 1) * block_width], 0.0) for n in range(blocks)
            )

        gate_grads = jnp.concatenate([diagonal(gw0), diagonal(gw1), small], axis=0)
        placed = jnp.zeros((gate_grads.shape[0], recur_width), F32)
        placed = lax.dynamic_update_slice_in_dim(placed, gate_grads, first, 1)
        gate_grads = lax.psum_scatter(placed, EVERY, scatter_dimension=1, tiled=True)
        grad_gate_weight = jnp.stack([gate_grads[:block_width], gate_grads[block_width : 2 * block_width]], axis=1)
        rest = gate_grads[2 * block_width :]
        taps, bias, logit_bias, decay_grad = rest[0:4], rest[4], rest[5:7], rest[7]
    return (
        outputs,
        grad_inputs,
        mix_sum,
        grad_in_weight,
        taps,
        bias,
        grad_gate_weight,
        logit_bias,
        decay_grad,
        grad_out_weight,
        mlp_sum,
        grad_mlp_in,
        grad_down_weight,
    )


def solution(mesh):
    seq, rows = mesh.shape["seq"], mesh.shape["rows"]
    grid = Mesh(mesh.devices.reshape(seq // 2, 2, rows // 2, 2), EVERY)
    row_axes, seq_axes = ("g", "c"), ("t", "i")
    tokens = P(row_axes, seq_axes, None)
    return jax.shard_map(
        per_device,
        mesh=grid,
        in_specs=(
            tokens,
            P(row_axes, seq_axes),
            P(),
            P(None, None, seq_axes),
            P(),
            P(),
            P(),
            P(),
            P(),
            P(None, seq_axes),
            P(),
            P(None, None, seq_axes),
            P(None, seq_axes),
            tokens,
        ),
        out_specs=(
            tokens,
            tokens,
            P(EVERY),
            P(EVERY, None, None),
            P(None, EVERY),
            P(EVERY),
            P(None, None, EVERY),
            P(None, EVERY),
            P(EVERY),
            P(EVERY, None),
            P(EVERY),
            P(EVERY, None, None),
            P(EVERY, None),
        ),
        check_vma=False,
    )
```
